32 devices in a mesh: rows: 4 (over y, core), mp: 8 (over z, x).
Axes of the slice: x: 2, y: 2, z: 4, core: 2. Of those that a mesh axis runs over, the one named last changes fastest.
Arguments:
- tokens: bfloat16 [8192, 1024], P(('rows', 'mp')), may hold values from -6 to 6
- segment_ids: int32 [8192], P('rows'), may hold values from 0 to 3, as said below
- cotangent: bfloat16 [8192, 1024], P(('rows', 'mp')), may hold values from -6 to 6
- ln_attn_gain: float32 [2, 1024], replicated, may hold values from 0.25 to 1.75
- ln_attn_bias: float32 [2, 1024], replicated, may hold values from -4 to 4
- qkv_weight: bfloat16 [2, 1024, 3, 1024], P(None, None, None, 'mp'), may hold values from -0.1875 to 0.1875
- qv_bias: float32 [2, 2, 1024], P(None, None, 'mp'), may hold values from -4 to 4
- head_scale: float32 [2, 16], replicated, may hold values from 0.25 to 1.75
- out_weight: bfloat16 [2, 1024, 1024], P(None, 'mp'), may hold values from -0.1875 to 0.1875
- out_bias: float32 [2, 1024], replicated, may hold values from -4 to 4
- ln_post_gain: float32 [2, 1024], replicated, may hold values from 0.25 to 1.75
- ln_post_bias: float32 [2, 1024], replicated, may hold values from -4 to 4
- ln_ffn_gain: float32 [2, 1024], replicated, may hold values from 0.25 to 1.75
- ln_ffn_bias: float32 [2, 1024], replicated, may hold values from -4 to 4
- fc1_weight: bfloat16 [2, 1024, 4096], P(None, None, 'mp'), may hold values from -0.1875 to 0.1875
- fc1_bias: float32 [2, 4096], P(None, 'mp'), may hold values from -4 to 4
- mid_gain: float32 [2, 4096], P(None, 'mp'), may hold values from 0.25 to 1.75
- mid_bias: float32 [2, 4096], P(None, 'mp'), may hold values from -4 to 4
- fc2_weight: bfloat16 [2, 4096, 1024], P(None, 'mp'), may hold values from -0.09375 to 0.09375
- fc2_bias: float32 [2, 1024], replicated, may hold values from -4 to 4
Outputs:
- layer_output: bfloat16 [8192, 1024], P(('rows', 'mp'))
- input_grad: float32 [8192, 1024], P(('rows', 'mp'))
- ln_attn_gain_grad: float32 [2, 1024], replicated
- ln_attn_bias_grad: float32 [2, 1024], replicated
- qkv_weight_grad: float32 [2, 1024, 3, 1024], P(None, None, None, 'mp')
- qv_bias_grad: float32 [2, 2, 1024], P(None, None, 'mp')
- head_scale_grad: float32 [2, 16], replicated
- out_weight_grad: float32 [2, 1024, 1024], P(None, 'mp')
- out_bias_grad: float32 [2, 1024], replicated
- ln_post_gain_grad: float32 [2, 1024], replicated
- ln_post_bias_grad: float32 [2, 1024], replicated
- ln_ffn_gain_grad: float32 [2, 1024], replicated
- ln_ffn_bias_grad: float32 [2, 1024], replicated
- fc1_weight_grad: float32 [2, 1024, 4096], P(None, None, 'mp')
- fc1_bias_grad: float32 [2, 4096], P(None, 'mp')
- mid_gain_grad: float32 [2, 4096], P(None, 'mp')
- mid_bias_grad: float32 [2, 4096], P(None, 'mp')
- fc2_weight_grad: float32 [2, 4096, 1024], P(None, 'mp')
- fc2_bias_grad: float32 [2, 1024], replicated
The draws below stay inside these ranges and needn't reach their ends.
Inputs may be any that keep to these rules, and one draw needn't show every extreme that they name: `segment_ids`: ids restart at 0 in every aligned group of 2048 tokens and never fall within it; in each group document 0 holds more than 1792 tokens and documents 1 to 3 lie in the group's last 256 tokens.
All inputs are finite; a program needn't handle non-finite values.
Results may differ from the reference program's by a relative error of at most 0.022.
Values may be sent and summed in bfloat16 or wider, within the bound.
A program may use at most 256 MiB of HBM per device.

```python
import jax
import jax.numpy as jnp
from jax import lax

D = 1024
HEADS = 16
FF = 4096
LAYERS = 2
TOK_GRP = 2048
TOK_DEV = 256
TOKENS = 8192


def draw_segment_ids(key, part):
    key = jax.random.fold_in(key, 11)
    first_key, second_key, third_key = jax.random.split(key, 3)
    groups = TOKENS // TOK_GRP
    tail_rows = 3 + jax.random.randint(first_key, (groups, 1), 0, TOK_DEV - 3)
    first_cut = 1 + jax.random.randint(second_key, (groups, 1), 0, 1 << 20) % (tail_rows - 2)
    second_cut = first_cut + 1 + jax.random.randint(third_key, (groups, 1), 0, 1 << 20) % (tail_rows - 1 - first_cut)
    positions = jnp.arange(TOK_GRP, dtype=jnp.int32)[None, :]
    begin = TOK_GRP - tail_rows
    doc_ids = (positions >= begin).astype(jnp.int32)
    doc_ids = doc_ids + (positions >= begin + first_cut).astype(jnp.int32)
    doc_ids = doc_ids + (positions >= begin + second_cut).astype(jnp.int32)
    return doc_ids.reshape(TOKENS).astype(jnp.int32)


def shard_levels(own_key, extent, shards, smallest, high):
    factor_of, own = 1.0, jax.random.fold_in(own_key, 6)
    for axis_at, blocks in shards:
        steps = jnp.exp(jax.random.uniform(jax.random.fold_in(own, axis_at), (blocks,), jnp.float32, smallest / len(shards), high / len(shards)))
        factor_of = factor_of * jnp.repeat(steps, extent[axis_at] // blocks).reshape([-1 if axis == axis_at else 1 for axis in range(len(extent))])
    return factor_of


def normal_values(own_key, extent, scale, reach, shards=(), kind=jnp.bfloat16):
    array = scale * jax.random.normal(own_key, extent, jnp.float32)
    if shards:
        array = array * shard_levels(own_key, extent, shards, -0.22, 0.18)
    return jnp.clip(array, -reach, reach).astype(kind)


def setup_inputs(seed: int = 0) -> dict:
    streams_of = jax.random.split(jax.random.key(seed), 21)
    tokens = normal_values(streams_of[0], (TOKENS, D), 1.0, 6.0, ((0, 32),))
    segment_ids = draw_segment_ids(jax.random.fold_in(streams_of[20], 71), 0)
    cotangent = normal_values(streams_of[2], (TOKENS, D), 1.0, 6.0, ((0, 32),))
    ln_attn_gain = jnp.clip(1.0 + 0.15 * jax.random.normal(streams_of[3], (LAYERS, D), jnp.float32), 0.25, 1.75)
    ln_attn_bias = normal_values(streams_of[4], (LAYERS, D), 0.3, 4.0, (), jnp.float32)
    qkv_weight = normal_values(streams_of[5], (LAYERS, D, 3, D), D ** -0.5, 0.1875, ((3, 8),))
    qv_bias = normal_values(streams_of[6], (LAYERS, 2, D), 0.3, 4.0, ((2, 8),), jnp.float32)
    head_scale = jnp.clip(1.0 + 0.15 * jax.random.normal(streams_of[7], (LAYERS, HEADS), jnp.float32), 0.25, 1.75)
    out_weight = normal_values(streams_of[8], (LAYERS, D, D), D ** -0.5, 0.1875, ((1, 8),))
    out_bias = normal_values(streams_of[9], (LAYERS, D), 0.3, 4.0, (), jnp.float32)
    ln_post_gain = jnp.clip(1.0 + 0.15 * jax.random.normal(streams_of[10], (LAYERS, D), jnp.float32), 0.25, 1.75)
    ln_post_bias = normal_values(streams_of[11], (LAYERS, D), 0.3, 4.0, (), jnp.float32)
    ln_ffn_gain = jnp.clip(1.0 + 0.15 * jax.random.normal(streams_of[12], (LAYERS, D), jnp.float32), 0.25, 1.75)
    ln_ffn_bias = normal_values(streams_of[13], (LAYERS, D), 0.3, 4.0, (), jnp.float32)
    fc1_weight = normal_values(streams_of[14], (LAYERS, D, FF), D ** -0.5, 0.1875, ((2, 8),))
    fc1_bias = normal_values(streams_of[15], (LAYERS, FF), 0.3, 4.0, ((1, 8),), jnp.float32)
    mid_gain = jnp.clip(1.0 + 0.15 * jax.random.normal(streams_of[16], (LAYERS, FF), jnp.float32), 0.25, 1.75)
    mid_bias = normal_values(streams_of[17], (LAYERS, FF), 0.3, 4.0, ((1, 8),), jnp.float32)
    fc2_weight = normal_values(streams_of[18], (LAYERS, FF, D), FF ** -0.5, 0.09375, ((1, 8),))
    fc2_bias = normal_values(streams_of[19], (LAYERS, D), 0.3, 4.0, (), jnp.float32)
    return dict(tokens=tokens, segment_ids=segment_ids, cotangent=cotangent, ln_attn_gain=ln_attn_gain, ln_attn_bias=ln_attn_bias, qkv_weight=qkv_weight, qv_bias=qv_bias, head_scale=head_scale, out_weight=out_weight, out_bias=out_bias, ln_post_gain=ln_post_gain, ln_post_bias=ln_post_bias, ln_ffn_gain=ln_ffn_gain, ln_ffn_bias=ln_ffn_bias, fc1_weight=fc1_weight, fc1_bias=fc1_bias, mid_gain=mid_gain, mid_bias=mid_bias, fc2_weight=fc2_weight, fc2_bias=fc2_bias)


epsilon = 1e-05
masked = -1e+30
highest = lax.Precision.HIGHEST

@jax.custom_vjp
def low(v):
    return lax.optimization_barrier(v.astype(jnp.bfloat16)).astype(jnp.float32)

@jax.custom_vjp
def low_back(v):
    return v

def low_keep(v):
    return (low(v), None)

def low_pass(kept, grad):
    return (grad,)

def back_keep(v):
    return (v, None)

def back_low(kept, grad):
    return (low(grad),)
low.defvjp(low_keep, low_pass)
low_back.defvjp(back_keep, back_low)

def norm_rows(values, gain_row, bias_row):
    average = lax.optimization_barrier(jnp.mean(values, axis=-1, keepdims=True))
    centered = values - average
    spread = lax.optimization_barrier(jnp.mean(centered * centered, axis=-1, keepdims=True))
    return centered * lax.rsqrt(spread + epsilon) * gain_row + bias_row

def norm_hidden(values, gain_row, bias_row):
    average = lax.optimization_barrier(jnp.mean(values, axis=-1, keepdims=True))
    spread = lax.optimization_barrier(jnp.mean(values * values, axis=-1, keepdims=True)) - average * average
    return (values - average) * lax.rsqrt(spread + epsilon) * gain_row + bias_row

def attend_group(queries, key_rows, value_rows, doc_rows):
    total_rows = queries.shape[0]
    block_rows = min(512, total_rows)
    positions = jnp.arange(total_rows, dtype=jnp.int32)
    factor = queries.shape[-1] ** (-0.5)

    def one_block(first_row):
        query_block = lax.dynamic_slice_in_dim(queries, first_row, block_rows, 0)
        scores = jnp.einsum('qhe,khe->hqk', query_block, key_rows, precision=highest) * factor
        scores = low_back(scores)
        query_place = first_row + jnp.arange(block_rows, dtype=jnp.int32)
        query_docs = lax.dynamic_slice_in_dim(doc_rows, first_row, block_rows, 0)
        allowed = (query_docs[:, None] == doc_rows[None, :]) & (query_place[:, None] >= positions[None, :])
        scores = jnp.where(allowed[None], scores, masked)
        probabilities = low(jax.nn.softmax(scores, axis=-1))
        return jnp.einsum('hqk,khe->qhe', probabilities, value_rows, precision=highest)
    starts = jnp.arange(total_rows // block_rows, dtype=jnp.int32) * block_rows
    return lax.map(jax.checkpoint(one_block), starts).reshape(queries.shape)

def layer_forward(residual, doc_groups, params):
    attn_gain, attn_bias, qkv_matrix, bias_pair, scale_heads, out_matrix, out_shift, post_gain, post_bias, ffn_gain, ffn_bias, first_matrix, first_shift, hidden_gain, hidden_bias, second_matrix, second_shift = params
    rows_all = residual.shape[0]
    model_width = residual.shape[1]
    heads_all = scale_heads.shape[0]
    head_width = model_width // heads_all
    groups = doc_groups.shape[0]
    group_rows = doc_groups.shape[1]
    attn_in = low(norm_rows(residual, attn_gain, attn_bias))
    projected = jnp.dot(attn_in, qkv_matrix.reshape(model_width, 3 * model_width), precision=highest)
    projected = projected.reshape(rows_all, 3, heads_all, head_width)
    bias_heads = bias_pair.reshape(2, heads_all, head_width)
    queries = low(low_back(projected[:, 0] + bias_heads[0]))
    key_rows = low(low_back(projected[:, 1]))
    value_rows = low(low_back(projected[:, 2] + bias_heads[1]))

    def per_group(members):
        return attend_group(members[0], members[1], members[2], members[3])
    grouped = (queries.reshape(groups, group_rows, heads_all, head_width), key_rows.reshape(groups, group_rows, heads_all, head_width), value_rows.reshape(groups, group_rows, heads_all, head_width), doc_groups)
    attended = lax.map(per_group, grouped).reshape(rows_all, heads_all, head_width)
    attended = low_back(attended)
    scaled = low((attended * scale_heads[None, :, None]).reshape(rows_all, model_width))
    branch = low_back(jnp.dot(scaled, out_matrix, precision=highest)) + out_shift
    middle = residual + norm_rows(branch, post_gain, post_bias)
    ffn_in = low(norm_rows(middle, ffn_gain, ffn_bias))
    before = low_back(jnp.dot(ffn_in, first_matrix, precision=highest) + first_shift)
    activated = jax.nn.gelu(before, approximate=False)
    mixed_rows = low(norm_hidden(activated, hidden_gain, hidden_bias))
    return middle + low_back(jnp.dot(mixed_rows, second_matrix, precision=highest)) + second_shift

def reference(tokens, segment_ids, cotangent, ln_attn_gain, ln_attn_bias, qkv_weight, qv_bias, head_scale, out_weight, out_bias, ln_post_gain, ln_post_bias, ln_ffn_gain, ln_ffn_bias, fc1_weight, fc1_bias, mid_gain, mid_bias, fc2_weight, fc2_bias):
    params = (ln_attn_gain.astype(jnp.float32), ln_attn_bias.astype(jnp.float32), qkv_weight.astype(jnp.float32), qv_bias.astype(jnp.float32), head_scale.astype(jnp.float32), out_weight.astype(jnp.float32), out_bias.astype(jnp.float32), ln_post_gain.astype(jnp.float32), ln_post_bias.astype(jnp.float32), ln_ffn_gain.astype(jnp.float32), ln_ffn_bias.astype(jnp.float32), fc1_weight.astype(jnp.float32), fc1_bias.astype(jnp.float32), mid_gain.astype(jnp.float32), mid_bias.astype(jnp.float32), fc2_weight.astype(jnp.float32), fc2_bias.astype(jnp.float32))
    doc_groups = segment_ids.reshape(-1, TOK_GRP)

    def forward(inputs, weights):
        residual = inputs
        for layer_index in range(LAYERS):
            residual = layer_forward(residual, doc_groups, tuple((member[layer_index] for member in weights)))
        return residual
    result, pullback = jax.vjp(forward, tokens.astype(jnp.float32), params)
    input_grad, weight_grads = pullback(cotangent.astype(jnp.float32))
    return (result.astype(jnp.bfloat16), input_grad, weight_grads[0], weight_grads[1], weight_grads[2], weight_grads[3], weight_grads[4], weight_grads[5], weight_grads[6], weight_grads[7], weight_grads[8], weight_grads[9], weight_grads[10], weight_grads[11], weight_grads[12], weight_grads[13], weight_grads[14], weight_grads[15], weight_grads[16])
```

```python
from functools import partial

import jax
import jax.numpy as jnp
from jax import lax
from jax.experimental import pallas as pl
from jax.experimental.pallas import tpu as pltpu
from jax.sharding import Mesh
from jax.sharding import PartitionSpec as P

epsilon = 1e-05
masked = -1e30


def partner(shard, axis, stride):
    return lax.ppermute(shard, axis, [(i, i ^ 1 << stride) for i in range(lax.axis_size(axis))])


def norm_local(values, gain_row, bias_row):
    average = jnp.mean(values, axis=-1, keepdims=True)
    centered = values - average
    spread = jnp.mean(centered * centered, axis=-1, keepdims=True)
    factor = lax.rsqrt(spread + epsilon)
    normal = centered * factor
    return (normal * gain_row + bias_row, normal, factor)


def norm_back(grad_out, normal, factor, gain_row):
    scaled = grad_out * gain_row
    inner_sum = jnp.mean(scaled * normal, axis=-1, keepdims=True)
    return factor * (scaled - jnp.mean(scaled, axis=-1, keepdims=True) - normal * inner_sum)


def collect_rows(normed_b):
    return lax.all_gather(normed_b, "mp", axis=0, tiled=True)


def collect_grads(gradient_b):
    return lax.all_gather(gradient_b, "mp", axis=0, tiled=True)


def reduce_branch(operand_b, weight_b, local_rows):

    def partial_term(first_row, count):
        return jnp.dot(operand_b, weight_b, preferred_element_type=jnp.float32)

    return lax.psum_scatter(
        partial_term(jnp.int32(0), local_rows * lax.axis_size("mp")).astype(jnp.bfloat16),
        "mp",
        scatter_dimension=0,
        tiled=True,
    ).astype(jnp.float32)


def reduce_grads(operand_b, weight_b, local_rows):

    def partial_term(first_row, count):
        return jnp.einsum("tc,dc->td", operand_b, weight_b, preferred_element_type=jnp.float32)

    return lax.psum_scatter(
        partial_term(jnp.int32(0), local_rows * lax.axis_size("mp")).astype(jnp.bfloat16),
        "mp",
        scatter_dimension=0,
        tiled=True,
    ).astype(jnp.float32)


def hidden_stats(first_sum, second_sum):
    return lax.psum((first_sum, second_sum), "mp")


def hidden_grad_stats(first_sum, second_sum):
    return lax.psum((first_sum, second_sum), "mp")


def join_cols(mine, other, is_upper):
    lower_part = jnp.where(is_upper, other, mine)
    upper_part = jnp.where(is_upper, mine, other)
    return jnp.concatenate([lower_part, upper_part], axis=-1)


def join_rows(mine, other, is_upper):
    lower_part = jnp.where(is_upper, other, mine)
    upper_part = jnp.where(is_upper, mine, other)
    return jnp.concatenate([lower_part, upper_part], axis=0)


def split_cols(values, cols_here, is_upper):
    lower_part = values[..., :cols_here]
    upper_part = values[..., cols_here:]
    return (
        jnp.where(is_upper, upper_part, lower_part),
        jnp.where(is_upper, lower_part, upper_part),
    )


def masked_scores(query_block, key_rows, query_start, block_rows, doc_rows, positions):
    factor = query_block.shape[-1] ** (-0.5)
    scores = (
        jnp.einsum("qhe,khe->hqk", query_block, key_rows, preferred_element_type=jnp.float32)
        * factor
    )
    query_place = query_start + jnp.arange(block_rows, dtype=jnp.int32)
    query_docs = lax.dynamic_slice_in_dim(doc_rows, query_start, block_rows, 0)
    allowed = (query_docs[:, None] == doc_rows[None, :]) & (
        query_place[:, None] >= positions[None, :]
    )
    return jnp.where(allowed[None], scores, masked)


def attend_forward(queries, key_rows, value_rows, doc_rows, row_offset):
    total_rows = queries.shape[0]
    block_rows = min(512, total_rows)
    positions = jnp.arange(key_rows.shape[0], dtype=jnp.int32)

    def one_block(first_row):
        query_block = lax.dynamic_slice_in_dim(queries, first_row, block_rows, 0)
        scores = masked_scores(
            query_block, key_rows, row_offset + first_row, block_rows, doc_rows, positions
        )
        row_peak = jnp.max(scores, axis=-1, keepdims=True)
        weights = jnp.exp(scores - row_peak)
        totals = jnp.sum(weights, axis=-1, keepdims=True)
        probabilities = (weights / totals).astype(jnp.bfloat16)
        output = jnp.einsum(
            "hqk,khe->qhe", probabilities, value_rows, preferred_element_type=jnp.float32
        )
        return (output, (row_peak + jnp.log(totals))[..., 0])

    starts = jnp.arange(total_rows // block_rows, dtype=jnp.int32) * block_rows
    outputs, log_totals = lax.map(one_block, starts)
    return (outputs.reshape(queries.shape), log_totals)


def attend_backward(queries, key_rows, value_rows, doc_rows, row_offset, log_totals, grad_out):
    total_rows = queries.shape[0]
    block_rows = min(512, total_rows)
    positions = jnp.arange(key_rows.shape[0], dtype=jnp.int32)
    factor = queries.shape[-1] ** (-0.5)

    def one_block(running, first_row):
        key_grad, value_grad = running
        query_block = lax.dynamic_slice_in_dim(queries, first_row, block_rows, 0)
        grad_block = lax.dynamic_slice_in_dim(grad_out, first_row, block_rows, 0)
        scores = masked_scores(
            query_block, key_rows, row_offset + first_row, block_rows, doc_rows, positions
        )
        block_totals = lax.dynamic_index_in_dim(
            log_totals, first_row // block_rows, 0, keepdims=False
        )
        probabilities = jnp.exp(scores - block_totals[..., None])
        prob_grad = jnp.einsum(
            "qhe,khe->hqk", grad_block, value_rows, preferred_element_type=jnp.float32
        )
        inner_sum = jnp.sum(probabilities * prob_grad, axis=-1, keepdims=True)
        score_grad = (probabilities * (prob_grad - inner_sum)).astype(jnp.bfloat16)
        query_grad = (
            jnp.einsum("hqk,khe->qhe", score_grad, key_rows, preferred_element_type=jnp.float32)
            * factor
        )
        key_grad = (
            key_grad
            + jnp.einsum(
                "hqk,qhe->khe", score_grad, query_block, preferred_element_type=jnp.float32
            )
            * factor
        )
        value_grad = value_grad + jnp.einsum(
            "hqk,qhe->khe",
            probabilities.astype(jnp.bfloat16),
            grad_block,
            preferred_element_type=jnp.float32,
        )
        return ((key_grad, value_grad), query_grad)

    starts = jnp.arange(total_rows // block_rows, dtype=jnp.int32) * block_rows
    zero_grads = jnp.zeros(key_rows.shape, jnp.float32)
    (key_grad, value_grad), query_grads = lax.scan(one_block, (zero_grads, zero_grads), starts)
    return (query_grads.reshape(queries.shape), key_grad, value_grad)


def stack_layers(layer_list, members):
    stacked = []
    for member_index in range(members):
        stacked.append(jnp.stack([entry[member_index] for entry in layer_list], axis=0))
    return stacked


def per_device(
    tokens,
    segment_ids,
    cotangent,
    ln_attn_gain,
    ln_attn_bias,
    qkv_weight,
    qv_bias,
    head_scale,
    out_weight,
    out_bias,
    ln_post_gain,
    ln_post_bias,
    ln_ffn_gain,
    ln_ffn_bias,
    fc1_weight,
    fc1_bias,
    mid_gain,
    mid_bias,
    fc2_weight,
    fc2_bias,
):
    layers = qkv_weight.shape[0]
    local_rows = tokens.shape[0]
    model_width = tokens.shape[1]
    cols_here = qkv_weight.shape[3]
    heads_all = head_scale.shape[1]
    head_width = model_width // heads_all
    pair_cols = 2 * cols_here
    pair_heads = pair_cols // head_width
    group_rows = segment_ids.shape[0]
    half_rows = group_rows // 2
    hidden_all = fc1_weight.shape[2] * lax.axis_size("mp")
    device_index = lax.axis_index("mp")
    is_upper = device_index % 2 == 1
    own_start = jnp.where(is_upper, half_rows, 0).astype(jnp.int32)
    other_start = jnp.where(is_upper, 0, half_rows).astype(jnp.int32)
    first_head = device_index // 2 * pair_heads
    pair_onehot = (
        (first_head + jnp.arange(pair_heads, dtype=jnp.int32))[:, None]
        == jnp.arange(heads_all, dtype=jnp.int32)[None, :]
    ).astype(jnp.float32)
    residual = tokens.astype(jnp.float32)
    stored = []
    for layer_index in range(layers):
        attn_in, attn_normal, attn_factor = norm_local(
            residual, ln_attn_gain[layer_index], ln_attn_bias[layer_index]
        )
        attn_rows = collect_rows(attn_in.astype(jnp.bfloat16))
        qkv_here = qkv_weight[layer_index].reshape(model_width, 3 * cols_here)
        projected = jnp.dot(attn_rows, qkv_here, preferred_element_type=jnp.float32).reshape(
            -1, 3, cols_here
        )
        bias_pair = qv_bias[layer_index]
        query_mine = (projected[:, 0] + bias_pair[0]).astype(jnp.bfloat16)
        key_mine = projected[:, 1].astype(jnp.bfloat16)
        value_mine = (projected[:, 2] + bias_pair[1]).astype(jnp.bfloat16)
        query_send = lax.dynamic_slice_in_dim(query_mine, other_start, half_rows, 0)
        query_recv, key_recv, value_recv = partner((query_send, key_mine, value_mine), "mp", 0)
        query_own = lax.dynamic_slice_in_dim(query_mine, own_start, half_rows, 0)
        queries = join_cols(query_own, query_recv, is_upper).reshape(
            half_rows, pair_heads, head_width
        )
        key_rows = join_cols(key_mine, key_recv, is_upper).reshape(
            group_rows, pair_heads, head_width
        )
        value_rows = join_cols(value_mine, value_recv, is_upper).reshape(
            group_rows, pair_heads, head_width
        )
        attended, log_totals = attend_forward(queries, key_rows, value_rows, segment_ids, own_start)
        pair_scale = jnp.sum(pair_onehot * head_scale[layer_index][None, :], axis=1)
        scaled_half = (
            (attended * pair_scale[None, :, None])
            .astype(jnp.bfloat16)
            .reshape(half_rows, pair_cols)
        )
        own_cols, other_cols = split_cols(scaled_half, cols_here, is_upper)
        scaled_recv = partner(other_cols, "mp", 0)
        scaled_mine = join_rows(own_cols, scaled_recv, is_upper)
        branch = (
            reduce_branch(scaled_mine, out_weight[layer_index], local_rows) + out_bias[layer_index]
        )
        post_out, post_normal, post_factor = norm_local(
            branch, ln_post_gain[layer_index], ln_post_bias[layer_index]
        )
        middle = residual + post_out
        ffn_in, ffn_normal, ffn_factor = norm_local(
            middle, ln_ffn_gain[layer_index], ln_ffn_bias[layer_index]
        )
        ffn_rows = collect_rows(ffn_in.astype(jnp.bfloat16))
        before_gelu = (
            jnp.dot(ffn_rows, fc1_weight[layer_index], preferred_element_type=jnp.float32)
            + fc1_bias[layer_index]
        )
        activated = jax.nn.gelu(before_gelu, approximate=False)
        first_sum, second_sum = hidden_stats(
            jnp.sum(activated, axis=1), jnp.sum(activated * activated, axis=1)
        )
        average = first_sum / hidden_all
        spread = second_sum / hidden_all - average * average
        hidden_factor = lax.rsqrt(spread + epsilon)[:, None]
        hidden_normal = (activated - average[:, None]) * hidden_factor
        mixed_b = (hidden_normal * mid_gain[layer_index] + mid_bias[layer_index]).astype(
            jnp.bfloat16
        )
        ffn_out = reduce_branch(mixed_b, fc2_weight[layer_index], local_rows)
        stored.append(
            (
                attn_normal,
                attn_factor,
                attn_rows,
                queries,
                key_rows,
                value_rows,
                attended,
                log_totals,
                pair_scale,
                scaled_mine,
                post_normal,
                post_factor,
                ffn_normal,
                ffn_factor,
                ffn_rows,
                before_gelu,
                hidden_normal,
                hidden_factor,
                mixed_b,
            )
        )
        residual = middle + ffn_out + fc2_bias[layer_index]
    layer_output = residual.astype(jnp.bfloat16)
    gradient = cotangent.astype(jnp.float32)
    sharded_list = []
    shared_list = []
    for layer_index in reversed(range(layers)):
        (
            attn_normal,
            attn_factor,
            attn_rows,
            queries,
            key_rows,
            value_rows,
            attended,
            log_totals,
            pair_scale,
            scaled_mine,
            post_normal,
            post_factor,
            ffn_normal,
            ffn_factor,
            ffn_rows,
            before_gelu,
            hidden_normal,
            hidden_factor,
            mixed_b,
        ) = stored[layer_index]
        qkv_here = qkv_weight[layer_index].reshape(model_width, 3 * cols_here)
        second_shift_grad = jnp.sum(gradient, axis=0)
        grad_rows = collect_grads(gradient.astype(jnp.bfloat16))
        mixed_grad = jnp.einsum(
            "td,fd->tf", grad_rows, fc2_weight[layer_index], preferred_element_type=jnp.float32
        )
        second_grad = jnp.einsum(
            "tf,td->fd", mixed_b, grad_rows, preferred_element_type=jnp.float32
        )
        hidden_gain_grad = jnp.sum(mixed_grad * hidden_normal, axis=0)
        hidden_shift_grad = jnp.sum(mixed_grad, axis=0)
        normal_grad = mixed_grad * mid_gain[layer_index]
        grad_first, grad_second = hidden_grad_stats(
            jnp.sum(normal_grad, axis=1), jnp.sum(normal_grad * hidden_normal, axis=1)
        )
        active_grad = hidden_factor * (
            normal_grad
            - grad_first[:, None] / hidden_all
            - hidden_normal * grad_second[:, None] / hidden_all
        )
        gelu_pull = jax.vjp(partial(jax.nn.gelu, approximate=False), before_gelu)[1]
        pre_grad_b = gelu_pull(active_grad)[0].astype(jnp.bfloat16)
        first_shift_grad = jnp.sum(pre_grad_b, axis=0, dtype=jnp.float32)
        first_grad = jnp.einsum(
            "td,tf->df", ffn_rows, pre_grad_b, preferred_element_type=jnp.float32
        )
        ffn_in_grad = reduce_grads(pre_grad_b, fc1_weight[layer_index], local_rows)
        ffn_gain_grad = jnp.sum(ffn_in_grad * ffn_normal, axis=0)
        ffn_bias_grad = jnp.sum(ffn_in_grad, axis=0)
        middle_grad = gradient + norm_back(
            ffn_in_grad, ffn_normal, ffn_factor, ln_ffn_gain[layer_index]
        )
        post_gain_grad = jnp.sum(middle_grad * post_normal, axis=0)
        post_bias_grad = jnp.sum(middle_grad, axis=0)
        branch_grad = norm_back(middle_grad, post_normal, post_factor, ln_post_gain[layer_index])
        out_shift_grad = jnp.sum(branch_grad, axis=0)
        branch_rows = collect_grads(branch_grad.astype(jnp.bfloat16))
        scaled_grad = jnp.einsum(
            "td,cd->tc", branch_rows, out_weight[layer_index], preferred_element_type=jnp.float32
        )
        out_grad = jnp.einsum(
            "tc,td->cd", scaled_mine, branch_rows, preferred_element_type=jnp.float32
        )
        grad_send = lax.dynamic_slice_in_dim(scaled_grad, other_start, half_rows, 0)
        grad_recv = partner(grad_send.astype(jnp.bfloat16), "mp", 0).astype(grad_send.dtype)
        grad_own = lax.dynamic_slice_in_dim(scaled_grad, own_start, half_rows, 0)
        scaled_pair = join_cols(grad_own, grad_recv, is_upper).reshape(
            half_rows, pair_heads, head_width
        )
        pair_scale_grad = jnp.sum(attended * scaled_pair, axis=(0, 2))
        scale_grad = jnp.sum(pair_onehot * pair_scale_grad[:, None], axis=0)
        attended_grad_b = (scaled_pair * pair_scale[None, :, None]).astype(jnp.bfloat16)
        query_grad, key_grad, value_grad = attend_backward(
            queries, key_rows, value_rows, segment_ids, own_start, log_totals, attended_grad_b
        )
        query_own, query_other = split_cols(
            query_grad.reshape(half_rows, pair_cols), cols_here, is_upper
        )
        key_own, key_other = split_cols(
            key_grad.reshape(group_rows, pair_cols), cols_here, is_upper
        )
        value_own, value_other = split_cols(
            value_grad.reshape(group_rows, pair_cols), cols_here, is_upper
        )
        query_recv, key_recv, value_recv = (
            partner(query_other.astype(jnp.bfloat16), "mp", 0).astype(query_other.dtype),
            partner(key_other.astype(jnp.bfloat16), "mp", 0).astype(key_other.dtype),
            partner(value_other.astype(jnp.bfloat16), "mp", 0).astype(value_other.dtype),
        )
        query_grad_b = join_rows(query_own, query_recv, is_upper).astype(jnp.bfloat16)
        key_grad_b = (key_own + key_recv).astype(jnp.bfloat16)
        value_grad_b = (value_own + value_recv).astype(jnp.bfloat16)
        proj_grad = jnp.stack([query_grad_b, key_grad_b, value_grad_b], axis=1).reshape(
            -1, 3 * cols_here
        )
        pair_grad = jnp.stack(
            [
                jnp.sum(query_grad_b, axis=0, dtype=jnp.float32),
                jnp.sum(value_grad_b, axis=0, dtype=jnp.float32),
            ],
            axis=0,
        )
        qkv_grad = jnp.einsum(
            "td,tc->dc", attn_rows, proj_grad, preferred_element_type=jnp.float32
        ).reshape(model_width, 3, cols_here)
        attn_in_grad = reduce_grads(proj_grad, qkv_here, local_rows)
        attn_gain_grad = jnp.sum(attn_in_grad * attn_normal, axis=0)
        attn_bias_grad = jnp.sum(attn_in_grad, axis=0)
        gradient = middle_grad + norm_back(
            attn_in_grad, attn_normal, attn_factor, ln_attn_gain[layer_index]
        )
        sharded_list.insert(
            0,
            (
                qkv_grad,
                pair_grad,
                out_grad,
                first_grad,
                first_shift_grad,
                hidden_gain_grad,
                hidden_shift_grad,
                second_grad,
            ),
        )
        shared_list.insert(
            0,
            (
                attn_gain_grad,
                attn_bias_grad,
                scale_grad,
                out_shift_grad,
                post_gain_grad,
                post_bias_grad,
                ffn_gain_grad,
                ffn_bias_grad,
                second_shift_grad,
            ),
        )
    sharded = stack_layers(sharded_list, 8)
    shared = stack_layers(shared_list, 9)
    sharded = (
        lax.psum(sharded[0].astype(jnp.bfloat16), "rows").astype(jnp.float32),
        lax.psum(sharded[1].astype(jnp.bfloat16), "rows").astype(jnp.float32),
        lax.psum(sharded[2].astype(jnp.bfloat16), "rows").astype(jnp.float32),
        lax.psum(sharded[3].astype(jnp.bfloat16), "rows").astype(jnp.float32),
        lax.psum(sharded[4].astype(jnp.bfloat16), "rows").astype(jnp.float32),
        lax.psum(sharded[5].astype(jnp.bfloat16), "rows").astype(jnp.float32),
        lax.psum(sharded[6].astype(jnp.bfloat16), "rows").astype(jnp.float32),
        lax.psum(sharded[7].astype(jnp.bfloat16), "rows").astype(jnp.float32),
    )
    shared = lax.psum(
        (
            shared[0],
            shared[1],
            shared[2],
            shared[3],
            shared[4],
            shared[5],
            shared[6],
            shared[7],
            shared[8],
        ),
        ("rows", "mp"),
    )
    return (
        layer_output,
        gradient,
        shared[0],
        shared[1],
        sharded[0],
        sharded[1],
        shared[2],
        sharded[2],
        shared[3],
        shared[4],
        shared[5],
        shared[6],
        shared[7],
        sharded[3],
        sharded[4],
        sharded[5],
        sharded[6],
        sharded[7],
        shared[8],
    )


MESH_ID = pl.DeviceIdType.MESH
PLANE = ("core", "y", "x")
EVERY = ("y", "core", "z", "x")
f32 = jnp.float32
bf16 = jnp.bfloat16


def vmem_params(collective_id=None, mib=48):
    if collective_id is None:
        return pltpu.CompilerParams(vmem_limit_bytes=mib * 2**20)
    return pltpu.CompilerParams(
        vmem_limit_bytes=mib * 2**20, collective_id=collective_id, has_side_effects=True
    )


def plane_pairs():
    pairs = []
    for y in range(2):
        for core in range(2):
            for z in range(4):
                for x in range(2):
                    source = ((y * 2 + core) * 4 + z) * 2 + x
                    target = (((z % 2) * 2 + z // 2) * 4 + (2 * y + core)) * 2 + x
                    pairs.append((source, target))
    return pairs


def to_plane(values):
    return lax.ppermute(values, EVERY, plane_pairs())


def from_plane(values):
    return lax.ppermute(values, EVERY, [(target, source) for source, target in plane_pairs()])


def greet(peers):
    barrier = pltpu.get_barrier_semaphore()
    for peer in peers:
        pl.semaphore_signal(barrier, inc=1, device_id=peer, device_id_type=MESH_ID)
    pl.semaphore_wait(barrier, len(peers))


def gather_kernel(x_ref, o_ref, send_sem, recv_sem, own_sem):
    rows = x_ref.shape[0]
    half = rows // 2
    x, y, core = lax.axis_index("x"), lax.axis_index("y"), lax.axis_index("core")
    to_x, to_y, to_core = {"x": 1 - x}, {"y": 1 - y}, {"core": 1 - core}
    greet((to_x, to_y, to_core))

    def place(at_x, at_y, part=None):
        first = ((2 * core + at_y) * 2 + at_x) * rows
        if part is None:
            return o_ref.at[pl.ds(pl.multiple_of(first, rows), rows)]
        return o_ref.at[pl.ds(pl.multiple_of(first + part * half, half), half)]

    def copy(index, source, target, peer):
        return pltpu.make_async_remote_copy(
            src_ref=source,
            dst_ref=target,
            send_sem=send_sem.at[index],
            recv_sem=recv_sem.at[index],
            device_id=peer,
            device_id_type=MESH_ID,
        )

    own = place(x, y)
    copy_0 = copy(0, x_ref, own, to_x)
    copy_1 = copy(1, x_ref, own, to_y)
    copy_2 = copy(2, x_ref, own, to_core)
    copy_0.start()
    copy_1.start()
    copy_2.start()
    keep = pltpu.make_async_copy(x_ref, own, own_sem)
    keep.start()
    copy_0.wait_recv()
    copy_4 = copy(4, place(1 - x, y, 0), place(1 - x, y, 0), to_y)
    copy_3 = copy(3, place(1 - x, y), place(1 - x, y), to_core)
    copy_4.start()
    copy_3.start()
    copy_1.wait_recv()
    copy_6 = copy(6, place(x, 1 - y, 1), place(x, 1 - y, 1), to_x)
    copy_5 = copy(5, place(x, 1 - y), place(x, 1 - y), to_core)
    copy_6.start()
    copy_5.start()
    copy_4.wait_recv()
    copy_7 = copy(7, place(1 - x, 1 - y, 0), place(1 - x, 1 - y, 0), to_core)
    copy_7.start()
    copy_6.wait_recv()
    copy_8 = copy(8, place(1 - x, 1 - y, 1), place(1 - x, 1 - y, 1), to_core)
    copy_8.start()
    for arriving in (copy_2, copy_3, copy_5, copy_7, copy_8):
        arriving.wait_recv()
    for sent in (copy_0, copy_1, copy_2, copy_3, copy_4, copy_5, copy_6, copy_7, copy_8):
        sent.wait_send()
    keep.wait()


def plane_gather(block_b):
    rows, width = block_b.shape
    return pl.pallas_call(
        gather_kernel,
        out_shape=jax.ShapeDtypeStruct((8 * rows, width), block_b.dtype),
        in_specs=[pl.BlockSpec(memory_space=pltpu.VMEM)],
        out_specs=pl.BlockSpec(memory_space=pltpu.VMEM),
        scratch_shapes=[
            pltpu.SemaphoreType.DMA((9,)),
            pltpu.SemaphoreType.DMA((9,)),
            pltpu.SemaphoreType.DMA,
        ],
        compiler_params=vmem_params(1),
    )(block_b)


def scatter_kernel(
    weight_dim,
    a_ref,
    w_ref,
    o_ref,
    sib_out,
    sib_in,
    diag_out,
    diag_in,
    last_x_out,
    last_y_out,
    last_x_in,
    last_y_in,
    wait_x,
    wait_y,
    send_sem,
    recv_sem,
):
    rows = o_ref.shape[0]
    half = rows // 2
    x, y, core = lax.axis_index("x"), lax.axis_index("y"), lax.axis_index("core")
    to_x, to_y, to_core = {"x": 1 - x}, {"y": 1 - y}, {"core": 1 - core}
    greet((to_x, to_y, to_core))

    def term(at_core, at_x, at_y):
        first = pl.multiple_of(((2 * at_core + at_y) * 2 + at_x) * rows, rows)
        return lax.dot_general(
            a_ref[pl.ds(first, rows), :],
            w_ref[...],
            (((1,), (weight_dim,)), ((), ())),
            preferred_element_type=f32,
        )

    def copy(index, source, target, peer):
        return pltpu.make_async_remote_copy(
            src_ref=source,
            dst_ref=target,
            send_sem=send_sem.at[index],
            recv_sem=recv_sem.at[index],
            device_id=peer,
            device_id_type=MESH_ID,
        )

    places = ((1 - x, 1 - y), (1 - x, y), (x, 1 - y), (x, y))
    siblings = [copy(i, sib_out.at[i], sib_in.at[i], to_core) for i in range(4)]

    def help_sibling(i):
        sib_out[i] = term(1 - core, *places[i]).astype(bf16)
        siblings[i].start()

    def joined(i):
        mine = term(core, *places[i])
        siblings[i].wait_recv()
        return mine + sib_in[i].astype(f32)

    help_sibling(0)
    help_sibling(1)
    total = joined(0)
    diag_out[...] = total.astype(bf16)
    diag_x = copy(4, diag_out.at[pl.ds(0, half)], diag_in.at[0], to_x)
    diag_y = copy(5, diag_out.at[pl.ds(half, half)], diag_in.at[1], to_y)
    diag_x.start()
    diag_y.start()
    help_sibling(2)
    total = joined(1)
    last_x_out[0] = total[:half].astype(bf16)
    x_0 = copy(6, last_x_out.at[0], last_x_in.at[0], to_x)
    x_0.start()
    wait_x[...] = total[half:]
    help_sibling(3)
    total = joined(2)
    last_y_out[1] = total[half:].astype(bf16)
    y_1 = copy(7, last_y_out.at[1], last_y_in.at[1], to_y)
    y_1.start()
    wait_y[...] = total[:half]
    diag_y.wait_recv()
    last_x_out[1] = (wait_x[...] + diag_in[1].astype(f32)).astype(bf16)
    x_1 = copy(8, last_x_out.at[1], last_x_in.at[1], to_x)
    x_1.start()
    diag_x.wait_recv()
    last_y_out[0] = (wait_y[...] + diag_in[0].astype(f32)).astype(bf16)
    y_0 = copy(9, last_y_out.at[0], last_y_in.at[0], to_y)
    y_0.start()
    o_ref[...] = joined(3)
    x_0.wait_recv()
    y_1.wait_recv()
    x_1.wait_recv()
    y_0.wait_recv()
    for part in range(2):
        piece = pl.ds(part * half, half)
        o_ref[piece, :] += last_x_in[part].astype(f32) + last_y_in[part].astype(f32)
    for sent in (*siblings, diag_x, diag_y, x_0, y_1, x_1, y_0):
        sent.wait_send()


def plane_scatter(operand_b, weight_b, weight_dim, collective_id):
    rows = operand_b.shape[0] // 8
    half = rows // 2
    width = weight_b.shape[1 - weight_dim]
    return pl.pallas_call(
        partial(scatter_kernel, weight_dim),
        out_shape=jax.ShapeDtypeStruct((rows, width), f32),
        in_specs=[pl.BlockSpec(memory_space=pltpu.VMEM)] * 2,
        out_specs=pl.BlockSpec(memory_space=pltpu.VMEM),
        scratch_shapes=[
            pltpu.VMEM((4, rows, width), bf16),
            pltpu.VMEM((4, rows, width), bf16),
            pltpu.VMEM((rows, width), bf16),
            pltpu.VMEM((2, half, width), bf16),
            pltpu.VMEM((2, half, width), bf16),
            pltpu.VMEM((2, half, width), bf16),
            pltpu.VMEM((2, half, width), bf16),
            pltpu.VMEM((2, half, width), bf16),
            pltpu.VMEM((half, width), f32),
            pltpu.VMEM((half, width), f32),
            pltpu.SemaphoreType.DMA((10,)),
            pltpu.SemaphoreType.DMA((10,)),
        ],
        compiler_params=vmem_params(collective_id),
    )(operand_b, weight_b)


def plane_sum_kernel(v_ref, o_ref, got, send_sem, recv_sem):
    x, y, core = lax.axis_index("x"), lax.axis_index("y"), lax.axis_index("core")
    peers = []
    for flip in range(1, 8):
        at_x = 1 - x if flip & 1 else x
        at_y = 1 - y if flip & 2 else y
        at_core = 1 - core if flip & 4 else core
        peers.append({"x": at_x, "y": at_y, "core": at_core})
    greet(peers)
    me = (2 * core + y) * 2 + x
    copies = []
    for index, peer in enumerate(peers):
        copies.append(
            pltpu.make_async_remote_copy(
                src_ref=v_ref,
                dst_ref=got.at[index],
                send_sem=send_sem.at[index],
                recv_sem=recv_sem.at[index],
                device_id=peer,
                device_id_type=MESH_ID,
            )
        )
    for each in copies:
        each.start()
    for each in copies:
        each.wait_recv()
    by_x = [v_ref[...] + got[0]]
    for flip in (2, 4, 6):
        by_x.append(got[flip - 1] + got[flip])
    o_ref[...] = (by_x[0] + by_x[1]) + (by_x[2] + by_x[3])
    for each in copies:
        each.wait_send()


def plane_sum(values):
    return pl.pallas_call(
        plane_sum_kernel,
        out_shape=jax.ShapeDtypeStruct(values.shape, f32),
        in_specs=[pl.BlockSpec(memory_space=pltpu.VMEM)],
        out_specs=pl.BlockSpec(memory_space=pltpu.VMEM),
        scratch_shapes=[
            pltpu.VMEM((7, *values.shape), f32),
            pltpu.SemaphoreType.DMA((7,)),
            pltpu.SemaphoreType.DMA((7,)),
        ],
        compiler_params=vmem_params(6),
    )(values)


BLOCK = 256


def head_masks(head_width, width):
    lane = lax.broadcasted_iota(jnp.int32, (1, width), 1)
    lower = (lane < head_width).astype(bf16)
    return lower, (1 - lower).astype(bf16)


def attend_kernel(head_width, q_ref, k_ref, v_ref, dq_ref, dk_ref, o_ref, l_ref, s_buf, acc, top):
    block = pl.program_id(0)
    width = q_ref.shape[1]
    low_mask, high_mask = head_masks(head_width, width)
    q = q_ref[...]
    pair = jnp.concatenate([q * low_mask, q * high_mask], axis=0)
    top[...] = jnp.full_like(top, masked)

    def scores(at):
        keys = k_ref[pl.ds(pl.multiple_of(at * BLOCK, BLOCK), BLOCK), :]
        return lax.dot_general(pair, keys, (((1,), (1,)), ((), ())), preferred_element_type=f32)

    def first_pass(at, carry):
        s = scores(at)
        s_buf[at] = s
        top[...] = jnp.maximum(top[...], jnp.maximum(s[:, :128], s[:, 128:]))
        return carry

    lax.fori_loop(0, block, first_pass, 0)
    docs = dq_ref[...]
    docs = jnp.concatenate([docs, docs], axis=0)
    place = lax.broadcasted_iota(jnp.int32, (2 * BLOCK, BLOCK), 0)
    place = jnp.where(place >= BLOCK, place - BLOCK, place)
    allowed = (docs == dk_ref[...]) & (
        place >= lax.broadcasted_iota(jnp.int32, (2 * BLOCK, BLOCK), 1)
    )
    s = jnp.where(allowed, scores(block), masked)
    shift = jnp.where(docs == 0, 0.0, masked)
    peak = jnp.maximum(
        jnp.max(top[...], axis=1, keepdims=True) + shift, jnp.max(s, axis=1, keepdims=True)
    )
    p = jnp.exp(s - peak)
    top[...] = p[:, :128] + p[:, 128:]
    values = v_ref[pl.ds(pl.multiple_of(block * BLOCK, BLOCK), BLOCK), :]
    acc[...] = jnp.dot(p.astype(bf16), values, preferred_element_type=f32)
    base = peak - shift

    def second_pass(at, carry):
        p = jnp.exp(s_buf[at] - base)
        top[...] += p[:, :128] + p[:, 128:]
        values = v_ref[pl.ds(pl.multiple_of(at * BLOCK, BLOCK), BLOCK), :]
        acc[...] += jnp.dot(p.astype(bf16), values, preferred_element_type=f32)
        return carry

    lax.fori_loop(0, block, second_pass, 0)
    total = jnp.sum(top[...], axis=1, keepdims=True)
    out = acc[...] / total
    lane = lax.broadcasted_iota(jnp.int32, (BLOCK, width), 1)
    o_ref[...] = jnp.where(lane < head_width, out[:BLOCK], out[BLOCK:])
    logs = jnp.broadcast_to(peak + jnp.log(total), (2 * BLOCK, 128))
    l_ref[0] = jnp.transpose(logs)[0:1, :]


def attend_plane(q, k, v, doc_col, doc_row, head_width):
    rows, width = q.shape
    blocks = rows // BLOCK
    whole = pl.BlockSpec((rows, width), lambda i: (0, 0))
    part = pl.BlockSpec((BLOCK, width), lambda i: (i, 0))
    return pl.pallas_call(
        partial(attend_kernel, head_width),
        grid=(blocks,),
        out_shape=(
            jax.ShapeDtypeStruct((rows, width), f32),
            jax.ShapeDtypeStruct((blocks, 1, 2 * BLOCK), f32),
        ),
        in_specs=[
            part,
            whole,
            whole,
            pl.BlockSpec((BLOCK, 1), lambda i: (i, 0)),
            pl.BlockSpec((1, BLOCK), lambda i: (0, i)),
        ],
        out_specs=(part, pl.BlockSpec((1, 1, 2 * BLOCK), lambda i: (i, 0, 0))),
        scratch_shapes=[
            pltpu.VMEM((blocks, 2 * BLOCK, BLOCK), f32),
            pltpu.VMEM((2 * BLOCK, width), f32),
            pltpu.VMEM((2 * BLOCK, 128), f32),
        ],
        compiler_params=vmem_params(),
    )(q, k, v, doc_col, doc_row)


def attend_back_kernel(
    head_width,
    q_ref,
    k_ref,
    v_ref,
    do_ref,
    o_ref,
    l_ref,
    dcol_ref,
    drow_ref,
    gq_ref,
    gk_ref,
    gv_ref,
    acc_k,
    acc_v,
    acc_q,
):
    block = pl.program_id(0)
    width = q_ref.shape[1]
    low_mask, high_mask = head_masks(head_width, width)
    q = q_ref[...]
    pair_q = jnp.concatenate([q * low_mask, q * high_mask], axis=0)
    do = do_ref[...]
    pair_do = jnp.concatenate([do * low_mask, do * high_mask], axis=0)
    o = o_ref[...]
    inner = jnp.sum(
        jnp.concatenate([o, o], axis=0) * pair_do.astype(f32), axis=1, keepdims=True
    )
    inner = jnp.transpose(jnp.broadcast_to(inner, (2 * BLOCK, 128)))[0:1, :]
    logs = l_ref[0]
    docs = drow_ref[...]
    docs = jnp.concatenate([docs, docs], axis=1)

    @pl.when(block == 0)
    def _():
        acc_k[...] = jnp.zeros_like(acc_k)
        acc_v[...] = jnp.zeros_like(acc_v)

    def step(at, base, allowed):
        piece = pl.ds(pl.multiple_of(at * BLOCK, BLOCK), BLOCK)
        keys = k_ref[piece, :]
        s = lax.dot_general(keys, pair_q, (((1,), (1,)), ((), ())), preferred_element_type=f32)
        p = jnp.exp(s - base)
        if allowed is not None:
            p = jnp.where(allowed, p, 0.0)
        dp = lax.dot_general(
            v_ref[piece, :], pair_do, (((1,), (1,)), ((), ())), preferred_element_type=f32
        )
        ds = (p * (dp - inner)).astype(bf16)
        acc_v[piece, :] += jnp.dot(p.astype(bf16), pair_do, preferred_element_type=f32)
        acc_k[piece, :] += jnp.dot(ds, pair_q, preferred_element_type=f32)
        return lax.dot_general(ds, keys, (((0,), (0,)), ((), ())), preferred_element_type=f32)

    place = lax.broadcasted_iota(jnp.int32, (BLOCK, 2 * BLOCK), 1)
    place = jnp.where(place >= BLOCK, place - BLOCK, place)
    allowed = (docs == dcol_ref[...]) & (
        place >= lax.broadcasted_iota(jnp.int32, (BLOCK, 2 * BLOCK), 0)
    )
    acc_q[...] = step(block, logs, allowed)
    base = jnp.where(docs == 0, logs, -masked)

    def earlier(at, carry):
        acc_q[...] += step(at, base, None)
        return carry

    lax.fori_loop(0, block, earlier, 0)
    lane = lax.broadcasted_iota(jnp.int32, (BLOCK, width), 1)
    grad = jnp.where(lane < head_width, acc_q[:BLOCK, :], acc_q[BLOCK:, :])
    gq_ref[...] = (grad * head_width**-0.5).astype(bf16)

    @pl.when(block == pl.num_programs(0) - 1)
    def _():
        gk_ref[...] = acc_k[...].astype(bf16)
        gv_ref[...] = acc_v[...].astype(bf16)


def attend_plane_back(q, k, v, do, o, logs, doc_col, doc_row, head_width):
    rows, width = q.shape
    blocks = rows // BLOCK
    whole = pl.BlockSpec((rows, width), lambda i: (0, 0))
    part = pl.BlockSpec((BLOCK, width), lambda i: (i, 0))
    return pl.pallas_call(
        partial(attend_back_kernel, head_width),
        grid=(blocks,),
        out_shape=(jax.ShapeDtypeStruct((rows, width), bf16),) * 3,
        in_specs=[
            part,
            whole,
            whole,
            part,
            part,
            pl.BlockSpec((1, 1, 2 * BLOCK), lambda i: (i, 0, 0)),
            pl.BlockSpec((BLOCK, 1), lambda i: (i, 0)),
            pl.BlockSpec((1, BLOCK), lambda i: (0, i)),
        ],
        out_specs=(part, whole, whole),
        scratch_shapes=[
            pltpu.VMEM((rows, width), f32),
            pltpu.VMEM((rows, width), f32),
            pltpu.VMEM((2 * BLOCK, width), f32),
        ],
        compiler_params=vmem_params(),
    )(q, k, v, do, o, logs, doc_col, doc_row)


def swap_core(values):
    return lax.ppermute(values, "core", [(0, 1), (1, 0)])


def by_core(own, other, core, axis):
    lower = jnp.where(core == 0, own, other)
    upper = jnp.where(core == 0, other, own)
    return jnp.concatenate([lower, upper], axis=axis)


def plane_device(
    tokens,
    segment_ids,
    cotangent,
    ln_attn_gain,
    ln_attn_bias,
    qkv_weight,
    qv_bias,
    head_scale,
    out_weight,
    out_bias,
    ln_post_gain,
    ln_post_bias,
    ln_ffn_gain,
    ln_ffn_bias,
    fc1_weight,
    fc1_bias,
    mid_gain,
    mid_bias,
    fc2_weight,
    fc2_bias,
):
    layers = qkv_weight.shape[0]
    model_width = tokens.shape[1]
    heads_all = head_scale.shape[1]
    head_width = model_width // heads_all
    hidden_here = fc1_weight.shape[2]
    hidden_all = hidden_here * 8
    quarter = hidden_here // 4
    half_width = model_width // 2
    x, y, core = lax.axis_index("x"), lax.axis_index("y"), lax.axis_index("core")
    quarter_at = 2 * y + core
    factor = head_width**-0.5

    residual = to_plane(tokens).astype(f32)
    docs = to_plane(segment_ids)
    doc_col, doc_row = docs[:, None], docs[None, :]
    gradient = to_plane(cotangent).astype(f32)

    def own_heads(stacked):
        return lax.dynamic_slice_in_dim(stacked, 2 * core, 2, 0)

    def other_heads(stacked):
        return lax.dynamic_slice_in_dim(stacked, 2 * (1 - core), 2, 0)

    def cut(values, at, size, axis):
        return lax.dynamic_slice_in_dim(values, at * size, size, axis)

    def gather_attn(layer_index):
        qkv = cut(cut(qkv_weight[layer_index], core, half_width, 0), y, head_width, 2)
        stacked = lax.all_gather(qkv, "z", axis=0)
        recv = swap_core(other_heads(stacked))
        qkv = by_core(own_heads(stacked), recv, core, 1)
        qkv = jnp.transpose(qkv, (1, 2, 0, 3)).reshape(model_width, 6 * head_width)
        out = cut(cut(out_weight[layer_index], y, head_width, 0), core, half_width, 1)
        stacked = lax.all_gather(out, "z", axis=0)
        recv = swap_core(other_heads(stacked))
        out = by_core(own_heads(stacked), recv, core, 2)
        return qkv, out.reshape(2 * head_width, model_width)

    def gather_ffn(layer_index):
        first = cut(fc1_weight[layer_index], quarter_at, quarter, 1)
        first = lax.all_gather(first, "z", axis=1, tiled=True)
        second = cut(fc2_weight[layer_index], quarter_at, quarter, 0)
        second = lax.all_gather(second, "z", axis=0, tiled=True)
        return first, second

    small = jnp.concatenate(
        [
            cut(qv_bias, y, head_width, 2).reshape(layers, 2 * head_width),
            cut(fc1_bias, quarter_at, quarter, 1),
            cut(mid_gain, quarter_at, quarter, 1),
            cut(mid_bias, quarter_at, quarter, 1),
        ],
        axis=1,
    )
    small = lax.all_gather(small, "z", axis=0)
    bias_heads = own_heads(small[:, :, : 2 * head_width]).reshape(2, layers, 2, head_width)
    bias_heads = jnp.transpose(bias_heads, (1, 2, 0, 3)).reshape(layers, 2, 2 * head_width)

    def hidden_rows(at):
        first = 2 * head_width + at * quarter
        part = small[:, :, first : first + quarter]
        return jnp.transpose(part, (1, 0, 2)).reshape(layers, 4 * quarter)

    shift_hidden, gain_hidden, bias_hidden = hidden_rows(0), hidden_rows(1), hidden_rows(2)
    head_ids = ((2 * core + jnp.arange(2)) * 2 + x) * 2 + y
    head_onehot = (head_ids[:, None] == jnp.arange(heads_all)[None, :]).astype(f32)

    stored = []
    for layer in range(layers):
        qkv_here, out_here = gather_attn(layer)
        first_here, second_here = gather_ffn(layer)
        attn_in, attn_normal, attn_factor = norm_local(
            residual, ln_attn_gain[layer], ln_attn_bias[layer]
        )
        attn_rows = plane_gather(attn_in.astype(bf16))
        projected = jnp.dot(attn_rows, qkv_here, preferred_element_type=f32)
        width = 2 * head_width
        q = (projected[:, :width] + bias_heads[layer, 0]).astype(bf16) * factor
        q = q.astype(bf16)
        k = projected[:, width : 2 * width].astype(bf16)
        v = (projected[:, 2 * width :] + bias_heads[layer, 1]).astype(bf16)
        attended, logs = attend_plane(q, k, v, doc_col, doc_row, head_width)
        scale = jnp.sum(head_onehot * head_scale[layer][None, :], axis=1)
        scale_row = jnp.repeat(scale, head_width)[None, :]
        scaled = (attended * scale_row).astype(bf16)
        branch = plane_scatter(scaled, out_here, 0, 2) + out_bias[layer]
        post_out, post_normal, post_factor = norm_local(
            branch, ln_post_gain[layer], ln_post_bias[layer]
        )
        middle = residual + post_out
        ffn_in, ffn_normal, ffn_factor = norm_local(middle, ln_ffn_gain[layer], ln_ffn_bias[layer])
        ffn_rows = plane_gather(ffn_in.astype(bf16))
        before = jnp.dot(ffn_rows, first_here, preferred_element_type=f32) + shift_hidden[layer]
        activated = jax.nn.gelu(before, approximate=False)
        sums = plane_sum(
            jnp.stack([jnp.sum(activated, axis=1), jnp.sum(activated * activated, axis=1)])
        )
        average = sums[0] / hidden_all
        spread = sums[1] / hidden_all - average * average
        hidden_factor = lax.rsqrt(spread + epsilon)[:, None]
        hidden_normal = (activated - average[:, None]) * hidden_factor
        mixed = (hidden_normal * gain_hidden[layer] + bias_hidden[layer]).astype(bf16)
        ffn_out = plane_scatter(mixed, second_here, 0, 3)
        stored.append(
            (
                qkv_here,
                out_here,
                first_here,
                second_here,
                attn_normal,
                attn_factor,
                attn_rows,
                q,
                k,
                v,
                attended,
                logs,
                scale_row,
                scaled,
                post_normal,
                post_factor,
                ffn_normal,
                ffn_factor,
                ffn_rows,
                before,
                hidden_normal,
                hidden_factor,
                mixed,
            )
        )
        residual = middle + ffn_out + fc2_bias[layer]
    layer_output = from_plane(residual.astype(bf16))

    def share_ffn(grad):
        mine = lax.psum_scatter(grad.astype(bf16), "z", scatter_dimension=0, tiled=True)
        return lax.all_gather(mine, ("y", "core"), axis=0, tiled=True).astype(f32)

    def share_attn(grad):
        grad = jnp.transpose(grad.astype(bf16), (1, 0, 2, 3))
        own = cut(grad, core, half_width, 3)
        recv = swap_core(cut(grad, 1 - core, half_width, 3))
        stacked = by_core(own, recv, core, 0)
        mine = lax.psum_scatter(stacked, "z", scatter_dimension=0)
        full = lax.all_gather(mine, ("y", "core"), axis=0)
        full = full.reshape(2, 2, 4, head_width, half_width).astype(f32)
        qkv = jnp.transpose(full[:, :, :3], (1, 4, 2, 0, 3))
        out = jnp.transpose(full[:, :, 3], (0, 2, 1, 3))
        return (
            qkv.reshape(model_width, 3, 2 * head_width),
            out.reshape(2 * head_width, model_width),
        )

    big = [None] * layers
    little = [None] * layers
    for layer in reversed(range(layers)):
        (
            qkv_here,
            out_here,
            first_here,
            second_here,
            attn_normal,
            attn_factor,
            attn_rows,
            q,
            k,
            v,
            attended,
            logs,
            scale_row,
            scaled,
            post_normal,
            post_factor,
            ffn_normal,
            ffn_factor,
            ffn_rows,
            before,
            hidden_normal,
            hidden_factor,
            mixed,
        ) = stored[layer]
        second_shift_grad = jnp.sum(gradient, axis=0)
        grad_rows = plane_gather(gradient.astype(bf16))
        mixed_grad = jnp.einsum(
            "td,fd->tf", grad_rows, second_here, preferred_element_type=f32
        )
        second_grad = share_ffn(
            jnp.einsum("tf,td->fd", mixed, grad_rows, preferred_element_type=f32)
        )
        hidden_gain_grad = jnp.sum(mixed_grad * hidden_normal, axis=0)
        hidden_shift_grad = jnp.sum(mixed_grad, axis=0)
        normal_grad = mixed_grad * gain_hidden[layer]
        sums = plane_sum(
            jnp.stack(
                [jnp.sum(normal_grad, axis=1), jnp.sum(normal_grad * hidden_normal, axis=1)]
            )
        )
        active_grad = hidden_factor * (
            normal_grad
            - sums[0][:, None] / hidden_all
            - hidden_normal * sums[1][:, None] / hidden_all
        )
        gelu_pull = jax.vjp(partial(jax.nn.gelu, approximate=False), before)[1]
        pre_grad = gelu_pull(active_grad)[0].astype(bf16)
        first_shift_grad = jnp.sum(pre_grad, axis=0, dtype=f32)
        first_grad = share_ffn(
            jnp.einsum("tf,td->fd", pre_grad, ffn_rows, preferred_element_type=f32)
        ).T
        ffn_in_grad = plane_scatter(pre_grad, first_here, 1, 4)
        ffn_gain_grad = jnp.sum(ffn_in_grad * ffn_normal, axis=0)
        ffn_bias_grad = jnp.sum(ffn_in_grad, axis=0)
        middle_grad = gradient + norm_back(ffn_in_grad, ffn_normal, ffn_factor, ln_ffn_gain[layer])
        post_gain_grad = jnp.sum(middle_grad * post_normal, axis=0)
        post_bias_grad = jnp.sum(middle_grad, axis=0)
        branch_grad = norm_back(middle_grad, post_normal, post_factor, ln_post_gain[layer])
        out_shift_grad = jnp.sum(branch_grad, axis=0)
        branch_rows = plane_gather(branch_grad.astype(bf16))
        scaled_grad = jnp.einsum("td,cd->tc", branch_rows, out_here, preferred_element_type=f32)
        out_grad = jnp.einsum("tc,td->cd", scaled, branch_rows, preferred_element_type=f32)
        scale_cols = jnp.sum(attended * scaled_grad, axis=0)
        scale_grad = jnp.sum(
            head_onehot * jnp.sum(scale_cols.reshape(2, head_width), axis=1)[:, None], axis=0
        )
        attended_grad = (scaled_grad * scale_row).astype(bf16)
        gq, gk, gv = attend_plane_back(
            q, k, v, attended_grad, attended, logs, doc_col, doc_row, head_width
        )
        proj_grad = jnp.concatenate([gq, gk, gv], axis=1)
        bias_grad = jnp.stack(
            [jnp.sum(gq, axis=0, dtype=f32), jnp.sum(gv, axis=0, dtype=f32)], axis=0
        )
        qkv_grad = jnp.einsum("tc,td->cd", proj_grad, attn_rows, preferred_element_type=f32)
        qkv_grad, out_grad = share_attn(
            jnp.concatenate([qkv_grad, out_grad], axis=0).reshape(4, 2, head_width, model_width)
        )
        attn_in_grad = plane_scatter(proj_grad, qkv_here, 1, 5)
        attn_gain_grad = jnp.sum(attn_in_grad * attn_normal, axis=0)
        attn_bias_grad = jnp.sum(attn_in_grad, axis=0)
        gradient = middle_grad + norm_back(
            attn_in_grad, attn_normal, attn_factor, ln_attn_gain[layer]
        )
        big[layer] = (qkv_grad, out_grad, first_grad, second_grad)
        hidden = jnp.stack([first_shift_grad, hidden_gain_grad, hidden_shift_grad])
        hidden = lax.dynamic_update_slice(
            jnp.zeros((3, 4, 2, 4, quarter), f32),
            hidden.reshape(3, 4, 1, 1, quarter),
            (0, 0, x, quarter_at, 0),
        )
        bias_grad = lax.dynamic_update_slice(
            jnp.zeros((2, 4, 2, 2, head_width), f32),
            bias_grad.reshape(2, 2, 1, 1, head_width),
            (0, 2 * core, x, y, 0),
        )
        little[layer] = jnp.concatenate(
            [
                hidden.reshape(-1),
                bias_grad.reshape(-1),
                attn_gain_grad,
                attn_bias_grad,
                out_shift_grad,
                post_gain_grad,
                post_bias_grad,
                ffn_gain_grad,
                ffn_bias_grad,
                second_shift_grad,
                scale_grad,
                jnp.zeros((-heads_all % 128,), f32),
            ]
        )
    input_grad = from_plane(gradient.astype(bf16)).astype(f32)
    stacked = lax.psum(jnp.stack(little), EVERY)
    shard = 2 * lax.axis_index("z") + x
    hidden = stacked[:, : 3 * hidden_all].reshape(layers, 3, 8, hidden_here)
    hidden = lax.dynamic_index_in_dim(hidden, shard, 2, keepdims=False)
    rest = stacked[:, 3 * hidden_all :]
    bias_grad = rest[:, : 2 * model_width].reshape(layers, 2, 8, model_width // 8)
    bias_grad = lax.dynamic_index_in_dim(bias_grad, shard, 2, keepdims=False)
    rest = rest[:, 2 * model_width :]
    vectors = [rest[:, i * model_width : (i + 1) * model_width] for i in range(8)]
    scale_grad = rest[:, 8 * model_width : 8 * model_width + heads_all]
    weights = [jnp.stack([big[layer][i] for layer in range(layers)]) for i in range(4)]
    return (
        layer_output,
        input_grad,
        vectors[0],
        vectors[1],
        weights[0],
        bias_grad,
        scale_grad,
        weights[1],
        vectors[2],
        vectors[3],
        vectors[4],
        vectors[5],
        vectors[6],
        weights[2],
        hidden[:, 0],
        hidden[:, 1],
        hidden[:, 2],
        weights[3],
        vectors[7],
    )


def split_specs(rows, mp):
    both = tuple(rows) + tuple(mp)
    in_specs = (
        P(both, None),
        P(rows),
        P(both, None),
        P(),
        P(),
        P(None, None, None, mp),
        P(None, None, mp),
        P(),
        P(None, mp, None),
        P(),
        P(),
        P(),
        P(),
        P(),
        P(None, None, mp),
        P(None, mp),
        P(None, mp),
        P(None, mp),
        P(None, mp, None),
        P(),
    )
    out_specs = (
        P(both, None),
        P(both, None),
        P(),
        P(),
        P(None, None, None, mp),
        P(None, None, mp),
        P(),
        P(None, mp, None),
        P(),
        P(),
        P(),
        P(),
        P(),
        P(None, None, mp),
        P(None, mp),
        P(None, mp),
        P(None, mp),
        P(None, mp, None),
        P(),
    )
    return in_specs, out_specs


def solution(mesh):
    if mesh.shape["rows"] == 4 and mesh.shape["mp"] == 8:
        planes = Mesh(mesh.devices.reshape(2, 2, 4, 2), ("y", "core", "z", "x"))
        in_specs, out_specs = split_specs(("y", "core"), ("z", "x"))
        return jax.shard_map(
            plane_device, mesh=planes, in_specs=in_specs, out_specs=out_specs, check_vma=False
        )
    in_specs, out_specs = split_specs(("rows",), ("mp",))
    return jax.shard_map(
        per_device, mesh=mesh, in_specs=in_specs, out_specs=out_specs, check_vma=False
    )
```

```python
from functools import partial

import jax
import jax.numpy as jnp
from jax import lax
from jax.experimental import pallas as pl
from jax.experimental.pallas import tpu as pltpu
from jax.sharding import Mesh
from jax.sharding import PartitionSpec as P

epsilon = 1e-05
masked = -1e30


def partner(shard, axis, stride):
    return lax.ppermute(shard, axis, [(i, i ^ 1 << stride) for i in range(lax.axis_size(axis))])


def norm_local(values, gain_row, bias_row):
    average = jnp.mean(values, axis=-1, keepdims=True)
    centered = values - average
    spread = jnp.mean(centered * centered, axis=-1, keepdims=True)
    factor = lax.rsqrt(spread + epsilon)
    normal = centered * factor
    return (normal * gain_row + bias_row, normal, factor)


def norm_back(grad_out, normal, factor, gain_row):
    scaled = grad_out * gain_row
    inner_sum = jnp.mean(scaled * normal, axis=-1, keepdims=True)
    return factor * (scaled - jnp.mean(scaled, axis=-1, keepdims=True) - normal * inner_sum)


def collect_rows(normed_b):
    return lax.all_gather(normed_b, "mp", axis=0, tiled=True)


def collect_grads(gradient_b):
    return lax.all_gather(gradient_b, "mp", axis=0, tiled=True)


def reduce_branch(operand_b, weight_b, local_rows):

    def partial_term(first_row, count):
        return jnp.dot(operand_b, weight_b, preferred_element_type=jnp.float32)

    return lax.psum_scatter(
        partial_term(jnp.int32(0), local_rows * lax.axis_size("mp")).astype(jnp.bfloat16),
        "mp",
        scatter_dimension=0,
        tiled=True,
    ).astype(jnp.float32)


def reduce_grads(operand_b, weight_b, local_rows):

    def partial_term(first_row, count):
        return jnp.einsum("tc,dc->td", operand_b, weight_b, preferred_element_type=jnp.float32)

    return lax.psum_scatter(
        partial_term(jnp.int32(0), local_rows * lax.axis_size("mp")).astype(jnp.bfloat16),
        "mp",
        scatter_dimension=0,
        tiled=True,
    ).astype(jnp.float32)


def hidden_stats(first_sum, second_sum):
    return lax.psum((first_sum, second_sum), "mp")


def hidden_grad_stats(first_sum, second_sum):
    return lax.psum((first_sum, second_sum), "mp")


def join_cols(mine, other, is_upper):
    lower_part = jnp.where(is_upper, other, mine)
    upper_part = jnp.where(is_upper, mine, other)
    return jnp.concatenate([lower_part, upper_part], axis=-1)


def join_rows(mine, other, is_upper):
    lower_part = jnp.where(is_upper, other, mine)
    upper_part = jnp.where(is_upper, mine, other)
    return jnp.concatenate([lower_part, upper_part], axis=0)


def split_cols(values, cols_here, is_upper):
    lower_part = values[..., :cols_here]
    upper_part = values[..., cols_here:]
    return (
        jnp.where(is_upper, upper_part, lower_part),
        jnp.where(is_upper, lower_part, upper_part),
    )


def masked_scores(query_block, key_rows, query_start, block_rows, doc_rows, positions):
    factor = query_block.shape[-1] ** (-0.5)
    scores = (
        jnp.einsum("qhe,khe->hqk", query_block, key_rows, preferred_element_type=jnp.float32)
        * factor
    )
    query_place = query_start + jnp.arange(block_rows, dtype=jnp.int32)
    query_docs = lax.dynamic_slice_in_dim(doc_rows, query_start, block_rows, 0)
    allowed = (query_docs[:, None] == doc_rows[None, :]) & (
        query_place[:, None] >= positions[None, :]
    )
    return jnp.where(allowed[None], scores, masked)


def attend_forward(queries, key_rows, value_rows, doc_rows, row_offset):
    total_rows = queries.shape[0]
    block_rows = min(512, total_rows)
    positions = jnp.arange(key_rows.shape[0], dtype=jnp.int32)

    def one_block(first_row):
        query_block = lax.dynamic_slice_in_dim(queries, first_row, block_rows, 0)
        scores = masked_scores(
            query_block, key_rows, row_offset + first_row, block_rows, doc_rows, positions
        )
        row_peak = jnp.max(scores, axis=-1, keepdims=True)
        weights = jnp.exp(scores - row_peak)
        totals = jnp.sum(weights, axis=-1, keepdims=True)
        probabilities = (weights / totals).astype(jnp.bfloat16)
        output = jnp.einsum(
            "hqk,khe->qhe", probabilities, value_rows, preferred_element_type=jnp.float32
        )
        return (output, (row_peak + jnp.log(totals))[..., 0])

    starts = jnp.arange(total_rows // block_rows, dtype=jnp.int32) * block_rows
    outputs, log_totals = lax.map(one_block, starts)
    return (outputs.reshape(queries.shape), log_totals)


def attend_backward(queries, key_rows, value_rows, doc_rows, row_offset, log_totals, grad_out):
    total_rows = queries.shape[0]
    block_rows = min(512, total_rows)
    positions = jnp.arange(key_rows.shape[0], dtype=jnp.int32)
    factor = queries.shape[-1] ** (-0.5)

    def one_block(running, first_row):
        key_grad, value_grad = running
        query_block = lax.dynamic_slice_in_dim(queries, first_row, block_rows, 0)
        grad_block = lax.dynamic_slice_in_dim(grad_out, first_row, block_rows, 0)
        scores = masked_scores(
            query_block, key_rows, row_offset + first_row, block_rows, doc_rows, positions
        )
        block_totals = lax.dynamic_index_in_dim(
            log_totals, first_row // block_rows, 0, keepdims=False
        )
        probabilities = jnp.exp(scores - block_totals[..., None])
        prob_grad = jnp.einsum(
            "qhe,khe->hqk", grad_block, value_rows, preferred_element_type=jnp.float32
        )
        inner_sum = jnp.sum(probabilities * prob_grad, axis=-1, keepdims=True)
        score_grad = (probabilities * (prob_grad - inner_sum)).astype(jnp.bfloat16)
        query_grad = (
            jnp.einsum("hqk,khe->qhe", score_grad, key_rows, preferred_element_type=jnp.float32)
            * factor
        )
        key_grad = (
            key_grad
            + jnp.einsum(
                "hqk,qhe->khe", score_grad, query_block, preferred_element_type=jnp.float32
            )
            * factor
        )
        value_grad = value_grad + jnp.einsum(
            "hqk,qhe->khe",
            probabilities.astype(jnp.bfloat16),
            grad_block,
            preferred_element_type=jnp.float32,
        )
        return ((key_grad, value_grad), query_grad)

    starts = jnp.arange(total_rows // block_rows, dtype=jnp.int32) * block_rows
    zero_grads = jnp.zeros(key_rows.shape, jnp.float32)
    (key_grad, value_grad), query_grads = lax.scan(one_block, (zero_grads, zero_grads), starts)
    return (query_grads.reshape(queries.shape), key_grad, value_grad)


def stack_layers(layer_list, members):
    stacked = []
    for member_index in range(members):
        stacked.append(jnp.stack([entry[member_index] for entry in layer_list], axis=0))
    return stacked


def per_device(
    tokens,
    segment_ids,
    cotangent,
    ln_attn_gain,
    ln_attn_bias,
    qkv_weight,
    qv_bias,
    head_scale,
    out_weight,
    out_bias,
    ln_post_gain,
    ln_post_bias,
    ln_ffn_gain,
    ln_ffn_bias,
    fc1_weight,
    fc1_bias,
    mid_gain,
    mid_bias,
    fc2_weight,
    fc2_bias,
):
    layers = qkv_weight.shape[0]
    local_rows = tokens.shape[0]
    model_width = tokens.shape[1]
    cols_here = qkv_weight.shape[3]
    heads_all = head_scale.shape[1]
    head_width = model_width // heads_all
    pair_cols = 2 * cols_here
    pair_heads = pair_cols // head_width
    group_rows = segment_ids.shape[0]
    half_rows = group_rows // 2
    hidden_all = fc1_weight.shape[2] * lax.axis_size("mp")
    device_index = lax.axis_index("mp")
    is_upper = device_index % 2 == 1
    own_start = jnp.where(is_upper, half_rows, 0).astype(jnp.int32)
    other_start = jnp.where(is_upper, 0, half_rows).astype(jnp.int32)
    first_head = device_index // 2 * pair_heads
    pair_onehot = (
        (first_head + jnp.arange(pair_heads, dtype=jnp.int32))[:, None]
        == jnp.arange(heads_all, dtype=jnp.int32)[None, :]
    ).astype(jnp.float32)
    residual = tokens.astype(jnp.float32)
    stored = []
    for layer_index in range(layers):
        attn_in, attn_normal, attn_factor = norm_local(
            residual, ln_attn_gain[layer_index], ln_attn_bias[layer_index]
        )
        attn_rows = collect_rows(attn_in.astype(jnp.bfloat16))
        qkv_here = qkv_weight[layer_index].reshape(model_width, 3 * cols_here)
        projected = jnp.dot(attn_rows, qkv_here, preferred_element_type=jnp.float32).reshape(
            -1, 3, cols_here
        )
        bias_pair = qv_bias[layer_index]
        query_mine = (projected[:, 0] + bias_pair[0]).astype(jnp.bfloat16)
        key_mine = projected[:, 1].astype(jnp.bfloat16)
        value_mine = (projected[:, 2] + bias_pair[1]).astype(jnp.bfloat16)
        query_send = lax.dynamic_slice_in_dim(query_mine, other_start, half_rows, 0)
        query_recv, key_recv, value_recv = partner((query_send, key_mine, value_mine), "mp", 0)
        query_own = lax.dynamic_slice_in_dim(query_mine, own_start, half_rows, 0)
        queries = join_cols(query_own, query_recv, is_upper).reshape(
            half_rows, pair_heads, head_width
        )
        key_rows = join_cols(key_mine, key_recv, is_upper).reshape(
            group_rows, pair_heads, head_width
        )
        value_rows = join_cols(value_mine, value_recv, is_upper).reshape(
            group_rows, pair_heads, head_width
        )
        attended, log_totals = attend_forward(queries, key_rows, value_rows, segment_ids, own_start)
        pair_scale = jnp.sum(pair_onehot * head_scale[layer_index][None, :], axis=1)
        scaled_half = (
            (attended * pair_scale[None, :, None])
            .astype(jnp.bfloat16)
            .reshape(half_rows, pair_cols)
        )
        own_cols, other_cols = split_cols(scaled_half, cols_here, is_upper)
        scaled_recv = partner(other_cols, "mp", 0)
        scaled_mine = join_rows(own_cols, scaled_recv, is_upper)
        branch = (
            reduce_branch(scaled_mine, out_weight[layer_index], local_rows) + out_bias[layer_index]
        )
        post_out, post_normal, post_factor = norm_local(
            branch, ln_post_gain[layer_index], ln_post_bias[layer_index]
        )
        middle = residual + post_out
        ffn_in, ffn_normal, ffn_factor = norm_local(
            middle, ln_ffn_gain[layer_index], ln_ffn_bias[layer_index]
        )
        ffn_rows = collect_rows(ffn_in.astype(jnp.bfloat16))
        before_gelu = (
            jnp.dot(ffn_rows, fc1_weight[layer_index], preferred_element_type=jnp.float32)
            + fc1_bias[layer_index]
        )
        activated = jax.nn.gelu(before_gelu, approximate=False)
        first_sum, second_sum = hidden_stats(
            jnp.sum(activated, axis=1), jnp.sum(activated * activated, axis=1)
        )
        average = first_sum / hidden_all
        spread = second_sum / hidden_all - average * average
        hidden_factor = lax.rsqrt(spread + epsilon)[:, None]
        hidden_normal = (activated - average[:, None]) * hidden_factor
        mixed_b = (hidden_normal * mid_gain[layer_index] + mid_bias[layer_index]).astype(
            jnp.bfloat16
        )
        ffn_out = reduce_branch(mixed_b, fc2_weight[layer_index], local_rows)
        stored.append(
            (
                attn_normal,
                attn_factor,
                attn_rows,
                queries,
                key_rows,
                value_rows,
                attended,
                log_totals,
                pair_scale,
                scaled_mine,
                post_normal,
                post_factor,
                ffn_normal,
                ffn_factor,
                ffn_rows,
                before_gelu,
                hidden_normal,
                hidden_factor,
                mixed_b,
            )
        )
        residual = middle + ffn_out + fc2_bias[layer_index]
    layer_output = residual.astype(jnp.bfloat16)
    gradient = cotangent.astype(jnp.float32)
    sharded_list = []
    shared_list = []
    for layer_index in reversed(range(layers)):
        (
            attn_normal,
            attn_factor,
            attn_rows,
            queries,
            key_rows,
            value_rows,
            attended,
            log_totals,
            pair_scale,
            scaled_mine,
            post_normal,
            post_factor,
            ffn_normal,
            ffn_factor,
            ffn_rows,
            before_gelu,
            hidden_normal,
            hidden_factor,
            mixed_b,
        ) = stored[layer_index]
        qkv_here = qkv_weight[layer_index].reshape(model_width, 3 * cols_here)
        second_shift_grad = jnp.sum(gradient, axis=0)
        grad_rows = collect_grads(gradient.astype(jnp.bfloat16))
        mixed_grad = jnp.einsum(
            "td,fd->tf", grad_rows, fc2_weight[layer_index], preferred_element_type=jnp.float32
        )
        second_grad = jnp.einsum(
            "tf,td->fd", mixed_b, grad_rows, preferred_element_type=jnp.float32
        )
        hidden_gain_grad = jnp.sum(mixed_grad * hidden_normal, axis=0)
        hidden_shift_grad = jnp.sum(mixed_grad, axis=0)
        normal_grad = mixed_grad * mid_gain[layer_index]
        grad_first, grad_second = hidden_grad_stats(
            jnp.sum(normal_grad, axis=1), jnp.sum(normal_grad * hidden_normal, axis=1)
        )
        active_grad = hidden_factor * (
            normal_grad
            - grad_first[:, None] / hidden_all
            - hidden_normal * grad_second[:, None] / hidden_all
        )
        gelu_pull = jax.vjp(partial(jax.nn.gelu, approximate=False), before_gelu)[1]
        pre_grad_b = gelu_pull(active_grad)[0].astype(jnp.bfloat16)
        first_shift_grad = jnp.sum(pre_grad_b, axis=0, dtype=jnp.float32)
        first_grad = jnp.einsum(
            "td,tf->df", ffn_rows, pre_grad_b, preferred_element_type=jnp.float32
        )
        ffn_in_grad = reduce_grads(pre_grad_b, fc1_weight[layer_index], local_rows)
        ffn_gain_grad = jnp.sum(ffn_in_grad * ffn_normal, axis=0)
        ffn_bias_grad = jnp.sum(ffn_in_grad, axis=0)
        middle_grad = gradient + norm_back(
            ffn_in_grad, ffn_normal, ffn_factor, ln_ffn_gain[layer_index]
        )
        post_gain_grad = jnp.sum(middle_grad * post_normal, axis=0)
        post_bias_grad = jnp.sum(middle_grad, axis=0)
        branch_grad = norm_back(middle_grad, post_normal, post_factor, ln_post_gain[layer_index])
        out_shift_grad = jnp.sum(branch_grad, axis=0)
        branch_rows = collect_grads(branch_grad.astype(jnp.bfloat16))
        scaled_grad = jnp.einsum(
            "td,cd->tc", branch_rows, out_weight[layer_index], preferred_element_type=jnp.float32
        )
        out_grad = jnp.einsum(
            "tc,td->cd", scaled_mine, branch_rows, preferred_element_type=jnp.float32
        )
        grad_send = lax.dynamic_slice_in_dim(scaled_grad, other_start, half_rows, 0)
        grad_recv = partner(grad_send.astype(jnp.bfloat16), "mp", 0).astype(grad_send.dtype)
        grad_own = lax.dynamic_slice_in_dim(scaled_grad, own_start, half_rows, 0)
        scaled_pair = join_cols(grad_own, grad_recv, is_upper).reshape(
            half_rows, pair_heads, head_width
        )
        pair_scale_grad = jnp.sum(attended * scaled_pair, axis=(0, 2))
        scale_grad = jnp.sum(pair_onehot * pair_scale_grad[:, None], axis=0)
        attended_grad_b = (scaled_pair * pair_scale[None, :, None]).astype(jnp.bfloat16)
        query_grad, key_grad, value_grad = attend_backward(
            queries, key_rows, value_rows, segment_ids, own_start, log_totals, attended_grad_b
        )
        query_own, query_other = split_cols(
            query_grad.reshape(half_rows, pair_cols), cols_here, is_upper
        )
        key_own, key_other = split_cols(
            key_grad.reshape(group_rows, pair_cols), cols_here, is_upper
        )
        value_own, value_other = split_cols(
            value_grad.reshape(group_rows, pair_cols), cols_here, is_upper
        )
        query_recv, key_recv, value_recv = (
            partner(query_other.astype(jnp.bfloat16), "mp", 0).astype(query_other.dtype),
            partner(key_other.astype(jnp.bfloat16), "mp", 0).astype(key_other.dtype),
            partner(value_other.astype(jnp.bfloat16), "mp", 0).astype(value_other.dtype),
        )
        query_grad_b = join_rows(query_own, query_recv, is_upper).astype(jnp.bfloat16)
        key_grad_b = (key_own + key_recv).astype(jnp.bfloat16)
        value_grad_b = (value_own + value_recv).astype(jnp.bfloat16)
        proj_grad = jnp.stack([query_grad_b, key_grad_b, value_grad_b], axis=1).reshape(
            -1, 3 * cols_here
        )
        pair_grad = jnp.stack(
            [
                jnp.sum(query_grad_b, axis=0, dtype=jnp.float32),
                jnp.sum(value_grad_b, axis=0, dtype=jnp.float32),
            ],
            axis=0,
        )
        qkv_grad = jnp.einsum(
            "td,tc->dc", attn_rows, proj_grad, preferred_element_type=jnp.float32
        ).reshape(model_width, 3, cols_here)
        attn_in_grad = reduce_grads(proj_grad, qkv_here, local_rows)
        attn_gain_grad = jnp.sum(attn_in_grad * attn_normal, axis=0)
        attn_bias_grad = jnp.sum(attn_in_grad, axis=0)
        gradient = middle_grad + norm_back(
            attn_in_grad, attn_normal, attn_factor, ln_attn_gain[layer_index]
        )
        sharded_list.insert(
            0,
            (
                qkv_grad,
                pair_grad,
                out_grad,
                first_grad,
                first_shift_grad,
                hidden_gain_grad,
                hidden_shift_grad,
                second_grad,
            ),
        )
        shared_list.insert(
            0,
            (
                attn_gain_grad,
                attn_bias_grad,
                scale_grad,
                out_shift_grad,
                post_gain_grad,
                post_bias_grad,
                ffn_gain_grad,
                ffn_bias_grad,
                second_shift_grad,
            ),
        )
    sharded = stack_layers(sharded_list, 8)
    shared = stack_layers(shared_list, 9)
    sharded = (
        lax.psum(sharded[0].astype(jnp.bfloat16), "rows").astype(jnp.float32),
        lax.psum(sharded[1].astype(jnp.bfloat16), "rows").astype(jnp.float32),
        lax.psum(sharded[2].astype(jnp.bfloat16), "rows").astype(jnp.float32),
        lax.psum(sharded[3].astype(jnp.bfloat16), "rows").astype(jnp.float32),
        lax.psum(sharded[4].astype(jnp.bfloat16), "rows").astype(jnp.float32),
        lax.psum(sharded[5].astype(jnp.bfloat16), "rows").astype(jnp.float32),
        lax.psum(sharded[6].astype(jnp.bfloat16), "rows").astype(jnp.float32),
        lax.psum(sharded[7].astype(jnp.bfloat16), "rows").astype(jnp.float32),
    )
    shared = lax.psum(
        (
            shared[0],
            shared[1],
            shared[2],
            shared[3],
            shared[4],
            shared[5],
            shared[6],
            shared[7],
            shared[8],
        ),
        ("rows", "mp"),
    )
    return (
        layer_output,
        gradient,
        shared[0],
        shared[1],
        sharded[0],
        sharded[1],
        shared[2],
        sharded[2],
        shared[3],
        shared[4],
        shared[5],
        shared[6],
        shared[7],
        sharded[3],
        sharded[4],
        sharded[5],
        sharded[6],
        sharded[7],
        shared[8],
    )


MESH_ID = pl.DeviceIdType.MESH
PLANE = ("core", "y", "x")
EVERY = ("y", "core", "z", "x")
f32 = jnp.float32
bf16 = jnp.bfloat16


def vmem_params(collective_id=None, mib=48):
    if collective_id is None:
        return pltpu.CompilerParams(vmem_limit_bytes=mib * 2**20)
    return pltpu.CompilerParams(
        vmem_limit_bytes=mib * 2**20, collective_id=collective_id, has_side_effects=True
    )


def plane_pairs():
    pairs = []
    for y in range(2):
        for core in range(2):
            for z in range(4):
                for x in range(2):
                    source = ((y * 2 + core) * 4 + z) * 2 + x
                    target = (((z % 2) * 2 + z // 2) * 4 + (2 * y + core)) * 2 + x
                    pairs.append((source, target))
    return pairs


def to_plane(values):
    return lax.ppermute(values, EVERY, plane_pairs())


def from_plane(values):
    return lax.ppermute(values, EVERY, [(target, source) for source, target in plane_pairs()])


class Here:
    def __init__(self):
        self.x, self.y = lax.axis_index("x"), lax.axis_index("y")
        self.core, self.z = lax.axis_index("core"), lax.axis_index("z")

    def peer(self, flip_x, flip_y, flip_core, step_z):
        place = {}
        if flip_x:
            place["x"] = 1 - self.x
        if flip_y:
            place["y"] = 1 - self.y
        if flip_core:
            place["core"] = 1 - self.core
        if step_z:
            place["z"] = lax.rem(self.z + step_z, 4)
        return place


BY_X, BY_Y, BY_CORE = (1, 0, 0, 0), (0, 1, 0, 0), (0, 0, 1, 0)
BY_Z = tuple((0, 0, 0, step) for step in (1, 2, 3))
BY_LINE = BY_Z + tuple((0, 0, 1, step) for step in range(4))
BY_PLANE = tuple((flip & 1, flip >> 1 & 1, flip >> 2, 0) for flip in range(1, 8))


def remote(source, target, send_sem, recv_sem, place):
    return pltpu.make_async_remote_copy(
        src_ref=source,
        dst_ref=target,
        send_sem=send_sem,
        recv_sem=recv_sem,
        device_id=place,
        device_id_type=MESH_ID,
    )


def dma_sems(count):
    return pltpu.SemaphoreType.DMA((count,))


class Task:
    arrays = ()
    spaces = ()
    outs = ()
    out_spaces = ()
    scratch = ()
    reach = ()

    def start(self, here, ins, outs, scratch):
        pass

    def finish(self, here, ins, outs, scratch):
        pass


def run_tasks(ids, *tasks):
    reach = []
    for task in tasks:
        reach += [way for way in task.reach if way not in reach]

    def kernel(*refs):
        refs = list(refs)
        views = [[], [], []]
        for kind, name in enumerate(("arrays", "outs", "scratch")):
            for task in tasks:
                count = len(getattr(task, name))
                views[kind].append(refs[:count])
                refs = refs[count:]
        here = Here()
        barrier = pltpu.get_barrier_semaphore()
        for way in reach:
            pl.semaphore_signal(barrier, inc=1, device_id=here.peer(*way), device_id_type=MESH_ID)
        pl.semaphore_wait(barrier, len(reach))
        for task, *held in zip(tasks, *views):
            task.start(here, *held)
        for task, *held in zip(tasks, *views):
            task.finish(here, *held)

    results = pl.pallas_call(
        kernel,
        out_shape=[out for task in tasks for out in task.outs],
        in_specs=[pl.BlockSpec(memory_space=s) for task in tasks for s in task.spaces],
        out_specs=[pl.BlockSpec(memory_space=s) for task in tasks for s in task.out_spaces],
        scratch_shapes=[each for task in tasks for each in task.scratch],
        compiler_params=vmem_params(next(ids)),
    )(*[array for task in tasks for array in task.arrays])
    results = list(results)
    split = []
    for task in tasks:
        split.append(results[: len(task.outs)])
        results = results[len(task.outs) :]
    return split


class PlaneGather(Task):
    def __init__(self, block):
        rows, width = block.shape
        self.arrays, self.spaces = (block,), (pltpu.VMEM,)
        self.outs = (jax.ShapeDtypeStruct((8 * rows, width), block.dtype),)
        self.out_spaces = (pltpu.VMEM,)
        self.scratch = (dma_sems(11), dma_sems(11), pltpu.SemaphoreType.DMA)
        self.reach = (BY_X, BY_Y, BY_CORE)

    def place(self, here, o_ref, at_x, at_y, part=None):
        rows = o_ref.shape[0] // 8
        first = ((2 * here.core + at_y) * 2 + at_x) * rows
        if part is None:
            return o_ref.at[pl.ds(pl.multiple_of(first, rows), rows)]
        half = rows // 2
        return o_ref.at[pl.ds(pl.multiple_of(first + part * half, half), half)]

    def copies(self, here, x_ref, o_ref, send_sem, recv_sem):
        x, y = here.x, here.y
        half = x_ref.shape[0] // 2
        to_x, to_y, to_core = here.peer(*BY_X), here.peer(*BY_Y), here.peer(*BY_CORE)

        def copy(index, source, target, way):
            return remote(source, target, send_sem.at[index], recv_sem.at[index], way)

        def pass_on(index, way, *at):
            return copy(index, self.place(here, o_ref, *at), self.place(here, o_ref, *at), way)

        own = [self.place(here, o_ref, x, y, part) for part in (0, 1)]
        mine = [x_ref.at[pl.ds(part * half, half)] for part in (0, 1)]
        return [
            copy(0, mine[0], own[0], to_x),
            copy(1, mine[1], own[1], to_y),
            copy(2, mine[1], own[1], to_x),
            copy(3, mine[0], own[0], to_y),
            copy(4, x_ref, self.place(here, o_ref, x, y), to_core),
            pass_on(5, to_y, 1 - x, y, 0),
            pass_on(6, to_x, x, 1 - y, 1),
            pass_on(7, to_core, 1 - x, y),
            pass_on(8, to_core, x, 1 - y),
            pass_on(9, to_core, 1 - x, 1 - y, 0),
            pass_on(10, to_core, 1 - x, 1 - y, 1),
        ]

    def keep(self, here, x_ref, o_ref, own_sem):
        return pltpu.make_async_copy(x_ref, self.place(here, o_ref, here.x, here.y), own_sem)

    def start(self, here, ins, outs, scratch):
        copies = self.copies(here, ins[0], outs[0], scratch[0], scratch[1])
        for index in range(5):
            copies[index].start()
        self.keep(here, ins[0], outs[0], scratch[2]).start()

    def finish(self, here, ins, outs, scratch):
        copies = self.copies(here, ins[0], outs[0], scratch[0], scratch[1])
        copies[0].wait_recv()
        copies[5].start()
        copies[1].wait_recv()
        copies[6].start()
        copies[2].wait_recv()
        copies[7].start()
        copies[3].wait_recv()
        copies[8].start()
        copies[5].wait_recv()
        copies[9].start()
        copies[6].wait_recv()
        copies[10].start()
        for index in (4, 7, 8, 9, 10):
            copies[index].wait_recv()
        for each in copies:
            each.wait_send()
        self.keep(here, ins[0], outs[0], scratch[2]).wait()


class PlaneScatter(Task):
    def __init__(self, operand, weight, weight_dim):
        rows = operand.shape[0] // 8
        half = rows // 2
        width = weight.shape[1 - weight_dim]
        self.weight_dim = weight_dim
        self.arrays, self.spaces = (operand, weight), (pltpu.VMEM,) * 2
        self.outs, self.out_spaces = (jax.ShapeDtypeStruct((rows, width), f32),), (pltpu.VMEM,)
        self.scratch = (
            pltpu.VMEM((4, rows, width), bf16),
            pltpu.VMEM((4, rows, width), bf16),
            pltpu.VMEM((rows, width), bf16),
            pltpu.VMEM((2, half, width), bf16),
            pltpu.VMEM((2, half, width), bf16),
            pltpu.VMEM((2, half, width), bf16),
            pltpu.VMEM((2, half, width), bf16),
            pltpu.VMEM((2, half, width), bf16),
            pltpu.VMEM((half, width), f32),
            pltpu.VMEM((half, width), f32),
            dma_sems(10),
            dma_sems(10),
        )
        self.reach = (BY_X, BY_Y, BY_CORE)

    def rows_of(self, ins, first, rows):
        return ins[0][pl.ds(first, rows), :]

    def finish(self, here, ins, outs, scratch):
        w_ref, o_ref = ins[1], outs[0]
        (
            sib_out,
            sib_in,
            diag_out,
            diag_in,
            last_x_out,
            last_y_out,
            last_x_in,
            last_y_in,
            wait_x,
            wait_y,
            send_sem,
            recv_sem,
        ) = scratch
        rows = o_ref.shape[0]
        half = rows // 2
        x, y, core = here.x, here.y, here.core
        to_x, to_y, to_core = here.peer(*BY_X), here.peer(*BY_Y), here.peer(*BY_CORE)

        def term(at_core, at_x, at_y):
            first = pl.multiple_of(((2 * at_core + at_y) * 2 + at_x) * rows, rows)
            return lax.dot_general(
                self.rows_of(ins, first, rows),
                w_ref[...],
                (((1,), (self.weight_dim,)), ((), ())),
                preferred_element_type=f32,
            )

        def copy(index, source, target, way):
            return remote(source, target, send_sem.at[index], recv_sem.at[index], way)

        places = ((1 - x, 1 - y), (1 - x, y), (x, 1 - y), (x, y))
        siblings = [copy(i, sib_out.at[i], sib_in.at[i], to_core) for i in range(4)]

        def help_sibling(i):
            sib_out[i] = term(1 - core, *places[i]).astype(bf16)
            siblings[i].start()

        def joined(i):
            mine = term(core, *places[i])
            siblings[i].wait_recv()
            return mine + sib_in[i].astype(f32)

        help_sibling(0)
        help_sibling(1)
        total = joined(0)
        diag_out[...] = total.astype(bf16)
        diag_x = copy(4, diag_out.at[pl.ds(0, half)], diag_in.at[0], to_x)
        diag_y = copy(5, diag_out.at[pl.ds(half, half)], diag_in.at[1], to_y)
        diag_x.start()
        diag_y.start()
        help_sibling(2)
        total = joined(1)
        last_x_out[0] = total[:half].astype(bf16)
        x_0 = copy(6, last_x_out.at[0], last_x_in.at[0], to_x)
        x_0.start()
        wait_x[...] = total[half:]
        total = joined(2)
        last_y_out[1] = total[half:].astype(bf16)
        y_1 = copy(7, last_y_out.at[1], last_y_in.at[1], to_y)
        y_1.start()
        wait_y[...] = total[:half]
        help_sibling(3)
        diag_y.wait_recv()
        last_x_out[1] = (wait_x[...] + diag_in[1].astype(f32)).astype(bf16)
        x_1 = copy(8, last_x_out.at[1], last_x_in.at[1], to_x)
        x_1.start()
        diag_x.wait_recv()
        last_y_out[0] = (wait_y[...] + diag_in[0].astype(f32)).astype(bf16)
        y_0 = copy(9, last_y_out.at[0], last_y_in.at[0], to_y)
        y_0.start()
        o_ref[...] = joined(3)
        for part, (by_x, by_y) in enumerate(((x_0, y_0), (x_1, y_1))):
            by_x.wait_recv()
            by_y.wait_recv()
            piece = pl.ds(part * half, half)
            o_ref[piece, :] += last_x_in[part].astype(f32) + last_y_in[part].astype(f32)
        for sent in (*siblings, diag_x, diag_y, x_0, y_1, x_1, y_0):
            sent.wait_send()


class PlaneSum(Task):
    def __init__(self, values):
        self.arrays, self.spaces = (values,), (pltpu.VMEM,)
        self.outs = (jax.ShapeDtypeStruct(values.shape, f32),)
        self.out_spaces = (pltpu.VMEM,)
        self.scratch = (pltpu.VMEM((7, *values.shape), f32), dma_sems(7), dma_sems(7))
        self.reach = BY_PLANE

    def copies(self, here, ins, scratch):
        got, send_sem, recv_sem = scratch
        return [
            remote(ins[0], got.at[i], send_sem.at[i], recv_sem.at[i], here.peer(*way))
            for i, way in enumerate(BY_PLANE)
        ]

    def start(self, here, ins, outs, scratch):
        for each in self.copies(here, ins, scratch):
            each.start()

    def finish(self, here, ins, outs, scratch):
        copies = self.copies(here, ins, scratch)
        for each in copies:
            each.wait_recv()
        got = scratch[0]
        by_x = [ins[0][...] + got[0]]
        for flip in (2, 4, 6):
            by_x.append(got[flip - 1] + got[flip])
        outs[0][...] = (by_x[0] + by_x[1]) + (by_x[2] + by_x[3])
        for each in copies:
            each.wait_send()


class LineGather(Task):
    def __init__(self, values):
        self.arrays, self.spaces = (values,), (pl.ANY,)
        self.outs = (jax.ShapeDtypeStruct((4, *values.shape), values.dtype),)
        self.out_spaces = (pl.ANY,)
        self.scratch = (dma_sems(4), dma_sems(3))
        self.reach = BY_Z

    def copies(self, here, ins, outs, scratch):
        target = outs[0].at[here.z]
        keep = pltpu.make_async_copy(ins[0], target, scratch[0].at[3])
        return keep, [
            remote(ins[0], target, scratch[0].at[i], scratch[1].at[i], here.peer(*way))
            for i, way in enumerate(BY_Z)
        ]

    def start(self, here, ins, outs, scratch):
        keep, copies = self.copies(here, ins, outs, scratch)
        for each in copies:
            each.start()
        keep.start()

    def finish(self, here, ins, outs, scratch):
        keep, copies = self.copies(here, ins, outs, scratch)
        for each in copies:
            each.wait()
        keep.wait()


class HeadGather(Task):
    def __init__(self, values):
        kinds, wide, half = values.shape
        self.arrays, self.spaces = (values,), (pl.ANY,)
        self.outs = (jax.ShapeDtypeStruct((kinds, 2, wide, 2 * half), values.dtype),)
        self.out_spaces = (pl.ANY,)
        self.scratch = (dma_sems(4), dma_sems(4))
        self.reach = BY_LINE

    def piece(self, outs, shard, part):
        half = outs[0].shape[3] // 2
        return outs[0].at[:, shard, :, pl.ds(pl.multiple_of(part * half, half), half)]

    def copies(self, here, ins, outs, scratch):
        shard, target_core = lax.rem(here.z, 2), here.z // 2
        target = self.piece(outs, shard, here.core)
        recv_sem = scratch[1].at[2 * shard + here.core]
        keep = pltpu.make_async_copy(ins[0], target, recv_sem)
        return keep, [
            remote(
                ins[0],
                target,
                scratch[0].at[step],
                recv_sem,
                {"core": target_core, "z": lax.rem(here.z + step, 4)},
            )
            for step in range(4)
        ]

    def start(self, here, ins, outs, scratch):
        keep, copies = self.copies(here, ins, outs, scratch)
        for each in copies[1:]:
            each.start()
        at_home = here.z // 2 == here.core
        pl.when(at_home)(keep.start)
        pl.when(jnp.logical_not(at_home))(copies[0].start)

    def finish(self, here, ins, outs, scratch):
        keep, copies = self.copies(here, ins, outs, scratch)
        for shard in range(2):
            for part in range(2):
                piece = self.piece(outs, shard, part)
                pltpu.make_async_copy(piece, piece, scratch[1].at[2 * shard + part]).wait()
        for each in copies[1:]:
            each.wait_send()
        pl.when(here.z // 2 != here.core)(copies[0].wait_send)


class LineScatter(Task):
    def __init__(self, values):
        shape = values.shape[1:]
        self.arrays, self.spaces = (values,), (pltpu.VMEM,)
        self.outs, self.out_spaces = (jax.ShapeDtypeStruct(shape, values.dtype),), (pltpu.VMEM,)
        self.scratch = (pltpu.VMEM((3, *shape), values.dtype), dma_sems(3), dma_sems(3))
        self.reach = BY_Z

    def copies(self, here, ins, scratch):
        got, send_sem, recv_sem = scratch
        return [
            remote(
                ins[0].at[lax.rem(here.z + i + 1, 4)],
                got.at[i],
                send_sem.at[i],
                recv_sem.at[i],
                here.peer(*way),
            )
            for i, way in enumerate(BY_Z)
        ]

    def start(self, here, ins, outs, scratch):
        for each in self.copies(here, ins, scratch):
            each.start()

    def finish(self, here, ins, outs, scratch):
        copies = self.copies(here, ins, scratch)
        for each in copies:
            each.wait_recv()
        total = ins[0][here.z].astype(f32)
        for i in range(3):
            total = total + scratch[0][i].astype(f32)
        outs[0][...] = total.astype(outs[0].dtype)
        for each in copies:
            each.wait_send()


class HeadScatter(Task):
    def __init__(self, values):
        kinds, _, wide, width = values.shape
        shape = (kinds, wide, width // 2)
        self.arrays, self.spaces = (values,), (pltpu.VMEM,)
        self.outs, self.out_spaces = (jax.ShapeDtypeStruct(shape, values.dtype),), (pltpu.VMEM,)
        self.scratch = (pltpu.VMEM((4, *shape), values.dtype), dma_sems(4), dma_sems(4))
        self.reach = BY_LINE

    def copies(self, here, ins, scratch):
        got, send_sem, recv_sem = scratch
        half = ins[0].shape[3] // 2
        triples = []
        for shard in range(2):
            for part in range(2):
                source = ins[0].at[:, shard, :, pl.ds(part * half, half)]
                target_z = 2 * here.core + shard
                slot = recv_sem.at[here.z]
                away = remote(
                    source,
                    got.at[here.z],
                    send_sem.at[2 * shard + part],
                    slot,
                    {"core": part, "z": target_z},
                )
                stay = pltpu.make_async_copy(source, got.at[here.z], slot)
                at_home = (target_z == here.z) & (here.core == part)
                triples.append((away, stay, at_home))
        return triples

    def start(self, here, ins, outs, scratch):
        for away, stay, at_home in self.copies(here, ins, scratch):
            pl.when(at_home)(stay.start)
            pl.when(jnp.logical_not(at_home))(away.start)

    def finish(self, here, ins, outs, scratch):
        got, send_sem, recv_sem = scratch
        for plane in range(4):
            pltpu.make_async_copy(got.at[plane], got.at[plane], recv_sem.at[plane]).wait()
        total = got[0].astype(f32)
        for plane in range(1, 4):
            total = total + got[plane].astype(f32)
        outs[0][...] = total.astype(outs[0].dtype)
        for away, stay, at_home in self.copies(here, ins, scratch):
            pl.when(jnp.logical_not(at_home))(away.wait_send)


class RowsGather(Task):
    def __init__(self, values):
        self.arrays, self.spaces = (values,), (pl.ANY,)
        self.outs = (jax.ShapeDtypeStruct((4, *values.shape), values.dtype),)
        self.out_spaces = (pl.ANY,)
        self.scratch = (dma_sems(4), dma_sems(3))
        self.reach = (BY_Y, BY_CORE)

    def copies(self, here, ins, outs, scratch):
        send_sem, recv_sem = scratch
        own = outs[0].at[2 * here.y + here.core]
        over = outs[0].at[2 * (1 - here.y) + here.core]
        to_y, to_core = here.peer(*BY_Y), here.peer(*BY_CORE)
        return (
            pltpu.make_async_copy(ins[0], own, send_sem.at[3]),
            remote(ins[0], own, send_sem.at[0], recv_sem.at[0], to_y),
            remote(ins[0], own, send_sem.at[1], recv_sem.at[1], to_core),
            remote(over, over, send_sem.at[2], recv_sem.at[2], to_core),
        )

    def start(self, here, ins, outs, scratch):
        keep, by_y, by_core, again = self.copies(here, ins, outs, scratch)
        by_y.start()
        by_core.start()
        keep.start()

    def finish(self, here, ins, outs, scratch):
        keep, by_y, by_core, again = self.copies(here, ins, outs, scratch)
        by_y.wait_recv()
        again.start()
        by_core.wait_recv()
        again.wait_recv()
        for each in (by_y, by_core, again):
            each.wait_send()
        keep.wait()


class PlaneThenLineSum(Task):
    def __init__(self, values, ready):
        rows, width = values.shape
        both = (rows + ready.shape[0], width)
        self.plane = PlaneSum(values)
        self.arrays, self.spaces = (values, ready), (pltpu.VMEM,) * 2
        self.outs, self.out_spaces = (jax.ShapeDtypeStruct(both, f32),), (pltpu.VMEM,)
        self.scratch = (
            *self.plane.scratch,
            pltpu.VMEM((4, *both), f32),
            pltpu.VMEM(both, f32),
            dma_sems(3),
            dma_sems(4),
        )
        self.reach = BY_PLANE + BY_Z

    def start(self, here, ins, outs, scratch):
        self.plane.start(here, ins[:1], None, scratch[:3])

    def finish(self, here, ins, outs, scratch):
        got, mine, send_sem, recv_sem = scratch[3:]
        rows = ins[0].shape[0]
        first = ins[1].shape[0]
        self.plane.finish(here, ins[:1], (mine.at[pl.ds(first, rows)],), scratch[:3])
        mine[:first, :] = ins[1][...]
        copies = [
            remote(mine, got.at[here.z], send_sem.at[i], recv_sem.at[here.z], here.peer(*way))
            for i, way in enumerate(BY_Z)
        ]
        for each in copies:
            each.start()
        keep = pltpu.make_async_copy(mine, got.at[here.z], recv_sem.at[here.z])
        keep.start()
        for plane in range(4):
            pltpu.make_async_copy(got.at[plane], got.at[plane], recv_sem.at[plane]).wait()
        outs[0][...] = (got[0] + got[1]) + (got[2] + got[3])
        for each in copies:
            each.wait_send()


BLOCK = 256


def head_masks(head_width, width):
    lane = lax.broadcasted_iota(jnp.int32, (1, width), 1)
    lower = (lane < head_width).astype(bf16)
    return lower, (1 - lower).astype(bf16)


def attend_kernel(head_width, q_ref, k_ref, v_ref, dq_ref, dk_ref, o_ref, l_ref, s_buf, acc, top):
    block = pl.program_id(0)
    width = q_ref.shape[1]
    low_mask, high_mask = head_masks(head_width, width)
    q = q_ref[...]
    pair = jnp.concatenate([q * low_mask, q * high_mask], axis=0)
    top[...] = jnp.full_like(top, masked)

    def scores(at):
        keys = k_ref[pl.ds(pl.multiple_of(at * BLOCK, BLOCK), BLOCK), :]
        return lax.dot_general(pair, keys, (((1,), (1,)), ((), ())), preferred_element_type=f32)

    def first_pass(at, carry):
        s = scores(at)
        s_buf[at] = s
        top[...] = jnp.maximum(top[...], jnp.maximum(s[:, :128], s[:, 128:]))
        return carry

    lax.fori_loop(0, block, first_pass, 0)
    docs = dq_ref[...]
    docs = jnp.concatenate([docs, docs], axis=0)
    place = lax.broadcasted_iota(jnp.int32, (2 * BLOCK, BLOCK), 0)
    place = jnp.where(place >= BLOCK, place - BLOCK, place)
    allowed = (docs == dk_ref[...]) & (
        place >= lax.broadcasted_iota(jnp.int32, (2 * BLOCK, BLOCK), 1)
    )
    s = jnp.where(allowed, scores(block), masked)
    shift = jnp.where(docs == 0, 0.0, masked)
    peak = jnp.maximum(
        jnp.max(top[...], axis=1, keepdims=True) + shift, jnp.max(s, axis=1, keepdims=True)
    )
    p = jnp.exp(s - peak)
    top[...] = p[:, :128] + p[:, 128:]
    values = v_ref[pl.ds(pl.multiple_of(block * BLOCK, BLOCK), BLOCK), :]
    acc[...] = jnp.dot(p.astype(bf16), values, preferred_element_type=f32)
    base = peak - shift

    def second_pass(at, carry):
        p = jnp.exp(s_buf[at] - base)
        top[...] += p[:, :128] + p[:, 128:]
        values = v_ref[pl.ds(pl.multiple_of(at * BLOCK, BLOCK), BLOCK), :]
        acc[...] += jnp.dot(p.astype(bf16), values, preferred_element_type=f32)
        return carry

    lax.fori_loop(0, block, second_pass, 0)
    total = jnp.sum(top[...], axis=1, keepdims=True)
    out = acc[...] / total
    lane = lax.broadcasted_iota(jnp.int32, (BLOCK, width), 1)
    o_ref[...] = jnp.where(lane < head_width, out[:BLOCK], out[BLOCK:])
    logs = jnp.broadcast_to(peak + jnp.log(total), (2 * BLOCK, 128))
    l_ref[0] = jnp.transpose(logs)[0:1, :]


def attend_plane(q, k, v, doc_col, doc_row, head_width):
    rows, width = q.shape
    blocks = rows // BLOCK
    whole = pl.BlockSpec((rows, width), lambda i: (0, 0))
    part = pl.BlockSpec((BLOCK, width), lambda i: (i, 0))
    return pl.pallas_call(
        partial(attend_kernel, head_width),
        grid=(blocks,),
        out_shape=(
            jax.ShapeDtypeStruct((rows, width), f32),
            jax.ShapeDtypeStruct((blocks, 1, 2 * BLOCK), f32),
        ),
        in_specs=[
            part,
            whole,
            whole,
            pl.BlockSpec((BLOCK, 1), lambda i: (i, 0)),
            pl.BlockSpec((1, BLOCK), lambda i: (0, i)),
        ],
        out_specs=(part, pl.BlockSpec((1, 1, 2 * BLOCK), lambda i: (i, 0, 0))),
        scratch_shapes=[
            pltpu.VMEM((blocks, 2 * BLOCK, BLOCK), f32),
            pltpu.VMEM((2 * BLOCK, width), f32),
            pltpu.VMEM((2 * BLOCK, 128), f32),
        ],
        compiler_params=vmem_params(),
    )(q, k, v, doc_col, doc_row)


def attend_back_kernel(
    head_width,
    q_ref,
    k_ref,
    v_ref,
    do_ref,
    o_ref,
    l_ref,
    dcol_ref,
    drow_ref,
    gq_ref,
    gk_ref,
    gv_ref,
    acc_k,
    acc_v,
    acc_q,
):
    block = pl.program_id(0)
    width = q_ref.shape[1]
    low_mask, high_mask = head_masks(head_width, width)
    q = q_ref[...]
    pair_q = jnp.concatenate([q * low_mask, q * high_mask], axis=0)
    do = do_ref[...]
    pair_do = jnp.concatenate([do * low_mask, do * high_mask], axis=0)
    o = o_ref[...]
    inner = jnp.sum(
        jnp.concatenate([o, o], axis=0) * pair_do.astype(f32), axis=1, keepdims=True
    )
    inner = jnp.transpose(jnp.broadcast_to(inner, (2 * BLOCK, 128)))[0:1, :]
    logs = l_ref[0]
    docs = drow_ref[...]
    docs = jnp.concatenate([docs, docs], axis=1)

    @pl.when(block == 0)
    def _():
        acc_k[...] = jnp.zeros_like(acc_k)
        acc_v[...] = jnp.zeros_like(acc_v)

    def step(at, base, allowed):
        piece = pl.ds(pl.multiple_of(at * BLOCK, BLOCK), BLOCK)
        keys = k_ref[piece, :]
        s = lax.dot_general(keys, pair_q, (((1,), (1,)), ((), ())), preferred_element_type=f32)
        p = jnp.exp(s - base)
        if allowed is not None:
            p = jnp.where(allowed, p, 0.0)
        dp = lax.dot_general(
            v_ref[piece, :], pair_do, (((1,), (1,)), ((), ())), preferred_element_type=f32
        )
        ds = (p * (dp - inner)).astype(bf16)
        acc_v[piece, :] += jnp.dot(p.astype(bf16), pair_do, preferred_element_type=f32)
        acc_k[piece, :] += jnp.dot(ds, pair_q, preferred_element_type=f32)
        return lax.dot_general(ds, keys, (((0,), (0,)), ((), ())), preferred_element_type=f32)

    place = lax.broadcasted_iota(jnp.int32, (BLOCK, 2 * BLOCK), 1)
    place = jnp.where(place >= BLOCK, place - BLOCK, place)
    allowed = (docs == dcol_ref[...]) & (
        place >= lax.broadcasted_iota(jnp.int32, (BLOCK, 2 * BLOCK), 0)
    )
    acc_q[...] = step(block, logs, allowed)
    base = jnp.where(docs == 0, logs, -masked)

    def earlier(at, carry):
        acc_q[...] += step(at, base, None)
        return carry

    lax.fori_loop(0, block, earlier, 0)
    lane = lax.broadcasted_iota(jnp.int32, (BLOCK, width), 1)
    grad = jnp.where(lane < head_width, acc_q[:BLOCK, :], acc_q[BLOCK:, :])
    gq_ref[...] = (grad * head_width**-0.5).astype(bf16)

    @pl.when(block == pl.num_programs(0) - 1)
    def _():
        gk_ref[...] = acc_k[...].astype(bf16)
        gv_ref[...] = acc_v[...].astype(bf16)


def attend_plane_back(q, k, v, do, o, logs, doc_col, doc_row, head_width):
    rows, width = q.shape
    blocks = rows // BLOCK
    whole = pl.BlockSpec((rows, width), lambda i: (0, 0))
    part = pl.BlockSpec((BLOCK, width), lambda i: (i, 0))
    return pl.pallas_call(
        partial(attend_back_kernel, head_width),
        grid=(blocks,),
        out_shape=(jax.ShapeDtypeStruct((rows, width), bf16),) * 3,
        in_specs=[
            part,
            whole,
            whole,
            part,
            part,
            pl.BlockSpec((1, 1, 2 * BLOCK), lambda i: (i, 0, 0)),
            pl.BlockSpec((BLOCK, 1), lambda i: (i, 0)),
            pl.BlockSpec((1, BLOCK), lambda i: (0, i)),
        ],
        out_specs=(part, whole, whole),
        scratch_shapes=[
            pltpu.VMEM((rows, width), f32),
            pltpu.VMEM((rows, width), f32),
            pltpu.VMEM((2 * BLOCK, width), f32),
        ],
        compiler_params=vmem_params(),
    )(q, k, v, do, o, logs, doc_col, doc_row)


def plane_device(
    tokens,
    segment_ids,
    cotangent,
    ln_attn_gain,
    ln_attn_bias,
    qkv_weight,
    qv_bias,
    head_scale,
    out_weight,
    out_bias,
    ln_post_gain,
    ln_post_bias,
    ln_ffn_gain,
    ln_ffn_bias,
    fc1_weight,
    fc1_bias,
    mid_gain,
    mid_bias,
    fc2_weight,
    fc2_bias,
):
    layers = qkv_weight.shape[0]
    model_width = tokens.shape[1]
    heads_all = head_scale.shape[1]
    head_width = model_width // heads_all
    hidden_here = fc1_weight.shape[2]
    hidden_all = hidden_here * 8
    quarter = hidden_here // 4
    half_width = model_width // 2
    x, y, core = lax.axis_index("x"), lax.axis_index("y"), lax.axis_index("core")
    quarter_at = 2 * y + core
    factor = head_width**-0.5

    residual = to_plane(tokens).astype(f32)
    docs = to_plane(segment_ids)
    doc_col, doc_row = docs[:, None], docs[None, :]
    gradient = to_plane(cotangent).astype(f32)

    def cut(values, at, size, axis):
        return lax.dynamic_slice_in_dim(values, at * size, size, axis)

    head_parts, first_parts, second_parts = [], [], []
    for layer in range(layers):
        qkv = cut(cut(qkv_weight[layer], core, half_width, 0), y, head_width, 2)
        out = cut(cut(out_weight[layer], y, head_width, 0), core, half_width, 1)
        head_parts.append(jnp.concatenate([jnp.transpose(qkv, (1, 2, 0)), out[None]], axis=0))
        first_parts.append(cut(fc1_weight[layer], quarter_at, quarter, 1).T)
        second_parts.append(cut(fc2_weight[layer], quarter_at, quarter, 0))
    small = jnp.concatenate(
        [
            cut(qv_bias, y, head_width, 2).reshape(layers, 2 * head_width),
            cut(fc1_bias, quarter_at, quarter, 1),
            cut(mid_gain, quarter_at, quarter, 1),
            cut(mid_bias, quarter_at, quarter, 1),
        ],
        axis=1,
    )
    head_ids = ((2 * core + jnp.arange(2)) * 2 + x) * 2 + y
    head_onehot = (head_ids[:, None] == jnp.arange(heads_all)[None, :]).astype(f32)
    width = 2 * head_width
    heads_here, first_here, second_here = [None] * layers, [None] * layers, [None] * layers

    ids = iter(range(1, 64))

    def plane_sum(values):
        return run_tasks(ids, PlaneSum(values))[0][0]

    stored = []
    for layer in range(layers):
        attn_in, attn_normal, attn_factor = norm_local(
            residual, ln_attn_gain[layer], ln_attn_bias[layer]
        )
        if layer == 0:
            ((attn_rows,), (heads_here[0],), (small,)) = run_tasks(
                ids, PlaneGather(attn_in.astype(bf16)), HeadGather(head_parts[0]), LineGather(small)
            )
            bias_heads = lax.dynamic_slice_in_dim(small[:, :, :width], 2 * core, 2, 0)
            bias_heads = jnp.transpose(
                bias_heads.reshape(2, layers, 2, head_width), (1, 2, 0, 3)
            ).reshape(layers, 2, width)

            def hidden_rows(at):
                part = small[:, :, width + at * quarter : width + (at + 1) * quarter]
                return jnp.transpose(part, (1, 0, 2)).reshape(layers, 4 * quarter)

            shift_hidden, gain_hidden, bias_hidden = map(hidden_rows, range(3))
            beside = [(first_parts, first_here, 0), (second_parts, second_here, 0)]
            beside += [(head_parts, heads_here, 1)]
        else:
            ((attn_rows,), (first,)) = run_tasks(
                ids, PlaneGather(attn_in.astype(bf16)), LineGather(first_parts[layer])
            )
            first_here[layer] = first.reshape(4 * quarter, model_width)
            beside = [(second_parts, second_here, 1), None, None]
        qkv_here = heads_here[layer][:3].reshape(3 * width, model_width)
        out_here = heads_here[layer][3].reshape(width, model_width)

        def with_weights(main, item):
            if item is None:
                return run_tasks(ids, main)[0][0]
            parts, here_list, at = item
            kind = HeadGather if parts is head_parts else LineGather
            ((result,), (got,)) = run_tasks(ids, main, kind(parts[at]))
            here_list[at] = got if kind is HeadGather else got.reshape(4 * quarter, model_width)
            return result

        projected = jnp.einsum("td,cd->tc", attn_rows, qkv_here, preferred_element_type=f32)
        q = (projected[:, :width] + bias_heads[layer, 0]).astype(bf16) * factor
        q = q.astype(bf16)
        k = projected[:, width : 2 * width].astype(bf16)
        v = (projected[:, 2 * width :] + bias_heads[layer, 1]).astype(bf16)
        attended, logs = attend_plane(q, k, v, doc_col, doc_row, head_width)
        scale = jnp.sum(head_onehot * head_scale[layer][None, :], axis=1)
        scale_row = jnp.repeat(scale, head_width)[None, :]
        scaled = (attended * scale_row).astype(bf16)
        branch = with_weights(PlaneScatter(scaled, out_here, 0), beside[0])
        branch = branch + out_bias[layer]
        post_out, post_normal, post_factor = norm_local(
            branch, ln_post_gain[layer], ln_post_bias[layer]
        )
        middle = residual + post_out
        ffn_in, ffn_normal, ffn_factor = norm_local(middle, ln_ffn_gain[layer], ln_ffn_bias[layer])
        ffn_rows = with_weights(
            PlaneGather(ffn_in.astype(bf16)), beside[1]
        )
        before = jnp.einsum("td,fd->tf", ffn_rows, first_here[layer], preferred_element_type=f32)
        before = before + shift_hidden[layer]
        activated = jax.nn.gelu(before, approximate=False)
        sums = plane_sum(
            jnp.stack([jnp.sum(activated, axis=1), jnp.sum(activated * activated, axis=1)])
        )
        average = sums[0] / hidden_all
        spread = sums[1] / hidden_all - average * average
        hidden_factor = lax.rsqrt(spread + epsilon)[:, None]
        hidden_normal = (activated - average[:, None]) * hidden_factor
        mixed = (hidden_normal * gain_hidden[layer] + bias_hidden[layer]).astype(bf16)
        ffn_out = with_weights(
            PlaneScatter(mixed, second_here[layer], 0), beside[2]
        )
        stored.append(
            (
                qkv_here,
                out_here,
                attn_normal,
                attn_factor,
                attn_rows,
                q,
                k,
                v,
                attended,
                logs,
                scale_row,
                scaled,
                post_normal,
                post_factor,
                ffn_normal,
                ffn_factor,
                ffn_rows,
                before,
                hidden_normal,
                hidden_factor,
                mixed,
            )
        )
        residual = middle + ffn_out + fc2_bias[layer]
    layer_output = from_plane(residual.astype(bf16))

    def by_shard(grad):
        return grad.astype(bf16).reshape(4, quarter, model_width)

    def ffn_shard(grad):
        return grad.reshape(4 * quarter, model_width).astype(f32)

    def head_shard(grad):
        full = grad.reshape(2, 2, 4, head_width, half_width).astype(f32)
        qkv = jnp.transpose(full[:, :, :3], (1, 4, 2, 0, 3))
        out = jnp.transpose(full[:, :, 3], (0, 2, 1, 3))
        return (
            qkv.reshape(model_width, 3, 2 * head_width),
            out.reshape(2 * head_width, model_width),
        )

    pending = None
    first_done, second_done = [None] * layers, [None] * layers
    heads_done, hidden_done = [None] * layers, [None] * layers
    vector_grads = [None] * layers
    norm_grads = []
    for layer in reversed(range(layers)):
        (
            qkv_here,
            out_here,
            attn_normal,
            attn_factor,
            attn_rows,
            q,
            k,
            v,
            attended,
            logs,
            scale_row,
            scaled,
            post_normal,
            post_factor,
            ffn_normal,
            ffn_factor,
            ffn_rows,
            before,
            hidden_normal,
            hidden_factor,
            mixed,
        ) = stored[layer]
        second_shift_grad = jnp.sum(gradient, axis=0)
        sides = [] if pending is None else [RowsGather(each) for each in pending]
        ((grad_rows,), *got) = run_tasks(ids, PlaneGather(gradient.astype(bf16)), *sides)
        if pending is not None:
            heads_done[layer + 1], hidden_done[layer + 1] = got[0][0], got[1][0]
        mixed_grad = jnp.einsum(
            "td,fd->tf", grad_rows, second_here[layer], preferred_element_type=f32
        )
        second_grad = jnp.einsum("tf,td->fd", mixed, grad_rows, preferred_element_type=f32)
        hidden_gain_grad = jnp.sum(mixed_grad * hidden_normal, axis=0)
        hidden_shift_grad = jnp.sum(mixed_grad, axis=0)
        normal_grad = mixed_grad * gain_hidden[layer]
        sums = plane_sum(
            jnp.stack(
                [jnp.sum(normal_grad, axis=1), jnp.sum(normal_grad * hidden_normal, axis=1)]
            )
        )
        active_grad = hidden_factor * (
            normal_grad
            - sums[0][:, None] / hidden_all
            - hidden_normal * sums[1][:, None] / hidden_all
        )
        gelu_pull = jax.vjp(partial(jax.nn.gelu, approximate=False), before)[1]
        pre_grad = gelu_pull(active_grad)[0].astype(bf16)
        first_shift_grad = jnp.sum(pre_grad, axis=0, dtype=f32)
        first_grad = jnp.einsum("tf,td->fd", pre_grad, ffn_rows, preferred_element_type=f32)
        ((ffn_in_grad,), (second_grad,)) = run_tasks(
            ids, PlaneScatter(pre_grad, first_here[layer], 0), LineScatter(by_shard(second_grad))
        )
        ffn_gain_grad = jnp.sum(ffn_in_grad * ffn_normal, axis=0)
        ffn_bias_grad = jnp.sum(ffn_in_grad, axis=0)
        middle_grad = gradient + norm_back(ffn_in_grad, ffn_normal, ffn_factor, ln_ffn_gain[layer])
        post_gain_grad = jnp.sum(middle_grad * post_normal, axis=0)
        post_bias_grad = jnp.sum(middle_grad, axis=0)
        branch_grad = norm_back(middle_grad, post_normal, post_factor, ln_post_gain[layer])
        out_shift_grad = jnp.sum(branch_grad, axis=0)
        ((branch_rows,), (first_grad,), (second_grad,)) = run_tasks(
            ids,
            PlaneGather(branch_grad.astype(bf16)),
            LineScatter(by_shard(first_grad)),
            RowsGather(second_grad),
        )
        second_done[layer] = second_grad
        scaled_grad = jnp.einsum("td,cd->tc", branch_rows, out_here, preferred_element_type=f32)
        out_grad = jnp.einsum("tc,td->cd", scaled, branch_rows, preferred_element_type=f32)
        scale_cols = jnp.sum(attended * scaled_grad, axis=0)
        scale_grad = jnp.sum(
            head_onehot * jnp.sum(scale_cols.reshape(2, head_width), axis=1)[:, None], axis=0
        )
        attended_grad = (scaled_grad * scale_row).astype(bf16)
        gq, gk, gv = attend_plane_back(
            q, k, v, attended_grad, attended, logs, doc_col, doc_row, head_width
        )
        proj_grad = jnp.concatenate([gq, gk, gv], axis=1)
        bias_grad = jnp.stack(
            [jnp.sum(gq, axis=0, dtype=f32), jnp.sum(gv, axis=0, dtype=f32)], axis=0
        )
        qkv_grad = jnp.einsum("tc,td->cd", proj_grad, attn_rows, preferred_element_type=f32)
        heads_grad = jnp.concatenate([qkv_grad.astype(bf16), out_grad.astype(bf16)], axis=0)
        heads_grad = heads_grad.reshape(4, 2, head_width, model_width)
        bias_grad = jnp.transpose(bias_grad.reshape(2, 2, head_width), (1, 0, 2))
        hidden_grad = jnp.stack([first_shift_grad, hidden_gain_grad, hidden_shift_grad])
        hidden_grad = jnp.concatenate(
            [
                jnp.transpose(hidden_grad.reshape(3, 4, quarter), (1, 0, 2)).reshape(4, -1),
                lax.dynamic_update_slice(
                    jnp.zeros((4, width), f32), bias_grad.reshape(2, width), (2 * core, 0)
                ),
            ],
            axis=1,
        ).reshape(4, -1, 128)
        vector_grads[layer] = jnp.stack(
            [
                out_shift_grad,
                post_gain_grad,
                post_bias_grad,
                ffn_gain_grad,
                ffn_bias_grad,
                second_shift_grad,
                jnp.pad(scale_grad, (0, model_width - heads_all)),
            ]
        )
        sides = [HeadScatter(heads_grad), LineScatter(hidden_grad), RowsGather(first_grad)]
        if layer == 0:
            early = [vector_grads[each] for each in range(layers)] + norm_grads
            sides.append(PlaneSum(jnp.concatenate(early, axis=0)))
        ((attn_in_grad,), (heads_grad,), (hidden_grad,), (first_grad,), *rest) = run_tasks(
            ids, PlaneScatter(proj_grad, qkv_here, 0), *sides
        )
        pending = (heads_grad, hidden_grad)
        first_done[layer] = first_grad
        attn_norm_grads = jnp.stack(
            [jnp.sum(attn_in_grad * attn_normal, axis=0), jnp.sum(attn_in_grad, axis=0)]
        )
        norm_grads.insert(0, attn_norm_grads)
        gradient = middle_grad + norm_back(
            attn_in_grad, attn_normal, attn_factor, ln_attn_gain[layer]
        )
    input_grad = from_plane(gradient.astype(bf16)).astype(f32)
    ((vectors,), *got) = run_tasks(
        ids,
        PlaneThenLineSum(norm_grads[0], rest[0][0]),
        RowsGather(pending[0]),
        RowsGather(pending[1]),
    )
    heads_done[0], hidden_done[0] = got[0][0], got[1][0]
    per_layer = vectors[: 7 * layers].reshape(layers, 7, model_width)
    later = vectors[7 * layers :].reshape(layers, 2, model_width)[::-1]
    heads_done = [head_shard(each) for each in heads_done]
    hidden = jnp.stack(hidden_done).reshape(layers, 4, -1)
    bias_grad = jnp.sum(hidden[:, :, 3 * quarter :].reshape(layers, 2, 2, 2, head_width), axis=2)
    bias_grad = jnp.transpose(bias_grad, (0, 2, 1, 3)).reshape(layers, 2, width)
    hidden = hidden[:, :, : 3 * quarter].reshape(layers, 4, 3, quarter)
    hidden = jnp.transpose(hidden, (0, 2, 1, 3)).reshape(layers, 3, hidden_here)
    return (
        layer_output,
        input_grad,
        later[:, 0],
        later[:, 1],
        jnp.stack([each[0] for each in heads_done]),
        bias_grad,
        per_layer[:, 6, :heads_all],
        jnp.stack([each[1] for each in heads_done]),
        per_layer[:, 0],
        per_layer[:, 1],
        per_layer[:, 2],
        per_layer[:, 3],
        per_layer[:, 4],
        jnp.stack([ffn_shard(each).T for each in first_done]),
        hidden[:, 0],
        hidden[:, 1],
        hidden[:, 2],
        jnp.stack([ffn_shard(each) for each in second_done]),
        per_layer[:, 5],
    )


def split_specs(rows, mp):
    both = tuple(rows) + tuple(mp)
    in_specs = (
        P(both, None),
        P(rows),
        P(both, None),
        P(),
        P(),
        P(None, None, None, mp),
        P(None, None, mp),
        P(),
        P(None, mp, None),
        P(),
        P(),
        P(),
        P(),
        P(),
        P(None, None, mp),
        P(None, mp),
        P(None, mp),
        P(None, mp),
        P(None, mp, None),
        P(),
    )
    out_specs = (
        P(both, None),
        P(both, None),
        P(),
        P(),
        P(None, None, None, mp),
        P(None, None, mp),
        P(),
        P(None, mp, None),
        P(),
        P(),
        P(),
        P(),
        P(),
        P(None, None, mp),
        P(None, mp),
        P(None, mp),
        P(None, mp),
        P(None, mp, None),
        P(),
    )
    return in_specs, out_specs


def solution(mesh):
    if mesh.shape["rows"] == 4 and mesh.shape["mp"] == 8:
        planes = Mesh(mesh.devices.reshape(2, 2, 4, 2), ("y", "core", "z", "x"))
        in_specs, out_specs = split_specs(("y", "core"), ("z", "x"))
        return jax.shard_map(
            plane_device, mesh=planes, in_specs=in_specs, out_specs=out_specs, check_vma=False
        )
    in_specs, out_specs = split_specs(("rows",), ("mp",))
    return jax.shard_map(
        per_device, mesh=mesh, in_specs=in_specs, out_specs=out_specs, check_vma=False
    )
```

```python
from functools import partial

import jax
import jax.numpy as jnp
from jax import lax
from jax.experimental import pallas as pl
from jax.experimental.pallas import tpu as pltpu
from jax.sharding import Mesh
from jax.sharding import PartitionSpec as P

epsilon = 1e-05
masked = -1e30


def partner(shard, axis, stride):
    return lax.ppermute(shard, axis, [(i, i ^ 1 << stride) for i in range(lax.axis_size(axis))])


def norm_local(values, gain_row, bias_row):
    average = jnp.mean(values, axis=-1, keepdims=True)
    centered = values - average
    spread = jnp.mean(centered * centered, axis=-1, keepdims=True)
    factor = lax.rsqrt(spread + epsilon)
    normal = centered * factor
    return (normal * gain_row + bias_row, normal, factor)


def norm_back(grad_out, normal, factor, gain_row):
    scaled = grad_out * gain_row
    inner_sum = jnp.mean(scaled * normal, axis=-1, keepdims=True)
    return factor * (scaled - jnp.mean(scaled, axis=-1, keepdims=True) - normal * inner_sum)


def collect_rows(normed_b):
    return lax.all_gather(normed_b, "mp", axis=0, tiled=True)


def collect_grads(gradient_b):
    return lax.all_gather(gradient_b, "mp", axis=0, tiled=True)


def reduce_branch(operand_b, weight_b, local_rows):

    def partial_term(first_row, count):
        return jnp.dot(operand_b, weight_b, preferred_element_type=jnp.float32)

    return lax.psum_scatter(
        partial_term(jnp.int32(0), local_rows * lax.axis_size("mp")).astype(jnp.bfloat16),
        "mp",
        scatter_dimension=0,
        tiled=True,
    ).astype(jnp.float32)


def reduce_grads(operand_b, weight_b, local_rows):

    def partial_term(first_row, count):
        return jnp.einsum("tc,dc->td", operand_b, weight_b, preferred_element_type=jnp.float32)

    return lax.psum_scatter(
        partial_term(jnp.int32(0), local_rows * lax.axis_size("mp")).astype(jnp.bfloat16),
        "mp",
        scatter_dimension=0,
        tiled=True,
    ).astype(jnp.float32)


def hidden_stats(first_sum, second_sum):
    return lax.psum((first_sum, second_sum), "mp")


def hidden_grad_stats(first_sum, second_sum):
    return lax.psum((first_sum, second_sum), "mp")


def join_cols(mine, other, is_upper):
    lower_part = jnp.where(is_upper, other, mine)
    upper_part = jnp.where(is_upper, mine, other)
    return jnp.concatenate([lower_part, upper_part], axis=-1)


def join_rows(mine, other, is_upper):
    lower_part = jnp.where(is_upper, other, mine)
    upper_part = jnp.where(is_upper, mine, other)
    return jnp.concatenate([lower_part, upper_part], axis=0)


def split_cols(values, cols_here, is_upper):
    lower_part = values[..., :cols_here]
    upper_part = values[..., cols_here:]
    return (
        jnp.where(is_upper, upper_part, lower_part),
        jnp.where(is_upper, lower_part, upper_part),
    )


def masked_scores(query_block, key_rows, query_start, block_rows, doc_rows, positions):
    factor = query_block.shape[-1] ** (-0.5)
    scores = (
        jnp.einsum("qhe,khe->hqk", query_block, key_rows, preferred_element_type=jnp.float32)
        * factor
    )
    query_place = query_start + jnp.arange(block_rows, dtype=jnp.int32)
    query_docs = lax.dynamic_slice_in_dim(doc_rows, query_start, block_rows, 0)
    allowed = (query_docs[:, None] == doc_rows[None, :]) & (
        query_place[:, None] >= positions[None, :]
    )
    return jnp.where(allowed[None], scores, masked)


def attend_forward(queries, key_rows, value_rows, doc_rows, row_offset):
    total_rows = queries.shape[0]
    block_rows = min(512, total_rows)
    positions = jnp.arange(key_rows.shape[0], dtype=jnp.int32)

    def one_block(first_row):
        query_block = lax.dynamic_slice_in_dim(queries, first_row, block_rows, 0)
        scores = masked_scores(
            query_block, key_rows, row_offset + first_row, block_rows, doc_rows, positions
        )
        row_peak = jnp.max(scores, axis=-1, keepdims=True)
        weights = jnp.exp(scores - row_peak)
        totals = jnp.sum(weights, axis=-1, keepdims=True)
        probabilities = (weights / totals).astype(jnp.bfloat16)
        output = jnp.einsum(
            "hqk,khe->qhe", probabilities, value_rows, preferred_element_type=jnp.float32
        )
        return (output, (row_peak + jnp.log(totals))[..., 0])

    starts = jnp.arange(total_rows // block_rows, dtype=jnp.int32) * block_rows
    outputs, log_totals = lax.map(one_block, starts)
    return (outputs.reshape(queries.shape), log_totals)


def attend_backward(queries, key_rows, value_rows, doc_rows, row_offset, log_totals, grad_out):
    total_rows = queries.shape[0]
    block_rows = min(512, total_rows)
    positions = jnp.arange(key_rows.shape[0], dtype=jnp.int32)
    factor = queries.shape[-1] ** (-0.5)

    def one_block(running, first_row):
        key_grad, value_grad = running
        query_block = lax.dynamic_slice_in_dim(queries, first_row, block_rows, 0)
        grad_block = lax.dynamic_slice_in_dim(grad_out, first_row, block_rows, 0)
        scores = masked_scores(
            query_block, key_rows, row_offset + first_row, block_rows, doc_rows, positions
        )
        block_totals = lax.dynamic_index_in_dim(
            log_totals, first_row // block_rows, 0, keepdims=False
        )
        probabilities = jnp.exp(scores - block_totals[..., None])
        prob_grad = jnp.einsum(
            "qhe,khe->hqk", grad_block, value_rows, preferred_element_type=jnp.float32
        )
        inner_sum = jnp.sum(probabilities * prob_grad, axis=-1, keepdims=True)
        score_grad = (probabilities * (prob_grad - inner_sum)).astype(jnp.bfloat16)
        query_grad = (
            jnp.einsum("hqk,khe->qhe", score_grad, key_rows, preferred_element_type=jnp.float32)
            * factor
        )
        key_grad = (
            key_grad
            + jnp.einsum(
                "hqk,qhe->khe", score_grad, query_block, preferred_element_type=jnp.float32
            )
            * factor
        )
        value_grad = value_grad + jnp.einsum(
            "hqk,qhe->khe",
            probabilities.astype(jnp.bfloat16),
            grad_block,
            preferred_element_type=jnp.float32,
        )
        return ((key_grad, value_grad), query_grad)

    starts = jnp.arange(total_rows // block_rows, dtype=jnp.int32) * block_rows
    zero_grads = jnp.zeros(key_rows.shape, jnp.float32)
    (key_grad, value_grad), query_grads = lax.scan(one_block, (zero_grads, zero_grads), starts)
    return (query_grads.reshape(queries.shape), key_grad, value_grad)


def stack_layers(layer_list, members):
    stacked = []
    for member_index in range(members):
        stacked.append(jnp.stack([entry[member_index] for entry in layer_list], axis=0))
    return stacked


def per_device(
    tokens,
    segment_ids,
    cotangent,
    ln_attn_gain,
    ln_attn_bias,
    qkv_weight,
    qv_bias,
    head_scale,
    out_weight,
    out_bias,
    ln_post_gain,
    ln_post_bias,
    ln_ffn_gain,
    ln_ffn_bias,
    fc1_weight,
    fc1_bias,
    mid_gain,
    mid_bias,
    fc2_weight,
    fc2_bias,
):
    layers = qkv_weight.shape[0]
    local_rows = tokens.shape[0]
    model_width = tokens.shape[1]
    cols_here = qkv_weight.shape[3]
    heads_all = head_scale.shape[1]
    head_width = model_width // heads_all
    pair_cols = 2 * cols_here
    pair_heads = pair_cols // head_width
    group_rows = segment_ids.shape[0]
    half_rows = group_rows // 2
    hidden_all = fc1_weight.shape[2] * lax.axis_size("mp")
    device_index = lax.axis_index("mp")
    is_upper = device_index % 2 == 1
    own_start = jnp.where(is_upper, half_rows, 0).astype(jnp.int32)
    other_start = jnp.where(is_upper, 0, half_rows).astype(jnp.int32)
    first_head = device_index // 2 * pair_heads
    pair_onehot = (
        (first_head + jnp.arange(pair_heads, dtype=jnp.int32))[:, None]
        == jnp.arange(heads_all, dtype=jnp.int32)[None, :]
    ).astype(jnp.float32)
    residual = tokens.astype(jnp.float32)
    stored = []
    for layer_index in range(layers):
        attn_in, attn_normal, attn_factor = norm_local(
            residual, ln_attn_gain[layer_index], ln_attn_bias[layer_index]
        )
        attn_rows = collect_rows(attn_in.astype(jnp.bfloat16))
        qkv_here = qkv_weight[layer_index].reshape(model_width, 3 * cols_here)
        projected = jnp.dot(attn_rows, qkv_here, preferred_element_type=jnp.float32).reshape(
            -1, 3, cols_here
        )
        bias_pair = qv_bias[layer_index]
        query_mine = (projected[:, 0] + bias_pair[0]).astype(jnp.bfloat16)
        key_mine = projected[:, 1].astype(jnp.bfloat16)
        value_mine = (projected[:, 2] + bias_pair[1]).astype(jnp.bfloat16)
        query_send = lax.dynamic_slice_in_dim(query_mine, other_start, half_rows, 0)
        query_recv, key_recv, value_recv = partner((query_send, key_mine, value_mine), "mp", 0)
        query_own = lax.dynamic_slice_in_dim(query_mine, own_start, half_rows, 0)
        queries = join_cols(query_own, query_recv, is_upper).reshape(
            half_rows, pair_heads, head_width
        )
        key_rows = join_cols(key_mine, key_recv, is_upper).reshape(
            group_rows, pair_heads, head_width
        )
        value_rows = join_cols(value_mine, value_recv, is_upper).reshape(
            group_rows, pair_heads, head_width
        )
        attended, log_totals = attend_forward(queries, key_rows, value_rows, segment_ids, own_start)
        pair_scale = jnp.sum(pair_onehot * head_scale[layer_index][None, :], axis=1)
        scaled_half = (
            (attended * pair_scale[None, :, None])
            .astype(jnp.bfloat16)
            .reshape(half_rows, pair_cols)
        )
        own_cols, other_cols = split_cols(scaled_half, cols_here, is_upper)
        scaled_recv = partner(other_cols, "mp", 0)
        scaled_mine = join_rows(own_cols, scaled_recv, is_upper)
        branch = (
            reduce_branch(scaled_mine, out_weight[layer_index], local_rows) + out_bias[layer_index]
        )
        post_out, post_normal, post_factor = norm_local(
            branch, ln_post_gain[layer_index], ln_post_bias[layer_index]
        )
        middle = residual + post_out
        ffn_in, ffn_normal, ffn_factor = norm_local(
            middle, ln_ffn_gain[layer_index], ln_ffn_bias[layer_index]
        )
        ffn_rows = collect_rows(ffn_in.astype(jnp.bfloat16))
        before_gelu = (
            jnp.dot(ffn_rows, fc1_weight[layer_index], preferred_element_type=jnp.float32)
            + fc1_bias[layer_index]
        )
        activated = jax.nn.gelu(before_gelu, approximate=False)
        first_sum, second_sum = hidden_stats(
            jnp.sum(activated, axis=1), jnp.sum(activated * activated, axis=1)
        )
        average = first_sum / hidden_all
        spread = second_sum / hidden_all - average * average
        hidden_factor = lax.rsqrt(spread + epsilon)[:, None]
        hidden_normal = (activated - average[:, None]) * hidden_factor
        mixed_b = (hidden_normal * mid_gain[layer_index] + mid_bias[layer_index]).astype(
            jnp.bfloat16
        )
        ffn_out = reduce_branch(mixed_b, fc2_weight[layer_index], local_rows)
        stored.append(
            (
                attn_normal,
                attn_factor,
                attn_rows,
                queries,
                key_rows,
                value_rows,
                attended,
                log_totals,
                pair_scale,
                scaled_mine,
                post_normal,
                post_factor,
                ffn_normal,
                ffn_factor,
                ffn_rows,
                before_gelu,
                hidden_normal,
                hidden_factor,
                mixed_b,
            )
        )
        residual = middle + ffn_out + fc2_bias[layer_index]
    layer_output = residual.astype(jnp.bfloat16)
    gradient = cotangent.astype(jnp.float32)
    sharded_list = []
    shared_list = []
    for layer_index in reversed(range(layers)):
        (
            attn_normal,
            attn_factor,
            attn_rows,
            queries,
            key_rows,
            value_rows,
            attended,
            log_totals,
            pair_scale,
            scaled_mine,
            post_normal,
            post_factor,
            ffn_normal,
            ffn_factor,
            ffn_rows,
            before_gelu,
            hidden_normal,
            hidden_factor,
            mixed_b,
        ) = stored[layer_index]
        qkv_here = qkv_weight[layer_index].reshape(model_width, 3 * cols_here)
        second_shift_grad = jnp.sum(gradient, axis=0)
        grad_rows = collect_grads(gradient.astype(jnp.bfloat16))
        mixed_grad = jnp.einsum(
            "td,fd->tf", grad_rows, fc2_weight[layer_index], preferred_element_type=jnp.float32
        )
        second_grad = jnp.einsum(
            "tf,td->fd", mixed_b, grad_rows, preferred_element_type=jnp.float32
        )
        hidden_gain_grad = jnp.sum(mixed_grad * hidden_normal, axis=0)
        hidden_shift_grad = jnp.sum(mixed_grad, axis=0)
        normal_grad = mixed_grad * mid_gain[layer_index]
        grad_first, grad_second = hidden_grad_stats(
            jnp.sum(normal_grad, axis=1), jnp.sum(normal_grad * hidden_normal, axis=1)
        )
        active_grad = hidden_factor * (
            normal_grad
            - grad_first[:, None] / hidden_all
            - hidden_normal * grad_second[:, None] / hidden_all
        )
        gelu_pull = jax.vjp(partial(jax.nn.gelu, approximate=False), before_gelu)[1]
        pre_grad_b = gelu_pull(active_grad)[0].astype(jnp.bfloat16)
        first_shift_grad = jnp.sum(pre_grad_b, axis=0, dtype=jnp.float32)
        first_grad = jnp.einsum(
            "td,tf->df", ffn_rows, pre_grad_b, preferred_element_type=jnp.float32
        )
        ffn_in_grad = reduce_grads(pre_grad_b, fc1_weight[layer_index], local_rows)
        ffn_gain_grad = jnp.sum(ffn_in_grad * ffn_normal, axis=0)
        ffn_bias_grad = jnp.sum(ffn_in_grad, axis=0)
        middle_grad = gradient + norm_back(
            ffn_in_grad, ffn_normal, ffn_factor, ln_ffn_gain[layer_index]
        )
        post_gain_grad = jnp.sum(middle_grad * post_normal, axis=0)
        post_bias_grad = jnp.sum(middle_grad, axis=0)
        branch_grad = norm_back(middle_grad, post_normal, post_factor, ln_post_gain[layer_index])
        out_shift_grad = jnp.sum(branch_grad, axis=0)
        branch_rows = collect_grads(branch_grad.astype(jnp.bfloat16))
        scaled_grad = jnp.einsum(
            "td,cd->tc", branch_rows, out_weight[layer_index], preferred_element_type=jnp.float32
        )
        out_grad = jnp.einsum(
            "tc,td->cd", scaled_mine, branch_rows, preferred_element_type=jnp.float32
        )
        grad_send = lax.dynamic_slice_in_dim(scaled_grad, other_start, half_rows, 0)
        grad_recv = partner(grad_send.astype(jnp.bfloat16), "mp", 0).astype(grad_send.dtype)
        grad_own = lax.dynamic_slice_in_dim(scaled_grad, own_start, half_rows, 0)
        scaled_pair = join_cols(grad_own, grad_recv, is_upper).reshape(
            half_rows, pair_heads, head_width
        )
        pair_scale_grad = jnp.sum(attended * scaled_pair, axis=(0, 2))
        scale_grad = jnp.sum(pair_onehot * pair_scale_grad[:, None], axis=0)
        attended_grad_b = (scaled_pair * pair_scale[None, :, None]).astype(jnp.bfloat16)
        query_grad, key_grad, value_grad = attend_backward(
            queries, key_rows, value_rows, segment_ids, own_start, log_totals, attended_grad_b
        )
        query_own, query_other = split_cols(
            query_grad.reshape(half_rows, pair_cols), cols_here, is_upper
        )
        key_own, key_other = split_cols(
            key_grad.reshape(group_rows, pair_cols), cols_here, is_upper
        )
        value_own, value_other = split_cols(
            value_grad.reshape(group_rows, pair_cols), cols_here, is_upper
        )
        query_recv, key_recv, value_recv = (
            partner(query_other.astype(jnp.bfloat16), "mp", 0).astype(query_other.dtype),
            partner(key_other.astype(jnp.bfloat16), "mp", 0).astype(key_other.dtype),
            partner(value_other.astype(jnp.bfloat16), "mp", 0).astype(value_other.dtype),
        )
        query_grad_b = join_rows(query_own, query_recv, is_upper).astype(jnp.bfloat16)
        key_grad_b = (key_own + key_recv).astype(jnp.bfloat16)
        value_grad_b = (value_own + value_recv).astype(jnp.bfloat16)
        proj_grad = jnp.stack([query_grad_b, key_grad_b, value_grad_b], axis=1).reshape(
            -1, 3 * cols_here
        )
        pair_grad = jnp.stack(
            [
                jnp.sum(query_grad_b, axis=0, dtype=jnp.float32),
                jnp.sum(value_grad_b, axis=0, dtype=jnp.float32),
            ],
            axis=0,
        )
        qkv_grad = jnp.einsum(
            "td,tc->dc", attn_rows, proj_grad, preferred_element_type=jnp.float32
        ).reshape(model_width, 3, cols_here)
        attn_in_grad = reduce_grads(proj_grad, qkv_here, local_rows)
        attn_gain_grad = jnp.sum(attn_in_grad * attn_normal, axis=0)
        attn_bias_grad = jnp.sum(attn_in_grad, axis=0)
        gradient = middle_grad + norm_back(
            attn_in_grad, attn_normal, attn_factor, ln_attn_gain[layer_index]
        )
        sharded_list.insert(
            0,
            (
                qkv_grad,
                pair_grad,
                out_grad,
                first_grad,
                first_shift_grad,
                hidden_gain_grad,
                hidden_shift_grad,
                second_grad,
            ),
        )
        shared_list.insert(
            0,
            (
                attn_gain_grad,
                attn_bias_grad,
                scale_grad,
                out_shift_grad,
                post_gain_grad,
                post_bias_grad,
                ffn_gain_grad,
                ffn_bias_grad,
                second_shift_grad,
            ),
        )
    sharded = stack_layers(sharded_list, 8)
    shared = stack_layers(shared_list, 9)
    sharded = (
        lax.psum(sharded[0].astype(jnp.bfloat16), "rows").astype(jnp.float32),
        lax.psum(sharded[1].astype(jnp.bfloat16), "rows").astype(jnp.float32),
        lax.psum(sharded[2].astype(jnp.bfloat16), "rows").astype(jnp.float32),
        lax.psum(sharded[3].astype(jnp.bfloat16), "rows").astype(jnp.float32),
        lax.psum(sharded[4].astype(jnp.bfloat16), "rows").astype(jnp.float32),
        lax.psum(sharded[5].astype(jnp.bfloat16), "rows").astype(jnp.float32),
        lax.psum(sharded[6].astype(jnp.bfloat16), "rows").astype(jnp.float32),
        lax.psum(sharded[7].astype(jnp.bfloat16), "rows").astype(jnp.float32),
    )
    shared = lax.psum(
        (
            shared[0],
            shared[1],
            shared[2],
            shared[3],
            shared[4],
            shared[5],
            shared[6],
            shared[7],
            shared[8],
        ),
        ("rows", "mp"),
    )
    return (
        layer_output,
        gradient,
        shared[0],
        shared[1],
        sharded[0],
        sharded[1],
        shared[2],
        sharded[2],
        shared[3],
        shared[4],
        shared[5],
        shared[6],
        shared[7],
        sharded[3],
        sharded[4],
        sharded[5],
        sharded[6],
        sharded[7],
        shared[8],
    )


MESH_ID = pl.DeviceIdType.MESH
PLANE = ("core", "y", "x")
EVERY = ("y", "core", "z", "x")
f32 = jnp.float32
bf16 = jnp.bfloat16


def vmem_params(collective_id=None, mib=24):
    if collective_id is None:
        return pltpu.CompilerParams(vmem_limit_bytes=mib * 2**20)
    return pltpu.CompilerParams(
        vmem_limit_bytes=mib * 2**20, collective_id=collective_id, has_side_effects=True
    )


def plane_pairs():
    pairs = []
    for y in range(2):
        for core in range(2):
            for z in range(4):
                for x in range(2):
                    source = ((y * 2 + core) * 4 + z) * 2 + x
                    target = (((z % 2) * 2 + z // 2) * 4 + (2 * y + core)) * 2 + x
                    pairs.append((source, target))
    return pairs


def to_plane(values):
    return lax.ppermute(values, EVERY, plane_pairs())


def from_plane(values):
    return lax.ppermute(values, EVERY, [(target, source) for source, target in plane_pairs()])


class Here:
    def __init__(self):
        self.x, self.y = lax.axis_index("x"), lax.axis_index("y")
        self.core, self.z = lax.axis_index("core"), lax.axis_index("z")

    def peer(self, flip_x, flip_y, flip_core, step_z):
        place = {}
        if flip_x:
            place["x"] = 1 - self.x
        if flip_y:
            place["y"] = 1 - self.y
        if flip_core:
            place["core"] = 1 - self.core
        if step_z:
            place["z"] = lax.rem(self.z + step_z, 4)
        return place


BY_X, BY_Y, BY_CORE = (1, 0, 0, 0), (0, 1, 0, 0), (0, 0, 1, 0)
BY_Z = tuple((0, 0, 0, step) for step in (1, 2, 3))
BY_LINE = BY_Z + tuple((0, 0, 1, step) for step in range(4))
BY_PLANE = tuple((flip & 1, flip >> 1 & 1, flip >> 2, 0) for flip in range(1, 8))


def remote(source, target, send_sem, recv_sem, place):
    return pltpu.make_async_remote_copy(
        src_ref=source,
        dst_ref=target,
        send_sem=send_sem,
        recv_sem=recv_sem,
        device_id=place,
        device_id_type=MESH_ID,
    )


def dma_sems(count):
    return pltpu.SemaphoreType.DMA((count,))


class Task:
    arrays = ()
    spaces = ()
    outs = ()
    out_spaces = ()
    scratch = ()
    reach = ()

    def start(self, here, ins, outs, scratch):
        pass

    def finish(self, here, ins, outs, scratch):
        pass


def run_tasks(ids, *tasks, mib=24):
    reach = []
    for task in tasks:
        reach += [way for way in task.reach if way not in reach]

    def kernel(*refs):
        refs = list(refs)
        views = [[], [], []]
        for kind, name in enumerate(("arrays", "outs", "scratch")):
            for task in tasks:
                count = len(getattr(task, name))
                views[kind].append(refs[:count])
                refs = refs[count:]
        here = Here()
        barrier = pltpu.get_barrier_semaphore()
        for way in reach:
            pl.semaphore_signal(barrier, inc=1, device_id=here.peer(*way), device_id_type=MESH_ID)
        pl.semaphore_wait(barrier, len(reach))
        for task, *held in zip(tasks, *views):
            task.start(here, *held)
        for task, *held in zip(tasks, *views):
            task.finish(here, *held)

    results = pl.pallas_call(
        kernel,
        out_shape=[out for task in tasks for out in task.outs],
        in_specs=[pl.BlockSpec(memory_space=s) for task in tasks for s in task.spaces],
        out_specs=[pl.BlockSpec(memory_space=s) for task in tasks for s in task.out_spaces],
        scratch_shapes=[each for task in tasks for each in task.scratch],
        compiler_params=vmem_params(next(ids), mib),
    )(*[array for task in tasks for array in task.arrays])
    results = list(results)
    split = []
    for task in tasks:
        split.append(results[: len(task.outs)])
        results = results[len(task.outs) :]
    return split


class PlaneGather(Task):
    def __init__(self, block):
        rows, width = block.shape
        self.arrays, self.spaces = (block,), (pltpu.VMEM,)
        self.outs = (jax.ShapeDtypeStruct((8 * rows, width), block.dtype),)
        self.out_spaces = (pltpu.VMEM,)
        self.scratch = (dma_sems(11), dma_sems(11), pltpu.SemaphoreType.DMA)
        self.reach = (BY_X, BY_Y, BY_CORE)

    def place(self, here, o_ref, at_x, at_y, part=None):
        rows = o_ref.shape[0] // 8
        first = ((2 * here.core + at_y) * 2 + at_x) * rows
        if part is None:
            return o_ref.at[pl.ds(pl.multiple_of(first, rows), rows)]
        half = rows // 2
        return o_ref.at[pl.ds(pl.multiple_of(first + part * half, half), half)]

    def copies(self, here, x_ref, o_ref, send_sem, recv_sem):
        x, y = here.x, here.y
        half = x_ref.shape[0] // 2
        to_x, to_y, to_core = here.peer(*BY_X), here.peer(*BY_Y), here.peer(*BY_CORE)

        def copy(index, source, target, way):
            return remote(source, target, send_sem.at[index], recv_sem.at[index], way)

        def pass_on(index, way, *at):
            return copy(index, self.place(here, o_ref, *at), self.place(here, o_ref, *at), way)

        own = [self.place(here, o_ref, x, y, part) for part in (0, 1)]
        mine = [x_ref.at[pl.ds(part * half, half)] for part in (0, 1)]
        return [
            copy(0, mine[0], own[0], to_x),
            copy(1, mine[1], own[1], to_y),
            copy(2, mine[1], own[1], to_x),
            copy(3, mine[0], own[0], to_y),
            copy(4, x_ref, self.place(here, o_ref, x, y), to_core),
            pass_on(5, to_y, 1 - x, y, 0),
            pass_on(6, to_x, x, 1 - y, 1),
            pass_on(7, to_core, 1 - x, y),
            pass_on(8, to_core, x, 1 - y),
            pass_on(9, to_core, 1 - x, 1 - y, 0),
            pass_on(10, to_core, 1 - x, 1 - y, 1),
        ]

    def keep(self, here, x_ref, o_ref, own_sem):
        return pltpu.make_async_copy(x_ref, self.place(here, o_ref, here.x, here.y), own_sem)

    def start(self, here, ins, outs, scratch):
        copies = self.copies(here, ins[0], outs[0], scratch[0], scratch[1])
        for index in range(5):
            copies[index].start()
        self.keep(here, ins[0], outs[0], scratch[2]).start()

    def finish(self, here, ins, outs, scratch, work=None):
        rows = ins[0].shape[0]
        copies = self.copies(here, ins[0], outs[0], scratch[0], scratch[1])

        def done(flip_core, flip_x, flip_y):
            if work is not None:
                at_core = 1 - here.core if flip_core else here.core
                at_x = 1 - here.x if flip_x else here.x
                at_y = 1 - here.y if flip_y else here.y
                work(pl.multiple_of(((2 * at_core + at_y) * 2 + at_x) * rows, rows))

        self.keep(here, ins[0], outs[0], scratch[2]).wait()
        done(0, 0, 0)
        copies[4].wait_recv()
        done(1, 0, 0)
        for index in range(4):
            copies[index].wait_recv()
            copies[5 + index].start()
        done(0, 1, 0)
        done(0, 0, 1)
        copies[7].wait_recv()
        done(1, 1, 0)
        copies[8].wait_recv()
        done(1, 0, 1)
        copies[5].wait_recv()
        copies[9].start()
        copies[6].wait_recv()
        copies[10].start()
        done(0, 1, 1)
        copies[9].wait_recv()
        copies[10].wait_recv()
        done(1, 1, 1)
        for each in copies:
            each.wait_send()


class PlaneScatter(Task):
    def __init__(self, rows, width, weight_dim):
        half = rows // 2
        self.weight_dim = weight_dim
        self.scratch = (
            pltpu.VMEM((4, rows, width), bf16),
            pltpu.VMEM((4, rows, width), bf16),
            pltpu.VMEM((rows, width), bf16),
            pltpu.VMEM((2, half, width), bf16),
            pltpu.VMEM((2, half, width), bf16),
            pltpu.VMEM((2, half, width), bf16),
            pltpu.VMEM((2, half, width), bf16),
            pltpu.VMEM((2, half, width), bf16),
            pltpu.VMEM((half, width), f32),
            pltpu.VMEM((half, width), f32),
            dma_sems(10),
            dma_sems(10),
        )
        self.reach = (BY_X, BY_Y, BY_CORE)

    def finish(self, here, ins, outs, scratch, rows_of, weight_of, early=None, idle=None):
        o_ref = outs[0]
        (
            sib_out,
            sib_in,
            diag_out,
            diag_in,
            last_x_out,
            last_y_out,
            last_x_in,
            last_y_in,
            wait_x,
            wait_y,
            send_sem,
            recv_sem,
        ) = scratch
        rows = o_ref.shape[0]
        half = rows // 2
        x, y, core = here.x, here.y, here.core
        to_x, to_y, to_core = here.peer(*BY_X), here.peer(*BY_Y), here.peer(*BY_CORE)

        def term(at_core, at_x, at_y):
            first = pl.multiple_of(((2 * at_core + at_y) * 2 + at_x) * rows, rows)
            return lax.dot_general(
                rows_of(first),
                weight_of(),
                (((1,), (self.weight_dim,)), ((), ())),
                preferred_element_type=f32,
            )

        def copy(index, source, target, way):
            return remote(source, target, send_sem.at[index], recv_sem.at[index], way)

        places = ((1 - x, 1 - y), (1 - x, y), (x, 1 - y), (x, y))
        siblings = [copy(i, sib_out.at[i], sib_in.at[i], to_core) for i in range(4)]

        def help_sibling(i):
            sib_out[i] = term(1 - core, *places[i]).astype(bf16)
            siblings[i].start()

        def joined(i):
            mine = term(core, *places[i])
            siblings[i].wait_recv()
            return mine + sib_in[i].astype(f32)

        help_sibling(0)
        total = joined(0)
        diag_out[...] = total.astype(bf16)
        diag_x = copy(4, diag_out.at[pl.ds(0, half)], diag_in.at[0], to_x)
        diag_y = copy(5, diag_out.at[pl.ds(half, half)], diag_in.at[1], to_y)
        diag_x.start()
        diag_y.start()
        help_sibling(1)
        total = joined(1)
        last_x_out[0] = total[:half].astype(bf16)
        x_0 = copy(6, last_x_out.at[0], last_x_in.at[0], to_x)
        x_0.start()
        wait_x[...] = total[half:]
        if early is not None:
            early()
        help_sibling(2)
        total = joined(2)
        last_y_out[1] = total[half:].astype(bf16)
        y_1 = copy(7, last_y_out.at[1], last_y_in.at[1], to_y)
        y_1.start()
        wait_y[...] = total[:half]
        help_sibling(3)
        diag_y.wait_recv()
        last_x_out[1] = (wait_x[...] + diag_in[1].astype(f32)).astype(bf16)
        x_1 = copy(8, last_x_out.at[1], last_x_in.at[1], to_x)
        x_1.start()
        diag_x.wait_recv()
        last_y_out[0] = (wait_y[...] + diag_in[0].astype(f32)).astype(bf16)
        y_0 = copy(9, last_y_out.at[0], last_y_in.at[0], to_y)
        y_0.start()
        o_ref[...] = joined(3)
        if idle is not None:
            idle()
        for part, (by_x, by_y) in enumerate(((x_0, y_0), (x_1, y_1))):
            by_x.wait_recv()
            by_y.wait_recv()
            piece = pl.ds(part * half, half)
            o_ref[piece, :] += last_x_in[part].astype(f32) + last_y_in[part].astype(f32)
        for sent in (*siblings, diag_x, diag_y, x_0, y_1, x_1, y_0):
            sent.wait_send()


class PlaneSum(Task):
    def __init__(self, values):
        self.arrays, self.spaces = (values,), (pltpu.VMEM,)
        self.outs = (jax.ShapeDtypeStruct(values.shape, f32),)
        self.out_spaces = (pltpu.VMEM,)
        self.scratch = (pltpu.VMEM((7, *values.shape), f32), dma_sems(7), dma_sems(7))
        self.reach = BY_PLANE

    def copies(self, here, ins, scratch):
        got, send_sem, recv_sem = scratch
        return [
            remote(ins[0], got.at[i], send_sem.at[i], recv_sem.at[i], here.peer(*way))
            for i, way in enumerate(BY_PLANE)
        ]

    def start(self, here, ins, outs, scratch):
        for each in self.copies(here, ins, scratch):
            each.start()

    def finish(self, here, ins, outs, scratch):
        copies = self.copies(here, ins, scratch)
        for each in copies:
            each.wait_recv()
        got = scratch[0]
        by_x = [ins[0][...] + got[0]]
        for flip in (2, 4, 6):
            by_x.append(got[flip - 1] + got[flip])
        outs[0][...] = (by_x[0] + by_x[1]) + (by_x[2] + by_x[3])
        for each in copies:
            each.wait_send()


class LineGather(Task):
    def __init__(self, values):
        self.arrays, self.spaces = (values,), (pl.ANY,)
        self.outs = (jax.ShapeDtypeStruct((4, *values.shape), values.dtype),)
        self.out_spaces = (pl.ANY,)
        self.scratch = (dma_sems(4), dma_sems(3))
        self.reach = BY_Z

    def copies(self, here, ins, outs, scratch):
        target = outs[0].at[here.z]
        keep = pltpu.make_async_copy(ins[0], target, scratch[0].at[3])
        return keep, [
            remote(ins[0], target, scratch[0].at[i], scratch[1].at[i], here.peer(*way))
            for i, way in enumerate(BY_Z)
        ]

    def start(self, here, ins, outs, scratch):
        keep, copies = self.copies(here, ins, outs, scratch)
        for each in copies:
            each.start()
        keep.start()

    def finish(self, here, ins, outs, scratch):
        keep, copies = self.copies(here, ins, outs, scratch)
        for each in copies:
            each.wait()
        keep.wait()


class HeadGather(Task):
    def __init__(self, values):
        kinds, wide, half = values.shape
        self.arrays, self.spaces = (values,), (pl.ANY,)
        self.outs = (jax.ShapeDtypeStruct((kinds, 2, wide, 2 * half), values.dtype),)
        self.out_spaces = (pl.ANY,)
        self.scratch = (dma_sems(4), dma_sems(4))
        self.reach = BY_LINE

    def piece(self, outs, shard, part):
        half = outs[0].shape[3] // 2
        return outs[0].at[:, shard, :, pl.ds(pl.multiple_of(part * half, half), half)]

    def copies(self, here, ins, outs, scratch):
        shard, target_core = lax.rem(here.z, 2), here.z // 2
        target = self.piece(outs, shard, here.core)
        recv_sem = scratch[1].at[2 * shard + here.core]
        keep = pltpu.make_async_copy(ins[0], target, recv_sem)
        return keep, [
            remote(
                ins[0],
                target,
                scratch[0].at[step],
                recv_sem,
                {"core": target_core, "z": lax.rem(here.z + step, 4)},
            )
            for step in range(4)
        ]

    def start(self, here, ins, outs, scratch):
        keep, copies = self.copies(here, ins, outs, scratch)
        for each in copies[1:]:
            each.start()
        at_home = here.z // 2 == here.core
        pl.when(at_home)(keep.start)
        pl.when(jnp.logical_not(at_home))(copies[0].start)

    def finish(self, here, ins, outs, scratch):
        keep, copies = self.copies(here, ins, outs, scratch)
        for shard in range(2):
            for part in range(2):
                piece = self.piece(outs, shard, part)
                pltpu.make_async_copy(piece, piece, scratch[1].at[2 * shard + part]).wait()
        for each in copies[1:]:
            each.wait_send()
        pl.when(here.z // 2 != here.core)(copies[0].wait_send)


class LineScatter(Task):
    def __init__(self, values):
        shape = values.shape[1:]
        self.arrays, self.spaces = (values,), (pltpu.VMEM,)
        self.outs, self.out_spaces = (jax.ShapeDtypeStruct(shape, values.dtype),), (pltpu.VMEM,)
        self.scratch = (pltpu.VMEM((3, *shape), values.dtype), dma_sems(3), dma_sems(3))
        self.reach = BY_Z

    def copies(self, here, ins, scratch):
        got, send_sem, recv_sem = scratch
        return [
            remote(
                ins[0].at[lax.rem(here.z + i + 1, 4)],
                got.at[i],
                send_sem.at[i],
                recv_sem.at[i],
                here.peer(*way),
            )
            for i, way in enumerate(BY_Z)
        ]

    def start(self, here, ins, outs, scratch):
        for each in self.copies(here, ins, scratch):
            each.start()

    def finish(self, here, ins, outs, scratch):
        copies = self.copies(here, ins, scratch)
        for each in copies:
            each.wait_recv()
        total = ins[0][here.z].astype(f32)
        for i in range(3):
            total = total + scratch[0][i].astype(f32)
        outs[0][...] = total.astype(outs[0].dtype)
        for each in copies:
            each.wait_send()


class HeadScatter(Task):
    def __init__(self, values):
        kinds, _, wide, width = values.shape
        shape = (kinds, wide, width // 2)
        self.arrays, self.spaces = (values,), (pltpu.VMEM,)
        self.outs, self.out_spaces = (jax.ShapeDtypeStruct(shape, values.dtype),), (pltpu.VMEM,)
        self.scratch = (pltpu.VMEM((4, *shape), values.dtype), dma_sems(4), dma_sems(4))
        self.reach = BY_LINE

    def copies(self, here, ins, scratch):
        got, send_sem, recv_sem = scratch
        half = ins[0].shape[3] // 2
        triples = []
        for shard in range(2):
            for part in range(2):
                source = ins[0].at[:, shard, :, pl.ds(part * half, half)]
                target_z = 2 * here.core + shard
                slot = recv_sem.at[here.z]
                away = remote(
                    source,
                    got.at[here.z],
                    send_sem.at[2 * shard + part],
                    slot,
                    {"core": part, "z": target_z},
                )
                stay = pltpu.make_async_copy(source, got.at[here.z], slot)
                at_home = (target_z == here.z) & (here.core == part)
                triples.append((away, stay, at_home))
        return triples

    def start(self, here, ins, outs, scratch):
        for away, stay, at_home in self.copies(here, ins, scratch):
            pl.when(at_home)(stay.start)
            pl.when(jnp.logical_not(at_home))(away.start)

    def finish(self, here, ins, outs, scratch):
        got, send_sem, recv_sem = scratch
        for plane in range(4):
            pltpu.make_async_copy(got.at[plane], got.at[plane], recv_sem.at[plane]).wait()
        total = got[0].astype(f32)
        for plane in range(1, 4):
            total = total + got[plane].astype(f32)
        outs[0][...] = total.astype(outs[0].dtype)
        for away, stay, at_home in self.copies(here, ins, scratch):
            pl.when(jnp.logical_not(at_home))(away.wait_send)


class RowsGather(Task):
    def __init__(self, values):
        self.arrays, self.spaces = (values,), (pl.ANY,)
        self.outs = (jax.ShapeDtypeStruct((4, *values.shape), values.dtype),)
        self.out_spaces = (pl.ANY,)
        self.scratch = (dma_sems(4), dma_sems(3))
        self.reach = (BY_Y, BY_CORE)

    def copies(self, here, ins, outs, scratch):
        send_sem, recv_sem = scratch
        own = outs[0].at[2 * here.y + here.core]
        over = outs[0].at[2 * (1 - here.y) + here.core]
        to_y, to_core = here.peer(*BY_Y), here.peer(*BY_CORE)
        return (
            pltpu.make_async_copy(ins[0], own, send_sem.at[3]),
            remote(ins[0], own, send_sem.at[0], recv_sem.at[0], to_y),
            remote(ins[0], own, send_sem.at[1], recv_sem.at[1], to_core),
            remote(over, over, send_sem.at[2], recv_sem.at[2], to_core),
        )

    def start(self, here, ins, outs, scratch):
        keep, by_y, by_core, again = self.copies(here, ins, outs, scratch)
        by_y.start()
        by_core.start()
        keep.start()

    def finish(self, here, ins, outs, scratch):
        keep, by_y, by_core, again = self.copies(here, ins, outs, scratch)
        by_y.wait_recv()
        again.start()
        by_core.wait_recv()
        again.wait_recv()
        for each in (by_y, by_core, again):
            each.wait_send()
        keep.wait()


class PlaneThenLineSum(Task):
    def __init__(self, values, ready):
        rows, width = values.shape
        both = (rows + ready.shape[0], width)
        self.plane = PlaneSum(values)
        self.arrays, self.spaces = (values, ready), (pltpu.VMEM,) * 2
        self.outs, self.out_spaces = (jax.ShapeDtypeStruct(both, f32),), (pltpu.VMEM,)
        self.scratch = (
            *self.plane.scratch,
            pltpu.VMEM((4, *both), f32),
            pltpu.VMEM(both, f32),
            dma_sems(3),
            dma_sems(4),
        )
        self.reach = BY_PLANE + BY_Z

    def start(self, here, ins, outs, scratch):
        self.plane.start(here, ins[:1], None, scratch[:3])

    def finish(self, here, ins, outs, scratch):
        got, mine, send_sem, recv_sem = scratch[3:]
        rows = ins[0].shape[0]
        first = ins[1].shape[0]
        self.plane.finish(here, ins[:1], (mine.at[pl.ds(first, rows)],), scratch[:3])
        mine[:first, :] = ins[1][...]
        copies = [
            remote(mine, got.at[here.z], send_sem.at[i], recv_sem.at[here.z], here.peer(*way))
            for i, way in enumerate(BY_Z)
        ]
        for each in copies:
            each.start()
        keep = pltpu.make_async_copy(mine, got.at[here.z], recv_sem.at[here.z])
        keep.start()
        for plane in range(4):
            pltpu.make_async_copy(got.at[plane], got.at[plane], recv_sem.at[plane]).wait()
        outs[0][...] = (got[0] + got[1]) + (got[2] + got[3])
        for each in copies:
            each.wait_send()


def to_columns(upper, lower):
    place = lax.broadcasted_iota(jnp.int32, (128, upper.shape[1]), 0)
    return jnp.transpose(jnp.where(place < 64, upper, lower))


def both_columns(upper, lower):
    lane = lax.broadcasted_iota(jnp.int32, (upper.shape[0], 128), 1)
    return jnp.where(lane < 64, upper, lower)


def in_chunks(rows, chunk, step):
    def one(index, carry):
        step(pl.multiple_of(index * chunk, chunk))
        return carry

    lax.fori_loop(0, rows // chunk, one, 0)


def fold(values):
    total = values[:8]
    for first in range(8, values.shape[0], 8):
        total = total + values[first : first + 8]
    return total


class Parts(Task):
    def use(self, **parts):
        self.parts = parts
        self.scratch = list(self.scratch)
        self.at = {}
        reach = []
        for name, part in parts.items():
            self.at[name] = (len(self.scratch), len(self.scratch) + len(part.scratch))
            self.scratch += list(part.scratch)
            reach += [way for way in part.reach if way not in reach]
        self.reach = reach

    def held(self, scratch, name):
        first, last = self.at[name]
        return scratch[first:last]


CHUNK = 32


class FfnForward(Parts):
    def __init__(self, block, first, second, shift, gain, bias):
        rows, width = block.shape
        hidden = second.shape[0]
        self.arrays = (block, first, second, shift, gain, bias)
        self.spaces = (pltpu.VMEM,) * 6
        self.outs = (
            jax.ShapeDtypeStruct((rows, width), f32),
            jax.ShapeDtypeStruct((8 * rows, width), bf16),
            jax.ShapeDtypeStruct((8 * rows, hidden), f32),
            jax.ShapeDtypeStruct((8 * rows, hidden), bf16),
            jax.ShapeDtypeStruct((2, 8 * rows), f32),
        )
        self.out_spaces = (pltpu.VMEM, pl.ANY, pl.ANY, pl.ANY, pltpu.VMEM)
        self.scratch = (
            pltpu.VMEM((8 * rows, width), bf16),
            pltpu.VMEM((8 * rows, hidden), f32),
            pltpu.VMEM((8 * rows, hidden), f32),
            pltpu.VMEM((8 * rows, hidden), bf16),
            pltpu.VMEM((2, 8 * rows), f32),
            pltpu.VMEM((rows, 128), f32),
            dma_sems(3),
        )
        self.use(
            gather=PlaneGather(block),
            scatter=PlaneScatter(rows, width, 0),
            sums=PlaneSum(jax.ShapeDtypeStruct((2, 8 * rows), f32)),
        )

    def start(self, here, ins, outs, scratch):
        self.parts["gather"].start(here, ins[:1], scratch[:1], self.held(scratch, "gather"))

    def finish(self, here, ins, outs, scratch):
        block_ref, first_ref, second_ref, shift_ref, gain_ref, bias_ref = ins
        out_ref, rows_out, before_out, mixed_out, total_ref = outs
        rows_buf, before, active, mixed, sums, columns, save = scratch[:7]
        rows = block_ref.shape[0]
        hidden_all = 8 * second_ref.shape[0]

        def work(first):
            before[pl.ds(first, rows), :] = lax.dot_general(
                rows_buf[pl.ds(first, rows), :],
                first_ref[...],
                (((1,), (0,)), ((), ())),
                preferred_element_type=f32,
            )

            def step(at):
                piece = pl.ds(pl.multiple_of(first + at, CHUNK), CHUNK)
                u = before[piece, :] + shift_ref[...]
                before[piece, :] = u
                a = 0.5 * u * (1.0 + lax.erf(u * 0.5**0.5))
                active[piece, :] = a
                columns[pl.ds(at, CHUNK), :] = both_columns(
                    jnp.sum(a, axis=1, keepdims=True), jnp.sum(a * a, axis=1, keepdims=True)
                )

            in_chunks(rows, CHUNK, step)
            turned = jnp.transpose(columns[...])
            sums[0:1, pl.ds(first, rows)] = turned[0:1]
            sums[1:2, pl.ds(first, rows)] = turned[64:65]

        self.parts["gather"].finish(
            here, ins[:1], scratch[:1], self.held(scratch, "gather"), work
        )
        held = self.held(scratch, "sums")
        self.parts["sums"].start(here, (sums,), None, held)
        keep_rows = pltpu.make_async_copy(rows_buf, rows_out, save.at[0])
        keep_rows.start()
        keep_before = pltpu.make_async_copy(before, before_out, save.at[1])
        keep_before.start()
        self.parts["sums"].finish(here, (sums,), (total_ref,), held)

        def rows_of(first):
            average = total_ref[0:1, pl.ds(first, rows)] / hidden_all
            spread = total_ref[1:2, pl.ds(first, rows)] / hidden_all - average * average
            columns[...] = to_columns(average, lax.rsqrt(spread + epsilon))

            def step(at):
                piece = pl.ds(pl.multiple_of(first + at, CHUNK), CHUNK)
                pair = columns[pl.ds(at, CHUNK), :]
                normal = (active[piece, :] - pair[:, 0:1]) * pair[:, 64:65]
                mixed[piece, :] = (normal * gain_ref[...] + bias_ref[...]).astype(bf16)

            in_chunks(rows, CHUNK, step)
            return mixed[pl.ds(first, rows), :]

        keep_mixed = pltpu.make_async_copy(mixed, mixed_out, save.at[2])
        self.parts["scatter"].finish(
            here,
            None,
            (out_ref,),
            self.held(scratch, "scatter"),
            rows_of,
            lambda: second_ref[...],
            idle=keep_mixed.start,
        )
        keep_rows.wait()
        keep_before.wait()
        keep_mixed.wait()


class FfnBackward(Parts):
    def __init__(self, block, first, second, gain, before, mixed, ffn_rows, totals):
        rows, width = block.shape
        hidden = second.shape[0]
        self.arrays = (block, first, second, gain, totals, before, mixed, ffn_rows)
        self.spaces = (pltpu.VMEM,) * 5 + (pl.ANY,) * 3
        self.outs = (
            jax.ShapeDtypeStruct((rows, width), f32),
            jax.ShapeDtypeStruct((4, width, hidden // 4), bf16),
            jax.ShapeDtypeStruct((hidden // 4, width), bf16),
            jax.ShapeDtypeStruct((3, hidden), f32),
        )
        self.out_spaces = (pltpu.VMEM,) * 4
        self.scratch = (
            pltpu.VMEM((8 * rows, width), bf16),
            pltpu.VMEM((8 * rows, hidden), f32),
            pltpu.VMEM((8 * rows, hidden), f32),
            pltpu.VMEM((8 * rows, hidden), f32),
            pltpu.VMEM((8 * rows, hidden), bf16),
            pltpu.VMEM((8 * rows, width), bf16),
            pltpu.VMEM((8 * rows, hidden), bf16),
            pltpu.VMEM((hidden, width), f32),
            pltpu.VMEM((2, 8 * rows), f32),
            pltpu.VMEM((2, 8 * rows), f32),
            pltpu.VMEM((rows, 128), f32),
            pltpu.VMEM((rows, 128), f32),
            pltpu.VMEM((3, 8, hidden), f32),
            dma_sems(3),
            pltpu.VMEM((4, hidden // 4, width), bf16),
        )
        self.use(
            gather=PlaneGather(block),
            scatter=PlaneScatter(rows, width, 1),
            second=LineScatter(jax.ShapeDtypeStruct((4, hidden // 4, width), bf16)),
            sums=PlaneSum(jax.ShapeDtypeStruct((2, 8 * rows), f32)),
        )

    def loads(self, ins, scratch):
        pairs = ((ins[5], scratch[1]), (ins[6], scratch[4]), (ins[7], scratch[5]))
        return [
            pltpu.make_async_copy(source, target, scratch[13].at[i])
            for i, (source, target) in enumerate(pairs)
        ]

    def start(self, here, ins, outs, scratch):
        self.parts["gather"].start(here, ins[:1], scratch[:1], self.held(scratch, "gather"))
        for each in self.loads(ins, scratch):
            each.start()

    def finish(self, here, ins, outs, scratch):
        block_ref, first_ref, second_ref, gain_ref, totals_ref = ins[:5]
        out_ref, first_grad, second_quarter, small_ref = outs
        second_grad = scratch[14]
        (
            rows_buf,
            before,
            normal_buf,
            grads,
            mixed,
            ffn_rows,
            pre_grad,
            second_sum,
            sums,
            got,
            columns,
            factors,
            small,
        ) = scratch[:13]
        rows = block_ref.shape[0]
        hidden_all = 8 * second_ref.shape[0]
        load_before, load_mixed, load_rows = self.loads(ins, scratch)
        load_before.wait()
        load_mixed.wait()
        second_sum[...] = jnp.zeros_like(second_sum)
        small[...] = jnp.zeros_like(small)

        def factor_columns(first):
            average = totals_ref[0:1, pl.ds(first, rows)] / hidden_all
            spread = totals_ref[1:2, pl.ds(first, rows)] / hidden_all - average * average
            factors[...] = to_columns(average, lax.rsqrt(spread + epsilon))

        def work(first):
            block = pl.ds(first, rows)
            grads[block, :] = lax.dot_general(
                rows_buf[block, :],
                second_ref[...],
                (((1,), (1,)), ((), ())),
                preferred_element_type=f32,
            )
            second_sum[...] += lax.dot_general(
                mixed[block, :],
                rows_buf[block, :],
                (((0,), (0,)), ((), ())),
                preferred_element_type=f32,
            )
            factor_columns(first)

            def step(at):
                piece = pl.ds(pl.multiple_of(first + at, CHUNK), CHUNK)
                pair = factors[pl.ds(at, CHUNK), :]
                u = before[piece, :]
                area = 0.5 * (1.0 + lax.erf(u * 0.5**0.5))
                before[piece, :] = area + u * (jnp.exp(-0.5 * u * u) * (0.5 / jnp.pi) ** 0.5)
                normal = (u * area - pair[:, 0:1]) * pair[:, 64:65]
                normal_buf[piece, :] = normal
                grad = grads[piece, :]
                small[0] += fold(grad * normal)
                small[1] += fold(grad)
                scaled = grad * gain_ref[...]
                grads[piece, :] = scaled
                columns[pl.ds(at, CHUNK), :] = both_columns(
                    jnp.sum(scaled, axis=1, keepdims=True),
                    jnp.sum(scaled * normal, axis=1, keepdims=True),
                )

            in_chunks(rows, CHUNK, step)
            turned = jnp.transpose(columns[...])
            sums[0:1, pl.ds(first, rows)] = turned[0:1]
            sums[1:2, pl.ds(first, rows)] = turned[64:65]

        self.parts["gather"].finish(
            here, ins[:1], scratch[:1], self.held(scratch, "gather"), work
        )
        held = self.held(scratch, "sums")
        self.parts["sums"].start(here, (sums,), None, held)
        second_grad[...] = second_sum[...].astype(bf16).reshape(second_grad.shape)
        self.parts["second"].start(here, (second_grad,), None, self.held(scratch, "second"))
        self.parts["sums"].finish(here, (sums,), (got,), held)

        def rows_of(first):
            factor_columns(first)
            columns[...] = to_columns(
                got[0:1, pl.ds(first, rows)] / hidden_all,
                got[1:2, pl.ds(first, rows)] / hidden_all,
            )

            def step(at):
                piece = pl.ds(pl.multiple_of(first + at, CHUNK), CHUNK)
                pair = columns[pl.ds(at, CHUNK), :]
                factor = factors[pl.ds(at, CHUNK), :][:, 64:65]
                active_grad = factor * (
                    grads[piece, :] - pair[:, 0:1] - normal_buf[piece, :] * pair[:, 64:65]
                )
                rounded = (active_grad * before[piece, :]).astype(bf16)
                pre_grad[piece, :] = rounded
                small[2] += fold(rounded.astype(f32))

            in_chunks(rows, CHUNK, step)
            return pre_grad[pl.ds(first, rows), :]

        def idle():
            load_rows.wait()
            whole = lax.dot_general(
                ffn_rows[...],
                pre_grad[...],
                (((0,), (0,)), ((), ())),
                preferred_element_type=f32,
            ).astype(bf16)
            part = first_grad.shape[2]
            for i in range(4):
                first_grad[i] = whole[:, i * part : (i + 1) * part]

        self.parts["scatter"].finish(
            here,
            None,
            (out_ref,),
            self.held(scratch, "scatter"),
            rows_of,
            lambda: first_ref[...],
            idle=idle,
        )
        held = self.held(scratch, "second")
        self.parts["second"].finish(here, (second_grad,), (second_quarter,), held)
        for i in range(3):
            small_ref[i : i + 1, :] = jnp.sum(small[i], axis=0, keepdims=True)


class WeightGather(Task):
    def __init__(self, weights, layer, axis):
        self.layer, self.axis = layer, axis
        self.arrays, self.spaces = (weights,), (pl.ANY,)
        self.outs = (jax.ShapeDtypeStruct(weights.shape[1:], weights.dtype),)
        self.out_spaces = (pl.ANY,)
        self.scratch = (dma_sems(4), dma_sems(3))
        self.reach = BY_Z

    def copies(self, here, ins, outs, scratch):
        part = outs[0].shape[self.axis] // 4

        def cut(ref, at):
            piece = pl.ds(pl.multiple_of(at * part, part), part)
            return ref.at[piece, :] if self.axis == 0 else ref.at[:, piece]

        source = cut(ins[0].at[self.layer], 2 * here.y + here.core)
        target = cut(outs[0], here.z)
        keep = pltpu.make_async_copy(source, target, scratch[0].at[3])
        return keep, [
            remote(source, target, scratch[0].at[i], scratch[1].at[i], here.peer(*way))
            for i, way in enumerate(BY_Z)
        ]

    def start(self, here, ins, outs, scratch):
        keep, copies = self.copies(here, ins, outs, scratch)
        for each in copies:
            each.start()
        keep.start()

    def finish(self, here, ins, outs, scratch):
        keep, copies = self.copies(here, ins, outs, scratch)
        for each in copies:
            each.wait()
        keep.wait()


class LineThenRows(Parts):
    def __init__(self, values):
        shape = jax.ShapeDtypeStruct(values.shape[1:], values.dtype)
        self.arrays, self.spaces = (values,), (pltpu.VMEM,)
        self.outs = (jax.ShapeDtypeStruct((4, *shape.shape), values.dtype),)
        self.out_spaces = (pl.ANY,)
        self.scratch = (pltpu.VMEM(shape.shape, values.dtype),)
        self.use(line=LineScatter(values), rows=RowsGather(shape))

    def start(self, here, ins, outs, scratch):
        self.parts["line"].start(here, ins, None, self.held(scratch, "line"))

    def finish(self, here, ins, outs, scratch):
        self.parts["line"].finish(here, ins, scratch[:1], self.held(scratch, "line"))
        held = self.held(scratch, "rows")
        self.parts["rows"].start(here, scratch[:1], outs, held)
        self.parts["rows"].finish(here, scratch[:1], outs, held)


BLOCK = 256
SPAN = 512


def head_masks(head_width, width):
    lane = lax.broadcasted_iota(jnp.int32, (1, width), 1)
    lower = (lane < head_width).astype(bf16)
    return lower, (1 - lower).astype(bf16)


def by_head(values, head_width):
    lower, upper = head_masks(head_width, values.shape[1])
    return jnp.concatenate([values * lower, values * upper], axis=0)


def from_heads(pair, head_width):
    rows = pair.shape[0] // 2
    lane = lax.broadcasted_iota(jnp.int32, (rows, pair.shape[1]), 1)
    return jnp.where(lane < head_width, pair[:rows], pair[rows:])


def tile_facts(doc_ref, first, key_first, keys):
    docs = doc_ref[:, pl.ds(first, BLOCK)]
    docs = jnp.concatenate([docs, docs], axis=1)
    key_docs = doc_ref[:, pl.ds(pl.multiple_of(key_first, keys), keys)]
    key_docs = jnp.transpose(jnp.broadcast_to(key_docs, (128, keys)))[:, 0:1]
    place = lax.broadcasted_iota(jnp.int32, (keys, 2 * BLOCK), 1)
    place = jnp.where(place >= BLOCK, place - BLOCK, place) + (first - key_first)
    allowed = (docs == key_docs) & (place >= lax.broadcasted_iota(jnp.int32, place.shape, 0))
    return docs, allowed


def attend_block(
    head_width, first, q_ref, k_ref, v_cols, doc_ref, o_ref, l_ref, s_buf, acc, top, total
):
    block = first // BLOCK
    last = first // SPAN
    pair = by_head(q_ref[pl.ds(first, BLOCK), :], head_width)

    def scores(at):
        keys = k_ref[pl.ds(pl.multiple_of(at * SPAN, SPAN), SPAN), :]
        return lax.dot_general(keys, pair, (((1,), (1,)), ((), ())), preferred_element_type=f32)

    top[...] = jnp.full_like(top, masked)

    def first_pass(at, carry):
        s = scores(at)
        s_buf[at] = s
        peak = s[:8]
        for row in range(8, SPAN, 8):
            peak = jnp.maximum(peak, s[row : row + 8])
        top[...] = jnp.maximum(top[...], peak)
        return carry

    lax.fori_loop(0, last, first_pass, 0)
    docs, allowed = tile_facts(doc_ref, first, last * SPAN, SPAN)
    s = jnp.where(allowed, scores(last), masked)
    shift = jnp.where(docs == 0, 0.0, masked)
    peak = jnp.maximum(
        jnp.max(top[...], axis=0, keepdims=True) + shift, jnp.max(s, axis=0, keepdims=True)
    )

    def weigh(at, p):
        values = v_cols[:, pl.ds(pl.multiple_of(at * SPAN, SPAN), SPAN)]
        return jnp.dot(values, p.astype(bf16), preferred_element_type=f32)

    p = jnp.exp(s - peak)
    total[...] = fold(p)
    acc[...] = weigh(last, p)
    base = peak - shift

    def second_pass(at, carry):
        p = jnp.exp(s_buf[at] - base)
        total[...] += fold(p)
        acc[...] += weigh(at, p)
        return carry

    lax.fori_loop(0, last, second_pass, 0)
    sums = jnp.sum(total[...], axis=0, keepdims=True)
    out = from_heads(jnp.transpose(acc[...] / sums), head_width)
    o_ref[pl.ds(first, BLOCK), :] = out
    l_ref[block] = peak + jnp.log(sums)
    return out


def attend_block_back(
    head_width,
    first,
    do,
    q_ref,
    k_ref,
    k_cols,
    v_ref,
    o_ref,
    l_ref,
    doc_ref,
    acc_k,
    acc_v,
    acc_q,
):
    block = first // BLOCK
    rows = pl.ds(first, BLOCK)
    pair_q = by_head(q_ref[rows, :], head_width)
    pair_do = by_head(do, head_width)
    out = o_ref[rows, :]
    inner = jnp.sum(
        jnp.concatenate([out, out], axis=0) * pair_do.astype(f32), axis=1, keepdims=True
    )
    inner = jnp.transpose(jnp.broadcast_to(inner, (2 * BLOCK, 128)))[0:1, :]
    logs = l_ref[block]
    docs, allowed = tile_facts(doc_ref, first, first, BLOCK)

    def step(at, base, allowed):
        piece = pl.ds(pl.multiple_of(at * BLOCK, BLOCK), BLOCK)
        s = lax.dot_general(
            k_ref[piece, :], pair_q, (((1,), (1,)), ((), ())), preferred_element_type=f32
        )
        dp = lax.dot_general(
            v_ref[piece, :], pair_do, (((1,), (1,)), ((), ())), preferred_element_type=f32
        )
        p = jnp.exp(s - base)
        if allowed is not None:
            p = jnp.where(allowed, p, 0.0)
        ds = (p * (dp - inner)).astype(bf16)
        acc_v[piece, :] += jnp.dot(p.astype(bf16), pair_do, preferred_element_type=f32)
        acc_k[piece, :] += jnp.dot(ds, pair_q, preferred_element_type=f32)
        return jnp.dot(k_cols[:, piece], ds, preferred_element_type=f32)

    acc_q[...] = step(block, logs, allowed)
    base = jnp.where(docs == 0, logs, -masked)

    def earlier(at, carry):
        acc_q[...] += step(at, base, None)
        return carry

    lax.fori_loop(0, block, earlier, 0)
    grad = from_heads(jnp.transpose(acc_q[...]), head_width)
    return (grad * head_width**-0.5).astype(bf16)


def turned(values):
    return jnp.transpose(values.astype(f32)).astype(bf16)


class AttnForward(Parts):
    def __init__(self, block, docs, scale, heads, biases, layer, late):
        rows, width = block.shape
        kinds, wide = heads.shape[0], heads.shape[-2]
        self.head_width, self.layer, self.late = wide, layer, late
        here = 2 * wide
        self.arrays = (block, docs, scale, heads, biases)
        self.spaces = (pltpu.VMEM,) * 3 + ((pl.ANY,) if late else (pltpu.VMEM,)) * 2
        column = jax.ShapeDtypeStruct((8 * rows, here), bf16)
        self.outs = (
            jax.ShapeDtypeStruct((rows, width), f32),
            jax.ShapeDtypeStruct((8 * rows, width), bf16),
            column,
            column,
            column,
            column,
            jax.ShapeDtypeStruct((8 * rows, here), f32),
            jax.ShapeDtypeStruct((8 * rows // BLOCK, 1, 2 * BLOCK), f32),
        )
        self.out_spaces = (pltpu.VMEM, pl.ANY) + (pltpu.VMEM,) * 6
        self.scratch = (
            pltpu.VMEM((8 * rows, width), bf16),
            pltpu.VMEM((here, 8 * rows), bf16),
            pltpu.VMEM((8 * rows // SPAN, SPAN, 2 * BLOCK), f32),
            pltpu.VMEM((here, 2 * BLOCK), f32),
            pltpu.VMEM((8, 2 * BLOCK), f32),
            pltpu.VMEM((8, 2 * BLOCK), f32),
            dma_sems(1),
        )
        parts = dict(gather=PlaneGather(block), scatter=PlaneScatter(rows, width, 0))
        if late:
            parts.update(heads=HeadGather(heads), biases=LineGather(biases))
            self.outs += parts["heads"].outs + parts["biases"].outs
            self.out_spaces += (pltpu.VMEM,) * 2
        self.use(**parts)

    def start(self, here, ins, outs, scratch):
        self.parts["gather"].start(here, ins[:1], scratch[:1], self.held(scratch, "gather"))
        if self.late:
            self.parts["heads"].start(here, ins[3:4], outs[8:9], self.held(scratch, "heads"))
            self.parts["biases"].start(here, ins[4:5], outs[9:10], self.held(scratch, "biases"))

    def finish(self, here, ins, outs, scratch):
        block_ref, doc_ref, scale_ref = ins[:3]
        heads_ref, bias_ref = outs[8:10] if self.late else ins[3:5]
        out_ref, rows_out, q_ref, k_ref, v_ref, z_ref, o_ref, l_ref = outs[:8]
        rows_buf, v_cols, s_buf, acc, top, total, save = scratch[:7]
        rows, model_width = block_ref.shape
        wide = self.head_width
        width = 2 * wide

        def bias_row(at):
            pair = [
                bias_ref[2 * here.core + i, self.layer : self.layer + 1, at : at + width]
                for i in range(2)
            ]
            lane = lax.broadcasted_iota(jnp.int32, (1, width), 1)
            return jnp.where(lane < wide, pair[0], pair[1])

        def work(first):
            block = pl.ds(first, rows)
            projected = lax.dot_general(
                rows_buf[block, :],
                heads_ref[0:3].reshape(3 * width, model_width),
                (((1,), (1,)), ((), ())),
                preferred_element_type=f32,
            )
            q = (projected[:, :width] + bias_row(0)).astype(bf16).astype(f32)
            q_ref[block, :] = (q * wide**-0.5).astype(bf16)
            k_ref[block, :] = projected[:, width : 2 * width].astype(bf16)
            v = (projected[:, 2 * width :] + bias_row(width)).astype(bf16)
            v_ref[block, :] = v
            v_cols[:, block] = turned(v)

        self.parts["gather"].finish(
            here,
            ins[:1],
            scratch[:1],
            self.held(scratch, "gather"),
            None if self.late else work,
        )
        keep_rows = pltpu.make_async_copy(rows_buf, rows_out, save.at[0])
        keep_rows.start()
        if self.late:
            self.parts["heads"].finish(here, ins[3:4], outs[8:9], self.held(scratch, "heads"))
            self.parts["biases"].finish(here, ins[4:5], outs[9:10], self.held(scratch, "biases"))
            in_chunks(8 * rows, rows, work)

        def rows_of(first):
            out = attend_block(
                wide, first, q_ref, k_ref, v_cols, doc_ref, o_ref, l_ref, s_buf, acc, top, total
            )
            z = (out * scale_ref[...]).astype(bf16)
            z_ref[pl.ds(first, rows), :] = z
            return z

        self.parts["scatter"].finish(
            here,
            None,
            (out_ref,),
            self.held(scratch, "scatter"),
            rows_of,
            lambda: heads_ref[3].reshape(width, model_width),
        )
        keep_rows.wait()


class AttnBackward(Parts):
    def __init__(self, block, docs, scale, heads, q, k, v, z, o, logs, attn_rows):
        rows, width = block.shape
        kinds, _, wide, _ = heads.shape
        self.head_width = wide
        here = 2 * wide
        self.arrays = (block, docs, scale, heads, q, k, v, z, o, logs, attn_rows)
        self.spaces = (pltpu.VMEM,) * 10 + (pl.ANY,)
        self.outs = (
            jax.ShapeDtypeStruct((rows, width), f32),
            jax.ShapeDtypeStruct((kinds, wide, width // 2), bf16),
            jax.ShapeDtypeStruct((3, here), f32),
        )
        self.out_spaces = (pltpu.VMEM,) * 3
        self.scratch = (
            pltpu.VMEM((8 * rows, width), bf16),
            pltpu.VMEM((8 * rows, width), bf16),
            pltpu.VMEM((here, 8 * rows), bf16),
            pltpu.VMEM((8 * rows, here), f32),
            pltpu.VMEM((8 * rows, here), f32),
            pltpu.VMEM((here, 2 * BLOCK), f32),
            pltpu.VMEM((8 * rows, 3 * here), bf16),
            pltpu.VMEM((here, width), f32),
            pltpu.VMEM(heads.shape, bf16),
            pltpu.VMEM((3, 8, here), f32),
            dma_sems(1),
        )
        self.use(
            gather=PlaneGather(block),
            scatter=PlaneScatter(rows, width, 0),
            heads=HeadScatter(heads),
        )

    def load(self, ins, scratch):
        return pltpu.make_async_copy(ins[10], scratch[1], scratch[10].at[0])

    def start(self, here, ins, outs, scratch):
        self.parts["gather"].start(here, ins[:1], scratch[:1], self.held(scratch, "gather"))
        self.load(ins, scratch).start()

    def finish(self, here, ins, outs, scratch):
        block_ref, doc_ref, scale_ref, heads_ref, q_ref, k_ref, v_ref, z_ref, o_ref, l_ref = ins[:10]
        out_ref, quarter_ref, small_ref = outs
        (
            rows_buf,
            attn_rows,
            k_cols,
            acc_k,
            acc_v,
            acc_q,
            proj,
            out_sum,
            heads_grad,
            small,
        ) = scratch[:10]
        rows, model_width = block_ref.shape
        wide = self.head_width
        width = 2 * wide
        acc_k[...] = jnp.zeros_like(acc_k)
        acc_v[...] = jnp.zeros_like(acc_v)
        out_sum[...] = jnp.zeros_like(out_sum)
        small[...] = jnp.zeros_like(small)
        k_cols[...] = turned(k_ref[...])

        def work(first):
            block = pl.ds(first, rows)
            scaled_grad = lax.dot_general(
                rows_buf[block, :],
                heads_ref[3].reshape(width, model_width),
                (((1,), (1,)), ((), ())),
                preferred_element_type=f32,
            )
            out_sum[...] += lax.dot_general(
                z_ref[block, :],
                rows_buf[block, :],
                (((0,), (0,)), ((), ())),
                preferred_element_type=f32,
            )
            small[0] += fold(o_ref[block, :] * scaled_grad)
            grad = attend_block_back(
                wide,
                first,
                (scaled_grad * scale_ref[...]).astype(bf16),
                q_ref,
                k_ref,
                k_cols,
                v_ref,
                o_ref,
                l_ref,
                doc_ref,
                acc_k,
                acc_v,
                acc_q,
            )
            proj[block, 0:width] = grad
            small[1] += fold(grad.astype(f32))

        self.parts["gather"].finish(
            here, ins[:1], scratch[:1], self.held(scratch, "gather"), work
        )

        def settle(first):
            block = pl.ds(first, rows)
            proj[block, width : 2 * width] = acc_k[block, :].astype(bf16)
            value_grad = acc_v[block, :].astype(bf16)
            proj[block, 2 * width : 3 * width] = value_grad
            small[2] += fold(value_grad.astype(f32))

        in_chunks(8 * rows, rows, settle)
        held = self.held(scratch, "heads")

        def early():
            self.load(ins, scratch).wait()
            qkv_grad = lax.dot_general(
                proj[...],
                attn_rows[...],
                (((0,), (0,)), ((), ())),
                preferred_element_type=f32,
            )
            heads_grad[0:3] = qkv_grad.astype(bf16).reshape(3, 2, wide, model_width)
            heads_grad[3] = out_sum[...].astype(bf16).reshape(2, wide, model_width)
            self.parts["heads"].start(here, (heads_grad,), None, held)

        self.parts["scatter"].finish(
            here,
            None,
            (out_ref,),
            self.held(scratch, "scatter"),
            lambda first: proj[pl.ds(first, rows), :],
            lambda: heads_ref[0:3].reshape(3 * width, model_width),
            early=early,
        )
        self.parts["heads"].finish(here, (heads_grad,), (quarter_ref,), held)
        for i in range(3):
            small_ref[i : i + 1, :] = jnp.sum(small[i], axis=0, keepdims=True)


def format_kernel(f0, f1, s0, s1, h0, h1, first_ref, second_ref, qkv_ref, out_ref):
    part = first_ref.shape[2] // 4
    half = h0.shape[3]
    for layer, (first, second, heads) in enumerate(((f0, s0, h0), (f1, s1, h1))):
        for i in range(4):
            first_ref[layer, :, i * part : (i + 1) * part] = first[i].astype(f32)
            second_ref[layer, i * part : (i + 1) * part, :] = second[i].astype(f32)
        for core in range(2):
            here = pl.ds(core * half, half)
            for kind in range(3):
                pair = jnp.concatenate([heads[core, kind], heads[2 + core, kind]], axis=0)
                qkv_ref[layer, kind, here, :] = jnp.transpose(pair.astype(f32))
            for y in range(2):
                wide = heads.shape[2]
                out_ref[layer, y * wide : (y + 1) * wide, here] = heads[2 * y + core, 3].astype(f32)


def format_weights(first, second, heads):
    _, width, part = first[0].shape
    wide = heads[0].shape[2]
    return pl.pallas_call(
        format_kernel,
        out_shape=(
            jax.ShapeDtypeStruct((2, width, 4 * part), f32),
            jax.ShapeDtypeStruct((2, 4 * part, width), f32),
            jax.ShapeDtypeStruct((2, 3, width, 2 * wide), f32),
            jax.ShapeDtypeStruct((2, 2 * wide, width), f32),
        ),
        in_specs=[pl.BlockSpec(memory_space=pltpu.VMEM)] * 6,
        out_specs=[pl.BlockSpec(memory_space=pltpu.VMEM)] * 4,
        compiler_params=vmem_params(None, 40),
    )(*first, *second, *heads)


def plane_device(
    tokens,
    segment_ids,
    cotangent,
    ln_attn_gain,
    ln_attn_bias,
    qkv_weight,
    qv_bias,
    head_scale,
    out_weight,
    out_bias,
    ln_post_gain,
    ln_post_bias,
    ln_ffn_gain,
    ln_ffn_bias,
    fc1_weight,
    fc1_bias,
    mid_gain,
    mid_bias,
    fc2_weight,
    fc2_bias,
):
    layers = qkv_weight.shape[0]
    model_width = tokens.shape[1]
    heads_all = head_scale.shape[1]
    head_width = model_width // heads_all
    hidden_here = fc1_weight.shape[2]
    hidden_all = hidden_here * 8
    quarter = hidden_here // 4
    half_width = model_width // 2
    x, y, core = lax.axis_index("x"), lax.axis_index("y"), lax.axis_index("core")
    quarter_at = 2 * y + core
    width = 2 * head_width
    ids = iter(range(1, 64))

    residual = to_plane(tokens).astype(f32)
    docs = to_plane(segment_ids).astype(f32)[None, :]
    gradient = to_plane(cotangent).astype(f32)

    def cut(values, at, size, axis):
        return lax.dynamic_slice_in_dim(values, at * size, size, axis)

    head_parts = []
    for layer in range(layers):
        qkv = cut(cut(qkv_weight[layer], core, half_width, 0), y, head_width, 2)
        out = cut(cut(out_weight[layer], y, head_width, 0), core, half_width, 1)
        head_parts.append(jnp.concatenate([jnp.transpose(qkv, (1, 2, 0)), out[None]], axis=0))
    bias_heads = cut(qv_bias, y, head_width, 2)
    small = jnp.concatenate(
        [
            jnp.concatenate([bias_heads, bias_heads], axis=2).reshape(layers, 2 * width),
            cut(fc1_bias, quarter_at, quarter, 1),
            cut(mid_gain, quarter_at, quarter, 1),
            cut(mid_bias, quarter_at, quarter, 1),
        ],
        axis=1,
    )
    head_ids = ((2 * core + jnp.arange(2)) * 2 + x) * 2 + y
    head_onehot = (head_ids[:, None] == jnp.arange(heads_all)[None, :]).astype(f32)
    heads_here = [None] * layers

    stored = []
    for layer in range(layers):
        attn_in, attn_normal, attn_factor = norm_local(
            residual, ln_attn_gain[layer], ln_attn_bias[layer]
        )
        scale = jnp.sum(head_onehot * head_scale[layer][None, :], axis=1)
        scale_row = jnp.repeat(scale, head_width)[None, :]
        late = layer == 0
        ((branch, attn_rows, q, k, v, scaled, attended, logs, *got), (first_here,), (second_here,)) = (
            run_tasks(
                ids,
                AttnForward(
                    attn_in.astype(bf16),
                    docs,
                    scale_row,
                    head_parts[0] if late else heads_here[layer],
                    small,
                    layer,
                    late,
                ),
                WeightGather(fc1_weight, layer, 1),
                WeightGather(fc2_weight, layer, 0),
                mib=40,
            )
        )
        if late:
            heads_here[0], small = got

            def hidden_rows(at):
                part = small[:, :, 2 * width + at * quarter : 2 * width + (at + 1) * quarter]
                return jnp.transpose(part, (1, 0, 2)).reshape(layers, 4 * quarter)

            shift_hidden, gain_hidden, bias_hidden = map(hidden_rows, range(3))
        branch = branch + out_bias[layer]
        post_out, post_normal, post_factor = norm_local(
            branch, ln_post_gain[layer], ln_post_bias[layer]
        )
        middle = residual + post_out
        ffn_in, ffn_normal, ffn_factor = norm_local(middle, ln_ffn_gain[layer], ln_ffn_bias[layer])
        ((ffn_out, ffn_rows, before, mixed, totals), *got) = run_tasks(
            ids,
            FfnForward(
                ffn_in.astype(bf16),
                first_here,
                second_here,
                shift_hidden[layer][None],
                gain_hidden[layer][None],
                bias_hidden[layer][None],
            ),
            *([HeadGather(head_parts[layer + 1])] if layer + 1 < layers else []),
            mib=48,
        )
        if got:
            heads_here[layer + 1] = got[0][0]
        stored.append(
            (
                first_here,
                second_here,
                attn_normal,
                attn_factor,
                attn_rows,
                q,
                k,
                v,
                attended,
                logs,
                scale_row,
                scaled,
                post_normal,
                post_factor,
                ffn_normal,
                ffn_factor,
                ffn_rows,
                before,
                mixed,
                totals,
            )
        )
        residual = middle + ffn_out + fc2_bias[layer]
    layer_output = from_plane(residual.astype(bf16))

    first_done, second_done = [None] * layers, [None] * layers
    heads_done, hidden_done = [None] * layers, [None] * layers
    early_vectors, late_vectors = [None] * layers, [None] * layers
    pending = None
    for layer in reversed(range(layers)):
        (
            first_here,
            second_here,
            attn_normal,
            attn_factor,
            attn_rows,
            q,
            k,
            v,
            attended,
            logs,
            scale_row,
            scaled,
            post_normal,
            post_factor,
            ffn_normal,
            ffn_factor,
            ffn_rows,
            before,
            mixed,
            totals,
        ) = stored[layer]
        second_shift_grad = jnp.sum(gradient, axis=0)
        sides = []
        if pending is not None:
            sides = [RowsGather(pending[0]), RowsGather(pending[1]), LineThenRows(pending[2])]
        ((ffn_in_grad, first_grad, second_grad, hidden_grad), *got) = run_tasks(
            ids,
            FfnBackward(
                gradient.astype(bf16),
                first_here,
                second_here,
                gain_hidden[layer][None],
                before,
                mixed,
                ffn_rows,
                totals,
            ),
            *sides,
            mib=60,
        )
        if got:
            first_done[layer + 1], heads_done[layer + 1], hidden_done[layer + 1] = (
                each[0] for each in got
            )
        ffn_gain_grad = jnp.sum(ffn_in_grad * ffn_normal, axis=0)
        ffn_bias_grad = jnp.sum(ffn_in_grad, axis=0)
        middle_grad = gradient + norm_back(ffn_in_grad, ffn_normal, ffn_factor, ln_ffn_gain[layer])
        post_gain_grad = jnp.sum(middle_grad * post_normal, axis=0)
        post_bias_grad = jnp.sum(middle_grad, axis=0)
        branch_grad = norm_back(middle_grad, post_normal, post_factor, ln_post_gain[layer])
        out_shift_grad = jnp.sum(branch_grad, axis=0)
        early_vectors[layer] = jnp.stack(
            [
                out_shift_grad,
                post_gain_grad,
                post_bias_grad,
                ffn_gain_grad,
                ffn_bias_grad,
                second_shift_grad,
            ]
        )
        sides = [LineScatter(first_grad), RowsGather(second_grad)]
        if layer == 0:
            known = early_vectors + late_vectors[1:]
            count = sum(each.shape[0] for each in known)
            known.append(jnp.zeros((-count % 8, model_width), f32))
            sides.append(PlaneSum(jnp.concatenate(known, axis=0)))
        ((attn_in_grad, heads_grad, small_grad), (first_grad,), (second_done[layer],), *rest) = (
            run_tasks(
                ids,
                AttnBackward(
                    branch_grad.astype(bf16),
                    docs,
                    scale_row,
                    heads_here[layer],
                    q,
                    k,
                    v,
                    scaled,
                    attended,
                    logs,
                    attn_rows,
                ),
                *sides,
                mib=48,
            )
        )
        scale_grad = jnp.sum(
            head_onehot * jnp.sum(small_grad[0].reshape(2, head_width), axis=1)[:, None], axis=0
        )
        bias_grad = jnp.transpose(small_grad[1:].reshape(2, 2, head_width), (1, 0, 2))
        hidden_grad = jnp.roll(hidden_grad, 1, axis=0).reshape(3, 4, quarter)
        hidden_grad = jnp.concatenate(
            [
                jnp.transpose(hidden_grad, (1, 0, 2)).reshape(4, -1),
                lax.dynamic_update_slice(
                    jnp.zeros((4, width), f32), bias_grad.reshape(2, width), (2 * core, 0)
                ),
            ],
            axis=1,
        ).reshape(4, -1, 128)
        pending = (first_grad, heads_grad, hidden_grad)
        late_vectors[layer] = jnp.stack(
            [
                jnp.sum(attn_in_grad * attn_normal, axis=0),
                jnp.sum(attn_in_grad, axis=0),
                jnp.pad(scale_grad, (0, model_width - heads_all)),
            ]
        )
        gradient = middle_grad + norm_back(
            attn_in_grad, attn_normal, attn_factor, ln_attn_gain[layer]
        )
    input_grad = from_plane(gradient.astype(bf16)).astype(f32)
    ((vectors,), (first_done[0],), (heads_done[0],), (hidden_done[0],)) = run_tasks(
        ids,
        PlaneThenLineSum(late_vectors[0], rest[0][0]),
        RowsGather(pending[0]),
        RowsGather(pending[1]),
        LineThenRows(pending[2]),
    )
    early = vectors[: 6 * layers].reshape(layers, 6, model_width)
    late = jnp.stack([vectors[-3:], vectors[6 * layers : 6 * layers + 3]])
    first_grad, second_grad, qkv_grad, out_grad = format_weights(
        first_done,
        second_done,
        heads_done,
    )
    hidden = jnp.stack(hidden_done).reshape(layers, 4, -1)
    bias_grad = jnp.sum(hidden[:, :, 3 * quarter :].reshape(layers, 2, 2, 2, head_width), axis=2)
    bias_grad = jnp.transpose(bias_grad, (0, 2, 1, 3)).reshape(layers, 2, width)
    hidden = hidden[:, :, : 3 * quarter].reshape(layers, 4, 3, quarter)
    hidden = jnp.transpose(hidden, (0, 2, 1, 3)).reshape(layers, 3, hidden_here)
    return (
        layer_output,
        input_grad,
        late[:, 0],
        late[:, 1],
        jnp.transpose(qkv_grad, (0, 2, 1, 3)),
        bias_grad,
        late[:, 2, :heads_all],
        out_grad,
        early[:, 0],
        early[:, 1],
        early[:, 2],
        early[:, 3],
        early[:, 4],
        first_grad,
        hidden[:, 0],
        hidden[:, 1],
        hidden[:, 2],
        second_grad,
        early[:, 5],
    )


def split_specs(rows, mp):
    both = tuple(rows) + tuple(mp)
    in_specs = (
        P(both, None),
        P(rows),
        P(both, None),
        P(),
        P(),
        P(None, None, None, mp),
        P(None, None, mp),
        P(),
        P(None, mp, None),
        P(),
        P(),
        P(),
        P(),
        P(),
        P(None, None, mp),
        P(None, mp),
        P(None, mp),
        P(None, mp),
        P(None, mp, None),
        P(),
    )
    out_specs = (
        P(both, None),
        P(both, None),
        P(),
        P(),
        P(None, None, None, mp),
        P(None, None, mp),
        P(),
        P(None, mp, None),
        P(),
        P(),
        P(),
        P(),
        P(),
        P(None, None, mp),
        P(None, mp),
        P(None, mp),
        P(None, mp),
        P(None, mp, None),
        P(),
    )
    return in_specs, out_specs


def solution(mesh):
    if mesh.shape["rows"] == 4 and mesh.shape["mp"] == 8:
        planes = Mesh(mesh.devices.reshape(2, 2, 4, 2), ("y", "core", "z", "x"))
        in_specs, out_specs = split_specs(("y", "core"), ("z", "x"))
        return jax.shard_map(
            plane_device, mesh=planes, in_specs=in_specs, out_specs=out_specs, check_vma=False
        )
    in_specs, out_specs = split_specs(("rows",), ("mp",))
    return jax.shard_map(
        per_device, mesh=mesh, in_specs=in_specs, out_specs=out_specs, check_vma=False
    )
```

```python
from functools import partial

import jax
import jax.numpy as jnp
from jax import lax
from jax.experimental import pallas as pl
from jax.experimental.pallas import tpu as pltpu
from jax.sharding import Mesh
from jax.sharding import PartitionSpec as P

epsilon = 1e-05
masked = -1e30


def partner(shard, axis, stride):
    return lax.ppermute(shard, axis, [(i, i ^ 1 << stride) for i in range(lax.axis_size(axis))])


def norm_local(values, gain_row, bias_row):
    average = jnp.mean(values, axis=-1, keepdims=True)
    centered = values - average
    spread = jnp.mean(centered * centered, axis=-1, keepdims=True)
    factor = lax.rsqrt(spread + epsilon)
    normal = centered * factor
    return (normal * gain_row + bias_row, normal, factor)


def norm_back(grad_out, normal, factor, gain_row):
    scaled = grad_out * gain_row
    inner_sum = jnp.mean(scaled * normal, axis=-1, keepdims=True)
    return factor * (scaled - jnp.mean(scaled, axis=-1, keepdims=True) - normal * inner_sum)


def collect_rows(normed_b):
    return lax.all_gather(normed_b, "mp", axis=0, tiled=True)


def collect_grads(gradient_b):
    return lax.all_gather(gradient_b, "mp", axis=0, tiled=True)


def reduce_branch(operand_b, weight_b, local_rows):

    def partial_term(first_row, count):
        return jnp.dot(operand_b, weight_b, preferred_element_type=jnp.float32)

    return lax.psum_scatter(
        partial_term(jnp.int32(0), local_rows * lax.axis_size("mp")).astype(jnp.bfloat16),
        "mp",
        scatter_dimension=0,
        tiled=True,
    ).astype(jnp.float32)


def reduce_grads(operand_b, weight_b, local_rows):

    def partial_term(first_row, count):
        return jnp.einsum("tc,dc->td", operand_b, weight_b, preferred_element_type=jnp.float32)

    return lax.psum_scatter(
        partial_term(jnp.int32(0), local_rows * lax.axis_size("mp")).astype(jnp.bfloat16),
        "mp",
        scatter_dimension=0,
        tiled=True,
    ).astype(jnp.float32)


def hidden_stats(first_sum, second_sum):
    return lax.psum((first_sum, second_sum), "mp")


def hidden_grad_stats(first_sum, second_sum):
    return lax.psum((first_sum, second_sum), "mp")


def join_cols(mine, other, is_upper):
    lower_part = jnp.where(is_upper, other, mine)
    upper_part = jnp.where(is_upper, mine, other)
    return jnp.concatenate([lower_part, upper_part], axis=-1)


def join_rows(mine, other, is_upper):
    lower_part = jnp.where(is_upper, other, mine)
    upper_part = jnp.where(is_upper, mine, other)
    return jnp.concatenate([lower_part, upper_part], axis=0)


def split_cols(values, cols_here, is_upper):
    lower_part = values[..., :cols_here]
    upper_part = values[..., cols_here:]
    return (
        jnp.where(is_upper, upper_part, lower_part),
        jnp.where(is_upper, lower_part, upper_part),
    )


def masked_scores(query_block, key_rows, query_start, block_rows, doc_rows, positions):
    factor = query_block.shape[-1] ** (-0.5)
    scores = (
        jnp.einsum("qhe,khe->hqk", query_block, key_rows, preferred_element_type=jnp.float32)
        * factor
    )
    query_place = query_start + jnp.arange(block_rows, dtype=jnp.int32)
    query_docs = lax.dynamic_slice_in_dim(doc_rows, query_start, block_rows, 0)
    allowed = (query_docs[:, None] == doc_rows[None, :]) & (
        query_place[:, None] >= positions[None, :]
    )
    return jnp.where(allowed[None], scores, masked)


def attend_forward(queries, key_rows, value_rows, doc_rows, row_offset):
    total_rows = queries.shape[0]
    block_rows = min(512, total_rows)
    positions = jnp.arange(key_rows.shape[0], dtype=jnp.int32)

    def one_block(first_row):
        query_block = lax.dynamic_slice_in_dim(queries, first_row, block_rows, 0)
        scores = masked_scores(
            query_block, key_rows, row_offset + first_row, block_rows, doc_rows, positions
        )
        row_peak = jnp.max(scores, axis=-1, keepdims=True)
        weights = jnp.exp(scores - row_peak)
        totals = jnp.sum(weights, axis=-1, keepdims=True)
        probabilities = (weights / totals).astype(jnp.bfloat16)
        output = jnp.einsum(
            "hqk,khe->qhe", probabilities, value_rows, preferred_element_type=jnp.float32
        )
        return (output, (row_peak + jnp.log(totals))[..., 0])

    starts = jnp.arange(total_rows // block_rows, dtype=jnp.int32) * block_rows
    outputs, log_totals = lax.map(one_block, starts)
    return (outputs.reshape(queries.shape), log_totals)


def attend_backward(queries, key_rows, value_rows, doc_rows, row_offset, log_totals, grad_out):
    total_rows = queries.shape[0]
    block_rows = min(512, total_rows)
    positions = jnp.arange(key_rows.shape[0], dtype=jnp.int32)
    factor = queries.shape[-1] ** (-0.5)

    def one_block(running, first_row):
        key_grad, value_grad = running
        query_block = lax.dynamic_slice_in_dim(queries, first_row, block_rows, 0)
        grad_block = lax.dynamic_slice_in_dim(grad_out, first_row, block_rows, 0)
        scores = masked_scores(
            query_block, key_rows, row_offset + first_row, block_rows, doc_rows, positions
        )
        block_totals = lax.dynamic_index_in_dim(
            log_totals, first_row // block_rows, 0, keepdims=False
        )
        probabilities = jnp.exp(scores - block_totals[..., None])
        prob_grad = jnp.einsum(
            "qhe,khe->hqk", grad_block, value_rows, preferred_element_type=jnp.float32
        )
        inner_sum = jnp.sum(probabilities * prob_grad, axis=-1, keepdims=True)
        score_grad = (probabilities * (prob_grad - inner_sum)).astype(jnp.bfloat16)
        query_grad = (
            jnp.einsum("hqk,khe->qhe", score_grad, key_rows, preferred_element_type=jnp.float32)
            * factor
        )
        key_grad = (
            key_grad
            + jnp.einsum(
                "hqk,qhe->khe", score_grad, query_block, preferred_element_type=jnp.float32
            )
            * factor
        )
        value_grad = value_grad + jnp.einsum(
            "hqk,qhe->khe",
            probabilities.astype(jnp.bfloat16),
            grad_block,
            preferred_element_type=jnp.float32,
        )
        return ((key_grad, value_grad), query_grad)

    starts = jnp.arange(total_rows // block_rows, dtype=jnp.int32) * block_rows
    zero_grads = jnp.zeros(key_rows.shape, jnp.float32)
    (key_grad, value_grad), query_grads = lax.scan(one_block, (zero_grads, zero_grads), starts)
    return (query_grads.reshape(queries.shape), key_grad, value_grad)


def stack_layers(layer_list, members):
    stacked = []
    for member_index in range(members):
        stacked.append(jnp.stack([entry[member_index] for entry in layer_list], axis=0))
    return stacked


def per_device(
    tokens,
    segment_ids,
    cotangent,
    ln_attn_gain,
    ln_attn_bias,
    qkv_weight,
    qv_bias,
    head_scale,
    out_weight,
    out_bias,
    ln_post_gain,
    ln_post_bias,
    ln_ffn_gain,
    ln_ffn_bias,
    fc1_weight,
    fc1_bias,
    mid_gain,
    mid_bias,
    fc2_weight,
    fc2_bias,
):
    layers = qkv_weight.shape[0]
    local_rows = tokens.shape[0]
    model_width = tokens.shape[1]
    cols_here = qkv_weight.shape[3]
    heads_all = head_scale.shape[1]
    head_width = model_width // heads_all
    pair_cols = 2 * cols_here
    pair_heads = pair_cols // head_width
    group_rows = segment_ids.shape[0]
    half_rows = group_rows // 2
    hidden_all = fc1_weight.shape[2] * lax.axis_size("mp")
    device_index = lax.axis_index("mp")
    is_upper = device_index % 2 == 1
    own_start = jnp.where(is_upper, half_rows, 0).astype(jnp.int32)
    other_start = jnp.where(is_upper, 0, half_rows).astype(jnp.int32)
    first_head = device_index // 2 * pair_heads
    pair_onehot = (
        (first_head + jnp.arange(pair_heads, dtype=jnp.int32))[:, None]
        == jnp.arange(heads_all, dtype=jnp.int32)[None, :]
    ).astype(jnp.float32)
    residual = tokens.astype(jnp.float32)
    stored = []
    for layer_index in range(layers):
        attn_in, attn_normal, attn_factor = norm_local(
            residual, ln_attn_gain[layer_index], ln_attn_bias[layer_index]
        )
        attn_rows = collect_rows(attn_in.astype(jnp.bfloat16))
        qkv_here = qkv_weight[layer_index].reshape(model_width, 3 * cols_here)
        projected = jnp.dot(attn_rows, qkv_here, preferred_element_type=jnp.float32).reshape(
            -1, 3, cols_here
        )
        bias_pair = qv_bias[layer_index]
        query_mine = (projected[:, 0] + bias_pair[0]).astype(jnp.bfloat16)
        key_mine = projected[:, 1].astype(jnp.bfloat16)
        value_mine = (projected[:, 2] + bias_pair[1]).astype(jnp.bfloat16)
        query_send = lax.dynamic_slice_in_dim(query_mine, other_start, half_rows, 0)
        query_recv, key_recv, value_recv = partner((query_send, key_mine, value_mine), "mp", 0)
        query_own = lax.dynamic_slice_in_dim(query_mine, own_start, half_rows, 0)
        queries = join_cols(query_own, query_recv, is_upper).reshape(
            half_rows, pair_heads, head_width
        )
        key_rows = join_cols(key_mine, key_recv, is_upper).reshape(
            group_rows, pair_heads, head_width
        )
        value_rows = join_cols(value_mine, value_recv, is_upper).reshape(
            group_rows, pair_heads, head_width
        )
        attended, log_totals = attend_forward(queries, key_rows, value_rows, segment_ids, own_start)
        pair_scale = jnp.sum(pair_onehot * head_scale[layer_index][None, :], axis=1)
        scaled_half = (
            (attended * pair_scale[None, :, None])
            .astype(jnp.bfloat16)
            .reshape(half_rows, pair_cols)
        )
        own_cols, other_cols = split_cols(scaled_half, cols_here, is_upper)
        scaled_recv = partner(other_cols, "mp", 0)
        scaled_mine = join_rows(own_cols, scaled_recv, is_upper)
        branch = (
            reduce_branch(scaled_mine, out_weight[layer_index], local_rows) + out_bias[layer_index]
        )
        post_out, post_normal, post_factor = norm_local(
            branch, ln_post_gain[layer_index], ln_post_bias[layer_index]
        )
        middle = residual + post_out
        ffn_in, ffn_normal, ffn_factor = norm_local(
            middle, ln_ffn_gain[layer_index], ln_ffn_bias[layer_index]
        )
        ffn_rows = collect_rows(ffn_in.astype(jnp.bfloat16))
        before_gelu = (
            jnp.dot(ffn_rows, fc1_weight[layer_index], preferred_element_type=jnp.float32)
            + fc1_bias[layer_index]
        )
        activated = jax.nn.gelu(before_gelu, approximate=False)
        first_sum, second_sum = hidden_stats(
            jnp.sum(activated, axis=1), jnp.sum(activated * activated, axis=1)
        )
        average = first_sum / hidden_all
        spread = second_sum / hidden_all - average * average
        hidden_factor = lax.rsqrt(spread + epsilon)[:, None]
        hidden_normal = (activated - average[:, None]) * hidden_factor
        mixed_b = (hidden_normal * mid_gain[layer_index] + mid_bias[layer_index]).astype(
            jnp.bfloat16
        )
        ffn_out = reduce_branch(mixed_b, fc2_weight[layer_index], local_rows)
        stored.append(
            (
                attn_normal,
                attn_factor,
                attn_rows,
                queries,
                key_rows,
                value_rows,
                attended,
                log_totals,
                pair_scale,
                scaled_mine,
                post_normal,
                post_factor,
                ffn_normal,
                ffn_factor,
                ffn_rows,
                before_gelu,
                hidden_normal,
                hidden_factor,
                mixed_b,
            )
        )
        residual = middle + ffn_out + fc2_bias[layer_index]
    layer_output = residual.astype(jnp.bfloat16)
    gradient = cotangent.astype(jnp.float32)
    sharded_list = []
    shared_list = []
    for layer_index in reversed(range(layers)):
        (
            attn_normal,
            attn_factor,
            attn_rows,
            queries,
            key_rows,
            value_rows,
            attended,
            log_totals,
            pair_scale,
            scaled_mine,
            post_normal,
            post_factor,
            ffn_normal,
            ffn_factor,
            ffn_rows,
            before_gelu,
            hidden_normal,
            hidden_factor,
            mixed_b,
        ) = stored[layer_index]
        qkv_here = qkv_weight[layer_index].reshape(model_width, 3 * cols_here)
        second_shift_grad = jnp.sum(gradient, axis=0)
        grad_rows = collect_grads(gradient.astype(jnp.bfloat16))
        mixed_grad = jnp.einsum(
            "td,fd->tf", grad_rows, fc2_weight[layer_index], preferred_element_type=jnp.float32
        )
        second_grad = jnp.einsum(
            "tf,td->fd", mixed_b, grad_rows, preferred_element_type=jnp.float32
        )
        hidden_gain_grad = jnp.sum(mixed_grad * hidden_normal, axis=0)
        hidden_shift_grad = jnp.sum(mixed_grad, axis=0)
        normal_grad = mixed_grad * mid_gain[layer_index]
        grad_first, grad_second = hidden_grad_stats(
            jnp.sum(normal_grad, axis=1), jnp.sum(normal_grad * hidden_normal, axis=1)
        )
        active_grad = hidden_factor * (
            normal_grad
            - grad_first[:, None] / hidden_all
            - hidden_normal * grad_second[:, None] / hidden_all
        )
        gelu_pull = jax.vjp(partial(jax.nn.gelu, approximate=False), before_gelu)[1]
        pre_grad_b = gelu_pull(active_grad)[0].astype(jnp.bfloat16)
        first_shift_grad = jnp.sum(pre_grad_b, axis=0, dtype=jnp.float32)
        first_grad = jnp.einsum(
            "td,tf->df", ffn_rows, pre_grad_b, preferred_element_type=jnp.float32
        )
        ffn_in_grad = reduce_grads(pre_grad_b, fc1_weight[layer_index], local_rows)
        ffn_gain_grad = jnp.sum(ffn_in_grad * ffn_normal, axis=0)
        ffn_bias_grad = jnp.sum(ffn_in_grad, axis=0)
        middle_grad = gradient + norm_back(
            ffn_in_grad, ffn_normal, ffn_factor, ln_ffn_gain[layer_index]
        )
        post_gain_grad = jnp.sum(middle_grad * post_normal, axis=0)
        post_bias_grad = jnp.sum(middle_grad, axis=0)
        branch_grad = norm_back(middle_grad, post_normal, post_factor, ln_post_gain[layer_index])
        out_shift_grad = jnp.sum(branch_grad, axis=0)
        branch_rows = collect_grads(branch_grad.astype(jnp.bfloat16))
        scaled_grad = jnp.einsum(
            "td,cd->tc", branch_rows, out_weight[layer_index], preferred_element_type=jnp.float32
        )
        out_grad = jnp.einsum(
            "tc,td->cd", scaled_mine, branch_rows, preferred_element_type=jnp.float32
        )
        grad_send = lax.dynamic_slice_in_dim(scaled_grad, other_start, half_rows, 0)
        grad_recv = partner(grad_send.astype(jnp.bfloat16), "mp", 0).astype(grad_send.dtype)
        grad_own = lax.dynamic_slice_in_dim(scaled_grad, own_start, half_rows, 0)
        scaled_pair = join_cols(grad_own, grad_recv, is_upper).reshape(
            half_rows, pair_heads, head_width
        )
        pair_scale_grad = jnp.sum(attended * scaled_pair, axis=(0, 2))
        scale_grad = jnp.sum(pair_onehot * pair_scale_grad[:, None], axis=0)
        attended_grad_b = (scaled_pair * pair_scale[None, :, None]).astype(jnp.bfloat16)
        query_grad, key_grad, value_grad = attend_backward(
            queries, key_rows, value_rows, segment_ids, own_start, log_totals, attended_grad_b
        )
        query_own, query_other = split_cols(
            query_grad.reshape(half_rows, pair_cols), cols_here, is_upper
        )
        key_own, key_other = split_cols(
            key_grad.reshape(group_rows, pair_cols), cols_here, is_upper
        )
        value_own, value_other = split_cols(
            value_grad.reshape(group_rows, pair_cols), cols_here, is_upper
        )
        query_recv, key_recv, value_recv = (
            partner(query_other.astype(jnp.bfloat16), "mp", 0).astype(query_other.dtype),
            partner(key_other.astype(jnp.bfloat16), "mp", 0).astype(key_other.dtype),
            partner(value_other.astype(jnp.bfloat16), "mp", 0).astype(value_other.dtype),
        )
        query_grad_b = join_rows(query_own, query_recv, is_upper).astype(jnp.bfloat16)
        key_grad_b = (key_own + key_recv).astype(jnp.bfloat16)
        value_grad_b = (value_own + value_recv).astype(jnp.bfloat16)
        proj_grad = jnp.stack([query_grad_b, key_grad_b, value_grad_b], axis=1).reshape(
            -1, 3 * cols_here
        )
        pair_grad = jnp.stack(
            [
                jnp.sum(query_grad_b, axis=0, dtype=jnp.float32),
                jnp.sum(value_grad_b, axis=0, dtype=jnp.float32),
            ],
            axis=0,
        )
        qkv_grad = jnp.einsum(
            "td,tc->dc", attn_rows, proj_grad, preferred_element_type=jnp.float32
        ).reshape(model_width, 3, cols_here)
        attn_in_grad = reduce_grads(proj_grad, qkv_here, local_rows)
        attn_gain_grad = jnp.sum(attn_in_grad * attn_normal, axis=0)
        attn_bias_grad = jnp.sum(attn_in_grad, axis=0)
        gradient = middle_grad + norm_back(
            attn_in_grad, attn_normal, attn_factor, ln_attn_gain[layer_index]
        )
        sharded_list.insert(
            0,
            (
                qkv_grad,
                pair_grad,
                out_grad,
                first_grad,
                first_shift_grad,
                hidden_gain_grad,
                hidden_shift_grad,
                second_grad,
            ),
        )
        shared_list.insert(
            0,
            (
                attn_gain_grad,
                attn_bias_grad,
                scale_grad,
                out_shift_grad,
                post_gain_grad,
                post_bias_grad,
                ffn_gain_grad,
                ffn_bias_grad,
                second_shift_grad,
            ),
        )
    sharded = stack_layers(sharded_list, 8)
    shared = stack_layers(shared_list, 9)
    sharded = (
        lax.psum(sharded[0].astype(jnp.bfloat16), "rows").astype(jnp.float32),
        lax.psum(sharded[1].astype(jnp.bfloat16), "rows").astype(jnp.float32),
        lax.psum(sharded[2].astype(jnp.bfloat16), "rows").astype(jnp.float32),
        lax.psum(sharded[3].astype(jnp.bfloat16), "rows").astype(jnp.float32),
        lax.psum(sharded[4].astype(jnp.bfloat16), "rows").astype(jnp.float32),
        lax.psum(sharded[5].astype(jnp.bfloat16), "rows").astype(jnp.float32),
        lax.psum(sharded[6].astype(jnp.bfloat16), "rows").astype(jnp.float32),
        lax.psum(sharded[7].astype(jnp.bfloat16), "rows").astype(jnp.float32),
    )
    shared = lax.psum(
        (
            shared[0],
            shared[1],
            shared[2],
            shared[3],
            shared[4],
            shared[5],
            shared[6],
            shared[7],
            shared[8],
        ),
        ("rows", "mp"),
    )
    return (
        layer_output,
        gradient,
        shared[0],
        shared[1],
        sharded[0],
        sharded[1],
        shared[2],
        sharded[2],
        shared[3],
        shared[4],
        shared[5],
        shared[6],
        shared[7],
        sharded[3],
        sharded[4],
        sharded[5],
        sharded[6],
        sharded[7],
        shared[8],
    )


MESH_ID = pl.DeviceIdType.MESH
PLANE = ("core", "y", "x")
EVERY = ("y", "core", "z", "x")
f32 = jnp.float32
bf16 = jnp.bfloat16


def vmem_params(collective_id=None, mib=24):
    if collective_id is None:
        return pltpu.CompilerParams(vmem_limit_bytes=mib * 2**20)
    return pltpu.CompilerParams(
        vmem_limit_bytes=mib * 2**20, collective_id=collective_id, has_side_effects=True
    )


class Here:
    def __init__(self):
        self.x, self.y = lax.axis_index("x"), lax.axis_index("y")
        self.core, self.z = lax.axis_index("core"), lax.axis_index("z")

    def peer(self, flip_x, flip_y, flip_core, step_z):
        place = {}
        if flip_x:
            place["x"] = 1 - self.x
        if flip_y:
            place["y"] = 1 - self.y
        if flip_core:
            place["core"] = 1 - self.core
        if step_z:
            place["z"] = lax.rem(self.z + step_z, 4)
        return place

    def block(self, at_core, at_x, at_y):
        return (2 * at_core + lax.rem(at_y + self.z, 2)) * 2 + at_x


BY_X, BY_Y, BY_CORE = (1, 0, 0, 0), (0, 1, 0, 0), (0, 0, 1, 0)
BY_Z = tuple((0, 0, 0, step) for step in (1, 2, 3))
BY_LINE = BY_Z + tuple((0, 0, 1, step) for step in range(4))
BY_PLANE = tuple((flip & 1, flip >> 1 & 1, flip >> 2, 0) for flip in range(1, 8))


def remote(source, target, send_sem, recv_sem, place):
    return pltpu.make_async_remote_copy(
        src_ref=source,
        dst_ref=target,
        send_sem=send_sem,
        recv_sem=recv_sem,
        device_id=place,
        device_id_type=MESH_ID,
    )


def dma_sems(count):
    return pltpu.SemaphoreType.DMA((count,))


class Task:
    arrays = ()
    spaces = ()
    outs = ()
    out_spaces = ()
    scratch = ()
    reach = ()

    def between(self):
        pass

    def start(self, here, ins, outs, scratch):
        pass

    def middle(self, here, ins, outs, scratch):
        pass

    def finish(self, here, ins, outs, scratch):
        pass


def run_tasks(ids, *tasks, mib=24):
    reach = []
    for task in tasks:
        reach += [way for way in task.reach if way not in reach]

    def kernel(*refs):
        refs = list(refs)
        views = [[], [], []]
        for kind, name in enumerate(("arrays", "outs", "scratch")):
            for task in tasks:
                count = len(getattr(task, name))
                views[kind].append(refs[:count])
                refs = refs[count:]
        here = Here()
        barrier = pltpu.get_barrier_semaphore()
        for way in reach:
            pl.semaphore_signal(barrier, inc=1, device_id=here.peer(*way), device_id_type=MESH_ID)
        pl.semaphore_wait(barrier, len(reach))
        for task, *held in zip(tasks, *views):
            task.start(here, *held)

        def between():
            for task, *held in zip(tasks, *views):
                task.middle(here, *held)

        tasks[0].between = between
        for task, *held in zip(tasks, *views):
            task.finish(here, *held)

    results = pl.pallas_call(
        kernel,
        out_shape=[out for task in tasks for out in task.outs],
        in_specs=[pl.BlockSpec(memory_space=s) for task in tasks for s in task.spaces],
        out_specs=[pl.BlockSpec(memory_space=s) for task in tasks for s in task.out_spaces],
        scratch_shapes=[each for task in tasks for each in task.scratch],
        compiler_params=vmem_params(next(ids), mib),
    )(*[array for task in tasks for array in task.arrays])
    results = list(results)
    split = []
    for task in tasks:
        split.append(results[: len(task.outs)])
        results = results[len(task.outs) :]
    return split


class PlaneMove(Task):
    def __init__(self, values, back=False):
        self.back = back
        self.arrays, self.spaces = (values,), (pltpu.HBM,)
        self.outs = (jax.ShapeDtypeStruct(values.shape, values.dtype),)
        self.out_spaces = (pltpu.HBM,)
        self.scratch = (
            pltpu.VMEM((2, *values.shape), values.dtype),
            dma_sems(3),
            dma_sems(3),
        )
        self.reach = (BY_Y,) + BY_LINE

    def bend(self, here):
        return lax.rem(here.z + here.core, 2) == here.y

    def ends(self, here):
        targets = [{"core": here.z // 2, "z": 2 * y + here.core} for y in range(2)]
        at_home = [(here.z // 2 == here.core) & (2 * y + here.core == here.z) for y in range(2)]
        origin_core = lax.rem(here.z, 2)
        origin_z = 2 * here.core + lax.rem(here.y + origin_core, 2)
        origin_home = (origin_core == here.core) & (origin_z == here.z)
        return targets, at_home, {"core": origin_core, "z": origin_z}, origin_home

    def plan(self, here, ins, outs, scratch):
        held, send, recv = scratch
        targets, at_home, origin, origin_home = self.ends(here)
        bend = self.bend(here)
        to_y = here.peer(*BY_Y)
        legs = {}
        if not self.back:
            legs["own"] = (bend, pltpu.make_async_copy(ins[0], held.at[here.y], recv.at[1]))
            legs["over"] = (
                jnp.logical_not(bend),
                remote(ins[0], held.at[here.y], send.at[2], recv.at[0], to_y),
            )
            for y in range(2):
                away = remote(held.at[y], outs[0], send.at[y], recv.at[2], targets[y])
                stay = pltpu.make_async_copy(held.at[y], outs[0], recv.at[2])
                legs["away", y] = (bend & jnp.logical_not(at_home[y]), away)
                legs["stay", y] = (bend & at_home[y], stay)
        else:
            group = here.z // 2
            for y in range(2):
                mine = group == y
                away = remote(ins[0], held.at[y], send.at[2], recv.at[y], origin)
                stay = pltpu.make_async_copy(ins[0], held.at[y], recv.at[y])
                legs["away", y] = (mine & jnp.logical_not(origin_home), away)
                legs["stay", y] = (mine & origin_home, stay)
                own = pltpu.make_async_copy(held.at[y], outs[0], recv.at[2])
                legs["own", y] = (bend & (here.y == y), own)
                over = remote(held.at[y], outs[0], send.at[y], recv.at[2], to_y)
                legs["over", y] = (bend & (here.y != y), over)
        return legs

    def start(self, here, ins, outs, scratch):
        legs = self.plan(here, ins, outs, scratch)
        firsts = ("away", "stay") if self.back else ("own", "over")
        for key, (when, copy) in legs.items():
            if key in firsts or key[0] in firsts:
                pl.when(when)(copy.start)
        self.moved = False

    def middle(self, here, ins, outs, scratch):
        legs = self.plan(here, ins, outs, scratch)
        held, send, recv = scratch
        bend = self.bend(here)

        @pl.when(bend)
        def _():
            for slot in range(2):
                pltpu.make_async_copy(held.at[0], held.at[0], recv.at[slot]).wait()

        seconds = ("own", "over") if self.back else ("away", "stay")
        for key, (when, copy) in legs.items():
            if not isinstance(key, str) and key[0] in seconds:
                pl.when(when)(copy.start)
        self.moved = True

    def finish(self, here, ins, outs, scratch):
        if not self.moved:
            self.middle(here, ins, outs, scratch)
        legs = self.plan(here, ins, outs, scratch)
        pltpu.make_async_copy(outs[0], outs[0], scratch[2].at[2]).wait()
        for key, (when, copy) in legs.items():
            if key == "over" or key[0] in ("away", "over"):
                pl.when(when)(copy.wait_send)


class PlaneGather(Task):
    def __init__(self, block):
        rows, width = block.shape
        self.arrays, self.spaces = (block,), (pltpu.VMEM,)
        self.outs = (jax.ShapeDtypeStruct((8 * rows, width), block.dtype),)
        self.out_spaces = (pltpu.VMEM,)
        self.scratch = (dma_sems(11), dma_sems(11), pltpu.SemaphoreType.DMA)
        self.reach = (BY_X, BY_Y, BY_CORE)

    def place(self, here, o_ref, at_x, at_y, part=None):
        rows = o_ref.shape[0] // 8
        first = here.block(here.core, at_x, at_y) * rows
        if part is None:
            return o_ref.at[pl.ds(pl.multiple_of(first, rows), rows)]
        half = rows // 2
        return o_ref.at[pl.ds(pl.multiple_of(first + part * half, half), half)]

    def copies(self, here, x_ref, o_ref, send_sem, recv_sem):
        x, y = here.x, here.y
        half = x_ref.shape[0] // 2
        to_x, to_y, to_core = here.peer(*BY_X), here.peer(*BY_Y), here.peer(*BY_CORE)

        def copy(index, source, target, way):
            return remote(source, target, send_sem.at[index], recv_sem.at[index], way)

        def pass_on(index, way, *at):
            return copy(index, self.place(here, o_ref, *at), self.place(here, o_ref, *at), way)

        own = [self.place(here, o_ref, x, y, part) for part in (0, 1)]
        mine = [x_ref.at[pl.ds(part * half, half)] for part in (0, 1)]
        return [
            copy(0, mine[0], own[0], to_x),
            copy(1, mine[1], own[1], to_y),
            copy(2, mine[1], own[1], to_x),
            copy(3, mine[0], own[0], to_y),
            copy(4, x_ref, self.place(here, o_ref, x, y), to_core),
            pass_on(5, to_y, 1 - x, y, 0),
            pass_on(6, to_x, x, 1 - y, 1),
            pass_on(7, to_core, 1 - x, y),
            pass_on(8, to_core, x, 1 - y),
            pass_on(9, to_core, 1 - x, 1 - y, 0),
            pass_on(10, to_core, 1 - x, 1 - y, 1),
        ]

    def keep(self, here, x_ref, o_ref, own_sem):
        return pltpu.make_async_copy(x_ref, self.place(here, o_ref, here.x, here.y), own_sem)

    def start(self, here, ins, outs, scratch):
        copies = self.copies(here, ins[0], outs[0], scratch[0], scratch[1])
        for index in range(5):
            copies[index].start()
        self.keep(here, ins[0], outs[0], scratch[2]).start()

    def finish(self, here, ins, outs, scratch, work=None):
        rows = ins[0].shape[0]
        copies = self.copies(here, ins[0], outs[0], scratch[0], scratch[1])

        def done(flip_core, flip_x, flip_y):
            if work is not None:
                at_core = 1 - here.core if flip_core else here.core
                at_x = 1 - here.x if flip_x else here.x
                at_y = 1 - here.y if flip_y else here.y
                work(pl.multiple_of(here.block(at_core, at_x, at_y) * rows, rows))

        self.keep(here, ins[0], outs[0], scratch[2]).wait()
        done(0, 0, 0)
        copies[4].wait_recv()
        done(1, 0, 0)
        for index in range(4):
            copies[index].wait_recv()
            copies[5 + index].start()
        done(0, 1, 0)
        done(0, 0, 1)
        copies[7].wait_recv()
        done(1, 1, 0)
        copies[8].wait_recv()
        done(1, 0, 1)
        copies[5].wait_recv()
        copies[9].start()
        copies[6].wait_recv()
        copies[10].start()
        done(0, 1, 1)
        copies[9].wait_recv()
        copies[10].wait_recv()
        done(1, 1, 1)
        for each in copies:
            each.wait_send()


class PlaneScatter(Task):
    def __init__(self, rows, width, weight_dim):
        half = rows // 2
        self.weight_dim = weight_dim
        self.scratch = (
            pltpu.VMEM((4, rows, width), bf16),
            pltpu.VMEM((4, rows, width), bf16),
            pltpu.VMEM((rows, width), bf16),
            pltpu.VMEM((2, half, width), bf16),
            pltpu.VMEM((2, half, width), bf16),
            pltpu.VMEM((2, half, width), bf16),
            pltpu.VMEM((2, half, width), bf16),
            pltpu.VMEM((2, half, width), bf16),
            pltpu.VMEM((half, width), f32),
            pltpu.VMEM((half, width), f32),
            dma_sems(10),
            dma_sems(10),
        )
        self.reach = (BY_X, BY_Y, BY_CORE)

    def finish(self, here, ins, outs, scratch, rows_of, weight_of, early=None, idle=None):
        o_ref = outs[0]
        (
            sib_out,
            sib_in,
            diag_out,
            diag_in,
            last_x_out,
            last_y_out,
            last_x_in,
            last_y_in,
            wait_x,
            wait_y,
            send_sem,
            recv_sem,
        ) = scratch
        rows = o_ref.shape[0]
        half = rows // 2
        x, y, core = here.x, here.y, here.core
        to_x, to_y, to_core = here.peer(*BY_X), here.peer(*BY_Y), here.peer(*BY_CORE)

        def term(at_core, at_x, at_y):
            first = pl.multiple_of(here.block(at_core, at_x, at_y) * rows, rows)
            return lax.dot_general(
                rows_of(first),
                weight_of(),
                (((1,), (self.weight_dim,)), ((), ())),
                preferred_element_type=f32,
            )

        def copy(index, source, target, way):
            return remote(source, target, send_sem.at[index], recv_sem.at[index], way)

        places = ((1 - x, 1 - y), (1 - x, y), (x, 1 - y), (x, y))
        siblings = [copy(i, sib_out.at[i], sib_in.at[i], to_core) for i in range(4)]

        def help_sibling(i):
            sib_out[i] = term(1 - core, *places[i]).astype(bf16)
            siblings[i].start()

        def joined(i):
            mine = term(core, *places[i])
            siblings[i].wait_recv()
            return mine + sib_in[i].astype(f32)

        help_sibling(0)
        total = joined(0)
        diag_out[...] = total.astype(bf16)
        diag_x = copy(4, diag_out.at[pl.ds(0, half)], diag_in.at[0], to_x)
        diag_y = copy(5, diag_out.at[pl.ds(half, half)], diag_in.at[1], to_y)
        diag_x.start()
        diag_y.start()
        help_sibling(1)
        total = joined(1)
        last_x_out[0] = total[:half].astype(bf16)
        x_0 = copy(6, last_x_out.at[0], last_x_in.at[0], to_x)
        x_0.start()
        wait_x[...] = total[half:]
        if early is not None:
            early()
        help_sibling(2)
        total = joined(2)
        last_y_out[1] = total[half:].astype(bf16)
        y_1 = copy(7, last_y_out.at[1], last_y_in.at[1], to_y)
        y_1.start()
        wait_y[...] = total[:half]
        help_sibling(3)
        diag_y.wait_recv()
        last_x_out[1] = (wait_x[...] + diag_in[1].astype(f32)).astype(bf16)
        x_1 = copy(8, last_x_out.at[1], last_x_in.at[1], to_x)
        x_1.start()
        diag_x.wait_recv()
        last_y_out[0] = (wait_y[...] + diag_in[0].astype(f32)).astype(bf16)
        y_0 = copy(9, last_y_out.at[0], last_y_in.at[0], to_y)
        y_0.start()
        o_ref[...] = joined(3)
        if idle is not None:
            idle()
        for part, (by_x, by_y) in enumerate(((x_0, y_0), (x_1, y_1))):
            by_x.wait_recv()
            by_y.wait_recv()
            piece = pl.ds(part * half, half)
            o_ref[piece, :] += last_x_in[part].astype(f32) + last_y_in[part].astype(f32)
        for sent in (*siblings, diag_x, diag_y, x_0, y_1, x_1, y_0):
            sent.wait_send()


class PlaneSum(Task):
    def __init__(self, values):
        self.arrays, self.spaces = (values,), (pltpu.VMEM,)
        self.outs = (jax.ShapeDtypeStruct(values.shape, f32),)
        self.out_spaces = (pltpu.VMEM,)
        self.scratch = (pltpu.VMEM((7, *values.shape), f32), dma_sems(7), dma_sems(7))
        self.reach = BY_PLANE

    def copies(self, here, ins, scratch):
        got, send_sem, recv_sem = scratch
        return [
            remote(ins[0], got.at[i], send_sem.at[i], recv_sem.at[i], here.peer(*way))
            for i, way in enumerate(BY_PLANE)
        ]

    def start(self, here, ins, outs, scratch):
        for each in self.copies(here, ins, scratch):
            each.start()

    def finish(self, here, ins, outs, scratch):
        copies = self.copies(here, ins, scratch)
        for each in copies:
            each.wait_recv()
        got = scratch[0]
        by_x = [ins[0][...] + got[0]]
        for flip in (2, 4, 6):
            by_x.append(got[flip - 1] + got[flip])
        outs[0][...] = (by_x[0] + by_x[1]) + (by_x[2] + by_x[3])
        for each in copies:
            each.wait_send()


class LineGather(Task):
    def __init__(self, values):
        self.arrays, self.spaces = (values,), (pltpu.HBM,)
        self.outs = (jax.ShapeDtypeStruct((4, *values.shape), values.dtype),)
        self.out_spaces = (pltpu.HBM,)
        self.scratch = (dma_sems(4), dma_sems(3))
        self.reach = BY_Z

    def copies(self, here, ins, outs, scratch):
        target = outs[0].at[here.z]
        keep = pltpu.make_async_copy(ins[0], target, scratch[0].at[3])
        return keep, [
            remote(ins[0], target, scratch[0].at[i], scratch[1].at[i], here.peer(*way))
            for i, way in enumerate(BY_Z)
        ]

    def start(self, here, ins, outs, scratch):
        keep, copies = self.copies(here, ins, outs, scratch)
        for each in copies:
            each.start()
        keep.start()

    def finish(self, here, ins, outs, scratch):
        keep, copies = self.copies(here, ins, outs, scratch)
        for each in copies:
            each.wait()
        keep.wait()


class HeadGather(Task):
    def __init__(self, qkv, out, layer, midway=False):
        _, kinds, both, width = qkv.shape
        self.layer, self.midway = layer, midway
        self.arrays, self.spaces = (qkv, out), (pltpu.HBM,) * 2
        self.outs = (jax.ShapeDtypeStruct((kinds + 1, 2, both // 2, width), qkv.dtype),)
        self.out_spaces = (pltpu.HBM,)
        self.scratch = (dma_sems(8), dma_sems(8))
        self.reach = BY_LINE

    def pieces(self, outs, shard, part):
        half = outs[0].shape[3] // 2
        columns = pl.ds(pl.multiple_of(part * half, half), half)
        return outs[0].at[pl.ds(0, 3), shard, :, columns], outs[0].at[3, shard, :, columns]

    def copies(self, here, ins, outs, scratch):
        shard, target_core = lax.rem(here.z, 2), here.z // 2
        wide, half = outs[0].shape[2], outs[0].shape[3] // 2
        rows = pl.ds(pl.multiple_of(here.y * wide, wide), wide)
        columns = pl.ds(pl.multiple_of(here.core * half, half), half)
        sources = (ins[0].at[self.layer, :, rows, columns], ins[1].at[self.layer, rows, columns])
        targets = self.pieces(outs, shard, here.core)
        keeps, aways = [], []
        for kind in range(2):
            recv_sem = scratch[1].at[4 * kind + 2 * shard + here.core]
            keeps.append(pltpu.make_async_copy(sources[kind], targets[kind], recv_sem))
            for step in range(4):
                place = {"core": target_core, "z": lax.rem(here.z + step, 4)}
                send_sem = scratch[0].at[4 * kind + step]
                aways.append(remote(sources[kind], targets[kind], send_sem, recv_sem, place))
        return keeps, aways

    def begin(self, here, ins, outs, scratch):
        keeps, aways = self.copies(here, ins, outs, scratch)
        for index, each in enumerate(aways):
            if index % 4:
                each.start()
        at_home = here.z // 2 == here.core
        for kind in range(2):
            pl.when(at_home)(keeps[kind].start)
            pl.when(jnp.logical_not(at_home))(aways[4 * kind].start)

    def start(self, *held):
        if not self.midway:
            self.begin(*held)

    def middle(self, *held):
        if self.midway:
            self.begin(*held)

    def finish(self, here, ins, outs, scratch):
        keeps, aways = self.copies(here, ins, outs, scratch)
        for shard in range(2):
            for part in range(2):
                for kind, piece in enumerate(self.pieces(outs, shard, part)):
                    recv_sem = scratch[1].at[4 * kind + 2 * shard + part]
                    pltpu.make_async_copy(piece, piece, recv_sem).wait()
        for index, each in enumerate(aways):
            if index % 4:
                each.wait_send()
        for kind in range(2):
            pl.when(here.z // 2 != here.core)(aways[4 * kind].wait_send)


class LineScatter(Task):
    def __init__(self, values):
        shape = values.shape[1:]
        self.arrays, self.spaces = (values,), (pltpu.VMEM,)
        self.outs, self.out_spaces = (jax.ShapeDtypeStruct(shape, values.dtype),), (pltpu.VMEM,)
        self.scratch = (pltpu.VMEM((3, *shape), values.dtype), dma_sems(3), dma_sems(3))
        self.reach = BY_Z

    def copies(self, here, ins, scratch):
        got, send_sem, recv_sem = scratch
        return [
            remote(
                ins[0].at[lax.rem(here.z + i + 1, 4)],
                got.at[i],
                send_sem.at[i],
                recv_sem.at[i],
                here.peer(*way),
            )
            for i, way in enumerate(BY_Z)
        ]

    def start(self, here, ins, outs, scratch):
        for each in self.copies(here, ins, scratch):
            each.start()

    def finish(self, here, ins, outs, scratch):
        copies = self.copies(here, ins, scratch)
        for each in copies:
            each.wait_recv()
        total = ins[0][here.z].astype(f32)
        for i in range(3):
            total = total + scratch[0][i].astype(f32)
        outs[0][...] = total.astype(outs[0].dtype)
        for each in copies:
            each.wait_send()


class HeadScatter(Task):
    def __init__(self, values):
        kinds, _, wide, width = values.shape
        shape = (kinds, wide, width // 2)
        self.arrays, self.spaces = (values,), (pltpu.VMEM,)
        self.outs, self.out_spaces = (jax.ShapeDtypeStruct(shape, values.dtype),), (pltpu.VMEM,)
        self.scratch = (pltpu.VMEM((4, *shape), values.dtype), dma_sems(4), dma_sems(4))
        self.reach = BY_LINE

    def copies(self, here, ins, scratch):
        got, send_sem, recv_sem = scratch
        half = ins[0].shape[3] // 2
        triples = []
        for shard in range(2):
            for part in range(2):
                source = ins[0].at[:, shard, :, pl.ds(part * half, half)]
                target_z = 2 * here.core + shard
                slot = recv_sem.at[here.z]
                away = remote(
                    source,
                    got.at[here.z],
                    send_sem.at[2 * shard + part],
                    slot,
                    {"core": part, "z": target_z},
                )
                stay = pltpu.make_async_copy(source, got.at[here.z], slot)
                at_home = (target_z == here.z) & (here.core == part)
                triples.append((away, stay, at_home))
        return triples

    def start(self, here, ins, outs, scratch):
        for away, stay, at_home in self.copies(here, ins, scratch):
            pl.when(at_home)(stay.start)
            pl.when(jnp.logical_not(at_home))(away.start)

    def finish(self, here, ins, outs, scratch):
        got, send_sem, recv_sem = scratch
        for plane in range(4):
            pltpu.make_async_copy(got.at[plane], got.at[plane], recv_sem.at[plane]).wait()
        total = got[0].astype(f32)
        for plane in range(1, 4):
            total = total + got[plane].astype(f32)
        outs[0][...] = total.astype(outs[0].dtype)
        for away, stay, at_home in self.copies(here, ins, scratch):
            pl.when(jnp.logical_not(at_home))(away.wait_send)


class RowsGather(Task):
    def __init__(self, values):
        self.arrays, self.spaces = (values,), (pltpu.HBM,)
        self.outs = (jax.ShapeDtypeStruct((4, *values.shape), values.dtype),)
        self.out_spaces = (pltpu.HBM,)
        self.scratch = (dma_sems(4), dma_sems(3))
        self.reach = (BY_Y, BY_CORE)

    def copies(self, here, ins, outs, scratch):
        send_sem, recv_sem = scratch
        own = outs[0].at[2 * here.y + here.core]
        over = outs[0].at[2 * (1 - here.y) + here.core]
        to_y, to_core = here.peer(*BY_Y), here.peer(*BY_CORE)
        return (
            pltpu.make_async_copy(ins[0], own, send_sem.at[3]),
            remote(ins[0], own, send_sem.at[0], recv_sem.at[0], to_y),
            remote(ins[0], own, send_sem.at[1], recv_sem.at[1], to_core),
            remote(over, over, send_sem.at[2], recv_sem.at[2], to_core),
        )

    def start(self, here, ins, outs, scratch):
        keep, by_y, by_core, again = self.copies(here, ins, outs, scratch)
        by_y.start()
        by_core.start()
        keep.start()

    def finish(self, here, ins, outs, scratch):
        keep, by_y, by_core, again = self.copies(here, ins, outs, scratch)
        by_y.wait_recv()
        again.start()
        by_core.wait_recv()
        again.wait_recv()
        for each in (by_y, by_core, again):
            each.wait_send()
        keep.wait()


class PlaneThenLineSum(Task):
    def __init__(self, values, ready):
        rows, width = values.shape
        both = (rows + ready.shape[0], width)
        self.plane = PlaneSum(values)
        self.arrays, self.spaces = (values, ready), (pltpu.VMEM,) * 2
        self.outs, self.out_spaces = (jax.ShapeDtypeStruct(both, f32),), (pltpu.VMEM,)
        self.scratch = (
            *self.plane.scratch,
            pltpu.VMEM((4, *both), f32),
            pltpu.VMEM(both, f32),
            dma_sems(3),
            dma_sems(4),
        )
        self.reach = BY_PLANE + BY_Z

    def start(self, here, ins, outs, scratch):
        self.plane.start(here, ins[:1], None, scratch[:3])

    def finish(self, here, ins, outs, scratch):
        got, mine, send_sem, recv_sem = scratch[3:]
        rows = ins[0].shape[0]
        first = ins[1].shape[0]
        self.plane.finish(here, ins[:1], (mine.at[pl.ds(first, rows)],), scratch[:3])
        mine[:first, :] = ins[1][...]
        copies = [
            remote(mine, got.at[here.z], send_sem.at[i], recv_sem.at[here.z], here.peer(*way))
            for i, way in enumerate(BY_Z)
        ]
        for each in copies:
            each.start()
        keep = pltpu.make_async_copy(mine, got.at[here.z], recv_sem.at[here.z])
        keep.start()
        for plane in range(4):
            pltpu.make_async_copy(got.at[plane], got.at[plane], recv_sem.at[plane]).wait()
        outs[0][...] = (got[0] + got[1]) + (got[2] + got[3])
        for each in copies:
            each.wait_send()


def to_columns(upper, lower):
    place = lax.broadcasted_iota(jnp.int32, (128, upper.shape[1]), 0)
    return jnp.transpose(jnp.where(place < 64, upper, lower))


def both_columns(upper, lower):
    lane = lax.broadcasted_iota(jnp.int32, (upper.shape[0], 128), 1)
    return jnp.where(lane < 64, upper, lower)


def in_chunks(rows, chunk, step):
    def one(index, carry):
        step(pl.multiple_of(index * chunk, chunk))
        return carry

    lax.fori_loop(0, rows // chunk, one, 0)


def fold(values):
    total = values[:8]
    for first in range(8, values.shape[0], 8):
        total = total + values[first : first + 8]
    return total


class Parts(Task):
    def use(self, **parts):
        self.parts = parts
        self.scratch = list(self.scratch)
        self.at = {}
        reach = []
        for name, part in parts.items():
            self.at[name] = (len(self.scratch), len(self.scratch) + len(part.scratch))
            self.scratch += list(part.scratch)
            reach += [way for way in part.reach if way not in reach]
        self.reach = reach

    def held(self, scratch, name):
        first, last = self.at[name]
        return scratch[first:last]


CHUNK = 32


class FfnForward(Parts):
    def __init__(self, block, first, second, shift, gain, bias, layer, late):
        rows, width = block.shape
        hidden = first.shape[1]
        self.late = late
        self.arrays = (block, first, second, shift, gain, bias)
        self.spaces = (pltpu.VMEM,) * 2 + (pltpu.HBM if late else pltpu.VMEM,) + (pltpu.VMEM,) * 3
        self.outs = (
            jax.ShapeDtypeStruct((rows, width), f32),
            jax.ShapeDtypeStruct((8 * rows, width), bf16),
            jax.ShapeDtypeStruct((8 * rows, hidden), f32),
            jax.ShapeDtypeStruct((8 * rows, hidden), f32),
            jax.ShapeDtypeStruct((8 * rows, hidden), bf16),
            jax.ShapeDtypeStruct((2, 8 * rows), f32),
        )
        self.out_spaces = (pltpu.VMEM,) + (pltpu.HBM,) * 4 + (pltpu.VMEM,)
        self.scratch = (
            pltpu.VMEM((8 * rows, width), bf16),
            pltpu.VMEM((8 * rows, hidden), f32),
            pltpu.VMEM((8 * rows, hidden), f32),
            pltpu.VMEM((8 * rows, hidden), bf16),
            pltpu.VMEM((2, 8 * rows), f32),
            pltpu.VMEM((rows, 128), f32),
            dma_sems(4),
        )
        parts = dict(
            gather=PlaneGather(block),
            scatter=PlaneScatter(rows, width, 0),
            sums=PlaneSum(jax.ShapeDtypeStruct((2, 8 * rows), f32)),
        )
        if late:
            parts["second"] = WeightGather(second, layer, 0)
            self.outs += parts["second"].outs
            self.out_spaces += (pltpu.VMEM,)
        self.use(**parts)

    def start(self, here, ins, outs, scratch):
        self.parts["gather"].start(here, ins[:1], scratch[:1], self.held(scratch, "gather"))
        if self.late:
            held = self.held(scratch, "second")
            self.parts["second"].start(here, ins[2:3], outs[6:7], held)

    def finish(self, here, ins, outs, scratch):
        block_ref, first_ref, second_ref, shift_ref, gain_ref, bias_ref = ins
        out_ref, rows_out, slope_out, normal_out, mixed_out, total_ref = outs[:6]
        if self.late:
            second_ref = outs[6]
        rows_buf, before, active, mixed, sums, columns, save = scratch[:7]
        rows = block_ref.shape[0]
        hidden_all = 8 * first_ref.shape[1]

        def work(first):
            before[pl.ds(first, rows), :] = lax.dot_general(
                rows_buf[pl.ds(first, rows), :],
                first_ref[...],
                (((1,), (0,)), ((), ())),
                preferred_element_type=f32,
            )

            def step(at):
                piece = pl.ds(pl.multiple_of(first + at, CHUNK), CHUNK)
                u = before[piece, :] + shift_ref[...]
                area = 0.5 * (1.0 + lax.erf(u * 0.5**0.5))
                a = u * area
                active[piece, :] = a
                before[piece, :] = area + u * (jnp.exp(-0.5 * u * u) * (0.5 / jnp.pi) ** 0.5)
                columns[pl.ds(at, CHUNK), :] = both_columns(
                    jnp.sum(a, axis=1, keepdims=True), jnp.sum(a * a, axis=1, keepdims=True)
                )

            in_chunks(rows, CHUNK, step)
            turned = jnp.transpose(columns[...])
            sums[0:1, pl.ds(first, rows)] = turned[0:1]
            sums[1:2, pl.ds(first, rows)] = turned[64:65]

        self.parts["gather"].finish(
            here, ins[:1], scratch[:1], self.held(scratch, "gather"), work
        )
        held = self.held(scratch, "sums")
        self.parts["sums"].start(here, (sums,), None, held)
        keep_rows = pltpu.make_async_copy(rows_buf, rows_out, save.at[0])
        keep_rows.start()
        keep_slope = pltpu.make_async_copy(before, slope_out, save.at[1])
        keep_slope.start()
        self.parts["sums"].finish(here, (sums,), (total_ref,), held)
        if self.late:
            held = self.held(scratch, "second")
            self.parts["second"].finish(here, ins[2:3], outs[6:7], held)
        self.between()

        def rows_of(first):
            average = total_ref[0:1, pl.ds(first, rows)] / hidden_all
            spread = total_ref[1:2, pl.ds(first, rows)] / hidden_all - average * average
            columns[...] = to_columns(average, lax.rsqrt(spread + epsilon))

            def step(at):
                piece = pl.ds(pl.multiple_of(first + at, CHUNK), CHUNK)
                pair = columns[pl.ds(at, CHUNK), :]
                normal = (active[piece, :] - pair[:, 0:1]) * pair[:, 64:65]
                active[piece, :] = normal
                mixed[piece, :] = (normal * gain_ref[...] + bias_ref[...]).astype(bf16)

            in_chunks(rows, CHUNK, step)
            return mixed[pl.ds(first, rows), :]

        keep_mixed = pltpu.make_async_copy(mixed, mixed_out, save.at[2])
        keep_normal = pltpu.make_async_copy(active, normal_out, save.at[3])

        def idle():
            keep_mixed.start()
            keep_normal.start()

        self.parts["scatter"].finish(
            here,
            None,
            (out_ref,),
            self.held(scratch, "scatter"),
            rows_of,
            lambda: second_ref[...],
            idle=idle,
        )
        for each in (keep_rows, keep_slope, keep_mixed, keep_normal):
            each.wait()


class FfnBackward(Parts):
    def __init__(self, block, first, second, gain, slope, normal, mixed, ffn_rows, totals):
        rows, width = block.shape
        hidden = second.shape[0]
        self.arrays = (block, first, second, gain, totals, slope, normal, mixed, ffn_rows)
        self.spaces = (pltpu.VMEM,) * 5 + (pltpu.HBM,) * 4
        self.outs = (
            jax.ShapeDtypeStruct((rows, width), f32),
            jax.ShapeDtypeStruct((4, width, hidden // 4), bf16),
            jax.ShapeDtypeStruct((hidden // 4, width), bf16),
            jax.ShapeDtypeStruct((3, hidden), f32),
        )
        self.out_spaces = (pltpu.VMEM,) * 4
        self.scratch = (
            pltpu.VMEM((8 * rows, width), bf16),
            pltpu.VMEM((8 * rows, hidden), f32),
            pltpu.VMEM((8 * rows, hidden), f32),
            pltpu.VMEM((8 * rows, hidden), f32),
            pltpu.VMEM((8 * rows, hidden), bf16),
            pltpu.VMEM((8 * rows, width), bf16),
            pltpu.VMEM((8 * rows, hidden), bf16),
            pltpu.VMEM((hidden, width), f32),
            pltpu.VMEM((2, 8 * rows), f32),
            pltpu.VMEM((2, 8 * rows), f32),
            pltpu.VMEM((rows, 128), f32),
            pltpu.VMEM((rows, 128), f32),
            pltpu.VMEM((3, 8, hidden), f32),
            dma_sems(4),
            pltpu.VMEM((4, hidden // 4, width), bf16),
        )
        self.use(
            gather=PlaneGather(block),
            scatter=PlaneScatter(rows, width, 1),
            second=LineScatter(jax.ShapeDtypeStruct((4, hidden // 4, width), bf16)),
            sums=PlaneSum(jax.ShapeDtypeStruct((2, 8 * rows), f32)),
        )

    def loads(self, ins, scratch):
        targets = (scratch[2], scratch[4], scratch[1], scratch[5])
        return [
            pltpu.make_async_copy(source, target, scratch[13].at[i])
            for i, (source, target) in enumerate(zip((ins[6], ins[7], ins[5], ins[8]), targets))
        ]

    def start(self, here, ins, outs, scratch):
        self.parts["gather"].start(here, ins[:1], scratch[:1], self.held(scratch, "gather"))
        for each in self.loads(ins, scratch):
            each.start()

    def finish(self, here, ins, outs, scratch):
        block_ref, first_ref, second_ref, gain_ref, totals_ref = ins[:5]
        out_ref, first_grad, second_quarter, small_ref = outs
        second_grad = scratch[14]
        (
            rows_buf,
            slope,
            normal_buf,
            grads,
            mixed,
            ffn_rows,
            pre_grad,
            second_sum,
            sums,
            got,
            columns,
            factors,
            small,
        ) = scratch[:13]
        rows = block_ref.shape[0]
        hidden_all = 8 * first_ref.shape[1]
        load_normal, load_mixed, load_slope, load_rows = self.loads(ins, scratch)
        load_normal.wait()
        load_mixed.wait()
        second_sum[...] = jnp.zeros_like(second_sum)
        small[...] = jnp.zeros_like(small)

        def factor_columns(first):
            average = totals_ref[0:1, pl.ds(first, rows)] / hidden_all
            spread = totals_ref[1:2, pl.ds(first, rows)] / hidden_all - average * average
            factors[...] = to_columns(average, lax.rsqrt(spread + epsilon))

        def work(first):
            block = pl.ds(first, rows)
            grads[block, :] = lax.dot_general(
                rows_buf[block, :],
                second_ref[...],
                (((1,), (1,)), ((), ())),
                preferred_element_type=f32,
            )
            second_sum[...] += lax.dot_general(
                mixed[block, :],
                rows_buf[block, :],
                (((0,), (0,)), ((), ())),
                preferred_element_type=f32,
            )

            def step(at):
                piece = pl.ds(pl.multiple_of(first + at, CHUNK), CHUNK)
                normal = normal_buf[piece, :]
                grad = grads[piece, :]
                small[0] += fold(grad * normal)
                small[1] += fold(grad)
                scaled = grad * gain_ref[...]
                grads[piece, :] = scaled
                columns[pl.ds(at, CHUNK), :] = both_columns(
                    jnp.sum(scaled, axis=1, keepdims=True),
                    jnp.sum(scaled * normal, axis=1, keepdims=True),
                )

            in_chunks(rows, CHUNK, step)
            turned = jnp.transpose(columns[...])
            sums[0:1, pl.ds(first, rows)] = turned[0:1]
            sums[1:2, pl.ds(first, rows)] = turned[64:65]

        self.parts["gather"].finish(
            here, ins[:1], scratch[:1], self.held(scratch, "gather"), work
        )
        held = self.held(scratch, "sums")
        self.parts["sums"].start(here, (sums,), None, held)
        second_grad[...] = second_sum[...].astype(bf16).reshape(second_grad.shape)
        self.parts["second"].start(here, (second_grad,), None, self.held(scratch, "second"))
        self.parts["sums"].finish(here, (sums,), (got,), held)
        load_slope.wait()
        self.between()

        def rows_of(first):
            factor_columns(first)
            columns[...] = to_columns(
                got[0:1, pl.ds(first, rows)] / hidden_all,
                got[1:2, pl.ds(first, rows)] / hidden_all,
            )

            def step(at):
                piece = pl.ds(pl.multiple_of(first + at, CHUNK), CHUNK)
                pair = columns[pl.ds(at, CHUNK), :]
                factor = factors[pl.ds(at, CHUNK), :][:, 64:65]
                active_grad = factor * (
                    grads[piece, :] - pair[:, 0:1] - normal_buf[piece, :] * pair[:, 64:65]
                )
                rounded = (active_grad * slope[piece, :]).astype(bf16)
                pre_grad[piece, :] = rounded
                small[2] += fold(rounded.astype(f32))

            in_chunks(rows, CHUNK, step)
            return pre_grad[pl.ds(first, rows), :]

        def idle():
            load_rows.wait()
            whole = lax.dot_general(
                ffn_rows[...],
                pre_grad[...],
                (((0,), (0,)), ((), ())),
                preferred_element_type=f32,
            ).astype(bf16)
            part = first_grad.shape[2]
            for i in range(4):
                first_grad[i] = whole[:, i * part : (i + 1) * part]

        self.parts["scatter"].finish(
            here,
            None,
            (out_ref,),
            self.held(scratch, "scatter"),
            rows_of,
            lambda: first_ref[...],
            idle=idle,
        )
        held = self.held(scratch, "second")
        self.parts["second"].finish(here, (second_grad,), (second_quarter,), held)
        for i in range(3):
            small_ref[i : i + 1, :] = jnp.sum(small[i], axis=0, keepdims=True)


class WeightGather(Task):
    def __init__(self, weights, layer, axis, midway=False):
        self.layer, self.axis, self.midway = layer, axis, midway
        self.arrays, self.spaces = (weights,), (pltpu.HBM,)
        self.outs = (jax.ShapeDtypeStruct(weights.shape[1:], weights.dtype),)
        self.out_spaces = (pltpu.HBM,)
        self.scratch = (dma_sems(4), dma_sems(3))
        self.reach = BY_Z

    def copies(self, here, ins, outs, scratch):
        part = outs[0].shape[self.axis] // 4

        def cut(ref, at):
            piece = pl.ds(pl.multiple_of(at * part, part), part)
            return ref.at[piece, :] if self.axis == 0 else ref.at[:, piece]

        source = cut(ins[0].at[self.layer], 2 * here.y + here.core)
        target = cut(outs[0], here.z)
        keep = pltpu.make_async_copy(source, target, scratch[0].at[3])
        return keep, [
            remote(source, target, scratch[0].at[i], scratch[1].at[i], here.peer(*way))
            for i, way in enumerate(BY_Z)
        ]

    def begin(self, here, ins, outs, scratch):
        keep, copies = self.copies(here, ins, outs, scratch)
        for each in copies:
            each.start()
        keep.start()

    def start(self, *held):
        if not self.midway:
            self.begin(*held)

    def middle(self, *held):
        if self.midway:
            self.begin(*held)

    def finish(self, here, ins, outs, scratch):
        keep, copies = self.copies(here, ins, outs, scratch)
        for each in copies:
            each.wait()
        keep.wait()


class LineThenRows(Parts):
    moved = False

    def __init__(self, values):
        shape = jax.ShapeDtypeStruct(values.shape[1:], values.dtype)
        self.arrays, self.spaces = (values,), (pltpu.VMEM,)
        self.outs = (jax.ShapeDtypeStruct((4, *shape.shape), values.dtype),)
        self.out_spaces = (pltpu.HBM,)
        self.scratch = (pltpu.VMEM(shape.shape, values.dtype),)
        self.use(line=LineScatter(values), rows=RowsGather(shape))

    def start(self, here, ins, outs, scratch):
        self.parts["line"].start(here, ins, None, self.held(scratch, "line"))

    def middle(self, here, ins, outs, scratch):
        self.parts["line"].finish(here, ins, scratch[:1], self.held(scratch, "line"))
        self.parts["rows"].start(here, scratch[:1], outs, self.held(scratch, "rows"))
        self.moved = True

    def finish(self, here, ins, outs, scratch):
        if not self.moved:
            self.middle(here, ins, outs, scratch)
        self.parts["rows"].finish(here, scratch[:1], outs, self.held(scratch, "rows"))


BLOCK = 256
SPAN = 512


def head_masks(head_width, width):
    lane = lax.broadcasted_iota(jnp.int32, (1, width), 1)
    lower = (lane < head_width).astype(bf16)
    return lower, (1 - lower).astype(bf16)


def by_head(values, head_width):
    lower, upper = head_masks(head_width, values.shape[1])
    return jnp.concatenate([values * lower, values * upper], axis=0)


def from_heads(pair, head_width):
    rows = pair.shape[0] // 2
    lane = lax.broadcasted_iota(jnp.int32, (rows, pair.shape[1]), 1)
    return jnp.where(lane < head_width, pair[:rows], pair[rows:])


def tile_facts(doc_ref, first, key_first, keys):
    docs = doc_ref[:, pl.ds(first, BLOCK)]
    docs = jnp.concatenate([docs, docs], axis=1)
    key_docs = doc_ref[:, pl.ds(pl.multiple_of(key_first, keys), keys)]
    key_docs = jnp.transpose(jnp.broadcast_to(key_docs, (128, keys)))[:, 0:1]
    place = lax.broadcasted_iota(jnp.int32, (keys, 2 * BLOCK), 1)
    place = jnp.where(place >= BLOCK, place - BLOCK, place) + (first - key_first)
    allowed = (docs == key_docs) & (place >= lax.broadcasted_iota(jnp.int32, place.shape, 0))
    return docs, allowed


def attend_block(
    head_width, first, q_ref, k_ref, v_cols, doc_ref, o_ref, l_ref, s_buf, acc, top, total
):
    block = first // BLOCK
    last = first // SPAN
    pair = by_head(q_ref[pl.ds(first, BLOCK), :], head_width)

    def scores(at):
        keys = k_ref[pl.ds(pl.multiple_of(at * SPAN, SPAN), SPAN), :]
        return lax.dot_general(keys, pair, (((1,), (1,)), ((), ())), preferred_element_type=f32)

    top[...] = jnp.full_like(top, masked)

    def first_pass(at, carry):
        s = scores(at)
        s_buf[at] = s
        peak = s[:8]
        for row in range(8, SPAN, 8):
            peak = jnp.maximum(peak, s[row : row + 8])
        top[...] = jnp.maximum(top[...], peak)
        return carry

    lax.fori_loop(0, last, first_pass, 0)
    docs, allowed = tile_facts(doc_ref, first, last * SPAN, SPAN)
    s = jnp.where(allowed, scores(last), masked)
    shift = jnp.where(docs == 0, 0.0, masked)
    peak = jnp.maximum(
        jnp.max(top[...], axis=0, keepdims=True) + shift, jnp.max(s, axis=0, keepdims=True)
    )

    def weigh(at, p):
        values = v_cols[:, pl.ds(pl.multiple_of(at * SPAN, SPAN), SPAN)]
        return jnp.dot(values, p.astype(bf16), preferred_element_type=f32)

    p = jnp.exp(s - peak)
    total[...] = fold(p)
    acc[...] = weigh(last, p)
    base = peak - shift

    def second_pass(at, carry):
        p = jnp.exp(s_buf[at] - base)
        total[...] += fold(p)
        acc[...] += weigh(at, p)
        return carry

    lax.fori_loop(0, last, second_pass, 0)
    sums = jnp.sum(total[...], axis=0, keepdims=True)
    out = from_heads(jnp.transpose(acc[...] / sums), head_width)
    o_ref[pl.ds(first, BLOCK), :] = out
    l_ref[block] = peak + jnp.log(sums)
    return out


def attend_block_back(
    head_width,
    first,
    do,
    q_ref,
    k_ref,
    k_cols,
    v_ref,
    o_ref,
    l_ref,
    doc_ref,
    acc_k,
    acc_v,
    acc_q,
):
    block = first // BLOCK
    rows = pl.ds(first, BLOCK)
    pair_q = by_head(q_ref[rows, :], head_width)
    pair_do = by_head(do, head_width)
    out = o_ref[rows, :]
    inner = jnp.sum(
        jnp.concatenate([out, out], axis=0) * pair_do.astype(f32), axis=1, keepdims=True
    )
    inner = jnp.transpose(jnp.broadcast_to(inner, (2 * BLOCK, 128)))[0:1, :]
    logs = l_ref[block]
    docs, allowed = tile_facts(doc_ref, first, first, BLOCK)

    def step(at, base, allowed):
        piece = pl.ds(pl.multiple_of(at * BLOCK, BLOCK), BLOCK)
        s = lax.dot_general(
            k_ref[piece, :], pair_q, (((1,), (1,)), ((), ())), preferred_element_type=f32
        )
        dp = lax.dot_general(
            v_ref[piece, :], pair_do, (((1,), (1,)), ((), ())), preferred_element_type=f32
        )
        p = jnp.exp(s - base)
        if allowed is not None:
            p = jnp.where(allowed, p, 0.0)
        ds = (p * (dp - inner)).astype(bf16)
        acc_v[piece, :] += jnp.dot(p.astype(bf16), pair_do, preferred_element_type=f32)
        acc_k[piece, :] += jnp.dot(ds, pair_q, preferred_element_type=f32)
        return jnp.dot(k_cols[:, piece], ds, preferred_element_type=f32)

    acc_q[...] = step(block, logs, allowed)
    base = jnp.where(docs == 0, logs, -masked)

    def earlier(at, carry):
        acc_q[...] += step(at, base, None)
        return carry

    lax.fori_loop(0, block, earlier, 0)
    grad = from_heads(jnp.transpose(acc_q[...]), head_width)
    return (grad * head_width**-0.5).astype(bf16)


def turned(values):
    return jnp.transpose(values.astype(f32)).astype(bf16)


class AttnForward(Parts):
    def __init__(self, block, docs, scale, heads, biases, wide, layer, late):
        rows, width = block.shape
        self.head_width, self.layer, self.late = wide, layer, late
        here = 2 * wide
        self.arrays = (block, docs, scale, biases, *heads)
        self.spaces = (pltpu.VMEM,) * 3 + (pltpu.HBM if late else pltpu.VMEM,) * (1 + len(heads))
        column = jax.ShapeDtypeStruct((8 * rows, here), bf16)
        self.outs = (
            jax.ShapeDtypeStruct((rows, width), f32),
            jax.ShapeDtypeStruct((8 * rows, width), bf16),
            column,
            column,
            column,
            column,
            jax.ShapeDtypeStruct((8 * rows, here), f32),
            jax.ShapeDtypeStruct((8 * rows // BLOCK, 1, 2 * BLOCK), f32),
        )
        self.out_spaces = (pltpu.VMEM, pltpu.HBM) + (pltpu.VMEM,) * 6
        self.scratch = (
            pltpu.VMEM((8 * rows, width), bf16),
            pltpu.VMEM((here, 8 * rows), bf16),
            pltpu.VMEM((8 * rows // SPAN, SPAN, 2 * BLOCK), f32),
            pltpu.VMEM((here, 2 * BLOCK), f32),
            pltpu.VMEM((8, 2 * BLOCK), f32),
            pltpu.VMEM((8, 2 * BLOCK), f32),
            dma_sems(1),
        )
        parts = dict(gather=PlaneGather(block), scatter=PlaneScatter(rows, width, 0))
        if late:
            parts.update(heads=HeadGather(*heads, layer), biases=LineGather(biases))
            self.outs += parts["heads"].outs + parts["biases"].outs
            self.out_spaces += (pltpu.VMEM,) * 2
        self.use(**parts)

    def start(self, here, ins, outs, scratch):
        self.parts["gather"].start(here, ins[:1], scratch[:1], self.held(scratch, "gather"))
        if self.late:
            self.parts["heads"].start(here, ins[4:6], outs[8:9], self.held(scratch, "heads"))
            self.parts["biases"].start(here, ins[3:4], outs[9:10], self.held(scratch, "biases"))

    def finish(self, here, ins, outs, scratch):
        block_ref, doc_ref, scale_ref = ins[:3]
        heads_ref, bias_ref = outs[8:10] if self.late else (ins[4], ins[3])
        out_ref, rows_out, q_ref, k_ref, v_ref, z_ref, o_ref, l_ref = outs[:8]
        rows_buf, v_cols, s_buf, acc, top, total, save = scratch[:7]
        rows, model_width = block_ref.shape
        wide = self.head_width
        width = 2 * wide

        def bias_row(at):
            pair = [
                bias_ref[2 * here.core + i, self.layer : self.layer + 1, at : at + width]
                for i in range(2)
            ]
            lane = lax.broadcasted_iota(jnp.int32, (1, width), 1)
            return jnp.where(lane < wide, pair[0], pair[1])

        def work(first):
            block = pl.ds(first, rows)
            projected = lax.dot_general(
                rows_buf[block, :],
                heads_ref[0:3].reshape(3 * width, model_width),
                (((1,), (1,)), ((), ())),
                preferred_element_type=f32,
            )
            q = (projected[:, :width] + bias_row(0)).astype(bf16).astype(f32)
            q_ref[block, :] = (q * wide**-0.5).astype(bf16)
            k_ref[block, :] = projected[:, width : 2 * width].astype(bf16)
            v = (projected[:, 2 * width :] + bias_row(width)).astype(bf16)
            v_ref[block, :] = v
            v_cols[:, block] = turned(v)

        self.parts["gather"].finish(
            here,
            ins[:1],
            scratch[:1],
            self.held(scratch, "gather"),
            None if self.late else work,
        )
        keep_rows = pltpu.make_async_copy(rows_buf, rows_out, save.at[0])
        keep_rows.start()
        if self.late:
            self.parts["heads"].finish(here, ins[4:6], outs[8:9], self.held(scratch, "heads"))
            self.parts["biases"].finish(here, ins[3:4], outs[9:10], self.held(scratch, "biases"))
            in_chunks(8 * rows, rows, work)
        self.between()

        def rows_of(first):
            out = attend_block(
                wide, first, q_ref, k_ref, v_cols, doc_ref, o_ref, l_ref, s_buf, acc, top, total
            )
            z = (out * scale_ref[...]).astype(bf16)
            z_ref[pl.ds(first, rows), :] = z
            return z

        self.parts["scatter"].finish(
            here,
            None,
            (out_ref,),
            self.held(scratch, "scatter"),
            rows_of,
            lambda: heads_ref[3].reshape(width, model_width),
        )
        keep_rows.wait()


class AttnBackward(Parts):
    def __init__(self, block, docs, scale, heads, q, k, v, z, o, logs, attn_rows, ship):
        rows, width = block.shape
        kinds, _, wide, _ = heads.shape
        self.head_width = wide
        here = 2 * wide
        self.arrays = (block, docs, scale, heads, q, k, v, z, o, logs, attn_rows)
        self.spaces = (pltpu.VMEM,) * 10 + (pltpu.HBM,)
        self.outs = (
            jax.ShapeDtypeStruct((rows, width), f32),
            jax.ShapeDtypeStruct((kinds, wide, width // 2) if ship else heads.shape, bf16),
            jax.ShapeDtypeStruct((3, here), f32),
        )
        self.ship = ship
        self.out_spaces = (pltpu.VMEM,) * 3
        self.scratch = (
            pltpu.VMEM((8 * rows, width), bf16),
            pltpu.VMEM((8 * rows, width), bf16),
            pltpu.VMEM((here, 8 * rows), bf16),
            pltpu.VMEM((8 * rows, here), f32),
            pltpu.VMEM((8 * rows, here), f32),
            pltpu.VMEM((here, 2 * BLOCK), f32),
            pltpu.VMEM((8 * rows, 3 * here), bf16),
            pltpu.VMEM((here, width), f32),
            pltpu.VMEM((3, 8, here), f32),
            dma_sems(1),
            *([pltpu.VMEM(heads.shape, bf16)] if ship else []),
        )
        parts = dict(gather=PlaneGather(block), scatter=PlaneScatter(rows, width, 0))
        if ship:
            parts["heads"] = HeadScatter(heads)
        self.use(**parts)

    def load(self, ins, scratch):
        return pltpu.make_async_copy(ins[10], scratch[1], scratch[9].at[0])

    def start(self, here, ins, outs, scratch):
        self.parts["gather"].start(here, ins[:1], scratch[:1], self.held(scratch, "gather"))
        self.load(ins, scratch).start()

    def finish(self, here, ins, outs, scratch):
        block_ref, doc_ref, scale_ref, heads_ref, q_ref, k_ref, v_ref, z_ref, o_ref, l_ref = ins[:10]
        out_ref, quarter_ref, small_ref = outs
        (
            rows_buf,
            attn_rows,
            k_cols,
            acc_k,
            acc_v,
            acc_q,
            proj,
            out_sum,
            small,
        ) = scratch[:9]
        heads_grad = scratch[10] if self.ship else quarter_ref
        rows, model_width = block_ref.shape
        wide = self.head_width
        width = 2 * wide
        acc_k[...] = jnp.zeros_like(acc_k)
        acc_v[...] = jnp.zeros_like(acc_v)
        out_sum[...] = jnp.zeros_like(out_sum)
        small[...] = jnp.zeros_like(small)
        k_cols[...] = turned(k_ref[...])

        def work(first):
            block = pl.ds(first, rows)
            scaled_grad = lax.dot_general(
                rows_buf[block, :],
                heads_ref[3].reshape(width, model_width),
                (((1,), (1,)), ((), ())),
                preferred_element_type=f32,
            )
            out_sum[...] += lax.dot_general(
                z_ref[block, :],
                rows_buf[block, :],
                (((0,), (0,)), ((), ())),
                preferred_element_type=f32,
            )
            small[0] += fold(o_ref[block, :] * scaled_grad)
            grad = attend_block_back(
                wide,
                first,
                (scaled_grad * scale_ref[...]).astype(bf16),
                q_ref,
                k_ref,
                k_cols,
                v_ref,
                o_ref,
                l_ref,
                doc_ref,
                acc_k,
                acc_v,
                acc_q,
            )
            proj[block, 0:width] = grad
            small[1] += fold(grad.astype(f32))

        self.parts["gather"].finish(
            here, ins[:1], scratch[:1], self.held(scratch, "gather"), work
        )

        def settle(first):
            block = pl.ds(first, rows)
            proj[block, width : 2 * width] = acc_k[block, :].astype(bf16)
            value_grad = acc_v[block, :].astype(bf16)
            proj[block, 2 * width : 3 * width] = value_grad
            small[2] += fold(value_grad.astype(f32))

        in_chunks(8 * rows, rows, settle)
        self.between()

        def early():
            self.load(ins, scratch).wait()
            qkv_grad = lax.dot_general(
                proj[...],
                attn_rows[...],
                (((0,), (0,)), ((), ())),
                preferred_element_type=f32,
            )
            heads_grad[0:3] = qkv_grad.astype(bf16).reshape(3, 2, wide, model_width)
            heads_grad[3] = out_sum[...].astype(bf16).reshape(2, wide, model_width)
            if self.ship:
                self.parts["heads"].start(here, (heads_grad,), None, self.held(scratch, "heads"))

        self.parts["scatter"].finish(
            here,
            None,
            (out_ref,),
            self.held(scratch, "scatter"),
            lambda first: proj[pl.ds(first, rows), :],
            lambda: heads_ref[0:3].reshape(3 * width, model_width),
            early=early,
        )
        if self.ship:
            held = self.held(scratch, "heads")
            self.parts["heads"].finish(here, (heads_grad,), (quarter_ref,), held)
        for i in range(3):
            small_ref[i : i + 1, :] = jnp.sum(small[i], axis=0, keepdims=True)


def format_kernel(f0, f1, s0, s1, h0, h1, first_ref, second_ref, qkv_ref, out_ref):
    part = first_ref.shape[2] // 4
    half = h0.shape[3]
    for layer, (first, second, heads) in enumerate(((f0, s0, h0), (f1, s1, h1))):
        for i in range(4):
            first_ref[layer, :, i * part : (i + 1) * part] = first[i].astype(f32)
            second_ref[layer, i * part : (i + 1) * part, :] = second[i].astype(f32)
        for core in range(2):
            here = pl.ds(core * half, half)
            for kind in range(3):
                pair = jnp.concatenate([heads[core, kind], heads[2 + core, kind]], axis=0)
                qkv_ref[layer, kind, here, :] = jnp.transpose(pair.astype(f32))
            for y in range(2):
                wide = heads.shape[2]
                out_ref[layer, y * wide : (y + 1) * wide, here] = heads[2 * y + core, 3].astype(f32)


def format_weights(first, second, heads):
    _, width, part = first[0].shape
    wide = heads[0].shape[2]
    return pl.pallas_call(
        format_kernel,
        out_shape=(
            jax.ShapeDtypeStruct((2, width, 4 * part), f32),
            jax.ShapeDtypeStruct((2, 4 * part, width), f32),
            jax.ShapeDtypeStruct((2, 3, width, 2 * wide), f32),
            jax.ShapeDtypeStruct((2, 2 * wide, width), f32),
        ),
        in_specs=[pl.BlockSpec(memory_space=pltpu.VMEM)] * 6,
        out_specs=[pl.BlockSpec(memory_space=pltpu.VMEM)] * 4,
        compiler_params=vmem_params(None, 40),
    )(*first, *second, *heads)


def plane_device(
    tokens,
    segment_ids,
    cotangent,
    ln_attn_gain,
    ln_attn_bias,
    qkv_weight,
    qv_bias,
    head_scale,
    out_weight,
    out_bias,
    ln_post_gain,
    ln_post_bias,
    ln_ffn_gain,
    ln_ffn_bias,
    fc1_weight,
    fc1_bias,
    mid_gain,
    mid_bias,
    fc2_weight,
    fc2_bias,
):
    layers = qkv_weight.shape[0]
    model_width = tokens.shape[1]
    heads_all = head_scale.shape[1]
    head_width = model_width // heads_all
    hidden_here = fc1_weight.shape[2]
    hidden_all = hidden_here * 8
    quarter = hidden_here // 4
    half_width = model_width // 2
    x, y, core = lax.axis_index("x"), lax.axis_index("y"), lax.axis_index("core")
    quarter_at = 2 * y + core
    width = 2 * head_width
    ids = iter(range(1, 64))

    doc_row = segment_ids.astype(f32)[None, :]
    ((residual,), (docs,)) = run_tasks(ids, PlaneMove(tokens), PlaneMove(doc_row))
    residual = residual.astype(f32)

    def cut(values, at, size, axis):
        return lax.dynamic_slice_in_dim(values, at * size, size, axis)

    qkv_rows = jnp.transpose(qkv_weight, (0, 2, 3, 1))
    bias_heads = cut(qv_bias, y, head_width, 2)
    small = jnp.concatenate(
        [
            jnp.concatenate([bias_heads, bias_heads], axis=2).reshape(layers, 2 * width),
            cut(fc1_bias, quarter_at, quarter, 1),
            cut(mid_gain, quarter_at, quarter, 1),
            cut(mid_bias, quarter_at, quarter, 1),
        ],
        axis=1,
    )
    head_ids = ((2 * core + jnp.arange(2)) * 2 + x) * 2 + y
    head_onehot = (head_ids[:, None] == jnp.arange(heads_all)[None, :]).astype(f32)
    heads_here = [None] * layers

    stored = []
    for layer in range(layers):
        attn_in, attn_normal, attn_factor = norm_local(
            residual, ln_attn_gain[layer], ln_attn_bias[layer]
        )
        scale = jnp.sum(head_onehot * head_scale[layer][None, :], axis=1)
        scale_row = jnp.repeat(scale, head_width)[None, :]
        late = layer == 0
        sides = [WeightGather(fc1_weight, layer, 1, late)]
        if not late:
            sides.append(WeightGather(fc2_weight, layer, 0))
        ((branch, attn_rows, q, k, v, scaled, attended, logs, *got), (first_here,), *rest) = (
            run_tasks(
                ids,
                AttnForward(
                    attn_in.astype(bf16),
                    docs,
                    scale_row,
                    (qkv_rows, out_weight) if late else (heads_here[layer],),
                    small,
                    head_width,
                    layer,
                    late,
                ),
                *sides,
                mib=40,
            )
        )
        if late:
            heads_here[0], small = got

            def hidden_rows(at):
                part = small[:, :, 2 * width + at * quarter : 2 * width + (at + 1) * quarter]
                return jnp.transpose(part, (1, 0, 2)).reshape(layers, 4 * quarter)

            shift_hidden, gain_hidden, bias_hidden = map(hidden_rows, range(3))
        branch = branch + out_bias[layer]
        post_out, post_normal, post_factor = norm_local(
            branch, ln_post_gain[layer], ln_post_bias[layer]
        )
        middle = residual + post_out
        ffn_in, ffn_normal, ffn_factor = norm_local(middle, ln_ffn_gain[layer], ln_ffn_bias[layer])
        sides = []
        if layer + 1 < layers:
            sides.append(HeadGather(qkv_rows, out_weight, layer + 1, late))
        else:
            sides.append(PlaneMove(cotangent))
        ((ffn_out, ffn_rows, slope, hidden_normal, mixed, totals, *got), (side,)) = run_tasks(
            ids,
            FfnForward(
                ffn_in.astype(bf16),
                first_here,
                fc2_weight if late else rest[0][0],
                shift_hidden[layer][None],
                gain_hidden[layer][None],
                bias_hidden[layer][None],
                layer,
                late,
            ),
            *sides,
            mib=48,
        )
        second_here = got[0] if late else rest[0][0]
        if layer + 1 < layers:
            heads_here[layer + 1] = side
        stored.append(
            (
                first_here,
                second_here,
                attn_normal,
                attn_factor,
                attn_rows,
                q,
                k,
                v,
                attended,
                logs,
                scale_row,
                scaled,
                post_normal,
                post_factor,
                ffn_normal,
                ffn_factor,
                ffn_rows,
                slope,
                hidden_normal,
                mixed,
                totals,
            )
        )
        residual = middle + ffn_out + fc2_bias[layer]
    gradient_b = side
    gradient = gradient_b.astype(f32)

    first_done, second_done = [None] * layers, [None] * layers
    heads_done, hidden_done = [None] * layers, [None] * layers
    early_vectors, late_vectors = [None] * layers, [None] * layers
    pending = None
    for layer in reversed(range(layers)):
        (
            first_here,
            second_here,
            attn_normal,
            attn_factor,
            attn_rows,
            q,
            k,
            v,
            attended,
            logs,
            scale_row,
            scaled,
            post_normal,
            post_factor,
            ffn_normal,
            ffn_factor,
            ffn_rows,
            slope,
            hidden_normal,
            mixed,
            totals,
        ) = stored[layer]
        second_shift_grad = jnp.sum(gradient, axis=0)
        if pending is None:
            sides = [PlaneMove(residual.astype(bf16), back=True)]
        else:
            sides = [HeadScatter(pending[0]), LineThenRows(pending[1])]
        ((ffn_in_grad, first_grad, second_grad, hidden_grad), *got) = run_tasks(
            ids,
            FfnBackward(
                gradient_b,
                first_here,
                second_here,
                gain_hidden[layer][None],
                slope,
                hidden_normal,
                mixed,
                ffn_rows,
                totals,
            ),
            *sides,
            mib=60,
        )
        if pending is None:
            layer_output = got[0][0]
        else:
            heads_grad, hidden_done[layer + 1] = got[0][0], got[1][0]
        ffn_gain_grad = jnp.sum(ffn_in_grad * ffn_normal, axis=0)
        ffn_bias_grad = jnp.sum(ffn_in_grad, axis=0)
        middle_grad = gradient + norm_back(ffn_in_grad, ffn_normal, ffn_factor, ln_ffn_gain[layer])
        post_gain_grad = jnp.sum(middle_grad * post_normal, axis=0)
        post_bias_grad = jnp.sum(middle_grad, axis=0)
        branch_grad = norm_back(middle_grad, post_normal, post_factor, ln_post_gain[layer])
        out_shift_grad = jnp.sum(branch_grad, axis=0)
        early_vectors[layer] = jnp.stack(
            [
                out_shift_grad,
                post_gain_grad,
                post_bias_grad,
                ffn_gain_grad,
                ffn_bias_grad,
                second_shift_grad,
            ]
        )
        sides = [LineThenRows(first_grad), RowsGather(second_grad)]
        if layer == 0:
            sides.append(RowsGather(heads_grad))
            known = early_vectors + late_vectors[1:]
            count = sum(each.shape[0] for each in known)
            known.append(jnp.zeros((-count % 8, model_width), f32))
            sides.append(PlaneSum(jnp.concatenate(known, axis=0)))
        ((attn_in_grad, heads_grad, small_grad), (first_done[layer],), (second_done[layer],), *rest) = (
            run_tasks(
                ids,
                AttnBackward(
                    branch_grad.astype(bf16),
                    docs,
                    scale_row,
                    heads_here[layer],
                    q,
                    k,
                    v,
                    scaled,
                    attended,
                    logs,
                    attn_rows,
                    layer == 0,
                ),
                *sides,
                mib=48,
            )
        )
        scale_grad = jnp.sum(
            head_onehot * jnp.sum(small_grad[0].reshape(2, head_width), axis=1)[:, None], axis=0
        )
        bias_grad = jnp.transpose(small_grad[1:].reshape(2, 2, head_width), (1, 0, 2))
        hidden_grad = jnp.roll(hidden_grad, 1, axis=0).reshape(3, 4, quarter)
        hidden_grad = jnp.concatenate(
            [
                jnp.transpose(hidden_grad, (1, 0, 2)).reshape(4, -1),
                lax.dynamic_update_slice(
                    jnp.zeros((4, width), f32), bias_grad.reshape(2, width), (2 * core, 0)
                ),
            ],
            axis=1,
        ).reshape(4, -1, 128)
        pending = (heads_grad, hidden_grad)
        late_vectors[layer] = jnp.stack(
            [
                jnp.sum(attn_in_grad * attn_normal, axis=0),
                jnp.sum(attn_in_grad, axis=0),
                jnp.pad(scale_grad, (0, model_width - heads_all)),
            ]
        )
        gradient = middle_grad + norm_back(
            attn_in_grad, attn_normal, attn_factor, ln_attn_gain[layer]
        )
        gradient_b = gradient.astype(bf16)
    (heads_done[1],), (summed,) = rest
    ((vectors,), (heads_done[0],), (hidden_done[0],), (input_grad,)) = run_tasks(
        ids,
        PlaneThenLineSum(late_vectors[0], summed),
        RowsGather(pending[0]),
        LineThenRows(pending[1]),
        PlaneMove(gradient_b, back=True),
    )
    input_grad = input_grad.astype(f32)
    early = vectors[: 6 * layers].reshape(layers, 6, model_width)
    late = jnp.stack([vectors[-3:], vectors[6 * layers : 6 * layers + 3]])
    first_grad, second_grad, qkv_grad, out_grad = format_weights(
        first_done,
        second_done,
        heads_done,
    )
    hidden = jnp.stack(hidden_done).reshape(layers, 4, -1)
    bias_grad = jnp.sum(hidden[:, :, 3 * quarter :].reshape(layers, 2, 2, 2, head_width), axis=2)
    bias_grad = jnp.transpose(bias_grad, (0, 2, 1, 3)).reshape(layers, 2, width)
    hidden = hidden[:, :, : 3 * quarter].reshape(layers, 4, 3, quarter)
    hidden = jnp.transpose(hidden, (0, 2, 1, 3)).reshape(layers, 3, hidden_here)
    return (
        layer_output,
        input_grad,
        late[:, 0],
        late[:, 1],
        jnp.transpose(qkv_grad, (0, 2, 1, 3)),
        bias_grad,
        late[:, 2, :heads_all],
        out_grad,
        early[:, 0],
        early[:, 1],
        early[:, 2],
        early[:, 3],
        early[:, 4],
        first_grad,
        hidden[:, 0],
        hidden[:, 1],
        hidden[:, 2],
        second_grad,
        early[:, 5],
    )


def split_specs(rows, mp):
    both = tuple(rows) + tuple(mp)
    in_specs = (
        P(both, None),
        P(rows),
        P(both, None),
        P(),
        P(),
        P(None, None, None, mp),
        P(None, None, mp),
        P(),
        P(None, mp, None),
        P(),
        P(),
        P(),
        P(),
        P(),
        P(None, None, mp),
        P(None, mp),
        P(None, mp),
        P(None, mp),
        P(None, mp, None),
        P(),
    )
    out_specs = (
        P(both, None),
        P(both, None),
        P(),
        P(),
        P(None, None, None, mp),
        P(None, None, mp),
        P(),
        P(None, mp, None),
        P(),
        P(),
        P(),
        P(),
        P(),
        P(None, None, mp),
        P(None, mp),
        P(None, mp),
        P(None, mp),
        P(None, mp, None),
        P(),
    )
    return in_specs, out_specs


def solution(mesh):
    if mesh.shape["rows"] == 4 and mesh.shape["mp"] == 8:
        planes = Mesh(mesh.devices.reshape(2, 2, 4, 2), ("y", "core", "z", "x"))
        in_specs, out_specs = split_specs(("y", "core"), ("z", "x"))
        return jax.shard_map(
            plane_device, mesh=planes, in_specs=in_specs, out_specs=out_specs, check_vma=False
        )
    in_specs, out_specs = split_specs(("rows",), ("mp",))
    return jax.shard_map(
        per_device, mesh=mesh, in_specs=in_specs, out_specs=out_specs, check_vma=False
    )
```

```python
from functools import partial

import jax
import jax.numpy as jnp
from jax import lax
from jax.experimental import pallas as pl
from jax.experimental.pallas import tpu as pltpu
from jax.sharding import Mesh
from jax.sharding import PartitionSpec as P

epsilon = 1e-05
masked = -1e30


def partner(shard, axis, stride):
    return lax.ppermute(shard, axis, [(i, i ^ 1 << stride) for i in range(lax.axis_size(axis))])


def norm_local(values, gain_row, bias_row):
    average = jnp.mean(values, axis=-1, keepdims=True)
    centered = values - average
    spread = jnp.mean(centered * centered, axis=-1, keepdims=True)
    factor = lax.rsqrt(spread + epsilon)
    normal = centered * factor
    return (normal * gain_row + bias_row, normal, factor)


def norm_back(grad_out, normal, factor, gain_row):
    scaled = grad_out * gain_row
    inner_sum = jnp.mean(scaled * normal, axis=-1, keepdims=True)
    return factor * (scaled - jnp.mean(scaled, axis=-1, keepdims=True) - normal * inner_sum)


def collect_rows(normed_b):
    return lax.all_gather(normed_b, "mp", axis=0, tiled=True)


def collect_grads(gradient_b):
    return lax.all_gather(gradient_b, "mp", axis=0, tiled=True)


def reduce_branch(operand_b, weight_b, local_rows):

    def partial_term(first_row, count):
        return jnp.dot(operand_b, weight_b, preferred_element_type=jnp.float32)

    return lax.psum_scatter(
        partial_term(jnp.int32(0), local_rows * lax.axis_size("mp")).astype(jnp.bfloat16),
        "mp",
        scatter_dimension=0,
        tiled=True,
    ).astype(jnp.float32)


def reduce_grads(operand_b, weight_b, local_rows):

    def partial_term(first_row, count):
        return jnp.einsum("tc,dc->td", operand_b, weight_b, preferred_element_type=jnp.float32)

    return lax.psum_scatter(
        partial_term(jnp.int32(0), local_rows * lax.axis_size("mp")).astype(jnp.bfloat16),
        "mp",
        scatter_dimension=0,
        tiled=True,
    ).astype(jnp.float32)


def hidden_stats(first_sum, second_sum):
    return lax.psum((first_sum, second_sum), "mp")


def hidden_grad_stats(first_sum, second_sum):
    return lax.psum((first_sum, second_sum), "mp")


def join_cols(mine, other, is_upper):
    lower_part = jnp.where(is_upper, other, mine)
    upper_part = jnp.where(is_upper, mine, other)
    return jnp.concatenate([lower_part, upper_part], axis=-1)


def join_rows(mine, other, is_upper):
    lower_part = jnp.where(is_upper, other, mine)
    upper_part = jnp.where(is_upper, mine, other)
    return jnp.concatenate([lower_part, upper_part], axis=0)


def split_cols(values, cols_here, is_upper):
    lower_part = values[..., :cols_here]
    upper_part = values[..., cols_here:]
    return (
        jnp.where(is_upper, upper_part, lower_part),
        jnp.where(is_upper, lower_part, upper_part),
    )


def masked_scores(query_block, key_rows, query_start, block_rows, doc_rows, positions):
    factor = query_block.shape[-1] ** (-0.5)
    scores = (
        jnp.einsum("qhe,khe->hqk", query_block, key_rows, preferred_element_type=jnp.float32)
        * factor
    )
    query_place = query_start + jnp.arange(block_rows, dtype=jnp.int32)
    query_docs = lax.dynamic_slice_in_dim(doc_rows, query_start, block_rows, 0)
    allowed = (query_docs[:, None] == doc_rows[None, :]) & (
        query_place[:, None] >= positions[None, :]
    )
    return jnp.where(allowed[None], scores, masked)


def attend_forward(queries, key_rows, value_rows, doc_rows, row_offset):
    total_rows = queries.shape[0]
    block_rows = min(512, total_rows)
    positions = jnp.arange(key_rows.shape[0], dtype=jnp.int32)

    def one_block(first_row):
        query_block = lax.dynamic_slice_in_dim(queries, first_row, block_rows, 0)
        scores = masked_scores(
            query_block, key_rows, row_offset + first_row, block_rows, doc_rows, positions
        )
        row_peak = jnp.max(scores, axis=-1, keepdims=True)
        weights = jnp.exp(scores - row_peak)
        totals = jnp.sum(weights, axis=-1, keepdims=True)
        probabilities = (weights / totals).astype(jnp.bfloat16)
        output = jnp.einsum(
            "hqk,khe->qhe", probabilities, value_rows, preferred_element_type=jnp.float32
        )
        return (output, (row_peak + jnp.log(totals))[..., 0])

    starts = jnp.arange(total_rows // block_rows, dtype=jnp.int32) * block_rows
    outputs, log_totals = lax.map(one_block, starts)
    return (outputs.reshape(queries.shape), log_totals)


def attend_backward(queries, key_rows, value_rows, doc_rows, row_offset, log_totals, grad_out):
    total_rows = queries.shape[0]
    block_rows = min(512, total_rows)
    positions = jnp.arange(key_rows.shape[0], dtype=jnp.int32)
    factor = queries.shape[-1] ** (-0.5)

    def one_block(running, first_row):
        key_grad, value_grad = running
        query_block = lax.dynamic_slice_in_dim(queries, first_row, block_rows, 0)
        grad_block = lax.dynamic_slice_in_dim(grad_out, first_row, block_rows, 0)
        scores = masked_scores(
            query_block, key_rows, row_offset + first_row, block_rows, doc_rows, positions
        )
        block_totals = lax.dynamic_index_in_dim(
            log_totals, first_row // block_rows, 0, keepdims=False
        )
        probabilities = jnp.exp(scores - block_totals[..., None])
        prob_grad = jnp.einsum(
            "qhe,khe->hqk", grad_block, value_rows, preferred_element_type=jnp.float32
        )
        inner_sum = jnp.sum(probabilities * prob_grad, axis=-1, keepdims=True)
        score_grad = (probabilities * (prob_grad - inner_sum)).astype(jnp.bfloat16)
        query_grad = (
            jnp.einsum("hqk,khe->qhe", score_grad, key_rows, preferred_element_type=jnp.float32)
            * factor
        )
        key_grad = (
            key_grad
            + jnp.einsum(
                "hqk,qhe->khe", score_grad, query_block, preferred_element_type=jnp.float32
            )
            * factor
        )
        value_grad = value_grad + jnp.einsum(
            "hqk,qhe->khe",
            probabilities.astype(jnp.bfloat16),
            grad_block,
            preferred_element_type=jnp.float32,
        )
        return ((key_grad, value_grad), query_grad)

    starts = jnp.arange(total_rows // block_rows, dtype=jnp.int32) * block_rows
    zero_grads = jnp.zeros(key_rows.shape, jnp.float32)
    (key_grad, value_grad), query_grads = lax.scan(one_block, (zero_grads, zero_grads), starts)
    return (query_grads.reshape(queries.shape), key_grad, value_grad)


def stack_layers(layer_list, members):
    stacked = []
    for member_index in range(members):
        stacked.append(jnp.stack([entry[member_index] for entry in layer_list], axis=0))
    return stacked


def per_device(
    tokens,
    segment_ids,
    cotangent,
    ln_attn_gain,
    ln_attn_bias,
    qkv_weight,
    qv_bias,
    head_scale,
    out_weight,
    out_bias,
    ln_post_gain,
    ln_post_bias,
    ln_ffn_gain,
    ln_ffn_bias,
    fc1_weight,
    fc1_bias,
    mid_gain,
    mid_bias,
    fc2_weight,
    fc2_bias,
):
    layers = qkv_weight.shape[0]
    local_rows = tokens.shape[0]
    model_width = tokens.shape[1]
    cols_here = qkv_weight.shape[3]
    heads_all = head_scale.shape[1]
    head_width = model_width // heads_all
    pair_cols = 2 * cols_here
    pair_heads = pair_cols // head_width
    group_rows = segment_ids.shape[0]
    half_rows = group_rows // 2
    hidden_all = fc1_weight.shape[2] * lax.axis_size("mp")
    device_index = lax.axis_index("mp")
    is_upper = device_index % 2 == 1
    own_start = jnp.where(is_upper, half_rows, 0).astype(jnp.int32)
    other_start = jnp.where(is_upper, 0, half_rows).astype(jnp.int32)
    first_head = device_index // 2 * pair_heads
    pair_onehot = (
        (first_head + jnp.arange(pair_heads, dtype=jnp.int32))[:, None]
        == jnp.arange(heads_all, dtype=jnp.int32)[None, :]
    ).astype(jnp.float32)
    residual = tokens.astype(jnp.float32)
    stored = []
    for layer_index in range(layers):
        attn_in, attn_normal, attn_factor = norm_local(
            residual, ln_attn_gain[layer_index], ln_attn_bias[layer_index]
        )
        attn_rows = collect_rows(attn_in.astype(jnp.bfloat16))
        qkv_here = qkv_weight[layer_index].reshape(model_width, 3 * cols_here)
        projected = jnp.dot(attn_rows, qkv_here, preferred_element_type=jnp.float32).reshape(
            -1, 3, cols_here
        )
        bias_pair = qv_bias[layer_index]
        query_mine = (projected[:, 0] + bias_pair[0]).astype(jnp.bfloat16)
        key_mine = projected[:, 1].astype(jnp.bfloat16)
        value_mine = (projected[:, 2] + bias_pair[1]).astype(jnp.bfloat16)
        query_send = lax.dynamic_slice_in_dim(query_mine, other_start, half_rows, 0)
        query_recv, key_recv, value_recv = partner((query_send, key_mine, value_mine), "mp", 0)
        query_own = lax.dynamic_slice_in_dim(query_mine, own_start, half_rows, 0)
        queries = join_cols(query_own, query_recv, is_upper).reshape(
            half_rows, pair_heads, head_width
        )
        key_rows = join_cols(key_mine, key_recv, is_upper).reshape(
            group_rows, pair_heads, head_width
        )
        value_rows = join_cols(value_mine, value_recv, is_upper).reshape(
            group_rows, pair_heads, head_width
        )
        attended, log_totals = attend_forward(queries, key_rows, value_rows, segment_ids, own_start)
        pair_scale = jnp.sum(pair_onehot * head_scale[layer_index][None, :], axis=1)
        scaled_half = (
            (attended * pair_scale[None, :, None])
            .astype(jnp.bfloat16)
            .reshape(half_rows, pair_cols)
        )
        own_cols, other_cols = split_cols(scaled_half, cols_here, is_upper)
        scaled_recv = partner(other_cols, "mp", 0)
        scaled_mine = join_rows(own_cols, scaled_recv, is_upper)
        branch = (
            reduce_branch(scaled_mine, out_weight[layer_index], local_rows) + out_bias[layer_index]
        )
        post_out, post_normal, post_factor = norm_local(
            branch, ln_post_gain[layer_index], ln_post_bias[layer_index]
        )
        middle = residual + post_out
        ffn_in, ffn_normal, ffn_factor = norm_local(
            middle, ln_ffn_gain[layer_index], ln_ffn_bias[layer_index]
        )
        ffn_rows = collect_rows(ffn_in.astype(jnp.bfloat16))
        before_gelu = (
            jnp.dot(ffn_rows, fc1_weight[layer_index], preferred_element_type=jnp.float32)
            + fc1_bias[layer_index]
        )
        activated = jax.nn.gelu(before_gelu, approximate=False)
        first_sum, second_sum = hidden_stats(
            jnp.sum(activated, axis=1), jnp.sum(activated * activated, axis=1)
        )
        average = first_sum / hidden_all
        spread = second_sum / hidden_all - average * average
        hidden_factor = lax.rsqrt(spread + epsilon)[:, None]
        hidden_normal = (activated - average[:, None]) * hidden_factor
        mixed_b = (hidden_normal * mid_gain[layer_index] + mid_bias[layer_index]).astype(
            jnp.bfloat16
        )
        ffn_out = reduce_branch(mixed_b, fc2_weight[layer_index], local_rows)
        stored.append(
            (
                attn_normal,
                attn_factor,
                attn_rows,
                queries,
                key_rows,
                value_rows,
                attended,
                log_totals,
                pair_scale,
                scaled_mine,
                post_normal,
                post_factor,
                ffn_normal,
                ffn_factor,
                ffn_rows,
                before_gelu,
                hidden_normal,
                hidden_factor,
                mixed_b,
            )
        )
        residual = middle + ffn_out + fc2_bias[layer_index]
    layer_output = residual.astype(jnp.bfloat16)
    gradient = cotangent.astype(jnp.float32)
    sharded_list = []
    shared_list = []
    for layer_index in reversed(range(layers)):
        (
            attn_normal,
            attn_factor,
            attn_rows,
            queries,
            key_rows,
            value_rows,
            attended,
            log_totals,
            pair_scale,
            scaled_mine,
            post_normal,
            post_factor,
            ffn_normal,
            ffn_factor,
            ffn_rows,
            before_gelu,
            hidden_normal,
            hidden_factor,
            mixed_b,
        ) = stored[layer_index]
        qkv_here = qkv_weight[layer_index].reshape(model_width, 3 * cols_here)
        second_shift_grad = jnp.sum(gradient, axis=0)
        grad_rows = collect_grads(gradient.astype(jnp.bfloat16))
        mixed_grad = jnp.einsum(
            "td,fd->tf", grad_rows, fc2_weight[layer_index], preferred_element_type=jnp.float32
        )
        second_grad = jnp.einsum(
            "tf,td->fd", mixed_b, grad_rows, preferred_element_type=jnp.float32
        )
        hidden_gain_grad = jnp.sum(mixed_grad * hidden_normal, axis=0)
        hidden_shift_grad = jnp.sum(mixed_grad, axis=0)
        normal_grad = mixed_grad * mid_gain[layer_index]
        grad_first, grad_second = hidden_grad_stats(
            jnp.sum(normal_grad, axis=1), jnp.sum(normal_grad * hidden_normal, axis=1)
        )
        active_grad = hidden_factor * (
            normal_grad
            - grad_first[:, None] / hidden_all
            - hidden_normal * grad_second[:, None] / hidden_all
        )
        gelu_pull = jax.vjp(partial(jax.nn.gelu, approximate=False), before_gelu)[1]
        pre_grad_b = gelu_pull(active_grad)[0].astype(jnp.bfloat16)
        first_shift_grad = jnp.sum(pre_grad_b, axis=0, dtype=jnp.float32)
        first_grad = jnp.einsum(
            "td,tf->df", ffn_rows, pre_grad_b, preferred_element_type=jnp.float32
        )
        ffn_in_grad = reduce_grads(pre_grad_b, fc1_weight[layer_index], local_rows)
        ffn_gain_grad = jnp.sum(ffn_in_grad * ffn_normal, axis=0)
        ffn_bias_grad = jnp.sum(ffn_in_grad, axis=0)
        middle_grad = gradient + norm_back(
            ffn_in_grad, ffn_normal, ffn_factor, ln_ffn_gain[layer_index]
        )
        post_gain_grad = jnp.sum(middle_grad * post_normal, axis=0)
        post_bias_grad = jnp.sum(middle_grad, axis=0)
        branch_grad = norm_back(middle_grad, post_normal, post_factor, ln_post_gain[layer_index])
        out_shift_grad = jnp.sum(branch_grad, axis=0)
        branch_rows = collect_grads(branch_grad.astype(jnp.bfloat16))
        scaled_grad = jnp.einsum(
            "td,cd->tc", branch_rows, out_weight[layer_index], preferred_element_type=jnp.float32
        )
        out_grad = jnp.einsum(
            "tc,td->cd", scaled_mine, branch_rows, preferred_element_type=jnp.float32
        )
        grad_send = lax.dynamic_slice_in_dim(scaled_grad, other_start, half_rows, 0)
        grad_recv = partner(grad_send.astype(jnp.bfloat16), "mp", 0).astype(grad_send.dtype)
        grad_own = lax.dynamic_slice_in_dim(scaled_grad, own_start, half_rows, 0)
        scaled_pair = join_cols(grad_own, grad_recv, is_upper).reshape(
            half_rows, pair_heads, head_width
        )
        pair_scale_grad = jnp.sum(attended * scaled_pair, axis=(0, 2))
        scale_grad = jnp.sum(pair_onehot * pair_scale_grad[:, None], axis=0)
        attended_grad_b = (scaled_pair * pair_scale[None, :, None]).astype(jnp.bfloat16)
        query_grad, key_grad, value_grad = attend_backward(
            queries, key_rows, value_rows, segment_ids, own_start, log_totals, attended_grad_b
        )
        query_own, query_other = split_cols(
            query_grad.reshape(half_rows, pair_cols), cols_here, is_upper
        )
        key_own, key_other = split_cols(
            key_grad.reshape(group_rows, pair_cols), cols_here, is_upper
        )
        value_own, value_other = split_cols(
            value_grad.reshape(group_rows, pair_cols), cols_here, is_upper
        )
        query_recv, key_recv, value_recv = (
            partner(query_other.astype(jnp.bfloat16), "mp", 0).astype(query_other.dtype),
            partner(key_other.astype(jnp.bfloat16), "mp", 0).astype(key_other.dtype),
            partner(value_other.astype(jnp.bfloat16), "mp", 0).astype(value_other.dtype),
        )
        query_grad_b = join_rows(query_own, query_recv, is_upper).astype(jnp.bfloat16)
        key_grad_b = (key_own + key_recv).astype(jnp.bfloat16)
        value_grad_b = (value_own + value_recv).astype(jnp.bfloat16)
        proj_grad = jnp.stack([query_grad_b, key_grad_b, value_grad_b], axis=1).reshape(
            -1, 3 * cols_here
        )
        pair_grad = jnp.stack(
            [
                jnp.sum(query_grad_b, axis=0, dtype=jnp.float32),
                jnp.sum(value_grad_b, axis=0, dtype=jnp.float32),
            ],
            axis=0,
        )
        qkv_grad = jnp.einsum(
            "td,tc->dc", attn_rows, proj_grad, preferred_element_type=jnp.float32
        ).reshape(model_width, 3, cols_here)
        attn_in_grad = reduce_grads(proj_grad, qkv_here, local_rows)
        attn_gain_grad = jnp.sum(attn_in_grad * attn_normal, axis=0)
        attn_bias_grad = jnp.sum(attn_in_grad, axis=0)
        gradient = middle_grad + norm_back(
            attn_in_grad, attn_normal, attn_factor, ln_attn_gain[layer_index]
        )
        sharded_list.insert(
            0,
            (
                qkv_grad,
                pair_grad,
                out_grad,
                first_grad,
                first_shift_grad,
                hidden_gain_grad,
                hidden_shift_grad,
                second_grad,
            ),
        )
        shared_list.insert(
            0,
            (
                attn_gain_grad,
                attn_bias_grad,
                scale_grad,
                out_shift_grad,
                post_gain_grad,
                post_bias_grad,
                ffn_gain_grad,
                ffn_bias_grad,
                second_shift_grad,
            ),
        )
    sharded = stack_layers(sharded_list, 8)
    shared = stack_layers(shared_list, 9)
    sharded = (
        lax.psum(sharded[0].astype(jnp.bfloat16), "rows").astype(jnp.float32),
        lax.psum(sharded[1].astype(jnp.bfloat16), "rows").astype(jnp.float32),
        lax.psum(sharded[2].astype(jnp.bfloat16), "rows").astype(jnp.float32),
        lax.psum(sharded[3].astype(jnp.bfloat16), "rows").astype(jnp.float32),
        lax.psum(sharded[4].astype(jnp.bfloat16), "rows").astype(jnp.float32),
        lax.psum(sharded[5].astype(jnp.bfloat16), "rows").astype(jnp.float32),
        lax.psum(sharded[6].astype(jnp.bfloat16), "rows").astype(jnp.float32),
        lax.psum(sharded[7].astype(jnp.bfloat16), "rows").astype(jnp.float32),
    )
    shared = lax.psum(
        (
            shared[0],
            shared[1],
            shared[2],
            shared[3],
            shared[4],
            shared[5],
            shared[6],
            shared[7],
            shared[8],
        ),
        ("rows", "mp"),
    )
    return (
        layer_output,
        gradient,
        shared[0],
        shared[1],
        sharded[0],
        sharded[1],
        shared[2],
        sharded[2],
        shared[3],
        shared[4],
        shared[5],
        shared[6],
        shared[7],
        sharded[3],
        sharded[4],
        sharded[5],
        sharded[6],
        sharded[7],
        shared[8],
    )


MESH_ID = pl.DeviceIdType.MESH
PLANE = ("core", "y", "x")
EVERY = ("y", "core", "z", "x")
f32 = jnp.float32
bf16 = jnp.bfloat16


def vmem_params(collective_id=None, mib=24):
    if collective_id is None:
        return pltpu.CompilerParams(vmem_limit_bytes=mib * 2**20)
    return pltpu.CompilerParams(
        vmem_limit_bytes=mib * 2**20, collective_id=collective_id, has_side_effects=True
    )


class Here:
    def __init__(self):
        self.x, self.y = lax.axis_index("x"), lax.axis_index("y")
        self.core, self.z = lax.axis_index("core"), lax.axis_index("z")

    def peer(self, flip_x, flip_y, flip_core, step_z):
        place = {}
        if flip_x:
            place["x"] = 1 - self.x
        if flip_y:
            place["y"] = 1 - self.y
        if flip_core:
            place["core"] = 1 - self.core
        if step_z:
            place["z"] = lax.rem(self.z + step_z, 4)
        return place

    def block(self, at_core, at_x, at_y):
        return (2 * at_core + lax.rem(at_y + self.z, 2)) * 2 + at_x


BY_X, BY_Y, BY_CORE = (1, 0, 0, 0), (0, 1, 0, 0), (0, 0, 1, 0)
BY_Z = tuple((0, 0, 0, step) for step in (1, 2, 3))
BY_LINE = BY_Z + tuple((0, 0, 1, step) for step in range(4))
BY_PLANE = tuple((flip & 1, flip >> 1 & 1, flip >> 2, 0) for flip in range(1, 8))


def remote(source, target, send_sem, recv_sem, place):
    return pltpu.make_async_remote_copy(
        src_ref=source,
        dst_ref=target,
        send_sem=send_sem,
        recv_sem=recv_sem,
        device_id=place,
        device_id_type=MESH_ID,
    )


def dma_sems(count):
    return pltpu.SemaphoreType.DMA((count,))


class Task:
    arrays = ()
    spaces = ()
    outs = ()
    out_spaces = ()
    scratch = ()
    reach = ()

    def moment(self, name):
        pass

    def start(self, here, ins, outs, scratch):
        pass

    def at_moment(self, name, here, ins, outs, scratch):
        pass

    def finish(self, here, ins, outs, scratch):
        pass


def run_tasks(ids, *tasks, mib=24):
    reach = []
    for task in tasks:
        reach += [way for way in task.reach if way not in reach]

    def kernel(*refs):
        refs = list(refs)
        views = [[], [], []]
        for kind, name in enumerate(("arrays", "outs", "scratch")):
            for task in tasks:
                count = len(getattr(task, name))
                views[kind].append(refs[:count])
                refs = refs[count:]
        here = Here()
        barrier = pltpu.get_barrier_semaphore()
        for way in reach:
            pl.semaphore_signal(barrier, inc=1, device_id=here.peer(*way), device_id_type=MESH_ID)
        pl.semaphore_wait(barrier, len(reach))
        for task, *held in zip(tasks, *views):
            task.start(here, *held)

        def moment(name):
            for task, *held in zip(tasks, *views):
                task.at_moment(name, here, *held)

        tasks[0].moment = moment
        for task, *held in zip(tasks, *views):
            task.finish(here, *held)

    results = pl.pallas_call(
        kernel,
        out_shape=[out for task in tasks for out in task.outs],
        in_specs=[pl.BlockSpec(memory_space=s) for task in tasks for s in task.spaces],
        out_specs=[pl.BlockSpec(memory_space=s) for task in tasks for s in task.out_spaces],
        scratch_shapes=[each for task in tasks for each in task.scratch],
        compiler_params=vmem_params(next(ids), mib),
    )(*[array for task in tasks for array in task.arrays])
    results = list(results)
    split = []
    for task in tasks:
        split.append(results[: len(task.outs)])
        results = results[len(task.outs) :]
    return split


class PlaneMove(Task):
    def __init__(self, values, back=False, when="midway"):
        self.back, self.when = back, when
        self.arrays, self.spaces = (values,), (pltpu.HBM,)
        self.outs = (jax.ShapeDtypeStruct(values.shape, values.dtype),)
        self.out_spaces = (pltpu.HBM,)
        self.scratch = (
            pltpu.VMEM(values.shape, values.dtype),
            dma_sems(3),
            dma_sems(2),
        )
        self.reach = (BY_Y,) + BY_LINE

    def bend(self, here):
        return lax.rem(here.z + here.core, 2) == here.y

    def ends(self, here):
        targets = [{"core": here.z // 2, "z": 2 * y + here.core} for y in range(2)]
        at_home = [(here.z // 2 == here.core) & (2 * y + here.core == here.z) for y in range(2)]
        origin_core = lax.rem(here.z, 2)
        origin_z = 2 * here.core + lax.rem(here.y + origin_core, 2)
        origin_home = (origin_core == here.core) & (origin_z == here.z)
        return targets, at_home, {"core": origin_core, "z": origin_z}, origin_home

    def plan(self, here, ins, outs, scratch):
        held, send, recv = scratch
        targets, at_home, origin, origin_home = self.ends(here)
        bend = self.bend(here)
        away_from = jnp.logical_not
        to_y = here.peer(*BY_Y)
        first, second = [], []
        if not self.back:
            over = remote(ins[0], held, send.at[2], recv.at[0], to_y)
            first.append((away_from(bend), over, True))
            for y in range(2):
                for legs, source, when in (
                    (first, ins[0], bend & (here.y == y)),
                    (second, held, bend & (here.y != y)),
                ):
                    away = remote(source, outs[0], send.at[y], recv.at[1], targets[y])
                    stay = pltpu.make_async_copy(source, outs[0], recv.at[1])
                    legs.append((when & away_from(at_home[y]), away, True))
                    legs.append((when & at_home[y], stay, False))
        else:
            ends_there = here.z // 2 == here.y
            for goes_on, target, slot in ((False, outs[0], 1), (True, held, 0)):
                when = away_from(ends_there) if goes_on else ends_there
                away = remote(ins[0], target, send.at[int(goes_on)], recv.at[slot], origin)
                stay = pltpu.make_async_copy(ins[0], target, recv.at[slot])
                first.append((when & away_from(origin_home), away, True))
                first.append((when & origin_home, stay, False))
            over = remote(held, outs[0], send.at[2], recv.at[1], to_y)
            second.append((bend, over, True))
        return first, second

    def start(self, here, ins, outs, scratch):
        for when, copy, _ in self.plan(here, ins, outs, scratch)[0]:
            pl.when(when)(copy.start)

    def at_moment(self, name, here, ins, outs, scratch):
        if name == self.when:
            held, _, recv = scratch

            @pl.when(self.bend(here))
            def _():
                pltpu.make_async_copy(held, held, recv.at[0]).wait()

            for when, copy, _ in self.plan(here, ins, outs, scratch)[1]:
                pl.when(when)(copy.start)

    def finish(self, here, ins, outs, scratch):
        self.at_moment("end", here, ins, outs, scratch)
        pltpu.make_async_copy(outs[0], outs[0], scratch[2].at[1]).wait()
        for legs in self.plan(here, ins, outs, scratch):
            for when, copy, is_remote in legs:
                if is_remote:
                    pl.when(when)(copy.wait_send)


class PlaneGather(Task):
    def __init__(self, block):
        rows, width = block.shape
        self.arrays, self.spaces = (block,), (pltpu.VMEM,)
        self.outs = (jax.ShapeDtypeStruct((8 * rows, width), block.dtype),)
        self.out_spaces = (pltpu.VMEM,)
        self.scratch = (dma_sems(11), dma_sems(11), pltpu.SemaphoreType.DMA)
        self.reach = (BY_X, BY_Y, BY_CORE)

    def place(self, here, o_ref, at_x, at_y, part=None):
        rows = o_ref.shape[0] // 8
        first = here.block(here.core, at_x, at_y) * rows
        if part is None:
            return o_ref.at[pl.ds(pl.multiple_of(first, rows), rows)]
        half = rows // 2
        return o_ref.at[pl.ds(pl.multiple_of(first + part * half, half), half)]

    def copies(self, here, x_ref, o_ref, send_sem, recv_sem):
        x, y = here.x, here.y
        half = x_ref.shape[0] // 2
        to_x, to_y, to_core = here.peer(*BY_X), here.peer(*BY_Y), here.peer(*BY_CORE)

        def copy(index, source, target, way):
            return remote(source, target, send_sem.at[index], recv_sem.at[index], way)

        def pass_on(index, way, *at):
            return copy(index, self.place(here, o_ref, *at), self.place(here, o_ref, *at), way)

        own = [self.place(here, o_ref, x, y, part) for part in (0, 1)]
        mine = [x_ref.at[pl.ds(part * half, half)] for part in (0, 1)]
        return [
            copy(0, mine[0], own[0], to_x),
            copy(1, mine[1], own[1], to_y),
            copy(2, mine[1], own[1], to_x),
            copy(3, mine[0], own[0], to_y),
            copy(4, x_ref, self.place(here, o_ref, x, y), to_core),
            pass_on(5, to_y, 1 - x, y, 0),
            pass_on(6, to_x, x, 1 - y, 1),
            pass_on(7, to_core, 1 - x, y),
            pass_on(8, to_core, x, 1 - y),
            pass_on(9, to_core, 1 - x, 1 - y, 0),
            pass_on(10, to_core, 1 - x, 1 - y, 1),
        ]

    def keep(self, here, x_ref, o_ref, own_sem):
        return pltpu.make_async_copy(x_ref, self.place(here, o_ref, here.x, here.y), own_sem)

    def start(self, here, ins, outs, scratch):
        copies = self.copies(here, ins[0], outs[0], scratch[0], scratch[1])
        for index in range(5):
            copies[index].start()
        self.keep(here, ins[0], outs[0], scratch[2]).start()

    def finish(self, here, ins, outs, scratch, work=None, soon=None):
        rows = ins[0].shape[0]
        copies = self.copies(here, ins[0], outs[0], scratch[0], scratch[1])

        def done(flip_core, flip_x, flip_y):
            if work is not None:
                at_core = 1 - here.core if flip_core else here.core
                at_x = 1 - here.x if flip_x else here.x
                at_y = 1 - here.y if flip_y else here.y
                work(pl.multiple_of(here.block(at_core, at_x, at_y) * rows, rows))

        self.keep(here, ins[0], outs[0], scratch[2]).wait()
        done(0, 0, 0)
        copies[4].wait_recv()
        done(1, 0, 0)
        for index in range(4):
            copies[index].wait_recv()
            copies[5 + index].start()
        done(0, 1, 0)
        done(0, 0, 1)
        copies[7].wait_recv()
        done(1, 1, 0)
        copies[8].wait_recv()
        done(1, 0, 1)
        copies[5].wait_recv()
        copies[9].start()
        copies[6].wait_recv()
        copies[10].start()
        done(0, 1, 1)
        if soon is not None:
            soon()
        copies[9].wait_recv()
        copies[10].wait_recv()
        done(1, 1, 1)
        for each in copies:
            each.wait_send()


class PlaneScatter(Task):
    def __init__(self, rows, width, weight_dim):
        half = rows // 2
        self.weight_dim = weight_dim
        self.scratch = (
            pltpu.VMEM((4, rows, width), bf16),
            pltpu.VMEM((4, rows, width), bf16),
            pltpu.VMEM((rows, width), bf16),
            pltpu.VMEM((2, half, width), bf16),
            pltpu.VMEM((2, half, width), bf16),
            pltpu.VMEM((2, half, width), bf16),
            pltpu.VMEM((2, half, width), bf16),
            pltpu.VMEM((2, half, width), bf16),
            pltpu.VMEM((half, width), f32),
            pltpu.VMEM((half, width), f32),
            dma_sems(10),
            dma_sems(10),
        )
        self.reach = (BY_X, BY_Y, BY_CORE)

    def finish(self, here, ins, outs, scratch, rows_of, weight_of, early=None, idle=None):
        o_ref = outs[0]
        (
            sib_out,
            sib_in,
            diag_out,
            diag_in,
            last_x_out,
            last_y_out,
            last_x_in,
            last_y_in,
            wait_x,
            wait_y,
            send_sem,
            recv_sem,
        ) = scratch
        rows = o_ref.shape[0]
        half = rows // 2
        x, y, core = here.x, here.y, here.core
        to_x, to_y, to_core = here.peer(*BY_X), here.peer(*BY_Y), here.peer(*BY_CORE)

        def term(at_core, at_x, at_y):
            first = pl.multiple_of(here.block(at_core, at_x, at_y) * rows, rows)
            return lax.dot_general(
                rows_of(first),
                weight_of(),
                (((1,), (self.weight_dim,)), ((), ())),
                preferred_element_type=f32,
            )

        def copy(index, source, target, way):
            return remote(source, target, send_sem.at[index], recv_sem.at[index], way)

        places = ((1 - x, 1 - y), (1 - x, y), (x, 1 - y), (x, y))
        siblings = [copy(i, sib_out.at[i], sib_in.at[i], to_core) for i in range(4)]

        def help_sibling(i):
            sib_out[i] = term(1 - core, *places[i]).astype(bf16)
            siblings[i].start()

        def joined(i):
            mine = term(core, *places[i])
            siblings[i].wait_recv()
            return mine + sib_in[i].astype(f32)

        help_sibling(0)
        total = joined(0)
        diag_out[...] = total.astype(bf16)
        diag_x = copy(4, diag_out.at[pl.ds(0, half)], diag_in.at[0], to_x)
        diag_y = copy(5, diag_out.at[pl.ds(half, half)], diag_in.at[1], to_y)
        diag_x.start()
        diag_y.start()
        help_sibling(1)
        total = joined(1)
        last_x_out[0] = total[:half].astype(bf16)
        x_0 = copy(6, last_x_out.at[0], last_x_in.at[0], to_x)
        x_0.start()
        wait_x[...] = total[half:]
        if early is not None:
            early()
        help_sibling(2)
        total = joined(2)
        last_y_out[1] = total[half:].astype(bf16)
        y_1 = copy(7, last_y_out.at[1], last_y_in.at[1], to_y)
        y_1.start()
        wait_y[...] = total[:half]
        help_sibling(3)
        diag_y.wait_recv()
        last_x_out[1] = (wait_x[...] + diag_in[1].astype(f32)).astype(bf16)
        x_1 = copy(8, last_x_out.at[1], last_x_in.at[1], to_x)
        x_1.start()
        diag_x.wait_recv()
        last_y_out[0] = (wait_y[...] + diag_in[0].astype(f32)).astype(bf16)
        y_0 = copy(9, last_y_out.at[0], last_y_in.at[0], to_y)
        y_0.start()
        o_ref[...] = joined(3)
        if idle is not None:
            idle()
        for part, (by_x, by_y) in enumerate(((x_0, y_0), (x_1, y_1))):
            by_x.wait_recv()
            by_y.wait_recv()
            piece = pl.ds(part * half, half)
            o_ref[piece, :] += last_x_in[part].astype(f32) + last_y_in[part].astype(f32)
        for sent in (*siblings, diag_x, diag_y, x_0, y_1, x_1, y_0):
            sent.wait_send()


class PlaneSum(Task):
    def __init__(self, values):
        self.arrays, self.spaces = (values,), (pltpu.VMEM,)
        self.outs = (jax.ShapeDtypeStruct(values.shape, f32),)
        self.out_spaces = (pltpu.VMEM,)
        self.scratch = (pltpu.VMEM((7, *values.shape), f32), dma_sems(7), dma_sems(7))
        self.reach = BY_PLANE

    def copies(self, here, ins, scratch):
        got, send_sem, recv_sem = scratch
        return [
            remote(ins[0], got.at[i], send_sem.at[i], recv_sem.at[i], here.peer(*way))
            for i, way in enumerate(BY_PLANE)
        ]

    def start(self, here, ins, outs, scratch):
        for each in self.copies(here, ins, scratch):
            each.start()

    def finish(self, here, ins, outs, scratch):
        copies = self.copies(here, ins, scratch)
        for each in copies:
            each.wait_recv()
        got = scratch[0]
        by_x = [ins[0][...] + got[0]]
        for flip in (2, 4, 6):
            by_x.append(got[flip - 1] + got[flip])
        outs[0][...] = (by_x[0] + by_x[1]) + (by_x[2] + by_x[3])
        for each in copies:
            each.wait_send()


class LineGather(Task):
    def __init__(self, values):
        self.arrays, self.spaces = (values,), (pltpu.HBM,)
        self.outs = (jax.ShapeDtypeStruct((4, *values.shape), values.dtype),)
        self.out_spaces = (pltpu.HBM,)
        self.scratch = (dma_sems(4), dma_sems(3))
        self.reach = BY_Z

    def copies(self, here, ins, outs, scratch):
        target = outs[0].at[here.z]
        keep = pltpu.make_async_copy(ins[0], target, scratch[0].at[3])
        return keep, [
            remote(ins[0], target, scratch[0].at[i], scratch[1].at[i], here.peer(*way))
            for i, way in enumerate(BY_Z)
        ]

    def start(self, here, ins, outs, scratch):
        keep, copies = self.copies(here, ins, outs, scratch)
        for each in copies:
            each.start()
        keep.start()

    def finish(self, here, ins, outs, scratch):
        keep, copies = self.copies(here, ins, outs, scratch)
        for each in copies:
            each.wait()
        keep.wait()


class HeadGather(Task):
    def __init__(self, qkv, out, layer, when="start"):
        _, kinds, both, width = qkv.shape
        self.layer, self.when = layer, when
        self.arrays, self.spaces = (qkv, out), (pltpu.HBM,) * 2
        self.outs = (jax.ShapeDtypeStruct((kinds + 1, 2, both // 2, width), qkv.dtype),)
        self.out_spaces = (pltpu.HBM,)
        self.scratch = (dma_sems(8), dma_sems(8))
        self.reach = BY_LINE

    def pieces(self, outs, shard, part):
        half = outs[0].shape[3] // 2
        columns = pl.ds(pl.multiple_of(part * half, half), half)
        return outs[0].at[pl.ds(0, 3), shard, :, columns], outs[0].at[3, shard, :, columns]

    def copies(self, here, ins, outs, scratch):
        shard, target_core = lax.rem(here.z, 2), here.z // 2
        wide, half = outs[0].shape[2], outs[0].shape[3] // 2
        rows = pl.ds(pl.multiple_of(here.y * wide, wide), wide)
        columns = pl.ds(pl.multiple_of(here.core * half, half), half)
        sources = (ins[0].at[self.layer, :, rows, columns], ins[1].at[self.layer, rows, columns])
        targets = self.pieces(outs, shard, here.core)
        keeps, aways = [], []
        for kind in range(2):
            recv_sem = scratch[1].at[4 * kind + 2 * shard + here.core]
            keeps.append(pltpu.make_async_copy(sources[kind], targets[kind], recv_sem))
            for step in range(4):
                place = {"core": target_core, "z": lax.rem(here.z + step, 4)}
                send_sem = scratch[0].at[4 * kind + step]
                aways.append(remote(sources[kind], targets[kind], send_sem, recv_sem, place))
        return keeps, aways

    def begin(self, here, ins, outs, scratch):
        keeps, aways = self.copies(here, ins, outs, scratch)
        for index, each in enumerate(aways):
            if index % 4:
                each.start()
        at_home = here.z // 2 == here.core
        for kind in range(2):
            pl.when(at_home)(keeps[kind].start)
            pl.when(jnp.logical_not(at_home))(aways[4 * kind].start)

    def start(self, *held):
        self.at_moment("start", *held)

    def at_moment(self, name, *held):
        if name == self.when:
            self.begin(*held)

    def finish(self, here, ins, outs, scratch):
        keeps, aways = self.copies(here, ins, outs, scratch)
        for shard in range(2):
            for part in range(2):
                for kind, piece in enumerate(self.pieces(outs, shard, part)):
                    recv_sem = scratch[1].at[4 * kind + 2 * shard + part]
                    pltpu.make_async_copy(piece, piece, recv_sem).wait()
        for index, each in enumerate(aways):
            if index % 4:
                each.wait_send()
        for kind in range(2):
            pl.when(here.z // 2 != here.core)(aways[4 * kind].wait_send)


class LineScatter(Task):
    def __init__(self, values):
        shape = values.shape[1:]
        self.arrays, self.spaces = (values,), (pltpu.VMEM,)
        self.outs, self.out_spaces = (jax.ShapeDtypeStruct(shape, values.dtype),), (pltpu.VMEM,)
        self.scratch = (pltpu.VMEM((3, *shape), values.dtype), dma_sems(3), dma_sems(3))
        self.reach = BY_Z

    def copies(self, here, ins, scratch):
        got, send_sem, recv_sem = scratch
        return [
            remote(
                ins[0].at[lax.rem(here.z + i + 1, 4)],
                got.at[i],
                send_sem.at[i],
                recv_sem.at[i],
                here.peer(*way),
            )
            for i, way in enumerate(BY_Z)
        ]

    def start(self, here, ins, outs, scratch):
        for each in self.copies(here, ins, scratch):
            each.start()

    def finish(self, here, ins, outs, scratch):
        copies = self.copies(here, ins, scratch)
        for each in copies:
            each.wait_recv()
        total = ins[0][here.z].astype(f32)
        for i in range(3):
            total = total + scratch[0][i].astype(f32)
        outs[0][...] = total.astype(outs[0].dtype)
        for each in copies:
            each.wait_send()


class HeadScatter(Task):
    def __init__(self, values):
        kinds, _, wide, width = values.shape
        shape = (kinds, wide, width // 2)
        self.arrays, self.spaces = (values,), (pltpu.VMEM,)
        self.outs, self.out_spaces = (jax.ShapeDtypeStruct(shape, values.dtype),), (pltpu.VMEM,)
        self.scratch = (pltpu.VMEM((4, *shape), values.dtype), dma_sems(4), dma_sems(4))
        self.reach = BY_LINE

    def copies(self, here, ins, scratch):
        got, send_sem, recv_sem = scratch
        half = ins[0].shape[3] // 2
        triples = []
        for shard in range(2):
            for part in range(2):
                source = ins[0].at[:, shard, :, pl.ds(part * half, half)]
                target_z = 2 * here.core + shard
                slot = recv_sem.at[here.z]
                away = remote(
                    source,
                    got.at[here.z],
                    send_sem.at[2 * shard + part],
                    slot,
                    {"core": part, "z": target_z},
                )
                stay = pltpu.make_async_copy(source, got.at[here.z], slot)
                at_home = (target_z == here.z) & (here.core == part)
                triples.append((away, stay, at_home))
        return triples

    def start(self, here, ins, outs, scratch):
        for away, stay, at_home in self.copies(here, ins, scratch):
            pl.when(at_home)(stay.start)
            pl.when(jnp.logical_not(at_home))(away.start)

    def finish(self, here, ins, outs, scratch):
        got, send_sem, recv_sem = scratch
        for plane in range(4):
            pltpu.make_async_copy(got.at[plane], got.at[plane], recv_sem.at[plane]).wait()
        total = got[0].astype(f32)
        for plane in range(1, 4):
            total = total + got[plane].astype(f32)
        outs[0][...] = total.astype(outs[0].dtype)
        for away, stay, at_home in self.copies(here, ins, scratch):
            pl.when(jnp.logical_not(at_home))(away.wait_send)


class RowsGather(Task):
    def __init__(self, values, when="start"):
        self.when = when
        self.arrays, self.spaces = (values,), (pltpu.HBM,)
        self.outs = (jax.ShapeDtypeStruct((4, *values.shape), values.dtype),)
        self.out_spaces = (pltpu.HBM,)
        self.scratch = (dma_sems(4), dma_sems(3))
        self.reach = (BY_Y, BY_CORE)

    def copies(self, here, ins, outs, scratch):
        send_sem, recv_sem = scratch
        own = outs[0].at[2 * here.y + here.core]
        over = outs[0].at[2 * (1 - here.y) + here.core]
        to_y, to_core = here.peer(*BY_Y), here.peer(*BY_CORE)
        return (
            pltpu.make_async_copy(ins[0], own, send_sem.at[3]),
            remote(ins[0], own, send_sem.at[0], recv_sem.at[0], to_y),
            remote(ins[0], own, send_sem.at[1], recv_sem.at[1], to_core),
            remote(over, over, send_sem.at[2], recv_sem.at[2], to_core),
        )

    def start(self, *held):
        self.at_moment("start", *held)

    def at_moment(self, name, *held):
        if name == self.when:
            self.begin(*held)

    def begin(self, here, ins, outs, scratch):
        keep, by_y, by_core, again = self.copies(here, ins, outs, scratch)
        by_y.start()
        by_core.start()
        keep.start()

    def finish(self, here, ins, outs, scratch):
        keep, by_y, by_core, again = self.copies(here, ins, outs, scratch)
        by_y.wait_recv()
        again.start()
        by_core.wait_recv()
        again.wait_recv()
        for each in (by_y, by_core, again):
            each.wait_send()
        keep.wait()


class StepSum(Task):
    def __init__(self, values):
        self.arrays, self.spaces = (values,), (pltpu.VMEM,)
        self.outs = (jax.ShapeDtypeStruct(values.shape, f32),)
        self.out_spaces = (pltpu.VMEM,)
        self.scratch = (
            pltpu.VMEM((2, *values.shape), f32),
            pltpu.VMEM((3, *values.shape), f32),
            dma_sems(3),
            dma_sems(3),
        )
        self.reach = (BY_X, BY_Y, BY_CORE)

    def leg(self, here, index, source, scratch):
        _, got, send_sem, recv_sem = scratch
        way = here.peer(*self.reach[index])
        return remote(source, got.at[index], send_sem.at[index], recv_sem.at[index], way)

    def start(self, here, ins, outs, scratch):
        self.leg(here, 0, ins[0], scratch).start()

    def at_moment(self, name, here, ins, outs, scratch):
        part, got = scratch[:2]
        if name == "midway":
            self.leg(here, 0, ins[0], scratch).wait()
            part[0] = ins[0][...] + got[0]
            self.leg(here, 1, part.at[0], scratch).start()
        if name == "closing":
            self.leg(here, 1, part.at[0], scratch).wait()
            part[1] = part[0] + got[1]
            self.leg(here, 2, part.at[1], scratch).start()

    def finish(self, here, ins, outs, scratch):
        part, got = scratch[:2]
        self.leg(here, 2, part.at[1], scratch).wait()
        outs[0][...] = part[1] + got[2]


class LineSum(Task):
    def __init__(self, values):
        self.arrays, self.spaces = (values,), (pltpu.VMEM,)
        self.outs = (jax.ShapeDtypeStruct(values.shape, f32),)
        self.out_spaces = (pltpu.VMEM,)
        self.scratch = (pltpu.VMEM((4, *values.shape), f32), dma_sems(3), dma_sems(4))
        self.reach = BY_Z

    def copies(self, here, ins, scratch):
        got, send_sem, recv_sem = scratch
        there, slot = got.at[here.z], recv_sem.at[here.z]
        keep = pltpu.make_async_copy(ins[0], there, slot)
        return keep, [
            remote(ins[0], there, send_sem.at[i], slot, here.peer(*way))
            for i, way in enumerate(BY_Z)
        ]

    def start(self, here, ins, outs, scratch):
        keep, copies = self.copies(here, ins, scratch)
        for each in copies:
            each.start()
        keep.start()

    def finish(self, here, ins, outs, scratch):
        got, _, recv_sem = scratch
        _, copies = self.copies(here, ins, scratch)
        for plane in range(4):
            pltpu.make_async_copy(got.at[plane], got.at[plane], recv_sem.at[plane]).wait()
        outs[0][...] = (got[0] + got[1]) + (got[2] + got[3])
        for each in copies:
            each.wait_send()


def to_columns(upper, lower):
    place = lax.broadcasted_iota(jnp.int32, (128, upper.shape[1]), 0)
    return jnp.transpose(jnp.where(place < 64, upper, lower))


def both_columns(upper, lower):
    lane = lax.broadcasted_iota(jnp.int32, (upper.shape[0], 128), 1)
    return jnp.where(lane < 64, upper, lower)


def in_chunks(rows, chunk, step):
    def one(index, carry):
        step(pl.multiple_of(index * chunk, chunk))
        return carry

    lax.fori_loop(0, rows // chunk, one, 0)


def fold(values):
    total = values[:8]
    for first in range(8, values.shape[0], 8):
        total = total + values[first : first + 8]
    return total


class Parts(Task):
    def use(self, **parts):
        self.parts = parts
        self.scratch = list(self.scratch)
        self.at = {}
        reach = []
        for name, part in parts.items():
            self.at[name] = (len(self.scratch), len(self.scratch) + len(part.scratch))
            self.scratch += list(part.scratch)
            reach += [way for way in part.reach if way not in reach]
        self.reach = reach

    def held(self, scratch, name):
        first, last = self.at[name]
        return scratch[first:last]


class PlaneThenLineSum(Parts):
    def __init__(self, values):
        self.arrays, self.spaces = (values,), (pltpu.VMEM,)
        self.outs = (jax.ShapeDtypeStruct(values.shape, f32),)
        self.out_spaces = (pltpu.VMEM,)
        self.scratch = (pltpu.VMEM(values.shape, f32),)
        self.use(plane=PlaneSum(values), line=LineSum(values))

    def start(self, here, ins, outs, scratch):
        self.parts["plane"].start(here, ins, None, self.held(scratch, "plane"))

    def finish(self, here, ins, outs, scratch):
        self.parts["plane"].finish(here, ins, scratch[:1], self.held(scratch, "plane"))
        held = self.held(scratch, "line")
        self.parts["line"].start(here, scratch[:1], None, held)
        self.moment("midway")
        self.parts["line"].finish(here, scratch[:1], outs, held)


def norm_pull(grad_out, normal, factor, gain_row):
    scaled = grad_out * gain_row
    width = scaled.shape[1]
    mean = jnp.sum(scaled, axis=1, keepdims=True) / width
    inner = jnp.sum(scaled * normal, axis=1, keepdims=True) / width
    return factor * (scaled - mean - normal * inner)


NARROW = 128
CHUNK = 256


class FfnForward(Parts):
    def __init__(self, block, first, second, shift, gain, bias, layer, late):
        rows, width = block.shape
        hidden = first.shape[1]
        self.late = late
        self.arrays = (block, first, second, shift, gain, bias)
        self.spaces = (pltpu.VMEM,) * 2 + (pltpu.HBM if late else pltpu.VMEM,) + (pltpu.VMEM,) * 3
        self.outs = (
            jax.ShapeDtypeStruct((rows, width), f32),
            jax.ShapeDtypeStruct((8 * rows, width), bf16),
            jax.ShapeDtypeStruct((8 * rows, hidden), f32),
            jax.ShapeDtypeStruct((8 * rows, hidden), f32),
            jax.ShapeDtypeStruct((8 * rows, hidden), bf16),
            jax.ShapeDtypeStruct((2, 8 * rows), f32),
        )
        self.out_spaces = (pltpu.VMEM,) + (pltpu.HBM,) * 4 + (pltpu.VMEM,)
        self.scratch = (
            pltpu.VMEM((8 * rows, width), bf16),
            pltpu.VMEM((8 * rows, hidden), f32),
            pltpu.VMEM((8 * rows, hidden), f32),
            pltpu.VMEM((8 * rows, hidden), bf16),
            pltpu.VMEM((2, 8 * rows), f32),
            pltpu.VMEM((rows, 128), f32),
            dma_sems(4),
        )
        parts = dict(
            gather=PlaneGather(block),
            scatter=PlaneScatter(rows, width, 0),
            sums=PlaneSum(jax.ShapeDtypeStruct((2, 8 * rows), f32)),
        )
        if late:
            parts["second"] = WeightGather(second, layer, 0)
            self.outs += parts["second"].outs
            self.out_spaces += (pltpu.VMEM,)
        self.use(**parts)

    def start(self, here, ins, outs, scratch):
        self.parts["gather"].start(here, ins[:1], scratch[:1], self.held(scratch, "gather"))
        if self.late:
            held = self.held(scratch, "second")
            self.parts["second"].start(here, ins[2:3], outs[6:7], held)

    def finish(self, here, ins, outs, scratch):
        block_ref, first_ref, second_ref, shift_ref, gain_ref, bias_ref = ins
        out_ref, rows_out, slope_out, normal_out, mixed_out, total_ref = outs[:6]
        if self.late:
            second_ref = outs[6]
        rows_buf, before, active, mixed, sums, columns, save = scratch[:7]
        rows = block_ref.shape[0]
        hidden_all = 8 * first_ref.shape[1]

        def work(first):
            before[pl.ds(first, rows), :] = lax.dot_general(
                rows_buf[pl.ds(first, rows), :],
                first_ref[...],
                (((1,), (0,)), ((), ())),
                preferred_element_type=f32,
            )

            def step(at):
                piece = pl.ds(pl.multiple_of(first + at, CHUNK), CHUNK)
                u = before[piece, :] + shift_ref[...]
                area = 0.5 * (1.0 + lax.erf(u * 0.5**0.5))
                a = u * area
                active[piece, :] = a
                before[piece, :] = area + u * (jnp.exp(-0.5 * u * u) * (0.5 / jnp.pi) ** 0.5)
                columns[pl.ds(at, CHUNK), :] = both_columns(
                    jnp.sum(a, axis=1, keepdims=True), jnp.sum(a * a, axis=1, keepdims=True)
                )

            in_chunks(rows, CHUNK, step)
            turned = jnp.transpose(columns[...])
            sums[0:1, pl.ds(first, rows)] = turned[0:1]
            sums[1:2, pl.ds(first, rows)] = turned[64:65]

        self.parts["gather"].finish(
            here, ins[:1], scratch[:1], self.held(scratch, "gather"), work
        )
        held = self.held(scratch, "sums")
        self.parts["sums"].start(here, (sums,), None, held)
        keep_rows = pltpu.make_async_copy(rows_buf, rows_out, save.at[0])
        keep_rows.start()
        keep_slope = pltpu.make_async_copy(before, slope_out, save.at[1])
        keep_slope.start()
        self.parts["sums"].finish(here, (sums,), (total_ref,), held)
        if self.late:
            held = self.held(scratch, "second")
            self.parts["second"].finish(here, ins[2:3], outs[6:7], held)
        self.moment("midway")

        def rows_of(first):
            average = total_ref[0:1, pl.ds(first, rows)] / hidden_all
            spread = total_ref[1:2, pl.ds(first, rows)] / hidden_all - average * average
            columns[...] = to_columns(average, lax.rsqrt(spread + epsilon))

            def step(at):
                piece = pl.ds(pl.multiple_of(first + at, CHUNK), CHUNK)
                pair = columns[pl.ds(at, CHUNK), :]
                normal = (active[piece, :] - pair[:, 0:1]) * pair[:, 64:65]
                active[piece, :] = normal
                mixed[piece, :] = (normal * gain_ref[...] + bias_ref[...]).astype(bf16)

            in_chunks(rows, CHUNK, step)
            return mixed[pl.ds(first, rows), :]

        keep_mixed = pltpu.make_async_copy(mixed, mixed_out, save.at[2])
        keep_normal = pltpu.make_async_copy(active, normal_out, save.at[3])

        def idle():
            keep_mixed.start()
            keep_normal.start()
            self.moment("closing")

        self.parts["scatter"].finish(
            here,
            None,
            (out_ref,),
            self.held(scratch, "scatter"),
            rows_of,
            lambda: second_ref[...],
            idle=idle,
        )
        for each in (keep_rows, keep_slope, keep_mixed, keep_normal):
            each.wait()


class FfnBackward(Parts):
    def __init__(
        self, block, first, second, gain, slope, normal, mixed, ffn_rows, totals, gradient, norms
    ):
        rows, width = block.shape
        hidden = second.shape[0]
        self.arrays = (block, first, second, gain, totals, slope, normal, mixed, ffn_rows)
        self.spaces = (pltpu.VMEM,) * 5 + (pltpu.HBM,) * 4
        self.arrays += (gradient, *norms)
        self.spaces += (pltpu.VMEM,) * 7
        self.outs = (
            jax.ShapeDtypeStruct((rows, width), f32),
            jax.ShapeDtypeStruct((4, width, hidden // 4), bf16),
            jax.ShapeDtypeStruct((hidden // 4, width), bf16),
            jax.ShapeDtypeStruct((3, hidden), f32),
            jax.ShapeDtypeStruct((rows, width), bf16),
            jax.ShapeDtypeStruct((8, width), f32),
        )
        self.out_spaces = (pltpu.VMEM,) * 6
        self.scratch = (
            pltpu.VMEM((8 * rows, width), bf16),
            pltpu.VMEM((8 * rows, hidden), f32),
            pltpu.VMEM((8 * rows, hidden), f32),
            pltpu.VMEM((8 * rows, hidden), f32),
            pltpu.VMEM((8 * rows, hidden), bf16),
            pltpu.VMEM((8 * rows, width), bf16),
            pltpu.VMEM((8 * rows, hidden), bf16),
            pltpu.VMEM((hidden, width), f32),
            pltpu.VMEM((2, 8 * rows), f32),
            pltpu.VMEM((2, 8 * rows), f32),
            pltpu.VMEM((rows, 128), f32),
            pltpu.VMEM((rows, 128), f32),
            pltpu.VMEM((3, 8, hidden), f32),
            dma_sems(4),
            pltpu.VMEM((4, hidden // 4, width), bf16),
            pltpu.VMEM((6, 8, width), f32),
        )
        self.use(
            gather=PlaneGather(block),
            scatter=PlaneScatter(rows, width, 1),
            second=LineScatter(jax.ShapeDtypeStruct((4, hidden // 4, width), bf16)),
            sums=PlaneSum(jax.ShapeDtypeStruct((2, 8 * rows), f32)),
        )

    def loads(self, ins, scratch):
        targets = (scratch[2], scratch[4], scratch[1], scratch[5])
        return [
            pltpu.make_async_copy(source, target, scratch[13].at[i])
            for i, (source, target) in enumerate(zip((ins[6], ins[7], ins[5], ins[8]), targets))
        ]

    def start(self, here, ins, outs, scratch):
        self.parts["gather"].start(here, ins[:1], scratch[:1], self.held(scratch, "gather"))
        for each in self.loads(ins, scratch):
            each.start()

    def finish(self, here, ins, outs, scratch):
        block_ref, first_ref, second_ref, gain_ref, totals_ref = ins[:5]
        out_ref, first_grad, second_quarter, small_ref, branch_ref, vector_ref = outs
        second_grad, vectors = scratch[14:16]
        (
            rows_buf,
            slope,
            normal_buf,
            grads,
            mixed,
            ffn_rows,
            pre_grad,
            second_sum,
            sums,
            got,
            columns,
            factors,
            small,
        ) = scratch[:13]
        rows = block_ref.shape[0]
        hidden_all = 8 * first_ref.shape[1]
        load_normal, load_mixed, load_slope, load_rows = self.loads(ins, scratch)
        load_normal.wait()
        load_mixed.wait()
        second_sum[...] = jnp.zeros_like(second_sum)
        small[...] = jnp.zeros_like(small)

        def factor_columns(first):
            average = totals_ref[0:1, pl.ds(first, rows)] / hidden_all
            spread = totals_ref[1:2, pl.ds(first, rows)] / hidden_all - average * average
            factors[...] = to_columns(average, lax.rsqrt(spread + epsilon))

        def work(first):
            block = pl.ds(first, rows)
            grads[block, :] = lax.dot_general(
                rows_buf[block, :],
                second_ref[...],
                (((1,), (1,)), ((), ())),
                preferred_element_type=f32,
            )
            second_sum[...] += lax.dot_general(
                mixed[block, :],
                rows_buf[block, :],
                (((0,), (0,)), ((), ())),
                preferred_element_type=f32,
            )

            def step(at):
                piece = pl.ds(pl.multiple_of(first + at, CHUNK), CHUNK)
                normal = normal_buf[piece, :]
                grad = grads[piece, :]
                small[0] += fold(grad * normal)
                small[1] += fold(grad)
                scaled = grad * gain_ref[...]
                grads[piece, :] = scaled
                columns[pl.ds(at, CHUNK), :] = both_columns(
                    jnp.sum(scaled, axis=1, keepdims=True),
                    jnp.sum(scaled * normal, axis=1, keepdims=True),
                )

            in_chunks(rows, CHUNK, step)
            turned = jnp.transpose(columns[...])
            sums[0:1, pl.ds(first, rows)] = turned[0:1]
            sums[1:2, pl.ds(first, rows)] = turned[64:65]

        self.parts["gather"].finish(
            here, ins[:1], scratch[:1], self.held(scratch, "gather"), work
        )
        held = self.held(scratch, "sums")
        self.parts["sums"].start(here, (sums,), None, held)
        second_grad[...] = second_sum[...].astype(bf16).reshape(second_grad.shape)
        load_slope.wait()
        self.moment("midway")
        self.parts["second"].start(here, (second_grad,), None, self.held(scratch, "second"))
        self.parts["sums"].finish(here, (sums,), (got,), held)

        def rows_of(first):
            factor_columns(first)
            columns[...] = to_columns(
                got[0:1, pl.ds(first, rows)] / hidden_all,
                got[1:2, pl.ds(first, rows)] / hidden_all,
            )

            def step(at):
                piece = pl.ds(pl.multiple_of(first + at, CHUNK), CHUNK)
                pair = columns[pl.ds(at, CHUNK), :]
                factor = factors[pl.ds(at, CHUNK), :][:, 64:65]
                active_grad = factor * (
                    grads[piece, :] - pair[:, 0:1] - normal_buf[piece, :] * pair[:, 64:65]
                )
                rounded = (active_grad * slope[piece, :]).astype(bf16)
                pre_grad[piece, :] = rounded
                small[2] += fold(rounded.astype(f32))

            in_chunks(rows, CHUNK, step)
            return pre_grad[pl.ds(first, rows), :]

        def idle():
            load_rows.wait()
            whole = lax.dot_general(
                ffn_rows[...],
                pre_grad[...],
                (((0,), (0,)), ((), ())),
                preferred_element_type=f32,
            ).astype(bf16)
            part = first_grad.shape[2]
            for i in range(4):
                first_grad[i] = whole[:, i * part : (i + 1) * part]
            self.moment("closing")

        self.parts["scatter"].finish(
            here,
            None,
            (out_ref,),
            self.held(scratch, "scatter"),
            rows_of,
            lambda: first_ref[...],
            idle=idle,
        )
        gradient_ref, normal_1, factor_1, gain_1, normal_2, factor_2, gain_2 = ins[9:16]
        vectors[...] = jnp.zeros_like(vectors)

        def pull(at):
            piece = pl.ds(at, NARROW)
            grad, gradient = out_ref[piece, :], gradient_ref[piece, :]
            normal = normal_1[piece, :]
            vectors[3] += fold(grad * normal)
            vectors[4] += fold(grad)
            vectors[5] += fold(gradient)
            middle = gradient + norm_pull(grad, normal, factor_1[piece, :], gain_1[...])
            out_ref[piece, :] = middle
            normal = normal_2[piece, :]
            vectors[1] += fold(middle * normal)
            vectors[2] += fold(middle)
            branch = norm_pull(middle, normal, factor_2[piece, :], gain_2[...])
            vectors[0] += fold(branch)
            branch_ref[piece, :] = branch.astype(bf16)

        in_chunks(rows, NARROW, pull)
        vector_ref[...] = jnp.zeros_like(vector_ref)
        for i in range(6):
            vector_ref[i : i + 1, :] = jnp.sum(vectors[i], axis=0, keepdims=True)
        held = self.held(scratch, "second")
        self.parts["second"].finish(here, (second_grad,), (second_quarter,), held)
        for i in range(3):
            small_ref[i : i + 1, :] = jnp.sum(small[i], axis=0, keepdims=True)


class WeightGather(Task):
    def __init__(self, weights, layer, axis, when="start"):
        self.layer, self.axis, self.when = layer, axis, when
        self.arrays, self.spaces = (weights,), (pltpu.HBM,)
        self.outs = (jax.ShapeDtypeStruct(weights.shape[1:], weights.dtype),)
        self.out_spaces = (pltpu.HBM,)
        self.scratch = (dma_sems(4), dma_sems(3))
        self.reach = BY_Z

    def copies(self, here, ins, outs, scratch):
        part = outs[0].shape[self.axis] // 4

        def cut(ref, at):
            piece = pl.ds(pl.multiple_of(at * part, part), part)
            return ref.at[piece, :] if self.axis == 0 else ref.at[:, piece]

        source = cut(ins[0].at[self.layer], 2 * here.y + here.core)
        target = cut(outs[0], here.z)
        keep = pltpu.make_async_copy(source, target, scratch[0].at[3])
        return keep, [
            remote(source, target, scratch[0].at[i], scratch[1].at[i], here.peer(*way))
            for i, way in enumerate(BY_Z)
        ]

    def begin(self, here, ins, outs, scratch):
        keep, copies = self.copies(here, ins, outs, scratch)
        for each in copies:
            each.start()
        keep.start()

    def start(self, *held):
        self.at_moment("start", *held)

    def at_moment(self, name, *held):
        if name == self.when:
            self.begin(*held)

    def finish(self, here, ins, outs, scratch):
        keep, copies = self.copies(here, ins, outs, scratch)
        for each in copies:
            each.wait()
        keep.wait()


class ThenRows(Parts):
    def __init__(self, first, when):
        self.when = when
        shape = first.outs[0]
        self.arrays, self.spaces = first.arrays, first.spaces
        rows = RowsGather(shape)
        self.outs, self.out_spaces = rows.outs, rows.out_spaces
        self.scratch = (pltpu.VMEM(shape.shape, shape.dtype),)
        self.use(first=first, rows=rows)

    def start(self, here, ins, outs, scratch):
        self.parts["first"].start(here, ins, None, self.held(scratch, "first"))

    def at_moment(self, name, here, ins, outs, scratch):
        if name == self.when:
            self.parts["first"].finish(here, ins, scratch[:1], self.held(scratch, "first"))
            self.parts["rows"].begin(here, scratch[:1], outs, self.held(scratch, "rows"))

    def finish(self, here, ins, outs, scratch):
        self.at_moment("end", here, ins, outs, scratch)
        self.parts["rows"].finish(here, scratch[:1], outs, self.held(scratch, "rows"))


BLOCK = 256
SPAN = 512


def head_masks(head_width, width):
    lane = lax.broadcasted_iota(jnp.int32, (1, width), 1)
    lower = (lane < head_width).astype(bf16)
    return lower, (1 - lower).astype(bf16)


def by_head(values, head_width):
    lower, upper = head_masks(head_width, values.shape[1])
    return jnp.concatenate([values * lower, values * upper], axis=0)


def from_heads(pair, head_width):
    rows = pair.shape[0] // 2
    lane = lax.broadcasted_iota(jnp.int32, (rows, pair.shape[1]), 1)
    return jnp.where(lane < head_width, pair[:rows], pair[rows:])


def tile_facts(doc_ref, first, key_first, keys):
    docs = doc_ref[:, pl.ds(first, BLOCK)]
    docs = jnp.concatenate([docs, docs], axis=1)
    key_docs = doc_ref[:, pl.ds(pl.multiple_of(key_first, keys), keys)]
    key_docs = jnp.transpose(jnp.broadcast_to(key_docs, (128, keys)))[:, 0:1]
    place = lax.broadcasted_iota(jnp.int32, (keys, 2 * BLOCK), 1)
    place = jnp.where(place >= BLOCK, place - BLOCK, place) + (first - key_first)
    allowed = (docs == key_docs) & (place >= lax.broadcasted_iota(jnp.int32, place.shape, 0))
    return docs, allowed


def attend_block(
    head_width, first, q_ref, k_ref, v_cols, doc_ref, o_ref, l_ref, s_buf, acc, top, total
):
    block = first // BLOCK
    last = first // SPAN
    pair = by_head(q_ref[pl.ds(first, BLOCK), :], head_width)

    def scores(at):
        keys = k_ref[pl.ds(pl.multiple_of(at * SPAN, SPAN), SPAN), :]
        return lax.dot_general(keys, pair, (((1,), (1,)), ((), ())), preferred_element_type=f32)

    top[...] = jnp.full_like(top, masked)

    def first_pass(at, carry):
        s = scores(at)
        s_buf[at] = s
        peak = s[:8]
        for row in range(8, SPAN, 8):
            peak = jnp.maximum(peak, s[row : row + 8])
        top[...] = jnp.maximum(top[...], peak)
        return carry

    lax.fori_loop(0, last, first_pass, 0)
    docs, allowed = tile_facts(doc_ref, first, last * SPAN, SPAN)
    s = jnp.where(allowed, scores(last), masked)
    shift = jnp.where(docs == 0, 0.0, masked)
    peak = jnp.maximum(
        jnp.max(top[...], axis=0, keepdims=True) + shift, jnp.max(s, axis=0, keepdims=True)
    )

    def weigh(at, p):
        values = v_cols[:, pl.ds(pl.multiple_of(at * SPAN, SPAN), SPAN)]
        return jnp.dot(values, p.astype(bf16), preferred_element_type=f32)

    p = jnp.exp(s - peak)
    total[...] = fold(p)
    acc[...] = weigh(last, p)
    base = peak - shift

    def second_pass(at, carry):
        p = jnp.exp(s_buf[at] - base)
        total[...] += fold(p)
        acc[...] += weigh(at, p)
        return carry

    lax.fori_loop(0, last, second_pass, 0)
    sums = jnp.sum(total[...], axis=0, keepdims=True)
    out = from_heads(jnp.transpose(acc[...] / sums), head_width)
    o_ref[pl.ds(first, BLOCK), :] = out
    l_ref[block] = peak + jnp.log(sums)
    return out


def attend_block_back(
    head_width,
    first,
    do,
    q_ref,
    k_ref,
    k_cols,
    v_ref,
    o_ref,
    l_ref,
    doc_ref,
    acc_k,
    acc_v,
    acc_q,
):
    block = first // BLOCK
    rows = pl.ds(first, BLOCK)
    pair_q = by_head(q_ref[rows, :], head_width)
    pair_do = by_head(do, head_width)
    out = o_ref[rows, :]
    inner = jnp.sum(
        jnp.concatenate([out, out], axis=0) * pair_do.astype(f32), axis=1, keepdims=True
    )
    inner = jnp.transpose(jnp.broadcast_to(inner, (2 * BLOCK, 128)))[0:1, :]
    logs = l_ref[block]
    docs, allowed = tile_facts(doc_ref, first, first, BLOCK)

    def step(at, base, allowed):
        piece = pl.ds(pl.multiple_of(at * BLOCK, BLOCK), BLOCK)
        s = lax.dot_general(
            k_ref[piece, :], pair_q, (((1,), (1,)), ((), ())), preferred_element_type=f32
        )
        dp = lax.dot_general(
            v_ref[piece, :], pair_do, (((1,), (1,)), ((), ())), preferred_element_type=f32
        )
        p = jnp.exp(s - base)
        if allowed is not None:
            p = jnp.where(allowed, p, 0.0)
        ds = (p * (dp - inner)).astype(bf16)
        acc_v[piece, :] += jnp.dot(p.astype(bf16), pair_do, preferred_element_type=f32)
        acc_k[piece, :] += jnp.dot(ds, pair_q, preferred_element_type=f32)
        return jnp.dot(k_cols[:, piece], ds, preferred_element_type=f32)

    acc_q[...] = step(block, logs, allowed)
    base = jnp.where(docs == 0, logs, -masked)

    def earlier(at, carry):
        acc_q[...] += step(at, base, None)
        return carry

    lax.fori_loop(0, block, earlier, 0)
    grad = from_heads(jnp.transpose(acc_q[...]), head_width)
    return (grad * head_width**-0.5).astype(bf16)


def turned(values):
    return jnp.transpose(values.astype(f32)).astype(bf16)


class AttnForward(Parts):
    def __init__(self, block, docs, scale, heads, biases, wide, layer, late=None):
        rows, width = block.shape
        self.head_width, self.layer, self.late = wide, layer, late
        here = 2 * wide
        self.arrays = (block, docs, scale, biases, *heads)
        far = pltpu.HBM if late else pltpu.VMEM
        self.spaces = (far, far, pltpu.VMEM) + (far,) * (1 + len(heads))
        column = jax.ShapeDtypeStruct((8 * rows, here), bf16)
        self.outs = (
            jax.ShapeDtypeStruct((rows, width), f32),
            jax.ShapeDtypeStruct((8 * rows, width), bf16),
            column,
            column,
            column,
            column,
            jax.ShapeDtypeStruct((8 * rows, here), f32),
            jax.ShapeDtypeStruct((8 * rows // BLOCK, 1, 2 * BLOCK), f32),
        )
        self.out_spaces = (pltpu.VMEM, pltpu.HBM) + (pltpu.VMEM,) * 6
        self.scratch = (
            pltpu.VMEM((8 * rows, width), bf16),
            pltpu.VMEM((here, 8 * rows), bf16),
            pltpu.VMEM((8 * rows // SPAN, SPAN, 2 * BLOCK), f32),
            pltpu.VMEM((here, 2 * BLOCK), f32),
            pltpu.VMEM((8, 2 * BLOCK), f32),
            pltpu.VMEM((8, 2 * BLOCK), f32),
            dma_sems(1),
        )
        parts = dict(gather=PlaneGather(block), scatter=PlaneScatter(rows, width, 0))
        if late:
            parts.update(heads=HeadGather(*heads, layer), biases=LineGather(biases))
            parts.update(tokens=PlaneMove(block, when="push"), docs=PlaneMove(docs, when="push"))
            self.outs += parts["heads"].outs + parts["biases"].outs
            self.outs += (jax.ShapeDtypeStruct(docs.shape, f32),)
            self.outs += (jax.ShapeDtypeStruct(block.shape, f32),) * 2
            self.outs += (jax.ShapeDtypeStruct((rows, 1), f32),)
            self.out_spaces += (pltpu.VMEM,) * 6
            self.scratch += (pltpu.VMEM(block.shape, bf16), pltpu.VMEM(block.shape, bf16))
            self.arrays += tuple(late)
            self.spaces += (pltpu.VMEM,) * 2
        self.use(**parts)

    def start(self, here, ins, outs, scratch):
        if self.late:
            for name, at, target in (("tokens", 0, scratch[7]), ("docs", 1, outs[10])):
                self.parts[name].start(here, (ins[at],), (target,), self.held(scratch, name))
        else:
            self.parts["gather"].start(here, ins[:1], scratch[:1], self.held(scratch, "gather"))

    def first_norm(self, here, ins, outs, scratch):
        tokens, block = scratch[7:9]
        residual_ref, normal_ref, factor_ref = outs[11:14]
        moves = [
            (self.parts[name], (here, (ins[at],), (target,), self.held(scratch, name)))
            for name, at, target in (("tokens", 0, tokens), ("docs", 1, outs[10]))
        ]
        for part, held in moves:
            part.at_moment("push", *held)
        self.parts["biases"].start(here, ins[3:4], outs[9:10], self.held(scratch, "biases"))
        self.parts["heads"].start(here, ins[4:6], outs[8:9], self.held(scratch, "heads"))
        for part, held in moves:
            part.finish(*held)
        values = tokens[...].astype(f32)
        residual_ref[...] = values
        width = values.shape[1]
        centered = values - jnp.sum(values, axis=1, keepdims=True) / width
        spread = jnp.sum(centered * centered, axis=1, keepdims=True) / width
        factor = lax.rsqrt(spread + epsilon)
        factor_ref[...] = factor
        normal = centered * factor
        normal_ref[...] = normal
        block[...] = (normal * ins[6][...] + ins[7][...]).astype(bf16)
        return block

    def finish(self, here, ins, outs, scratch):
        block_ref, doc_ref, scale_ref = ins[:3]
        heads_ref, bias_ref = outs[8:10] if self.late else (ins[4], ins[3])
        if self.late:
            doc_ref = outs[10]
            block_ref = self.first_norm(here, ins, outs, scratch)
            self.parts["gather"].start(
                here, (block_ref,), scratch[:1], self.held(scratch, "gather")
            )
        out_ref, rows_out, q_ref, k_ref, v_ref, z_ref, o_ref, l_ref = outs[:8]
        rows_buf, v_cols, s_buf, acc, top, total, save = scratch[:7]
        rows, model_width = block_ref.shape
        wide = self.head_width
        width = 2 * wide

        def bias_row(at):
            pair = [
                bias_ref[2 * here.core + i, self.layer : self.layer + 1, at : at + width]
                for i in range(2)
            ]
            lane = lax.broadcasted_iota(jnp.int32, (1, width), 1)
            return jnp.where(lane < wide, pair[0], pair[1])

        def work(first):
            block = pl.ds(first, rows)
            projected = lax.dot_general(
                rows_buf[block, :],
                heads_ref[0:3].reshape(3 * width, model_width),
                (((1,), (1,)), ((), ())),
                preferred_element_type=f32,
            )
            q = (projected[:, :width] + bias_row(0)).astype(bf16).astype(f32)
            q_ref[block, :] = (q * wide**-0.5).astype(bf16)
            k_ref[block, :] = projected[:, width : 2 * width].astype(bf16)
            v = (projected[:, 2 * width :] + bias_row(width)).astype(bf16)
            v_ref[block, :] = v
            v_cols[:, block] = turned(v)

        self.parts["gather"].finish(
            here,
            (block_ref,),
            scratch[:1],
            self.held(scratch, "gather"),
            None if self.late else work,
        )
        keep_rows = pltpu.make_async_copy(rows_buf, rows_out, save.at[0])
        keep_rows.start()
        if self.late:
            self.parts["heads"].finish(here, ins[4:6], outs[8:9], self.held(scratch, "heads"))
            self.parts["biases"].finish(here, ins[3:4], outs[9:10], self.held(scratch, "biases"))
            in_chunks(8 * rows, rows, work)
        self.moment("midway")

        def rows_of(first):
            out = attend_block(
                wide, first, q_ref, k_ref, v_cols, doc_ref, o_ref, l_ref, s_buf, acc, top, total
            )
            z = (out * scale_ref[...]).astype(bf16)
            z_ref[pl.ds(first, rows), :] = z
            return z

        self.parts["scatter"].finish(
            here,
            None,
            (out_ref,),
            self.held(scratch, "scatter"),
            rows_of,
            lambda: heads_ref[3].reshape(width, model_width),
            idle=lambda: self.moment("closing"),
        )
        keep_rows.wait()


class AttnBackward(Parts):
    def __init__(
        self, block, docs, scale, heads, q, k, v, z, o, logs, attn_rows, ship, norm, hidden
    ):
        rows, width = block.shape
        kinds, _, wide, _ = heads.shape
        self.head_width = wide
        here = 2 * wide
        self.arrays = (block, docs, scale, heads, q, k, v, z, o, logs, attn_rows)
        self.spaces = (pltpu.VMEM,) * 10 + (pltpu.HBM,)
        self.arrays += (*norm, hidden)
        self.spaces += (pltpu.VMEM,) * 5
        self.outs = (
            jax.ShapeDtypeStruct((rows, width), f32),
            jax.ShapeDtypeStruct((kinds, wide, width // 2) if ship else heads.shape, bf16),
            jax.ShapeDtypeStruct((4, 4, here), f32),
            jax.ShapeDtypeStruct((rows, width), bf16),
            jax.ShapeDtypeStruct((8, width), f32),
        )
        self.ship = ship
        self.out_spaces = (pltpu.VMEM,) * 5
        self.scratch = (
            pltpu.VMEM((8 * rows, width), bf16),
            pltpu.VMEM((8 * rows, width), bf16),
            pltpu.VMEM((here, 8 * rows), bf16),
            pltpu.VMEM((8 * rows, here), f32),
            pltpu.VMEM((8 * rows, here), f32),
            pltpu.VMEM((here, 2 * BLOCK), f32),
            pltpu.VMEM((8 * rows, 3 * here), bf16),
            pltpu.VMEM((here, width), f32),
            pltpu.VMEM((3, 8, here), f32),
            dma_sems(1),
            pltpu.VMEM((2, 8, width), f32),
            *([pltpu.VMEM(heads.shape, bf16)] if ship else []),
        )
        parts = dict(gather=PlaneGather(block), scatter=PlaneScatter(rows, width, 0))
        if ship:
            parts["heads"] = HeadScatter(heads)
        self.use(**parts)

    def load(self, ins, scratch):
        return pltpu.make_async_copy(ins[10], scratch[1], scratch[9].at[0])

    def start(self, here, ins, outs, scratch):
        self.parts["gather"].start(here, ins[:1], scratch[:1], self.held(scratch, "gather"))
        self.load(ins, scratch).start()

    def finish(self, here, ins, outs, scratch):
        block_ref, doc_ref, scale_ref, heads_ref, q_ref, k_ref, v_ref, z_ref, o_ref, l_ref = ins[:10]
        out_ref, quarter_ref, hidden_ref, rounded_ref, vector_ref = outs
        middle_ref, normal_ref, factor_ref, gain_ref, sums_ref = ins[11:16]
        (
            rows_buf,
            attn_rows,
            k_cols,
            acc_k,
            acc_v,
            acc_q,
            proj,
            out_sum,
            small,
        ) = scratch[:9]
        vectors = scratch[10]
        heads_grad = scratch[11] if self.ship else quarter_ref
        rows, model_width = block_ref.shape
        wide = self.head_width
        width = 2 * wide
        acc_k[...] = jnp.zeros_like(acc_k)
        acc_v[...] = jnp.zeros_like(acc_v)
        out_sum[...] = jnp.zeros_like(out_sum)
        small[...] = jnp.zeros_like(small)
        k_cols[...] = turned(k_ref[...])

        def work(first):
            block = pl.ds(first, rows)
            scaled_grad = lax.dot_general(
                rows_buf[block, :],
                heads_ref[3].reshape(width, model_width),
                (((1,), (1,)), ((), ())),
                preferred_element_type=f32,
            )
            out_sum[...] += lax.dot_general(
                z_ref[block, :],
                rows_buf[block, :],
                (((0,), (0,)), ((), ())),
                preferred_element_type=f32,
            )
            small[0] += fold(o_ref[block, :] * scaled_grad)
            grad = attend_block_back(
                wide,
                first,
                (scaled_grad * scale_ref[...]).astype(bf16),
                q_ref,
                k_ref,
                k_cols,
                v_ref,
                o_ref,
                l_ref,
                doc_ref,
                acc_k,
                acc_v,
                acc_q,
            )
            proj[block, 0:width] = grad
            small[1] += fold(grad.astype(f32))

        self.parts["gather"].finish(
            here,
            ins[:1],
            scratch[:1],
            self.held(scratch, "gather"),
            work,
            lambda: self.moment("soon"),
        )

        def settle(first):
            block = pl.ds(first, rows)
            proj[block, width : 2 * width] = acc_k[block, :].astype(bf16)
            value_grad = acc_v[block, :].astype(bf16)
            proj[block, 2 * width : 3 * width] = value_grad
            small[2] += fold(value_grad.astype(f32))

        in_chunks(8 * rows, rows, settle)
        self.moment("midway")

        def early():
            self.load(ins, scratch).wait()
            qkv_grad = lax.dot_general(
                proj[...],
                attn_rows[...],
                (((0,), (0,)), ((), ())),
                preferred_element_type=f32,
            )
            heads_grad[0:3] = qkv_grad.astype(bf16).reshape(3, 2, wide, model_width)
            heads_grad[3] = out_sum[...].astype(bf16).reshape(2, wide, model_width)
            if self.ship:
                self.parts["heads"].start(here, (heads_grad,), None, self.held(scratch, "heads"))

        early()
        self.parts["scatter"].finish(
            here,
            None,
            (out_ref,),
            self.held(scratch, "scatter"),
            lambda first: proj[pl.ds(first, rows), :],
            lambda: heads_ref[0:3].reshape(3 * width, model_width),
            idle=lambda: self.moment("closing"),
        )
        vectors[...] = jnp.zeros_like(vectors)

        def pull(at):
            piece = pl.ds(at, NARROW)
            grad, normal = out_ref[piece, :], normal_ref[piece, :]
            vectors[0] += fold(grad * normal)
            vectors[1] += fold(grad)
            gradient = middle_ref[piece, :] + norm_pull(
                grad, normal, factor_ref[piece, :], gain_ref[...]
            )
            out_ref[piece, :] = gradient
            rounded_ref[piece, :] = gradient.astype(bf16)

        in_chunks(rows, NARROW, pull)
        scale_cols, query_cols, value_cols = (
            jnp.sum(small[i], axis=0, keepdims=True) for i in range(3)
        )
        vector_ref[...] = jnp.zeros_like(vector_ref)
        for i in range(2):
            vector_ref[i : i + 1, :] = jnp.sum(vectors[i], axis=0, keepdims=True)
        lane = lax.broadcasted_iota(jnp.int32, (1, width), 1)
        place = lax.broadcasted_iota(jnp.int32, (1, model_width), 1)
        scale_row = jnp.zeros((1, model_width), f32)
        for i in range(2):
            head = ((2 * here.core + i) * 2 + here.x) * 2 + here.y
            own = (lane >= i * wide) & (lane < (i + 1) * wide)
            total = jnp.sum(jnp.where(own, scale_cols, 0.0), axis=1, keepdims=True)
            scale_row = scale_row + jnp.where(place == head, total, 0.0)
        vector_ref[2:3, :] = scale_row
        pairs = [
            jnp.concatenate(
                [cols[:, i * wide : (i + 1) * wide] for cols in (query_cols, value_cols)], axis=1
            )
            for i in range(2)
        ]
        for shard in range(4):
            for row, source in enumerate((2, 0, 1)):
                cut = sums_ref[source : source + 1, shard * width : (shard + 1) * width]
                hidden_ref[shard, row : row + 1, :] = cut
            own = here.core == shard // 2
            hidden_ref[shard, 3:4, :] = jnp.where(own, pairs[shard % 2], 0.0)
        if self.ship:
            held = self.held(scratch, "heads")
            self.parts["heads"].finish(here, (heads_grad,), (quarter_ref,), held)


def finish_kernel(layers, *refs):
    (layer_ref, grad_ref), refs = refs[:2], refs[2:]
    groups = []
    for _ in range(6):
        groups.append(refs[:layers])
        refs = refs[layers:]
    firsts, seconds, heads_all, hiddens, earlies, lates = groups
    (
        layer_out,
        grad_out,
        attn_gain,
        attn_bias,
        qkv_out,
        bias_out,
        scale_out,
        out_out,
        out_shift,
        post_gain,
        post_bias,
        ffn_gain,
        ffn_bias,
        first_out,
        first_shift,
        mid_gain,
        mid_bias,
        second_out,
        second_shift,
    ) = refs
    layer_out[...] = layer_ref[...]
    grad_out[...] = grad_ref[...].astype(f32)
    for layer in range(layers):
        first, second, heads, hidden = (g[layer] for g in (firsts, seconds, heads_all, hiddens))
        part = first.shape[2]
        wide, half = heads.shape[2:]
        row = slice(layer, layer + 1)
        for i, ref in enumerate((out_shift, post_gain, post_bias, ffn_gain, ffn_bias, second_shift)):
            ref[row, :] = earlies[layer][i : i + 1, :]
        for i, ref in enumerate((attn_gain, attn_bias)):
            ref[row, :] = lates[layer][i : i + 1, :]
        scale_out[row, :] = lates[layer][2:3, 0 : scale_out.shape[1]]
        for i in range(4):
            cut = slice(i * part, (i + 1) * part)
            first_out[layer, :, cut] = first[i].astype(f32)
            second_out[layer, cut, :] = second[i].astype(f32)
            for at, ref in enumerate((first_shift, mid_gain, mid_bias)):
                ref[row, cut] = hidden[i, at : at + 1, :]
        biases = [hidden[2 * y, 3:4, :] + hidden[2 * y + 1, 3:4, :] for y in range(2)]
        for i in range(2):
            bias_out[layer, i : i + 1, :] = jnp.concatenate(
                [each[:, i * wide : (i + 1) * wide] for each in biases], axis=1
            )
        for core in range(2):
            here = slice(core * half, (core + 1) * half)
            for kind in range(3):
                pair = jnp.concatenate([heads[core, kind], heads[2 + core, kind]], axis=0)
                qkv_out[layer, kind, here, :] = jnp.transpose(pair.astype(f32))
            for y in range(2):
                out_out[layer, y * wide : (y + 1) * wide, here] = heads[2 * y + core, 3].astype(f32)


def finish_all(layer_output, gradient, heads_count, *groups):
    firsts, seconds, heads = groups[:3]
    layers = len(firsts)
    rows, width = layer_output.shape
    part = firsts[0].shape[2]
    wide = heads[0].shape[2]
    vector = jax.ShapeDtypeStruct((layers, width), f32)
    hidden = jax.ShapeDtypeStruct((layers, 4 * part), f32)
    outs = (
        jax.ShapeDtypeStruct((rows, width), bf16),
        jax.ShapeDtypeStruct((rows, width), f32),
        vector,
        vector,
        jax.ShapeDtypeStruct((layers, 3, width, 2 * wide), f32),
        jax.ShapeDtypeStruct((layers, 2, 2 * wide), f32),
        jax.ShapeDtypeStruct((layers, heads_count), f32),
        jax.ShapeDtypeStruct((layers, 2 * wide, width), f32),
        vector,
        vector,
        vector,
        vector,
        vector,
        jax.ShapeDtypeStruct((layers, width, 4 * part), f32),
        hidden,
        hidden,
        hidden,
        jax.ShapeDtypeStruct((layers, 4 * part, width), f32),
        vector,
    )
    arrays = [layer_output, gradient] + [each for group in groups for each in group]
    results = list(
        pl.pallas_call(
            partial(finish_kernel, layers),
            out_shape=outs,
            in_specs=[pl.BlockSpec(memory_space=pltpu.VMEM)] * len(arrays),
            out_specs=[pl.BlockSpec(memory_space=pltpu.VMEM)] * len(outs),
            compiler_params=vmem_params(None, 44),
        )(*arrays)
    )
    results[4] = jnp.transpose(results[4], (0, 2, 1, 3))
    return tuple(results)


def plane_device(
    tokens,
    segment_ids,
    cotangent,
    ln_attn_gain,
    ln_attn_bias,
    qkv_weight,
    qv_bias,
    head_scale,
    out_weight,
    out_bias,
    ln_post_gain,
    ln_post_bias,
    ln_ffn_gain,
    ln_ffn_bias,
    fc1_weight,
    fc1_bias,
    mid_gain,
    mid_bias,
    fc2_weight,
    fc2_bias,
):
    layers = qkv_weight.shape[0]
    model_width = tokens.shape[1]
    heads_all = head_scale.shape[1]
    head_width = model_width // heads_all
    hidden_here = fc1_weight.shape[2]
    hidden_all = hidden_here * 8
    quarter = hidden_here // 4
    half_width = model_width // 2
    x, y, core = lax.axis_index("x"), lax.axis_index("y"), lax.axis_index("core")
    quarter_at = 2 * y + core
    width = 2 * head_width
    ids = iter(range(1, 64))

    docs = segment_ids.astype(f32)[None, :]

    def cut(values, at, size, axis):
        return lax.dynamic_slice_in_dim(values, at * size, size, axis)

    qkv_rows = jnp.transpose(qkv_weight, (0, 2, 3, 1))
    bias_heads = cut(qv_bias, y, head_width, 2)
    small = jnp.concatenate(
        [
            jnp.concatenate([bias_heads, bias_heads], axis=2).reshape(layers, 2 * width),
            cut(fc1_bias, quarter_at, quarter, 1),
            cut(mid_gain, quarter_at, quarter, 1),
            cut(mid_bias, quarter_at, quarter, 1),
        ],
        axis=1,
    )
    head_ids = ((2 * core + jnp.arange(2)) * 2 + x) * 2 + y
    head_onehot = (head_ids[:, None] == jnp.arange(heads_all)[None, :]).astype(f32)
    heads_here = [None] * layers

    stored = []
    for layer in range(layers):
        late = None
        if layer == 0:
            late = (ln_attn_gain[layer][None], ln_attn_bias[layer][None])
            block = tokens
        else:
            attn_in, attn_normal, attn_factor = norm_local(
                residual, ln_attn_gain[layer], ln_attn_bias[layer]
            )
            block = attn_in.astype(bf16)
        scale = jnp.sum(head_onehot * head_scale[layer][None, :], axis=1)
        scale_row = jnp.repeat(scale, head_width)[None, :]
        sides = [WeightGather(fc1_weight, layer, 1, "midway" if late else "start")]
        if not late:
            sides.append(WeightGather(fc2_weight, layer, 0))
        ((branch, attn_rows, q, k, v, scaled, attended, logs, *got), (first_here,), *rest) = (
            run_tasks(
                ids,
                AttnForward(
                    block,
                    docs,
                    scale_row,
                    (qkv_rows, out_weight) if late else (heads_here[layer],),
                    small,
                    head_width,
                    layer,
                    late,
                ),
                *sides,
                mib=40,
            )
        )
        if late:
            heads_here[0], small, docs, residual, attn_normal, attn_factor = got

            def hidden_rows(at):
                part = small[:, :, 2 * width + at * quarter : 2 * width + (at + 1) * quarter]
                return jnp.transpose(part, (1, 0, 2)).reshape(layers, 4 * quarter)

            shift_hidden, gain_hidden, bias_hidden = map(hidden_rows, range(3))
        branch = branch + out_bias[layer]
        post_out, post_normal, post_factor = norm_local(
            branch, ln_post_gain[layer], ln_post_bias[layer]
        )
        middle = residual + post_out
        ffn_in, ffn_normal, ffn_factor = norm_local(middle, ln_ffn_gain[layer], ln_ffn_bias[layer])
        sides = []
        if layer + 1 < layers:
            sides.append(HeadGather(qkv_rows, out_weight, layer + 1, "midway" if late else "start"))
        else:
            sides.append(PlaneMove(cotangent))
        ((ffn_out, ffn_rows, slope, hidden_normal, mixed, totals, *got), (side,)) = run_tasks(
            ids,
            FfnForward(
                ffn_in.astype(bf16),
                first_here,
                fc2_weight if late else rest[0][0],
                shift_hidden[layer][None],
                gain_hidden[layer][None],
                bias_hidden[layer][None],
                layer,
                late is not None,
            ),
            *sides,
            mib=48,
        )
        second_here = got[0] if late else rest[0][0]
        if layer + 1 < layers:
            heads_here[layer + 1] = side
        stored.append(
            (
                first_here,
                second_here,
                attn_normal,
                attn_factor,
                attn_rows,
                q,
                k,
                v,
                attended,
                logs,
                scale_row,
                scaled,
                post_normal,
                post_factor,
                ffn_normal,
                ffn_factor,
                ffn_rows,
                slope,
                hidden_normal,
                mixed,
                totals,
            )
        )
        residual = middle + ffn_out + fc2_bias[layer]
    gradient_b = side
    gradient = gradient_b.astype(f32)

    first_done, second_done = [None] * layers, [None] * layers
    heads_done, hidden_done = [None] * layers, [None] * layers
    early_done, late_done = [None] * layers, [None] * layers
    late_vectors = None
    for layer in reversed(range(layers)):
        (
            first_here,
            second_here,
            attn_normal,
            attn_factor,
            attn_rows,
            q,
            k,
            v,
            attended,
            logs,
            scale_row,
            scaled,
            post_normal,
            post_factor,
            ffn_normal,
            ffn_factor,
            ffn_rows,
            slope,
            hidden_normal,
            mixed,
            totals,
        ) = stored[layer]
        last = layer + 1 == layers
        if last:
            sides = [PlaneMove(residual.astype(bf16), back=True)]
        else:
            sides = [RowsGather(heads_grad, "midway")]
            sides.append(ThenRows(LineScatter(hidden_grad), "closing"))
            sides += [LineSum(early_vectors), StepSum(late_vectors)]
        ((gradient, first_grad, second_grad, hidden_sums, branch_b, early_vectors), *got) = (
            run_tasks(
                ids,
                FfnBackward(
                    gradient_b,
                    first_here,
                    second_here,
                    gain_hidden[layer][None],
                    slope,
                    hidden_normal,
                    mixed,
                    ffn_rows,
                    totals,
                    gradient,
                    (
                        ffn_normal,
                        ffn_factor,
                        ln_ffn_gain[layer][None],
                        post_normal,
                        post_factor,
                        ln_post_gain[layer][None],
                    ),
                ),
                *sides,
                mib=60,
            )
        )
        if last:
            layer_output = got[0][0]
        else:
            heads_done[layer + 1], hidden_done[layer + 1] = got[0][0], got[1][0]
            early_done[layer + 1], late_vectors = got[2][0], got[3][0]
        sides = [ThenRows(LineScatter(first_grad), "soon"), RowsGather(second_grad)]
        sides.append(StepSum(early_vectors))
        if not last:
            sides.append(LineSum(late_vectors))
        ((gradient, heads_grad, hidden_grad, gradient_b, late_vectors), *got) = run_tasks(
            ids,
            AttnBackward(
                branch_b,
                docs,
                scale_row,
                heads_here[layer],
                q,
                k,
                v,
                scaled,
                attended,
                logs,
                attn_rows,
                True,
                (gradient, attn_normal, attn_factor, ln_attn_gain[layer][None]),
                hidden_sums,
            ),
            *sides,
            mib=48,
        )
        first_done[layer], second_done[layer], early_vectors = got[0][0], got[1][0], got[2][0]
        if not last:
            late_done[layer + 1] = got[3][0]
    ((late_done[0],), (early_done[0],), (input_grad,), (heads_done[0],), (hidden_done[0],)) = (
        run_tasks(
            ids,
            PlaneThenLineSum(late_vectors),
            LineSum(early_vectors),
            PlaneMove(gradient_b, back=True),
            RowsGather(heads_grad),
            ThenRows(LineScatter(hidden_grad), "midway"),
        )
    )
    return finish_all(
        layer_output,
        input_grad,
        heads_all,
        first_done,
        second_done,
        heads_done,
        hidden_done,
        early_done,
        late_done,
    )


def split_specs(rows, mp):
    both = tuple(rows) + tuple(mp)
    in_specs = (
        P(both, None),
        P(rows),
        P(both, None),
        P(),
        P(),
        P(None, None, None, mp),
        P(None, None, mp),
        P(),
        P(None, mp, None),
        P(),
        P(),
        P(),
        P(),
        P(),
        P(None, None, mp),
        P(None, mp),
        P(None, mp),
        P(None, mp),
        P(None, mp, None),
        P(),
    )
    out_specs = (
        P(both, None),
        P(both, None),
        P(),
        P(),
        P(None, None, None, mp),
        P(None, None, mp),
        P(),
        P(None, mp, None),
        P(),
        P(),
        P(),
        P(),
        P(),
        P(None, None, mp),
        P(None, mp),
        P(None, mp),
        P(None, mp),
        P(None, mp, None),
        P(),
    )
    return in_specs, out_specs


def solution(mesh):
    if mesh.shape["rows"] == 4 and mesh.shape["mp"] == 8:
        planes = Mesh(mesh.devices.reshape(2, 2, 4, 2), ("y", "core", "z", "x"))
        in_specs, out_specs = split_specs(("y", "core"), ("z", "x"))
        return jax.shard_map(
            plane_device, mesh=planes, in_specs=in_specs, out_specs=out_specs, check_vma=False
        )
    in_specs, out_specs = split_specs(("rows",), ("mp",))
    return jax.shard_map(
        per_device, mesh=mesh, in_specs=in_specs, out_specs=out_specs, check_vma=False
    )
```

```python
from functools import partial

import jax
import jax.numpy as jnp
from jax import lax
from jax.experimental import pallas as pl
from jax.experimental.pallas import tpu as pltpu
from jax.sharding import Mesh
from jax.sharding import PartitionSpec as P

epsilon = 1e-05
masked = -1e30


def partner(shard, axis, stride):
    return lax.ppermute(shard, axis, [(i, i ^ 1 << stride) for i in range(lax.axis_size(axis))])


def norm_local(values, gain_row, bias_row):
    average = jnp.mean(values, axis=-1, keepdims=True)
    centered = values - average
    spread = jnp.mean(centered * centered, axis=-1, keepdims=True)
    factor = lax.rsqrt(spread + epsilon)
    normal = centered * factor
    return (normal * gain_row + bias_row, normal, factor)


def norm_back(grad_out, normal, factor, gain_row):
    scaled = grad_out * gain_row
    inner_sum = jnp.mean(scaled * normal, axis=-1, keepdims=True)
    return factor * (scaled - jnp.mean(scaled, axis=-1, keepdims=True) - normal * inner_sum)


def collect_rows(normed_b):
    return lax.all_gather(normed_b, "mp", axis=0, tiled=True)


def collect_grads(gradient_b):
    return lax.all_gather(gradient_b, "mp", axis=0, tiled=True)


def reduce_branch(operand_b, weight_b, local_rows):

    def partial_term(first_row, count):
        return jnp.dot(operand_b, weight_b, preferred_element_type=jnp.float32)

    return lax.psum_scatter(
        partial_term(jnp.int32(0), local_rows * lax.axis_size("mp")).astype(jnp.bfloat16),
        "mp",
        scatter_dimension=0,
        tiled=True,
    ).astype(jnp.float32)


def reduce_grads(operand_b, weight_b, local_rows):

    def partial_term(first_row, count):
        return jnp.einsum("tc,dc->td", operand_b, weight_b, preferred_element_type=jnp.float32)

    return lax.psum_scatter(
        partial_term(jnp.int32(0), local_rows * lax.axis_size("mp")).astype(jnp.bfloat16),
        "mp",
        scatter_dimension=0,
        tiled=True,
    ).astype(jnp.float32)


def hidden_stats(first_sum, second_sum):
    return lax.psum((first_sum, second_sum), "mp")


def hidden_grad_stats(first_sum, second_sum):
    return lax.psum((first_sum, second_sum), "mp")


def join_cols(mine, other, is_upper):
    lower_part = jnp.where(is_upper, other, mine)
    upper_part = jnp.where(is_upper, mine, other)
    return jnp.concatenate([lower_part, upper_part], axis=-1)


def join_rows(mine, other, is_upper):
    lower_part = jnp.where(is_upper, other, mine)
    upper_part = jnp.where(is_upper, mine, other)
    return jnp.concatenate([lower_part, upper_part], axis=0)


def split_cols(values, cols_here, is_upper):
    lower_part = values[..., :cols_here]
    upper_part = values[..., cols_here:]
    return (
        jnp.where(is_upper, upper_part, lower_part),
        jnp.where(is_upper, lower_part, upper_part),
    )


def masked_scores(query_block, key_rows, query_start, block_rows, doc_rows, positions):
    factor = query_block.shape[-1] ** (-0.5)
    scores = (
        jnp.einsum("qhe,khe->hqk", query_block, key_rows, preferred_element_type=jnp.float32)
        * factor
    )
    query_place = query_start + jnp.arange(block_rows, dtype=jnp.int32)
    query_docs = lax.dynamic_slice_in_dim(doc_rows, query_start, block_rows, 0)
    allowed = (query_docs[:, None] == doc_rows[None, :]) & (
        query_place[:, None] >= positions[None, :]
    )
    return jnp.where(allowed[None], scores, masked)


def attend_forward(queries, key_rows, value_rows, doc_rows, row_offset):
    total_rows = queries.shape[0]
    block_rows = min(512, total_rows)
    positions = jnp.arange(key_rows.shape[0], dtype=jnp.int32)

    def one_block(first_row):
        query_block = lax.dynamic_slice_in_dim(queries, first_row, block_rows, 0)
        scores = masked_scores(
            query_block, key_rows, row_offset + first_row, block_rows, doc_rows, positions
        )
        row_peak = jnp.max(scores, axis=-1, keepdims=True)
        weights = jnp.exp(scores - row_peak)
        totals = jnp.sum(weights, axis=-1, keepdims=True)
        probabilities = (weights / totals).astype(jnp.bfloat16)
        output = jnp.einsum(
            "hqk,khe->qhe", probabilities, value_rows, preferred_element_type=jnp.float32
        )
        return (output, (row_peak + jnp.log(totals))[..., 0])

    starts = jnp.arange(total_rows // block_rows, dtype=jnp.int32) * block_rows
    outputs, log_totals = lax.map(one_block, starts)
    return (outputs.reshape(queries.shape), log_totals)


def attend_backward(queries, key_rows, value_rows, doc_rows, row_offset, log_totals, grad_out):
    total_rows = queries.shape[0]
    block_rows = min(512, total_rows)
    positions = jnp.arange(key_rows.shape[0], dtype=jnp.int32)
    factor = queries.shape[-1] ** (-0.5)

    def one_block(running, first_row):
        key_grad, value_grad = running
        query_block = lax.dynamic_slice_in_dim(queries, first_row, block_rows, 0)
        grad_block = lax.dynamic_slice_in_dim(grad_out, first_row, block_rows, 0)
        scores = masked_scores(
            query_block, key_rows, row_offset + first_row, block_rows, doc_rows, positions
        )
        block_totals = lax.dynamic_index_in_dim(
            log_totals, first_row // block_rows, 0, keepdims=False
        )
        probabilities = jnp.exp(scores - block_totals[..., None])
        prob_grad = jnp.einsum(
            "qhe,khe->hqk", grad_block, value_rows, preferred_element_type=jnp.float32
        )
        inner_sum = jnp.sum(probabilities * prob_grad, axis=-1, keepdims=True)
        score_grad = (probabilities * (prob_grad - inner_sum)).astype(jnp.bfloat16)
        query_grad = (
            jnp.einsum("hqk,khe->qhe", score_grad, key_rows, preferred_element_type=jnp.float32)
            * factor
        )
        key_grad = (
            key_grad
            + jnp.einsum(
                "hqk,qhe->khe", score_grad, query_block, preferred_element_type=jnp.float32
            )
            * factor
        )
        value_grad = value_grad + jnp.einsum(
            "hqk,qhe->khe",
            probabilities.astype(jnp.bfloat16),
            grad_block,
            preferred_element_type=jnp.float32,
        )
        return ((key_grad, value_grad), query_grad)

    starts = jnp.arange(total_rows // block_rows, dtype=jnp.int32) * block_rows
    zero_grads = jnp.zeros(key_rows.shape, jnp.float32)
    (key_grad, value_grad), query_grads = lax.scan(one_block, (zero_grads, zero_grads), starts)
    return (query_grads.reshape(queries.shape), key_grad, value_grad)


def stack_layers(layer_list, members):
    stacked = []
    for member_index in range(members):
        stacked.append(jnp.stack([entry[member_index] for entry in layer_list], axis=0))
    return stacked


def per_device(
    tokens,
    segment_ids,
    cotangent,
    ln_attn_gain,
    ln_attn_bias,
    qkv_weight,
    qv_bias,
    head_scale,
    out_weight,
    out_bias,
    ln_post_gain,
    ln_post_bias,
    ln_ffn_gain,
    ln_ffn_bias,
    fc1_weight,
    fc1_bias,
    mid_gain,
    mid_bias,
    fc2_weight,
    fc2_bias,
):
    layers = qkv_weight.shape[0]
    local_rows = tokens.shape[0]
    model_width = tokens.shape[1]
    cols_here = qkv_weight.shape[3]
    heads_all = head_scale.shape[1]
    head_width = model_width // heads_all
    pair_cols = 2 * cols_here
    pair_heads = pair_cols // head_width
    group_rows = segment_ids.shape[0]
    half_rows = group_rows // 2
    hidden_all = fc1_weight.shape[2] * lax.axis_size("mp")
    device_index = lax.axis_index("mp")
    is_upper = device_index % 2 == 1
    own_start = jnp.where(is_upper, half_rows, 0).astype(jnp.int32)
    other_start = jnp.where(is_upper, 0, half_rows).astype(jnp.int32)
    first_head = device_index // 2 * pair_heads
    pair_onehot = (
        (first_head + jnp.arange(pair_heads, dtype=jnp.int32))[:, None]
        == jnp.arange(heads_all, dtype=jnp.int32)[None, :]
    ).astype(jnp.float32)
    residual = tokens.astype(jnp.float32)
    stored = []
    for layer_index in range(layers):
        attn_in, attn_normal, attn_factor = norm_local(
            residual, ln_attn_gain[layer_index], ln_attn_bias[layer_index]
        )
        attn_rows = collect_rows(attn_in.astype(jnp.bfloat16))
        qkv_here = qkv_weight[layer_index].reshape(model_width, 3 * cols_here)
        projected = jnp.dot(attn_rows, qkv_here, preferred_element_type=jnp.float32).reshape(
            -1, 3, cols_here
        )
        bias_pair = qv_bias[layer_index]
        query_mine = (projected[:, 0] + bias_pair[0]).astype(jnp.bfloat16)
        key_mine = projected[:, 1].astype(jnp.bfloat16)
        value_mine = (projected[:, 2] + bias_pair[1]).astype(jnp.bfloat16)
        query_send = lax.dynamic_slice_in_dim(query_mine, other_start, half_rows, 0)
        query_recv, key_recv, value_recv = partner((query_send, key_mine, value_mine), "mp", 0)
        query_own = lax.dynamic_slice_in_dim(query_mine, own_start, half_rows, 0)
        queries = join_cols(query_own, query_recv, is_upper).reshape(
            half_rows, pair_heads, head_width
        )
        key_rows = join_cols(key_mine, key_recv, is_upper).reshape(
            group_rows, pair_heads, head_width
        )
        value_rows = join_cols(value_mine, value_recv, is_upper).reshape(
            group_rows, pair_heads, head_width
        )
        attended, log_totals = attend_forward(queries, key_rows, value_rows, segment_ids, own_start)
        pair_scale = jnp.sum(pair_onehot * head_scale[layer_index][None, :], axis=1)
        scaled_half = (
            (attended * pair_scale[None, :, None])
            .astype(jnp.bfloat16)
            .reshape(half_rows, pair_cols)
        )
        own_cols, other_cols = split_cols(scaled_half, cols_here, is_upper)
        scaled_recv = partner(other_cols, "mp", 0)
        scaled_mine = join_rows(own_cols, scaled_recv, is_upper)
        branch = (
            reduce_branch(scaled_mine, out_weight[layer_index], local_rows) + out_bias[layer_index]
        )
        post_out, post_normal, post_factor = norm_local(
            branch, ln_post_gain[layer_index], ln_post_bias[layer_index]
        )
        middle = residual + post_out
        ffn_in, ffn_normal, ffn_factor = norm_local(
            middle, ln_ffn_gain[layer_index], ln_ffn_bias[layer_index]
        )
        ffn_rows = collect_rows(ffn_in.astype(jnp.bfloat16))
        before_gelu = (
            jnp.dot(ffn_rows, fc1_weight[layer_index], preferred_element_type=jnp.float32)
            + fc1_bias[layer_index]
        )
        activated = jax.nn.gelu(before_gelu, approximate=False)
        first_sum, second_sum = hidden_stats(
            jnp.sum(activated, axis=1), jnp.sum(activated * activated, axis=1)
        )
        average = first_sum / hidden_all
        spread = second_sum / hidden_all - average * average
        hidden_factor = lax.rsqrt(spread + epsilon)[:, None]
        hidden_normal = (activated - average[:, None]) * hidden_factor
        mixed_b = (hidden_normal * mid_gain[layer_index] + mid_bias[layer_index]).astype(
            jnp.bfloat16
        )
        ffn_out = reduce_branch(mixed_b, fc2_weight[layer_index], local_rows)
        stored.append(
            (
                attn_normal,
                attn_factor,
                attn_rows,
                queries,
                key_rows,
                value_rows,
                attended,
                log_totals,
                pair_scale,
                scaled_mine,
                post_normal,
                post_factor,
                ffn_normal,
                ffn_factor,
                ffn_rows,
                before_gelu,
                hidden_normal,
                hidden_factor,
                mixed_b,
            )
        )
        residual = middle + ffn_out + fc2_bias[layer_index]
    layer_output = residual.astype(jnp.bfloat16)
    gradient = cotangent.astype(jnp.float32)
    sharded_list = []
    shared_list = []
    for layer_index in reversed(range(layers)):
        (
            attn_normal,
            attn_factor,
            attn_rows,
            queries,
            key_rows,
            value_rows,
            attended,
            log_totals,
            pair_scale,
            scaled_mine,
            post_normal,
            post_factor,
            ffn_normal,
            ffn_factor,
            ffn_rows,
            before_gelu,
            hidden_normal,
            hidden_factor,
            mixed_b,
        ) = stored[layer_index]
        qkv_here = qkv_weight[layer_index].reshape(model_width, 3 * cols_here)
        second_shift_grad = jnp.sum(gradient, axis=0)
        grad_rows = collect_grads(gradient.astype(jnp.bfloat16))
        mixed_grad = jnp.einsum(
            "td,fd->tf", grad_rows, fc2_weight[layer_index], preferred_element_type=jnp.float32
        )
        second_grad = jnp.einsum(
            "tf,td->fd", mixed_b, grad_rows, preferred_element_type=jnp.float32
        )
        hidden_gain_grad = jnp.sum(mixed_grad * hidden_normal, axis=0)
        hidden_shift_grad = jnp.sum(mixed_grad, axis=0)
        normal_grad = mixed_grad * mid_gain[layer_index]
        grad_first, grad_second = hidden_grad_stats(
            jnp.sum(normal_grad, axis=1), jnp.sum(normal_grad * hidden_normal, axis=1)
        )
        active_grad = hidden_factor * (
            normal_grad
            - grad_first[:, None] / hidden_all
            - hidden_normal * grad_second[:, None] / hidden_all
        )
        gelu_pull = jax.vjp(partial(jax.nn.gelu, approximate=False), before_gelu)[1]
        pre_grad_b = gelu_pull(active_grad)[0].astype(jnp.bfloat16)
        first_shift_grad = jnp.sum(pre_grad_b, axis=0, dtype=jnp.float32)
        first_grad = jnp.einsum(
            "td,tf->df", ffn_rows, pre_grad_b, preferred_element_type=jnp.float32
        )
        ffn_in_grad = reduce_grads(pre_grad_b, fc1_weight[layer_index], local_rows)
        ffn_gain_grad = jnp.sum(ffn_in_grad * ffn_normal, axis=0)
        ffn_bias_grad = jnp.sum(ffn_in_grad, axis=0)
        middle_grad = gradient + norm_back(
            ffn_in_grad, ffn_normal, ffn_factor, ln_ffn_gain[layer_index]
        )
        post_gain_grad = jnp.sum(middle_grad * post_normal, axis=0)
        post_bias_grad = jnp.sum(middle_grad, axis=0)
        branch_grad = norm_back(middle_grad, post_normal, post_factor, ln_post_gain[layer_index])
        out_shift_grad = jnp.sum(branch_grad, axis=0)
        branch_rows = collect_grads(branch_grad.astype(jnp.bfloat16))
        scaled_grad = jnp.einsum(
            "td,cd->tc", branch_rows, out_weight[layer_index], preferred_element_type=jnp.float32
        )
        out_grad = jnp.einsum(
            "tc,td->cd", scaled_mine, branch_rows, preferred_element_type=jnp.float32
        )
        grad_send = lax.dynamic_slice_in_dim(scaled_grad, other_start, half_rows, 0)
        grad_recv = partner(grad_send.astype(jnp.bfloat16), "mp", 0).astype(grad_send.dtype)
        grad_own = lax.dynamic_slice_in_dim(scaled_grad, own_start, half_rows, 0)
        scaled_pair = join_cols(grad_own, grad_recv, is_upper).reshape(
            half_rows, pair_heads, head_width
        )
        pair_scale_grad = jnp.sum(attended * scaled_pair, axis=(0, 2))
        scale_grad = jnp.sum(pair_onehot * pair_scale_grad[:, None], axis=0)
        attended_grad_b = (scaled_pair * pair_scale[None, :, None]).astype(jnp.bfloat16)
        query_grad, key_grad, value_grad = attend_backward(
            queries, key_rows, value_rows, segment_ids, own_start, log_totals, attended_grad_b
        )
        query_own, query_other = split_cols(
            query_grad.reshape(half_rows, pair_cols), cols_here, is_upper
        )
        key_own, key_other = split_cols(
            key_grad.reshape(group_rows, pair_cols), cols_here, is_upper
        )
        value_own, value_other = split_cols(
            value_grad.reshape(group_rows, pair_cols), cols_here, is_upper
        )
        query_recv, key_recv, value_recv = (
            partner(query_other.astype(jnp.bfloat16), "mp", 0).astype(query_other.dtype),
            partner(key_other.astype(jnp.bfloat16), "mp", 0).astype(key_other.dtype),
            partner(value_other.astype(jnp.bfloat16), "mp", 0).astype(value_other.dtype),
        )
        query_grad_b = join_rows(query_own, query_recv, is_upper).astype(jnp.bfloat16)
        key_grad_b = (key_own + key_recv).astype(jnp.bfloat16)
        value_grad_b = (value_own + value_recv).astype(jnp.bfloat16)
        proj_grad = jnp.stack([query_grad_b, key_grad_b, value_grad_b], axis=1).reshape(
            -1, 3 * cols_here
        )
        pair_grad = jnp.stack(
            [
                jnp.sum(query_grad_b, axis=0, dtype=jnp.float32),
                jnp.sum(value_grad_b, axis=0, dtype=jnp.float32),
            ],
            axis=0,
        )
        qkv_grad = jnp.einsum(
            "td,tc->dc", attn_rows, proj_grad, preferred_element_type=jnp.float32
        ).reshape(model_width, 3, cols_here)
        attn_in_grad = reduce_grads(proj_grad, qkv_here, local_rows)
        attn_gain_grad = jnp.sum(attn_in_grad * attn_normal, axis=0)
        attn_bias_grad = jnp.sum(attn_in_grad, axis=0)
        gradient = middle_grad + norm_back(
            attn_in_grad, attn_normal, attn_factor, ln_attn_gain[layer_index]
        )
        sharded_list.insert(
            0,
            (
                qkv_grad,
                pair_grad,
                out_grad,
                first_grad,
                first_shift_grad,
                hidden_gain_grad,
                hidden_shift_grad,
                second_grad,
            ),
        )
        shared_list.insert(
            0,
            (
                attn_gain_grad,
                attn_bias_grad,
                scale_grad,
                out_shift_grad,
                post_gain_grad,
                post_bias_grad,
                ffn_gain_grad,
                ffn_bias_grad,
                second_shift_grad,
            ),
        )
    sharded = stack_layers(sharded_list, 8)
    shared = stack_layers(shared_list, 9)
    sharded = (
        lax.psum(sharded[0].astype(jnp.bfloat16), "rows").astype(jnp.float32),
        lax.psum(sharded[1].astype(jnp.bfloat16), "rows").astype(jnp.float32),
        lax.psum(sharded[2].astype(jnp.bfloat16), "rows").astype(jnp.float32),
        lax.psum(sharded[3].astype(jnp.bfloat16), "rows").astype(jnp.float32),
        lax.psum(sharded[4].astype(jnp.bfloat16), "rows").astype(jnp.float32),
        lax.psum(sharded[5].astype(jnp.bfloat16), "rows").astype(jnp.float32),
        lax.psum(sharded[6].astype(jnp.bfloat16), "rows").astype(jnp.float32),
        lax.psum(sharded[7].astype(jnp.bfloat16), "rows").astype(jnp.float32),
    )
    shared = lax.psum(
        (
            shared[0],
            shared[1],
            shared[2],
            shared[3],
            shared[4],
            shared[5],
            shared[6],
            shared[7],
            shared[8],
        ),
        ("rows", "mp"),
    )
    return (
        layer_output,
        gradient,
        shared[0],
        shared[1],
        sharded[0],
        sharded[1],
        shared[2],
        sharded[2],
        shared[3],
        shared[4],
        shared[5],
        shared[6],
        shared[7],
        sharded[3],
        sharded[4],
        sharded[5],
        sharded[6],
        sharded[7],
        shared[8],
    )


MESH_ID = pl.DeviceIdType.MESH
PLANE = ("core", "y", "x")
EVERY = ("y", "core", "z", "x")
f32 = jnp.float32
bf16 = jnp.bfloat16


def vmem_params(collective_id=None, mib=24):
    if collective_id is None:
        return pltpu.CompilerParams(vmem_limit_bytes=mib * 2**20)
    return pltpu.CompilerParams(
        vmem_limit_bytes=mib * 2**20, collective_id=collective_id, has_side_effects=True
    )


class Here:
    def __init__(self):
        self.x, self.y = lax.axis_index("x"), lax.axis_index("y")
        self.core, self.z = lax.axis_index("core"), lax.axis_index("z")

    def peer(self, flip_x, flip_y, flip_core, step_z):
        place = {}
        if flip_x:
            place["x"] = 1 - self.x
        if flip_y:
            place["y"] = 1 - self.y
        if flip_core:
            place["core"] = 1 - self.core
        if step_z:
            place["z"] = lax.rem(self.z + step_z, 4)
        return place

    def block(self, at_core, at_x, at_y):
        return (2 * at_core + lax.rem(at_y + self.z, 2)) * 2 + at_x


BY_X, BY_Y, BY_CORE = (1, 0, 0, 0), (0, 1, 0, 0), (0, 0, 1, 0)
BY_Z = tuple((0, 0, 0, step) for step in (1, 2, 3))
BY_LINE = BY_Z + tuple((0, 0, 1, step) for step in range(4))
BY_PLANE = tuple((flip & 1, flip >> 1 & 1, flip >> 2, 0) for flip in range(1, 8))


def remote(source, target, send_sem, recv_sem, place):
    return pltpu.make_async_remote_copy(
        src_ref=source,
        dst_ref=target,
        send_sem=send_sem,
        recv_sem=recv_sem,
        device_id=place,
        device_id_type=MESH_ID,
    )


def dma_sems(count):
    return pltpu.SemaphoreType.DMA((count,))


class Task:
    arrays = ()
    spaces = ()
    outs = ()
    out_spaces = ()
    scratch = ()
    reach = ()

    def moment(self, name):
        pass

    def start(self, here, ins, outs, scratch):
        pass

    def at_moment(self, name, here, ins, outs, scratch):
        pass

    def finish(self, here, ins, outs, scratch):
        pass


def run_tasks(ids, *tasks):
    reach = []
    for task in tasks:
        reach += [way for way in task.reach if way not in reach]

    near = []
    for task in tasks:
        near += [space == pltpu.VMEM for space in task.spaces]
    arrays = [array for task in tasks for array in task.arrays]
    loaded = [i for i, each in enumerate(near) if each]

    def kernel(*refs):
        refs = list(refs)
        *refs, load_sem = refs
        held = refs[len(refs) - len(loaded) :]
        refs = refs[: len(refs) - len(loaded)]
        loads = []
        for slot, index in enumerate(loaded):
            loads.append(pltpu.make_async_copy(refs[index], held[slot], load_sem.at[slot]))
            loads[-1].start()
            refs[index] = held[slot]
        views = [[], [], []]
        for kind, name in enumerate(("arrays", "outs", "scratch")):
            for task in tasks:
                count = len(getattr(task, name))
                views[kind].append(refs[:count])
                refs = refs[count:]
        here = Here()
        barrier = pltpu.get_barrier_semaphore()
        for way in reach:
            pl.semaphore_signal(barrier, inc=1, device_id=here.peer(*way), device_id_type=MESH_ID)
        pl.semaphore_wait(barrier, len(reach))
        for each in loads:
            each.wait()
        for task, *held in zip(tasks, *views):
            task.start(here, *held)

        def moment(name):
            for task, *held in zip(tasks, *views):
                task.at_moment(name, here, *held)

        tasks[0].moment = moment
        for task, *held in zip(tasks, *views):
            task.finish(here, *held)

    results = pl.pallas_call(
        kernel,
        out_shape=[out for task in tasks for out in task.outs],
        in_specs=[pl.BlockSpec(memory_space=pltpu.HBM)] * len(arrays),
        out_specs=[pl.BlockSpec(memory_space=s) for task in tasks for s in task.out_spaces],
        scratch_shapes=[each for task in tasks for each in task.scratch]
        + [pltpu.VMEM(arrays[i].shape, arrays[i].dtype) for i in loaded]
        + [dma_sems(len(loaded))],
        compiler_params=vmem_params(next(ids), 60),
    )(*arrays)
    results = list(results)
    split = []
    for task in tasks:
        split.append(results[: len(task.outs)])
        results = results[len(task.outs) :]
    return split


class PlaneMove(Task):
    def __init__(self, values, back=False, when="midway"):
        self.back, self.when = back, when
        self.arrays, self.spaces = (values,), (pltpu.HBM,)
        self.outs = (jax.ShapeDtypeStruct(values.shape, values.dtype),)
        self.out_spaces = (pltpu.HBM,)
        self.scratch = (
            pltpu.VMEM(values.shape, values.dtype),
            dma_sems(3),
            dma_sems(2),
        )
        self.reach = (BY_Y,) + BY_LINE

    def bend(self, here):
        return lax.rem(here.z + here.core, 2) == here.y

    def ends(self, here):
        targets = [{"core": here.z // 2, "z": 2 * y + here.core} for y in range(2)]
        at_home = [(here.z // 2 == here.core) & (2 * y + here.core == here.z) for y in range(2)]
        origin_core = lax.rem(here.z, 2)
        origin_z = 2 * here.core + lax.rem(here.y + origin_core, 2)
        origin_home = (origin_core == here.core) & (origin_z == here.z)
        return targets, at_home, {"core": origin_core, "z": origin_z}, origin_home

    def plan(self, here, ins, outs, scratch):
        held, send, recv = scratch
        targets, at_home, origin, origin_home = self.ends(here)
        bend = self.bend(here)
        away_from = jnp.logical_not
        to_y = here.peer(*BY_Y)
        first, second = [], []
        if not self.back:
            over = remote(ins[0], held, send.at[2], recv.at[0], to_y)
            first.append((away_from(bend), over, True))
            for y in range(2):
                for legs, source, when in (
                    (first, ins[0], bend & (here.y == y)),
                    (second, held, bend & (here.y != y)),
                ):
                    away = remote(source, outs[0], send.at[y], recv.at[1], targets[y])
                    stay = pltpu.make_async_copy(source, outs[0], recv.at[1])
                    legs.append((when & away_from(at_home[y]), away, True))
                    legs.append((when & at_home[y], stay, False))
        else:
            ends_there = here.z // 2 == here.y
            for goes_on, target, slot in ((False, outs[0], 1), (True, held, 0)):
                when = away_from(ends_there) if goes_on else ends_there
                away = remote(ins[0], target, send.at[int(goes_on)], recv.at[slot], origin)
                stay = pltpu.make_async_copy(ins[0], target, recv.at[slot])
                first.append((when & away_from(origin_home), away, True))
                first.append((when & origin_home, stay, False))
            over = remote(held, outs[0], send.at[2], recv.at[1], to_y)
            second.append((bend, over, True))
        return first, second

    def start(self, here, ins, outs, scratch):
        for when, copy, _ in self.plan(here, ins, outs, scratch)[0]:
            pl.when(when)(copy.start)

    def at_moment(self, name, here, ins, outs, scratch):
        if name == self.when:
            held, _, recv = scratch

            @pl.when(self.bend(here))
            def _():
                pltpu.make_async_copy(held, held, recv.at[0]).wait()

            for when, copy, _ in self.plan(here, ins, outs, scratch)[1]:
                pl.when(when)(copy.start)

    def finish(self, here, ins, outs, scratch):
        self.at_moment("end", here, ins, outs, scratch)
        pltpu.make_async_copy(outs[0], outs[0], scratch[2].at[1]).wait()
        for legs in self.plan(here, ins, outs, scratch):
            for when, copy, is_remote in legs:
                if is_remote:
                    pl.when(when)(copy.wait_send)


class PlaneGather(Task):
    def __init__(self, block):
        rows, width = block.shape
        self.arrays, self.spaces = (block,), (pltpu.VMEM,)
        self.outs = (jax.ShapeDtypeStruct((8 * rows, width), block.dtype),)
        self.out_spaces = (pltpu.VMEM,)
        self.scratch = (dma_sems(11), dma_sems(11), pltpu.SemaphoreType.DMA)
        self.reach = (BY_X, BY_Y, BY_CORE)

    def place(self, here, o_ref, at_x, at_y, part=None):
        rows = o_ref.shape[0] // 8
        first = here.block(here.core, at_x, at_y) * rows
        if part is None:
            return o_ref.at[pl.ds(pl.multiple_of(first, rows), rows)]
        half = rows // 2
        return o_ref.at[pl.ds(pl.multiple_of(first + part * half, half), half)]

    def copies(self, here, x_ref, o_ref, send_sem, recv_sem):
        x, y = here.x, here.y
        half = x_ref.shape[0] // 2
        to_x, to_y, to_core = here.peer(*BY_X), here.peer(*BY_Y), here.peer(*BY_CORE)

        def copy(index, source, target, way):
            return remote(source, target, send_sem.at[index], recv_sem.at[index], way)

        def pass_on(index, way, *at):
            return copy(index, self.place(here, o_ref, *at), self.place(here, o_ref, *at), way)

        own = [self.place(here, o_ref, x, y, part) for part in (0, 1)]
        mine = [x_ref.at[pl.ds(part * half, half)] for part in (0, 1)]
        return [
            copy(0, mine[0], own[0], to_x),
            copy(1, mine[1], own[1], to_y),
            copy(2, mine[1], own[1], to_x),
            copy(3, mine[0], own[0], to_y),
            copy(4, x_ref, self.place(here, o_ref, x, y), to_core),
            pass_on(5, to_y, 1 - x, y, 0),
            pass_on(6, to_x, x, 1 - y, 1),
            pass_on(7, to_core, 1 - x, y),
            pass_on(8, to_core, x, 1 - y),
            pass_on(9, to_core, 1 - x, 1 - y, 0),
            pass_on(10, to_core, 1 - x, 1 - y, 1),
        ]

    def keep(self, here, x_ref, o_ref, own_sem):
        return pltpu.make_async_copy(x_ref, self.place(here, o_ref, here.x, here.y), own_sem)

    def start(self, here, ins, outs, scratch):
        copies = self.copies(here, ins[0], outs[0], scratch[0], scratch[1])
        for index in range(5):
            copies[index].start()
        self.keep(here, ins[0], outs[0], scratch[2]).start()

    def finish(self, here, ins, outs, scratch, work=None, soon=None):
        rows = ins[0].shape[0]
        copies = self.copies(here, ins[0], outs[0], scratch[0], scratch[1])

        def done(flip_core, flip_x, flip_y):
            if work is not None:
                at_core = 1 - here.core if flip_core else here.core
                at_x = 1 - here.x if flip_x else here.x
                at_y = 1 - here.y if flip_y else here.y
                work(pl.multiple_of(here.block(at_core, at_x, at_y) * rows, rows))

        self.keep(here, ins[0], outs[0], scratch[2]).wait()
        done(0, 0, 0)
        copies[4].wait_recv()
        done(1, 0, 0)
        for index in range(4):
            copies[index].wait_recv()
            copies[5 + index].start()
        done(0, 1, 0)
        done(0, 0, 1)
        copies[7].wait_recv()
        done(1, 1, 0)
        copies[8].wait_recv()
        done(1, 0, 1)
        copies[5].wait_recv()
        copies[9].start()
        copies[6].wait_recv()
        copies[10].start()
        done(0, 1, 1)
        if soon is not None:
            soon()
        copies[9].wait_recv()
        copies[10].wait_recv()
        done(1, 1, 1)
        for each in copies:
            each.wait_send()


class PlaneScatter(Task):
    def __init__(self, rows, width, weight_dim):
        half = rows // 2
        self.weight_dim = weight_dim
        self.scratch = (
            pltpu.VMEM((4, rows, width), bf16),
            pltpu.VMEM((4, rows, width), bf16),
            pltpu.VMEM((rows, width), bf16),
            pltpu.VMEM((2, half, width), bf16),
            pltpu.VMEM((2, half, width), bf16),
            pltpu.VMEM((2, half, width), bf16),
            pltpu.VMEM((2, half, width), bf16),
            pltpu.VMEM((2, half, width), bf16),
            pltpu.VMEM((half, width), f32),
            pltpu.VMEM((half, width), f32),
            dma_sems(10),
            dma_sems(10),
        )
        self.reach = (BY_X, BY_Y, BY_CORE)

    def finish(self, here, ins, outs, scratch, rows_of, weight_of, early=None, idle=None):
        o_ref = outs[0]
        (
            sib_out,
            sib_in,
            diag_out,
            diag_in,
            last_x_out,
            last_y_out,
            last_x_in,
            last_y_in,
            wait_x,
            wait_y,
            send_sem,
            recv_sem,
        ) = scratch
        rows = o_ref.shape[0]
        half = rows // 2
        x, y, core = here.x, here.y, here.core
        to_x, to_y, to_core = here.peer(*BY_X), here.peer(*BY_Y), here.peer(*BY_CORE)

        def term(at_core, at_x, at_y):
            first = pl.multiple_of(here.block(at_core, at_x, at_y) * rows, rows)
            return lax.dot_general(
                rows_of(first),
                weight_of(),
                (((1,), (self.weight_dim,)), ((), ())),
                preferred_element_type=f32,
            )

        def copy(index, source, target, way):
            return remote(source, target, send_sem.at[index], recv_sem.at[index], way)

        places = ((1 - x, 1 - y), (1 - x, y), (x, 1 - y), (x, y))
        siblings = [copy(i, sib_out.at[i], sib_in.at[i], to_core) for i in range(4)]

        def help_sibling(i):
            sib_out[i] = term(1 - core, *places[i]).astype(bf16)
            siblings[i].start()

        def joined(i):
            mine = term(core, *places[i])
            siblings[i].wait_recv()
            return mine + sib_in[i].astype(f32)

        help_sibling(0)
        total = joined(0)
        diag_out[...] = total.astype(bf16)
        diag_x = copy(4, diag_out.at[pl.ds(0, half)], diag_in.at[0], to_x)
        diag_y = copy(5, diag_out.at[pl.ds(half, half)], diag_in.at[1], to_y)
        diag_x.start()
        diag_y.start()
        help_sibling(1)
        total = joined(1)
        last_x_out[0] = total[:half].astype(bf16)
        x_0 = copy(6, last_x_out.at[0], last_x_in.at[0], to_x)
        x_0.start()
        wait_x[...] = total[half:]
        if early is not None:
            early()
        help_sibling(2)
        total = joined(2)
        last_y_out[1] = total[half:].astype(bf16)
        y_1 = copy(7, last_y_out.at[1], last_y_in.at[1], to_y)
        y_1.start()
        wait_y[...] = total[:half]
        help_sibling(3)
        diag_y.wait_recv()
        last_x_out[1] = (wait_x[...] + diag_in[1].astype(f32)).astype(bf16)
        x_1 = copy(8, last_x_out.at[1], last_x_in.at[1], to_x)
        x_1.start()
        diag_x.wait_recv()
        last_y_out[0] = (wait_y[...] + diag_in[0].astype(f32)).astype(bf16)
        y_0 = copy(9, last_y_out.at[0], last_y_in.at[0], to_y)
        y_0.start()
        o_ref[...] = joined(3)
        if idle is not None:
            idle()
        for part, (by_x, by_y) in enumerate(((x_0, y_0), (x_1, y_1))):
            by_x.wait_recv()
            by_y.wait_recv()
            piece = pl.ds(part * half, half)
            o_ref[piece, :] += last_x_in[part].astype(f32) + last_y_in[part].astype(f32)
        for sent in (*siblings, diag_x, diag_y, x_0, y_1, x_1, y_0):
            sent.wait_send()


class PlaneSum(Task):
    def __init__(self, values):
        self.arrays, self.spaces = (values,), (pltpu.VMEM,)
        self.outs = (jax.ShapeDtypeStruct(values.shape, f32),)
        self.out_spaces = (pltpu.VMEM,)
        self.scratch = (pltpu.VMEM((7, *values.shape), f32), dma_sems(7), dma_sems(7))
        self.reach = BY_PLANE

    def copies(self, here, ins, scratch):
        got, send_sem, recv_sem = scratch
        return [
            remote(ins[0], got.at[i], send_sem.at[i], recv_sem.at[i], here.peer(*way))
            for i, way in enumerate(BY_PLANE)
        ]

    def start(self, here, ins, outs, scratch):
        for each in self.copies(here, ins, scratch):
            each.start()

    def finish(self, here, ins, outs, scratch):
        copies = self.copies(here, ins, scratch)
        for each in copies:
            each.wait_recv()
        got = scratch[0]
        by_x = [ins[0][...] + got[0]]
        for flip in (2, 4, 6):
            by_x.append(got[flip - 1] + got[flip])
        outs[0][...] = (by_x[0] + by_x[1]) + (by_x[2] + by_x[3])
        for each in copies:
            each.wait_send()


class LineGather(Task):
    def __init__(self, values):
        self.arrays, self.spaces = (values,), (pltpu.HBM,)
        self.outs = (jax.ShapeDtypeStruct((4, *values.shape), values.dtype),)
        self.out_spaces = (pltpu.HBM,)
        self.scratch = (dma_sems(4), dma_sems(3))
        self.reach = BY_Z

    def copies(self, here, ins, outs, scratch):
        target = outs[0].at[here.z]
        keep = pltpu.make_async_copy(ins[0], target, scratch[0].at[3])
        return keep, [
            remote(ins[0], target, scratch[0].at[i], scratch[1].at[i], here.peer(*way))
            for i, way in enumerate(BY_Z)
        ]

    def start(self, here, ins, outs, scratch):
        keep, copies = self.copies(here, ins, outs, scratch)
        for each in copies:
            each.start()
        keep.start()

    def finish(self, here, ins, outs, scratch):
        keep, copies = self.copies(here, ins, outs, scratch)
        for each in copies:
            each.wait()
        keep.wait()


class HeadGather(Task):
    def __init__(self, qkv, out, layer, when="start"):
        _, kinds, both, width = qkv.shape
        self.layer, self.when = layer, when
        self.arrays, self.spaces = (qkv, out), (pltpu.HBM,) * 2
        self.outs = (jax.ShapeDtypeStruct((kinds + 1, 2, both // 2, width), qkv.dtype),)
        self.out_spaces = (pltpu.HBM,)
        self.scratch = (dma_sems(8), dma_sems(8))
        self.reach = BY_LINE

    def pieces(self, outs, shard, part):
        half = outs[0].shape[3] // 2
        columns = pl.ds(pl.multiple_of(part * half, half), half)
        return outs[0].at[pl.ds(0, 3), shard, :, columns], outs[0].at[3, shard, :, columns]

    def copies(self, here, ins, outs, scratch):
        shard, target_core = lax.rem(here.z, 2), here.z // 2
        wide, half = outs[0].shape[2], outs[0].shape[3] // 2
        rows = pl.ds(pl.multiple_of(here.y * wide, wide), wide)
        columns = pl.ds(pl.multiple_of(here.core * half, half), half)
        sources = (ins[0].at[self.layer, :, rows, columns], ins[1].at[self.layer, rows, columns])
        targets = self.pieces(outs, shard, here.core)
        keeps, aways = [], []
        for kind in range(2):
            recv_sem = scratch[1].at[4 * kind + 2 * shard + here.core]
            keeps.append(pltpu.make_async_copy(sources[kind], targets[kind], recv_sem))
            for step in range(4):
                place = {"core": target_core, "z": lax.rem(here.z + step, 4)}
                send_sem = scratch[0].at[4 * kind + step]
                aways.append(remote(sources[kind], targets[kind], send_sem, recv_sem, place))
        return keeps, aways

    def begin(self, here, ins, outs, scratch):
        keeps, aways = self.copies(here, ins, outs, scratch)
        for index, each in enumerate(aways):
            if index % 4:
                each.start()
        at_home = here.z // 2 == here.core
        for kind in range(2):
            pl.when(at_home)(keeps[kind].start)
            pl.when(jnp.logical_not(at_home))(aways[4 * kind].start)

    def start(self, *held):
        self.at_moment("start", *held)

    def at_moment(self, name, *held):
        if name == self.when:
            self.begin(*held)

    def arrive(self, kind, outs, scratch):
        for shard in range(2):
            for part in range(2):
                piece = self.pieces(outs, shard, part)[kind]
                recv_sem = scratch[1].at[4 * kind + 2 * shard + part]
                pltpu.make_async_copy(piece, piece, recv_sem).wait()

    def sent(self, here, ins, outs, scratch):
        keeps, aways = self.copies(here, ins, outs, scratch)
        for index, each in enumerate(aways):
            if index % 4:
                each.wait_send()
        for kind in range(2):
            pl.when(here.z // 2 != here.core)(aways[4 * kind].wait_send)

    def finish(self, here, ins, outs, scratch):
        for kind in range(2):
            self.arrive(kind, outs, scratch)
        self.sent(here, ins, outs, scratch)


class LineScatter(Task):
    def __init__(self, values):
        shape = values.shape[1:]
        self.arrays, self.spaces = (values,), (pltpu.VMEM,)
        self.outs, self.out_spaces = (jax.ShapeDtypeStruct(shape, values.dtype),), (pltpu.VMEM,)
        self.scratch = (pltpu.VMEM((3, *shape), values.dtype), dma_sems(3), dma_sems(3))
        self.reach = BY_Z

    def copies(self, here, ins, scratch):
        got, send_sem, recv_sem = scratch
        return [
            remote(
                ins[0].at[lax.rem(here.z + i + 1, 4)],
                got.at[i],
                send_sem.at[i],
                recv_sem.at[i],
                here.peer(*way),
            )
            for i, way in enumerate(BY_Z)
        ]

    def start(self, here, ins, outs, scratch):
        for each in self.copies(here, ins, scratch):
            each.start()

    def finish(self, here, ins, outs, scratch):
        copies = self.copies(here, ins, scratch)
        for each in copies:
            each.wait_recv()
        total = ins[0][here.z].astype(f32)
        for i in range(3):
            total = total + scratch[0][i].astype(f32)
        outs[0][...] = total.astype(outs[0].dtype)
        for each in copies:
            each.wait_send()


class HeadScatter(Task):
    def __init__(self, values):
        kinds, _, wide, width = values.shape
        shape = (kinds, wide, width // 2)
        self.arrays, self.spaces = (values,), (pltpu.VMEM,)
        self.outs, self.out_spaces = (jax.ShapeDtypeStruct(shape, values.dtype),), (pltpu.VMEM,)
        self.scratch = (pltpu.VMEM((4, *shape), values.dtype), dma_sems(4), dma_sems(4))
        self.reach = BY_LINE

    def copies(self, here, ins, scratch):
        got, send_sem, recv_sem = scratch
        half = ins[0].shape[3] // 2
        triples = []
        for shard in range(2):
            for part in range(2):
                source = ins[0].at[:, shard, :, pl.ds(part * half, half)]
                target_z = 2 * here.core + shard
                slot = recv_sem.at[here.z]
                away = remote(
                    source,
                    got.at[here.z],
                    send_sem.at[2 * shard + part],
                    slot,
                    {"core": part, "z": target_z},
                )
                stay = pltpu.make_async_copy(source, got.at[here.z], slot)
                at_home = (target_z == here.z) & (here.core == part)
                triples.append((away, stay, at_home))
        return triples

    def start(self, here, ins, outs, scratch):
        for away, stay, at_home in self.copies(here, ins, scratch):
            pl.when(at_home)(stay.start)
            pl.when(jnp.logical_not(at_home))(away.start)

    def finish(self, here, ins, outs, scratch):
        got, send_sem, recv_sem = scratch
        for plane in range(4):
            pltpu.make_async_copy(got.at[plane], got.at[plane], recv_sem.at[plane]).wait()
        total = got[0].astype(f32)
        for plane in range(1, 4):
            total = total + got[plane].astype(f32)
        outs[0][...] = total.astype(outs[0].dtype)
        for away, stay, at_home in self.copies(here, ins, scratch):
            pl.when(jnp.logical_not(at_home))(away.wait_send)


class RowsGather(Task):
    def __init__(self, values, when="start"):
        self.when = when
        self.arrays, self.spaces = (values,), (pltpu.HBM,)
        self.outs = (jax.ShapeDtypeStruct((4, *values.shape), values.dtype),)
        self.out_spaces = (pltpu.HBM,)
        self.scratch = (dma_sems(4), dma_sems(3))
        self.reach = (BY_Y, BY_CORE)

    def copies(self, here, ins, outs, scratch):
        send_sem, recv_sem = scratch
        own = outs[0].at[2 * here.y + here.core]
        over = outs[0].at[2 * (1 - here.y) + here.core]
        to_y, to_core = here.peer(*BY_Y), here.peer(*BY_CORE)
        return (
            pltpu.make_async_copy(ins[0], own, send_sem.at[3]),
            remote(ins[0], own, send_sem.at[0], recv_sem.at[0], to_y),
            remote(ins[0], own, send_sem.at[1], recv_sem.at[1], to_core),
            remote(over, over, send_sem.at[2], recv_sem.at[2], to_core),
        )

    def start(self, *held):
        self.at_moment("start", *held)

    def at_moment(self, name, *held):
        if name == self.when:
            self.begin(*held)

    def begin(self, here, ins, outs, scratch):
        keep, by_y, by_core, again = self.copies(here, ins, outs, scratch)
        by_y.start()
        by_core.start()
        keep.start()

    def finish(self, here, ins, outs, scratch):
        keep, by_y, by_core, again = self.copies(here, ins, outs, scratch)
        by_y.wait_recv()
        again.start()
        by_core.wait_recv()
        again.wait_recv()
        for each in (by_y, by_core, again):
            each.wait_send()
        keep.wait()


class StepSum(Task):
    def __init__(self, values):
        self.arrays, self.spaces = (values,), (pltpu.VMEM,)
        self.outs = (jax.ShapeDtypeStruct(values.shape, f32),)
        self.out_spaces = (pltpu.VMEM,)
        self.scratch = (
            pltpu.VMEM((2, *values.shape), f32),
            pltpu.VMEM((3, *values.shape), f32),
            dma_sems(3),
            dma_sems(3),
        )
        self.reach = (BY_X, BY_Y, BY_CORE)

    def leg(self, here, index, source, scratch):
        _, got, send_sem, recv_sem = scratch
        way = here.peer(*self.reach[index])
        return remote(source, got.at[index], send_sem.at[index], recv_sem.at[index], way)

    def start(self, here, ins, outs, scratch):
        self.leg(here, 0, ins[0], scratch).start()

    def at_moment(self, name, here, ins, outs, scratch):
        part, got = scratch[:2]
        if name == "midway":
            self.leg(here, 0, ins[0], scratch).wait()
            part[0] = ins[0][...] + got[0]
            self.leg(here, 1, part.at[0], scratch).start()
        if name == "closing":
            self.leg(here, 1, part.at[0], scratch).wait()
            part[1] = part[0] + got[1]
            self.leg(here, 2, part.at[1], scratch).start()

    def finish(self, here, ins, outs, scratch):
        part, got = scratch[:2]
        self.leg(here, 2, part.at[1], scratch).wait()
        outs[0][...] = part[1] + got[2]


class LineSum(Task):
    def __init__(self, values):
        self.arrays, self.spaces = (values,), (pltpu.VMEM,)
        self.outs = (jax.ShapeDtypeStruct(values.shape, f32),)
        self.out_spaces = (pltpu.VMEM,)
        self.scratch = (pltpu.VMEM((4, *values.shape), f32), dma_sems(3), dma_sems(4))
        self.reach = BY_Z

    def copies(self, here, ins, scratch):
        got, send_sem, recv_sem = scratch
        there, slot = got.at[here.z], recv_sem.at[here.z]
        keep = pltpu.make_async_copy(ins[0], there, slot)
        return keep, [
            remote(ins[0], there, send_sem.at[i], slot, here.peer(*way))
            for i, way in enumerate(BY_Z)
        ]

    def start(self, here, ins, outs, scratch):
        keep, copies = self.copies(here, ins, scratch)
        for each in copies:
            each.start()
        keep.start()

    def finish(self, here, ins, outs, scratch):
        got, _, recv_sem = scratch
        _, copies = self.copies(here, ins, scratch)
        for plane in range(4):
            pltpu.make_async_copy(got.at[plane], got.at[plane], recv_sem.at[plane]).wait()
        outs[0][...] = (got[0] + got[1]) + (got[2] + got[3])
        for each in copies:
            each.wait_send()


def to_columns(upper, lower):
    place = lax.broadcasted_iota(jnp.int32, (128, upper.shape[1]), 0)
    return jnp.transpose(jnp.where(place < 64, upper, lower))


def both_columns(upper, lower):
    lane = lax.broadcasted_iota(jnp.int32, (upper.shape[0], 128), 1)
    return jnp.where(lane < 64, upper, lower)


def in_chunks(rows, chunk, step):
    def one(index, carry):
        step(pl.multiple_of(index * chunk, chunk))
        return carry

    lax.fori_loop(0, rows // chunk, one, 0)


def fold(values):
    total = values[:8]
    for first in range(8, values.shape[0], 8):
        total = total + values[first : first + 8]
    return total


class Parts(Task):
    def use(self, **parts):
        self.parts = parts
        self.scratch = list(self.scratch)
        self.at = {}
        reach = []
        for name, part in parts.items():
            self.at[name] = (len(self.scratch), len(self.scratch) + len(part.scratch))
            self.scratch += list(part.scratch)
            reach += [way for way in part.reach if way not in reach]
        self.reach = reach

    def held(self, scratch, name):
        first, last = self.at[name]
        return scratch[first:last]


def norm_pull(grad_out, normal, factor, gain_row):
    scaled = grad_out * gain_row
    width = scaled.shape[1]
    mean = jnp.sum(scaled, axis=1, keepdims=True) / width
    inner = jnp.sum(scaled * normal, axis=1, keepdims=True) / width
    return factor * (scaled - mean - normal * inner)


class StepThenLine(Parts):
    def __init__(self, values):
        self.arrays, self.spaces = (values,), (pltpu.VMEM,)
        self.outs = (jax.ShapeDtypeStruct(values.shape, f32),)
        self.out_spaces = (pltpu.VMEM,)
        self.scratch = (pltpu.VMEM(values.shape, f32),)
        self.use(step=StepSum(values), line=LineSum(values))

    def start(self, here, ins, outs, scratch):
        self.parts["step"].start(here, ins, scratch[:1], self.held(scratch, "step"))

    def at_moment(self, name, here, ins, outs, scratch):
        held = (here, ins, scratch[:1], self.held(scratch, "step"))
        self.parts["step"].at_moment(name, *held)
        if name == "tail":
            self.parts["step"].finish(*held)
            self.parts["line"].start(here, scratch[:1], outs, self.held(scratch, "line"))

    def finish(self, here, ins, outs, scratch):
        self.parts["line"].finish(here, scratch[:1], outs, self.held(scratch, "line"))


def normalize(values):
    width = values.shape[1]
    centered = values - jnp.sum(values, axis=1, keepdims=True) / width
    factor = lax.rsqrt(jnp.sum(centered * centered, axis=1, keepdims=True) / width + epsilon)
    return centered * factor, factor


def wide_column(column):
    return jnp.broadcast_to(column, (column.shape[0], 128))


def hidden_row(small_ref, layer, at, part):
    first = small_ref.shape[2] - (3 - at) * part
    return jnp.concatenate(
        [small_ref[z, layer : layer + 1, first : first + part] for z in range(4)], axis=1
    )


def scale_of(here, head_scale_ref, layer, wide):
    row = head_scale_ref[layer : layer + 1, :]
    place = lax.broadcasted_iota(jnp.int32, row.shape, 1)
    pair = []
    for i in range(2):
        head = ((2 * here.core + i) * 2 + here.x) * 2 + here.y
        pair.append(jnp.sum(jnp.where(place == head, row, 0.0), axis=1, keepdims=True))
    lane = lax.broadcasted_iota(jnp.int32, (1, 2 * wide), 1)
    return jnp.where(lane < wide, pair[0], pair[1])


NARROW = 128
CHUNK = 256


class FfnForward(Parts):
    def __init__(self, block, first, second, small, middle, shift, norm, layer, late):
        rows, width = block.shape
        hidden = first.shape[1]
        self.late, self.layer, self.last = late, layer, norm is None
        self.arrays = (block, first, second, small, middle, shift, *(norm or ()))
        self.spaces = (pltpu.VMEM,) * 2 + (pltpu.HBM if late else pltpu.VMEM,)
        self.spaces += (pltpu.VMEM,) * (len(self.arrays) - 3)
        self.outs = (
            jax.ShapeDtypeStruct((rows, width), f32),
            jax.ShapeDtypeStruct((8 * rows, width), bf16),
            jax.ShapeDtypeStruct((8 * rows, hidden), f32),
            jax.ShapeDtypeStruct((8 * rows, hidden), f32),
            jax.ShapeDtypeStruct((8 * rows, hidden), bf16),
            jax.ShapeDtypeStruct((2, 8 * rows), f32),
        )
        self.out_spaces = (pltpu.VMEM,) + (pltpu.HBM,) * 4 + (pltpu.VMEM,)
        self.outs += (jax.ShapeDtypeStruct((rows, width), bf16),)
        if norm:
            self.outs += (jax.ShapeDtypeStruct((rows, width), f32),)
            self.outs += (jax.ShapeDtypeStruct((rows, 128), f32),)
        self.out_spaces += (pltpu.VMEM,) * (len(self.outs) - 6)
        self.base = len(self.outs)
        self.scratch = (
            pltpu.VMEM((8 * rows, width), bf16),
            pltpu.VMEM((8 * rows, hidden), f32),
            pltpu.VMEM((8 * rows, hidden), f32),
            pltpu.VMEM((8 * rows, hidden), bf16),
            pltpu.VMEM((2, 8 * rows), f32),
            pltpu.VMEM((rows, 128), f32),
            dma_sems(4),
        )
        parts = dict(
            gather=PlaneGather(block),
            scatter=PlaneScatter(rows, width, 0),
            sums=PlaneSum(jax.ShapeDtypeStruct((2, 8 * rows), f32)),
        )
        if late:
            parts["second"] = WeightGather(second, layer, 0)
            self.outs += parts["second"].outs
            self.out_spaces += (pltpu.VMEM,)
        self.use(**parts)

    def start(self, here, ins, outs, scratch):
        self.parts["gather"].start(here, ins[:1], scratch[:1], self.held(scratch, "gather"))
        if self.late:
            held = self.held(scratch, "second")
            self.parts["second"].start(here, ins[2:3], outs[self.base :], held)

    def finish(self, here, ins, outs, scratch):
        block_ref, first_ref, second_ref, small_ref, middle_ref, row_ref = ins[:6]
        part = first_ref.shape[1] // 4
        shift, gain, bias = (hidden_row(small_ref, self.layer, at, part) for at in range(3))
        out_ref, rows_out, slope_out, normal_out, mixed_out, total_ref = outs[:6]
        if self.late:
            second_ref = outs[self.base]
        rows_buf, before, active, mixed, sums, columns, save = scratch[:7]
        rows = block_ref.shape[0]
        hidden_all = 8 * first_ref.shape[1]

        def work(first):
            before[pl.ds(first, rows), :] = lax.dot_general(
                rows_buf[pl.ds(first, rows), :],
                first_ref[...],
                (((1,), (0,)), ((), ())),
                preferred_element_type=f32,
            )

            def step(at):
                piece = pl.ds(pl.multiple_of(first + at, CHUNK), CHUNK)
                u = before[piece, :] + shift
                area = 0.5 * (1.0 + lax.erf(u * 0.5**0.5))
                a = u * area
                active[piece, :] = a
                before[piece, :] = area + u * (jnp.exp(-0.5 * u * u) * (0.5 / jnp.pi) ** 0.5)
                columns[pl.ds(at, CHUNK), :] = both_columns(
                    jnp.sum(a, axis=1, keepdims=True), jnp.sum(a * a, axis=1, keepdims=True)
                )

            in_chunks(rows, CHUNK, step)
            turned = jnp.transpose(columns[...])
            sums[0:1, pl.ds(first, rows)] = turned[0:1]
            sums[1:2, pl.ds(first, rows)] = turned[64:65]

        self.parts["gather"].finish(
            here, ins[:1], scratch[:1], self.held(scratch, "gather"), work
        )
        held = self.held(scratch, "sums")
        self.parts["sums"].start(here, (sums,), None, held)
        keep_rows = pltpu.make_async_copy(rows_buf, rows_out, save.at[0])
        keep_rows.start()
        keep_slope = pltpu.make_async_copy(before, slope_out, save.at[1])
        keep_slope.start()
        self.parts["sums"].finish(here, (sums,), (total_ref,), held)
        if self.late:
            held = self.held(scratch, "second")
            self.parts["second"].finish(here, ins[2:3], outs[self.base :], held)
        self.moment("midway")

        def rows_of(first):
            average = total_ref[0:1, pl.ds(first, rows)] / hidden_all
            spread = total_ref[1:2, pl.ds(first, rows)] / hidden_all - average * average
            columns[...] = to_columns(average, lax.rsqrt(spread + epsilon))

            def step(at):
                piece = pl.ds(pl.multiple_of(first + at, CHUNK), CHUNK)
                pair = columns[pl.ds(at, CHUNK), :]
                normal = (active[piece, :] - pair[:, 0:1]) * pair[:, 64:65]
                active[piece, :] = normal
                mixed[piece, :] = (normal * gain + bias).astype(bf16)

            in_chunks(rows, CHUNK, step)
            return mixed[pl.ds(first, rows), :]

        keep_mixed = pltpu.make_async_copy(mixed, mixed_out, save.at[2])
        keep_normal = pltpu.make_async_copy(active, normal_out, save.at[3])

        def idle():
            keep_mixed.start()
            keep_normal.start()
            self.moment("closing")

        self.parts["scatter"].finish(
            here,
            None,
            (out_ref,),
            self.held(scratch, "scatter"),
            rows_of,
            lambda: second_ref[...],
            idle=idle,
        )
        layer = slice(self.layer, self.layer + 1)
        after = slice(self.layer + 1, self.layer + 2)

        def settle(at):
            piece = pl.ds(at, NARROW)
            residual = middle_ref[piece, :] + out_ref[piece, :] + row_ref[layer, :]
            out_ref[piece, :] = residual
            if self.last:
                outs[6][piece, :] = residual.astype(bf16)
            else:
                normal, factor = normalize(residual)
                outs[6][piece, :] = (normal * ins[6][after, :] + ins[7][after, :]).astype(bf16)
                outs[7][piece, :] = normal
                outs[8][piece, :] = wide_column(factor)

        in_chunks(rows, NARROW, settle)
        for each in (keep_rows, keep_slope, keep_mixed, keep_normal):
            each.wait()


class FfnBackward(Parts):
    def __init__(
        self,
        block,
        first,
        second,
        small,
        slope,
        normal,
        mixed,
        ffn_rows,
        totals,
        gradient,
        norms,
        layer,
    ):
        self.layer = layer
        rows, width = block.shape
        hidden = second.shape[0]
        self.arrays = (block, first, second, small, totals, slope, normal, mixed, ffn_rows)
        self.spaces = (pltpu.VMEM,) * 5 + (pltpu.HBM,) * 4
        self.arrays += (gradient, *norms)
        self.spaces += (pltpu.VMEM,) * 7
        self.outs = (
            jax.ShapeDtypeStruct((rows, width), f32),
            jax.ShapeDtypeStruct((4, width, hidden // 4), bf16),
            jax.ShapeDtypeStruct((hidden // 4, width), bf16),
            jax.ShapeDtypeStruct((3, hidden), f32),
            jax.ShapeDtypeStruct((rows, width), bf16),
            jax.ShapeDtypeStruct((8, width), f32),
        )
        self.out_spaces = (pltpu.VMEM,) * 6
        self.scratch = (
            pltpu.VMEM((8 * rows, width), bf16),
            pltpu.VMEM((8 * rows, hidden), f32),
            pltpu.VMEM((8 * rows, hidden), f32),
            pltpu.VMEM((8 * rows, hidden), f32),
            pltpu.VMEM((8 * rows, hidden), bf16),
            pltpu.VMEM((8 * rows, width), bf16),
            pltpu.VMEM((8 * rows, hidden), bf16),
            pltpu.VMEM((hidden, width), f32),
            pltpu.VMEM((2, 8 * rows), f32),
            pltpu.VMEM((2, 8 * rows), f32),
            pltpu.VMEM((rows, 128), f32),
            pltpu.VMEM((rows, 128), f32),
            pltpu.VMEM((3, 8, hidden), f32),
            dma_sems(4),
            pltpu.VMEM((4, hidden // 4, width), bf16),
            pltpu.VMEM((6, 8, width), f32),
        )
        self.use(
            gather=PlaneGather(block),
            scatter=PlaneScatter(rows, width, 1),
            second=LineScatter(jax.ShapeDtypeStruct((4, hidden // 4, width), bf16)),
            sums=PlaneSum(jax.ShapeDtypeStruct((2, 8 * rows), f32)),
        )

    def loads(self, ins, scratch):
        targets = (scratch[2], scratch[4], scratch[1], scratch[5])
        return [
            pltpu.make_async_copy(source, target, scratch[13].at[i])
            for i, (source, target) in enumerate(zip((ins[6], ins[7], ins[5], ins[8]), targets))
        ]

    def start(self, here, ins, outs, scratch):
        self.parts["gather"].start(here, ins[:1], scratch[:1], self.held(scratch, "gather"))
        for each in self.loads(ins, scratch):
            each.start()

    def finish(self, here, ins, outs, scratch):
        block_ref, first_ref, second_ref, hidden_ref, totals_ref = ins[:5]
        mid_gain = hidden_row(hidden_ref, self.layer, 1, first_ref.shape[1] // 4)
        out_ref, first_grad, second_quarter, small_ref, branch_ref, vector_ref = outs
        second_grad, vectors = scratch[14:16]
        (
            rows_buf,
            slope,
            normal_buf,
            grads,
            mixed,
            ffn_rows,
            pre_grad,
            second_sum,
            sums,
            got,
            columns,
            factors,
            small,
        ) = scratch[:13]
        rows = block_ref.shape[0]
        hidden_all = 8 * first_ref.shape[1]
        load_normal, load_mixed, load_slope, load_rows = self.loads(ins, scratch)
        load_normal.wait()
        load_mixed.wait()
        second_sum[...] = jnp.zeros_like(second_sum)
        small[...] = jnp.zeros_like(small)

        def factor_columns(first):
            average = totals_ref[0:1, pl.ds(first, rows)] / hidden_all
            spread = totals_ref[1:2, pl.ds(first, rows)] / hidden_all - average * average
            factors[...] = to_columns(average, lax.rsqrt(spread + epsilon))

        def work(first):
            block = pl.ds(first, rows)
            grads[block, :] = lax.dot_general(
                rows_buf[block, :],
                second_ref[...],
                (((1,), (1,)), ((), ())),
                preferred_element_type=f32,
            )
            second_sum[...] += lax.dot_general(
                mixed[block, :],
                rows_buf[block, :],
                (((0,), (0,)), ((), ())),
                preferred_element_type=f32,
            )

            def step(at):
                piece = pl.ds(pl.multiple_of(first + at, CHUNK), CHUNK)
                normal = normal_buf[piece, :]
                grad = grads[piece, :]
                small[0] += fold(grad * normal)
                small[1] += fold(grad)
                scaled = grad * mid_gain
                grads[piece, :] = scaled
                columns[pl.ds(at, CHUNK), :] = both_columns(
                    jnp.sum(scaled, axis=1, keepdims=True),
                    jnp.sum(scaled * normal, axis=1, keepdims=True),
                )

            in_chunks(rows, CHUNK, step)
            turned = jnp.transpose(columns[...])
            sums[0:1, pl.ds(first, rows)] = turned[0:1]
            sums[1:2, pl.ds(first, rows)] = turned[64:65]

        self.parts["gather"].finish(
            here, ins[:1], scratch[:1], self.held(scratch, "gather"), work
        )
        held = self.held(scratch, "sums")
        self.parts["sums"].start(here, (sums,), None, held)
        second_grad[...] = second_sum[...].astype(bf16).reshape(second_grad.shape)
        load_slope.wait()
        self.moment("midway")
        self.parts["second"].start(here, (second_grad,), None, self.held(scratch, "second"))
        self.parts["sums"].finish(here, (sums,), (got,), held)

        def rows_of(first):
            factor_columns(first)
            columns[...] = to_columns(
                got[0:1, pl.ds(first, rows)] / hidden_all,
                got[1:2, pl.ds(first, rows)] / hidden_all,
            )

            def step(at):
                piece = pl.ds(pl.multiple_of(first + at, CHUNK), CHUNK)
                pair = columns[pl.ds(at, CHUNK), :]
                factor = factors[pl.ds(at, CHUNK), :][:, 64:65]
                active_grad = factor * (
                    grads[piece, :] - pair[:, 0:1] - normal_buf[piece, :] * pair[:, 64:65]
                )
                rounded = (active_grad * slope[piece, :]).astype(bf16)
                pre_grad[piece, :] = rounded
                small[2] += fold(rounded.astype(f32))

            in_chunks(rows, CHUNK, step)
            return pre_grad[pl.ds(first, rows), :]

        def idle():
            load_rows.wait()
            whole = lax.dot_general(
                ffn_rows[...],
                pre_grad[...],
                (((0,), (0,)), ((), ())),
                preferred_element_type=f32,
            ).astype(bf16)
            part = first_grad.shape[2]
            for i in range(4):
                first_grad[i] = whole[:, i * part : (i + 1) * part]
            self.moment("closing")

        self.parts["scatter"].finish(
            here,
            None,
            (out_ref,),
            self.held(scratch, "scatter"),
            rows_of,
            lambda: first_ref[...],
            idle=idle,
        )
        gradient_ref, normal_1, factor_1, gain_1, normal_2, factor_2, gain_2 = ins[9:16]
        vectors[...] = jnp.zeros_like(vectors)
        layer = slice(self.layer, self.layer + 1)

        def pull(at):
            piece = pl.ds(at, NARROW)
            grad, gradient = out_ref[piece, :], gradient_ref[piece, :].astype(f32)
            normal = normal_1[piece, :]
            vectors[3] += fold(grad * normal)
            vectors[4] += fold(grad)
            vectors[5] += fold(gradient)
            middle = gradient + norm_pull(
                grad, normal, factor_1[piece, 0:1], gain_1[layer, :]
            )
            out_ref[piece, :] = middle
            normal = normal_2[piece, :]
            vectors[1] += fold(middle * normal)
            vectors[2] += fold(middle)
            branch = norm_pull(middle, normal, factor_2[piece, 0:1], gain_2[layer, :])
            vectors[0] += fold(branch)
            branch_ref[piece, :] = branch.astype(bf16)

        in_chunks(rows, NARROW, pull)
        vector_ref[...] = jnp.zeros_like(vector_ref)
        for i in range(6):
            vector_ref[i : i + 1, :] = jnp.sum(vectors[i], axis=0, keepdims=True)
        held = self.held(scratch, "second")
        self.parts["second"].finish(here, (second_grad,), (second_quarter,), held)
        for i in range(3):
            small_ref[i : i + 1, :] = jnp.sum(small[i], axis=0, keepdims=True)


class WeightGather(Task):
    def __init__(self, weights, layer, axis, when="start"):
        self.layer, self.axis, self.when = layer, axis, when
        self.arrays, self.spaces = (weights,), (pltpu.HBM,)
        self.outs = (jax.ShapeDtypeStruct(weights.shape[1:], weights.dtype),)
        self.out_spaces = (pltpu.HBM,)
        self.scratch = (dma_sems(4), dma_sems(3))
        self.reach = BY_Z

    def copies(self, here, ins, outs, scratch):
        part = outs[0].shape[self.axis] // 4

        def cut(ref, at):
            piece = pl.ds(pl.multiple_of(at * part, part), part)
            return ref.at[piece, :] if self.axis == 0 else ref.at[:, piece]

        source = cut(ins[0].at[self.layer], 2 * here.y + here.core)
        target = cut(outs[0], here.z)
        keep = pltpu.make_async_copy(source, target, scratch[0].at[3])
        return keep, [
            remote(source, target, scratch[0].at[i], scratch[1].at[i], here.peer(*way))
            for i, way in enumerate(BY_Z)
        ]

    def begin(self, here, ins, outs, scratch):
        keep, copies = self.copies(here, ins, outs, scratch)
        for each in copies:
            each.start()
        keep.start()

    def start(self, *held):
        self.at_moment("start", *held)

    def at_moment(self, name, *held):
        if name == self.when:
            self.begin(*held)

    def finish(self, here, ins, outs, scratch):
        keep, copies = self.copies(here, ins, outs, scratch)
        for each in copies:
            each.wait()
        keep.wait()


class ThenRows(Parts):
    def __init__(self, first, when):
        self.when = when
        shape = first.outs[0]
        self.arrays, self.spaces = first.arrays, first.spaces
        rows = RowsGather(shape)
        self.outs, self.out_spaces = rows.outs, rows.out_spaces
        self.scratch = (pltpu.VMEM(shape.shape, shape.dtype),)
        self.use(first=first, rows=rows)

    def start(self, here, ins, outs, scratch):
        self.parts["first"].start(here, ins, None, self.held(scratch, "first"))

    def at_moment(self, name, here, ins, outs, scratch):
        if name == self.when:
            self.parts["first"].finish(here, ins, scratch[:1], self.held(scratch, "first"))
            self.parts["rows"].begin(here, scratch[:1], outs, self.held(scratch, "rows"))

    def finish(self, here, ins, outs, scratch):
        self.at_moment("end", here, ins, outs, scratch)
        self.parts["rows"].finish(here, scratch[:1], outs, self.held(scratch, "rows"))


BLOCK = 256
SPAN = 512


def head_masks(head_width, width):
    lane = lax.broadcasted_iota(jnp.int32, (1, width), 1)
    lower = (lane < head_width).astype(bf16)
    return lower, (1 - lower).astype(bf16)


def by_head(values, head_width):
    lower, upper = head_masks(head_width, values.shape[1])
    return jnp.concatenate([values * lower, values * upper], axis=0)


def from_heads(pair, head_width):
    rows = pair.shape[0] // 2
    lane = lax.broadcasted_iota(jnp.int32, (rows, pair.shape[1]), 1)
    return jnp.where(lane < head_width, pair[:rows], pair[rows:])


def tile_facts(doc_ref, first, key_first, keys):
    docs = doc_ref[:, pl.ds(first, BLOCK)]
    docs = jnp.concatenate([docs, docs], axis=1)
    key_docs = doc_ref[:, pl.ds(pl.multiple_of(key_first, keys), keys)]
    key_docs = jnp.transpose(jnp.broadcast_to(key_docs, (128, keys)))[:, 0:1]
    place = lax.broadcasted_iota(jnp.int32, (keys, 2 * BLOCK), 1)
    place = jnp.where(place >= BLOCK, place - BLOCK, place) + (first - key_first)
    allowed = (docs == key_docs) & (place >= lax.broadcasted_iota(jnp.int32, place.shape, 0))
    return docs, allowed


def attend_block(
    head_width, first, q_ref, k_ref, v_cols, doc_ref, o_ref, l_ref, s_buf, acc, top, total
):
    block = first // BLOCK
    last = first // SPAN
    pair = by_head(q_ref[pl.ds(first, BLOCK), :], head_width)

    def scores(at):
        keys = k_ref[pl.ds(pl.multiple_of(at * SPAN, SPAN), SPAN), :]
        return lax.dot_general(keys, pair, (((1,), (1,)), ((), ())), preferred_element_type=f32)

    top[...] = jnp.full_like(top, masked)

    def first_pass(at, carry):
        s = scores(at)
        s_buf[at] = s
        peak = s[:8]
        for row in range(8, SPAN, 8):
            peak = jnp.maximum(peak, s[row : row + 8])
        top[...] = jnp.maximum(top[...], peak)
        return carry

    lax.fori_loop(0, last, first_pass, 0)
    docs, allowed = tile_facts(doc_ref, first, last * SPAN, SPAN)
    s = jnp.where(allowed, scores(last), masked)
    shift = jnp.where(docs == 0, 0.0, masked)
    peak = jnp.maximum(
        jnp.max(top[...], axis=0, keepdims=True) + shift, jnp.max(s, axis=0, keepdims=True)
    )

    def weigh(at, p):
        values = v_cols[:, pl.ds(pl.multiple_of(at * SPAN, SPAN), SPAN)]
        return jnp.dot(values, p.astype(bf16), preferred_element_type=f32)

    p = jnp.exp(s - peak)
    total[...] = fold(p)
    acc[...] = weigh(last, p)
    base = peak - shift

    def second_pass(at, carry):
        p = jnp.exp(s_buf[at] - base)
        total[...] += fold(p)
        acc[...] += weigh(at, p)
        return carry

    lax.fori_loop(0, last, second_pass, 0)
    sums = jnp.sum(total[...], axis=0, keepdims=True)
    out = from_heads(jnp.transpose(acc[...] / sums), head_width)
    o_ref[pl.ds(first, BLOCK), :] = out
    l_ref[block] = peak + jnp.log(sums)
    return out


def attend_block_back(
    head_width,
    first,
    do,
    q_ref,
    k_ref,
    k_cols,
    v_ref,
    o_ref,
    l_ref,
    doc_ref,
    acc_k,
    acc_v,
    acc_q,
):
    block = first // BLOCK
    rows = pl.ds(first, BLOCK)
    pair_q = by_head(q_ref[rows, :], head_width)
    pair_do = by_head(do, head_width)
    out = o_ref[rows, :]
    inner = jnp.sum(
        jnp.concatenate([out, out], axis=0) * pair_do.astype(f32), axis=1, keepdims=True
    )
    inner = jnp.transpose(jnp.broadcast_to(inner, (2 * BLOCK, 128)))[0:1, :]
    logs = l_ref[block]
    docs, allowed = tile_facts(doc_ref, first, first, BLOCK)

    def step(at, base, allowed):
        piece = pl.ds(pl.multiple_of(at * BLOCK, BLOCK), BLOCK)
        s = lax.dot_general(
            k_ref[piece, :], pair_q, (((1,), (1,)), ((), ())), preferred_element_type=f32
        )
        dp = lax.dot_general(
            v_ref[piece, :], pair_do, (((1,), (1,)), ((), ())), preferred_element_type=f32
        )
        p = jnp.exp(s - base)
        if allowed is not None:
            p = jnp.where(allowed, p, 0.0)
        ds = (p * (dp - inner)).astype(bf16)
        acc_v[piece, :] += jnp.dot(p.astype(bf16), pair_do, preferred_element_type=f32)
        acc_k[piece, :] += jnp.dot(ds, pair_q, preferred_element_type=f32)
        return jnp.dot(k_cols[:, piece], ds, preferred_element_type=f32)

    acc_q[...] = step(block, logs, allowed)
    base = jnp.where(docs == 0, logs, -masked)

    def earlier(at, carry):
        acc_q[...] += step(at, base, None)
        return carry

    lax.fori_loop(0, block, earlier, 0)
    grad = from_heads(jnp.transpose(acc_q[...]), head_width)
    return (grad * head_width**-0.5).astype(bf16)


def turned(values):
    return jnp.transpose(values.astype(f32)).astype(bf16)


class AttnForward(Parts):
    def __init__(
        self, block, docs, scale, heads, biases, wide, layer, norms, residual=None, late=None
    ):
        rows, width = block.shape
        self.head_width, self.layer, self.late = wide, layer, late
        here = 2 * wide
        self.arrays = (block, docs, scale, biases, *heads)
        far = pltpu.HBM if late else pltpu.VMEM
        self.spaces = (far, far, pltpu.VMEM) + (far,) * (1 + len(heads))
        column = jax.ShapeDtypeStruct((8 * rows, here), bf16)
        self.outs = (
            jax.ShapeDtypeStruct((rows, width), f32),
            jax.ShapeDtypeStruct((8 * rows, width), bf16),
            column,
            column,
            column,
            column,
            jax.ShapeDtypeStruct((8 * rows, here), f32),
            jax.ShapeDtypeStruct((8 * rows // BLOCK, 1, 2 * BLOCK), f32),
        )
        wide_shape = jax.ShapeDtypeStruct((rows, 128), f32)
        self.outs += (self.outs[0], wide_shape, self.outs[0], wide_shape)
        self.outs += (jax.ShapeDtypeStruct((rows, width), bf16),)
        self.out_spaces = (pltpu.VMEM, pltpu.HBM) + (pltpu.VMEM,) * 11
        self.arrays += tuple(norms)
        self.spaces += (pltpu.VMEM,) * 5
        self.scratch = (
            pltpu.VMEM((8 * rows, width), bf16),
            pltpu.VMEM((here, 8 * rows), bf16),
            pltpu.VMEM((8 * rows // SPAN, SPAN, 2 * BLOCK), f32),
            pltpu.VMEM((here, 2 * BLOCK), f32),
            pltpu.VMEM((8, 2 * BLOCK), f32),
            pltpu.VMEM((8, 2 * BLOCK), f32),
            dma_sems(1),
        )
        parts = dict(gather=PlaneGather(block), scatter=PlaneScatter(rows, width, 0))
        if late:
            parts.update(heads=HeadGather(*heads, layer), biases=LineGather(biases))
            parts.update(tokens=PlaneMove(block, when="push"), docs=PlaneMove(docs, when="push"))
            self.outs += parts["heads"].outs + parts["biases"].outs
            self.outs += (jax.ShapeDtypeStruct(docs.shape, f32),)
            self.outs += (jax.ShapeDtypeStruct(block.shape, f32),) * 2
            self.outs += (wide_shape,)
            self.out_spaces += (pltpu.VMEM,) * 6
            self.scratch += (pltpu.VMEM(block.shape, bf16), pltpu.VMEM(block.shape, bf16))
            self.scratch += (pltpu.VMEM(docs.shape, docs.dtype),)
            self.arrays += tuple(late)
            self.spaces += (pltpu.VMEM,) * 2
        else:
            self.arrays += (residual,)
            self.spaces += (pltpu.VMEM,)
        self.base = 3 + 1 + len(heads)
        self.use(**parts)

    def start(self, here, ins, outs, scratch):
        if self.late:
            for name, at, target in (("tokens", 0, scratch[7]), ("docs", 1, scratch[9])):
                self.parts[name].start(here, (ins[at],), (target,), self.held(scratch, name))
        else:
            self.parts["gather"].start(here, ins[:1], scratch[:1], self.held(scratch, "gather"))

    def first_norm(self, here, ins, outs, scratch):
        tokens, block = scratch[7:9]
        residual_ref, normal_ref, factor_ref = outs[16:19]
        moves = [
            (self.parts[name], (here, (ins[at],), (target,), self.held(scratch, name)))
            for name, at, target in (("tokens", 0, tokens), ("docs", 1, scratch[9]))
        ]
        for part, held in moves:
            part.at_moment("push", *held)
        self.parts["biases"].start(here, ins[3:4], outs[14:15], self.held(scratch, "biases"))
        self.parts["heads"].start(here, ins[4:6], outs[13:14], self.held(scratch, "heads"))
        for part, held in moves:
            part.finish(*held)
        outs[15][...] = scratch[9][...].astype(f32)
        gain, bias = (ref[self.layer : self.layer + 1, :] for ref in ins[self.base + 5 :])
        values = tokens[...].astype(f32)
        residual_ref[...] = values
        normal, factor = normalize(values)
        factor_ref[...] = wide_column(factor)
        normal_ref[...] = normal
        block[...] = (normal * gain + bias).astype(bf16)
        return block

    def finish(self, here, ins, outs, scratch):
        block_ref, doc_ref, scale_ref = ins[:3]
        scale_row = scale_of(here, scale_ref, self.layer, self.head_width)
        heads_ref, bias_ref = outs[13:15] if self.late else (ins[4], ins[3])
        if self.late:
            doc_ref = outs[15]
            block_ref = self.first_norm(here, ins, outs, scratch)
            self.parts["gather"].start(
                here, (block_ref,), scratch[:1], self.held(scratch, "gather")
            )
        out_ref, rows_out, q_ref, k_ref, v_ref, z_ref, o_ref, l_ref = outs[:8]
        rows_buf, v_cols, s_buf, acc, top, total, save = scratch[:7]
        rows, model_width = block_ref.shape
        wide = self.head_width
        width = 2 * wide

        def bias_row(at):
            pair = [
                bias_ref[2 * here.core + i, self.layer : self.layer + 1, at : at + width]
                for i in range(2)
            ]
            lane = lax.broadcasted_iota(jnp.int32, (1, width), 1)
            return jnp.where(lane < wide, pair[0], pair[1])

        def work(first):
            block = pl.ds(first, rows)
            projected = lax.dot_general(
                rows_buf[block, :],
                heads_ref[0:3].reshape(3 * width, model_width),
                (((1,), (1,)), ((), ())),
                preferred_element_type=f32,
            )
            q = (projected[:, :width] + bias_row(0)).astype(bf16).astype(f32)
            q_ref[block, :] = (q * wide**-0.5).astype(bf16)
            k_ref[block, :] = projected[:, width : 2 * width].astype(bf16)
            v = (projected[:, 2 * width :] + bias_row(width)).astype(bf16)
            v_ref[block, :] = v
            v_cols[:, block] = turned(v)

        self.parts["gather"].finish(
            here,
            (block_ref,),
            scratch[:1],
            self.held(scratch, "gather"),
            None if self.late else work,
        )
        keep_rows = pltpu.make_async_copy(rows_buf, rows_out, save.at[0])
        keep_rows.start()
        if self.late:
            self.parts["heads"].arrive(0, outs[13:14], self.held(scratch, "heads"))
            self.parts["biases"].finish(here, ins[3:4], outs[14:15], self.held(scratch, "biases"))
            in_chunks(8 * rows, rows, work)
            self.parts["heads"].arrive(1, outs[13:14], self.held(scratch, "heads"))
        self.moment("midway")

        def rows_of(first):
            out = attend_block(
                wide, first, q_ref, k_ref, v_cols, doc_ref, o_ref, l_ref, s_buf, acc, top, total
            )
            z = (out * scale_row).astype(bf16)
            z_ref[pl.ds(first, rows), :] = z
            return z

        self.parts["scatter"].finish(
            here,
            None,
            (out_ref,),
            self.held(scratch, "scatter"),
            rows_of,
            lambda: heads_ref[3].reshape(width, model_width),
            idle=lambda: self.moment("closing"),
        )
        residual_ref = outs[16] if self.late else ins[self.base + 5]
        layer = slice(self.layer, self.layer + 1)
        shift, gain_1, bias_1, gain_2, bias_2 = (
            ref[layer, :] for ref in ins[self.base : self.base + 5]
        )
        normal_1, factor_1, normal_2, factor_2, next_ref = outs[8:13]

        def settle(at):
            piece = pl.ds(at, NARROW)
            normal, factor = normalize(out_ref[piece, :] + shift)
            normal_1[piece, :] = normal
            factor_1[piece, :] = wide_column(factor)
            middle = residual_ref[piece, :] + (normal * gain_1 + bias_1)
            out_ref[piece, :] = middle
            normal, factor = normalize(middle)
            normal_2[piece, :] = normal
            factor_2[piece, :] = wide_column(factor)
            next_ref[piece, :] = (normal * gain_2 + bias_2).astype(bf16)

        in_chunks(rows, NARROW, settle)
        keep_rows.wait()
        if self.late:
            held = self.held(scratch, "heads")
            self.parts["heads"].sent(here, ins[4:6], outs[13:14], held)


class AttnBackward(Parts):
    def __init__(
        self, block, docs, scale, heads, q, k, v, z, o, logs, attn_rows, norm, hidden, layer, end
    ):
        self.end = end
        self.layer = layer
        rows, width = block.shape
        kinds, _, wide, _ = heads.shape
        self.head_width = wide
        here = 2 * wide
        self.arrays = (block, docs, scale, heads, q, k, v, z, o, logs, attn_rows)
        self.spaces = (pltpu.VMEM,) * 10 + (pltpu.HBM,)
        self.arrays += (*norm, hidden)
        self.spaces += (pltpu.VMEM,) * 5
        move, heads_sum = PlaneMove(block, back=True, when="push"), HeadScatter(heads)
        vector, sums = jax.ShapeDtypeStruct((8, width), f32), jax.ShapeDtypeStruct((4, 4, here), f32)
        quarter = heads_sum.outs[0]
        if end:
            tail = dict(
                move=move,
                vectors=PlaneSum(vector),
                line=LineSum(vector),
                rows=RowsGather(quarter),
                hidden=ThenRows(LineScatter(sums), "push"),
            )
            self.outs = move.outs + (vector,) + tail["rows"].outs + tail["hidden"].outs
            self.out_spaces = (pltpu.HBM, pltpu.VMEM, pltpu.HBM, pltpu.HBM)
        else:
            self.outs = (jax.ShapeDtypeStruct((rows, width), f32), quarter, sums)
            self.outs += (jax.ShapeDtypeStruct((rows, width), bf16), vector)
            self.out_spaces = (pltpu.VMEM,) * 5
        self.scratch = (
            pltpu.VMEM((8 * rows, width), bf16),
            pltpu.VMEM((8 * rows, width), bf16),
            pltpu.VMEM((here, 8 * rows), bf16),
            pltpu.VMEM((8 * rows, here), f32),
            pltpu.VMEM((8 * rows, here), f32),
            pltpu.VMEM((here, 2 * BLOCK), f32),
            pltpu.VMEM((8 * rows, 3 * here), bf16),
            pltpu.VMEM((here, width), f32),
            pltpu.VMEM((3, 8, here), f32),
            dma_sems(1),
            pltpu.VMEM((2, 8, width), f32),
            pltpu.VMEM(heads.shape, bf16),
        )
        if end:
            self.scratch += (
                pltpu.VMEM((rows, width), f32),
                pltpu.VMEM(quarter.shape, bf16),
                pltpu.VMEM(sums.shape, f32),
                pltpu.VMEM((rows, width), bf16),
                pltpu.VMEM(vector.shape, f32),
                pltpu.VMEM(vector.shape, f32),
            )
        parts = dict(gather=PlaneGather(block), scatter=PlaneScatter(rows, width, 0))
        parts.update(heads=heads_sum, **(tail if end else {}))
        self.use(**parts)

    def load(self, ins, scratch):
        return pltpu.make_async_copy(ins[10], scratch[1], scratch[9].at[0])

    def start(self, here, ins, outs, scratch):
        self.parts["gather"].start(here, ins[:1], scratch[:1], self.held(scratch, "gather"))
        self.load(ins, scratch).start()

    def finish(self, here, ins, outs, scratch):
        block_ref, doc_ref, scale_ref, heads_ref, q_ref, k_ref, v_ref, z_ref, o_ref, l_ref = ins[:10]
        results = scratch[12:17] if self.end else outs
        out_ref, quarter_ref, hidden_ref, rounded_ref, vector_ref = results
        middle_ref, normal_ref, factor_ref, gain_ref, sums_ref = ins[11:16]
        (
            rows_buf,
            attn_rows,
            k_cols,
            acc_k,
            acc_v,
            acc_q,
            proj,
            out_sum,
            small,
        ) = scratch[:9]
        vectors = scratch[10]
        heads_grad = scratch[11]
        scale_row = scale_of(here, scale_ref, self.layer, self.head_width)
        rows, model_width = block_ref.shape
        wide = self.head_width
        width = 2 * wide
        acc_k[...] = jnp.zeros_like(acc_k)
        acc_v[...] = jnp.zeros_like(acc_v)
        out_sum[...] = jnp.zeros_like(out_sum)
        small[...] = jnp.zeros_like(small)
        k_cols[...] = turned(k_ref[...])

        def work(first):
            block = pl.ds(first, rows)
            scaled_grad = lax.dot_general(
                rows_buf[block, :],
                heads_ref[3].reshape(width, model_width),
                (((1,), (1,)), ((), ())),
                preferred_element_type=f32,
            )
            out_sum[...] += lax.dot_general(
                z_ref[block, :],
                rows_buf[block, :],
                (((0,), (0,)), ((), ())),
                preferred_element_type=f32,
            )
            small[0] += fold(o_ref[block, :] * scaled_grad)
            grad = attend_block_back(
                wide,
                first,
                (scaled_grad * scale_row).astype(bf16),
                q_ref,
                k_ref,
                k_cols,
                v_ref,
                o_ref,
                l_ref,
                doc_ref,
                acc_k,
                acc_v,
                acc_q,
            )
            proj[block, 0:width] = grad
            small[1] += fold(grad.astype(f32))

        self.parts["gather"].finish(
            here,
            ins[:1],
            scratch[:1],
            self.held(scratch, "gather"),
            work,
            lambda: self.moment("soon"),
        )

        def settle(first):
            block = pl.ds(first, rows)
            proj[block, width : 2 * width] = acc_k[block, :].astype(bf16)
            value_grad = acc_v[block, :].astype(bf16)
            proj[block, 2 * width : 3 * width] = value_grad
            small[2] += fold(value_grad.astype(f32))

        in_chunks(8 * rows, rows, settle)
        self.moment("midway")

        def early():
            self.load(ins, scratch).wait()
            qkv_grad = lax.dot_general(
                proj[...],
                attn_rows[...],
                (((0,), (0,)), ((), ())),
                preferred_element_type=f32,
            )
            heads_grad[0:3] = qkv_grad.astype(bf16).reshape(3, 2, wide, model_width)
            heads_grad[3] = out_sum[...].astype(bf16).reshape(2, wide, model_width)
            self.parts["heads"].start(here, (heads_grad,), None, self.held(scratch, "heads"))

        early()
        self.parts["scatter"].finish(
            here,
            None,
            (out_ref,),
            self.held(scratch, "scatter"),
            lambda first: proj[pl.ds(first, rows), :],
            lambda: heads_ref[0:3].reshape(3 * width, model_width),
            idle=lambda: self.moment("closing"),
        )
        vectors[...] = jnp.zeros_like(vectors)
        layer = slice(self.layer, self.layer + 1)

        def pull(at):
            piece = pl.ds(at, NARROW)
            grad, normal = out_ref[piece, :], normal_ref[piece, :]
            vectors[0] += fold(grad * normal)
            vectors[1] += fold(grad)
            gradient = middle_ref[piece, :] + norm_pull(
                grad, normal, factor_ref[piece, 0:1], gain_ref[layer, :]
            )
            out_ref[piece, :] = gradient
            rounded_ref[piece, :] = gradient.astype(bf16)

        in_chunks(rows, NARROW, pull)
        if self.end:
            home = (here, (rounded_ref,), outs[:1], self.held(scratch, "move"))
            self.parts["move"].start(*home)
        scale_cols, query_cols, value_cols = (
            jnp.sum(small[i], axis=0, keepdims=True) for i in range(3)
        )
        vector_ref[...] = jnp.zeros_like(vector_ref)
        for i in range(2):
            vector_ref[i : i + 1, :] = jnp.sum(vectors[i], axis=0, keepdims=True)
        lane = lax.broadcasted_iota(jnp.int32, (1, width), 1)
        place = lax.broadcasted_iota(jnp.int32, (1, model_width), 1)
        head_sums = jnp.zeros((1, model_width), f32)
        for i in range(2):
            head = ((2 * here.core + i) * 2 + here.x) * 2 + here.y
            own = (lane >= i * wide) & (lane < (i + 1) * wide)
            total = jnp.sum(jnp.where(own, scale_cols, 0.0), axis=1, keepdims=True)
            head_sums = head_sums + jnp.where(place == head, total, 0.0)
        vector_ref[2:3, :] = head_sums
        pairs = [
            jnp.concatenate(
                [cols[:, i * wide : (i + 1) * wide] for cols in (query_cols, value_cols)], axis=1
            )
            for i in range(2)
        ]
        for shard in range(4):
            for row, source in enumerate((2, 0, 1)):
                cut = sums_ref[source : source + 1, shard * width : (shard + 1) * width]
                hidden_ref[shard, row : row + 1, :] = cut
            own = here.core == shard // 2
            hidden_ref[shard, 3:4, :] = jnp.where(own, pairs[shard % 2], 0.0)
        self.moment("tail")
        held = (here, (heads_grad,), (quarter_ref,), self.held(scratch, "heads"))
        if not self.end:
            self.parts["heads"].finish(*held)
            return
        sum_held = (here, (vector_ref,), (scratch[17],), self.held(scratch, "vectors"))
        line_held = (here, (scratch[17],), outs[1:2], self.held(scratch, "line"))
        rows_held = (here, (quarter_ref,), outs[2:3], self.held(scratch, "rows"))
        hidden_held = (here, (hidden_ref,), outs[3:4], self.held(scratch, "hidden"))
        self.parts["vectors"].start(*sum_held)
        self.parts["hidden"].start(*hidden_held)
        self.parts["heads"].finish(*held)
        self.parts["rows"].begin(*rows_held)
        self.parts["vectors"].finish(*sum_held)
        self.parts["line"].start(*line_held)
        self.parts["move"].at_moment("push", *home)
        self.parts["hidden"].at_moment("push", *hidden_held)
        self.parts["line"].finish(*line_held)
        self.parts["rows"].finish(*rows_held)
        self.parts["hidden"].finish(*hidden_held)
        self.parts["move"].finish(*home)


def finish_kernel(layers, *refs):
    count = 2 + 6 * layers
    far, refs, sems = refs[:count], refs[count:-1], refs[-1]
    refs, near = refs[: len(refs) - count], refs[len(refs) - count :]
    loads = [pltpu.make_async_copy(a, b, sems.at[i]) for i, (a, b) in enumerate(zip(far, near))]
    order = [0, 1] + [2 + g * layers + i for i in range(layers - 1, -1, -1) for g in range(6)]
    for index in order:
        loads[index].start()
    refs = (*near, *refs)
    (layer_ref, grad_ref), refs = refs[:2], refs[2:]
    groups = []
    for _ in range(6):
        groups.append(refs[:layers])
        refs = refs[layers:]
    firsts, seconds, heads_all, hiddens, earlies, lates = groups
    (
        layer_out,
        grad_out,
        attn_gain,
        attn_bias,
        qkv_out,
        bias_out,
        scale_out,
        out_out,
        out_shift,
        post_gain,
        post_bias,
        ffn_gain,
        ffn_bias,
        first_out,
        first_shift,
        mid_gain,
        mid_bias,
        second_out,
        second_shift,
    ) = refs
    loads[0].wait()
    layer_out[...] = layer_ref[...]
    loads[1].wait()
    grad_out[...] = grad_ref[...].astype(f32)
    for layer in range(layers - 1, -1, -1):
        for group in range(6):
            loads[2 + group * layers + layer].wait()
        first, second, heads, hidden = (g[layer] for g in (firsts, seconds, heads_all, hiddens))
        part = first.shape[2]
        wide, half = heads.shape[2:]
        row = slice(layer, layer + 1)
        for i, ref in enumerate((out_shift, post_gain, post_bias, ffn_gain, ffn_bias, second_shift)):
            ref[row, :] = earlies[layer][i : i + 1, :]
        for i, ref in enumerate((attn_gain, attn_bias)):
            ref[row, :] = lates[layer][i : i + 1, :]
        scale_out[row, :] = lates[layer][2:3, 0 : scale_out.shape[1]]
        for i in range(4):
            cut = slice(i * part, (i + 1) * part)
            first_out[layer, :, cut] = first[i].astype(f32)
            second_out[layer, cut, :] = second[i].astype(f32)
            for at, ref in enumerate((first_shift, mid_gain, mid_bias)):
                ref[row, cut] = hidden[i, at : at + 1, :]
        biases = [hidden[2 * y, 3:4, :] + hidden[2 * y + 1, 3:4, :] for y in range(2)]
        for i in range(2):
            bias_out[layer, i : i + 1, :] = jnp.concatenate(
                [each[:, i * wide : (i + 1) * wide] for each in biases], axis=1
            )
        for core in range(2):
            here = slice(core * half, (core + 1) * half)
            for kind in range(3):
                pair = jnp.concatenate([heads[core, kind], heads[2 + core, kind]], axis=0)
                qkv_out[layer, kind, here, :] = jnp.transpose(pair.astype(f32))
            for y in range(2):
                out_out[layer, y * wide : (y + 1) * wide, here] = heads[2 * y + core, 3].astype(f32)


def finish_all(layer_output, gradient, heads_count, *groups):
    firsts, seconds, heads = groups[:3]
    layers = len(firsts)
    rows, width = layer_output.shape
    part = firsts[0].shape[2]
    wide = heads[0].shape[2]
    vector = jax.ShapeDtypeStruct((layers, width), f32)
    hidden = jax.ShapeDtypeStruct((layers, 4 * part), f32)
    outs = (
        jax.ShapeDtypeStruct((rows, width), bf16),
        jax.ShapeDtypeStruct((rows, width), f32),
        vector,
        vector,
        jax.ShapeDtypeStruct((layers, 3, width, 2 * wide), f32),
        jax.ShapeDtypeStruct((layers, 2, 2 * wide), f32),
        jax.ShapeDtypeStruct((layers, heads_count), f32),
        jax.ShapeDtypeStruct((layers, 2 * wide, width), f32),
        vector,
        vector,
        vector,
        vector,
        vector,
        jax.ShapeDtypeStruct((layers, width, 4 * part), f32),
        hidden,
        hidden,
        hidden,
        jax.ShapeDtypeStruct((layers, 4 * part, width), f32),
        vector,
    )
    arrays = [layer_output, gradient] + [each for group in groups for each in group]
    results = list(
        pl.pallas_call(
            partial(finish_kernel, layers),
            out_shape=outs,
            in_specs=[pl.BlockSpec(memory_space=pltpu.HBM)] * len(arrays),
            out_specs=[pl.BlockSpec(memory_space=pltpu.VMEM)] * len(outs),
            scratch_shapes=[
                *[pltpu.VMEM(each.shape, each.dtype) for each in arrays],
                dma_sems(len(arrays)),
            ],
            compiler_params=vmem_params(None, 60),
        )(*arrays)
    )
    results[4] = jnp.transpose(results[4], (0, 2, 1, 3))
    return tuple(results)


def plane_device(
    tokens,
    segment_ids,
    cotangent,
    ln_attn_gain,
    ln_attn_bias,
    qkv_weight,
    qv_bias,
    head_scale,
    out_weight,
    out_bias,
    ln_post_gain,
    ln_post_bias,
    ln_ffn_gain,
    ln_ffn_bias,
    fc1_weight,
    fc1_bias,
    mid_gain,
    mid_bias,
    fc2_weight,
    fc2_bias,
):
    layers = qkv_weight.shape[0]
    model_width = tokens.shape[1]
    heads_all = head_scale.shape[1]
    head_width = model_width // heads_all
    hidden_here = fc1_weight.shape[2]
    hidden_all = hidden_here * 8
    quarter = hidden_here // 4
    half_width = model_width // 2
    x, y, core = lax.axis_index("x"), lax.axis_index("y"), lax.axis_index("core")
    quarter_at = 2 * y + core
    width = 2 * head_width
    ids = iter(range(1, 64))

    docs = segment_ids[None, :]

    def cut(values, at, size, axis):
        return lax.dynamic_slice_in_dim(values, at * size, size, axis)

    qkv_rows = jnp.transpose(qkv_weight, (0, 2, 3, 1))
    bias_heads = cut(qv_bias, y, head_width, 2)
    small = jnp.concatenate(
        [
            jnp.concatenate([bias_heads, bias_heads], axis=2).reshape(layers, 2 * width),
            cut(fc1_bias, quarter_at, quarter, 1),
            cut(mid_gain, quarter_at, quarter, 1),
            cut(mid_bias, quarter_at, quarter, 1),
        ],
        axis=1,
    )
    heads_here = [None] * layers
    norms = (out_bias, ln_post_gain, ln_post_bias, ln_ffn_gain, ln_ffn_bias)
    attn_norm = (ln_attn_gain, ln_attn_bias)

    stored = []
    for layer in range(layers):
        first, last = layer == 0, layer + 1 == layers
        if first:
            task = AttnForward(
                tokens,
                docs,
                head_scale,
                (qkv_rows, out_weight),
                small,
                head_width,
                layer,
                norms,
                late=attn_norm,
            )
            sides = [WeightGather(fc1_weight, layer, 1, "midway")]
        else:
            task = AttnForward(
                block,
                docs,
                head_scale,
                (heads_here[layer],),
                small,
                head_width,
                layer,
                norms,
                residual=residual,
            )
            sides = [WeightGather(fc1_weight, layer, 1), WeightGather(fc2_weight, layer, 0)]
        (got, (first_here,), *rest) = run_tasks(ids, task, *sides)
        middle, attn_rows, q, k, v, scaled, attended, logs = got[:8]
        post_normal, post_factor, ffn_normal, ffn_factor, block = got[8:13]
        if first:
            heads_here[0], small, docs, _, attn_normal, attn_factor = got[13:]
        here = (attn_normal, attn_factor)
        sides = [PlaneMove(cotangent)]
        if not last:
            sides = [HeadGather(qkv_rows, out_weight, layer + 1, "midway" if first else "start")]
        (got, (side,)) = run_tasks(
            ids,
            FfnForward(
                block,
                first_here,
                fc2_weight if first else rest[0][0],
                small,
                middle,
                fc2_bias,
                None if last else attn_norm,
                layer,
                first,
            ),
            *sides,
        )
        residual, ffn_rows, slope, hidden_normal, mixed, totals, block = got[:7]
        second_here = got[-1] if first else rest[0][0]
        if not last:
            attn_normal, attn_factor = got[7:9]
            heads_here[layer + 1] = side
        stored.append(
            (
                first_here,
                second_here,
                *here,
                attn_rows,
                q,
                k,
                v,
                attended,
                logs,
                scaled,
                post_normal,
                post_factor,
                ffn_normal,
                ffn_factor,
                ffn_rows,
                slope,
                hidden_normal,
                mixed,
                totals,
            )
        )
    gradient = gradient_b = side

    first_done, second_done = [None] * layers, [None] * layers
    heads_done, hidden_done = [None] * layers, [None] * layers
    early_done, late_done = [None] * layers, [None] * layers
    late_vectors = None
    for layer in reversed(range(layers)):
        (
            first_here,
            second_here,
            attn_normal,
            attn_factor,
            attn_rows,
            q,
            k,
            v,
            attended,
            logs,
            scaled,
            post_normal,
            post_factor,
            ffn_normal,
            ffn_factor,
            ffn_rows,
            slope,
            hidden_normal,
            mixed,
            totals,
        ) = stored[layer]
        last = layer + 1 == layers
        if last:
            sides = [PlaneMove(block, back=True)]
        else:
            sides = [RowsGather(heads_grad, "midway")]
            sides.append(ThenRows(LineScatter(hidden_grad), "closing"))
            sides += [LineSum(early_vectors), StepSum(late_vectors)]
        ((gradient, first_grad, second_grad, hidden_sums, branch_b, early_vectors), *got) = (
            run_tasks(
                ids,
                FfnBackward(
                    gradient_b,
                    first_here,
                    second_here,
                    small,
                    slope,
                    hidden_normal,
                    mixed,
                    ffn_rows,
                    totals,
                    gradient,
                    (
                        ffn_normal,
                        ffn_factor,
                        ln_ffn_gain,
                        post_normal,
                        post_factor,
                        ln_post_gain,
                    ),
                    layer,
                ),
                *sides,
            )
        )
        if last:
            layer_output = got[0][0]
        else:
            heads_done[layer + 1], hidden_done[layer + 1] = got[0][0], got[1][0]
            early_done[layer + 1], late_vectors = got[2][0], got[3][0]
        sides = [ThenRows(LineScatter(first_grad), "soon"), RowsGather(second_grad)]
        sides.append(StepThenLine(early_vectors) if layer == 0 else StepSum(early_vectors))
        if not last:
            sides.append(LineSum(late_vectors))
        (results, *got) = run_tasks(
            ids,
            AttnBackward(
                branch_b,
                docs,
                head_scale,
                heads_here[layer],
                q,
                k,
                v,
                scaled,
                attended,
                logs,
                attn_rows,
                (gradient, attn_normal, attn_factor, ln_attn_gain),
                hidden_sums,
                layer,
                layer == 0,
            ),
            *sides,
        )
        first_done[layer], second_done[layer], early_vectors = got[0][0], got[1][0], got[2][0]
        if not last:
            late_done[layer + 1] = got[3][0]
        if layer == 0:
            input_grad, late_done[0], heads_done[0], hidden_done[0] = results
            early_done[0] = early_vectors
        else:
            gradient, heads_grad, hidden_grad, gradient_b, late_vectors = results
    return finish_all(
        layer_output,
        input_grad,
        heads_all,
        first_done,
        second_done,
        heads_done,
        hidden_done,
        early_done,
        late_done,
    )


def split_specs(rows, mp):
    both = tuple(rows) + tuple(mp)
    in_specs = (
        P(both, None),
        P(rows),
        P(both, None),
        P(),
        P(),
        P(None, None, None, mp),
        P(None, None, mp),
        P(),
        P(None, mp, None),
        P(),
        P(),
        P(),
        P(),
        P(),
        P(None, None, mp),
        P(None, mp),
        P(None, mp),
        P(None, mp),
        P(None, mp, None),
        P(),
    )
    out_specs = (
        P(both, None),
        P(both, None),
        P(),
        P(),
        P(None, None, None, mp),
        P(None, None, mp),
        P(),
        P(None, mp, None),
        P(),
        P(),
        P(),
        P(),
        P(),
        P(None, None, mp),
        P(None, mp),
        P(None, mp),
        P(None, mp),
        P(None, mp, None),
        P(),
    )
    return in_specs, out_specs


def solution(mesh):
    if mesh.shape["rows"] == 4 and mesh.shape["mp"] == 8:
        planes = Mesh(mesh.devices.reshape(2, 2, 4, 2), ("y", "core", "z", "x"))
        in_specs, out_specs = split_specs(("y", "core"), ("z", "x"))
        return jax.shard_map(
            plane_device, mesh=planes, in_specs=in_specs, out_specs=out_specs, check_vma=False
        )
    in_specs, out_specs = split_specs(("rows",), ("mp",))
    return jax.shard_map(
        per_device, mesh=mesh, in_specs=in_specs, out_specs=out_specs, check_vma=False
    )
```

```python
from functools import partial

import jax
import jax.numpy as jnp
from jax import lax
from jax.experimental import pallas as pl
from jax.experimental.pallas import tpu as pltpu
from jax.sharding import Mesh
from jax.sharding import PartitionSpec as P

epsilon = 1e-05
masked = -1e30


def partner(shard, axis, stride):
    return lax.ppermute(shard, axis, [(i, i ^ 1 << stride) for i in range(lax.axis_size(axis))])


def norm_local(values, gain_row, bias_row):
    average = jnp.mean(values, axis=-1, keepdims=True)
    centered = values - average
    spread = jnp.mean(centered * centered, axis=-1, keepdims=True)
    factor = lax.rsqrt(spread + epsilon)
    normal = centered * factor
    return (normal * gain_row + bias_row, normal, factor)


def norm_back(grad_out, normal, factor, gain_row):
    scaled = grad_out * gain_row
    inner_sum = jnp.mean(scaled * normal, axis=-1, keepdims=True)
    return factor * (scaled - jnp.mean(scaled, axis=-1, keepdims=True) - normal * inner_sum)


def collect_rows(normed_b):
    return lax.all_gather(normed_b, "mp", axis=0, tiled=True)


def collect_grads(gradient_b):
    return lax.all_gather(gradient_b, "mp", axis=0, tiled=True)


def reduce_branch(operand_b, weight_b, local_rows):

    def partial_term(first_row, count):
        return jnp.dot(operand_b, weight_b, preferred_element_type=jnp.float32)

    return lax.psum_scatter(
        partial_term(jnp.int32(0), local_rows * lax.axis_size("mp")).astype(jnp.bfloat16),
        "mp",
        scatter_dimension=0,
        tiled=True,
    ).astype(jnp.float32)


def reduce_grads(operand_b, weight_b, local_rows):

    def partial_term(first_row, count):
        return jnp.einsum("tc,dc->td", operand_b, weight_b, preferred_element_type=jnp.float32)

    return lax.psum_scatter(
        partial_term(jnp.int32(0), local_rows * lax.axis_size("mp")).astype(jnp.bfloat16),
        "mp",
        scatter_dimension=0,
        tiled=True,
    ).astype(jnp.float32)


def hidden_stats(first_sum, second_sum):
    return lax.psum((first_sum, second_sum), "mp")


def hidden_grad_stats(first_sum, second_sum):
    return lax.psum((first_sum, second_sum), "mp")


def join_cols(mine, other, is_upper):
    lower_part = jnp.where(is_upper, other, mine)
    upper_part = jnp.where(is_upper, mine, other)
    return jnp.concatenate([lower_part, upper_part], axis=-1)


def join_rows(mine, other, is_upper):
    lower_part = jnp.where(is_upper, other, mine)
    upper_part = jnp.where(is_upper, mine, other)
    return jnp.concatenate([lower_part, upper_part], axis=0)


def split_cols(values, cols_here, is_upper):
    lower_part = values[..., :cols_here]
    upper_part = values[..., cols_here:]
    return (
        jnp.where(is_upper, upper_part, lower_part),
        jnp.where(is_upper, lower_part, upper_part),
    )


def masked_scores(query_block, key_rows, query_start, block_rows, doc_rows, positions):
    factor = query_block.shape[-1] ** (-0.5)
    scores = (
        jnp.einsum("qhe,khe->hqk", query_block, key_rows, preferred_element_type=jnp.float32)
        * factor
    )
    query_place = query_start + jnp.arange(block_rows, dtype=jnp.int32)
    query_docs = lax.dynamic_slice_in_dim(doc_rows, query_start, block_rows, 0)
    allowed = (query_docs[:, None] == doc_rows[None, :]) & (
        query_place[:, None] >= positions[None, :]
    )
    return jnp.where(allowed[None], scores, masked)


def attend_forward(queries, key_rows, value_rows, doc_rows, row_offset):
    total_rows = queries.shape[0]
    block_rows = min(512, total_rows)
    positions = jnp.arange(key_rows.shape[0], dtype=jnp.int32)

    def one_block(first_row):
        query_block = lax.dynamic_slice_in_dim(queries, first_row, block_rows, 0)
        scores = masked_scores(
            query_block, key_rows, row_offset + first_row, block_rows, doc_rows, positions
        )
        row_peak = jnp.max(scores, axis=-1, keepdims=True)
        weights = jnp.exp(scores - row_peak)
        totals = jnp.sum(weights, axis=-1, keepdims=True)
        probabilities = (weights / totals).astype(jnp.bfloat16)
        output = jnp.einsum(
            "hqk,khe->qhe", probabilities, value_rows, preferred_element_type=jnp.float32
        )
        return (output, (row_peak + jnp.log(totals))[..., 0])

    starts = jnp.arange(total_rows // block_rows, dtype=jnp.int32) * block_rows
    outputs, log_totals = lax.map(one_block, starts)
    return (outputs.reshape(queries.shape), log_totals)


def attend_backward(queries, key_rows, value_rows, doc_rows, row_offset, log_totals, grad_out):
    total_rows = queries.shape[0]
    block_rows = min(512, total_rows)
    positions = jnp.arange(key_rows.shape[0], dtype=jnp.int32)
    factor = queries.shape[-1] ** (-0.5)

    def one_block(running, first_row):
        key_grad, value_grad = running
        query_block = lax.dynamic_slice_in_dim(queries, first_row, block_rows, 0)
        grad_block = lax.dynamic_slice_in_dim(grad_out, first_row, block_rows, 0)
        scores = masked_scores(
            query_block, key_rows, row_offset + first_row, block_rows, doc_rows, positions
        )
        block_totals = lax.dynamic_index_in_dim(
            log_totals, first_row // block_rows, 0, keepdims=False
        )
        probabilities = jnp.exp(scores - block_totals[..., None])
        prob_grad = jnp.einsum(
            "qhe,khe->hqk", grad_block, value_rows, preferred_element_type=jnp.float32
        )
        inner_sum = jnp.sum(probabilities * prob_grad, axis=-1, keepdims=True)
        score_grad = (probabilities * (prob_grad - inner_sum)).astype(jnp.bfloat16)
        query_grad = (
            jnp.einsum("hqk,khe->qhe", score_grad, key_rows, preferred_element_type=jnp.float32)
            * factor
        )
        key_grad = (
            key_grad
            + jnp.einsum(
                "hqk,qhe->khe", score_grad, query_block, preferred_element_type=jnp.float32
            )
            * factor
        )
        value_grad = value_grad + jnp.einsum(
            "hqk,qhe->khe",
            probabilities.astype(jnp.bfloat16),
            grad_block,
            preferred_element_type=jnp.float32,
        )
        return ((key_grad, value_grad), query_grad)

    starts = jnp.arange(total_rows // block_rows, dtype=jnp.int32) * block_rows
    zero_grads = jnp.zeros(key_rows.shape, jnp.float32)
    (key_grad, value_grad), query_grads = lax.scan(one_block, (zero_grads, zero_grads), starts)
    return (query_grads.reshape(queries.shape), key_grad, value_grad)


def stack_layers(layer_list, members):
    stacked = []
    for member_index in range(members):
        stacked.append(jnp.stack([entry[member_index] for entry in layer_list], axis=0))
    return stacked


def per_device(
    tokens,
    segment_ids,
    cotangent,
    ln_attn_gain,
    ln_attn_bias,
    qkv_weight,
    qv_bias,
    head_scale,
    out_weight,
    out_bias,
    ln_post_gain,
    ln_post_bias,
    ln_ffn_gain,
    ln_ffn_bias,
    fc1_weight,
    fc1_bias,
    mid_gain,
    mid_bias,
    fc2_weight,
    fc2_bias,
):
    layers = qkv_weight.shape[0]
    local_rows = tokens.shape[0]
    model_width = tokens.shape[1]
    cols_here = qkv_weight.shape[3]
    heads_all = head_scale.shape[1]
    head_width = model_width // heads_all
    pair_cols = 2 * cols_here
    pair_heads = pair_cols // head_width
    group_rows = segment_ids.shape[0]
    half_rows = group_rows // 2
    hidden_all = fc1_weight.shape[2] * lax.axis_size("mp")
    device_index = lax.axis_index("mp")
    is_upper = device_index % 2 == 1
    own_start = jnp.where(is_upper, half_rows, 0).astype(jnp.int32)
    other_start = jnp.where(is_upper, 0, half_rows).astype(jnp.int32)
    first_head = device_index // 2 * pair_heads
    pair_onehot = (
        (first_head + jnp.arange(pair_heads, dtype=jnp.int32))[:, None]
        == jnp.arange(heads_all, dtype=jnp.int32)[None, :]
    ).astype(jnp.float32)
    residual = tokens.astype(jnp.float32)
    stored = []
    for layer_index in range(layers):
        attn_in, attn_normal, attn_factor = norm_local(
            residual, ln_attn_gain[layer_index], ln_attn_bias[layer_index]
        )
        attn_rows = collect_rows(attn_in.astype(jnp.bfloat16))
        qkv_here = qkv_weight[layer_index].reshape(model_width, 3 * cols_here)
        projected = jnp.dot(attn_rows, qkv_here, preferred_element_type=jnp.float32).reshape(
            -1, 3, cols_here
        )
        bias_pair = qv_bias[layer_index]
        query_mine = (projected[:, 0] + bias_pair[0]).astype(jnp.bfloat16)
        key_mine = projected[:, 1].astype(jnp.bfloat16)
        value_mine = (projected[:, 2] + bias_pair[1]).astype(jnp.bfloat16)
        query_send = lax.dynamic_slice_in_dim(query_mine, other_start, half_rows, 0)
        query_recv, key_recv, value_recv = partner((query_send, key_mine, value_mine), "mp", 0)
        query_own = lax.dynamic_slice_in_dim(query_mine, own_start, half_rows, 0)
        queries = join_cols(query_own, query_recv, is_upper).reshape(
            half_rows, pair_heads, head_width
        )
        key_rows = join_cols(key_mine, key_recv, is_upper).reshape(
            group_rows, pair_heads, head_width
        )
        value_rows = join_cols(value_mine, value_recv, is_upper).reshape(
            group_rows, pair_heads, head_width
        )
        attended, log_totals = attend_forward(queries, key_rows, value_rows, segment_ids, own_start)
        pair_scale = jnp.sum(pair_onehot * head_scale[layer_index][None, :], axis=1)
        scaled_half = (
            (attended * pair_scale[None, :, None])
            .astype(jnp.bfloat16)
            .reshape(half_rows, pair_cols)
        )
        own_cols, other_cols = split_cols(scaled_half, cols_here, is_upper)
        scaled_recv = partner(other_cols, "mp", 0)
        scaled_mine = join_rows(own_cols, scaled_recv, is_upper)
        branch = (
            reduce_branch(scaled_mine, out_weight[layer_index], local_rows) + out_bias[layer_index]
        )
        post_out, post_normal, post_factor = norm_local(
            branch, ln_post_gain[layer_index], ln_post_bias[layer_index]
        )
        middle = residual + post_out
        ffn_in, ffn_normal, ffn_factor = norm_local(
            middle, ln_ffn_gain[layer_index], ln_ffn_bias[layer_index]
        )
        ffn_rows = collect_rows(ffn_in.astype(jnp.bfloat16))
        before_gelu = (
            jnp.dot(ffn_rows, fc1_weight[layer_index], preferred_element_type=jnp.float32)
            + fc1_bias[layer_index]
        )
        activated = jax.nn.gelu(before_gelu, approximate=False)
        first_sum, second_sum = hidden_stats(
            jnp.sum(activated, axis=1), jnp.sum(activated * activated, axis=1)
        )
        average = first_sum / hidden_all
        spread = second_sum / hidden_all - average * average
        hidden_factor = lax.rsqrt(spread + epsilon)[:, None]
        hidden_normal = (activated - average[:, None]) * hidden_factor
        mixed_b = (hidden_normal * mid_gain[layer_index] + mid_bias[layer_index]).astype(
            jnp.bfloat16
        )
        ffn_out = reduce_branch(mixed_b, fc2_weight[layer_index], local_rows)
        stored.append(
            (
                attn_normal,
                attn_factor,
                attn_rows,
                queries,
                key_rows,
                value_rows,
                attended,
                log_totals,
                pair_scale,
                scaled_mine,
                post_normal,
                post_factor,
                ffn_normal,
                ffn_factor,
                ffn_rows,
                before_gelu,
                hidden_normal,
                hidden_factor,
                mixed_b,
            )
        )
        residual = middle + ffn_out + fc2_bias[layer_index]
    layer_output = residual.astype(jnp.bfloat16)
    gradient = cotangent.astype(jnp.float32)
    sharded_list = []
    shared_list = []
    for layer_index in reversed(range(layers)):
        (
            attn_normal,
            attn_factor,
            attn_rows,
            queries,
            key_rows,
            value_rows,
            attended,
            log_totals,
            pair_scale,
            scaled_mine,
            post_normal,
            post_factor,
            ffn_normal,
            ffn_factor,
            ffn_rows,
            before_gelu,
            hidden_normal,
            hidden_factor,
            mixed_b,
        ) = stored[layer_index]
        qkv_here = qkv_weight[layer_index].reshape(model_width, 3 * cols_here)
        second_shift_grad = jnp.sum(gradient, axis=0)
        grad_rows = collect_grads(gradient.astype(jnp.bfloat16))
        mixed_grad = jnp.einsum(
            "td,fd->tf", grad_rows, fc2_weight[layer_index], preferred_element_type=jnp.float32
        )
        second_grad = jnp.einsum(
            "tf,td->fd", mixed_b, grad_rows, preferred_element_type=jnp.float32
        )
        hidden_gain_grad = jnp.sum(mixed_grad * hidden_normal, axis=0)
        hidden_shift_grad = jnp.sum(mixed_grad, axis=0)
        normal_grad = mixed_grad * mid_gain[layer_index]
        grad_first, grad_second = hidden_grad_stats(
            jnp.sum(normal_grad, axis=1), jnp.sum(normal_grad * hidden_normal, axis=1)
        )
        active_grad = hidden_factor * (
            normal_grad
            - grad_first[:, None] / hidden_all
            - hidden_normal * grad_second[:, None] / hidden_all
        )
        gelu_pull = jax.vjp(partial(jax.nn.gelu, approximate=False), before_gelu)[1]
        pre_grad_b = gelu_pull(active_grad)[0].astype(jnp.bfloat16)
        first_shift_grad = jnp.sum(pre_grad_b, axis=0, dtype=jnp.float32)
        first_grad = jnp.einsum(
            "td,tf->df", ffn_rows, pre_grad_b, preferred_element_type=jnp.float32
        )
        ffn_in_grad = reduce_grads(pre_grad_b, fc1_weight[layer_index], local_rows)
        ffn_gain_grad = jnp.sum(ffn_in_grad * ffn_normal, axis=0)
        ffn_bias_grad = jnp.sum(ffn_in_grad, axis=0)
        middle_grad = gradient + norm_back(
            ffn_in_grad, ffn_normal, ffn_factor, ln_ffn_gain[layer_index]
        )
        post_gain_grad = jnp.sum(middle_grad * post_normal, axis=0)
        post_bias_grad = jnp.sum(middle_grad, axis=0)
        branch_grad = norm_back(middle_grad, post_normal, post_factor, ln_post_gain[layer_index])
        out_shift_grad = jnp.sum(branch_grad, axis=0)
        branch_rows = collect_grads(branch_grad.astype(jnp.bfloat16))
        scaled_grad = jnp.einsum(
            "td,cd->tc", branch_rows, out_weight[layer_index], preferred_element_type=jnp.float32
        )
        out_grad = jnp.einsum(
            "tc,td->cd", scaled_mine, branch_rows, preferred_element_type=jnp.float32
        )
        grad_send = lax.dynamic_slice_in_dim(scaled_grad, other_start, half_rows, 0)
        grad_recv = partner(grad_send.astype(jnp.bfloat16), "mp", 0).astype(grad_send.dtype)
        grad_own = lax.dynamic_slice_in_dim(scaled_grad, own_start, half_rows, 0)
        scaled_pair = join_cols(grad_own, grad_recv, is_upper).reshape(
            half_rows, pair_heads, head_width
        )
        pair_scale_grad = jnp.sum(attended * scaled_pair, axis=(0, 2))
        scale_grad = jnp.sum(pair_onehot * pair_scale_grad[:, None], axis=0)
        attended_grad_b = (scaled_pair * pair_scale[None, :, None]).astype(jnp.bfloat16)
        query_grad, key_grad, value_grad = attend_backward(
            queries, key_rows, value_rows, segment_ids, own_start, log_totals, attended_grad_b
        )
        query_own, query_other = split_cols(
            query_grad.reshape(half_rows, pair_cols), cols_here, is_upper
        )
        key_own, key_other = split_cols(
            key_grad.reshape(group_rows, pair_cols), cols_here, is_upper
        )
        value_own, value_other = split_cols(
            value_grad.reshape(group_rows, pair_cols), cols_here, is_upper
        )
        query_recv, key_recv, value_recv = (
            partner(query_other.astype(jnp.bfloat16), "mp", 0).astype(query_other.dtype),
            partner(key_other.astype(jnp.bfloat16), "mp", 0).astype(key_other.dtype),
            partner(value_other.astype(jnp.bfloat16), "mp", 0).astype(value_other.dtype),
        )
        query_grad_b = join_rows(query_own, query_recv, is_upper).astype(jnp.bfloat16)
        key_grad_b = (key_own + key_recv).astype(jnp.bfloat16)
        value_grad_b = (value_own + value_recv).astype(jnp.bfloat16)
        proj_grad = jnp.stack([query_grad_b, key_grad_b, value_grad_b], axis=1).reshape(
            -1, 3 * cols_here
        )
        pair_grad = jnp.stack(
            [
                jnp.sum(query_grad_b, axis=0, dtype=jnp.float32),
                jnp.sum(value_grad_b, axis=0, dtype=jnp.float32),
            ],
            axis=0,
        )
        qkv_grad = jnp.einsum(
            "td,tc->dc", attn_rows, proj_grad, preferred_element_type=jnp.float32
        ).reshape(model_width, 3, cols_here)
        attn_in_grad = reduce_grads(proj_grad, qkv_here, local_rows)
        attn_gain_grad = jnp.sum(attn_in_grad * attn_normal, axis=0)
        attn_bias_grad = jnp.sum(attn_in_grad, axis=0)
        gradient = middle_grad + norm_back(
            attn_in_grad, attn_normal, attn_factor, ln_attn_gain[layer_index]
        )
        sharded_list.insert(
            0,
            (
                qkv_grad,
                pair_grad,
                out_grad,
                first_grad,
                first_shift_grad,
                hidden_gain_grad,
                hidden_shift_grad,
                second_grad,
            ),
        )
        shared_list.insert(
            0,
            (
                attn_gain_grad,
                attn_bias_grad,
                scale_grad,
                out_shift_grad,
                post_gain_grad,
                post_bias_grad,
                ffn_gain_grad,
                ffn_bias_grad,
                second_shift_grad,
            ),
        )
    sharded = stack_layers(sharded_list, 8)
    shared = stack_layers(shared_list, 9)
    sharded = (
        lax.psum(sharded[0].astype(jnp.bfloat16), "rows").astype(jnp.float32),
        lax.psum(sharded[1].astype(jnp.bfloat16), "rows").astype(jnp.float32),
        lax.psum(sharded[2].astype(jnp.bfloat16), "rows").astype(jnp.float32),
        lax.psum(sharded[3].astype(jnp.bfloat16), "rows").astype(jnp.float32),
        lax.psum(sharded[4].astype(jnp.bfloat16), "rows").astype(jnp.float32),
        lax.psum(sharded[5].astype(jnp.bfloat16), "rows").astype(jnp.float32),
        lax.psum(sharded[6].astype(jnp.bfloat16), "rows").astype(jnp.float32),
        lax.psum(sharded[7].astype(jnp.bfloat16), "rows").astype(jnp.float32),
    )
    shared = lax.psum(
        (
            shared[0],
            shared[1],
            shared[2],
            shared[3],
            shared[4],
            shared[5],
            shared[6],
            shared[7],
            shared[8],
        ),
        ("rows", "mp"),
    )
    return (
        layer_output,
        gradient,
        shared[0],
        shared[1],
        sharded[0],
        sharded[1],
        shared[2],
        sharded[2],
        shared[3],
        shared[4],
        shared[5],
        shared[6],
        shared[7],
        sharded[3],
        sharded[4],
        sharded[5],
        sharded[6],
        sharded[7],
        shared[8],
    )


MESH_ID = pl.DeviceIdType.MESH
PLANE = ("core", "y", "x")
EVERY = ("y", "core", "z", "x")
f32 = jnp.float32
bf16 = jnp.bfloat16


def vmem_params(collective_id=None, mib=24):
    if collective_id is None:
        return pltpu.CompilerParams(vmem_limit_bytes=mib * 2**20)
    return pltpu.CompilerParams(
        vmem_limit_bytes=mib * 2**20, collective_id=collective_id, has_side_effects=True
    )


class Here:
    def __init__(self):
        self.x, self.y = lax.axis_index("x"), lax.axis_index("y")
        self.core, self.z = lax.axis_index("core"), lax.axis_index("z")

    def peer(self, flip_x, flip_y, flip_core, step_z):
        place = {}
        if flip_x:
            place["x"] = 1 - self.x
        if flip_y:
            place["y"] = 1 - self.y
        if flip_core:
            place["core"] = 1 - self.core
        if step_z:
            place["z"] = lax.rem(self.z + step_z, 4)
        return place

    def block(self, at_core, at_x, at_y):
        return (2 * at_core + lax.rem(at_y + self.z, 2)) * 2 + at_x


BY_X, BY_Y, BY_CORE = (1, 0, 0, 0), (0, 1, 0, 0), (0, 0, 1, 0)
BY_Z = tuple((0, 0, 0, step) for step in (1, 2, 3))
BY_LINE = BY_Z + tuple((0, 0, 1, step) for step in range(4))
BY_PLANE = tuple((flip & 1, flip >> 1 & 1, flip >> 2, 0) for flip in range(1, 8))


def remote(source, target, send_sem, recv_sem, place):
    return pltpu.make_async_remote_copy(
        src_ref=source,
        dst_ref=target,
        send_sem=send_sem,
        recv_sem=recv_sem,
        device_id=place,
        device_id_type=MESH_ID,
    )


def dma_sems(count):
    return pltpu.SemaphoreType.DMA((count,))


class Task:
    arrays = ()
    spaces = ()
    outs = ()
    out_spaces = ()
    scratch = ()
    reach = ()

    def moment(self, name):
        pass

    def start(self, here, ins, outs, scratch):
        pass

    def at_moment(self, name, here, ins, outs, scratch):
        pass

    def finish(self, here, ins, outs, scratch):
        pass


def run_tasks(ids, *tasks):
    reach = []
    for task in tasks:
        reach += [way for way in task.reach if way not in reach]

    near = []
    for task in tasks:
        near += [space == pltpu.VMEM for space in task.spaces]
    arrays = [array for task in tasks for array in task.arrays]
    loaded = [i for i, each in enumerate(near) if each]

    def kernel(*refs):
        refs = list(refs)
        *refs, load_sem = refs
        held = refs[len(refs) - len(loaded) :]
        refs = refs[: len(refs) - len(loaded)]
        loads = []
        for slot, index in enumerate(loaded):
            loads.append(pltpu.make_async_copy(refs[index], held[slot], load_sem.at[slot]))
            loads[-1].start()
            refs[index] = held[slot]
        views = [[], [], []]
        for kind, name in enumerate(("arrays", "outs", "scratch")):
            for task in tasks:
                count = len(getattr(task, name))
                views[kind].append(refs[:count])
                refs = refs[count:]
        here = Here()
        barrier = pltpu.get_barrier_semaphore()
        for way in reach:
            pl.semaphore_signal(barrier, inc=1, device_id=here.peer(*way), device_id_type=MESH_ID)
        pl.semaphore_wait(barrier, len(reach))
        for each in loads:
            each.wait()
        for task, *held in zip(tasks, *views):
            task.start(here, *held)

        def moment(name):
            for task, *held in zip(tasks, *views):
                task.at_moment(name, here, *held)

        tasks[0].moment = moment
        for task, *held in zip(tasks, *views):
            task.finish(here, *held)

    results = pl.pallas_call(
        kernel,
        out_shape=[out for task in tasks for out in task.outs],
        in_specs=[pl.BlockSpec(memory_space=pltpu.HBM)] * len(arrays),
        out_specs=[pl.BlockSpec(memory_space=s) for task in tasks for s in task.out_spaces],
        scratch_shapes=[each for task in tasks for each in task.scratch]
        + [pltpu.VMEM(arrays[i].shape, arrays[i].dtype) for i in loaded]
        + [dma_sems(len(loaded))],
        compiler_params=vmem_params(next(ids), 60),
    )(*arrays)
    results = list(results)
    split = []
    for task in tasks:
        split.append(results[: len(task.outs)])
        results = results[len(task.outs) :]
    return split


class PlaneMove(Task):
    def __init__(self, values, back=False, when="midway"):
        self.back, self.when = back, when
        self.arrays, self.spaces = (values,), (pltpu.HBM,)
        self.outs = (jax.ShapeDtypeStruct(values.shape, values.dtype),)
        self.out_spaces = (pltpu.HBM,)
        self.scratch = (
            pltpu.VMEM(values.shape, values.dtype),
            dma_sems(3),
            dma_sems(2),
        )
        self.reach = (BY_Y,) + BY_LINE

    def bend(self, here):
        return lax.rem(here.z + here.core, 2) == here.y

    def ends(self, here):
        targets = [{"core": here.z // 2, "z": 2 * y + here.core} for y in range(2)]
        at_home = [(here.z // 2 == here.core) & (2 * y + here.core == here.z) for y in range(2)]
        origin_core = lax.rem(here.z, 2)
        origin_z = 2 * here.core + lax.rem(here.y + origin_core, 2)
        origin_home = (origin_core == here.core) & (origin_z == here.z)
        return targets, at_home, {"core": origin_core, "z": origin_z}, origin_home

    def plan(self, here, ins, outs, scratch):
        held, send, recv = scratch
        targets, at_home, origin, origin_home = self.ends(here)
        bend = self.bend(here)
        away_from = jnp.logical_not
        to_y = here.peer(*BY_Y)
        first, second = [], []
        if not self.back:
            over = remote(ins[0], held, send.at[2], recv.at[0], to_y)
            first.append((away_from(bend), over, True))
            for y in range(2):
                for legs, source, when in (
                    (first, ins[0], bend & (here.y == y)),
                    (second, held, bend & (here.y != y)),
                ):
                    away = remote(source, outs[0], send.at[y], recv.at[1], targets[y])
                    stay = pltpu.make_async_copy(source, outs[0], recv.at[1])
                    legs.append((when & away_from(at_home[y]), away, True))
                    legs.append((when & at_home[y], stay, False))
        else:
            ends_there = here.z // 2 == here.y
            for goes_on, target, slot in ((False, outs[0], 1), (True, held, 0)):
                when = away_from(ends_there) if goes_on else ends_there
                away = remote(ins[0], target, send.at[int(goes_on)], recv.at[slot], origin)
                stay = pltpu.make_async_copy(ins[0], target, recv.at[slot])
                first.append((when & away_from(origin_home), away, True))
                first.append((when & origin_home, stay, False))
            over = remote(held, outs[0], send.at[2], recv.at[1], to_y)
            second.append((bend, over, True))
        return first, second

    def start(self, here, ins, outs, scratch):
        for when, copy, _ in self.plan(here, ins, outs, scratch)[0]:
            pl.when(when)(copy.start)

    def at_moment(self, name, here, ins, outs, scratch):
        if name == self.when:
            held, _, recv = scratch

            @pl.when(self.bend(here))
            def _():
                pltpu.make_async_copy(held, held, recv.at[0]).wait()

            for when, copy, _ in self.plan(here, ins, outs, scratch)[1]:
                pl.when(when)(copy.start)

    def finish(self, here, ins, outs, scratch):
        self.at_moment("end", here, ins, outs, scratch)
        pltpu.make_async_copy(outs[0], outs[0], scratch[2].at[1]).wait()
        for legs in self.plan(here, ins, outs, scratch):
            for when, copy, is_remote in legs:
                if is_remote:
                    pl.when(when)(copy.wait_send)


class PlaneGather(Task):
    def __init__(self, block):
        rows, width = block.shape
        self.arrays, self.spaces = (block,), (pltpu.VMEM,)
        self.outs = (jax.ShapeDtypeStruct((8 * rows, width), block.dtype),)
        self.out_spaces = (pltpu.VMEM,)
        self.scratch = (dma_sems(11), dma_sems(11), pltpu.SemaphoreType.DMA)
        self.reach = (BY_X, BY_Y, BY_CORE)

    def place(self, here, o_ref, at_x, at_y, part=None):
        rows = o_ref.shape[0] // 8
        first = here.block(here.core, at_x, at_y) * rows
        if part is None:
            return o_ref.at[pl.ds(pl.multiple_of(first, rows), rows)]
        half = rows // 2
        return o_ref.at[pl.ds(pl.multiple_of(first + part * half, half), half)]

    def copies(self, here, x_ref, o_ref, send_sem, recv_sem):
        x, y = here.x, here.y
        half = x_ref.shape[0] // 2
        to_x, to_y, to_core = here.peer(*BY_X), here.peer(*BY_Y), here.peer(*BY_CORE)

        def copy(index, source, target, way):
            return remote(source, target, send_sem.at[index], recv_sem.at[index], way)

        def pass_on(index, way, *at):
            return copy(index, self.place(here, o_ref, *at), self.place(here, o_ref, *at), way)

        own = [self.place(here, o_ref, x, y, part) for part in (0, 1)]
        mine = [x_ref.at[pl.ds(part * half, half)] for part in (0, 1)]
        return [
            copy(0, mine[0], own[0], to_x),
            copy(1, mine[1], own[1], to_y),
            copy(2, mine[1], own[1], to_x),
            copy(3, mine[0], own[0], to_y),
            copy(4, x_ref, self.place(here, o_ref, x, y), to_core),
            pass_on(5, to_y, 1 - x, y, 0),
            pass_on(6, to_x, x, 1 - y, 1),
            pass_on(7, to_core, 1 - x, y),
            pass_on(8, to_core, x, 1 - y),
            pass_on(9, to_core, 1 - x, 1 - y, 0),
            pass_on(10, to_core, 1 - x, 1 - y, 1),
        ]

    def keep(self, here, x_ref, o_ref, own_sem):
        return pltpu.make_async_copy(x_ref, self.place(here, o_ref, here.x, here.y), own_sem)

    def start(self, here, ins, outs, scratch):
        copies = self.copies(here, ins[0], outs[0], scratch[0], scratch[1])
        for index in range(5):
            copies[index].start()
        self.keep(here, ins[0], outs[0], scratch[2]).start()

    def finish(self, here, ins, outs, scratch, work=None, moment=None):
        rows = ins[0].shape[0]
        copies = self.copies(here, ins[0], outs[0], scratch[0], scratch[1])

        def done(flip_core, flip_x, flip_y):
            if work is not None:
                at_core = 1 - here.core if flip_core else here.core
                at_x = 1 - here.x if flip_x else here.x
                at_y = 1 - here.y if flip_y else here.y
                work(pl.multiple_of(here.block(at_core, at_x, at_y) * rows, rows))

        self.keep(here, ins[0], outs[0], scratch[2]).wait()
        done(0, 0, 0)
        copies[4].wait_recv()
        done(1, 0, 0)
        for index in range(4):
            copies[index].wait_recv()
            copies[5 + index].start()
        if moment is not None:
            moment("spare")
        done(0, 1, 0)
        done(0, 0, 1)
        copies[7].wait_recv()
        done(1, 1, 0)
        copies[8].wait_recv()
        done(1, 0, 1)
        copies[5].wait_recv()
        copies[9].start()
        copies[6].wait_recv()
        copies[10].start()
        done(0, 1, 1)
        if moment is not None:
            moment("soon")
        copies[9].wait_recv()
        copies[10].wait_recv()
        done(1, 1, 1)
        for each in copies:
            each.wait_send()


class OrderedGather(PlaneGather):
    def ends(self, here):
        over_x = here.core == 0
        first = (jnp.where(over_x, 1 - here.x, here.x), jnp.where(over_x, here.y, 1 - here.y))
        second = (jnp.where(over_x, here.x, 1 - here.x), jnp.where(over_x, 1 - here.y, here.y))
        return first, second

    def copies(self, here, x_ref, o_ref, send_sem, recv_sem):
        half = x_ref.shape[0] // 2
        first, second = self.ends(here)
        to_first, to_second = ({"x": at[0], "y": at[1]} for at in (first, second))
        to_core = here.peer(*BY_CORE)

        def copy(index, source, target, way):
            return remote(source, target, send_sem.at[index], recv_sem.at[index], way)

        def pass_on(index, way, *at):
            return copy(index, self.place(here, o_ref, *at), self.place(here, o_ref, *at), way)

        own = [self.place(here, o_ref, here.x, here.y, part) for part in (0, 1)]
        mine = [x_ref.at[pl.ds(part * half, half)] for part in (0, 1)]
        far = (1 - here.x, 1 - here.y)
        return [
            copy(0, mine[0], own[0], to_first),
            copy(1, mine[1], own[1], to_first),
            copy(2, mine[1], own[1], to_second),
            copy(3, mine[0], own[0], to_second),
            copy(4, x_ref, self.place(here, o_ref, here.x, here.y), to_core),
            pass_on(5, to_second, *first, 0),
            pass_on(6, to_first, *second, 1),
            pass_on(7, to_core, *first),
            pass_on(8, to_core, *second),
            pass_on(9, to_core, *far, 0),
            pass_on(10, to_core, *far, 1),
        ]

    def start(self, here, ins, outs, scratch):
        copies = self.copies(here, ins[0], outs[0], scratch[0], scratch[1])
        for index in (0, 1, 4):
            copies[index].start()
        self.keep(here, ins[0], outs[0], scratch[2]).start()

    def finish(self, here, ins, outs, scratch, work=None, moment=None):
        rows = ins[0].shape[0]
        copies = self.copies(here, ins[0], outs[0], scratch[0], scratch[1])
        first, second = self.ends(here)
        far = (1 - here.x, 1 - here.y)

        def done(at_core, at):
            if work is not None:
                work(pl.multiple_of(here.block(at_core, *at) * rows, rows))

        self.keep(here, ins[0], outs[0], scratch[2]).wait()
        done(here.core, (here.x, here.y))
        copies[0].wait_send()
        copies[1].wait_send()
        copies[2].start()
        copies[3].start()
        copies[4].wait_recv()
        done(1 - here.core, (here.x, here.y))
        copies[0].wait_recv()
        copies[5].start()
        copies[1].wait_recv()
        copies[7].start()
        done(here.core, first)
        copies[7].wait_recv()
        done(1 - here.core, second)
        copies[2].wait_recv()
        copies[6].start()
        copies[3].wait_recv()
        copies[8].start()
        if moment is not None:
            moment("spare")
        done(here.core, second)
        copies[8].wait_recv()
        done(1 - here.core, first)
        copies[5].wait_recv()
        copies[9].start()
        copies[6].wait_recv()
        copies[10].start()
        done(here.core, far)
        if moment is not None:
            moment("soon")
        copies[9].wait_recv()
        copies[10].wait_recv()
        done(1 - here.core, far)
        for each in copies[2:]:
            each.wait_send()


class PlaneScatter(Task):
    def __init__(self, rows, width, weight_dim):
        half = rows // 2
        self.weight_dim = weight_dim
        self.scratch = (
            pltpu.VMEM((4, rows, width), bf16),
            pltpu.VMEM((4, rows, width), bf16),
            pltpu.VMEM((rows, width), bf16),
            pltpu.VMEM((2, half, width), bf16),
            pltpu.VMEM((2, half, width), bf16),
            pltpu.VMEM((2, half, width), bf16),
            pltpu.VMEM((2, half, width), bf16),
            pltpu.VMEM((2, half, width), bf16),
            pltpu.VMEM((half, width), f32),
            pltpu.VMEM((half, width), f32),
            dma_sems(10),
            dma_sems(10),
        )
        self.reach = (BY_X, BY_Y, BY_CORE)

    def finish(self, here, ins, outs, scratch, rows_of, weight_of, early=None, idle=None):
        o_ref = outs[0]
        (
            sib_out,
            sib_in,
            diag_out,
            diag_in,
            last_x_out,
            last_y_out,
            last_x_in,
            last_y_in,
            wait_x,
            wait_y,
            send_sem,
            recv_sem,
        ) = scratch
        rows = o_ref.shape[0]
        half = rows // 2
        x, y, core = here.x, here.y, here.core
        to_x, to_y, to_core = here.peer(*BY_X), here.peer(*BY_Y), here.peer(*BY_CORE)

        def term(at_core, at_x, at_y):
            first = pl.multiple_of(here.block(at_core, at_x, at_y) * rows, rows)
            return lax.dot_general(
                rows_of(first),
                weight_of(),
                (((1,), (self.weight_dim,)), ((), ())),
                preferred_element_type=f32,
            )

        def copy(index, source, target, way):
            return remote(source, target, send_sem.at[index], recv_sem.at[index], way)

        places = ((1 - x, 1 - y), (1 - x, y), (x, 1 - y), (x, y))
        siblings = [copy(i, sib_out.at[i], sib_in.at[i], to_core) for i in range(4)]

        def help_sibling(i):
            sib_out[i] = term(1 - core, *places[i]).astype(bf16)
            siblings[i].start()

        def joined(i):
            mine = term(core, *places[i])
            siblings[i].wait_recv()
            return mine + sib_in[i].astype(f32)

        help_sibling(0)
        total = joined(0)
        diag_out[...] = total.astype(bf16)
        diag_x = copy(4, diag_out.at[pl.ds(0, half)], diag_in.at[0], to_x)
        diag_y = copy(5, diag_out.at[pl.ds(half, half)], diag_in.at[1], to_y)
        diag_x.start()
        diag_y.start()
        help_sibling(1)
        total = joined(1)
        last_x_out[0] = total[:half].astype(bf16)
        x_0 = copy(6, last_x_out.at[0], last_x_in.at[0], to_x)
        x_0.start()
        wait_x[...] = total[half:]
        if early is not None:
            early()
        help_sibling(2)
        total = joined(2)
        last_y_out[1] = total[half:].astype(bf16)
        y_1 = copy(7, last_y_out.at[1], last_y_in.at[1], to_y)
        y_1.start()
        wait_y[...] = total[:half]
        help_sibling(3)
        diag_y.wait_recv()
        last_x_out[1] = (wait_x[...] + diag_in[1].astype(f32)).astype(bf16)
        x_1 = copy(8, last_x_out.at[1], last_x_in.at[1], to_x)
        x_1.start()
        diag_x.wait_recv()
        last_y_out[0] = (wait_y[...] + diag_in[0].astype(f32)).astype(bf16)
        y_0 = copy(9, last_y_out.at[0], last_y_in.at[0], to_y)
        y_0.start()
        o_ref[...] = joined(3)
        if idle is not None:
            idle()
        for part, (by_x, by_y) in enumerate(((x_0, y_0), (x_1, y_1))):
            by_x.wait_recv()
            by_y.wait_recv()
            piece = pl.ds(part * half, half)
            o_ref[piece, :] += last_x_in[part].astype(f32) + last_y_in[part].astype(f32)
        for sent in (*siblings, diag_x, diag_y, x_0, y_1, x_1, y_0):
            sent.wait_send()


class PlaneSum(Task):
    def __init__(self, values):
        self.arrays, self.spaces = (values,), (pltpu.VMEM,)
        self.outs = (jax.ShapeDtypeStruct(values.shape, f32),)
        self.out_spaces = (pltpu.VMEM,)
        self.scratch = (pltpu.VMEM((7, *values.shape), f32), dma_sems(7), dma_sems(7))
        self.reach = BY_PLANE

    def copies(self, here, ins, scratch):
        got, send_sem, recv_sem = scratch
        return [
            remote(ins[0], got.at[i], send_sem.at[i], recv_sem.at[i], here.peer(*way))
            for i, way in enumerate(BY_PLANE)
        ]

    def start(self, here, ins, outs, scratch):
        for each in self.copies(here, ins, scratch):
            each.start()

    def finish(self, here, ins, outs, scratch):
        copies = self.copies(here, ins, scratch)
        for each in copies:
            each.wait_recv()
        got = scratch[0]
        by_x = [ins[0][...] + got[0]]
        for flip in (2, 4, 6):
            by_x.append(got[flip - 1] + got[flip])
        outs[0][...] = (by_x[0] + by_x[1]) + (by_x[2] + by_x[3])
        for each in copies:
            each.wait_send()


class LineGather(Task):
    def __init__(self, values):
        self.arrays, self.spaces = (values,), (pltpu.HBM,)
        self.outs = (jax.ShapeDtypeStruct((4, *values.shape), values.dtype),)
        self.out_spaces = (pltpu.HBM,)
        self.scratch = (dma_sems(4), dma_sems(3))
        self.reach = BY_Z

    def copies(self, here, ins, outs, scratch):
        target = outs[0].at[here.z]
        keep = pltpu.make_async_copy(ins[0], target, scratch[0].at[3])
        return keep, [
            remote(ins[0], target, scratch[0].at[i], scratch[1].at[i], here.peer(*way))
            for i, way in enumerate(BY_Z)
        ]

    def start(self, here, ins, outs, scratch):
        keep, copies = self.copies(here, ins, outs, scratch)
        for each in copies:
            each.start()
        keep.start()

    def finish(self, here, ins, outs, scratch):
        keep, copies = self.copies(here, ins, outs, scratch)
        for each in copies:
            each.wait()
        keep.wait()


class HeadGather(Task):
    def __init__(self, qkv, out, layer, when="start"):
        _, kinds, both, width = qkv.shape
        self.layer, self.when = layer, when
        self.arrays, self.spaces = (qkv, out), (pltpu.HBM,) * 2
        self.outs = (jax.ShapeDtypeStruct((kinds + 1, 2, both // 2, width), qkv.dtype),)
        self.out_spaces = (pltpu.HBM,)
        self.scratch = (dma_sems(8), dma_sems(8))
        self.reach = BY_LINE

    def pieces(self, outs, shard, part):
        half = outs[0].shape[3] // 2
        columns = pl.ds(pl.multiple_of(part * half, half), half)
        return outs[0].at[pl.ds(0, 3), shard, :, columns], outs[0].at[3, shard, :, columns]

    def copies(self, here, ins, outs, scratch):
        shard, target_core = lax.rem(here.z, 2), here.z // 2
        wide, half = outs[0].shape[2], outs[0].shape[3] // 2
        rows = pl.ds(pl.multiple_of(here.y * wide, wide), wide)
        columns = pl.ds(pl.multiple_of(here.core * half, half), half)
        sources = (ins[0].at[self.layer, :, rows, columns], ins[1].at[self.layer, rows, columns])
        targets = self.pieces(outs, shard, here.core)
        keeps, aways = [], []
        for kind in range(2):
            recv_sem = scratch[1].at[4 * kind + 2 * shard + here.core]
            keeps.append(pltpu.make_async_copy(sources[kind], targets[kind], recv_sem))
            for step in range(4):
                place = {"core": target_core, "z": lax.rem(here.z + step, 4)}
                send_sem = scratch[0].at[4 * kind + step]
                aways.append(remote(sources[kind], targets[kind], send_sem, recv_sem, place))
        return keeps, aways

    def begin(self, here, ins, outs, scratch):
        keeps, aways = self.copies(here, ins, outs, scratch)
        for index, each in enumerate(aways):
            if index % 4:
                each.start()
        at_home = here.z // 2 == here.core
        for kind in range(2):
            pl.when(at_home)(keeps[kind].start)
            pl.when(jnp.logical_not(at_home))(aways[4 * kind].start)

    def start(self, *held):
        self.at_moment("start", *held)

    def at_moment(self, name, *held):
        if name == self.when:
            self.begin(*held)

    def arrive(self, kind, outs, scratch):
        for shard in range(2):
            for part in range(2):
                piece = self.pieces(outs, shard, part)[kind]
                recv_sem = scratch[1].at[4 * kind + 2 * shard + part]
                pltpu.make_async_copy(piece, piece, recv_sem).wait()

    def sent(self, here, ins, outs, scratch):
        keeps, aways = self.copies(here, ins, outs, scratch)
        for index, each in enumerate(aways):
            if index % 4:
                each.wait_send()
        for kind in range(2):
            pl.when(here.z // 2 != here.core)(aways[4 * kind].wait_send)

    def finish(self, here, ins, outs, scratch):
        for kind in range(2):
            self.arrive(kind, outs, scratch)
        self.sent(here, ins, outs, scratch)


class LineScatter(Task):
    def __init__(self, values):
        shape = values.shape[1:]
        self.arrays, self.spaces = (values,), (pltpu.VMEM,)
        self.outs, self.out_spaces = (jax.ShapeDtypeStruct(shape, values.dtype),), (pltpu.VMEM,)
        self.scratch = (pltpu.VMEM((3, *shape), values.dtype), dma_sems(3), dma_sems(3))
        self.reach = BY_Z

    def copies(self, here, ins, scratch):
        got, send_sem, recv_sem = scratch
        return [
            remote(
                ins[0].at[lax.rem(here.z + i + 1, 4)],
                got.at[i],
                send_sem.at[i],
                recv_sem.at[i],
                here.peer(*way),
            )
            for i, way in enumerate(BY_Z)
        ]

    def start(self, here, ins, outs, scratch):
        for each in self.copies(here, ins, scratch):
            each.start()

    def finish(self, here, ins, outs, scratch):
        copies = self.copies(here, ins, scratch)
        for each in copies:
            each.wait_recv()
        total = ins[0][here.z].astype(f32)
        for i in range(3):
            total = total + scratch[0][i].astype(f32)
        outs[0][...] = total.astype(outs[0].dtype)
        for each in copies:
            each.wait_send()


class HeadScatter(Task):
    def __init__(self, values):
        kinds, _, wide, width = values.shape
        shape = (kinds, wide, width // 2)
        self.arrays, self.spaces = (values,), (pltpu.VMEM,)
        self.outs, self.out_spaces = (jax.ShapeDtypeStruct(shape, values.dtype),), (pltpu.VMEM,)
        self.scratch = (pltpu.VMEM((4, *shape), values.dtype), dma_sems(4), dma_sems(4))
        self.reach = BY_LINE

    def copies(self, here, ins, scratch):
        got, send_sem, recv_sem = scratch
        half = ins[0].shape[3] // 2
        triples = []
        for shard in range(2):
            for part in range(2):
                source = ins[0].at[:, shard, :, pl.ds(part * half, half)]
                target_z = 2 * here.core + shard
                slot = recv_sem.at[here.z]
                away = remote(
                    source,
                    got.at[here.z],
                    send_sem.at[2 * shard + part],
                    slot,
                    {"core": part, "z": target_z},
                )
                stay = pltpu.make_async_copy(source, got.at[here.z], slot)
                at_home = (target_z == here.z) & (here.core == part)
                triples.append((away, stay, at_home))
        return triples

    def start(self, here, ins, outs, scratch):
        for away, stay, at_home in self.copies(here, ins, scratch):
            pl.when(at_home)(stay.start)
            pl.when(jnp.logical_not(at_home))(away.start)

    def finish(self, here, ins, outs, scratch):
        got, send_sem, recv_sem = scratch
        for plane in range(4):
            pltpu.make_async_copy(got.at[plane], got.at[plane], recv_sem.at[plane]).wait()
        total = got[0].astype(f32)
        for plane in range(1, 4):
            total = total + got[plane].astype(f32)
        outs[0][...] = total.astype(outs[0].dtype)
        for away, stay, at_home in self.copies(here, ins, scratch):
            pl.when(jnp.logical_not(at_home))(away.wait_send)


class RowsGather(Task):
    def __init__(self, values, when="start"):
        self.when = when
        self.arrays, self.spaces = (values,), (pltpu.HBM,)
        self.outs = (jax.ShapeDtypeStruct((4, *values.shape), values.dtype),)
        self.out_spaces = (pltpu.HBM,)
        self.scratch = (dma_sems(4), dma_sems(3))
        self.reach = (BY_Y, BY_CORE)

    def copies(self, here, ins, outs, scratch):
        send_sem, recv_sem = scratch
        own = outs[0].at[2 * here.y + here.core]
        over = outs[0].at[2 * (1 - here.y) + here.core]
        to_y, to_core = here.peer(*BY_Y), here.peer(*BY_CORE)
        return (
            pltpu.make_async_copy(ins[0], own, send_sem.at[3]),
            remote(ins[0], own, send_sem.at[0], recv_sem.at[0], to_y),
            remote(ins[0], own, send_sem.at[1], recv_sem.at[1], to_core),
            remote(over, over, send_sem.at[2], recv_sem.at[2], to_core),
        )

    def start(self, *held):
        self.at_moment("start", *held)

    def at_moment(self, name, *held):
        if name == self.when:
            self.begin(*held)

    def begin(self, here, ins, outs, scratch):
        keep, by_y, by_core, again = self.copies(here, ins, outs, scratch)
        by_y.start()
        by_core.start()
        keep.start()

    def finish(self, here, ins, outs, scratch):
        keep, by_y, by_core, again = self.copies(here, ins, outs, scratch)
        by_y.wait_recv()
        again.start()
        by_core.wait_recv()
        again.wait_recv()
        for each in (by_y, by_core, again):
            each.wait_send()
        keep.wait()


class StepSum(Task):
    def __init__(self, values):
        self.arrays, self.spaces = (values,), (pltpu.VMEM,)
        self.outs = (jax.ShapeDtypeStruct(values.shape, f32),)
        self.out_spaces = (pltpu.VMEM,)
        self.scratch = (
            pltpu.VMEM((2, *values.shape), f32),
            pltpu.VMEM((3, *values.shape), f32),
            dma_sems(3),
            dma_sems(3),
        )
        self.reach = (BY_X, BY_Y, BY_CORE)

    def leg(self, here, index, source, scratch):
        _, got, send_sem, recv_sem = scratch
        way = here.peer(*self.reach[index])
        return remote(source, got.at[index], send_sem.at[index], recv_sem.at[index], way)

    def start(self, here, ins, outs, scratch):
        self.leg(here, 0, ins[0], scratch).start()

    def at_moment(self, name, here, ins, outs, scratch):
        part, got = scratch[:2]
        if name == "midway":
            self.leg(here, 0, ins[0], scratch).wait()
            part[0] = ins[0][...] + got[0]
            self.leg(here, 1, part.at[0], scratch).start()
        if name == "closing":
            self.leg(here, 1, part.at[0], scratch).wait()
            part[1] = part[0] + got[1]
            self.leg(here, 2, part.at[1], scratch).start()

    def finish(self, here, ins, outs, scratch):
        part, got = scratch[:2]
        self.leg(here, 2, part.at[1], scratch).wait()
        outs[0][...] = part[1] + got[2]


class LineSum(Task):
    def __init__(self, values):
        self.arrays, self.spaces = (values,), (pltpu.VMEM,)
        self.outs = (jax.ShapeDtypeStruct(values.shape, f32),)
        self.out_spaces = (pltpu.VMEM,)
        self.scratch = (pltpu.VMEM((4, *values.shape), f32), dma_sems(3), dma_sems(4))
        self.reach = BY_Z

    def copies(self, here, ins, scratch):
        got, send_sem, recv_sem = scratch
        there, slot = got.at[here.z], recv_sem.at[here.z]
        keep = pltpu.make_async_copy(ins[0], there, slot)
        return keep, [
            remote(ins[0], there, send_sem.at[i], slot, here.peer(*way))
            for i, way in enumerate(BY_Z)
        ]

    def start(self, here, ins, outs, scratch):
        keep, copies = self.copies(here, ins, scratch)
        for each in copies:
            each.start()
        keep.start()

    def finish(self, here, ins, outs, scratch):
        got, _, recv_sem = scratch
        _, copies = self.copies(here, ins, scratch)
        for plane in range(4):
            pltpu.make_async_copy(got.at[plane], got.at[plane], recv_sem.at[plane]).wait()
        outs[0][...] = (got[0] + got[1]) + (got[2] + got[3])
        for each in copies:
            each.wait_send()


def to_columns(upper, lower):
    place = lax.broadcasted_iota(jnp.int32, (128, upper.shape[1]), 0)
    return jnp.transpose(jnp.where(place < 64, upper, lower))


def both_columns(upper, lower):
    lane = lax.broadcasted_iota(jnp.int32, (upper.shape[0], 128), 1)
    return jnp.where(lane < 64, upper, lower)


def in_chunks(rows, chunk, step):
    def one(index, carry):
        step(pl.multiple_of(index * chunk, chunk))
        return carry

    lax.fori_loop(0, rows // chunk, one, 0)


def fold(values):
    total = values[:8]
    for first in range(8, values.shape[0], 8):
        total = total + values[first : first + 8]
    return total


class Parts(Task):
    def use(self, parts):
        self.parts = parts
        self.scratch = list(self.scratch)
        self.at = {}
        reach = []
        for name, part in parts.items():
            self.at[name] = (len(self.scratch), len(self.scratch) + len(part.scratch))
            self.scratch += list(part.scratch)
            reach += [way for way in part.reach if way not in reach]
        self.reach = reach

    def held(self, scratch, name):
        first, last = self.at[name]
        return scratch[first:last]


def norm_pull(grad_out, normal, factor, gain_row):
    scaled = grad_out * gain_row
    width = scaled.shape[1]
    mean = jnp.sum(scaled, axis=1, keepdims=True) / width
    inner = jnp.sum(scaled * normal, axis=1, keepdims=True) / width
    return factor * (scaled - mean - normal * inner)


class StepThenLine(Parts):
    def __init__(self, values):
        self.arrays, self.spaces = (values,), (pltpu.VMEM,)
        self.outs = (jax.ShapeDtypeStruct(values.shape, f32),)
        self.out_spaces = (pltpu.VMEM,)
        self.scratch = (pltpu.VMEM(values.shape, f32),)
        self.use(dict(step=StepSum(values), line=LineSum(values)))

    def start(self, here, ins, outs, scratch):
        self.parts["step"].start(here, ins, scratch[:1], self.held(scratch, "step"))

    def at_moment(self, name, here, ins, outs, scratch):
        held = (here, ins, scratch[:1], self.held(scratch, "step"))
        self.parts["step"].at_moment(name, *held)
        if name == "tail":
            self.parts["step"].finish(*held)
            self.parts["line"].start(here, scratch[:1], outs, self.held(scratch, "line"))

    def finish(self, here, ins, outs, scratch):
        self.parts["line"].finish(here, scratch[:1], outs, self.held(scratch, "line"))


def normalize(values):
    width = values.shape[1]
    centered = values - jnp.sum(values, axis=1, keepdims=True) / width
    factor = lax.rsqrt(jnp.sum(centered * centered, axis=1, keepdims=True) / width + epsilon)
    return centered * factor, factor


def wide_column(column):
    return jnp.broadcast_to(column, (column.shape[0], 128))


def hidden_row(small_ref, layer, at, part):
    first = small_ref.shape[2] - (3 - at) * part
    return jnp.concatenate(
        [small_ref[z, layer : layer + 1, first : first + part] for z in range(4)], axis=1
    )


def scale_of(here, head_scale_ref, layer, wide):
    row = head_scale_ref[layer : layer + 1, :]
    place = lax.broadcasted_iota(jnp.int32, row.shape, 1)
    pair = []
    for i in range(2):
        head = ((2 * here.core + i) * 2 + here.x) * 2 + here.y
        pair.append(jnp.sum(jnp.where(place == head, row, 0.0), axis=1, keepdims=True))
    lane = lax.broadcasted_iota(jnp.int32, (1, 2 * wide), 1)
    return jnp.where(lane < wide, pair[0], pair[1])


NARROW = 128
CHUNK = 256


class FfnForward(Parts):
    def __init__(self, block, first, second, small, middle, shift, norm, layer, late):
        rows, width = block.shape
        hidden = first.shape[1]
        self.late, self.layer, self.last = late, layer, norm is None
        self.arrays = (block, first, second, small, middle, shift, *(norm or ()))
        self.spaces = (pltpu.VMEM,) * 2 + (pltpu.HBM if late else pltpu.VMEM,)
        self.spaces += (pltpu.VMEM,) * (len(self.arrays) - 3)
        self.outs = (
            jax.ShapeDtypeStruct((rows, width), f32),
            jax.ShapeDtypeStruct((8 * rows, width), bf16),
            jax.ShapeDtypeStruct((8 * rows, hidden), f32),
            jax.ShapeDtypeStruct((8 * rows, hidden), f32),
            jax.ShapeDtypeStruct((8 * rows, hidden), bf16),
            jax.ShapeDtypeStruct((2, 8 * rows), f32),
        )
        self.out_spaces = (pltpu.VMEM,) + (pltpu.HBM,) * 4 + (pltpu.VMEM,)
        self.outs += (jax.ShapeDtypeStruct((rows, width), bf16),)
        if norm:
            self.outs += (jax.ShapeDtypeStruct((rows, width), f32),)
            self.outs += (jax.ShapeDtypeStruct((rows, 128), f32),)
        self.out_spaces += (pltpu.VMEM,) * (len(self.outs) - 6)
        self.base = len(self.outs)
        self.scratch = (
            pltpu.VMEM((8 * rows, width), bf16),
            pltpu.VMEM((8 * rows, hidden), f32),
            pltpu.VMEM((8 * rows, hidden), f32),
            pltpu.VMEM((8 * rows, hidden), bf16),
            pltpu.VMEM((2, 8 * rows), f32),
            pltpu.VMEM((rows, 128), f32),
            dma_sems(4),
        )
        parts = dict(
            gather=PlaneGather(block),
            scatter=PlaneScatter(rows, width, 0),
            sums=PlaneSum(jax.ShapeDtypeStruct((2, 8 * rows), f32)),
        )
        if late:
            parts["second"] = WeightGather(second, layer, 0)
            self.outs += parts["second"].outs
            self.out_spaces += (pltpu.VMEM,)
        self.use(parts)

    def start(self, here, ins, outs, scratch):
        self.parts["gather"].start(here, ins[:1], scratch[:1], self.held(scratch, "gather"))
        if self.late:
            held = self.held(scratch, "second")
            self.parts["second"].start(here, ins[2:3], outs[self.base :], held)

    def finish(self, here, ins, outs, scratch):
        block_ref, first_ref, second_ref, small_ref, middle_ref, row_ref = ins[:6]
        part = first_ref.shape[1] // 4
        shift, gain, bias = (hidden_row(small_ref, self.layer, at, part) for at in range(3))
        out_ref, rows_out, slope_out, normal_out, mixed_out, total_ref = outs[:6]
        if self.late:
            second_ref = outs[self.base]
        rows_buf, before, active, mixed, sums, columns, save = scratch[:7]
        rows = block_ref.shape[0]
        hidden_all = 8 * first_ref.shape[1]

        def work(first):
            before[pl.ds(first, rows), :] = lax.dot_general(
                rows_buf[pl.ds(first, rows), :],
                first_ref[...],
                (((1,), (0,)), ((), ())),
                preferred_element_type=f32,
            )

            def step(at):
                piece = pl.ds(pl.multiple_of(first + at, CHUNK), CHUNK)
                u = before[piece, :] + shift
                area = 0.5 * (1.0 + lax.erf(u * 0.5**0.5))
                a = u * area
                active[piece, :] = a
                before[piece, :] = area + u * (jnp.exp(-0.5 * u * u) * (0.5 / jnp.pi) ** 0.5)
                columns[pl.ds(at, CHUNK), :] = both_columns(
                    jnp.sum(a, axis=1, keepdims=True), jnp.sum(a * a, axis=1, keepdims=True)
                )

            in_chunks(rows, CHUNK, step)
            turned = jnp.transpose(columns[...])
            sums[0:1, pl.ds(first, rows)] = turned[0:1]
            sums[1:2, pl.ds(first, rows)] = turned[64:65]

        self.parts["gather"].finish(
            here, ins[:1], scratch[:1], self.held(scratch, "gather"), work
        )
        held = self.held(scratch, "sums")
        self.parts["sums"].start(here, (sums,), None, held)
        keep_rows = pltpu.make_async_copy(rows_buf, rows_out, save.at[0])
        keep_rows.start()
        keep_slope = pltpu.make_async_copy(before, slope_out, save.at[1])
        keep_slope.start()
        self.parts["sums"].finish(here, (sums,), (total_ref,), held)
        if self.late:
            held = self.held(scratch, "second")
            self.parts["second"].finish(here, ins[2:3], outs[self.base :], held)
        self.moment("midway")

        def rows_of(first):
            average = total_ref[0:1, pl.ds(first, rows)] / hidden_all
            spread = total_ref[1:2, pl.ds(first, rows)] / hidden_all - average * average
            columns[...] = to_columns(average, lax.rsqrt(spread + epsilon))

            def step(at):
                piece = pl.ds(pl.multiple_of(first + at, CHUNK), CHUNK)
                pair = columns[pl.ds(at, CHUNK), :]
                normal = (active[piece, :] - pair[:, 0:1]) * pair[:, 64:65]
                active[piece, :] = normal
                mixed[piece, :] = (normal * gain + bias).astype(bf16)

            in_chunks(rows, CHUNK, step)
            return mixed[pl.ds(first, rows), :]

        keep_mixed = pltpu.make_async_copy(mixed, mixed_out, save.at[2])
        keep_normal = pltpu.make_async_copy(active, normal_out, save.at[3])

        def idle():
            keep_mixed.start()
            keep_normal.start()
            self.moment("closing")

        self.parts["scatter"].finish(
            here,
            None,
            (out_ref,),
            self.held(scratch, "scatter"),
            rows_of,
            lambda: second_ref[...],
            idle=idle,
        )
        layer = slice(self.layer, self.layer + 1)
        after = slice(self.layer + 1, self.layer + 2)

        def settle(at):
            piece = pl.ds(at, NARROW)
            residual = middle_ref[piece, :] + out_ref[piece, :] + row_ref[layer, :]
            out_ref[piece, :] = residual
            if self.last:
                outs[6][piece, :] = residual.astype(bf16)
            else:
                normal, factor = normalize(residual)
                outs[6][piece, :] = (normal * ins[6][after, :] + ins[7][after, :]).astype(bf16)
                outs[7][piece, :] = normal
                outs[8][piece, :] = wide_column(factor)

        in_chunks(rows, NARROW, settle)
        for each in (keep_rows, keep_slope, keep_mixed, keep_normal):
            each.wait()


class FfnBackward(Parts):
    def __init__(
        self,
        block,
        first,
        second,
        small,
        slope,
        normal,
        mixed,
        ffn_rows,
        totals,
        gradient,
        norms,
        layer,
    ):
        self.layer = layer
        rows, width = block.shape
        hidden = second.shape[0]
        self.arrays = (block, first, second, small, totals, slope, normal, mixed, ffn_rows)
        self.spaces = (pltpu.VMEM,) * 5 + (pltpu.HBM,) * 4
        self.arrays += (gradient, *norms)
        self.spaces += (pltpu.VMEM,) * 7
        self.outs = (
            jax.ShapeDtypeStruct((rows, width), f32),
            jax.ShapeDtypeStruct((4, width, hidden // 4), bf16),
            jax.ShapeDtypeStruct((hidden // 4, width), bf16),
            jax.ShapeDtypeStruct((3, hidden), f32),
            jax.ShapeDtypeStruct((rows, width), bf16),
            jax.ShapeDtypeStruct((8, width), f32),
        )
        self.out_spaces = (pltpu.VMEM,) * 6
        self.scratch = (
            pltpu.VMEM((8 * rows, width), bf16),
            pltpu.VMEM((8 * rows, hidden), f32),
            pltpu.VMEM((8 * rows, hidden), f32),
            pltpu.VMEM((8 * rows, hidden), f32),
            pltpu.VMEM((8 * rows, hidden), bf16),
            pltpu.VMEM((8 * rows, width), bf16),
            pltpu.VMEM((8 * rows, hidden), bf16),
            pltpu.VMEM((hidden, width), f32),
            pltpu.VMEM((2, 8 * rows), f32),
            pltpu.VMEM((2, 8 * rows), f32),
            pltpu.VMEM((rows, 128), f32),
            pltpu.VMEM((rows, 128), f32),
            pltpu.VMEM((3, 8, hidden), f32),
            dma_sems(4),
            pltpu.VMEM((4, hidden // 4, width), bf16),
            pltpu.VMEM((6, 8, width), f32),
        )
        self.use(
            dict(
            gather=PlaneGather(block),
            scatter=PlaneScatter(rows, width, 1),
            second=LineScatter(jax.ShapeDtypeStruct((4, hidden // 4, width), bf16)),
            sums=PlaneSum(jax.ShapeDtypeStruct((2, 8 * rows), f32)),
            )
        )

    def loads(self, ins, scratch):
        targets = (scratch[2], scratch[4], scratch[1], scratch[5])
        return [
            pltpu.make_async_copy(source, target, scratch[13].at[i])
            for i, (source, target) in enumerate(zip((ins[6], ins[7], ins[5], ins[8]), targets))
        ]

    def start(self, here, ins, outs, scratch):
        self.parts["gather"].start(here, ins[:1], scratch[:1], self.held(scratch, "gather"))
        for each in self.loads(ins, scratch):
            each.start()

    def finish(self, here, ins, outs, scratch):
        block_ref, first_ref, second_ref, hidden_ref, totals_ref = ins[:5]
        mid_gain = hidden_row(hidden_ref, self.layer, 1, first_ref.shape[1] // 4)
        out_ref, first_grad, second_quarter, small_ref, branch_ref, vector_ref = outs
        second_grad, vectors = scratch[14:16]
        (
            rows_buf,
            slope,
            normal_buf,
            grads,
            mixed,
            ffn_rows,
            pre_grad,
            second_sum,
            sums,
            got,
            columns,
            factors,
            small,
        ) = scratch[:13]
        rows = block_ref.shape[0]
        hidden_all = 8 * first_ref.shape[1]
        load_normal, load_mixed, load_slope, load_rows = self.loads(ins, scratch)
        load_normal.wait()
        load_mixed.wait()
        second_sum[...] = jnp.zeros_like(second_sum)
        small[...] = jnp.zeros_like(small)

        def factor_columns(first):
            average = totals_ref[0:1, pl.ds(first, rows)] / hidden_all
            spread = totals_ref[1:2, pl.ds(first, rows)] / hidden_all - average * average
            factors[...] = to_columns(average, lax.rsqrt(spread + epsilon))

        def work(first):
            block = pl.ds(first, rows)
            grads[block, :] = lax.dot_general(
                rows_buf[block, :],
                second_ref[...],
                (((1,), (1,)), ((), ())),
                preferred_element_type=f32,
            )
            second_sum[...] += lax.dot_general(
                mixed[block, :],
                rows_buf[block, :],
                (((0,), (0,)), ((), ())),
                preferred_element_type=f32,
            )

            def step(at):
                piece = pl.ds(pl.multiple_of(first + at, CHUNK), CHUNK)
                normal = normal_buf[piece, :]
                grad = grads[piece, :]
                small[0] += fold(grad * normal)
                small[1] += fold(grad)
                scaled = grad * mid_gain
                grads[piece, :] = scaled
                columns[pl.ds(at, CHUNK), :] = both_columns(
                    jnp.sum(scaled, axis=1, keepdims=True),
                    jnp.sum(scaled * normal, axis=1, keepdims=True),
                )

            in_chunks(rows, CHUNK, step)
            turned = jnp.transpose(columns[...])
            sums[0:1, pl.ds(first, rows)] = turned[0:1]
            sums[1:2, pl.ds(first, rows)] = turned[64:65]

        self.parts["gather"].finish(
            here, ins[:1], scratch[:1], self.held(scratch, "gather"), work
        )
        held = self.held(scratch, "sums")
        self.parts["sums"].start(here, (sums,), None, held)
        second_grad[...] = second_sum[...].astype(bf16).reshape(second_grad.shape)
        load_slope.wait()
        self.moment("midway")
        self.parts["second"].start(here, (second_grad,), None, self.held(scratch, "second"))
        self.parts["sums"].finish(here, (sums,), (got,), held)

        def rows_of(first):
            factor_columns(first)
            columns[...] = to_columns(
                got[0:1, pl.ds(first, rows)] / hidden_all,
                got[1:2, pl.ds(first, rows)] / hidden_all,
            )

            def step(at):
                piece = pl.ds(pl.multiple_of(first + at, CHUNK), CHUNK)
                pair = columns[pl.ds(at, CHUNK), :]
                factor = factors[pl.ds(at, CHUNK), :][:, 64:65]
                active_grad = factor * (
                    grads[piece, :] - pair[:, 0:1] - normal_buf[piece, :] * pair[:, 64:65]
                )
                rounded = (active_grad * slope[piece, :]).astype(bf16)
                pre_grad[piece, :] = rounded
                small[2] += fold(rounded.astype(f32))

            in_chunks(rows, CHUNK, step)
            return pre_grad[pl.ds(first, rows), :]

        def idle():
            load_rows.wait()
            whole = lax.dot_general(
                ffn_rows[...],
                pre_grad[...],
                (((0,), (0,)), ((), ())),
                preferred_element_type=f32,
            ).astype(bf16)
            part = first_grad.shape[2]
            for i in range(4):
                first_grad[i] = whole[:, i * part : (i + 1) * part]
            self.moment("closing")

        self.parts["scatter"].finish(
            here,
            None,
            (out_ref,),
            self.held(scratch, "scatter"),
            rows_of,
            lambda: first_ref[...],
            idle=idle,
        )
        gradient_ref, normal_1, factor_1, gain_1, normal_2, factor_2, gain_2 = ins[9:16]
        vectors[...] = jnp.zeros_like(vectors)
        layer = slice(self.layer, self.layer + 1)

        def pull(at):
            piece = pl.ds(at, NARROW)
            grad, gradient = out_ref[piece, :], gradient_ref[piece, :].astype(f32)
            normal = normal_1[piece, :]
            vectors[3] += fold(grad * normal)
            vectors[4] += fold(grad)
            vectors[5] += fold(gradient)
            middle = gradient + norm_pull(
                grad, normal, factor_1[piece, 0:1], gain_1[layer, :]
            )
            out_ref[piece, :] = middle
            normal = normal_2[piece, :]
            vectors[1] += fold(middle * normal)
            vectors[2] += fold(middle)
            branch = norm_pull(middle, normal, factor_2[piece, 0:1], gain_2[layer, :])
            vectors[0] += fold(branch)
            branch_ref[piece, :] = branch.astype(bf16)

        in_chunks(rows, NARROW, pull)
        vector_ref[...] = jnp.zeros_like(vector_ref)
        for i in range(6):
            vector_ref[i : i + 1, :] = jnp.sum(vectors[i], axis=0, keepdims=True)
        held = self.held(scratch, "second")
        self.parts["second"].finish(here, (second_grad,), (second_quarter,), held)
        for i in range(3):
            small_ref[i : i + 1, :] = jnp.sum(small[i], axis=0, keepdims=True)


class WeightGather(Task):
    def __init__(self, weights, layer, axis, when="start"):
        self.layer, self.axis, self.when = layer, axis, when
        self.arrays, self.spaces = (weights,), (pltpu.HBM,)
        self.outs = (jax.ShapeDtypeStruct(weights.shape[1:], weights.dtype),)
        self.out_spaces = (pltpu.HBM,)
        self.scratch = (dma_sems(4), dma_sems(3))
        self.reach = BY_Z

    def copies(self, here, ins, outs, scratch):
        part = outs[0].shape[self.axis] // 4

        def cut(ref, at):
            piece = pl.ds(pl.multiple_of(at * part, part), part)
            return ref.at[piece, :] if self.axis == 0 else ref.at[:, piece]

        source = cut(ins[0].at[self.layer], 2 * here.y + here.core)
        target = cut(outs[0], here.z)
        keep = pltpu.make_async_copy(source, target, scratch[0].at[3])
        return keep, [
            remote(source, target, scratch[0].at[i], scratch[1].at[i], here.peer(*way))
            for i, way in enumerate(BY_Z)
        ]

    def begin(self, here, ins, outs, scratch):
        keep, copies = self.copies(here, ins, outs, scratch)
        for each in copies:
            each.start()
        keep.start()

    def start(self, *held):
        self.at_moment("start", *held)

    def at_moment(self, name, *held):
        if name == self.when:
            self.begin(*held)

    def finish(self, here, ins, outs, scratch):
        keep, copies = self.copies(here, ins, outs, scratch)
        for each in copies:
            each.wait()
        keep.wait()


class ThenRows(Parts):
    def __init__(self, first, when):
        self.when = when
        shape = first.outs[0]
        self.arrays, self.spaces = first.arrays, first.spaces
        rows = RowsGather(shape)
        self.outs, self.out_spaces = rows.outs, rows.out_spaces
        self.scratch = (pltpu.VMEM(shape.shape, shape.dtype),)
        self.use(dict(first=first, rows=rows))

    def start(self, here, ins, outs, scratch):
        self.parts["first"].start(here, ins, None, self.held(scratch, "first"))

    def at_moment(self, name, here, ins, outs, scratch):
        if name == self.when:
            self.parts["first"].finish(here, ins, scratch[:1], self.held(scratch, "first"))
            self.parts["rows"].begin(here, scratch[:1], outs, self.held(scratch, "rows"))

    def finish(self, here, ins, outs, scratch):
        self.at_moment("end", here, ins, outs, scratch)
        self.parts["rows"].finish(here, scratch[:1], outs, self.held(scratch, "rows"))


BLOCK = 256
SPAN = 512


def head_masks(head_width, width):
    lane = lax.broadcasted_iota(jnp.int32, (1, width), 1)
    lower = (lane < head_width).astype(bf16)
    return lower, (1 - lower).astype(bf16)


def by_head(values, head_width):
    lower, upper = head_masks(head_width, values.shape[1])
    return jnp.concatenate([values * lower, values * upper], axis=0)


def from_heads(pair, head_width):
    rows = pair.shape[0] // 2
    lane = lax.broadcasted_iota(jnp.int32, (rows, pair.shape[1]), 1)
    return jnp.where(lane < head_width, pair[:rows], pair[rows:])


def tile_facts(doc_ref, first, key_first, keys):
    docs = doc_ref[:, pl.ds(first, BLOCK)]
    docs = jnp.concatenate([docs, docs], axis=1)
    key_docs = doc_ref[:, pl.ds(pl.multiple_of(key_first, keys), keys)]
    key_docs = jnp.transpose(jnp.broadcast_to(key_docs, (128, keys)))[:, 0:1]
    place = lax.broadcasted_iota(jnp.int32, (keys, 2 * BLOCK), 1)
    place = jnp.where(place >= BLOCK, place - BLOCK, place) + (first - key_first)
    allowed = (docs == key_docs) & (place >= lax.broadcasted_iota(jnp.int32, place.shape, 0))
    return docs, allowed


def attend_block(
    head_width, first, q_ref, k_ref, v_cols, doc_ref, o_ref, l_ref, s_buf, acc, top, total
):
    block = first // BLOCK
    last = first // SPAN
    pair = by_head(q_ref[pl.ds(first, BLOCK), :], head_width)

    def scores(at):
        keys = k_ref[pl.ds(pl.multiple_of(at * SPAN, SPAN), SPAN), :]
        return lax.dot_general(keys, pair, (((1,), (1,)), ((), ())), preferred_element_type=f32)

    top[...] = jnp.full_like(top, masked)

    def first_pass(at, carry):
        s = scores(at)
        s_buf[at] = s
        peak = s[:8]
        for row in range(8, SPAN, 8):
            peak = jnp.maximum(peak, s[row : row + 8])
        top[...] = jnp.maximum(top[...], peak)
        return carry

    lax.fori_loop(0, last, first_pass, 0)
    docs, allowed = tile_facts(doc_ref, first, last * SPAN, SPAN)
    s = jnp.where(allowed, scores(last), masked)
    shift = jnp.where(docs == 0, 0.0, masked)
    peak = jnp.maximum(
        jnp.max(top[...], axis=0, keepdims=True) + shift, jnp.max(s, axis=0, keepdims=True)
    )

    def weigh(at, p):
        values = v_cols[:, pl.ds(pl.multiple_of(at * SPAN, SPAN), SPAN)]
        return jnp.dot(values, p.astype(bf16), preferred_element_type=f32)

    p = jnp.exp(s - peak)
    total[...] = fold(p)
    acc[...] = weigh(last, p)
    base = peak - shift

    def second_pass(at, carry):
        p = jnp.exp(s_buf[at] - base)
        total[...] += fold(p)
        acc[...] += weigh(at, p)
        return carry

    lax.fori_loop(0, last, second_pass, 0)
    sums = jnp.sum(total[...], axis=0, keepdims=True)
    out = from_heads(jnp.transpose(acc[...] / sums), head_width)
    o_ref[pl.ds(first, BLOCK), :] = out
    l_ref[block] = peak + jnp.log(sums)
    return out


def attend_block_back(
    head_width,
    first,
    do,
    q_ref,
    k_ref,
    k_cols,
    v_ref,
    o_ref,
    l_ref,
    doc_ref,
    acc_k,
    acc_v,
    acc_q,
):
    block = first // BLOCK
    rows = pl.ds(first, BLOCK)
    pair_q = by_head(q_ref[rows, :], head_width)
    pair_do = by_head(do, head_width)
    out = o_ref[rows, :]
    inner = jnp.sum(
        jnp.concatenate([out, out], axis=0) * pair_do.astype(f32), axis=1, keepdims=True
    )
    inner = jnp.transpose(jnp.broadcast_to(inner, (2 * BLOCK, 128)))[0:1, :]
    logs = l_ref[block]
    docs, allowed = tile_facts(doc_ref, first, first, BLOCK)

    def step(at, base, allowed):
        piece = pl.ds(pl.multiple_of(at * BLOCK, BLOCK), BLOCK)
        s = lax.dot_general(
            k_ref[piece, :], pair_q, (((1,), (1,)), ((), ())), preferred_element_type=f32
        )
        dp = lax.dot_general(
            v_ref[piece, :], pair_do, (((1,), (1,)), ((), ())), preferred_element_type=f32
        )
        p = jnp.exp(s - base)
        if allowed is not None:
            p = jnp.where(allowed, p, 0.0)
        ds = (p * (dp - inner)).astype(bf16)
        acc_v[piece, :] += jnp.dot(p.astype(bf16), pair_do, preferred_element_type=f32)
        acc_k[piece, :] += jnp.dot(ds, pair_q, preferred_element_type=f32)
        return jnp.dot(k_cols[:, piece], ds, preferred_element_type=f32)

    acc_q[...] = step(block, logs, allowed)
    base = jnp.where(docs == 0, logs, -masked)

    def earlier(at, carry):
        acc_q[...] += step(at, base, None)
        return carry

    lax.fori_loop(0, block, earlier, 0)
    grad = from_heads(jnp.transpose(acc_q[...]), head_width)
    return (grad * head_width**-0.5).astype(bf16)


def turned(values):
    return jnp.transpose(values.astype(f32)).astype(bf16)


class AttnForward(Parts):
    def __init__(
        self, block, docs, scale, heads, biases, wide, layer, norms, residual=None, late=None
    ):
        rows, width = block.shape
        self.head_width, self.layer, self.late = wide, layer, late
        here = 2 * wide
        self.arrays = (block, docs, scale, biases, *heads)
        far = pltpu.HBM if late else pltpu.VMEM
        self.spaces = (far, far, pltpu.VMEM) + (far,) * (1 + len(heads))
        column = jax.ShapeDtypeStruct((8 * rows, here), bf16)
        self.outs = (
            jax.ShapeDtypeStruct((rows, width), f32),
            jax.ShapeDtypeStruct((8 * rows, width), bf16),
            column,
            column,
            column,
            column,
            jax.ShapeDtypeStruct((8 * rows, here), f32),
            jax.ShapeDtypeStruct((8 * rows // BLOCK, 1, 2 * BLOCK), f32),
        )
        wide_shape = jax.ShapeDtypeStruct((rows, 128), f32)
        self.outs += (self.outs[0], wide_shape, self.outs[0], wide_shape)
        self.outs += (jax.ShapeDtypeStruct((rows, width), bf16),)
        self.out_spaces = (pltpu.VMEM, pltpu.HBM) + (pltpu.VMEM,) * 11
        self.arrays += tuple(norms)
        self.spaces += (pltpu.VMEM,) * 5
        self.scratch = (
            pltpu.VMEM((8 * rows, width), bf16),
            pltpu.VMEM((here, 8 * rows), bf16),
            pltpu.VMEM((8 * rows // SPAN, SPAN, 2 * BLOCK), f32),
            pltpu.VMEM((here, 2 * BLOCK), f32),
            pltpu.VMEM((8, 2 * BLOCK), f32),
            pltpu.VMEM((8, 2 * BLOCK), f32),
            dma_sems(1),
        )
        parts = dict(gather=PlaneGather(block), scatter=PlaneScatter(rows, width, 0))
        if late:
            parts.update(heads=HeadGather(*heads, layer), biases=LineGather(biases))
            half = jax.ShapeDtypeStruct((rows // 2, width), block.dtype)
            for i in range(2):
                parts["tokens", i] = PlaneMove(half, when="push")
            parts["docs"] = PlaneMove(docs, when="push")
            self.outs += parts["heads"].outs + parts["biases"].outs
            self.outs += (jax.ShapeDtypeStruct(docs.shape, f32),)
            self.outs += (jax.ShapeDtypeStruct(block.shape, f32),) * 2
            self.outs += (wide_shape,)
            self.out_spaces += (pltpu.VMEM,) * 6
            self.scratch += (pltpu.VMEM(block.shape, bf16), pltpu.VMEM(block.shape, bf16))
            self.scratch += (pltpu.VMEM(docs.shape, docs.dtype),)
            self.arrays += tuple(late)
            self.spaces += (pltpu.VMEM,) * 2
        else:
            self.arrays += (residual,)
            self.spaces += (pltpu.VMEM,)
        self.base = 3 + 1 + len(heads)
        self.use(parts)

    def start(self, here, ins, outs, scratch):
        if self.late:
            for part, held in self.moves(here, ins, scratch):
                part.start(*held)
        else:
            self.parts["gather"].start(here, ins[:1], scratch[:1], self.held(scratch, "gather"))

    def moves(self, here, ins, scratch):
        half = ins[0].shape[0] // 2
        triples = []
        for i in range(2):
            piece = pl.ds(i * half, half)
            triples.append((("tokens", i), ins[0].at[piece], scratch[7].at[piece]))
        triples.append(("docs", ins[1], scratch[9]))
        return [
            (self.parts[name], (here, (source,), (target,), self.held(scratch, name)))
            for name, source, target in triples
        ]

    def first_norm(self, here, ins, outs, scratch):
        tokens, block = scratch[7:9]
        residual_ref, normal_ref, factor_ref = outs[16:19]
        moves = self.moves(here, ins, scratch)
        for part, held in moves:
            part.at_moment("push", *held)
        self.parts["biases"].start(here, ins[3:4], outs[14:15], self.held(scratch, "biases"))
        self.parts["heads"].start(here, ins[4:6], outs[13:14], self.held(scratch, "heads"))
        for part, held in moves:
            part.finish(*held)
        outs[15][...] = scratch[9][...].astype(f32)
        gain, bias = (ref[self.layer : self.layer + 1, :] for ref in ins[self.base + 5 :])
        values = tokens[...].astype(f32)
        residual_ref[...] = values
        normal, factor = normalize(values)
        factor_ref[...] = wide_column(factor)
        normal_ref[...] = normal
        block[...] = (normal * gain + bias).astype(bf16)
        return block

    def finish(self, here, ins, outs, scratch):
        block_ref, doc_ref, scale_ref = ins[:3]
        scale_row = scale_of(here, scale_ref, self.layer, self.head_width)
        heads_ref, bias_ref = outs[13:15] if self.late else (ins[4], ins[3])
        if self.late:
            doc_ref = outs[15]
            block_ref = self.first_norm(here, ins, outs, scratch)
            self.parts["gather"].start(
                here, (block_ref,), scratch[:1], self.held(scratch, "gather")
            )
        out_ref, rows_out, q_ref, k_ref, v_ref, z_ref, o_ref, l_ref = outs[:8]
        rows_buf, v_cols, s_buf, acc, top, total, save = scratch[:7]
        rows, model_width = block_ref.shape
        wide = self.head_width
        width = 2 * wide

        def bias_row(at):
            pair = [
                bias_ref[2 * here.core + i, self.layer : self.layer + 1, at : at + width]
                for i in range(2)
            ]
            lane = lax.broadcasted_iota(jnp.int32, (1, width), 1)
            return jnp.where(lane < wide, pair[0], pair[1])

        def work(first):
            block = pl.ds(first, rows)
            projected = lax.dot_general(
                rows_buf[block, :],
                heads_ref[0:3].reshape(3 * width, model_width),
                (((1,), (1,)), ((), ())),
                preferred_element_type=f32,
            )
            q = (projected[:, :width] + bias_row(0)).astype(bf16).astype(f32)
            q_ref[block, :] = (q * wide**-0.5).astype(bf16)
            k_ref[block, :] = projected[:, width : 2 * width].astype(bf16)
            v = (projected[:, 2 * width :] + bias_row(width)).astype(bf16)
            v_ref[block, :] = v
            v_cols[:, block] = turned(v)

        self.parts["gather"].finish(
            here,
            (block_ref,),
            scratch[:1],
            self.held(scratch, "gather"),
            None if self.late else work,
        )
        keep_rows = pltpu.make_async_copy(rows_buf, rows_out, save.at[0])
        keep_rows.start()
        if self.late:
            self.parts["heads"].arrive(0, outs[13:14], self.held(scratch, "heads"))
            self.parts["biases"].finish(here, ins[3:4], outs[14:15], self.held(scratch, "biases"))
            in_chunks(8 * rows, rows, work)
            self.parts["heads"].arrive(1, outs[13:14], self.held(scratch, "heads"))
        self.moment("midway")

        def rows_of(first):
            out = attend_block(
                wide, first, q_ref, k_ref, v_cols, doc_ref, o_ref, l_ref, s_buf, acc, top, total
            )
            z = (out * scale_row).astype(bf16)
            z_ref[pl.ds(first, rows), :] = z
            return z

        self.parts["scatter"].finish(
            here,
            None,
            (out_ref,),
            self.held(scratch, "scatter"),
            rows_of,
            lambda: heads_ref[3].reshape(width, model_width),
            idle=lambda: self.moment("closing"),
        )
        residual_ref = outs[16] if self.late else ins[self.base + 5]
        layer = slice(self.layer, self.layer + 1)
        shift, gain_1, bias_1, gain_2, bias_2 = (
            ref[layer, :] for ref in ins[self.base : self.base + 5]
        )
        normal_1, factor_1, normal_2, factor_2, next_ref = outs[8:13]

        def settle(at):
            piece = pl.ds(at, NARROW)
            normal, factor = normalize(out_ref[piece, :] + shift)
            normal_1[piece, :] = normal
            factor_1[piece, :] = wide_column(factor)
            middle = residual_ref[piece, :] + (normal * gain_1 + bias_1)
            out_ref[piece, :] = middle
            normal, factor = normalize(middle)
            normal_2[piece, :] = normal
            factor_2[piece, :] = wide_column(factor)
            next_ref[piece, :] = (normal * gain_2 + bias_2).astype(bf16)

        in_chunks(rows, NARROW, settle)
        keep_rows.wait()
        if self.late:
            held = self.held(scratch, "heads")
            self.parts["heads"].sent(here, ins[4:6], outs[13:14], held)


class AttnBackward(Parts):
    def __init__(
        self, block, docs, scale, heads, q, k, v, z, o, logs, attn_rows, norm, hidden, layer, end
    ):
        self.end = end
        self.layer = layer
        rows, width = block.shape
        kinds, _, wide, _ = heads.shape
        self.head_width = wide
        here = 2 * wide
        self.arrays = (block, docs, scale, heads, q, k, v, z, o, logs, attn_rows)
        self.spaces = (pltpu.VMEM,) * 10 + (pltpu.HBM,)
        self.arrays += (*norm, hidden)
        self.spaces += (pltpu.VMEM,) * 5
        self.shipped = kinds if end else kinds // 2
        leaving = jax.ShapeDtypeStruct((self.shipped, *heads.shape[1:]), bf16)
        staying = jax.ShapeDtypeStruct((kinds - self.shipped, *heads.shape[1:]), bf16)
        heads_sum = HeadScatter(leaving)
        half_rows = jax.ShapeDtypeStruct((rows // 2, width), bf16)
        vector, sums = jax.ShapeDtypeStruct((8, width), f32), jax.ShapeDtypeStruct((4, 4, here), f32)
        quarter = heads_sum.outs[0]
        if end:
            tail = {("move", i): PlaneMove(half_rows, True, "push") for i in range(2)}
            tail.update(
                vectors=PlaneSum(vector),
                line=LineSum(vector),
                rows=RowsGather(quarter),
                hidden=ThenRows(LineScatter(sums), "push"),
            )
            self.outs = (jax.ShapeDtypeStruct((rows, width), bf16), vector) + tail["rows"].outs + tail["hidden"].outs
            self.out_spaces = (pltpu.HBM, pltpu.VMEM, pltpu.HBM, pltpu.HBM)
        else:
            self.outs = (jax.ShapeDtypeStruct((rows, width), f32), quarter, sums)
            self.outs += (jax.ShapeDtypeStruct((rows, width), bf16), vector, staying)
            self.out_spaces = (pltpu.VMEM,) * 6
        self.scratch = (
            pltpu.VMEM((8 * rows, width), bf16),
            pltpu.VMEM((8 * rows, width), bf16),
            pltpu.VMEM((here, 8 * rows), bf16),
            pltpu.VMEM((8 * rows, here), f32),
            pltpu.VMEM((8 * rows, here), f32),
            pltpu.VMEM((here, 2 * BLOCK), f32),
            pltpu.VMEM((8 * rows, 3 * here), bf16),
            pltpu.VMEM((here, width), f32),
            pltpu.VMEM((3, 8, here), f32),
            dma_sems(1),
            pltpu.VMEM((2, 8, width), f32),
            pltpu.VMEM(heads.shape, bf16),
        )
        if end:
            self.scratch += (
                pltpu.VMEM((rows, width), f32),
                pltpu.VMEM(quarter.shape, bf16),
                pltpu.VMEM(sums.shape, f32),
                pltpu.VMEM((rows, width), bf16),
                pltpu.VMEM(vector.shape, f32),
                pltpu.VMEM(vector.shape, f32),
            )
        parts = dict(gather=OrderedGather(block), scatter=PlaneScatter(rows, width, 0))
        parts.update(tail if end else {})
        parts["heads"] = heads_sum
        self.use(parts)

    def load(self, ins, scratch):
        return pltpu.make_async_copy(ins[10], scratch[1], scratch[9].at[0])

    def start(self, here, ins, outs, scratch):
        self.parts["gather"].start(here, ins[:1], scratch[:1], self.held(scratch, "gather"))
        self.load(ins, scratch).start()

    def finish(self, here, ins, outs, scratch):
        block_ref, doc_ref, scale_ref, heads_ref, q_ref, k_ref, v_ref, z_ref, o_ref, l_ref = ins[:10]
        results = scratch[12:17] if self.end else outs
        out_ref, quarter_ref, hidden_ref, rounded_ref, vector_ref = results[:5]
        middle_ref, normal_ref, factor_ref, gain_ref, sums_ref = ins[11:16]
        (
            rows_buf,
            attn_rows,
            k_cols,
            acc_k,
            acc_v,
            acc_q,
            proj,
            out_sum,
            small,
        ) = scratch[:9]
        vectors = scratch[10]
        heads_grad = scratch[11]
        leaving = (heads_grad.at[pl.ds(0, self.shipped)],)
        scale_row = scale_of(here, scale_ref, self.layer, self.head_width)
        rows, model_width = block_ref.shape
        wide = self.head_width
        width = 2 * wide
        acc_k[...] = jnp.zeros_like(acc_k)
        acc_v[...] = jnp.zeros_like(acc_v)
        out_sum[...] = jnp.zeros_like(out_sum)
        small[...] = jnp.zeros_like(small)
        k_cols[...] = turned(k_ref[...])

        def work(first):
            block = pl.ds(first, rows)
            scaled_grad = lax.dot_general(
                rows_buf[block, :],
                heads_ref[3].reshape(width, model_width),
                (((1,), (1,)), ((), ())),
                preferred_element_type=f32,
            )
            out_sum[...] += lax.dot_general(
                z_ref[block, :],
                rows_buf[block, :],
                (((0,), (0,)), ((), ())),
                preferred_element_type=f32,
            )
            small[0] += fold(o_ref[block, :] * scaled_grad)
            grad = attend_block_back(
                wide,
                first,
                (scaled_grad * scale_row).astype(bf16),
                q_ref,
                k_ref,
                k_cols,
                v_ref,
                o_ref,
                l_ref,
                doc_ref,
                acc_k,
                acc_v,
                acc_q,
            )
            proj[block, 0:width] = grad
            small[1] += fold(grad.astype(f32))

        self.parts["gather"].finish(
            here,
            ins[:1],
            scratch[:1],
            self.held(scratch, "gather"),
            work,
            self.moment,
        )

        def settle(first):
            block = pl.ds(first, rows)
            proj[block, width : 2 * width] = acc_k[block, :].astype(bf16)
            value_grad = acc_v[block, :].astype(bf16)
            proj[block, 2 * width : 3 * width] = value_grad
            small[2] += fold(value_grad.astype(f32))

        in_chunks(8 * rows, rows, settle)
        self.moment("midway")

        def early():
            self.load(ins, scratch).wait()
            qkv_grad = lax.dot_general(
                proj[...],
                attn_rows[...],
                (((0,), (0,)), ((), ())),
                preferred_element_type=f32,
            )
            heads_grad[0:3] = qkv_grad.astype(bf16).reshape(3, 2, wide, model_width)
            heads_grad[3] = out_sum[...].astype(bf16).reshape(2, wide, model_width)
            self.parts["heads"].start(here, leaving, None, self.held(scratch, "heads"))
            if not self.end:
                outs[5][...] = heads_grad[self.shipped :]

        early()
        self.parts["scatter"].finish(
            here,
            None,
            (out_ref,),
            self.held(scratch, "scatter"),
            lambda first: proj[pl.ds(first, rows), :],
            lambda: heads_ref[0:3].reshape(3 * width, model_width),
            idle=lambda: self.moment("closing"),
        )
        vectors[...] = jnp.zeros_like(vectors)
        layer = slice(self.layer, self.layer + 1)

        def pull(at):
            piece = pl.ds(at, NARROW)
            grad, normal = out_ref[piece, :], normal_ref[piece, :]
            vectors[0] += fold(grad * normal)
            vectors[1] += fold(grad)
            gradient = middle_ref[piece, :] + norm_pull(
                grad, normal, factor_ref[piece, 0:1], gain_ref[layer, :]
            )
            out_ref[piece, :] = gradient
            rounded_ref[piece, :] = gradient.astype(bf16)

        home = []
        if self.end:
            for i in range(2):
                piece = pl.ds(i * (rows // 2), rows // 2)
                held = self.held(scratch, ("move", i))
                refs = (rounded_ref.at[piece],), (outs[0].at[piece],)
                home.append((self.parts["move", i], (here, *refs, held)))
                pull(i * NARROW)
                home[i][0].start(*home[i][1])
        else:
            in_chunks(rows, NARROW, pull)
        scale_cols, query_cols, value_cols = (
            jnp.sum(small[i], axis=0, keepdims=True) for i in range(3)
        )
        vector_ref[...] = jnp.zeros_like(vector_ref)
        for i in range(2):
            vector_ref[i : i + 1, :] = jnp.sum(vectors[i], axis=0, keepdims=True)
        lane = lax.broadcasted_iota(jnp.int32, (1, width), 1)
        place = lax.broadcasted_iota(jnp.int32, (1, model_width), 1)
        head_sums = jnp.zeros((1, model_width), f32)
        for i in range(2):
            head = ((2 * here.core + i) * 2 + here.x) * 2 + here.y
            own = (lane >= i * wide) & (lane < (i + 1) * wide)
            total = jnp.sum(jnp.where(own, scale_cols, 0.0), axis=1, keepdims=True)
            head_sums = head_sums + jnp.where(place == head, total, 0.0)
        vector_ref[2:3, :] = head_sums
        pairs = [
            jnp.concatenate(
                [cols[:, i * wide : (i + 1) * wide] for cols in (query_cols, value_cols)], axis=1
            )
            for i in range(2)
        ]
        for shard in range(4):
            for row, source in enumerate((2, 0, 1)):
                cut = sums_ref[source : source + 1, shard * width : (shard + 1) * width]
                hidden_ref[shard, row : row + 1, :] = cut
            own = here.core == shard // 2
            hidden_ref[shard, 3:4, :] = jnp.where(own, pairs[shard % 2], 0.0)
        self.moment("tail")
        held = (here, leaving, (quarter_ref,), self.held(scratch, "heads"))
        if not self.end:
            self.parts["heads"].finish(*held)
            return
        sum_held = (here, (vector_ref,), (scratch[17],), self.held(scratch, "vectors"))
        line_held = (here, (scratch[17],), outs[1:2], self.held(scratch, "line"))
        rows_held = (here, (quarter_ref,), outs[2:3], self.held(scratch, "rows"))
        hidden_held = (here, (hidden_ref,), outs[3:4], self.held(scratch, "hidden"))
        self.parts["vectors"].start(*sum_held)
        self.parts["hidden"].start(*hidden_held)
        self.parts["heads"].finish(*held)
        self.parts["rows"].begin(*rows_held)
        self.parts["vectors"].finish(*sum_held)
        self.parts["line"].start(*line_held)
        for part, refs in home:
            part.at_moment("push", *refs)
        self.parts["hidden"].at_moment("push", *hidden_held)
        self.parts["line"].finish(*line_held)
        self.parts["rows"].finish(*rows_held)
        self.parts["hidden"].finish(*hidden_held)
        for part, refs in home:
            part.finish(*refs)


def finish_kernel(layers, *refs):
    count = 2 + 6 * layers
    far, refs, sems = refs[:count], refs[count:-1], refs[-1]
    refs, near = refs[: len(refs) - count], refs[len(refs) - count :]
    loads = [pltpu.make_async_copy(a, b, sems.at[i]) for i, (a, b) in enumerate(zip(far, near))]
    order = [0, 1] + [2 + g * layers + i for i in range(layers - 1, -1, -1) for g in range(6)]
    for index in order:
        loads[index].start()
    refs = (*near, *refs)
    (layer_ref, grad_ref), refs = refs[:2], refs[2:]
    groups = []
    for _ in range(6):
        groups.append(refs[:layers])
        refs = refs[layers:]
    firsts, seconds, heads_all, hiddens, earlies, lates = groups
    (
        layer_out,
        grad_out,
        attn_gain,
        attn_bias,
        qkv_out,
        bias_out,
        scale_out,
        out_out,
        out_shift,
        post_gain,
        post_bias,
        ffn_gain,
        ffn_bias,
        first_out,
        first_shift,
        mid_gain,
        mid_bias,
        second_out,
        second_shift,
    ) = refs
    loads[0].wait()
    layer_out[...] = layer_ref[...]
    loads[1].wait()
    grad_out[...] = grad_ref[...].astype(f32)
    for layer in range(layers - 1, -1, -1):
        for group in range(6):
            loads[2 + group * layers + layer].wait()
        first, second, heads, hidden = (g[layer] for g in (firsts, seconds, heads_all, hiddens))
        part = first.shape[2]
        wide, half = heads.shape[2:]
        row = slice(layer, layer + 1)
        for i, ref in enumerate((out_shift, post_gain, post_bias, ffn_gain, ffn_bias, second_shift)):
            ref[row, :] = earlies[layer][i : i + 1, :]
        for i, ref in enumerate((attn_gain, attn_bias)):
            ref[row, :] = lates[layer][i : i + 1, :]
        scale_out[row, :] = lates[layer][2:3, 0 : scale_out.shape[1]]
        for i in range(4):
            cut = slice(i * part, (i + 1) * part)
            first_out[layer, :, cut] = first[i].astype(f32)
            second_out[layer, cut, :] = second[i].astype(f32)
            for at, ref in enumerate((first_shift, mid_gain, mid_bias)):
                ref[row, cut] = hidden[i, at : at + 1, :]
        biases = [hidden[2 * y, 3:4, :] + hidden[2 * y + 1, 3:4, :] for y in range(2)]
        for i in range(2):
            bias_out[layer, i : i + 1, :] = jnp.concatenate(
                [each[:, i * wide : (i + 1) * wide] for each in biases], axis=1
            )
        for core in range(2):
            here = slice(core * half, (core + 1) * half)
            for kind in range(3):
                pair = jnp.concatenate([heads[core, kind], heads[2 + core, kind]], axis=0)
                qkv_out[layer, kind, here, :] = jnp.transpose(pair.astype(f32))
            for y in range(2):
                out_out[layer, y * wide : (y + 1) * wide, here] = heads[2 * y + core, 3].astype(f32)


def finish_all(layer_output, gradient, heads_count, *groups):
    firsts, seconds, heads = groups[:3]
    layers = len(firsts)
    rows, width = layer_output.shape
    part = firsts[0].shape[2]
    wide = heads[0].shape[2]
    vector = jax.ShapeDtypeStruct((layers, width), f32)
    hidden = jax.ShapeDtypeStruct((layers, 4 * part), f32)
    outs = (
        jax.ShapeDtypeStruct((rows, width), bf16),
        jax.ShapeDtypeStruct((rows, width), f32),
        vector,
        vector,
        jax.ShapeDtypeStruct((layers, 3, width, 2 * wide), f32),
        jax.ShapeDtypeStruct((layers, 2, 2 * wide), f32),
        jax.ShapeDtypeStruct((layers, heads_count), f32),
        jax.ShapeDtypeStruct((layers, 2 * wide, width), f32),
        vector,
        vector,
        vector,
        vector,
        vector,
        jax.ShapeDtypeStruct((layers, width, 4 * part), f32),
        hidden,
        hidden,
        hidden,
        jax.ShapeDtypeStruct((layers, 4 * part, width), f32),
        vector,
    )
    arrays = [layer_output, gradient] + [each for group in groups for each in group]
    results = list(
        pl.pallas_call(
            partial(finish_kernel, layers),
            out_shape=outs,
            in_specs=[pl.BlockSpec(memory_space=pltpu.HBM)] * len(arrays),
            out_specs=[pl.BlockSpec(memory_space=pltpu.VMEM)] * len(outs),
            scratch_shapes=[
                *[pltpu.VMEM(each.shape, each.dtype) for each in arrays],
                dma_sems(len(arrays)),
            ],
            compiler_params=vmem_params(None, 60),
        )(*arrays)
    )
    results[4] = jnp.transpose(results[4], (0, 2, 1, 3))
    return tuple(results)


def plane_device(
    tokens,
    segment_ids,
    cotangent,
    ln_attn_gain,
    ln_attn_bias,
    qkv_weight,
    qv_bias,
    head_scale,
    out_weight,
    out_bias,
    ln_post_gain,
    ln_post_bias,
    ln_ffn_gain,
    ln_ffn_bias,
    fc1_weight,
    fc1_bias,
    mid_gain,
    mid_bias,
    fc2_weight,
    fc2_bias,
):
    layers = qkv_weight.shape[0]
    model_width = tokens.shape[1]
    heads_all = head_scale.shape[1]
    head_width = model_width // heads_all
    hidden_here = fc1_weight.shape[2]
    hidden_all = hidden_here * 8
    quarter = hidden_here // 4
    half_width = model_width // 2
    x, y, core = lax.axis_index("x"), lax.axis_index("y"), lax.axis_index("core")
    quarter_at = 2 * y + core
    width = 2 * head_width
    ids = iter(range(1, 64))

    docs = segment_ids[None, :]

    def cut(values, at, size, axis):
        return lax.dynamic_slice_in_dim(values, at * size, size, axis)

    qkv_rows = jnp.transpose(qkv_weight, (0, 2, 3, 1))
    bias_heads = cut(qv_bias, y, head_width, 2)
    small = jnp.concatenate(
        [
            jnp.concatenate([bias_heads, bias_heads], axis=2).reshape(layers, 2 * width),
            cut(fc1_bias, quarter_at, quarter, 1),
            cut(mid_gain, quarter_at, quarter, 1),
            cut(mid_bias, quarter_at, quarter, 1),
        ],
        axis=1,
    )
    heads_here = [None] * layers
    norms = (out_bias, ln_post_gain, ln_post_bias, ln_ffn_gain, ln_ffn_bias)
    attn_norm = (ln_attn_gain, ln_attn_bias)

    stored = []
    for layer in range(layers):
        first, last = layer == 0, layer + 1 == layers
        if first:
            task = AttnForward(
                tokens,
                docs,
                head_scale,
                (qkv_rows, out_weight),
                small,
                head_width,
                layer,
                norms,
                late=attn_norm,
            )
            sides = [WeightGather(fc1_weight, layer, 1, "midway")]
        else:
            task = AttnForward(
                block,
                docs,
                head_scale,
                (heads_here[layer],),
                small,
                head_width,
                layer,
                norms,
                residual=residual,
            )
            sides = [WeightGather(fc1_weight, layer, 1), WeightGather(fc2_weight, layer, 0)]
        (got, (first_here,), *rest) = run_tasks(ids, task, *sides)
        middle, attn_rows, q, k, v, scaled, attended, logs = got[:8]
        post_normal, post_factor, ffn_normal, ffn_factor, block = got[8:13]
        if first:
            heads_here[0], small, docs, _, attn_normal, attn_factor = got[13:]
        here = (attn_normal, attn_factor)
        sides = [PlaneMove(cotangent)]
        if not last:
            sides = [HeadGather(qkv_rows, out_weight, layer + 1, "midway" if first else "start")]
        (got, (side,)) = run_tasks(
            ids,
            FfnForward(
                block,
                first_here,
                fc2_weight if first else rest[0][0],
                small,
                middle,
                fc2_bias,
                None if last else attn_norm,
                layer,
                first,
            ),
            *sides,
        )
        residual, ffn_rows, slope, hidden_normal, mixed, totals, block = got[:7]
        second_here = got[-1] if first else rest[0][0]
        if not last:
            attn_normal, attn_factor = got[7:9]
            heads_here[layer + 1] = side
        stored.append(
            (
                first_here,
                second_here,
                *here,
                attn_rows,
                q,
                k,
                v,
                attended,
                logs,
                scaled,
                post_normal,
                post_factor,
                ffn_normal,
                ffn_factor,
                ffn_rows,
                slope,
                hidden_normal,
                mixed,
                totals,
            )
        )
    gradient = gradient_b = side

    first_done, second_done = [None] * layers, [None] * layers
    heads_done, hidden_done = [None] * layers, [None] * layers
    early_done, late_done = [None] * layers, [None] * layers
    late_vectors = None
    for layer in reversed(range(layers)):
        (
            first_here,
            second_here,
            attn_normal,
            attn_factor,
            attn_rows,
            q,
            k,
            v,
            attended,
            logs,
            scaled,
            post_normal,
            post_factor,
            ffn_normal,
            ffn_factor,
            ffn_rows,
            slope,
            hidden_normal,
            mixed,
            totals,
        ) = stored[layer]
        last = layer + 1 == layers
        if last:
            sides = [PlaneMove(block, back=True)]
        else:
            sides = [HeadScatter(heads_rest), ThenRows(LineScatter(hidden_grad), "closing")]
            sides += [LineSum(early_vectors), StepSum(late_vectors)]
        ((gradient, first_grad, second_grad, hidden_sums, branch_b, early_vectors), *got) = (
            run_tasks(
                ids,
                FfnBackward(
                    gradient_b,
                    first_here,
                    second_here,
                    small,
                    slope,
                    hidden_normal,
                    mixed,
                    ffn_rows,
                    totals,
                    gradient,
                    (
                        ffn_normal,
                        ffn_factor,
                        ln_ffn_gain,
                        post_normal,
                        post_factor,
                        ln_post_gain,
                    ),
                    layer,
                ),
                *sides,
            )
        )
        if last:
            layer_output = got[0][0]
        else:
            heads_rest, hidden_done[layer + 1], early_done[layer + 1], late_vectors = (
                each[0] for each in got
            )
            heads_grad = jnp.concatenate([heads_grad, heads_rest], axis=0)
        sides = [ThenRows(LineScatter(first_grad), "soon"), RowsGather(second_grad, "spare")]
        sides.append(StepThenLine(early_vectors) if layer == 0 else StepSum(early_vectors))
        if not last:
            sides += [LineSum(late_vectors), RowsGather(heads_grad, "spare")]
        (results, *got) = run_tasks(
            ids,
            AttnBackward(
                branch_b,
                docs,
                head_scale,
                heads_here[layer],
                q,
                k,
                v,
                scaled,
                attended,
                logs,
                attn_rows,
                (gradient, attn_normal, attn_factor, ln_attn_gain),
                hidden_sums,
                layer,
                layer == 0,
            ),
            *sides,
        )
        first_done[layer], second_done[layer], early_vectors = got[0][0], got[1][0], got[2][0]
        if not last:
            late_done[layer + 1], heads_done[layer + 1] = got[3][0], got[4][0]
        if layer == 0:
            input_grad, late_done[0], heads_done[0], hidden_done[0] = results
            early_done[0] = early_vectors
        else:
            gradient, heads_grad, hidden_grad, gradient_b, late_vectors, heads_rest = results
    return finish_all(
        layer_output,
        input_grad,
        heads_all,
        first_done,
        second_done,
        heads_done,
        hidden_done,
        early_done,
        late_done,
    )


def split_specs(rows, mp):
    both = tuple(rows) + tuple(mp)
    in_specs = (
        P(both, None),
        P(rows),
        P(both, None),
        P(),
        P(),
        P(None, None, None, mp),
        P(None, None, mp),
        P(),
        P(None, mp, None),
        P(),
        P(),
        P(),
        P(),
        P(),
        P(None, None, mp),
        P(None, mp),
        P(None, mp),
        P(None, mp),
        P(None, mp, None),
        P(),
    )
    out_specs = (
        P(both, None),
        P(both, None),
        P(),
        P(),
        P(None, None, None, mp),
        P(None, None, mp),
        P(),
        P(None, mp, None),
        P(),
        P(),
        P(),
        P(),
        P(),
        P(None, None, mp),
        P(None, mp),
        P(None, mp),
        P(None, mp),
        P(None, mp, None),
        P(),
    )
    return in_specs, out_specs


def solution(mesh):
    if mesh.shape["rows"] == 4 and mesh.shape["mp"] == 8:
        planes = Mesh(mesh.devices.reshape(2, 2, 4, 2), ("y", "core", "z", "x"))
        in_specs, out_specs = split_specs(("y", "core"), ("z", "x"))
        return jax.shard_map(
            plane_device, mesh=planes, in_specs=in_specs, out_specs=out_specs, check_vma=False
        )
    in_specs, out_specs = split_specs(("rows",), ("mp",))
    return jax.shard_map(
        per_device, mesh=mesh, in_specs=in_specs, out_specs=out_specs, check_vma=False
    )
```

```python
from functools import partial

import jax
import jax.numpy as jnp
from jax import lax
from jax.experimental import pallas as pl
from jax.experimental.pallas import tpu as pltpu
from jax.sharding import Mesh
from jax.sharding import PartitionSpec as P

epsilon = 1e-05
masked = -1e30


def partner(shard, axis, stride):
    return lax.ppermute(shard, axis, [(i, i ^ 1 << stride) for i in range(lax.axis_size(axis))])


def norm_local(values, gain_row, bias_row):
    average = jnp.mean(values, axis=-1, keepdims=True)
    centered = values - average
    spread = jnp.mean(centered * centered, axis=-1, keepdims=True)
    factor = lax.rsqrt(spread + epsilon)
    normal = centered * factor
    return (normal * gain_row + bias_row, normal, factor)


def norm_back(grad_out, normal, factor, gain_row):
    scaled = grad_out * gain_row
    inner_sum = jnp.mean(scaled * normal, axis=-1, keepdims=True)
    return factor * (scaled - jnp.mean(scaled, axis=-1, keepdims=True) - normal * inner_sum)


def collect_rows(normed_b):
    return lax.all_gather(normed_b, "mp", axis=0, tiled=True)


def collect_grads(gradient_b):
    return lax.all_gather(gradient_b, "mp", axis=0, tiled=True)


def reduce_branch(operand_b, weight_b, local_rows):

    def partial_term(first_row, count):
        return jnp.dot(operand_b, weight_b, preferred_element_type=jnp.float32)

    return lax.psum_scatter(
        partial_term(jnp.int32(0), local_rows * lax.axis_size("mp")).astype(jnp.bfloat16),
        "mp",
        scatter_dimension=0,
        tiled=True,
    ).astype(jnp.float32)


def reduce_grads(operand_b, weight_b, local_rows):

    def partial_term(first_row, count):
        return jnp.einsum("tc,dc->td", operand_b, weight_b, preferred_element_type=jnp.float32)

    return lax.psum_scatter(
        partial_term(jnp.int32(0), local_rows * lax.axis_size("mp")).astype(jnp.bfloat16),
        "mp",
        scatter_dimension=0,
        tiled=True,
    ).astype(jnp.float32)


def hidden_stats(first_sum, second_sum):
    return lax.psum((first_sum, second_sum), "mp")


def hidden_grad_stats(first_sum, second_sum):
    return lax.psum((first_sum, second_sum), "mp")


def join_cols(mine, other, is_upper):
    lower_part = jnp.where(is_upper, other, mine)
    upper_part = jnp.where(is_upper, mine, other)
    return jnp.concatenate([lower_part, upper_part], axis=-1)


def join_rows(mine, other, is_upper):
    lower_part = jnp.where(is_upper, other, mine)
    upper_part = jnp.where(is_upper, mine, other)
    return jnp.concatenate([lower_part, upper_part], axis=0)


def split_cols(values, cols_here, is_upper):
    lower_part = values[..., :cols_here]
    upper_part = values[..., cols_here:]
    return (
        jnp.where(is_upper, upper_part, lower_part),
        jnp.where(is_upper, lower_part, upper_part),
    )


def masked_scores(query_block, key_rows, query_start, block_rows, doc_rows, positions):
    factor = query_block.shape[-1] ** (-0.5)
    scores = (
        jnp.einsum("qhe,khe->hqk", query_block, key_rows, preferred_element_type=jnp.float32)
        * factor
    )
    query_place = query_start + jnp.arange(block_rows, dtype=jnp.int32)
    query_docs = lax.dynamic_slice_in_dim(doc_rows, query_start, block_rows, 0)
    allowed = (query_docs[:, None] == doc_rows[None, :]) & (
        query_place[:, None] >= positions[None, :]
    )
    return jnp.where(allowed[None], scores, masked)


def attend_forward(queries, key_rows, value_rows, doc_rows, row_offset):
    total_rows = queries.shape[0]
    block_rows = min(512, total_rows)
    positions = jnp.arange(key_rows.shape[0], dtype=jnp.int32)

    def one_block(first_row):
        query_block = lax.dynamic_slice_in_dim(queries, first_row, block_rows, 0)
        scores = masked_scores(
            query_block, key_rows, row_offset + first_row, block_rows, doc_rows, positions
        )
        row_peak = jnp.max(scores, axis=-1, keepdims=True)
        weights = jnp.exp(scores - row_peak)
        totals = jnp.sum(weights, axis=-1, keepdims=True)
        probabilities = (weights / totals).astype(jnp.bfloat16)
        output = jnp.einsum(
            "hqk,khe->qhe", probabilities, value_rows, preferred_element_type=jnp.float32
        )
        return (output, (row_peak + jnp.log(totals))[..., 0])

    starts = jnp.arange(total_rows // block_rows, dtype=jnp.int32) * block_rows
    outputs, log_totals = lax.map(one_block, starts)
    return (outputs.reshape(queries.shape), log_totals)


def attend_backward(queries, key_rows, value_rows, doc_rows, row_offset, log_totals, grad_out):
    total_rows = queries.shape[0]
    block_rows = min(512, total_rows)
    positions = jnp.arange(key_rows.shape[0], dtype=jnp.int32)
    factor = queries.shape[-1] ** (-0.5)

    def one_block(running, first_row):
        key_grad, value_grad = running
        query_block = lax.dynamic_slice_in_dim(queries, first_row, block_rows, 0)
        grad_block = lax.dynamic_slice_in_dim(grad_out, first_row, block_rows, 0)
        scores = masked_scores(
            query_block, key_rows, row_offset + first_row, block_rows, doc_rows, positions
        )
        block_totals = lax.dynamic_index_in_dim(
            log_totals, first_row // block_rows, 0, keepdims=False
        )
        probabilities = jnp.exp(scores - block_totals[..., None])
        prob_grad = jnp.einsum(
            "qhe,khe->hqk", grad_block, value_rows, preferred_element_type=jnp.float32
        )
        inner_sum = jnp.sum(probabilities * prob_grad, axis=-1, keepdims=True)
        score_grad = (probabilities * (prob_grad - inner_sum)).astype(jnp.bfloat16)
        query_grad = (
            jnp.einsum("hqk,khe->qhe", score_grad, key_rows, preferred_element_type=jnp.float32)
            * factor
        )
        key_grad = (
            key_grad
            + jnp.einsum(
                "hqk,qhe->khe", score_grad, query_block, preferred_element_type=jnp.float32
            )
            * factor
        )
        value_grad = value_grad + jnp.einsum(
            "hqk,qhe->khe",
            probabilities.astype(jnp.bfloat16),
            grad_block,
            preferred_element_type=jnp.float32,
        )
        return ((key_grad, value_grad), query_grad)

    starts = jnp.arange(total_rows // block_rows, dtype=jnp.int32) * block_rows
    zero_grads = jnp.zeros(key_rows.shape, jnp.float32)
    (key_grad, value_grad), query_grads = lax.scan(one_block, (zero_grads, zero_grads), starts)
    return (query_grads.reshape(queries.shape), key_grad, value_grad)


def stack_layers(layer_list, members):
    stacked = []
    for member_index in range(members):
        stacked.append(jnp.stack([entry[member_index] for entry in layer_list], axis=0))
    return stacked


def per_device(
    tokens,
    segment_ids,
    cotangent,
    ln_attn_gain,
    ln_attn_bias,
    qkv_weight,
    qv_bias,
    head_scale,
    out_weight,
    out_bias,
    ln_post_gain,
    ln_post_bias,
    ln_ffn_gain,
    ln_ffn_bias,
    fc1_weight,
    fc1_bias,
    mid_gain,
    mid_bias,
    fc2_weight,
    fc2_bias,
):
    layers = qkv_weight.shape[0]
    local_rows = tokens.shape[0]
    model_width = tokens.shape[1]
    cols_here = qkv_weight.shape[3]
    heads_all = head_scale.shape[1]
    head_width = model_width // heads_all
    pair_cols = 2 * cols_here
    pair_heads = pair_cols // head_width
    group_rows = segment_ids.shape[0]
    half_rows = group_rows // 2
    hidden_all = fc1_weight.shape[2] * lax.axis_size("mp")
    device_index = lax.axis_index("mp")
    is_upper = device_index % 2 == 1
    own_start = jnp.where(is_upper, half_rows, 0).astype(jnp.int32)
    other_start = jnp.where(is_upper, 0, half_rows).astype(jnp.int32)
    first_head = device_index // 2 * pair_heads
    pair_onehot = (
        (first_head + jnp.arange(pair_heads, dtype=jnp.int32))[:, None]
        == jnp.arange(heads_all, dtype=jnp.int32)[None, :]
    ).astype(jnp.float32)
    residual = tokens.astype(jnp.float32)
    stored = []
    for layer_index in range(layers):
        attn_in, attn_normal, attn_factor = norm_local(
            residual, ln_attn_gain[layer_index], ln_attn_bias[layer_index]
        )
        attn_rows = collect_rows(attn_in.astype(jnp.bfloat16))
        qkv_here = qkv_weight[layer_index].reshape(model_width, 3 * cols_here)
        projected = jnp.dot(attn_rows, qkv_here, preferred_element_type=jnp.float32).reshape(
            -1, 3, cols_here
        )
        bias_pair = qv_bias[layer_index]
        query_mine = (projected[:, 0] + bias_pair[0]).astype(jnp.bfloat16)
        key_mine = projected[:, 1].astype(jnp.bfloat16)
        value_mine = (projected[:, 2] + bias_pair[1]).astype(jnp.bfloat16)
        query_send = lax.dynamic_slice_in_dim(query_mine, other_start, half_rows, 0)
        query_recv, key_recv, value_recv = partner((query_send, key_mine, value_mine), "mp", 0)
        query_own = lax.dynamic_slice_in_dim(query_mine, own_start, half_rows, 0)
        queries = join_cols(query_own, query_recv, is_upper).reshape(
            half_rows, pair_heads, head_width
        )
        key_rows = join_cols(key_mine, key_recv, is_upper).reshape(
            group_rows, pair_heads, head_width
        )
        value_rows = join_cols(value_mine, value_recv, is_upper).reshape(
            group_rows, pair_heads, head_width
        )
        attended, log_totals = attend_forward(queries, key_rows, value_rows, segment_ids, own_start)
        pair_scale = jnp.sum(pair_onehot * head_scale[layer_index][None, :], axis=1)
        scaled_half = (
            (attended * pair_scale[None, :, None])
            .astype(jnp.bfloat16)
            .reshape(half_rows, pair_cols)
        )
        own_cols, other_cols = split_cols(scaled_half, cols_here, is_upper)
        scaled_recv = partner(other_cols, "mp", 0)
        scaled_mine = join_rows(own_cols, scaled_recv, is_upper)
        branch = (
            reduce_branch(scaled_mine, out_weight[layer_index], local_rows) + out_bias[layer_index]
        )
        post_out, post_normal, post_factor = norm_local(
            branch, ln_post_gain[layer_index], ln_post_bias[layer_index]
        )
        middle = residual + post_out
        ffn_in, ffn_normal, ffn_factor = norm_local(
            middle, ln_ffn_gain[layer_index], ln_ffn_bias[layer_index]
        )
        ffn_rows = collect_rows(ffn_in.astype(jnp.bfloat16))
        before_gelu = (
            jnp.dot(ffn_rows, fc1_weight[layer_index], preferred_element_type=jnp.float32)
            + fc1_bias[layer_index]
        )
        activated = jax.nn.gelu(before_gelu, approximate=False)
        first_sum, second_sum = hidden_stats(
            jnp.sum(activated, axis=1), jnp.sum(activated * activated, axis=1)
        )
        average = first_sum / hidden_all
        spread = second_sum / hidden_all - average * average
        hidden_factor = lax.rsqrt(spread + epsilon)[:, None]
        hidden_normal = (activated - average[:, None]) * hidden_factor
        mixed_b = (hidden_normal * mid_gain[layer_index] + mid_bias[layer_index]).astype(
            jnp.bfloat16
        )
        ffn_out = reduce_branch(mixed_b, fc2_weight[layer_index], local_rows)
        stored.append(
            (
                attn_normal,
                attn_factor,
                attn_rows,
                queries,
                key_rows,
                value_rows,
                attended,
                log_totals,
                pair_scale,
                scaled_mine,
                post_normal,
                post_factor,
                ffn_normal,
                ffn_factor,
                ffn_rows,
                before_gelu,
                hidden_normal,
                hidden_factor,
                mixed_b,
            )
        )
        residual = middle + ffn_out + fc2_bias[layer_index]
    layer_output = residual.astype(jnp.bfloat16)
    gradient = cotangent.astype(jnp.float32)
    sharded_list = []
    shared_list = []
    for layer_index in reversed(range(layers)):
        (
            attn_normal,
            attn_factor,
            attn_rows,
            queries,
            key_rows,
            value_rows,
            attended,
            log_totals,
            pair_scale,
            scaled_mine,
            post_normal,
            post_factor,
            ffn_normal,
            ffn_factor,
            ffn_rows,
            before_gelu,
            hidden_normal,
            hidden_factor,
            mixed_b,
        ) = stored[layer_index]
        qkv_here = qkv_weight[layer_index].reshape(model_width, 3 * cols_here)
        second_shift_grad = jnp.sum(gradient, axis=0)
        grad_rows = collect_grads(gradient.astype(jnp.bfloat16))
        mixed_grad = jnp.einsum(
            "td,fd->tf", grad_rows, fc2_weight[layer_index], preferred_element_type=jnp.float32
        )
        second_grad = jnp.einsum(
            "tf,td->fd", mixed_b, grad_rows, preferred_element_type=jnp.float32
        )
        hidden_gain_grad = jnp.sum(mixed_grad * hidden_normal, axis=0)
        hidden_shift_grad = jnp.sum(mixed_grad, axis=0)
        normal_grad = mixed_grad * mid_gain[layer_index]
        grad_first, grad_second = hidden_grad_stats(
            jnp.sum(normal_grad, axis=1), jnp.sum(normal_grad * hidden_normal, axis=1)
        )
        active_grad = hidden_factor * (
            normal_grad
            - grad_first[:, None] / hidden_all
            - hidden_normal * grad_second[:, None] / hidden_all
        )
        gelu_pull = jax.vjp(partial(jax.nn.gelu, approximate=False), before_gelu)[1]
        pre_grad_b = gelu_pull(active_grad)[0].astype(jnp.bfloat16)
        first_shift_grad = jnp.sum(pre_grad_b, axis=0, dtype=jnp.float32)
        first_grad = jnp.einsum(
            "td,tf->df", ffn_rows, pre_grad_b, preferred_element_type=jnp.float32
        )
        ffn_in_grad = reduce_grads(pre_grad_b, fc1_weight[layer_index], local_rows)
        ffn_gain_grad = jnp.sum(ffn_in_grad * ffn_normal, axis=0)
        ffn_bias_grad = jnp.sum(ffn_in_grad, axis=0)
        middle_grad = gradient + norm_back(
            ffn_in_grad, ffn_normal, ffn_factor, ln_ffn_gain[layer_index]
        )
        post_gain_grad = jnp.sum(middle_grad * post_normal, axis=0)
        post_bias_grad = jnp.sum(middle_grad, axis=0)
        branch_grad = norm_back(middle_grad, post_normal, post_factor, ln_post_gain[layer_index])
        out_shift_grad = jnp.sum(branch_grad, axis=0)
        branch_rows = collect_grads(branch_grad.astype(jnp.bfloat16))
        scaled_grad = jnp.einsum(
            "td,cd->tc", branch_rows, out_weight[layer_index], preferred_element_type=jnp.float32
        )
        out_grad = jnp.einsum(
            "tc,td->cd", scaled_mine, branch_rows, preferred_element_type=jnp.float32
        )
        grad_send = lax.dynamic_slice_in_dim(scaled_grad, other_start, half_rows, 0)
        grad_recv = partner(grad_send.astype(jnp.bfloat16), "mp", 0).astype(grad_send.dtype)
        grad_own = lax.dynamic_slice_in_dim(scaled_grad, own_start, half_rows, 0)
        scaled_pair = join_cols(grad_own, grad_recv, is_upper).reshape(
            half_rows, pair_heads, head_width
        )
        pair_scale_grad = jnp.sum(attended * scaled_pair, axis=(0, 2))
        scale_grad = jnp.sum(pair_onehot * pair_scale_grad[:, None], axis=0)
        attended_grad_b = (scaled_pair * pair_scale[None, :, None]).astype(jnp.bfloat16)
        query_grad, key_grad, value_grad = attend_backward(
            queries, key_rows, value_rows, segment_ids, own_start, log_totals, attended_grad_b
        )
        query_own, query_other = split_cols(
            query_grad.reshape(half_rows, pair_cols), cols_here, is_upper
        )
        key_own, key_other = split_cols(
            key_grad.reshape(group_rows, pair_cols), cols_here, is_upper
        )
        value_own, value_other = split_cols(
            value_grad.reshape(group_rows, pair_cols), cols_here, is_upper
        )
        query_recv, key_recv, value_recv = (
            partner(query_other.astype(jnp.bfloat16), "mp", 0).astype(query_other.dtype),
            partner(key_other.astype(jnp.bfloat16), "mp", 0).astype(key_other.dtype),
            partner(value_other.astype(jnp.bfloat16), "mp", 0).astype(value_other.dtype),
        )
        query_grad_b = join_rows(query_own, query_recv, is_upper).astype(jnp.bfloat16)
        key_grad_b = (key_own + key_recv).astype(jnp.bfloat16)
        value_grad_b = (value_own + value_recv).astype(jnp.bfloat16)
        proj_grad = jnp.stack([query_grad_b, key_grad_b, value_grad_b], axis=1).reshape(
            -1, 3 * cols_here
        )
        pair_grad = jnp.stack(
            [
                jnp.sum(query_grad_b, axis=0, dtype=jnp.float32),
                jnp.sum(value_grad_b, axis=0, dtype=jnp.float32),
            ],
            axis=0,
        )
        qkv_grad = jnp.einsum(
            "td,tc->dc", attn_rows, proj_grad, preferred_element_type=jnp.float32
        ).reshape(model_width, 3, cols_here)
        attn_in_grad = reduce_grads(proj_grad, qkv_here, local_rows)
        attn_gain_grad = jnp.sum(attn_in_grad * attn_normal, axis=0)
        attn_bias_grad = jnp.sum(attn_in_grad, axis=0)
        gradient = middle_grad + norm_back(
            attn_in_grad, attn_normal, attn_factor, ln_attn_gain[layer_index]
        )
        sharded_list.insert(
            0,
            (
                qkv_grad,
                pair_grad,
                out_grad,
                first_grad,
                first_shift_grad,
                hidden_gain_grad,
                hidden_shift_grad,
                second_grad,
            ),
        )
        shared_list.insert(
            0,
            (
                attn_gain_grad,
                attn_bias_grad,
                scale_grad,
                out_shift_grad,
                post_gain_grad,
                post_bias_grad,
                ffn_gain_grad,
                ffn_bias_grad,
                second_shift_grad,
            ),
        )
    sharded = stack_layers(sharded_list, 8)
    shared = stack_layers(shared_list, 9)
    sharded = (
        lax.psum(sharded[0].astype(jnp.bfloat16), "rows").astype(jnp.float32),
        lax.psum(sharded[1].astype(jnp.bfloat16), "rows").astype(jnp.float32),
        lax.psum(sharded[2].astype(jnp.bfloat16), "rows").astype(jnp.float32),
        lax.psum(sharded[3].astype(jnp.bfloat16), "rows").astype(jnp.float32),
        lax.psum(sharded[4].astype(jnp.bfloat16), "rows").astype(jnp.float32),
        lax.psum(sharded[5].astype(jnp.bfloat16), "rows").astype(jnp.float32),
        lax.psum(sharded[6].astype(jnp.bfloat16), "rows").astype(jnp.float32),
        lax.psum(sharded[7].astype(jnp.bfloat16), "rows").astype(jnp.float32),
    )
    shared = lax.psum(
        (
            shared[0],
            shared[1],
            shared[2],
            shared[3],
            shared[4],
            shared[5],
            shared[6],
            shared[7],
            shared[8],
        ),
        ("rows", "mp"),
    )
    return (
        layer_output,
        gradient,
        shared[0],
        shared[1],
        sharded[0],
        sharded[1],
        shared[2],
        sharded[2],
        shared[3],
        shared[4],
        shared[5],
        shared[6],
        shared[7],
        sharded[3],
        sharded[4],
        sharded[5],
        sharded[6],
        sharded[7],
        shared[8],
    )


MESH_ID = pl.DeviceIdType.MESH
PLANE = ("core", "y", "x")
EVERY = ("y", "core", "z", "x")
f32 = jnp.float32
bf16 = jnp.bfloat16
GATHER, SCATTER, SECOND, MIDWAY = "gather", "scatter", "second", "midway"


def vmem_params(collective_id=None, mib=24):
    if collective_id is None:
        return pltpu.CompilerParams(vmem_limit_bytes=mib * 2**20)
    return pltpu.CompilerParams(
        vmem_limit_bytes=mib * 2**20, collective_id=collective_id, has_side_effects=True
    )


class Here:
    def __init__(self):
        self.x, self.y = lax.axis_index("x"), lax.axis_index("y")
        self.core, self.z = lax.axis_index("core"), lax.axis_index("z")

    def peer(self, flip_x, flip_y, flip_core, step_z):
        place = {}
        if flip_x:
            place["x"] = 1 - self.x
        if flip_y:
            place["y"] = 1 - self.y
        if flip_core:
            place["core"] = 1 - self.core
        if step_z:
            place["z"] = lax.rem(self.z + step_z, 4)
        return place

    def block(self, at_core, at_x, at_y):
        return (2 * at_core + lax.rem(at_y + self.z, 2)) * 2 + at_x


BY_X, BY_Y, BY_CORE = (1, 0, 0, 0), (0, 1, 0, 0), (0, 0, 1, 0)
BY_Z = tuple((0, 0, 0, step) for step in (1, 2, 3))
BY_LINE = BY_Z + tuple((0, 0, 1, step) for step in range(4))
BY_PLANE = tuple((flip & 1, flip >> 1 & 1, flip >> 2, 0) for flip in range(1, 8))


def remote(source, target, send_sem, recv_sem, place):
    return pltpu.make_async_remote_copy(
        src_ref=source,
        dst_ref=target,
        send_sem=send_sem,
        recv_sem=recv_sem,
        device_id=place,
        device_id_type=MESH_ID,
    )


def dma_sems(count):
    return pltpu.SemaphoreType.DMA((count,))


class Task:
    arrays = ()
    spaces = ()
    outs = ()
    out_spaces = ()
    scratch = ()
    reach = ()

    def moment(self, name):
        pass

    def start(self, here, ins, outs, scratch):
        pass

    def at_moment(self, name, here, ins, outs, scratch):
        pass

    def finish(self, here, ins, outs, scratch):
        pass


def run_tasks(ids, *tasks):
    reach = []
    for task in tasks:
        reach += [way for way in task.reach if way not in reach]

    near = []
    for task in tasks:
        near += [space == pltpu.VMEM for space in task.spaces]
    arrays = [array for task in tasks for array in task.arrays]
    loaded = [i for i, each in enumerate(near) if each]

    def kernel(*refs):
        refs = list(refs)
        *refs, load_sem = refs
        held = refs[len(refs) - len(loaded) :]
        refs = refs[: len(refs) - len(loaded)]
        loads = []
        for slot, index in enumerate(loaded):
            loads.append(pltpu.make_async_copy(refs[index], held[slot], load_sem.at[slot]))
            loads[-1].start()
            refs[index] = held[slot]
        views = [[], [], []]
        for kind, name in enumerate(("arrays", "outs", "scratch")):
            for task in tasks:
                count = len(getattr(task, name))
                views[kind].append(refs[:count])
                refs = refs[count:]
        here = Here()
        barrier = pltpu.get_barrier_semaphore()
        for way in reach:
            pl.semaphore_signal(barrier, inc=1, device_id=here.peer(*way), device_id_type=MESH_ID)
        pl.semaphore_wait(barrier, len(reach))
        for each in loads:
            each.wait()
        for task, *held in zip(tasks, *views):
            task.start(here, *held)

        def moment(name):
            for task, *held in zip(tasks, *views):
                task.at_moment(name, here, *held)

        tasks[0].moment = moment
        for task, *held in zip(tasks, *views):
            task.finish(here, *held)

    results = pl.pallas_call(
        kernel,
        out_shape=[out for task in tasks for out in task.outs],
        in_specs=[pl.BlockSpec(memory_space=pltpu.HBM)] * len(arrays),
        out_specs=[pl.BlockSpec(memory_space=s) for task in tasks for s in task.out_spaces],
        scratch_shapes=[each for task in tasks for each in task.scratch]
        + [pltpu.VMEM(arrays[i].shape, arrays[i].dtype) for i in loaded]
        + [dma_sems(len(loaded))],
        compiler_params=vmem_params(next(ids), 60),
    )(*arrays)
    results = list(results)
    split = []
    for task in tasks:
        split.append(results[: len(task.outs)])
        results = results[len(task.outs) :]
    return split


class PlaneMove(Task):
    def __init__(self, values, back=False, when=MIDWAY):
        self.back, self.when = back, when
        self.arrays, self.spaces = (values,), (pltpu.HBM,)
        self.outs = (jax.ShapeDtypeStruct(values.shape, values.dtype),)
        self.out_spaces = (pltpu.HBM,)
        self.scratch = (
            pltpu.VMEM(values.shape, values.dtype),
            dma_sems(3),
            dma_sems(2),
        )
        self.reach = (BY_Y,) + BY_LINE

    def bend(self, here):
        return lax.rem(here.z + here.core, 2) == here.y

    def ends(self, here):
        targets = [{"core": here.z // 2, "z": 2 * y + here.core} for y in range(2)]
        at_home = [(here.z // 2 == here.core) & (2 * y + here.core == here.z) for y in range(2)]
        origin_core = lax.rem(here.z, 2)
        origin_z = 2 * here.core + lax.rem(here.y + origin_core, 2)
        origin_home = (origin_core == here.core) & (origin_z == here.z)
        return targets, at_home, {"core": origin_core, "z": origin_z}, origin_home

    def plan(self, here, ins, outs, scratch):
        held, send, recv = scratch
        targets, at_home, origin, origin_home = self.ends(here)
        bend = self.bend(here)
        away_from = jnp.logical_not
        to_y = here.peer(*BY_Y)
        first, second = [], []
        if not self.back:
            over = remote(ins[0], held, send.at[2], recv.at[0], to_y)
            first.append((away_from(bend), over, True))
            for y in range(2):
                for legs, source, when in (
                    (first, ins[0], bend & (here.y == y)),
                    (second, held, bend & (here.y != y)),
                ):
                    away = remote(source, outs[0], send.at[y], recv.at[1], targets[y])
                    stay = pltpu.make_async_copy(source, outs[0], recv.at[1])
                    legs.append((when & away_from(at_home[y]), away, True))
                    legs.append((when & at_home[y], stay, False))
        else:
            ends_there = here.z // 2 == here.y
            for goes_on, target, slot in ((False, outs[0], 1), (True, held, 0)):
                when = away_from(ends_there) if goes_on else ends_there
                away = remote(ins[0], target, send.at[int(goes_on)], recv.at[slot], origin)
                stay = pltpu.make_async_copy(ins[0], target, recv.at[slot])
                first.append((when & away_from(origin_home), away, True))
                first.append((when & origin_home, stay, False))
            over = remote(held, outs[0], send.at[2], recv.at[1], to_y)
            second.append((bend, over, True))
        return first, second

    def start(self, here, ins, outs, scratch):
        for when, copy, _ in self.plan(here, ins, outs, scratch)[0]:
            pl.when(when)(copy.start)

    def at_moment(self, name, here, ins, outs, scratch):
        if name == self.when:
            held, _, recv = scratch

            @pl.when(self.bend(here))
            def _():
                pltpu.make_async_copy(held, held, recv.at[0]).wait()

            for when, copy, _ in self.plan(here, ins, outs, scratch)[1]:
                pl.when(when)(copy.start)

    def finish(self, here, ins, outs, scratch):
        self.at_moment("end", here, ins, outs, scratch)
        pltpu.make_async_copy(outs[0], outs[0], scratch[2].at[1]).wait()
        for legs in self.plan(here, ins, outs, scratch):
            for when, copy, is_remote in legs:
                if is_remote:
                    pl.when(when)(copy.wait_send)


class PlaneGather(Task):
    def __init__(self, block):
        rows, width = block.shape
        self.arrays, self.spaces = (block,), (pltpu.VMEM,)
        self.outs = (jax.ShapeDtypeStruct((8 * rows, width), block.dtype),)
        self.out_spaces = (pltpu.VMEM,)
        self.scratch = (dma_sems(11), dma_sems(11), pltpu.SemaphoreType.DMA)
        self.reach = (BY_X, BY_Y, BY_CORE)

    def place(self, here, o_ref, at_x, at_y, part=None):
        rows = o_ref.shape[0] // 8
        first = here.block(here.core, at_x, at_y) * rows
        if part is None:
            return o_ref.at[pl.ds(pl.multiple_of(first, rows), rows)]
        half = rows // 2
        return o_ref.at[pl.ds(pl.multiple_of(first + part * half, half), half)]

    def copies(self, here, x_ref, o_ref, send_sem, recv_sem):
        x, y = here.x, here.y
        half = x_ref.shape[0] // 2
        to_x, to_y, to_core = here.peer(*BY_X), here.peer(*BY_Y), here.peer(*BY_CORE)

        def copy(index, source, target, way):
            return remote(source, target, send_sem.at[index], recv_sem.at[index], way)

        def pass_on(index, way, *at):
            return copy(index, self.place(here, o_ref, *at), self.place(here, o_ref, *at), way)

        own = [self.place(here, o_ref, x, y, part) for part in (0, 1)]
        mine = [x_ref.at[pl.ds(part * half, half)] for part in (0, 1)]
        return [
            copy(0, mine[0], own[0], to_x),
            copy(1, mine[1], own[1], to_y),
            copy(2, mine[1], own[1], to_x),
            copy(3, mine[0], own[0], to_y),
            copy(4, x_ref, self.place(here, o_ref, x, y), to_core),
            pass_on(5, to_y, 1 - x, y, 0),
            pass_on(6, to_x, x, 1 - y, 1),
            pass_on(7, to_core, 1 - x, y),
            pass_on(8, to_core, x, 1 - y),
            pass_on(9, to_core, 1 - x, 1 - y, 0),
            pass_on(10, to_core, 1 - x, 1 - y, 1),
        ]

    def keep(self, here, x_ref, o_ref, own_sem):
        return pltpu.make_async_copy(x_ref, self.place(here, o_ref, here.x, here.y), own_sem)

    def start(self, here, ins, outs, scratch):
        copies = self.copies(here, ins[0], outs[0], scratch[0], scratch[1])
        for index in range(5):
            copies[index].start()
        self.keep(here, ins[0], outs[0], scratch[2]).start()

    def finish(self, here, ins, outs, scratch, work=None, moment=None):
        rows = ins[0].shape[0]
        copies = self.copies(here, ins[0], outs[0], scratch[0], scratch[1])

        def done(flip_core, flip_x, flip_y):
            if work is not None:
                at_core = 1 - here.core if flip_core else here.core
                at_x = 1 - here.x if flip_x else here.x
                at_y = 1 - here.y if flip_y else here.y
                work(pl.multiple_of(here.block(at_core, at_x, at_y) * rows, rows))

        self.keep(here, ins[0], outs[0], scratch[2]).wait()
        done(0, 0, 0)
        copies[4].wait_recv()
        done(1, 0, 0)
        for index in range(4):
            copies[index].wait_recv()
            copies[5 + index].start()
        if moment is not None:
            moment("spare")
        done(0, 1, 0)
        done(0, 0, 1)
        copies[7].wait_recv()
        done(1, 1, 0)
        copies[8].wait_recv()
        done(1, 0, 1)
        copies[5].wait_recv()
        copies[9].start()
        copies[6].wait_recv()
        copies[10].start()
        done(0, 1, 1)
        if moment is not None:
            moment("soon")
        copies[9].wait_recv()
        copies[10].wait_recv()
        done(1, 1, 1)
        for each in copies:
            each.wait_send()


class OrderedGather(PlaneGather):
    def ends(self, here):
        over_x = here.core == 0
        first = (jnp.where(over_x, 1 - here.x, here.x), jnp.where(over_x, here.y, 1 - here.y))
        second = (jnp.where(over_x, here.x, 1 - here.x), jnp.where(over_x, 1 - here.y, here.y))
        return first, second

    def copies(self, here, x_ref, o_ref, send_sem, recv_sem):
        half = x_ref.shape[0] // 2
        first, second = self.ends(here)
        to_first, to_second = ({"x": at[0], "y": at[1]} for at in (first, second))
        to_core = here.peer(*BY_CORE)

        def copy(index, source, target, way):
            return remote(source, target, send_sem.at[index], recv_sem.at[index], way)

        def pass_on(index, way, *at):
            return copy(index, self.place(here, o_ref, *at), self.place(here, o_ref, *at), way)

        own = [self.place(here, o_ref, here.x, here.y, part) for part in (0, 1)]
        mine = [x_ref.at[pl.ds(part * half, half)] for part in (0, 1)]
        far = (1 - here.x, 1 - here.y)
        return [
            copy(0, mine[0], own[0], to_first),
            copy(1, mine[1], own[1], to_first),
            copy(2, mine[1], own[1], to_second),
            copy(3, mine[0], own[0], to_second),
            copy(4, x_ref, self.place(here, o_ref, here.x, here.y), to_core),
            pass_on(5, to_second, *first, 0),
            pass_on(6, to_first, *second, 1),
            pass_on(7, to_core, *first),
            pass_on(8, to_core, *second),
            pass_on(9, to_core, *far, 0),
            pass_on(10, to_core, *far, 1),
        ]

    def start(self, here, ins, outs, scratch):
        copies = self.copies(here, ins[0], outs[0], scratch[0], scratch[1])
        for index in (0, 1, 4):
            copies[index].start()
        self.keep(here, ins[0], outs[0], scratch[2]).start()

    def finish(self, here, ins, outs, scratch, work=None, moment=None):
        rows = ins[0].shape[0]
        copies = self.copies(here, ins[0], outs[0], scratch[0], scratch[1])
        first, second = self.ends(here)
        far = (1 - here.x, 1 - here.y)

        def done(at_core, at):
            if work is not None:
                work(pl.multiple_of(here.block(at_core, *at) * rows, rows))

        self.keep(here, ins[0], outs[0], scratch[2]).wait()
        done(here.core, (here.x, here.y))
        copies[0].wait_send()
        copies[1].wait_send()
        copies[2].start()
        copies[3].start()
        copies[4].wait_recv()
        done(1 - here.core, (here.x, here.y))
        copies[0].wait_recv()
        copies[5].start()
        copies[1].wait_recv()
        copies[7].start()
        done(here.core, first)
        copies[7].wait_recv()
        done(1 - here.core, second)
        copies[2].wait_recv()
        copies[6].start()
        copies[3].wait_recv()
        copies[8].start()
        if moment is not None:
            moment("spare")
        done(here.core, second)
        copies[8].wait_recv()
        done(1 - here.core, first)
        copies[5].wait_recv()
        copies[9].start()
        copies[6].wait_recv()
        copies[10].start()
        done(here.core, far)
        if moment is not None:
            moment("soon")
        copies[9].wait_recv()
        copies[10].wait_recv()
        done(1 - here.core, far)
        for each in copies[2:]:
            each.wait_send()


class PlaneScatter(Task):
    def __init__(self, rows, width, weight_dim):
        half = rows // 2
        self.weight_dim = weight_dim
        self.scratch = (
            pltpu.VMEM((4, rows, width), bf16),
            pltpu.VMEM((4, rows, width), bf16),
            pltpu.VMEM((rows, width), bf16),
            pltpu.VMEM((2, half, width), bf16),
            pltpu.VMEM((2, half, width), bf16),
            pltpu.VMEM((2, half, width), bf16),
            pltpu.VMEM((2, half, width), bf16),
            pltpu.VMEM((2, half, width), bf16),
            pltpu.VMEM((half, width), f32),
            pltpu.VMEM((half, width), f32),
            dma_sems(10),
            dma_sems(10),
        )
        self.reach = (BY_X, BY_Y, BY_CORE)

    def finish(self, here, ins, outs, scratch, rows_of, weight_of, early=None, idle=None):
        o_ref = outs[0]
        (
            sib_out,
            sib_in,
            diag_out,
            diag_in,
            last_x_out,
            last_y_out,
            last_x_in,
            last_y_in,
            wait_x,
            wait_y,
            send_sem,
            recv_sem,
        ) = scratch
        rows = o_ref.shape[0]
        half = rows // 2
        x, y, core = here.x, here.y, here.core
        to_x, to_y, to_core = here.peer(*BY_X), here.peer(*BY_Y), here.peer(*BY_CORE)

        def term(at_core, at_x, at_y):
            first = pl.multiple_of(here.block(at_core, at_x, at_y) * rows, rows)
            return lax.dot_general(
                rows_of(first),
                weight_of(),
                (((1,), (self.weight_dim,)), ((), ())),
                preferred_element_type=f32,
            )

        def copy(index, source, target, way):
            return remote(source, target, send_sem.at[index], recv_sem.at[index], way)

        places = ((1 - x, 1 - y), (1 - x, y), (x, 1 - y), (x, y))
        siblings = [copy(i, sib_out.at[i], sib_in.at[i], to_core) for i in range(4)]

        def help_sibling(i):
            sib_out[i] = term(1 - core, *places[i]).astype(bf16)
            siblings[i].start()

        def joined(i):
            mine = term(core, *places[i])
            siblings[i].wait_recv()
            return mine + sib_in[i].astype(f32)

        help_sibling(0)
        total = joined(0)
        diag_out[...] = total.astype(bf16)
        diag_x = copy(4, diag_out.at[pl.ds(0, half)], diag_in.at[0], to_x)
        diag_y = copy(5, diag_out.at[pl.ds(half, half)], diag_in.at[1], to_y)
        diag_x.start()
        diag_y.start()
        help_sibling(1)
        total = joined(1)
        last_x_out[0] = total[:half].astype(bf16)
        x_0 = copy(6, last_x_out.at[0], last_x_in.at[0], to_x)
        x_0.start()
        wait_x[...] = total[half:]
        if early is not None:
            early()
        help_sibling(2)
        total = joined(2)
        last_y_out[1] = total[half:].astype(bf16)
        y_1 = copy(7, last_y_out.at[1], last_y_in.at[1], to_y)
        y_1.start()
        wait_y[...] = total[:half]
        help_sibling(3)
        diag_y.wait_recv()
        last_x_out[1] = (wait_x[...] + diag_in[1].astype(f32)).astype(bf16)
        x_1 = copy(8, last_x_out.at[1], last_x_in.at[1], to_x)
        x_1.start()
        diag_x.wait_recv()
        last_y_out[0] = (wait_y[...] + diag_in[0].astype(f32)).astype(bf16)
        y_0 = copy(9, last_y_out.at[0], last_y_in.at[0], to_y)
        y_0.start()
        o_ref[...] = joined(3)
        if idle is not None:
            idle()
        for part, (by_x, by_y) in enumerate(((x_0, y_0), (x_1, y_1))):
            by_x.wait_recv()
            by_y.wait_recv()
            piece = pl.ds(part * half, half)
            o_ref[piece, :] += last_x_in[part].astype(f32) + last_y_in[part].astype(f32)
        for sent in (*siblings, diag_x, diag_y, x_0, y_1, x_1, y_0):
            sent.wait_send()


class PlaneSum(Task):
    def __init__(self, values):
        self.arrays, self.spaces = (values,), (pltpu.VMEM,)
        self.outs = (jax.ShapeDtypeStruct(values.shape, f32),)
        self.out_spaces = (pltpu.VMEM,)
        self.scratch = (pltpu.VMEM((7, *values.shape), f32), dma_sems(7), dma_sems(7))
        self.reach = BY_PLANE

    def copies(self, here, ins, scratch):
        got, send_sem, recv_sem = scratch
        return [
            remote(ins[0], got.at[i], send_sem.at[i], recv_sem.at[i], here.peer(*way))
            for i, way in enumerate(BY_PLANE)
        ]

    def start(self, here, ins, outs, scratch):
        for each in self.copies(here, ins, scratch):
            each.start()

    def finish(self, here, ins, outs, scratch):
        copies = self.copies(here, ins, scratch)
        for each in copies:
            each.wait_recv()
        got = scratch[0]
        by_x = [ins[0][...] + got[0]]
        for flip in (2, 4, 6):
            by_x.append(got[flip - 1] + got[flip])
        outs[0][...] = (by_x[0] + by_x[1]) + (by_x[2] + by_x[3])
        for each in copies:
            each.wait_send()


class LineGather(Task):
    def __init__(self, values):
        self.arrays, self.spaces = (values,), (pltpu.HBM,)
        self.outs = (jax.ShapeDtypeStruct((4, *values.shape), values.dtype),)
        self.out_spaces = (pltpu.HBM,)
        self.scratch = (dma_sems(4), dma_sems(3))
        self.reach = BY_Z

    def copies(self, here, ins, outs, scratch):
        target = outs[0].at[here.z]
        keep = pltpu.make_async_copy(ins[0], target, scratch[0].at[3])
        return keep, [
            remote(ins[0], target, scratch[0].at[i], scratch[1].at[i], here.peer(*way))
            for i, way in enumerate(BY_Z)
        ]

    def start(self, here, ins, outs, scratch):
        keep, copies = self.copies(here, ins, outs, scratch)
        for each in copies:
            each.start()
        keep.start()

    def finish(self, here, ins, outs, scratch):
        keep, copies = self.copies(here, ins, outs, scratch)
        for each in copies:
            each.wait()
        keep.wait()


class HeadGather(Task):
    def __init__(self, qkv, out, layer, when="start"):
        _, kinds, both, width = qkv.shape
        self.layer, self.when = layer, when
        self.arrays, self.spaces = (qkv, out), (pltpu.HBM,) * 2
        self.outs = (jax.ShapeDtypeStruct((kinds + 1, 2, both // 2, width), qkv.dtype),)
        self.out_spaces = (pltpu.HBM,)
        self.scratch = (dma_sems(8), dma_sems(8))
        self.reach = BY_LINE

    def pieces(self, outs, shard, part):
        half = outs[0].shape[3] // 2
        columns = pl.ds(pl.multiple_of(part * half, half), half)
        return outs[0].at[pl.ds(0, 3), shard, :, columns], outs[0].at[3, shard, :, columns]

    def copies(self, here, ins, outs, scratch):
        shard, target_core = lax.rem(here.z, 2), here.z // 2
        wide, half = outs[0].shape[2], outs[0].shape[3] // 2
        rows = pl.ds(pl.multiple_of(here.y * wide, wide), wide)
        columns = pl.ds(pl.multiple_of(here.core * half, half), half)
        sources = (ins[0].at[self.layer, :, rows, columns], ins[1].at[self.layer, rows, columns])
        targets = self.pieces(outs, shard, here.core)
        keeps, aways = [], []
        for kind in range(2):
            recv_sem = scratch[1].at[4 * kind + 2 * shard + here.core]
            keeps.append(pltpu.make_async_copy(sources[kind], targets[kind], recv_sem))
            for step in range(4):
                place = {"core": target_core, "z": lax.rem(here.z + step, 4)}
                send_sem = scratch[0].at[4 * kind + step]
                aways.append(remote(sources[kind], targets[kind], send_sem, recv_sem, place))
        return keeps, aways

    def begin(self, here, ins, outs, scratch):
        keeps, aways = self.copies(here, ins, outs, scratch)
        for index, each in enumerate(aways):
            if index % 4:
                each.start()
        at_home = here.z // 2 == here.core
        for kind in range(2):
            pl.when(at_home)(keeps[kind].start)
            pl.when(jnp.logical_not(at_home))(aways[4 * kind].start)

    def start(self, *held):
        self.at_moment("start", *held)

    def at_moment(self, name, *held):
        if name == self.when:
            self.begin(*held)

    def arrive(self, kind, outs, scratch):
        for shard in range(2):
            for part in range(2):
                piece = self.pieces(outs, shard, part)[kind]
                recv_sem = scratch[1].at[4 * kind + 2 * shard + part]
                pltpu.make_async_copy(piece, piece, recv_sem).wait()

    def sent(self, here, ins, outs, scratch):
        keeps, aways = self.copies(here, ins, outs, scratch)
        for index, each in enumerate(aways):
            if index % 4:
                each.wait_send()
        for kind in range(2):
            pl.when(here.z // 2 != here.core)(aways[4 * kind].wait_send)

    def finish(self, here, ins, outs, scratch):
        for kind in range(2):
            self.arrive(kind, outs, scratch)
        self.sent(here, ins, outs, scratch)


class LineScatter(Task):
    def __init__(self, values):
        shape = values.shape[1:]
        self.arrays, self.spaces = (values,), (pltpu.VMEM,)
        self.outs, self.out_spaces = (jax.ShapeDtypeStruct(shape, values.dtype),), (pltpu.VMEM,)
        self.scratch = (pltpu.VMEM((3, *shape), values.dtype), dma_sems(3), dma_sems(3))
        self.reach = BY_Z

    def copies(self, here, ins, scratch):
        got, send_sem, recv_sem = scratch
        return [
            remote(
                ins[0].at[lax.rem(here.z + i + 1, 4)],
                got.at[i],
                send_sem.at[i],
                recv_sem.at[i],
                here.peer(*way),
            )
            for i, way in enumerate(BY_Z)
        ]

    def start(self, here, ins, outs, scratch):
        for each in self.copies(here, ins, scratch):
            each.start()

    def finish(self, here, ins, outs, scratch):
        copies = self.copies(here, ins, scratch)
        for each in copies:
            each.wait_recv()
        total = ins[0][here.z].astype(f32)
        for i in range(3):
            total = total + scratch[0][i].astype(f32)
        outs[0][...] = total.astype(outs[0].dtype)
        for each in copies:
            each.wait_send()


class HeadScatter(Task):
    def __init__(self, values):
        kinds, _, wide, width = values.shape
        shape = (kinds, wide, width // 2)
        self.arrays, self.spaces = (values,), (pltpu.VMEM,)
        self.outs, self.out_spaces = (jax.ShapeDtypeStruct(shape, values.dtype),), (pltpu.VMEM,)
        self.scratch = (pltpu.VMEM((4, *shape), values.dtype), dma_sems(4), dma_sems(4))
        self.reach = BY_LINE

    def copies(self, here, ins, scratch):
        got, send_sem, recv_sem = scratch
        half = ins[0].shape[3] // 2
        triples = []
        for shard in range(2):
            for part in range(2):
                source = ins[0].at[:, shard, :, pl.ds(part * half, half)]
                target_z = 2 * here.core + shard
                slot = recv_sem.at[here.z]
                away = remote(
                    source,
                    got.at[here.z],
                    send_sem.at[2 * shard + part],
                    slot,
                    {"core": part, "z": target_z},
                )
                stay = pltpu.make_async_copy(source, got.at[here.z], slot)
                at_home = (target_z == here.z) & (here.core == part)
                triples.append((away, stay, at_home))
        return triples

    def start(self, here, ins, outs, scratch):
        for away, stay, at_home in self.copies(here, ins, scratch):
            pl.when(at_home)(stay.start)
            pl.when(jnp.logical_not(at_home))(away.start)

    def finish(self, here, ins, outs, scratch):
        got, send_sem, recv_sem = scratch
        for plane in range(4):
            pltpu.make_async_copy(got.at[plane], got.at[plane], recv_sem.at[plane]).wait()
        total = got[0].astype(f32)
        for plane in range(1, 4):
            total = total + got[plane].astype(f32)
        outs[0][...] = total.astype(outs[0].dtype)
        for away, stay, at_home in self.copies(here, ins, scratch):
            pl.when(jnp.logical_not(at_home))(away.wait_send)


class RowsGather(Task):
    def __init__(self, values, when="start"):
        self.when = when
        self.arrays, self.spaces = (values,), (pltpu.HBM,)
        self.outs = (jax.ShapeDtypeStruct((4, *values.shape), values.dtype),)
        self.out_spaces = (pltpu.HBM,)
        self.scratch = (dma_sems(4), dma_sems(3))
        self.reach = (BY_Y, BY_CORE)

    def copies(self, here, ins, outs, scratch):
        send_sem, recv_sem = scratch
        own = outs[0].at[2 * here.y + here.core]
        over = outs[0].at[2 * (1 - here.y) + here.core]
        to_y, to_core = here.peer(*BY_Y), here.peer(*BY_CORE)
        return (
            pltpu.make_async_copy(ins[0], own, send_sem.at[3]),
            remote(ins[0], own, send_sem.at[0], recv_sem.at[0], to_y),
            remote(ins[0], own, send_sem.at[1], recv_sem.at[1], to_core),
            remote(over, over, send_sem.at[2], recv_sem.at[2], to_core),
        )

    def start(self, *held):
        self.at_moment("start", *held)

    def at_moment(self, name, *held):
        if name == self.when:
            self.begin(*held)

    def begin(self, here, ins, outs, scratch):
        keep, by_y, by_core, again = self.copies(here, ins, outs, scratch)
        by_y.start()
        by_core.start()
        keep.start()

    def finish(self, here, ins, outs, scratch):
        keep, by_y, by_core, again = self.copies(here, ins, outs, scratch)
        by_y.wait_recv()
        again.start()
        by_core.wait_recv()
        again.wait_recv()
        for each in (by_y, by_core, again):
            each.wait_send()
        keep.wait()


class StepSum(Task):
    def __init__(self, values):
        self.arrays, self.spaces = (values,), (pltpu.VMEM,)
        self.outs = (jax.ShapeDtypeStruct(values.shape, f32),)
        self.out_spaces = (pltpu.VMEM,)
        self.scratch = (
            pltpu.VMEM((2, *values.shape), f32),
            pltpu.VMEM((3, *values.shape), f32),
            dma_sems(3),
            dma_sems(3),
        )
        self.reach = (BY_X, BY_Y, BY_CORE)

    def leg(self, here, index, source, scratch):
        _, got, send_sem, recv_sem = scratch
        way = here.peer(*self.reach[index])
        return remote(source, got.at[index], send_sem.at[index], recv_sem.at[index], way)

    def start(self, here, ins, outs, scratch):
        self.leg(here, 0, ins[0], scratch).start()

    def at_moment(self, name, here, ins, outs, scratch):
        part, got = scratch[:2]
        if name == MIDWAY:
            self.leg(here, 0, ins[0], scratch).wait()
            part[0] = ins[0][...] + got[0]
            self.leg(here, 1, part.at[0], scratch).start()
        if name == "closing":
            self.leg(here, 1, part.at[0], scratch).wait()
            part[1] = part[0] + got[1]
            self.leg(here, 2, part.at[1], scratch).start()

    def finish(self, here, ins, outs, scratch):
        part, got = scratch[:2]
        self.leg(here, 2, part.at[1], scratch).wait()
        outs[0][...] = part[1] + got[2]


class LineSum(Task):
    def __init__(self, values):
        self.arrays, self.spaces = (values,), (pltpu.VMEM,)
        self.outs = (jax.ShapeDtypeStruct(values.shape, f32),)
        self.out_spaces = (pltpu.VMEM,)
        self.scratch = (pltpu.VMEM((4, *values.shape), f32), dma_sems(3), dma_sems(4))
        self.reach = BY_Z

    def copies(self, here, ins, scratch):
        got, send_sem, recv_sem = scratch
        there, slot = got.at[here.z], recv_sem.at[here.z]
        keep = pltpu.make_async_copy(ins[0], there, slot)
        return keep, [
            remote(ins[0], there, send_sem.at[i], slot, here.peer(*way))
            for i, way in enumerate(BY_Z)
        ]

    def start(self, here, ins, outs, scratch):
        keep, copies = self.copies(here, ins, scratch)
        for each in copies:
            each.start()
        keep.start()

    def finish(self, here, ins, outs, scratch):
        got, _, recv_sem = scratch
        _, copies = self.copies(here, ins, scratch)
        for plane in range(4):
            pltpu.make_async_copy(got.at[plane], got.at[plane], recv_sem.at[plane]).wait()
        outs[0][...] = (got[0] + got[1]) + (got[2] + got[3])
        for each in copies:
            each.wait_send()


def to_columns(upper, lower):
    place = lax.broadcasted_iota(jnp.int32, (128, upper.shape[1]), 0)
    return jnp.transpose(jnp.where(place < 64, upper, lower))


def both_columns(upper, lower):
    lane = lax.broadcasted_iota(jnp.int32, (upper.shape[0], 128), 1)
    return jnp.where(lane < 64, upper, lower)


def in_chunks(rows, chunk, step):
    def one(index, carry):
        step(pl.multiple_of(index * chunk, chunk))
        return carry

    lax.fori_loop(0, rows // chunk, one, 0)


def fold(values):
    total = values[:8]
    for first in range(8, values.shape[0], 8):
        total = total + values[first : first + 8]
    return total


class Parts(Task):
    def use(self, parts):
        self.parts = parts
        self.scratch = list(self.scratch)
        self.at = {}
        reach = []
        for name, part in parts.items():
            self.at[name] = (len(self.scratch), len(self.scratch) + len(part.scratch))
            self.scratch += list(part.scratch)
            reach += [way for way in part.reach if way not in reach]
        self.reach = reach

    def held(self, scratch, name):
        first, last = self.at[name]
        return scratch[first:last]


def norm_pull(grad_out, normal, factor, gain_row):
    scaled = grad_out * gain_row
    width = scaled.shape[1]
    mean = jnp.sum(scaled, axis=1, keepdims=True) / width
    inner = jnp.sum(scaled * normal, axis=1, keepdims=True) / width
    return factor * (scaled - mean - normal * inner)


class StepThenLine(Parts):
    def __init__(self, values):
        self.arrays, self.spaces = (values,), (pltpu.VMEM,)
        self.outs = (jax.ShapeDtypeStruct(values.shape, f32),)
        self.out_spaces = (pltpu.VMEM,)
        self.scratch = (pltpu.VMEM(values.shape, f32),)
        self.use(dict(step=StepSum(values), line=LineSum(values)))

    def start(self, here, ins, outs, scratch):
        self.parts["step"].start(here, ins, scratch[:1], self.held(scratch, "step"))

    def at_moment(self, name, here, ins, outs, scratch):
        held = (here, ins, scratch[:1], self.held(scratch, "step"))
        self.parts["step"].at_moment(name, *held)
        if name == "tail":
            self.parts["step"].finish(*held)
            self.parts["line"].start(here, scratch[:1], outs, self.held(scratch, "line"))

    def finish(self, here, ins, outs, scratch):
        self.parts["line"].finish(here, scratch[:1], outs, self.held(scratch, "line"))


def normalize(values):
    width = values.shape[1]
    centered = values - jnp.sum(values, axis=1, keepdims=True) / width
    factor = lax.rsqrt(jnp.sum(centered * centered, axis=1, keepdims=True) / width + epsilon)
    return centered * factor, factor


def wide_column(column):
    return jnp.broadcast_to(column, (column.shape[0], 128))


def hidden_row(small_ref, layer, at, part):
    first = small_ref.shape[2] - (3 - at) * part
    return jnp.concatenate(
        [small_ref[z, layer : layer + 1, first : first + part] for z in range(4)], axis=1
    )


def scale_of(here, head_scale_ref, layer, wide):
    row = head_scale_ref[layer : layer + 1, :]
    place = lax.broadcasted_iota(jnp.int32, row.shape, 1)
    pair = []
    for i in range(2):
        head = ((2 * here.core + i) * 2 + here.x) * 2 + here.y
        pair.append(jnp.sum(jnp.where(place == head, row, 0.0), axis=1, keepdims=True))
    lane = lax.broadcasted_iota(jnp.int32, (1, 2 * wide), 1)
    return jnp.where(lane < wide, pair[0], pair[1])


NARROW = 128
CHUNK = 256


class FfnForward(Parts):
    def __init__(self, block, first, second, small, middle, shift, norm, layer, late):
        rows, width = block.shape
        hidden = first.shape[1]
        self.late, self.layer, self.last = late, layer, norm is None
        self.arrays = (block, first, second, small, middle, shift, *(norm or ()))
        self.spaces = (pltpu.VMEM,) * 2 + (pltpu.HBM if late else pltpu.VMEM,)
        self.spaces += (pltpu.VMEM,) * (len(self.arrays) - 3)
        self.outs = (
            jax.ShapeDtypeStruct((rows, width), f32),
            jax.ShapeDtypeStruct((8 * rows, width), bf16),
            jax.ShapeDtypeStruct((8 * rows, hidden), f32),
            jax.ShapeDtypeStruct((8 * rows, hidden), f32),
            jax.ShapeDtypeStruct((8 * rows, hidden), bf16),
            jax.ShapeDtypeStruct((2, 8 * rows), f32),
        )
        self.out_spaces = (pltpu.VMEM,) + (pltpu.HBM,) * 4 + (pltpu.VMEM,)
        self.outs += (jax.ShapeDtypeStruct((rows, width), bf16),)
        if norm:
            self.outs += (jax.ShapeDtypeStruct((rows, width), f32),)
            self.outs += (jax.ShapeDtypeStruct((rows, 128), f32),)
        self.out_spaces += (pltpu.VMEM,) * (len(self.outs) - 6)
        self.base = len(self.outs)
        self.scratch = (
            pltpu.VMEM((8 * rows, width), bf16),
            pltpu.VMEM((8 * rows, hidden), f32),
            pltpu.VMEM((8 * rows, hidden), f32),
            pltpu.VMEM((8 * rows, hidden), bf16),
            pltpu.VMEM((2, 8 * rows), f32),
            pltpu.VMEM((rows, 128), f32),
            dma_sems(4),
        )
        parts = dict(
            gather=PlaneGather(block),
            scatter=PlaneScatter(rows, width, 0),
            sums=PlaneSum(jax.ShapeDtypeStruct((2, 8 * rows), f32)),
        )
        if late:
            parts[SECOND] = WeightGather(second, layer, 0)
            self.outs += parts[SECOND].outs
            self.out_spaces += (pltpu.VMEM,)
        self.use(parts)

    def start(self, here, ins, outs, scratch):
        self.parts[GATHER].start(here, ins[:1], scratch[:1], self.held(scratch, GATHER))
        if self.late:
            held = self.held(scratch, SECOND)
            self.parts[SECOND].start(here, ins[2:3], outs[self.base :], held)

    def finish(self, here, ins, outs, scratch):
        block_ref, first_ref, second_ref, small_ref, middle_ref, row_ref = ins[:6]
        part = first_ref.shape[1] // 4
        shift, gain, bias = (hidden_row(small_ref, self.layer, at, part) for at in range(3))
        out_ref, rows_out, slope_out, normal_out, mixed_out, total_ref = outs[:6]
        if self.late:
            second_ref = outs[self.base]
        rows_buf, before, active, mixed, sums, columns, save = scratch[:7]
        rows = block_ref.shape[0]
        hidden_all = 8 * first_ref.shape[1]

        def work(first):
            before[pl.ds(first, rows), :] = lax.dot_general(
                rows_buf[pl.ds(first, rows), :],
                first_ref[...],
                (((1,), (0,)), ((), ())),
                preferred_element_type=f32,
            )

            def step(at):
                piece = pl.ds(pl.multiple_of(first + at, CHUNK), CHUNK)
                u = before[piece, :] + shift
                area = 0.5 * (1.0 + lax.erf(u * 0.5**0.5))
                a = u * area
                active[piece, :] = a
                before[piece, :] = area + u * (jnp.exp(-0.5 * u * u) * (0.5 / jnp.pi) ** 0.5)
                columns[pl.ds(at, CHUNK), :] = both_columns(
                    jnp.sum(a, axis=1, keepdims=True), jnp.sum(a * a, axis=1, keepdims=True)
                )

            in_chunks(rows, CHUNK, step)
            turned = jnp.transpose(columns[...])
            sums[0:1, pl.ds(first, rows)] = turned[0:1]
            sums[1:2, pl.ds(first, rows)] = turned[64:65]

        self.parts[GATHER].finish(
            here, ins[:1], scratch[:1], self.held(scratch, GATHER), work
        )
        held = self.held(scratch, "sums")
        self.parts["sums"].start(here, (sums,), None, held)
        keep_rows = pltpu.make_async_copy(rows_buf, rows_out, save.at[0])
        keep_rows.start()
        keep_slope = pltpu.make_async_copy(before, slope_out, save.at[1])
        keep_slope.start()
        self.parts["sums"].finish(here, (sums,), (total_ref,), held)
        if self.late:
            held = self.held(scratch, SECOND)
            self.parts[SECOND].finish(here, ins[2:3], outs[self.base :], held)
        self.moment(MIDWAY)

        def rows_of(first):
            average = total_ref[0:1, pl.ds(first, rows)] / hidden_all
            spread = total_ref[1:2, pl.ds(first, rows)] / hidden_all - average * average
            columns[...] = to_columns(average, lax.rsqrt(spread + epsilon))

            def step(at):
                piece = pl.ds(pl.multiple_of(first + at, CHUNK), CHUNK)
                pair = columns[pl.ds(at, CHUNK), :]
                normal = (active[piece, :] - pair[:, 0:1]) * pair[:, 64:65]
                active[piece, :] = normal
                mixed[piece, :] = (normal * gain + bias).astype(bf16)

            in_chunks(rows, CHUNK, step)
            return mixed[pl.ds(first, rows), :]

        keep_mixed = pltpu.make_async_copy(mixed, mixed_out, save.at[2])
        keep_normal = pltpu.make_async_copy(active, normal_out, save.at[3])

        def idle():
            keep_mixed.start()
            keep_normal.start()
            self.moment("closing")

        self.parts[SCATTER].finish(
            here,
            None,
            (out_ref,),
            self.held(scratch, SCATTER),
            rows_of,
            lambda: second_ref[...],
            idle=idle,
        )
        layer = slice(self.layer, self.layer + 1)
        after = slice(self.layer + 1, self.layer + 2)

        def settle(at):
            piece = pl.ds(at, NARROW)
            residual = middle_ref[piece, :] + out_ref[piece, :] + row_ref[layer, :]
            out_ref[piece, :] = residual
            if self.last:
                outs[6][piece, :] = residual.astype(bf16)
            else:
                normal, factor = normalize(residual)
                outs[6][piece, :] = (normal * ins[6][after, :] + ins[7][after, :]).astype(bf16)
                outs[7][piece, :] = normal
                outs[8][piece, :] = wide_column(factor)

        in_chunks(rows, NARROW, settle)
        for each in (keep_rows, keep_slope, keep_mixed, keep_normal):
            each.wait()


class FfnBackward(Parts):
    def __init__(
        self,
        block,
        first,
        second,
        small,
        slope,
        normal,
        mixed,
        ffn_rows,
        totals,
        gradient,
        norms,
        layer,
    ):
        self.layer = layer
        rows, width = block.shape
        hidden = second.shape[0]
        self.arrays = (block, first, second, small, totals, slope, normal, mixed, ffn_rows)
        self.spaces = (pltpu.VMEM,) * 5 + (pltpu.HBM,) * 4
        self.arrays += (gradient, *norms)
        self.spaces += (pltpu.VMEM,) * 7
        self.outs = (
            jax.ShapeDtypeStruct((rows, width), f32),
            jax.ShapeDtypeStruct((4, width, hidden // 4), bf16),
            jax.ShapeDtypeStruct((hidden // 4, width), bf16),
            jax.ShapeDtypeStruct((3, hidden), f32),
            jax.ShapeDtypeStruct((rows, width), bf16),
            jax.ShapeDtypeStruct((8, width), f32),
        )
        self.out_spaces = (pltpu.VMEM,) * 6
        self.scratch = (
            pltpu.VMEM((8 * rows, width), bf16),
            pltpu.VMEM((8 * rows, hidden), f32),
            pltpu.VMEM((8 * rows, hidden), f32),
            pltpu.VMEM((8 * rows, hidden), f32),
            pltpu.VMEM((8 * rows, hidden), bf16),
            pltpu.VMEM((8 * rows, width), bf16),
            pltpu.VMEM((8 * rows, hidden), bf16),
            pltpu.VMEM((hidden, width), f32),
            pltpu.VMEM((2, 8 * rows), f32),
            pltpu.VMEM((2, 8 * rows), f32),
            pltpu.VMEM((rows, 128), f32),
            pltpu.VMEM((rows, 128), f32),
            pltpu.VMEM((3, 8, hidden), f32),
            dma_sems(4),
            pltpu.VMEM((4, hidden // 4, width), bf16),
            pltpu.VMEM((6, 8, width), f32),
        )
        self.use(
            dict(
            gather=PlaneGather(block),
            scatter=PlaneScatter(rows, width, 1),
            second=LineScatter(jax.ShapeDtypeStruct((4, hidden // 4, width), bf16)),
            sums=PlaneSum(jax.ShapeDtypeStruct((2, 8 * rows), f32)),
            )
        )

    def loads(self, ins, scratch):
        targets = (scratch[2], scratch[4], scratch[1], scratch[5])
        return [
            pltpu.make_async_copy(source, target, scratch[13].at[i])
            for i, (source, target) in enumerate(zip((ins[6], ins[7], ins[5], ins[8]), targets))
        ]

    def start(self, here, ins, outs, scratch):
        self.parts[GATHER].start(here, ins[:1], scratch[:1], self.held(scratch, GATHER))
        for each in self.loads(ins, scratch):
            each.start()

    def finish(self, here, ins, outs, scratch):
        block_ref, first_ref, second_ref, hidden_ref, totals_ref = ins[:5]
        mid_gain = hidden_row(hidden_ref, self.layer, 1, first_ref.shape[1] // 4)
        out_ref, first_grad, second_quarter, small_ref, branch_ref, vector_ref = outs
        second_grad, vectors = scratch[14:16]
        (
            rows_buf,
            slope,
            normal_buf,
            grads,
            mixed,
            ffn_rows,
            pre_grad,
            second_sum,
            sums,
            got,
            columns,
            factors,
            small,
        ) = scratch[:13]
        rows = block_ref.shape[0]
        hidden_all = 8 * first_ref.shape[1]
        load_normal, load_mixed, load_slope, load_rows = self.loads(ins, scratch)
        load_normal.wait()
        load_mixed.wait()
        second_sum[...] = jnp.zeros_like(second_sum)
        small[...] = jnp.zeros_like(small)

        def factor_columns(first):
            average = totals_ref[0:1, pl.ds(first, rows)] / hidden_all
            spread = totals_ref[1:2, pl.ds(first, rows)] / hidden_all - average * average
            factors[...] = to_columns(average, lax.rsqrt(spread + epsilon))

        def work(first):
            block = pl.ds(first, rows)
            grads[block, :] = lax.dot_general(
                rows_buf[block, :],
                second_ref[...],
                (((1,), (1,)), ((), ())),
                preferred_element_type=f32,
            )
            second_sum[...] += lax.dot_general(
                mixed[block, :],
                rows_buf[block, :],
                (((0,), (0,)), ((), ())),
                preferred_element_type=f32,
            )

            def step(at):
                piece = pl.ds(pl.multiple_of(first + at, CHUNK), CHUNK)
                normal = normal_buf[piece, :]
                grad = grads[piece, :]
                small[0] += fold(grad * normal)
                small[1] += fold(grad)
                scaled = grad * mid_gain
                grads[piece, :] = scaled
                columns[pl.ds(at, CHUNK), :] = both_columns(
                    jnp.sum(scaled, axis=1, keepdims=True),
                    jnp.sum(scaled * normal, axis=1, keepdims=True),
                )

            in_chunks(rows, CHUNK, step)
            turned = jnp.transpose(columns[...])
            sums[0:1, pl.ds(first, rows)] = turned[0:1]
            sums[1:2, pl.ds(first, rows)] = turned[64:65]

        self.parts[GATHER].finish(
            here, ins[:1], scratch[:1], self.held(scratch, GATHER), work
        )
        held = self.held(scratch, "sums")
        self.parts["sums"].start(here, (sums,), None, held)
        second_grad[...] = second_sum[...].astype(bf16).reshape(second_grad.shape)
        load_slope.wait()
        self.moment(MIDWAY)
        self.parts[SECOND].start(here, (second_grad,), None, self.held(scratch, SECOND))
        self.parts["sums"].finish(here, (sums,), (got,), held)

        def rows_of(first):
            factor_columns(first)
            columns[...] = to_columns(
                got[0:1, pl.ds(first, rows)] / hidden_all,
                got[1:2, pl.ds(first, rows)] / hidden_all,
            )

            def step(at):
                piece = pl.ds(pl.multiple_of(first + at, CHUNK), CHUNK)
                pair = columns[pl.ds(at, CHUNK), :]
                factor = factors[pl.ds(at, CHUNK), :][:, 64:65]
                active_grad = factor * (
                    grads[piece, :] - pair[:, 0:1] - normal_buf[piece, :] * pair[:, 64:65]
                )
                rounded = (active_grad * slope[piece, :]).astype(bf16)
                pre_grad[piece, :] = rounded
                small[2] += fold(rounded.astype(f32))

            in_chunks(rows, CHUNK, step)
            return pre_grad[pl.ds(first, rows), :]

        def idle():
            load_rows.wait()
            whole = lax.dot_general(
                ffn_rows[...],
                pre_grad[...],
                (((0,), (0,)), ((), ())),
                preferred_element_type=f32,
            ).astype(bf16)
            part = first_grad.shape[2]
            for i in range(4):
                first_grad[i] = whole[:, i * part : (i + 1) * part]
            self.moment("closing")

        self.parts[SCATTER].finish(
            here,
            None,
            (out_ref,),
            self.held(scratch, SCATTER),
            rows_of,
            lambda: first_ref[...],
            idle=idle,
        )
        gradient_ref, normal_1, factor_1, gain_1, normal_2, factor_2, gain_2 = ins[9:16]
        vectors[...] = jnp.zeros_like(vectors)
        layer = slice(self.layer, self.layer + 1)

        def pull(at):
            piece = pl.ds(at, NARROW)
            grad, gradient = out_ref[piece, :], gradient_ref[piece, :].astype(f32)
            normal = normal_1[piece, :]
            vectors[3] += fold(grad * normal)
            vectors[4] += fold(grad)
            vectors[5] += fold(gradient)
            middle = gradient + norm_pull(
                grad, normal, factor_1[piece, 0:1], gain_1[layer, :]
            )
            out_ref[piece, :] = middle
            normal = normal_2[piece, :]
            vectors[1] += fold(middle * normal)
            vectors[2] += fold(middle)
            branch = norm_pull(middle, normal, factor_2[piece, 0:1], gain_2[layer, :])
            vectors[0] += fold(branch)
            branch_ref[piece, :] = branch.astype(bf16)

        in_chunks(rows, NARROW, pull)
        vector_ref[...] = jnp.zeros_like(vector_ref)
        for i in range(6):
            vector_ref[i : i + 1, :] = jnp.sum(vectors[i], axis=0, keepdims=True)
        held = self.held(scratch, SECOND)
        self.parts[SECOND].finish(here, (second_grad,), (second_quarter,), held)
        for i in range(3):
            small_ref[i : i + 1, :] = jnp.sum(small[i], axis=0, keepdims=True)


class WeightGather(Task):
    def __init__(self, weights, layer, axis, when="start"):
        self.layer, self.axis, self.when = layer, axis, when
        self.arrays, self.spaces = (weights,), (pltpu.HBM,)
        self.outs = (jax.ShapeDtypeStruct(weights.shape[1:], weights.dtype),)
        self.out_spaces = (pltpu.HBM,)
        self.scratch = (dma_sems(4), dma_sems(3))
        self.reach = BY_Z

    def copies(self, here, ins, outs, scratch):
        part = outs[0].shape[self.axis] // 4

        def cut(ref, at):
            piece = pl.ds(pl.multiple_of(at * part, part), part)
            return ref.at[piece, :] if self.axis == 0 else ref.at[:, piece]

        source = cut(ins[0].at[self.layer], 2 * here.y + here.core)
        target = cut(outs[0], here.z)
        keep = pltpu.make_async_copy(source, target, scratch[0].at[3])
        return keep, [
            remote(source, target, scratch[0].at[i], scratch[1].at[i], here.peer(*way))
            for i, way in enumerate(BY_Z)
        ]

    def begin(self, here, ins, outs, scratch):
        keep, copies = self.copies(here, ins, outs, scratch)
        for each in copies:
            each.start()
        keep.start()

    def start(self, *held):
        self.at_moment("start", *held)

    def at_moment(self, name, *held):
        if name == self.when:
            self.begin(*held)

    def finish(self, here, ins, outs, scratch):
        keep, copies = self.copies(here, ins, outs, scratch)
        for each in copies:
            each.wait()
        keep.wait()


class ThenRows(Parts):
    def __init__(self, first, when):
        self.when = when
        shape = first.outs[0]
        self.arrays, self.spaces = first.arrays, first.spaces
        rows = RowsGather(shape)
        self.outs, self.out_spaces = rows.outs, rows.out_spaces
        self.scratch = (pltpu.VMEM(shape.shape, shape.dtype),)
        self.use(dict(first=first, rows=rows))

    def start(self, here, ins, outs, scratch):
        self.parts["first"].start(here, ins, None, self.held(scratch, "first"))

    def at_moment(self, name, here, ins, outs, scratch):
        if name == self.when:
            self.parts["first"].finish(here, ins, scratch[:1], self.held(scratch, "first"))
            self.parts["rows"].begin(here, scratch[:1], outs, self.held(scratch, "rows"))

    def finish(self, here, ins, outs, scratch):
        self.at_moment("end", here, ins, outs, scratch)
        self.parts["rows"].finish(here, scratch[:1], outs, self.held(scratch, "rows"))


BLOCK = 256
SPAN = 512


def head_masks(head_width, width):
    lane = lax.broadcasted_iota(jnp.int32, (1, width), 1)
    lower = (lane < head_width).astype(bf16)
    return lower, (1 - lower).astype(bf16)


def by_head(values, head_width):
    lower, upper = head_masks(head_width, values.shape[1])
    return jnp.concatenate([values * lower, values * upper], axis=0)


def from_heads(pair, head_width):
    rows = pair.shape[0] // 2
    lane = lax.broadcasted_iota(jnp.int32, (rows, pair.shape[1]), 1)
    return jnp.where(lane < head_width, pair[:rows], pair[rows:])


def tile_facts(doc_ref, first, key_first, keys):
    docs = doc_ref[:, pl.ds(first, BLOCK)]
    docs = jnp.concatenate([docs, docs], axis=1)
    key_docs = doc_ref[:, pl.ds(pl.multiple_of(key_first, keys), keys)]
    key_docs = jnp.transpose(jnp.broadcast_to(key_docs, (128, keys)))[:, 0:1]
    place = lax.broadcasted_iota(jnp.int32, (keys, 2 * BLOCK), 1)
    place = jnp.where(place >= BLOCK, place - BLOCK, place) + (first - key_first)
    allowed = (docs == key_docs) & (place >= lax.broadcasted_iota(jnp.int32, place.shape, 0))
    return docs, allowed


def attend_block(
    head_width, first, q_ref, k_ref, v_cols, doc_ref, o_ref, l_ref, s_buf, acc, top, total
):
    block = first // BLOCK
    last = first // SPAN
    pair = by_head(q_ref[pl.ds(first, BLOCK), :], head_width)

    def scores(at):
        keys = k_ref[pl.ds(pl.multiple_of(at * SPAN, SPAN), SPAN), :]
        return lax.dot_general(keys, pair, (((1,), (1,)), ((), ())), preferred_element_type=f32)

    top[...] = jnp.full_like(top, masked)

    def first_pass(at, carry):
        s = scores(at)
        s_buf[at] = s
        peak = s[:8]
        for row in range(8, SPAN, 8):
            peak = jnp.maximum(peak, s[row : row + 8])
        top[...] = jnp.maximum(top[...], peak)
        return carry

    lax.fori_loop(0, last, first_pass, 0)
    docs, allowed = tile_facts(doc_ref, first, last * SPAN, SPAN)
    s = jnp.where(allowed, scores(last), masked)
    shift = jnp.where(docs == 0, 0.0, masked)
    peak = jnp.maximum(
        jnp.max(top[...], axis=0, keepdims=True) + shift, jnp.max(s, axis=0, keepdims=True)
    )

    def weigh(at, p):
        values = v_cols[:, pl.ds(pl.multiple_of(at * SPAN, SPAN), SPAN)]
        return jnp.dot(values, p.astype(bf16), preferred_element_type=f32)

    p = jnp.exp(s - peak)
    total[...] = fold(p)
    acc[...] = weigh(last, p)
    base = peak - shift

    def second_pass(at, carry):
        p = jnp.exp(s_buf[at] - base)
        total[...] += fold(p)
        acc[...] += weigh(at, p)
        return carry

    lax.fori_loop(0, last, second_pass, 0)
    sums = jnp.sum(total[...], axis=0, keepdims=True)
    out = from_heads(jnp.transpose(acc[...] / sums), head_width)
    o_ref[pl.ds(first, BLOCK), :] = out
    l_ref[block] = peak + jnp.log(sums)
    return out


def attend_block_back(
    head_width,
    first,
    do,
    q_ref,
    k_ref,
    k_cols,
    v_ref,
    o_ref,
    l_ref,
    doc_ref,
    acc_k,
    acc_v,
    acc_q,
):
    block = first // BLOCK
    rows = pl.ds(first, BLOCK)
    pair_q = by_head(q_ref[rows, :], head_width)
    pair_do = by_head(do, head_width)
    out = o_ref[rows, :]
    inner = jnp.sum(
        jnp.concatenate([out, out], axis=0) * pair_do.astype(f32), axis=1, keepdims=True
    )
    inner = jnp.transpose(jnp.broadcast_to(inner, (2 * BLOCK, 128)))[0:1, :]
    logs = l_ref[block]
    docs, allowed = tile_facts(doc_ref, first, first, BLOCK)

    def step(at, base, allowed):
        piece = pl.ds(pl.multiple_of(at * BLOCK, BLOCK), BLOCK)
        s = lax.dot_general(
            k_ref[piece, :], pair_q, (((1,), (1,)), ((), ())), preferred_element_type=f32
        )
        dp = lax.dot_general(
            v_ref[piece, :], pair_do, (((1,), (1,)), ((), ())), preferred_element_type=f32
        )
        p = jnp.exp(s - base)
        if allowed is not None:
            p = jnp.where(allowed, p, 0.0)
        ds = (p * (dp - inner)).astype(bf16)
        acc_v[piece, :] += jnp.dot(p.astype(bf16), pair_do, preferred_element_type=f32)
        acc_k[piece, :] += jnp.dot(ds, pair_q, preferred_element_type=f32)
        return jnp.dot(k_cols[:, piece], ds, preferred_element_type=f32)

    acc_q[...] = step(block, logs, allowed)
    base = jnp.where(docs == 0, logs, -masked)

    def earlier(at, carry):
        acc_q[...] += step(at, base, None)
        return carry

    lax.fori_loop(0, block, earlier, 0)
    grad = from_heads(jnp.transpose(acc_q[...]), head_width)
    return (grad * head_width**-0.5).astype(bf16)


def turned(values):
    return jnp.transpose(values.astype(f32)).astype(bf16)


class AttnForward(Parts):
    def __init__(
        self, block, docs, scale, heads, biases, wide, layer, norms, residual=None, late=None
    ):
        rows, width = block.shape
        self.head_width, self.layer, self.late = wide, layer, late
        here = 2 * wide
        self.arrays = (block, docs, scale, biases, *heads)
        far = pltpu.HBM if late else pltpu.VMEM
        self.spaces = (far, far, pltpu.VMEM) + (far,) * (1 + len(heads))
        column = jax.ShapeDtypeStruct((8 * rows, here), bf16)
        self.outs = (
            jax.ShapeDtypeStruct((rows, width), f32),
            jax.ShapeDtypeStruct((8 * rows, width), bf16),
            column,
            column,
            column,
            column,
            jax.ShapeDtypeStruct((8 * rows, here), f32),
            jax.ShapeDtypeStruct((8 * rows // BLOCK, 1, 2 * BLOCK), f32),
        )
        wide_shape = jax.ShapeDtypeStruct((rows, 128), f32)
        self.outs += (self.outs[0], wide_shape, self.outs[0], wide_shape)
        self.outs += (jax.ShapeDtypeStruct((rows, width), bf16),)
        self.out_spaces = (pltpu.VMEM, pltpu.HBM) + (pltpu.VMEM,) * 11
        self.arrays += tuple(norms)
        self.spaces += (pltpu.VMEM,) * 5
        self.scratch = (
            pltpu.VMEM((8 * rows, width), bf16),
            pltpu.VMEM((here, 8 * rows), bf16),
            pltpu.VMEM((8 * rows // SPAN, SPAN, 2 * BLOCK), f32),
            pltpu.VMEM((here, 2 * BLOCK), f32),
            pltpu.VMEM((8, 2 * BLOCK), f32),
            pltpu.VMEM((8, 2 * BLOCK), f32),
            dma_sems(1),
        )
        parts = dict(gather=PlaneGather(block), scatter=PlaneScatter(rows, width, 0))
        if late:
            parts.update(heads=HeadGather(*heads, layer), biases=LineGather(biases))
            half = jax.ShapeDtypeStruct((rows // 2, width), block.dtype)
            for i in range(2):
                parts["tokens", i] = PlaneMove(half, when="push")
            parts["docs"] = PlaneMove(docs, when="push")
            self.outs += parts["heads"].outs + parts["biases"].outs
            self.outs += (jax.ShapeDtypeStruct(docs.shape, f32),)
            self.outs += (jax.ShapeDtypeStruct(block.shape, f32),) * 2
            self.outs += (wide_shape,)
            self.out_spaces += (pltpu.VMEM,) * 6
            self.scratch += (pltpu.VMEM(block.shape, bf16), pltpu.VMEM(block.shape, bf16))
            self.scratch += (pltpu.VMEM(docs.shape, docs.dtype),)
            self.arrays += tuple(late)
            self.spaces += (pltpu.VMEM,) * 2
        else:
            self.arrays += (residual,)
            self.spaces += (pltpu.VMEM,)
        self.base = 3 + 1 + len(heads)
        self.use(parts)

    def start(self, here, ins, outs, scratch):
        if self.late:
            for part, held in self.moves(here, ins, scratch):
                part.start(*held)
        else:
            self.parts[GATHER].start(here, ins[:1], scratch[:1], self.held(scratch, GATHER))

    def moves(self, here, ins, scratch):
        half = ins[0].shape[0] // 2
        triples = []
        for i in range(2):
            piece = pl.ds(i * half, half)
            triples.append((("tokens", i), ins[0].at[piece], scratch[7].at[piece]))
        triples.append(("docs", ins[1], scratch[9]))
        return [
            (self.parts[name], (here, (source,), (target,), self.held(scratch, name)))
            for name, source, target in triples
        ]

    def first_norm(self, here, ins, outs, scratch):
        tokens, block = scratch[7:9]
        residual_ref, normal_ref, factor_ref = outs[16:19]
        moves = self.moves(here, ins, scratch)
        for part, held in moves:
            part.at_moment("push", *held)
        self.parts["biases"].start(here, ins[3:4], outs[14:15], self.held(scratch, "biases"))
        self.parts["heads"].start(here, ins[4:6], outs[13:14], self.held(scratch, "heads"))
        for part, held in moves:
            part.finish(*held)
        outs[15][...] = scratch[9][...].astype(f32)
        gain, bias = (ref[self.layer : self.layer + 1, :] for ref in ins[self.base + 5 :])
        values = tokens[...].astype(f32)
        residual_ref[...] = values
        normal, factor = normalize(values)
        factor_ref[...] = wide_column(factor)
        normal_ref[...] = normal
        block[...] = (normal * gain + bias).astype(bf16)
        return block

    def finish(self, here, ins, outs, scratch):
        block_ref, doc_ref, scale_ref = ins[:3]
        scale_row = scale_of(here, scale_ref, self.layer, self.head_width)
        heads_ref, bias_ref = outs[13:15] if self.late else (ins[4], ins[3])
        if self.late:
            doc_ref = outs[15]
            block_ref = self.first_norm(here, ins, outs, scratch)
            self.parts[GATHER].start(
                here, (block_ref,), scratch[:1], self.held(scratch, GATHER)
            )
        out_ref, rows_out, q_ref, k_ref, v_ref, z_ref, o_ref, l_ref = outs[:8]
        rows_buf, v_cols, s_buf, acc, top, total, save = scratch[:7]
        rows, model_width = block_ref.shape
        wide = self.head_width
        width = 2 * wide

        def bias_row(at):
            pair = [
                bias_ref[2 * here.core + i, self.layer : self.layer + 1, at : at + width]
                for i in range(2)
            ]
            lane = lax.broadcasted_iota(jnp.int32, (1, width), 1)
            return jnp.where(lane < wide, pair[0], pair[1])

        def work(first):
            block = pl.ds(first, rows)
            projected = lax.dot_general(
                rows_buf[block, :],
                heads_ref[0:3].reshape(3 * width, model_width),
                (((1,), (1,)), ((), ())),
                preferred_element_type=f32,
            )
            q = (projected[:, :width] + bias_row(0)).astype(bf16).astype(f32)
            q_ref[block, :] = (q * wide**-0.5).astype(bf16)
            k_ref[block, :] = projected[:, width : 2 * width].astype(bf16)
            v = (projected[:, 2 * width :] + bias_row(width)).astype(bf16)
            v_ref[block, :] = v
            v_cols[:, block] = turned(v)

        self.parts[GATHER].finish(
            here,
            (block_ref,),
            scratch[:1],
            self.held(scratch, GATHER),
            None if self.late else work,
        )
        keep_rows = pltpu.make_async_copy(rows_buf, rows_out, save.at[0])
        keep_rows.start()
        if self.late:
            self.parts["heads"].arrive(0, outs[13:14], self.held(scratch, "heads"))
            self.parts["biases"].finish(here, ins[3:4], outs[14:15], self.held(scratch, "biases"))
            in_chunks(8 * rows, rows, work)
            self.parts["heads"].arrive(1, outs[13:14], self.held(scratch, "heads"))
        self.moment(MIDWAY)

        def rows_of(first):
            out = attend_block(
                wide, first, q_ref, k_ref, v_cols, doc_ref, o_ref, l_ref, s_buf, acc, top, total
            )
            z = (out * scale_row).astype(bf16)
            z_ref[pl.ds(first, rows), :] = z
            return z

        self.parts[SCATTER].finish(
            here,
            None,
            (out_ref,),
            self.held(scratch, SCATTER),
            rows_of,
            lambda: heads_ref[3].reshape(width, model_width),
            idle=lambda: self.moment("closing"),
        )
        residual_ref = outs[16] if self.late else ins[self.base + 5]
        layer = slice(self.layer, self.layer + 1)
        shift, gain_1, bias_1, gain_2, bias_2 = (
            ref[layer, :] for ref in ins[self.base : self.base + 5]
        )
        normal_1, factor_1, normal_2, factor_2, next_ref = outs[8:13]

        def settle(at):
            piece = pl.ds(at, NARROW)
            normal, factor = normalize(out_ref[piece, :] + shift)
            normal_1[piece, :] = normal
            factor_1[piece, :] = wide_column(factor)
            middle = residual_ref[piece, :] + (normal * gain_1 + bias_1)
            out_ref[piece, :] = middle
            normal, factor = normalize(middle)
            normal_2[piece, :] = normal
            factor_2[piece, :] = wide_column(factor)
            next_ref[piece, :] = (normal * gain_2 + bias_2).astype(bf16)

        in_chunks(rows, NARROW, settle)
        keep_rows.wait()
        if self.late:
            held = self.held(scratch, "heads")
            self.parts["heads"].sent(here, ins[4:6], outs[13:14], held)


class AttnBackward(Parts):
    def __init__(
        self, block, docs, scale, heads, q, k, v, z, o, logs, attn_rows, norm, hidden, layer, end
    ):
        self.end = end
        self.layer = layer
        rows, width = block.shape
        kinds, _, wide, _ = heads.shape
        self.head_width = wide
        here = 2 * wide
        self.arrays = (block, docs, scale, heads, q, k, v, z, o, logs, attn_rows)
        self.spaces = (pltpu.VMEM,) * 10 + (pltpu.HBM,)
        self.arrays += (*norm, hidden)
        self.spaces += (pltpu.VMEM,) * 5
        self.shipped = kinds if end else kinds // 2
        leaving = jax.ShapeDtypeStruct((self.shipped, *heads.shape[1:]), bf16)
        staying = jax.ShapeDtypeStruct((kinds - self.shipped, *heads.shape[1:]), bf16)
        heads_sum = HeadScatter(leaving)
        half_rows = jax.ShapeDtypeStruct((rows // 2, width), bf16)
        vector, sums = jax.ShapeDtypeStruct((8, width), f32), jax.ShapeDtypeStruct((4, 4, here), f32)
        quarter = heads_sum.outs[0]
        if end:
            tail = {("move", i): PlaneMove(half_rows, True, "push") for i in range(2)}
            tail.update(
                vectors=PlaneSum(vector),
                line=LineSum(vector),
                rows=RowsGather(quarter),
                hidden=ThenRows(LineScatter(sums), "push"),
            )
            self.outs = (jax.ShapeDtypeStruct((rows, width), bf16), vector) + tail["rows"].outs + tail["hidden"].outs
            self.out_spaces = (pltpu.HBM, pltpu.VMEM, pltpu.HBM, pltpu.HBM)
        else:
            self.outs = (jax.ShapeDtypeStruct((rows, width), f32), quarter, sums)
            self.outs += (jax.ShapeDtypeStruct((rows, width), bf16), vector, staying)
            self.out_spaces = (pltpu.VMEM,) * 6
        self.scratch = (
            pltpu.VMEM((8 * rows, width), bf16),
            pltpu.VMEM((8 * rows, width), bf16),
            pltpu.VMEM((here, 8 * rows), bf16),
            pltpu.VMEM((8 * rows, here), f32),
            pltpu.VMEM((8 * rows, here), f32),
            pltpu.VMEM((here, 2 * BLOCK), f32),
            pltpu.VMEM((8 * rows, 3 * here), bf16),
            pltpu.VMEM((here, width), f32),
            pltpu.VMEM((3, 8, here), f32),
            dma_sems(1),
            pltpu.VMEM((2, 8, width), f32),
            pltpu.VMEM(heads.shape, bf16),
        )
        if end:
            self.scratch += (
                pltpu.VMEM((rows, width), f32),
                pltpu.VMEM(quarter.shape, bf16),
                pltpu.VMEM(sums.shape, f32),
                pltpu.VMEM((rows, width), bf16),
                pltpu.VMEM(vector.shape, f32),
                pltpu.VMEM(vector.shape, f32),
            )
        parts = dict(gather=OrderedGather(block), scatter=PlaneScatter(rows, width, 0))
        parts.update(tail if end else {})
        parts["heads"] = heads_sum
        self.use(parts)

    def load(self, ins, scratch):
        return pltpu.make_async_copy(ins[10], scratch[1], scratch[9].at[0])

    def start(self, here, ins, outs, scratch):
        self.parts[GATHER].start(here, ins[:1], scratch[:1], self.held(scratch, GATHER))
        self.load(ins, scratch).start()

    def finish(self, here, ins, outs, scratch):
        block_ref, doc_ref, scale_ref, heads_ref, q_ref, k_ref, v_ref, z_ref, o_ref, l_ref = ins[:10]
        results = scratch[12:17] if self.end else outs
        out_ref, quarter_ref, hidden_ref, rounded_ref, vector_ref = results[:5]
        middle_ref, normal_ref, factor_ref, gain_ref, sums_ref = ins[11:16]
        (
            rows_buf,
            attn_rows,
            k_cols,
            acc_k,
            acc_v,
            acc_q,
            proj,
            out_sum,
            small,
        ) = scratch[:9]
        vectors = scratch[10]
        heads_grad = scratch[11]
        leaving = (heads_grad.at[pl.ds(0, self.shipped)],)
        scale_row = scale_of(here, scale_ref, self.layer, self.head_width)
        rows, model_width = block_ref.shape
        wide = self.head_width
        width = 2 * wide
        acc_k[...] = jnp.zeros_like(acc_k)
        acc_v[...] = jnp.zeros_like(acc_v)
        out_sum[...] = jnp.zeros_like(out_sum)
        small[...] = jnp.zeros_like(small)
        k_cols[...] = turned(k_ref[...])

        def work(first):
            block = pl.ds(first, rows)
            scaled_grad = lax.dot_general(
                rows_buf[block, :],
                heads_ref[3].reshape(width, model_width),
                (((1,), (1,)), ((), ())),
                preferred_element_type=f32,
            )
            out_sum[...] += lax.dot_general(
                z_ref[block, :],
                rows_buf[block, :],
                (((0,), (0,)), ((), ())),
                preferred_element_type=f32,
            )
            small[0] += fold(o_ref[block, :] * scaled_grad)
            grad = attend_block_back(
                wide,
                first,
                (scaled_grad * scale_row).astype(bf16),
                q_ref,
                k_ref,
                k_cols,
                v_ref,
                o_ref,
                l_ref,
                doc_ref,
                acc_k,
                acc_v,
                acc_q,
            )
            proj[block, 0:width] = grad
            small[1] += fold(grad.astype(f32))

        self.parts[GATHER].finish(
            here,
            ins[:1],
            scratch[:1],
            self.held(scratch, GATHER),
            work,
            self.moment,
        )

        def settle(first):
            block = pl.ds(first, rows)
            proj[block, width : 2 * width] = acc_k[block, :].astype(bf16)
            value_grad = acc_v[block, :].astype(bf16)
            proj[block, 2 * width : 3 * width] = value_grad
            small[2] += fold(value_grad.astype(f32))

        in_chunks(8 * rows, rows, settle)
        self.moment(MIDWAY)

        def early():
            self.load(ins, scratch).wait()
            qkv_grad = lax.dot_general(
                proj[...],
                attn_rows[...],
                (((0,), (0,)), ((), ())),
                preferred_element_type=f32,
            )
            heads_grad[0:3] = qkv_grad.astype(bf16).reshape(3, 2, wide, model_width)
            heads_grad[3] = out_sum[...].astype(bf16).reshape(2, wide, model_width)
            self.parts["heads"].start(here, leaving, None, self.held(scratch, "heads"))
            if not self.end:
                outs[5][...] = heads_grad[self.shipped :]

        early()
        self.parts[SCATTER].finish(
            here,
            None,
            (out_ref,),
            self.held(scratch, SCATTER),
            lambda first: proj[pl.ds(first, rows), :],
            lambda: heads_ref[0:3].reshape(3 * width, model_width),
            idle=lambda: self.moment("closing"),
        )
        vectors[...] = jnp.zeros_like(vectors)
        layer = slice(self.layer, self.layer + 1)

        def pull(at):
            piece = pl.ds(at, NARROW)
            grad, normal = out_ref[piece, :], normal_ref[piece, :]
            vectors[0] += fold(grad * normal)
            vectors[1] += fold(grad)
            gradient = middle_ref[piece, :] + norm_pull(
                grad, normal, factor_ref[piece, 0:1], gain_ref[layer, :]
            )
            out_ref[piece, :] = gradient
            rounded_ref[piece, :] = gradient.astype(bf16)

        home = []
        if self.end:
            for i in range(2):
                piece = pl.ds(i * (rows // 2), rows // 2)
                held = self.held(scratch, ("move", i))
                refs = (rounded_ref.at[piece],), (outs[0].at[piece],)
                home.append((self.parts["move", i], (here, *refs, held)))
                pull(i * NARROW)
                home[i][0].start(*home[i][1])
        else:
            in_chunks(rows, NARROW, pull)
        scale_cols, query_cols, value_cols = (
            jnp.sum(small[i], axis=0, keepdims=True) for i in range(3)
        )
        vector_ref[...] = jnp.zeros_like(vector_ref)
        for i in range(2):
            vector_ref[i : i + 1, :] = jnp.sum(vectors[i], axis=0, keepdims=True)
        lane = lax.broadcasted_iota(jnp.int32, (1, width), 1)
        place = lax.broadcasted_iota(jnp.int32, (1, model_width), 1)
        head_sums = jnp.zeros((1, model_width), f32)
        for i in range(2):
            head = ((2 * here.core + i) * 2 + here.x) * 2 + here.y
            own = (lane >= i * wide) & (lane < (i + 1) * wide)
            total = jnp.sum(jnp.where(own, scale_cols, 0.0), axis=1, keepdims=True)
            head_sums = head_sums + jnp.where(place == head, total, 0.0)
        vector_ref[2:3, :] = head_sums
        pairs = [
            jnp.concatenate(
                [cols[:, i * wide : (i + 1) * wide] for cols in (query_cols, value_cols)], axis=1
            )
            for i in range(2)
        ]
        for shard in range(4):
            for row, source in enumerate((2, 0, 1)):
                cut = sums_ref[source : source + 1, shard * width : (shard + 1) * width]
                hidden_ref[shard, row : row + 1, :] = cut
            own = here.core == shard // 2
            hidden_ref[shard, 3:4, :] = jnp.where(own, pairs[shard % 2], 0.0)
        self.moment("tail")
        held = (here, leaving, (quarter_ref,), self.held(scratch, "heads"))
        if not self.end:
            self.parts["heads"].finish(*held)
            return
        sum_held = (here, (vector_ref,), (scratch[17],), self.held(scratch, "vectors"))
        line_held = (here, (scratch[17],), outs[1:2], self.held(scratch, "line"))
        rows_held = (here, (quarter_ref,), outs[2:3], self.held(scratch, "rows"))
        hidden_held = (here, (hidden_ref,), outs[3:4], self.held(scratch, "hidden"))
        self.parts["vectors"].start(*sum_held)
        self.parts["hidden"].start(*hidden_held)
        self.parts["heads"].finish(*held)
        self.parts["rows"].begin(*rows_held)
        self.parts["vectors"].finish(*sum_held)
        self.parts["line"].start(*line_held)
        for part, refs in home:
            part.at_moment("push", *refs)
        self.parts["hidden"].at_moment("push", *hidden_held)
        self.parts["line"].finish(*line_held)
        self.parts["rows"].finish(*rows_held)
        self.parts["hidden"].finish(*hidden_held)
        for part, refs in home:
            part.finish(*refs)


def finish_kernel(layers, *refs):
    count = 2 + 6 * layers
    far, refs, sems = refs[:count], refs[count:-1], refs[-1]
    refs, near = refs[: len(refs) - count], refs[len(refs) - count :]
    loads = [pltpu.make_async_copy(a, b, sems.at[i]) for i, (a, b) in enumerate(zip(far, near))]
    order = [0, 1] + [2 + g * layers + i for i in range(layers - 1, -1, -1) for g in range(6)]
    for index in order:
        loads[index].start()
    refs = (*near, *refs)
    (layer_ref, grad_ref), refs = refs[:2], refs[2:]
    groups = []
    for _ in range(6):
        groups.append(refs[:layers])
        refs = refs[layers:]
    firsts, seconds, heads_all, hiddens, earlies, lates = groups
    (
        layer_out,
        grad_out,
        attn_gain,
        attn_bias,
        qkv_out,
        bias_out,
        scale_out,
        out_out,
        out_shift,
        post_gain,
        post_bias,
        ffn_gain,
        ffn_bias,
        first_out,
        first_shift,
        mid_gain,
        mid_bias,
        second_out,
        second_shift,
    ) = refs
    loads[0].wait()
    layer_out[...] = layer_ref[...]
    loads[1].wait()
    grad_out[...] = grad_ref[...].astype(f32)
    for layer in range(layers - 1, -1, -1):
        for group in range(6):
            loads[2 + group * layers + layer].wait()
        first, second, heads, hidden = (g[layer] for g in (firsts, seconds, heads_all, hiddens))
        part = first.shape[2]
        wide, half = heads.shape[2:]
        row = slice(layer, layer + 1)
        for i, ref in enumerate((out_shift, post_gain, post_bias, ffn_gain, ffn_bias, second_shift)):
            ref[row, :] = earlies[layer][i : i + 1, :]
        for i, ref in enumerate((attn_gain, attn_bias)):
            ref[row, :] = lates[layer][i : i + 1, :]
        scale_out[row, :] = lates[layer][2:3, 0 : scale_out.shape[1]]
        for i in range(4):
            cut = slice(i * part, (i + 1) * part)
            first_out[layer, :, cut] = first[i].astype(f32)
            second_out[layer, cut, :] = second[i].astype(f32)
            for at, ref in enumerate((first_shift, mid_gain, mid_bias)):
                ref[row, cut] = hidden[i, at : at + 1, :]
        biases = [hidden[2 * y, 3:4, :] + hidden[2 * y + 1, 3:4, :] for y in range(2)]
        for i in range(2):
            bias_out[layer, i : i + 1, :] = jnp.concatenate(
                [each[:, i * wide : (i + 1) * wide] for each in biases], axis=1
            )
        for core in range(2):
            here = slice(core * half, (core + 1) * half)
            for kind in range(3):
                pair = jnp.concatenate([heads[core, kind], heads[2 + core, kind]], axis=0)
                qkv_out[layer, kind, here, :] = jnp.transpose(pair.astype(f32))
            for y in range(2):
                out_out[layer, y * wide : (y + 1) * wide, here] = heads[2 * y + core, 3].astype(f32)


def finish_all(layer_output, gradient, heads_count, *groups):
    firsts, seconds, heads = groups[:3]
    layers = len(firsts)
    rows, width = layer_output.shape
    part = firsts[0].shape[2]
    wide = heads[0].shape[2]
    vector = jax.ShapeDtypeStruct((layers, width), f32)
    hidden = jax.ShapeDtypeStruct((layers, 4 * part), f32)
    outs = (
        jax.ShapeDtypeStruct((rows, width), bf16),
        jax.ShapeDtypeStruct((rows, width), f32),
        vector,
        vector,
        jax.ShapeDtypeStruct((layers, 3, width, 2 * wide), f32),
        jax.ShapeDtypeStruct((layers, 2, 2 * wide), f32),
        jax.ShapeDtypeStruct((layers, heads_count), f32),
        jax.ShapeDtypeStruct((layers, 2 * wide, width), f32),
        vector,
        vector,
        vector,
        vector,
        vector,
        jax.ShapeDtypeStruct((layers, width, 4 * part), f32),
        hidden,
        hidden,
        hidden,
        jax.ShapeDtypeStruct((layers, 4 * part, width), f32),
        vector,
    )
    arrays = [layer_output, gradient] + [each for group in groups for each in group]
    results = list(
        pl.pallas_call(
            partial(finish_kernel, layers),
            out_shape=outs,
            in_specs=[pl.BlockSpec(memory_space=pltpu.HBM)] * len(arrays),
            out_specs=[pl.BlockSpec(memory_space=pltpu.VMEM)] * len(outs),
            scratch_shapes=[
                *[pltpu.VMEM(each.shape, each.dtype) for each in arrays],
                dma_sems(len(arrays)),
            ],
            compiler_params=vmem_params(None, 60),
        )(*arrays)
    )
    results[4] = jnp.transpose(results[4], (0, 2, 1, 3))
    return tuple(results)


def plane_device(
    tokens,
    segment_ids,
    cotangent,
    ln_attn_gain,
    ln_attn_bias,
    qkv_weight,
    qv_bias,
    head_scale,
    out_weight,
    out_bias,
    ln_post_gain,
    ln_post_bias,
    ln_ffn_gain,
    ln_ffn_bias,
    fc1_weight,
    fc1_bias,
    mid_gain,
    mid_bias,
    fc2_weight,
    fc2_bias,
):
    layers = qkv_weight.shape[0]
    model_width = tokens.shape[1]
    heads_all = head_scale.shape[1]
    head_width = model_width // heads_all
    hidden_here = fc1_weight.shape[2]
    hidden_all = hidden_here * 8
    quarter = hidden_here // 4
    half_width = model_width // 2
    x, y, core = lax.axis_index("x"), lax.axis_index("y"), lax.axis_index("core")
    quarter_at = 2 * y + core
    width = 2 * head_width
    ids = iter(range(1, 64))

    docs = segment_ids[None, :]

    def cut(values, at, size, axis):
        return lax.dynamic_slice_in_dim(values, at * size, size, axis)

    qkv_rows = jnp.transpose(qkv_weight, (0, 2, 3, 1))
    bias_heads = cut(qv_bias, y, head_width, 2)
    small = jnp.concatenate(
        [
            jnp.concatenate([bias_heads, bias_heads], axis=2).reshape(layers, 2 * width),
            cut(fc1_bias, quarter_at, quarter, 1),
            cut(mid_gain, quarter_at, quarter, 1),
            cut(mid_bias, quarter_at, quarter, 1),
        ],
        axis=1,
    )
    heads_here = [None] * layers
    norms = (out_bias, ln_post_gain, ln_post_bias, ln_ffn_gain, ln_ffn_bias)
    attn_norm = (ln_attn_gain, ln_attn_bias)

    stored = []
    for layer in range(layers):
        first, last = layer == 0, layer + 1 == layers
        if first:
            task = AttnForward(
                tokens,
                docs,
                head_scale,
                (qkv_rows, out_weight),
                small,
                head_width,
                layer,
                norms,
                late=attn_norm,
            )
            sides = [WeightGather(fc1_weight, layer, 1, MIDWAY)]
        else:
            task = AttnForward(
                block,
                docs,
                head_scale,
                (heads_here[layer],),
                small,
                head_width,
                layer,
                norms,
                residual=residual,
            )
            sides = [WeightGather(fc1_weight, layer, 1), WeightGather(fc2_weight, layer, 0)]
        (got, (first_here,), *rest) = run_tasks(ids, task, *sides)
        middle, attn_rows, q, k, v, scaled, attended, logs = got[:8]
        post_normal, post_factor, ffn_normal, ffn_factor, block = got[8:13]
        if first:
            heads_here[0], small, docs, _, attn_normal, attn_factor = got[13:]
        here = (attn_normal, attn_factor)
        sides = [PlaneMove(cotangent)]
        if not last:
            sides = [HeadGather(qkv_rows, out_weight, layer + 1, MIDWAY if first else "start")]
        (got, (side,)) = run_tasks(
            ids,
            FfnForward(
                block,
                first_here,
                fc2_weight if first else rest[0][0],
                small,
                middle,
                fc2_bias,
                None if last else attn_norm,
                layer,
                first,
            ),
            *sides,
        )
        residual, ffn_rows, slope, hidden_normal, mixed, totals, block = got[:7]
        second_here = got[-1] if first else rest[0][0]
        if not last:
            attn_normal, attn_factor = got[7:9]
            heads_here[layer + 1] = side
        stored.append(
            (
                first_here,
                second_here,
                *here,
                attn_rows,
                q,
                k,
                v,
                attended,
                logs,
                scaled,
                post_normal,
                post_factor,
                ffn_normal,
                ffn_factor,
                ffn_rows,
                slope,
                hidden_normal,
                mixed,
                totals,
            )
        )
    gradient = gradient_b = side

    first_done, second_done = [None] * layers, [None] * layers
    heads_done, hidden_done = [None] * layers, [None] * layers
    early_done, late_done = [None] * layers, [None] * layers
    late_vectors = None
    for layer in reversed(range(layers)):
        (
            first_here,
            second_here,
            attn_normal,
            attn_factor,
            attn_rows,
            q,
            k,
            v,
            attended,
            logs,
            scaled,
            post_normal,
            post_factor,
            ffn_normal,
            ffn_factor,
            ffn_rows,
            slope,
            hidden_normal,
            mixed,
            totals,
        ) = stored[layer]
        last = layer + 1 == layers
        if last:
            sides = [PlaneMove(block, back=True)]
        else:
            sides = [HeadScatter(heads_rest), ThenRows(LineScatter(hidden_grad), "closing")]
            sides += [LineSum(early_vectors), StepSum(late_vectors)]
        ((gradient, first_grad, second_grad, hidden_sums, branch_b, early_vectors), *got) = (
            run_tasks(
                ids,
                FfnBackward(
                    gradient_b,
                    first_here,
                    second_here,
                    small,
                    slope,
                    hidden_normal,
                    mixed,
                    ffn_rows,
                    totals,
                    gradient,
                    (
                        ffn_normal,
                        ffn_factor,
                        ln_ffn_gain,
                        post_normal,
                        post_factor,
                        ln_post_gain,
                    ),
                    layer,
                ),
                *sides,
            )
        )
        if last:
            layer_output = got[0][0]
        else:
            heads_rest, hidden_done[layer + 1], early_done[layer + 1], late_vectors = (
                each[0] for each in got
            )
            heads_grad = jnp.concatenate([heads_grad, heads_rest], axis=0)
        sides = [ThenRows(LineScatter(first_grad), "soon"), RowsGather(second_grad, "spare")]
        sides.append(StepThenLine(early_vectors) if layer == 0 else StepSum(early_vectors))
        if not last:
            sides += [LineSum(late_vectors), RowsGather(heads_grad, "spare")]
        (results, *got) = run_tasks(
            ids,
            AttnBackward(
                branch_b,
                docs,
                head_scale,
                heads_here[layer],
                q,
                k,
                v,
                scaled,
                attended,
                logs,
                attn_rows,
                (gradient, attn_normal, attn_factor, ln_attn_gain),
                hidden_sums,
                layer,
                layer == 0,
            ),
            *sides,
        )
        first_done[layer], second_done[layer], early_vectors = got[0][0], got[1][0], got[2][0]
        if not last:
            late_done[layer + 1], heads_done[layer + 1] = got[3][0], got[4][0]
        if layer == 0:
            input_grad, late_done[0], heads_done[0], hidden_done[0] = results
            early_done[0] = early_vectors
        else:
            gradient, heads_grad, hidden_grad, gradient_b, late_vectors, heads_rest = results
    return finish_all(
        layer_output,
        input_grad,
        heads_all,
        first_done,
        second_done,
        heads_done,
        hidden_done,
        early_done,
        late_done,
    )


def split_specs(rows, mp):
    both = tuple(rows) + tuple(mp)
    in_specs = (
        P(both, None),
        P(rows),
        P(both, None),
        P(),
        P(),
        P(None, None, None, mp),
        P(None, None, mp),
        P(),
        P(None, mp, None),
        P(),
        P(),
        P(),
        P(),
        P(),
        P(None, None, mp),
        P(None, mp),
        P(None, mp),
        P(None, mp),
        P(None, mp, None),
        P(),
    )
    out_specs = (
        P(both, None),
        P(both, None),
        P(),
        P(),
        P(None, None, None, mp),
        P(None, None, mp),
        P(),
        P(None, mp, None),
        P(),
        P(),
        P(),
        P(),
        P(),
        P(None, None, mp),
        P(None, mp),
        P(None, mp),
        P(None, mp),
        P(None, mp, None),
        P(),
    )
    return in_specs, out_specs


def solution(mesh):
    if mesh.shape["rows"] == 4 and mesh.shape["mp"] == 8:
        planes = Mesh(mesh.devices.reshape(2, 2, 4, 2), ("y", "core", "z", "x"))
        in_specs, out_specs = split_specs(("y", "core"), ("z", "x"))
        return jax.shard_map(
            plane_device, mesh=planes, in_specs=in_specs, out_specs=out_specs, check_vma=False
        )
    in_specs, out_specs = split_specs(("rows",), ("mp",))
    return jax.shard_map(
        per_device, mesh=mesh, in_specs=in_specs, out_specs=out_specs, check_vma=False
    )
```

```python
from functools import partial

import jax
import jax.numpy as jnp
from jax import lax
from jax.experimental import pallas as pl
from jax.experimental.pallas import tpu as pltpu
from jax.sharding import Mesh
from jax.sharding import PartitionSpec as P

epsilon = 1e-05
masked = -1e30


def partner(shard, axis, stride):
    return lax.ppermute(shard, axis, [(i, i ^ 1 << stride) for i in range(lax.axis_size(axis))])


def norm_local(values, gain_row, bias_row):
    average = jnp.mean(values, axis=-1, keepdims=True)
    centered = values - average
    spread = jnp.mean(centered * centered, axis=-1, keepdims=True)
    factor = lax.rsqrt(spread + epsilon)
    normal = centered * factor
    return (normal * gain_row + bias_row, normal, factor)


def norm_back(grad_out, normal, factor, gain_row):
    scaled = grad_out * gain_row
    inner_sum = jnp.mean(scaled * normal, axis=-1, keepdims=True)
    return factor * (scaled - jnp.mean(scaled, axis=-1, keepdims=True) - normal * inner_sum)


def collect_rows(normed_b):
    return lax.all_gather(normed_b, "mp", axis=0, tiled=True)


def collect_grads(gradient_b):
    return lax.all_gather(gradient_b, "mp", axis=0, tiled=True)


def reduce_branch(operand_b, weight_b, local_rows):

    def partial_term(first_row, count):
        return jnp.dot(operand_b, weight_b, preferred_element_type=jnp.float32)

    return lax.psum_scatter(
        partial_term(jnp.int32(0), local_rows * lax.axis_size("mp")).astype(jnp.bfloat16),
        "mp",
        scatter_dimension=0,
        tiled=True,
    ).astype(jnp.float32)


def reduce_grads(operand_b, weight_b, local_rows):

    def partial_term(first_row, count):
        return jnp.einsum("tc,dc->td", operand_b, weight_b, preferred_element_type=jnp.float32)

    return lax.psum_scatter(
        partial_term(jnp.int32(0), local_rows * lax.axis_size("mp")).astype(jnp.bfloat16),
        "mp",
        scatter_dimension=0,
        tiled=True,
    ).astype(jnp.float32)


def hidden_stats(first_sum, second_sum):
    return lax.psum((first_sum, second_sum), "mp")


def hidden_grad_stats(first_sum, second_sum):
    return lax.psum((first_sum, second_sum), "mp")


def join_cols(mine, other, is_upper):
    lower_part = jnp.where(is_upper, other, mine)
    upper_part = jnp.where(is_upper, mine, other)
    return jnp.concatenate([lower_part, upper_part], axis=-1)


def join_rows(mine, other, is_upper):
    lower_part = jnp.where(is_upper, other, mine)
    upper_part = jnp.where(is_upper, mine, other)
    return jnp.concatenate([lower_part, upper_part], axis=0)


def split_cols(values, cols_here, is_upper):
    lower_part = values[..., :cols_here]
    upper_part = values[..., cols_here:]
    return (
        jnp.where(is_upper, upper_part, lower_part),
        jnp.where(is_upper, lower_part, upper_part),
    )


def masked_scores(query_block, key_rows, query_start, block_rows, doc_rows, positions):
    factor = query_block.shape[-1] ** (-0.5)
    scores = (
        jnp.einsum("qhe,khe->hqk", query_block, key_rows, preferred_element_type=jnp.float32)
        * factor
    )
    query_place = query_start + jnp.arange(block_rows, dtype=jnp.int32)
    query_docs = lax.dynamic_slice_in_dim(doc_rows, query_start, block_rows, 0)
    allowed = (query_docs[:, None] == doc_rows[None, :]) & (
        query_place[:, None] >= positions[None, :]
    )
    return jnp.where(allowed[None], scores, masked)


def attend_forward(queries, key_rows, value_rows, doc_rows, row_offset):
    total_rows = queries.shape[0]
    block_rows = min(512, total_rows)
    positions = jnp.arange(key_rows.shape[0], dtype=jnp.int32)

    def one_block(first_row):
        query_block = lax.dynamic_slice_in_dim(queries, first_row, block_rows, 0)
        scores = masked_scores(
            query_block, key_rows, row_offset + first_row, block_rows, doc_rows, positions
        )
        row_peak = jnp.max(scores, axis=-1, keepdims=True)
        weights = jnp.exp(scores - row_peak)
        totals = jnp.sum(weights, axis=-1, keepdims=True)
        probabilities = (weights / totals).astype(jnp.bfloat16)
        output = jnp.einsum(
            "hqk,khe->qhe", probabilities, value_rows, preferred_element_type=jnp.float32
        )
        return (output, (row_peak + jnp.log(totals))[..., 0])

    starts = jnp.arange(total_rows // block_rows, dtype=jnp.int32) * block_rows
    outputs, log_totals = lax.map(one_block, starts)
    return (outputs.reshape(queries.shape), log_totals)


def attend_backward(queries, key_rows, value_rows, doc_rows, row_offset, log_totals, grad_out):
    total_rows = queries.shape[0]
    block_rows = min(512, total_rows)
    positions = jnp.arange(key_rows.shape[0], dtype=jnp.int32)
    factor = queries.shape[-1] ** (-0.5)

    def one_block(running, first_row):
        key_grad, value_grad = running
        query_block = lax.dynamic_slice_in_dim(queries, first_row, block_rows, 0)
        grad_block = lax.dynamic_slice_in_dim(grad_out, first_row, block_rows, 0)
        scores = masked_scores(
            query_block, key_rows, row_offset + first_row, block_rows, doc_rows, positions
        )
        block_totals = lax.dynamic_index_in_dim(
            log_totals, first_row // block_rows, 0, keepdims=False
        )
        probabilities = jnp.exp(scores - block_totals[..., None])
        prob_grad = jnp.einsum(
            "qhe,khe->hqk", grad_block, value_rows, preferred_element_type=jnp.float32
        )
        inner_sum = jnp.sum(probabilities * prob_grad, axis=-1, keepdims=True)
        score_grad = (probabilities * (prob_grad - inner_sum)).astype(jnp.bfloat16)
        query_grad = (
            jnp.einsum("hqk,khe->qhe", score_grad, key_rows, preferred_element_type=jnp.float32)
            * factor
        )
        key_grad = (
            key_grad
            + jnp.einsum(
                "hqk,qhe->khe", score_grad, query_block, preferred_element_type=jnp.float32
            )
            * factor
        )
        value_grad = value_grad + jnp.einsum(
            "hqk,qhe->khe",
            probabilities.astype(jnp.bfloat16),
            grad_block,
            preferred_element_type=jnp.float32,
        )
        return ((key_grad, value_grad), query_grad)

    starts = jnp.arange(total_rows // block_rows, dtype=jnp.int32) * block_rows
    zero_grads = jnp.zeros(key_rows.shape, jnp.float32)
    (key_grad, value_grad), query_grads = lax.scan(one_block, (zero_grads, zero_grads), starts)
    return (query_grads.reshape(queries.shape), key_grad, value_grad)


def stack_layers(layer_list, members):
    stacked = []
    for member_index in range(members):
        stacked.append(jnp.stack([entry[member_index] for entry in layer_list], axis=0))
    return stacked


def per_device(
    tokens,
    segment_ids,
    cotangent,
    ln_attn_gain,
    ln_attn_bias,
    qkv_weight,
    qv_bias,
    head_scale,
    out_weight,
    out_bias,
    ln_post_gain,
    ln_post_bias,
    ln_ffn_gain,
    ln_ffn_bias,
    fc1_weight,
    fc1_bias,
    mid_gain,
    mid_bias,
    fc2_weight,
    fc2_bias,
):
    layers = qkv_weight.shape[0]
    local_rows = tokens.shape[0]
    model_width = tokens.shape[1]
    cols_here = qkv_weight.shape[3]
    heads_all = head_scale.shape[1]
    head_width = model_width // heads_all
    pair_cols = 2 * cols_here
    pair_heads = pair_cols // head_width
    group_rows = segment_ids.shape[0]
    half_rows = group_rows // 2
    hidden_all = fc1_weight.shape[2] * lax.axis_size("mp")
    device_index = lax.axis_index("mp")
    is_upper = device_index % 2 == 1
    own_start = jnp.where(is_upper, half_rows, 0).astype(jnp.int32)
    other_start = jnp.where(is_upper, 0, half_rows).astype(jnp.int32)
    first_head = device_index // 2 * pair_heads
    pair_onehot = (
        (first_head + jnp.arange(pair_heads, dtype=jnp.int32))[:, None]
        == jnp.arange(heads_all, dtype=jnp.int32)[None, :]
    ).astype(jnp.float32)
    residual = tokens.astype(jnp.float32)
    stored = []
    for layer_index in range(layers):
        attn_in, attn_normal, attn_factor = norm_local(
            residual, ln_attn_gain[layer_index], ln_attn_bias[layer_index]
        )
        attn_rows = collect_rows(attn_in.astype(jnp.bfloat16))
        qkv_here = qkv_weight[layer_index].reshape(model_width, 3 * cols_here)
        projected = jnp.dot(attn_rows, qkv_here, preferred_element_type=jnp.float32).reshape(
            -1, 3, cols_here
        )
        bias_pair = qv_bias[layer_index]
        query_mine = (projected[:, 0] + bias_pair[0]).astype(jnp.bfloat16)
        key_mine = projected[:, 1].astype(jnp.bfloat16)
        value_mine = (projected[:, 2] + bias_pair[1]).astype(jnp.bfloat16)
        query_send = lax.dynamic_slice_in_dim(query_mine, other_start, half_rows, 0)
        query_recv, key_recv, value_recv = partner((query_send, key_mine, value_mine), "mp", 0)
        query_own = lax.dynamic_slice_in_dim(query_mine, own_start, half_rows, 0)
        queries = join_cols(query_own, query_recv, is_upper).reshape(
            half_rows, pair_heads, head_width
        )
        key_rows = join_cols(key_mine, key_recv, is_upper).reshape(
            group_rows, pair_heads, head_width
        )
        value_rows = join_cols(value_mine, value_recv, is_upper).reshape(
            group_rows, pair_heads, head_width
        )
        attended, log_totals = attend_forward(queries, key_rows, value_rows, segment_ids, own_start)
        pair_scale = jnp.sum(pair_onehot * head_scale[layer_index][None, :], axis=1)
        scaled_half = (
            (attended * pair_scale[None, :, None])
            .astype(jnp.bfloat16)
            .reshape(half_rows, pair_cols)
        )
        own_cols, other_cols = split_cols(scaled_half, cols_here, is_upper)
        scaled_recv = partner(other_cols, "mp", 0)
        scaled_mine = join_rows(own_cols, scaled_recv, is_upper)
        branch = (
            reduce_branch(scaled_mine, out_weight[layer_index], local_rows) + out_bias[layer_index]
        )
        post_out, post_normal, post_factor = norm_local(
            branch, ln_post_gain[layer_index], ln_post_bias[layer_index]
        )
        middle = residual + post_out
        ffn_in, ffn_normal, ffn_factor = norm_local(
            middle, ln_ffn_gain[layer_index], ln_ffn_bias[layer_index]
        )
        ffn_rows = collect_rows(ffn_in.astype(jnp.bfloat16))
        before_gelu = (
            jnp.dot(ffn_rows, fc1_weight[layer_index], preferred_element_type=jnp.float32)
            + fc1_bias[layer_index]
        )
        activated = jax.nn.gelu(before_gelu, approximate=False)
        first_sum, second_sum = hidden_stats(
            jnp.sum(activated, axis=1), jnp.sum(activated * activated, axis=1)
        )
        average = first_sum / hidden_all
        spread = second_sum / hidden_all - average * average
        hidden_factor = lax.rsqrt(spread + epsilon)[:, None]
        hidden_normal = (activated - average[:, None]) * hidden_factor
        mixed_b = (hidden_normal * mid_gain[layer_index] + mid_bias[layer_index]).astype(
            jnp.bfloat16
        )
        ffn_out = reduce_branch(mixed_b, fc2_weight[layer_index], local_rows)
        stored.append(
            (
                attn_normal,
                attn_factor,
                attn_rows,
                queries,
                key_rows,
                value_rows,
                attended,
                log_totals,
                pair_scale,
                scaled_mine,
                post_normal,
                post_factor,
                ffn_normal,
                ffn_factor,
                ffn_rows,
                before_gelu,
                hidden_normal,
                hidden_factor,
                mixed_b,
            )
        )
        residual = middle + ffn_out + fc2_bias[layer_index]
    layer_output = residual.astype(jnp.bfloat16)
    gradient = cotangent.astype(jnp.float32)
    sharded_list = []
    shared_list = []
    for layer_index in reversed(range(layers)):
        (
            attn_normal,
            attn_factor,
            attn_rows,
            queries,
            key_rows,
            value_rows,
            attended,
            log_totals,
            pair_scale,
            scaled_mine,
            post_normal,
            post_factor,
            ffn_normal,
            ffn_factor,
            ffn_rows,
            before_gelu,
            hidden_normal,
            hidden_factor,
            mixed_b,
        ) = stored[layer_index]
        qkv_here = qkv_weight[layer_index].reshape(model_width, 3 * cols_here)
        second_shift_grad = jnp.sum(gradient, axis=0)
        grad_rows = collect_grads(gradient.astype(jnp.bfloat16))
        mixed_grad = jnp.einsum(
            "td,fd->tf", grad_rows, fc2_weight[layer_index], preferred_element_type=jnp.float32
        )
        second_grad = jnp.einsum(
            "tf,td->fd", mixed_b, grad_rows, preferred_element_type=jnp.float32
        )
        hidden_gain_grad = jnp.sum(mixed_grad * hidden_normal, axis=0)
        hidden_shift_grad = jnp.sum(mixed_grad, axis=0)
        normal_grad = mixed_grad * mid_gain[layer_index]
        grad_first, grad_second = hidden_grad_stats(
            jnp.sum(normal_grad, axis=1), jnp.sum(normal_grad * hidden_normal, axis=1)
        )
        active_grad = hidden_factor * (
            normal_grad
            - grad_first[:, None] / hidden_all
            - hidden_normal * grad_second[:, None] / hidden_all
        )
        gelu_pull = jax.vjp(partial(jax.nn.gelu, approximate=False), before_gelu)[1]
        pre_grad_b = gelu_pull(active_grad)[0].astype(jnp.bfloat16)
        first_shift_grad = jnp.sum(pre_grad_b, axis=0, dtype=jnp.float32)
        first_grad = jnp.einsum(
            "td,tf->df", ffn_rows, pre_grad_b, preferred_element_type=jnp.float32
        )
        ffn_in_grad = reduce_grads(pre_grad_b, fc1_weight[layer_index], local_rows)
        ffn_gain_grad = jnp.sum(ffn_in_grad * ffn_normal, axis=0)
        ffn_bias_grad = jnp.sum(ffn_in_grad, axis=0)
        middle_grad = gradient + norm_back(
            ffn_in_grad, ffn_normal, ffn_factor, ln_ffn_gain[layer_index]
        )
        post_gain_grad = jnp.sum(middle_grad * post_normal, axis=0)
        post_bias_grad = jnp.sum(middle_grad, axis=0)
        branch_grad = norm_back(middle_grad, post_normal, post_factor, ln_post_gain[layer_index])
        out_shift_grad = jnp.sum(branch_grad, axis=0)
        branch_rows = collect_grads(branch_grad.astype(jnp.bfloat16))
        scaled_grad = jnp.einsum(
            "td,cd->tc", branch_rows, out_weight[layer_index], preferred_element_type=jnp.float32
        )
        out_grad = jnp.einsum(
            "tc,td->cd", scaled_mine, branch_rows, preferred_element_type=jnp.float32
        )
        grad_send = lax.dynamic_slice_in_dim(scaled_grad, other_start, half_rows, 0)
        grad_recv = partner(grad_send.astype(jnp.bfloat16), "mp", 0).astype(grad_send.dtype)
        grad_own = lax.dynamic_slice_in_dim(scaled_grad, own_start, half_rows, 0)
        scaled_pair = join_cols(grad_own, grad_recv, is_upper).reshape(
            half_rows, pair_heads, head_width
        )
        pair_scale_grad = jnp.sum(attended * scaled_pair, axis=(0, 2))
        scale_grad = jnp.sum(pair_onehot * pair_scale_grad[:, None], axis=0)
        attended_grad_b = (scaled_pair * pair_scale[None, :, None]).astype(jnp.bfloat16)
        query_grad, key_grad, value_grad = attend_backward(
            queries, key_rows, value_rows, segment_ids, own_start, log_totals, attended_grad_b
        )
        query_own, query_other = split_cols(
            query_grad.reshape(half_rows, pair_cols), cols_here, is_upper
        )
        key_own, key_other = split_cols(
            key_grad.reshape(group_rows, pair_cols), cols_here, is_upper
        )
        value_own, value_other = split_cols(
            value_grad.reshape(group_rows, pair_cols), cols_here, is_upper
        )
        query_recv, key_recv, value_recv = (
            partner(query_other.astype(jnp.bfloat16), "mp", 0).astype(query_other.dtype),
            partner(key_other.astype(jnp.bfloat16), "mp", 0).astype(key_other.dtype),
            partner(value_other.astype(jnp.bfloat16), "mp", 0).astype(value_other.dtype),
        )
        query_grad_b = join_rows(query_own, query_recv, is_upper).astype(jnp.bfloat16)
        key_grad_b = (key_own + key_recv).astype(jnp.bfloat16)
        value_grad_b = (value_own + value_recv).astype(jnp.bfloat16)
        proj_grad = jnp.stack([query_grad_b, key_grad_b, value_grad_b], axis=1).reshape(
            -1, 3 * cols_here
        )
        pair_grad = jnp.stack(
            [
                jnp.sum(query_grad_b, axis=0, dtype=jnp.float32),
                jnp.sum(value_grad_b, axis=0, dtype=jnp.float32),
            ],
            axis=0,
        )
        qkv_grad = jnp.einsum(
            "td,tc->dc", attn_rows, proj_grad, preferred_element_type=jnp.float32
        ).reshape(model_width, 3, cols_here)
        attn_in_grad = reduce_grads(proj_grad, qkv_here, local_rows)
        attn_gain_grad = jnp.sum(attn_in_grad * attn_normal, axis=0)
        attn_bias_grad = jnp.sum(attn_in_grad, axis=0)
        gradient = middle_grad + norm_back(
            attn_in_grad, attn_normal, attn_factor, ln_attn_gain[layer_index]
        )
        sharded_list.insert(
            0,
            (
                qkv_grad,
                pair_grad,
                out_grad,
                first_grad,
                first_shift_grad,
                hidden_gain_grad,
                hidden_shift_grad,
                second_grad,
            ),
        )
        shared_list.insert(
            0,
            (
                attn_gain_grad,
                attn_bias_grad,
                scale_grad,
                out_shift_grad,
                post_gain_grad,
                post_bias_grad,
                ffn_gain_grad,
                ffn_bias_grad,
                second_shift_grad,
            ),
        )
    sharded = stack_layers(sharded_list, 8)
    shared = stack_layers(shared_list, 9)
    sharded = (
        lax.psum(sharded[0].astype(jnp.bfloat16), "rows").astype(jnp.float32),
        lax.psum(sharded[1].astype(jnp.bfloat16), "rows").astype(jnp.float32),
        lax.psum(sharded[2].astype(jnp.bfloat16), "rows").astype(jnp.float32),
        lax.psum(sharded[3].astype(jnp.bfloat16), "rows").astype(jnp.float32),
        lax.psum(sharded[4].astype(jnp.bfloat16), "rows").astype(jnp.float32),
        lax.psum(sharded[5].astype(jnp.bfloat16), "rows").astype(jnp.float32),
        lax.psum(sharded[6].astype(jnp.bfloat16), "rows").astype(jnp.float32),
        lax.psum(sharded[7].astype(jnp.bfloat16), "rows").astype(jnp.float32),
    )
    shared = lax.psum(
        (
            shared[0],
            shared[1],
            shared[2],
            shared[3],
            shared[4],
            shared[5],
            shared[6],
            shared[7],
            shared[8],
        ),
        ("rows", "mp"),
    )
    return (
        layer_output,
        gradient,
        shared[0],
        shared[1],
        sharded[0],
        sharded[1],
        shared[2],
        sharded[2],
        shared[3],
        shared[4],
        shared[5],
        shared[6],
        shared[7],
        sharded[3],
        sharded[4],
        sharded[5],
        sharded[6],
        sharded[7],
        shared[8],
    )


MESH_ID = pl.DeviceIdType.MESH
PLANE = ("core", "y", "x")
EVERY = ("y", "core", "z", "x")
f32 = jnp.float32
bf16 = jnp.bfloat16
GATHER, SCATTER, SECOND, MIDWAY = "gather", "scatter", "second", "midway"


def vmem_params(collective_id=None, mib=24):
    if collective_id is None:
        return pltpu.CompilerParams(vmem_limit_bytes=mib * 2**20)
    return pltpu.CompilerParams(
        vmem_limit_bytes=mib * 2**20, collective_id=collective_id, has_side_effects=True
    )


class Here:
    def __init__(self):
        self.x, self.y = lax.axis_index("x"), lax.axis_index("y")
        self.core, self.z = lax.axis_index("core"), lax.axis_index("z")

    def peer(self, flip_x, flip_y, flip_core, step_z):
        place = {}
        if flip_x:
            place["x"] = 1 - self.x
        if flip_y:
            place["y"] = 1 - self.y
        if flip_core:
            place["core"] = 1 - self.core
        if step_z:
            place["z"] = lax.rem(self.z + step_z, 4)
        return place

    def block(self, at_core, at_x, at_y):
        return (2 * at_core + lax.rem(at_y + self.z, 2)) * 2 + at_x


BY_X, BY_Y, BY_CORE = (1, 0, 0, 0), (0, 1, 0, 0), (0, 0, 1, 0)
BY_Z = tuple((0, 0, 0, step) for step in (1, 2, 3))
BY_LINE = BY_Z + tuple((0, 0, 1, step) for step in range(4))
BY_PLANE = tuple((flip & 1, flip >> 1 & 1, flip >> 2, 0) for flip in range(1, 8))


def remote(source, target, send_sem, recv_sem, place):
    return pltpu.make_async_remote_copy(
        src_ref=source,
        dst_ref=target,
        send_sem=send_sem,
        recv_sem=recv_sem,
        device_id=place,
        device_id_type=MESH_ID,
    )


def dma_sems(count):
    return pltpu.SemaphoreType.DMA((count,))


class Task:
    arrays = ()
    spaces = ()
    outs = ()
    out_spaces = ()
    scratch = ()
    reach = ()

    def moment(self, name):
        pass

    def start(self, here, ins, outs, scratch):
        pass

    def at_moment(self, name, here, ins, outs, scratch):
        pass

    def finish(self, here, ins, outs, scratch):
        pass


def run_tasks(ids, *tasks):
    reach = []
    for task in tasks:
        reach += [way for way in task.reach if way not in reach]

    near = []
    for task in tasks:
        near += [space == pltpu.VMEM for space in task.spaces]
    arrays = [array for task in tasks for array in task.arrays]
    loaded = [i for i, each in enumerate(near) if each]

    def kernel(*refs):
        refs = list(refs)
        *refs, load_sem = refs
        held = refs[len(refs) - len(loaded) :]
        refs = refs[: len(refs) - len(loaded)]
        loads = []
        for slot, index in enumerate(loaded):
            loads.append(pltpu.make_async_copy(refs[index], held[slot], load_sem.at[slot]))
            loads[-1].start()
            refs[index] = held[slot]
        views = [[], [], []]
        for kind, name in enumerate(("arrays", "outs", "scratch")):
            for task in tasks:
                count = len(getattr(task, name))
                views[kind].append(refs[:count])
                refs = refs[count:]
        here = Here()
        barrier = pltpu.get_barrier_semaphore()
        for way in reach:
            pl.semaphore_signal(barrier, inc=1, device_id=here.peer(*way), device_id_type=MESH_ID)
        pl.semaphore_wait(barrier, len(reach))
        for each in loads:
            each.wait()
        for task, *held in zip(tasks, *views):
            task.start(here, *held)

        def moment(name):
            for task, *held in zip(tasks, *views):
                task.at_moment(name, here, *held)

        tasks[0].moment = moment
        for task, *held in zip(tasks, *views):
            task.finish(here, *held)

    results = pl.pallas_call(
        kernel,
        out_shape=[out for task in tasks for out in task.outs],
        in_specs=[pl.BlockSpec(memory_space=pltpu.HBM)] * len(arrays),
        out_specs=[pl.BlockSpec(memory_space=s) for task in tasks for s in task.out_spaces],
        scratch_shapes=[each for task in tasks for each in task.scratch]
        + [pltpu.VMEM(arrays[i].shape, arrays[i].dtype) for i in loaded]
        + [dma_sems(len(loaded))],
        compiler_params=vmem_params(next(ids), 60),
    )(*arrays)
    results = list(results)
    split = []
    for task in tasks:
        split.append(results[: len(task.outs)])
        results = results[len(task.outs) :]
    return split


class PlaneMove(Task):
    def __init__(self, values, back=False, when=MIDWAY, first="start"):
        self.back, self.when, self.first = back, when, first
        self.arrays, self.spaces = (values,), (pltpu.HBM,)
        self.outs = (jax.ShapeDtypeStruct(values.shape, values.dtype),)
        self.out_spaces = (pltpu.HBM,)
        self.scratch = (
            pltpu.VMEM(values.shape, values.dtype),
            dma_sems(3),
            dma_sems(2),
        )
        self.reach = (BY_Y,) + BY_LINE

    def bend(self, here):
        return lax.rem(here.z + here.core, 2) == here.y

    def ends(self, here):
        targets = [{"core": here.z // 2, "z": 2 * y + here.core} for y in range(2)]
        at_home = [(here.z // 2 == here.core) & (2 * y + here.core == here.z) for y in range(2)]
        origin_core = lax.rem(here.z, 2)
        origin_z = 2 * here.core + lax.rem(here.y + origin_core, 2)
        origin_home = (origin_core == here.core) & (origin_z == here.z)
        return targets, at_home, {"core": origin_core, "z": origin_z}, origin_home

    def plan(self, here, ins, outs, scratch):
        held, send, recv = scratch
        targets, at_home, origin, origin_home = self.ends(here)
        bend = self.bend(here)
        away_from = jnp.logical_not
        to_y = here.peer(*BY_Y)
        first, second = [], []
        if not self.back:
            over = remote(ins[0], held, send.at[2], recv.at[0], to_y)
            first.append((away_from(bend), over, True))
            for y in range(2):
                for legs, source, when in (
                    (first, ins[0], bend & (here.y == y)),
                    (second, held, bend & (here.y != y)),
                ):
                    away = remote(source, outs[0], send.at[y], recv.at[1], targets[y])
                    stay = pltpu.make_async_copy(source, outs[0], recv.at[1])
                    legs.append((when & away_from(at_home[y]), away, True))
                    legs.append((when & at_home[y], stay, False))
        else:
            ends_there = here.z // 2 == here.y
            for goes_on, target, slot in ((False, outs[0], 1), (True, held, 0)):
                when = away_from(ends_there) if goes_on else ends_there
                away = remote(ins[0], target, send.at[int(goes_on)], recv.at[slot], origin)
                stay = pltpu.make_async_copy(ins[0], target, recv.at[slot])
                first.append((when & away_from(origin_home), away, True))
                first.append((when & origin_home, stay, False))
            over = remote(held, outs[0], send.at[2], recv.at[1], to_y)
            second.append((bend, over, True))
        return first, second

    def start(self, *held):
        self.at_moment("start", *held)

    def at_moment(self, name, here, ins, outs, scratch):
        if name == self.first:
            for when, copy, _ in self.plan(here, ins, outs, scratch)[0]:
                pl.when(when)(copy.start)
        if name == self.when:
            held, _, recv = scratch

            @pl.when(self.bend(here))
            def _():
                pltpu.make_async_copy(held, held, recv.at[0]).wait()

            for when, copy, _ in self.plan(here, ins, outs, scratch)[1]:
                pl.when(when)(copy.start)

    def finish(self, here, ins, outs, scratch):
        self.at_moment("end", here, ins, outs, scratch)
        pltpu.make_async_copy(outs[0], outs[0], scratch[2].at[1]).wait()
        for legs in self.plan(here, ins, outs, scratch):
            for when, copy, is_remote in legs:
                if is_remote:
                    pl.when(when)(copy.wait_send)


class PlaneGather(Task):
    def __init__(self, block):
        rows, width = block.shape
        self.arrays, self.spaces = (block,), (pltpu.VMEM,)
        self.outs = (jax.ShapeDtypeStruct((8 * rows, width), block.dtype),)
        self.out_spaces = (pltpu.VMEM,)
        self.scratch = (dma_sems(11), dma_sems(11), pltpu.SemaphoreType.DMA)
        self.reach = (BY_X, BY_Y, BY_CORE)

    def place(self, here, o_ref, at_x, at_y, part=None):
        rows = o_ref.shape[0] // 8
        first = here.block(here.core, at_x, at_y) * rows
        if part is None:
            return o_ref.at[pl.ds(pl.multiple_of(first, rows), rows)]
        half = rows // 2
        return o_ref.at[pl.ds(pl.multiple_of(first + part * half, half), half)]

    def copies(self, here, x_ref, o_ref, send_sem, recv_sem):
        x, y = here.x, here.y
        half = x_ref.shape[0] // 2
        to_x, to_y, to_core = here.peer(*BY_X), here.peer(*BY_Y), here.peer(*BY_CORE)

        def copy(index, source, target, way):
            return remote(source, target, send_sem.at[index], recv_sem.at[index], way)

        def pass_on(index, way, *at):
            return copy(index, self.place(here, o_ref, *at), self.place(here, o_ref, *at), way)

        own = [self.place(here, o_ref, x, y, part) for part in (0, 1)]
        mine = [x_ref.at[pl.ds(part * half, half)] for part in (0, 1)]
        return [
            copy(0, mine[0], own[0], to_x),
            copy(1, mine[1], own[1], to_y),
            copy(2, mine[1], own[1], to_x),
            copy(3, mine[0], own[0], to_y),
            copy(4, x_ref, self.place(here, o_ref, x, y), to_core),
            pass_on(5, to_y, 1 - x, y, 0),
            pass_on(6, to_x, x, 1 - y, 1),
            pass_on(7, to_core, 1 - x, y),
            pass_on(8, to_core, x, 1 - y),
            pass_on(9, to_core, 1 - x, 1 - y, 0),
            pass_on(10, to_core, 1 - x, 1 - y, 1),
        ]

    def keep(self, here, x_ref, o_ref, own_sem):
        return pltpu.make_async_copy(x_ref, self.place(here, o_ref, here.x, here.y), own_sem)

    def start(self, here, ins, outs, scratch):
        copies = self.copies(here, ins[0], outs[0], scratch[0], scratch[1])
        for index in range(5):
            copies[index].start()
        self.keep(here, ins[0], outs[0], scratch[2]).start()

    def finish(self, here, ins, outs, scratch, work=None, moment=None):
        rows = ins[0].shape[0]
        copies = self.copies(here, ins[0], outs[0], scratch[0], scratch[1])

        def done(flip_core, flip_x, flip_y):
            if work is not None:
                at_core = 1 - here.core if flip_core else here.core
                at_x = 1 - here.x if flip_x else here.x
                at_y = 1 - here.y if flip_y else here.y
                work(pl.multiple_of(here.block(at_core, at_x, at_y) * rows, rows))

        self.keep(here, ins[0], outs[0], scratch[2]).wait()
        done(0, 0, 0)
        copies[4].wait_recv()
        done(1, 0, 0)
        for index in range(4):
            copies[index].wait_recv()
            copies[5 + index].start()
        if moment is not None:
            moment("spare")
        done(0, 1, 0)
        done(0, 0, 1)
        copies[7].wait_recv()
        done(1, 1, 0)
        copies[8].wait_recv()
        done(1, 0, 1)
        copies[5].wait_recv()
        copies[9].start()
        copies[6].wait_recv()
        copies[10].start()
        done(0, 1, 1)
        if moment is not None:
            moment("soon")
        copies[9].wait_recv()
        copies[10].wait_recv()
        done(1, 1, 1)
        for each in copies:
            each.wait_send()


class OrderedGather(PlaneGather):
    def ends(self, here):
        over_x = here.core == 0
        first = (jnp.where(over_x, 1 - here.x, here.x), jnp.where(over_x, here.y, 1 - here.y))
        second = (jnp.where(over_x, here.x, 1 - here.x), jnp.where(over_x, 1 - here.y, here.y))
        return first, second

    def copies(self, here, x_ref, o_ref, send_sem, recv_sem):
        half = x_ref.shape[0] // 2
        first, second = self.ends(here)
        to_first, to_second = ({"x": at[0], "y": at[1]} for at in (first, second))
        to_core = here.peer(*BY_CORE)

        def copy(index, source, target, way):
            return remote(source, target, send_sem.at[index], recv_sem.at[index], way)

        def pass_on(index, way, *at):
            return copy(index, self.place(here, o_ref, *at), self.place(here, o_ref, *at), way)

        own = [self.place(here, o_ref, here.x, here.y, part) for part in (0, 1)]
        mine = [x_ref.at[pl.ds(part * half, half)] for part in (0, 1)]
        far = (1 - here.x, 1 - here.y)
        return [
            copy(0, mine[0], own[0], to_first),
            copy(1, mine[1], own[1], to_first),
            copy(2, mine[1], own[1], to_second),
            copy(3, mine[0], own[0], to_second),
            copy(4, x_ref, self.place(here, o_ref, here.x, here.y), to_core),
            pass_on(5, to_second, *first, 0),
            pass_on(6, to_first, *second, 1),
            pass_on(7, to_core, *first),
            pass_on(8, to_core, *second),
            pass_on(9, to_core, *far, 0),
            pass_on(10, to_core, *far, 1),
        ]

    def start(self, here, ins, outs, scratch):
        copies = self.copies(here, ins[0], outs[0], scratch[0], scratch[1])
        for index in (0, 1, 4):
            copies[index].start()
        self.keep(here, ins[0], outs[0], scratch[2]).start()

    def finish(self, here, ins, outs, scratch, work=None, moment=None):
        rows = ins[0].shape[0]
        copies = self.copies(here, ins[0], outs[0], scratch[0], scratch[1])
        first, second = self.ends(here)
        far = (1 - here.x, 1 - here.y)

        def done(at_core, at):
            if work is not None:
                work(pl.multiple_of(here.block(at_core, *at) * rows, rows))

        self.keep(here, ins[0], outs[0], scratch[2]).wait()
        done(here.core, (here.x, here.y))
        copies[0].wait_send()
        copies[1].wait_send()
        copies[2].start()
        copies[3].start()
        copies[4].wait_recv()
        done(1 - here.core, (here.x, here.y))
        copies[0].wait_recv()
        copies[5].start()
        copies[1].wait_recv()
        copies[7].start()
        done(here.core, first)
        copies[7].wait_recv()
        done(1 - here.core, second)
        copies[2].wait_recv()
        copies[6].start()
        copies[3].wait_recv()
        copies[8].start()
        if moment is not None:
            moment("spare")
        done(here.core, second)
        copies[8].wait_recv()
        done(1 - here.core, first)
        copies[5].wait_recv()
        copies[9].start()
        copies[6].wait_recv()
        copies[10].start()
        done(here.core, far)
        if moment is not None:
            moment("soon")
        copies[9].wait_recv()
        copies[10].wait_recv()
        done(1 - here.core, far)
        for each in copies[2:]:
            each.wait_send()


class PlaneScatter(Task):
    def __init__(self, rows, width, weight_dim):
        half = rows // 2
        self.weight_dim = weight_dim
        self.scratch = (
            pltpu.VMEM((4, rows, width), bf16),
            pltpu.VMEM((4, rows, width), bf16),
            pltpu.VMEM((rows, width), bf16),
            pltpu.VMEM((2, half, width), bf16),
            pltpu.VMEM((2, half, width), bf16),
            pltpu.VMEM((2, half, width), bf16),
            pltpu.VMEM((2, half, width), bf16),
            pltpu.VMEM((2, half, width), bf16),
            pltpu.VMEM((half, width), f32),
            pltpu.VMEM((half, width), f32),
            dma_sems(10),
            dma_sems(10),
        )
        self.reach = (BY_X, BY_Y, BY_CORE)

    def finish(self, here, ins, outs, scratch, rows_of, weight_of, early=None, idle=None):
        o_ref = outs[0]
        (
            sib_out,
            sib_in,
            diag_out,
            diag_in,
            last_x_out,
            last_y_out,
            last_x_in,
            last_y_in,
            wait_x,
            wait_y,
            send_sem,
            recv_sem,
        ) = scratch
        rows = o_ref.shape[0]
        half = rows // 2
        x, y, core = here.x, here.y, here.core
        to_x, to_y, to_core = here.peer(*BY_X), here.peer(*BY_Y), here.peer(*BY_CORE)

        def term(at_core, at_x, at_y):
            first = pl.multiple_of(here.block(at_core, at_x, at_y) * rows, rows)
            return lax.dot_general(
                rows_of(first),
                weight_of(),
                (((1,), (self.weight_dim,)), ((), ())),
                preferred_element_type=f32,
            )

        def copy(index, source, target, way):
            return remote(source, target, send_sem.at[index], recv_sem.at[index], way)

        places = ((1 - x, 1 - y), (1 - x, y), (x, 1 - y), (x, y))
        siblings = [copy(i, sib_out.at[i], sib_in.at[i], to_core) for i in range(4)]

        def help_sibling(i):
            sib_out[i] = term(1 - core, *places[i]).astype(bf16)
            siblings[i].start()

        def joined(i):
            mine = term(core, *places[i])
            siblings[i].wait_recv()
            return mine + sib_in[i].astype(f32)

        help_sibling(0)
        total = joined(0)
        diag_out[...] = total.astype(bf16)
        diag_x = copy(4, diag_out.at[pl.ds(0, half)], diag_in.at[0], to_x)
        diag_y = copy(5, diag_out.at[pl.ds(half, half)], diag_in.at[1], to_y)
        diag_x.start()
        diag_y.start()
        help_sibling(1)
        total = joined(1)
        last_x_out[0] = total[:half].astype(bf16)
        x_0 = copy(6, last_x_out.at[0], last_x_in.at[0], to_x)
        x_0.start()
        wait_x[...] = total[half:]
        if early is not None:
            early()
        help_sibling(2)
        total = joined(2)
        last_y_out[1] = total[half:].astype(bf16)
        y_1 = copy(7, last_y_out.at[1], last_y_in.at[1], to_y)
        y_1.start()
        wait_y[...] = total[:half]
        help_sibling(3)
        diag_y.wait_recv()
        last_x_out[1] = (wait_x[...] + diag_in[1].astype(f32)).astype(bf16)
        x_1 = copy(8, last_x_out.at[1], last_x_in.at[1], to_x)
        x_1.start()
        diag_x.wait_recv()
        last_y_out[0] = (wait_y[...] + diag_in[0].astype(f32)).astype(bf16)
        y_0 = copy(9, last_y_out.at[0], last_y_in.at[0], to_y)
        y_0.start()
        o_ref[...] = joined(3)
        if idle is not None:
            idle()
        for part, (by_x, by_y) in enumerate(((x_0, y_0), (x_1, y_1))):
            by_x.wait_recv()
            by_y.wait_recv()
            piece = pl.ds(part * half, half)
            o_ref[piece, :] += last_x_in[part].astype(f32) + last_y_in[part].astype(f32)
        for sent in (*siblings, diag_x, diag_y, x_0, y_1, x_1, y_0):
            sent.wait_send()


class PlaneSum(Task):
    def __init__(self, values):
        self.arrays, self.spaces = (values,), (pltpu.VMEM,)
        self.outs = (jax.ShapeDtypeStruct(values.shape, f32),)
        self.out_spaces = (pltpu.VMEM,)
        self.scratch = (pltpu.VMEM((7, *values.shape), f32), dma_sems(7), dma_sems(7))
        self.reach = BY_PLANE

    def copies(self, here, ins, scratch):
        got, send_sem, recv_sem = scratch
        return [
            remote(ins[0], got.at[i], send_sem.at[i], recv_sem.at[i], here.peer(*way))
            for i, way in enumerate(BY_PLANE)
        ]

    def start(self, here, ins, outs, scratch):
        for each in self.copies(here, ins, scratch):
            each.start()

    def finish(self, here, ins, outs, scratch):
        copies = self.copies(here, ins, scratch)
        for each in copies:
            each.wait_recv()
        got = scratch[0]
        by_x = [ins[0][...] + got[0]]
        for flip in (2, 4, 6):
            by_x.append(got[flip - 1] + got[flip])
        outs[0][...] = (by_x[0] + by_x[1]) + (by_x[2] + by_x[3])
        for each in copies:
            each.wait_send()


class LineGather(Task):
    def __init__(self, values):
        self.arrays, self.spaces = (values,), (pltpu.HBM,)
        self.outs = (jax.ShapeDtypeStruct((4, *values.shape), values.dtype),)
        self.out_spaces = (pltpu.HBM,)
        self.scratch = (dma_sems(4), dma_sems(3))
        self.reach = BY_Z

    def copies(self, here, ins, outs, scratch):
        target = outs[0].at[here.z]
        keep = pltpu.make_async_copy(ins[0], target, scratch[0].at[3])
        return keep, [
            remote(ins[0], target, scratch[0].at[i], scratch[1].at[i], here.peer(*way))
            for i, way in enumerate(BY_Z)
        ]

    def start(self, here, ins, outs, scratch):
        keep, copies = self.copies(here, ins, outs, scratch)
        for each in copies:
            each.start()
        keep.start()

    def finish(self, here, ins, outs, scratch):
        keep, copies = self.copies(here, ins, outs, scratch)
        for each in copies:
            each.wait()
        keep.wait()


class HeadGather(Task):
    def __init__(self, qkv, out, layer, when="start"):
        _, kinds, both, width = qkv.shape
        self.layer, self.when = layer, when
        self.arrays, self.spaces = (qkv, out), (pltpu.HBM,) * 2
        self.outs = (jax.ShapeDtypeStruct((kinds + 1, 2, both // 2, width), qkv.dtype),)
        self.out_spaces = (pltpu.HBM,)
        self.scratch = (dma_sems(8), dma_sems(8))
        self.reach = BY_LINE

    def pieces(self, outs, shard, part):
        half = outs[0].shape[3] // 2
        columns = pl.ds(pl.multiple_of(part * half, half), half)
        return outs[0].at[pl.ds(0, 3), shard, :, columns], outs[0].at[3, shard, :, columns]

    def copies(self, here, ins, outs, scratch):
        shard, target_core = lax.rem(here.z, 2), here.z // 2
        wide, half = outs[0].shape[2], outs[0].shape[3] // 2
        rows = pl.ds(pl.multiple_of(here.y * wide, wide), wide)
        columns = pl.ds(pl.multiple_of(here.core * half, half), half)
        sources = (ins[0].at[self.layer, :, rows, columns], ins[1].at[self.layer, rows, columns])
        targets = self.pieces(outs, shard, here.core)
        keeps, aways = [], []
        for kind in range(2):
            recv_sem = scratch[1].at[4 * kind + 2 * shard + here.core]
            keeps.append(pltpu.make_async_copy(sources[kind], targets[kind], recv_sem))
            for step in range(4):
                place = {"core": target_core, "z": lax.rem(here.z + step, 4)}
                send_sem = scratch[0].at[4 * kind + step]
                aways.append(remote(sources[kind], targets[kind], send_sem, recv_sem, place))
        return keeps, aways

    def begin(self, here, ins, outs, scratch):
        keeps, aways = self.copies(here, ins, outs, scratch)
        for index, each in enumerate(aways):
            if index % 4:
                each.start()
        at_home = here.z // 2 == here.core
        for kind in range(2):
            pl.when(at_home)(keeps[kind].start)
            pl.when(jnp.logical_not(at_home))(aways[4 * kind].start)

    def start(self, *held):
        self.at_moment("start", *held)

    def at_moment(self, name, *held):
        if name == self.when:
            self.begin(*held)

    def arrive(self, kind, outs, scratch):
        for shard in range(2):
            for part in range(2):
                piece = self.pieces(outs, shard, part)[kind]
                recv_sem = scratch[1].at[4 * kind + 2 * shard + part]
                pltpu.make_async_copy(piece, piece, recv_sem).wait()

    def sent(self, here, ins, outs, scratch):
        keeps, aways = self.copies(here, ins, outs, scratch)
        for index, each in enumerate(aways):
            if index % 4:
                each.wait_send()
        for kind in range(2):
            pl.when(here.z // 2 != here.core)(aways[4 * kind].wait_send)

    def finish(self, here, ins, outs, scratch):
        for kind in range(2):
            self.arrive(kind, outs, scratch)
        self.sent(here, ins, outs, scratch)


class LineScatter(Task):
    def __init__(self, values):
        shape = values.shape[1:]
        self.arrays, self.spaces = (values,), (pltpu.VMEM,)
        self.outs, self.out_spaces = (jax.ShapeDtypeStruct(shape, values.dtype),), (pltpu.VMEM,)
        self.scratch = (pltpu.VMEM((3, *shape), values.dtype), dma_sems(3), dma_sems(3))
        self.reach = BY_Z

    def copies(self, here, ins, scratch):
        got, send_sem, recv_sem = scratch
        return [
            remote(
                ins[0].at[lax.rem(here.z + i + 1, 4)],
                got.at[i],
                send_sem.at[i],
                recv_sem.at[i],
                here.peer(*way),
            )
            for i, way in enumerate(BY_Z)
        ]

    def start(self, here, ins, outs, scratch):
        for each in self.copies(here, ins, scratch):
            each.start()

    def finish(self, here, ins, outs, scratch):
        copies = self.copies(here, ins, scratch)
        for each in copies:
            each.wait_recv()
        total = ins[0][here.z].astype(f32)
        for i in range(3):
            total = total + scratch[0][i].astype(f32)
        outs[0][...] = total.astype(outs[0].dtype)
        for each in copies:
            each.wait_send()


class HeadScatter(Task):
    def __init__(self, values):
        kinds, _, wide, width = values.shape
        shape = (kinds, wide, width // 2)
        self.arrays, self.spaces = (values,), (pltpu.VMEM,)
        self.outs, self.out_spaces = (jax.ShapeDtypeStruct(shape, values.dtype),), (pltpu.VMEM,)
        self.scratch = (pltpu.VMEM((4, *shape), values.dtype), dma_sems(4), dma_sems(4))
        self.reach = BY_LINE

    def copies(self, here, ins, scratch):
        got, send_sem, recv_sem = scratch
        half = ins[0].shape[3] // 2
        triples = []
        for shard in range(2):
            for part in range(2):
                source = ins[0].at[:, shard, :, pl.ds(part * half, half)]
                target_z = 2 * here.core + shard
                slot = recv_sem.at[here.z]
                away = remote(
                    source,
                    got.at[here.z],
                    send_sem.at[2 * shard + part],
                    slot,
                    {"core": part, "z": target_z},
                )
                stay = pltpu.make_async_copy(source, got.at[here.z], slot)
                at_home = (target_z == here.z) & (here.core == part)
                triples.append((away, stay, at_home))
        return triples

    def start(self, here, ins, outs, scratch):
        for away, stay, at_home in self.copies(here, ins, scratch):
            pl.when(at_home)(stay.start)
            pl.when(jnp.logical_not(at_home))(away.start)

    def finish(self, here, ins, outs, scratch):
        got, send_sem, recv_sem = scratch
        for plane in range(4):
            pltpu.make_async_copy(got.at[plane], got.at[plane], recv_sem.at[plane]).wait()
        total = got[0].astype(f32)
        for plane in range(1, 4):
            total = total + got[plane].astype(f32)
        outs[0][...] = total.astype(outs[0].dtype)
        for away, stay, at_home in self.copies(here, ins, scratch):
            pl.when(jnp.logical_not(at_home))(away.wait_send)


class RowsGather(Task):
    def __init__(self, values, when="start"):
        self.when = when
        self.arrays, self.spaces = (values,), (pltpu.HBM,)
        self.outs = (jax.ShapeDtypeStruct((4, *values.shape), values.dtype),)
        self.out_spaces = (pltpu.HBM,)
        self.scratch = (dma_sems(4), dma_sems(3))
        self.reach = (BY_Y, BY_CORE)

    def copies(self, here, ins, outs, scratch):
        send_sem, recv_sem = scratch
        own = outs[0].at[2 * here.y + here.core]
        over = outs[0].at[2 * (1 - here.y) + here.core]
        to_y, to_core = here.peer(*BY_Y), here.peer(*BY_CORE)
        return (
            pltpu.make_async_copy(ins[0], own, send_sem.at[3]),
            remote(ins[0], own, send_sem.at[0], recv_sem.at[0], to_y),
            remote(ins[0], own, send_sem.at[1], recv_sem.at[1], to_core),
            remote(over, over, send_sem.at[2], recv_sem.at[2], to_core),
        )

    def start(self, *held):
        self.at_moment("start", *held)

    def at_moment(self, name, *held):
        if name == self.when:
            self.begin(*held)

    def begin(self, here, ins, outs, scratch):
        keep, by_y, by_core, again = self.copies(here, ins, outs, scratch)
        by_y.start()
        by_core.start()
        keep.start()

    def finish(self, here, ins, outs, scratch):
        keep, by_y, by_core, again = self.copies(here, ins, outs, scratch)
        by_y.wait_recv()
        again.start()
        by_core.wait_recv()
        again.wait_recv()
        for each in (by_y, by_core, again):
            each.wait_send()
        keep.wait()


class StepSum(Task):
    def __init__(self, values):
        self.arrays, self.spaces = (values,), (pltpu.VMEM,)
        self.outs = (jax.ShapeDtypeStruct(values.shape, f32),)
        self.out_spaces = (pltpu.VMEM,)
        self.scratch = (
            pltpu.VMEM((2, *values.shape), f32),
            pltpu.VMEM((3, *values.shape), f32),
            dma_sems(3),
            dma_sems(3),
        )
        self.reach = (BY_X, BY_Y, BY_CORE)

    def leg(self, here, index, source, scratch):
        _, got, send_sem, recv_sem = scratch
        way = here.peer(*self.reach[index])
        return remote(source, got.at[index], send_sem.at[index], recv_sem.at[index], way)

    def start(self, here, ins, outs, scratch):
        self.leg(here, 0, ins[0], scratch).start()

    def at_moment(self, name, here, ins, outs, scratch):
        part, got = scratch[:2]
        if name == MIDWAY:
            self.leg(here, 0, ins[0], scratch).wait()
            part[0] = ins[0][...] + got[0]
            self.leg(here, 1, part.at[0], scratch).start()
        if name == "closing":
            self.leg(here, 1, part.at[0], scratch).wait()
            part[1] = part[0] + got[1]
            self.leg(here, 2, part.at[1], scratch).start()

    def finish(self, here, ins, outs, scratch):
        part, got = scratch[:2]
        self.leg(here, 2, part.at[1], scratch).wait()
        outs[0][...] = part[1] + got[2]


class LineSum(Task):
    def __init__(self, values):
        self.arrays, self.spaces = (values,), (pltpu.VMEM,)
        self.outs = (jax.ShapeDtypeStruct(values.shape, f32),)
        self.out_spaces = (pltpu.VMEM,)
        self.scratch = (pltpu.VMEM((4, *values.shape), f32), dma_sems(3), dma_sems(4))
        self.reach = BY_Z

    def copies(self, here, ins, scratch):
        got, send_sem, recv_sem = scratch
        there, slot = got.at[here.z], recv_sem.at[here.z]
        keep = pltpu.make_async_copy(ins[0], there, slot)
        return keep, [
            remote(ins[0], there, send_sem.at[i], slot, here.peer(*way))
            for i, way in enumerate(BY_Z)
        ]

    def start(self, here, ins, outs, scratch):
        keep, copies = self.copies(here, ins, scratch)
        for each in copies:
            each.start()
        keep.start()

    def finish(self, here, ins, outs, scratch):
        got, _, recv_sem = scratch
        _, copies = self.copies(here, ins, scratch)
        for plane in range(4):
            pltpu.make_async_copy(got.at[plane], got.at[plane], recv_sem.at[plane]).wait()
        outs[0][...] = (got[0] + got[1]) + (got[2] + got[3])
        for each in copies:
            each.wait_send()


def to_columns(upper, lower):
    place = lax.broadcasted_iota(jnp.int32, (128, upper.shape[1]), 0)
    return jnp.transpose(jnp.where(place < 64, upper, lower))


def both_columns(upper, lower):
    lane = lax.broadcasted_iota(jnp.int32, (upper.shape[0], 128), 1)
    return jnp.where(lane < 64, upper, lower)


def in_chunks(rows, chunk, step):
    def one(index, carry):
        step(pl.multiple_of(index * chunk, chunk))
        return carry

    lax.fori_loop(0, rows // chunk, one, 0)


def fold(values):
    total = values[:8]
    for first in range(8, values.shape[0], 8):
        total = total + values[first : first + 8]
    return total


class Parts(Task):
    def use(self, parts):
        self.parts = parts
        self.scratch = list(self.scratch)
        self.at = {}
        reach = []
        for name, part in parts.items():
            self.at[name] = (len(self.scratch), len(self.scratch) + len(part.scratch))
            self.scratch += list(part.scratch)
            reach += [way for way in part.reach if way not in reach]
        self.reach = reach

    def held(self, scratch, name):
        first, last = self.at[name]
        return scratch[first:last]


def norm_pull(grad_out, normal, factor, gain_row):
    scaled = grad_out * gain_row
    width = scaled.shape[1]
    mean = jnp.sum(scaled, axis=1, keepdims=True) / width
    inner = jnp.sum(scaled * normal, axis=1, keepdims=True) / width
    return factor * (scaled - mean - normal * inner)


class StepThenLine(Parts):
    def __init__(self, values):
        self.arrays, self.spaces = (values,), (pltpu.VMEM,)
        self.outs = (jax.ShapeDtypeStruct(values.shape, f32),)
        self.out_spaces = (pltpu.VMEM,)
        self.scratch = (pltpu.VMEM(values.shape, f32),)
        self.use(dict(step=StepSum(values), line=LineSum(values)))

    def start(self, here, ins, outs, scratch):
        self.parts["step"].start(here, ins, scratch[:1], self.held(scratch, "step"))

    def at_moment(self, name, here, ins, outs, scratch):
        held = (here, ins, scratch[:1], self.held(scratch, "step"))
        self.parts["step"].at_moment(name, *held)
        if name == "tail":
            self.parts["step"].finish(*held)
            self.parts["line"].start(here, scratch[:1], outs, self.held(scratch, "line"))

    def finish(self, here, ins, outs, scratch):
        self.parts["line"].finish(here, scratch[:1], outs, self.held(scratch, "line"))


def normalize(values):
    width = values.shape[1]
    centered = values - jnp.sum(values, axis=1, keepdims=True) / width
    factor = lax.rsqrt(jnp.sum(centered * centered, axis=1, keepdims=True) / width + epsilon)
    return centered * factor, factor


def wide_column(column):
    return jnp.broadcast_to(column, (column.shape[0], 128))


def hidden_row(small_ref, layer, at, part):
    first = small_ref.shape[2] - (3 - at) * part
    return jnp.concatenate(
        [small_ref[z, layer : layer + 1, first : first + part] for z in range(4)], axis=1
    )


def scale_of(here, head_scale_ref, layer, wide):
    row = head_scale_ref[layer : layer + 1, :]
    place = lax.broadcasted_iota(jnp.int32, row.shape, 1)
    pair = []
    for i in range(2):
        head = ((2 * here.core + i) * 2 + here.x) * 2 + here.y
        pair.append(jnp.sum(jnp.where(place == head, row, 0.0), axis=1, keepdims=True))
    lane = lax.broadcasted_iota(jnp.int32, (1, 2 * wide), 1)
    return jnp.where(lane < wide, pair[0], pair[1])


NARROW = 128
CHUNK = 256


class FfnForward(Parts):
    def __init__(self, block, first, second, small, middle, shift, norm, layer, late):
        rows, width = block.shape
        hidden = first.shape[1]
        self.late, self.layer, self.last = late, layer, norm is None
        self.arrays = (block, first, second, small, middle, shift, *(norm or ()))
        self.spaces = (pltpu.VMEM,) * 2 + (pltpu.HBM if late else pltpu.VMEM,)
        self.spaces += (pltpu.VMEM,) * (len(self.arrays) - 3)
        self.outs = (
            jax.ShapeDtypeStruct((rows, width), f32),
            jax.ShapeDtypeStruct((8 * rows, width), bf16),
            jax.ShapeDtypeStruct((8 * rows, hidden), f32),
            jax.ShapeDtypeStruct((8 * rows, hidden), f32),
            jax.ShapeDtypeStruct((8 * rows, hidden), bf16),
            jax.ShapeDtypeStruct((2, 8 * rows), f32),
        )
        self.out_spaces = (pltpu.VMEM,) + (pltpu.HBM,) * 4 + (pltpu.VMEM,)
        self.outs += (jax.ShapeDtypeStruct((rows, width), bf16),)
        if norm:
            self.outs += (jax.ShapeDtypeStruct((rows, width), f32),)
            self.outs += (jax.ShapeDtypeStruct((rows, 128), f32),)
        self.out_spaces += (pltpu.VMEM,) * (len(self.outs) - 6)
        self.base = len(self.outs)
        self.scratch = (
            pltpu.VMEM((8 * rows, width), bf16),
            pltpu.VMEM((8 * rows, hidden), f32),
            pltpu.VMEM((8 * rows, hidden), f32),
            pltpu.VMEM((8 * rows, hidden), bf16),
            pltpu.VMEM((2, 8 * rows), f32),
            pltpu.VMEM((rows, 128), f32),
            dma_sems(4),
        )
        parts = dict(
            gather=PlaneGather(block),
            scatter=PlaneScatter(rows, width, 0),
            sums=PlaneSum(jax.ShapeDtypeStruct((2, 8 * rows), f32)),
        )
        if late:
            parts[SECOND] = WeightGather(second, layer, 0)
            self.outs += parts[SECOND].outs
            self.out_spaces += (pltpu.VMEM,)
        self.use(parts)

    def start(self, here, ins, outs, scratch):
        self.parts[GATHER].start(here, ins[:1], scratch[:1], self.held(scratch, GATHER))
        if self.late:
            held = self.held(scratch, SECOND)
            self.parts[SECOND].start(here, ins[2:3], outs[self.base :], held)

    def finish(self, here, ins, outs, scratch):
        block_ref, first_ref, second_ref, small_ref, middle_ref, row_ref = ins[:6]
        part = first_ref.shape[1] // 4
        shift, gain, bias = (hidden_row(small_ref, self.layer, at, part) for at in range(3))
        out_ref, rows_out, slope_out, normal_out, mixed_out, total_ref = outs[:6]
        if self.late:
            second_ref = outs[self.base]
        rows_buf, before, active, mixed, sums, columns, save = scratch[:7]
        rows = block_ref.shape[0]
        hidden_all = 8 * first_ref.shape[1]

        def work(first):
            before[pl.ds(first, rows), :] = lax.dot_general(
                rows_buf[pl.ds(first, rows), :],
                first_ref[...],
                (((1,), (0,)), ((), ())),
                preferred_element_type=f32,
            )

            def step(at):
                piece = pl.ds(pl.multiple_of(first + at, CHUNK), CHUNK)
                u = before[piece, :] + shift
                area = 0.5 * (1.0 + lax.erf(u * 0.5**0.5))
                a = u * area
                active[piece, :] = a
                before[piece, :] = area + u * (jnp.exp(-0.5 * u * u) * (0.5 / jnp.pi) ** 0.5)
                columns[pl.ds(at, CHUNK), :] = both_columns(
                    jnp.sum(a, axis=1, keepdims=True), jnp.sum(a * a, axis=1, keepdims=True)
                )

            in_chunks(rows, CHUNK, step)
            turned = jnp.transpose(columns[...])
            sums[0:1, pl.ds(first, rows)] = turned[0:1]
            sums[1:2, pl.ds(first, rows)] = turned[64:65]

        self.parts[GATHER].finish(
            here, ins[:1], scratch[:1], self.held(scratch, GATHER), work
        )
        held = self.held(scratch, "sums")
        self.parts["sums"].start(here, (sums,), None, held)
        keep_rows = pltpu.make_async_copy(rows_buf, rows_out, save.at[0])
        keep_rows.start()
        keep_slope = pltpu.make_async_copy(before, slope_out, save.at[1])
        keep_slope.start()
        self.parts["sums"].finish(here, (sums,), (total_ref,), held)
        if self.late:
            held = self.held(scratch, SECOND)
            self.parts[SECOND].finish(here, ins[2:3], outs[self.base :], held)
        self.moment(MIDWAY)

        def rows_of(first):
            average = total_ref[0:1, pl.ds(first, rows)] / hidden_all
            spread = total_ref[1:2, pl.ds(first, rows)] / hidden_all - average * average
            columns[...] = to_columns(average, lax.rsqrt(spread + epsilon))

            def step(at):
                piece = pl.ds(pl.multiple_of(first + at, CHUNK), CHUNK)
                pair = columns[pl.ds(at, CHUNK), :]
                normal = (active[piece, :] - pair[:, 0:1]) * pair[:, 64:65]
                active[piece, :] = normal
                mixed[piece, :] = (normal * gain + bias).astype(bf16)

            in_chunks(rows, CHUNK, step)
            return mixed[pl.ds(first, rows), :]

        keep_mixed = pltpu.make_async_copy(mixed, mixed_out, save.at[2])
        keep_normal = pltpu.make_async_copy(active, normal_out, save.at[3])

        def idle():
            keep_mixed.start()
            keep_normal.start()
            self.moment("closing")

        self.parts[SCATTER].finish(
            here,
            None,
            (out_ref,),
            self.held(scratch, SCATTER),
            rows_of,
            lambda: second_ref[...],
            idle=idle,
        )
        layer = slice(self.layer, self.layer + 1)
        after = slice(self.layer + 1, self.layer + 2)

        def settle(at):
            piece = pl.ds(at, NARROW)
            residual = middle_ref[piece, :] + out_ref[piece, :] + row_ref[layer, :]
            out_ref[piece, :] = residual
            if self.last:
                outs[6][piece, :] = residual.astype(bf16)
            else:
                normal, factor = normalize(residual)
                outs[6][piece, :] = (normal * ins[6][after, :] + ins[7][after, :]).astype(bf16)
                outs[7][piece, :] = normal
                outs[8][piece, :] = wide_column(factor)

        in_chunks(rows, NARROW, settle)
        for each in (keep_rows, keep_slope, keep_mixed, keep_normal):
            each.wait()


class FfnBackward(Parts):
    def __init__(
        self,
        block,
        first,
        second,
        small,
        slope,
        normal,
        mixed,
        ffn_rows,
        totals,
        gradient,
        norms,
        layer,
    ):
        self.layer = layer
        rows, width = block.shape
        hidden = second.shape[0]
        self.arrays = (block, first, second, small, totals, slope, normal, mixed, ffn_rows)
        self.spaces = (pltpu.VMEM,) * 5 + (pltpu.HBM,) * 4
        self.arrays += (gradient, *norms)
        self.spaces += (pltpu.VMEM,) * 7
        self.outs = (
            jax.ShapeDtypeStruct((rows, width), f32),
            jax.ShapeDtypeStruct((4, width, hidden // 4), bf16),
            jax.ShapeDtypeStruct((hidden // 4, width), bf16),
            jax.ShapeDtypeStruct((3, hidden), f32),
            jax.ShapeDtypeStruct((rows, width), bf16),
            jax.ShapeDtypeStruct((8, width), f32),
        )
        self.out_spaces = (pltpu.VMEM,) * 6
        self.scratch = (
            pltpu.VMEM((8 * rows, width), bf16),
            pltpu.VMEM((8 * rows, hidden), f32),
            pltpu.VMEM((8 * rows, hidden), f32),
            pltpu.VMEM((8 * rows, hidden), f32),
            pltpu.VMEM((8 * rows, hidden), bf16),
            pltpu.VMEM((8 * rows, width), bf16),
            pltpu.VMEM((8 * rows, hidden), bf16),
            pltpu.VMEM((hidden, width), f32),
            pltpu.VMEM((2, 8 * rows), f32),
            pltpu.VMEM((2, 8 * rows), f32),
            pltpu.VMEM((rows, 128), f32),
            pltpu.VMEM((rows, 128), f32),
            pltpu.VMEM((3, 8, hidden), f32),
            dma_sems(4),
            pltpu.VMEM((4, hidden // 4, width), bf16),
            pltpu.VMEM((6, 8, width), f32),
        )
        self.use(
            dict(
            gather=PlaneGather(block),
            scatter=PlaneScatter(rows, width, 1),
            second=LineScatter(jax.ShapeDtypeStruct((4, hidden // 4, width), bf16)),
            sums=PlaneSum(jax.ShapeDtypeStruct((2, 8 * rows), f32)),
            )
        )

    def loads(self, ins, scratch):
        targets = (scratch[2], scratch[4], scratch[1], scratch[5])
        return [
            pltpu.make_async_copy(source, target, scratch[13].at[i])
            for i, (source, target) in enumerate(zip((ins[6], ins[7], ins[5], ins[8]), targets))
        ]

    def start(self, here, ins, outs, scratch):
        self.parts[GATHER].start(here, ins[:1], scratch[:1], self.held(scratch, GATHER))
        for each in self.loads(ins, scratch):
            each.start()

    def finish(self, here, ins, outs, scratch):
        block_ref, first_ref, second_ref, hidden_ref, totals_ref = ins[:5]
        mid_gain = hidden_row(hidden_ref, self.layer, 1, first_ref.shape[1] // 4)
        out_ref, first_grad, second_quarter, small_ref, branch_ref, vector_ref = outs
        second_grad, vectors = scratch[14:16]
        (
            rows_buf,
            slope,
            normal_buf,
            grads,
            mixed,
            ffn_rows,
            pre_grad,
            second_sum,
            sums,
            got,
            columns,
            factors,
            small,
        ) = scratch[:13]
        rows = block_ref.shape[0]
        hidden_all = 8 * first_ref.shape[1]
        load_normal, load_mixed, load_slope, load_rows = self.loads(ins, scratch)
        load_normal.wait()
        load_mixed.wait()
        second_sum[...] = jnp.zeros_like(second_sum)
        small[...] = jnp.zeros_like(small)

        def factor_columns(first):
            average = totals_ref[0:1, pl.ds(first, rows)] / hidden_all
            spread = totals_ref[1:2, pl.ds(first, rows)] / hidden_all - average * average
            factors[...] = to_columns(average, lax.rsqrt(spread + epsilon))

        def work(first):
            block = pl.ds(first, rows)
            grads[block, :] = lax.dot_general(
                rows_buf[block, :],
                second_ref[...],
                (((1,), (1,)), ((), ())),
                preferred_element_type=f32,
            )
            second_sum[...] += lax.dot_general(
                mixed[block, :],
                rows_buf[block, :],
                (((0,), (0,)), ((), ())),
                preferred_element_type=f32,
            )

            def step(at):
                piece = pl.ds(pl.multiple_of(first + at, CHUNK), CHUNK)
                normal = normal_buf[piece, :]
                grad = grads[piece, :]
                small[0] += fold(grad * normal)
                small[1] += fold(grad)
                scaled = grad * mid_gain
                grads[piece, :] = scaled
                columns[pl.ds(at, CHUNK), :] = both_columns(
                    jnp.sum(scaled, axis=1, keepdims=True),
                    jnp.sum(scaled * normal, axis=1, keepdims=True),
                )

            in_chunks(rows, CHUNK, step)
            turned = jnp.transpose(columns[...])
            sums[0:1, pl.ds(first, rows)] = turned[0:1]
            sums[1:2, pl.ds(first, rows)] = turned[64:65]

        self.parts[GATHER].finish(
            here, ins[:1], scratch[:1], self.held(scratch, GATHER), work
        )
        held = self.held(scratch, "sums")
        self.parts["sums"].start(here, (sums,), None, held)
        second_grad[...] = second_sum[...].astype(bf16).reshape(second_grad.shape)
        load_slope.wait()
        self.moment(MIDWAY)
        self.parts[SECOND].start(here, (second_grad,), None, self.held(scratch, SECOND))
        self.parts["sums"].finish(here, (sums,), (got,), held)

        def rows_of(first):
            factor_columns(first)
            columns[...] = to_columns(
                got[0:1, pl.ds(first, rows)] / hidden_all,
                got[1:2, pl.ds(first, rows)] / hidden_all,
            )

            def step(at):
                piece = pl.ds(pl.multiple_of(first + at, CHUNK), CHUNK)
                pair = columns[pl.ds(at, CHUNK), :]
                factor = factors[pl.ds(at, CHUNK), :][:, 64:65]
                active_grad = factor * (
                    grads[piece, :] - pair[:, 0:1] - normal_buf[piece, :] * pair[:, 64:65]
                )
                rounded = (active_grad * slope[piece, :]).astype(bf16)
                pre_grad[piece, :] = rounded
                small[2] += fold(rounded.astype(f32))

            in_chunks(rows, CHUNK, step)
            return pre_grad[pl.ds(first, rows), :]

        def idle():
            load_rows.wait()
            whole = lax.dot_general(
                ffn_rows[...],
                pre_grad[...],
                (((0,), (0,)), ((), ())),
                preferred_element_type=f32,
            ).astype(bf16)
            part = first_grad.shape[2]
            for i in range(4):
                first_grad[i] = whole[:, i * part : (i + 1) * part]
            self.moment("closing")

        self.parts[SCATTER].finish(
            here,
            None,
            (out_ref,),
            self.held(scratch, SCATTER),
            rows_of,
            lambda: first_ref[...],
            idle=idle,
        )
        gradient_ref, normal_1, factor_1, gain_1, normal_2, factor_2, gain_2 = ins[9:16]
        vectors[...] = jnp.zeros_like(vectors)
        layer = slice(self.layer, self.layer + 1)

        def pull(at):
            piece = pl.ds(at, NARROW)
            grad, gradient = out_ref[piece, :], gradient_ref[piece, :].astype(f32)
            normal = normal_1[piece, :]
            vectors[3] += fold(grad * normal)
            vectors[4] += fold(grad)
            vectors[5] += fold(gradient)
            middle = gradient + norm_pull(
                grad, normal, factor_1[piece, 0:1], gain_1[layer, :]
            )
            out_ref[piece, :] = middle
            normal = normal_2[piece, :]
            vectors[1] += fold(middle * normal)
            vectors[2] += fold(middle)
            branch = norm_pull(middle, normal, factor_2[piece, 0:1], gain_2[layer, :])
            vectors[0] += fold(branch)
            branch_ref[piece, :] = branch.astype(bf16)

        in_chunks(rows, NARROW, pull)
        vector_ref[...] = jnp.zeros_like(vector_ref)
        for i in range(6):
            vector_ref[i : i + 1, :] = jnp.sum(vectors[i], axis=0, keepdims=True)
        held = self.held(scratch, SECOND)
        self.parts[SECOND].finish(here, (second_grad,), (second_quarter,), held)
        for i in range(3):
            small_ref[i : i + 1, :] = jnp.sum(small[i], axis=0, keepdims=True)


class WeightGather(Task):
    def __init__(self, weights, layer, axis, when="start"):
        self.layer, self.axis, self.when = layer, axis, when
        self.arrays, self.spaces = (weights,), (pltpu.HBM,)
        self.outs = (jax.ShapeDtypeStruct(weights.shape[1:], weights.dtype),)
        self.out_spaces = (pltpu.HBM,)
        self.scratch = (dma_sems(4), dma_sems(3))
        self.reach = BY_Z

    def copies(self, here, ins, outs, scratch):
        part = outs[0].shape[self.axis] // 4

        def cut(ref, at):
            piece = pl.ds(pl.multiple_of(at * part, part), part)
            return ref.at[piece, :] if self.axis == 0 else ref.at[:, piece]

        source = cut(ins[0].at[self.layer], 2 * here.y + here.core)
        target = cut(outs[0], here.z)
        keep = pltpu.make_async_copy(source, target, scratch[0].at[3])
        return keep, [
            remote(source, target, scratch[0].at[i], scratch[1].at[i], here.peer(*way))
            for i, way in enumerate(BY_Z)
        ]

    def begin(self, here, ins, outs, scratch):
        keep, copies = self.copies(here, ins, outs, scratch)
        for each in copies:
            each.start()
        keep.start()

    def start(self, *held):
        self.at_moment("start", *held)

    def at_moment(self, name, *held):
        if name == self.when:
            self.begin(*held)

    def finish(self, here, ins, outs, scratch):
        keep, copies = self.copies(here, ins, outs, scratch)
        for each in copies:
            each.wait()
        keep.wait()


class ThenRows(Parts):
    def __init__(self, first, when):
        self.when = when
        shape = first.outs[0]
        self.arrays, self.spaces = first.arrays, first.spaces
        rows = RowsGather(shape)
        self.outs, self.out_spaces = rows.outs, rows.out_spaces
        self.scratch = (pltpu.VMEM(shape.shape, shape.dtype),)
        self.use(dict(first=first, rows=rows))

    def start(self, here, ins, outs, scratch):
        self.parts["first"].start(here, ins, None, self.held(scratch, "first"))

    def at_moment(self, name, here, ins, outs, scratch):
        if name == self.when:
            self.parts["first"].finish(here, ins, scratch[:1], self.held(scratch, "first"))
            self.parts["rows"].begin(here, scratch[:1], outs, self.held(scratch, "rows"))

    def finish(self, here, ins, outs, scratch):
        self.at_moment("end", here, ins, outs, scratch)
        self.parts["rows"].finish(here, scratch[:1], outs, self.held(scratch, "rows"))


BLOCK = 256
SPAN = 512


def head_masks(head_width, width):
    lane = lax.broadcasted_iota(jnp.int32, (1, width), 1)
    lower = (lane < head_width).astype(bf16)
    return lower, (1 - lower).astype(bf16)


def by_head(values, head_width):
    lower, upper = head_masks(head_width, values.shape[1])
    return jnp.concatenate([values * lower, values * upper], axis=0)


def from_heads(pair, head_width):
    rows = pair.shape[0] // 2
    lane = lax.broadcasted_iota(jnp.int32, (rows, pair.shape[1]), 1)
    return jnp.where(lane < head_width, pair[:rows], pair[rows:])


def tile_facts(doc_ref, first, key_first, keys):
    docs = doc_ref[:, pl.ds(first, BLOCK)]
    docs = jnp.concatenate([docs, docs], axis=1)
    key_docs = doc_ref[:, pl.ds(pl.multiple_of(key_first, keys), keys)]
    key_docs = jnp.transpose(jnp.broadcast_to(key_docs, (128, keys)))[:, 0:1]
    place = lax.broadcasted_iota(jnp.int32, (keys, 2 * BLOCK), 1)
    place = jnp.where(place >= BLOCK, place - BLOCK, place) + (first - key_first)
    allowed = (docs == key_docs) & (place >= lax.broadcasted_iota(jnp.int32, place.shape, 0))
    return docs, allowed


def attend_block(
    head_width, first, q_ref, k_ref, v_cols, doc_ref, o_ref, l_ref, s_buf, acc, top, total
):
    block = first // BLOCK
    last = first // SPAN
    pair = by_head(q_ref[pl.ds(first, BLOCK), :], head_width)

    def scores(at):
        keys = k_ref[pl.ds(pl.multiple_of(at * SPAN, SPAN), SPAN), :]
        return lax.dot_general(keys, pair, (((1,), (1,)), ((), ())), preferred_element_type=f32)

    top[...] = jnp.full_like(top, masked)

    def first_pass(at, carry):
        s = scores(at)
        s_buf[at] = s
        peak = s[:8]
        for row in range(8, SPAN, 8):
            peak = jnp.maximum(peak, s[row : row + 8])
        top[...] = jnp.maximum(top[...], peak)
        return carry

    lax.fori_loop(0, last, first_pass, 0)
    docs, allowed = tile_facts(doc_ref, first, last * SPAN, SPAN)
    s = jnp.where(allowed, scores(last), masked)
    shift = jnp.where(docs == 0, 0.0, masked)
    peak = jnp.maximum(
        jnp.max(top[...], axis=0, keepdims=True) + shift, jnp.max(s, axis=0, keepdims=True)
    )

    def weigh(at, p):
        values = v_cols[:, pl.ds(pl.multiple_of(at * SPAN, SPAN), SPAN)]
        return jnp.dot(values, p.astype(bf16), preferred_element_type=f32)

    p = jnp.exp(s - peak)
    total[...] = fold(p)
    acc[...] = weigh(last, p)
    base = peak - shift

    def second_pass(at, carry):
        p = jnp.exp(s_buf[at] - base)
        total[...] += fold(p)
        acc[...] += weigh(at, p)
        return carry

    lax.fori_loop(0, last, second_pass, 0)
    sums = jnp.sum(total[...], axis=0, keepdims=True)
    out = from_heads(jnp.transpose(acc[...] / sums), head_width)
    o_ref[pl.ds(first, BLOCK), :] = out
    l_ref[block] = peak + jnp.log(sums)
    return out


def attend_block_back(
    head_width,
    first,
    do,
    q_ref,
    k_ref,
    k_cols,
    v_ref,
    o_ref,
    l_ref,
    doc_ref,
    acc_k,
    acc_v,
    acc_q,
):
    block = first // BLOCK
    rows = pl.ds(first, BLOCK)
    pair_q = by_head(q_ref[rows, :], head_width)
    pair_do = by_head(do, head_width)
    out = o_ref[rows, :]
    inner = jnp.sum(
        jnp.concatenate([out, out], axis=0) * pair_do.astype(f32), axis=1, keepdims=True
    )
    inner = jnp.transpose(jnp.broadcast_to(inner, (2 * BLOCK, 128)))[0:1, :]
    logs = l_ref[block]
    docs, allowed = tile_facts(doc_ref, first, first, BLOCK)

    def step(at, base, allowed):
        piece = pl.ds(pl.multiple_of(at * BLOCK, BLOCK), BLOCK)
        s = lax.dot_general(
            k_ref[piece, :], pair_q, (((1,), (1,)), ((), ())), preferred_element_type=f32
        )
        dp = lax.dot_general(
            v_ref[piece, :], pair_do, (((1,), (1,)), ((), ())), preferred_element_type=f32
        )
        p = jnp.exp(s - base)
        if allowed is not None:
            p = jnp.where(allowed, p, 0.0)
        ds = (p * (dp - inner)).astype(bf16)
        acc_v[piece, :] += jnp.dot(p.astype(bf16), pair_do, preferred_element_type=f32)
        acc_k[piece, :] += jnp.dot(ds, pair_q, preferred_element_type=f32)
        return jnp.dot(k_cols[:, piece], ds, preferred_element_type=f32)

    acc_q[...] = step(block, logs, allowed)
    base = jnp.where(docs == 0, logs, -masked)

    def earlier(at, carry):
        acc_q[...] += step(at, base, None)
        return carry

    lax.fori_loop(0, block, earlier, 0)
    grad = from_heads(jnp.transpose(acc_q[...]), head_width)
    return (grad * head_width**-0.5).astype(bf16)


def turned(values):
    return jnp.transpose(values.astype(f32)).astype(bf16)


class AttnForward(Parts):
    def __init__(
        self, block, docs, scale, heads, biases, wide, layer, norms, residual=None, late=None
    ):
        rows, width = block.shape
        self.head_width, self.layer, self.late = wide, layer, late
        here = 2 * wide
        self.arrays = (block, docs, scale, biases, *heads)
        far = pltpu.HBM if late else pltpu.VMEM
        self.spaces = (far, far, pltpu.VMEM) + (far,) * (1 + len(heads))
        column = jax.ShapeDtypeStruct((8 * rows, here), bf16)
        self.outs = (
            jax.ShapeDtypeStruct((rows, width), f32),
            jax.ShapeDtypeStruct((8 * rows, width), bf16),
            column,
            column,
            column,
            column,
            jax.ShapeDtypeStruct((8 * rows, here), f32),
            jax.ShapeDtypeStruct((8 * rows // BLOCK, 1, 2 * BLOCK), f32),
        )
        wide_shape = jax.ShapeDtypeStruct((rows, 128), f32)
        self.outs += (self.outs[0], wide_shape, self.outs[0], wide_shape)
        self.outs += (jax.ShapeDtypeStruct((rows, width), bf16),)
        self.out_spaces = (pltpu.VMEM, pltpu.HBM) + (pltpu.VMEM,) * 11
        self.arrays += tuple(norms)
        self.spaces += (pltpu.VMEM,) * 5
        self.scratch = (
            pltpu.VMEM((8 * rows, width), bf16),
            pltpu.VMEM((here, 8 * rows), bf16),
            pltpu.VMEM((8 * rows // SPAN, SPAN, 2 * BLOCK), f32),
            pltpu.VMEM((here, 2 * BLOCK), f32),
            pltpu.VMEM((8, 2 * BLOCK), f32),
            pltpu.VMEM((8, 2 * BLOCK), f32),
            dma_sems(1),
        )
        parts = dict(gather=PlaneGather(block), scatter=PlaneScatter(rows, width, 0))
        if late:
            parts.update(heads=HeadGather(*heads, layer), biases=LineGather(biases))
            half = jax.ShapeDtypeStruct((rows // 2, width), block.dtype)
            for i in range(2):
                parts["tokens", i] = PlaneMove(half, when="push")
            parts["docs"] = PlaneMove(docs, when="push")
            self.outs += parts["heads"].outs + parts["biases"].outs
            self.outs += (jax.ShapeDtypeStruct(docs.shape, f32),)
            self.outs += (jax.ShapeDtypeStruct(block.shape, f32),) * 2
            self.outs += (wide_shape,)
            self.out_spaces += (pltpu.VMEM,) * 6
            self.scratch += (pltpu.VMEM(block.shape, bf16), pltpu.VMEM(block.shape, bf16))
            self.scratch += (pltpu.VMEM(docs.shape, docs.dtype),)
            self.arrays += tuple(late)
            self.spaces += (pltpu.VMEM,) * 2
        else:
            self.arrays += (residual,)
            self.spaces += (pltpu.VMEM,)
        self.base = 3 + 1 + len(heads)
        self.use(parts)

    def start(self, here, ins, outs, scratch):
        if self.late:
            for part, held in self.moves(here, ins, scratch):
                part.start(*held)
        else:
            self.parts[GATHER].start(here, ins[:1], scratch[:1], self.held(scratch, GATHER))

    def moves(self, here, ins, scratch):
        half = ins[0].shape[0] // 2
        triples = []
        for i in range(2):
            piece = pl.ds(i * half, half)
            triples.append((("tokens", i), ins[0].at[piece], scratch[7].at[piece]))
        triples.append(("docs", ins[1], scratch[9]))
        return [
            (self.parts[name], (here, (source,), (target,), self.held(scratch, name)))
            for name, source, target in triples
        ]

    def first_norm(self, here, ins, outs, scratch):
        tokens, block = scratch[7:9]
        residual_ref, normal_ref, factor_ref = outs[16:19]
        moves = self.moves(here, ins, scratch)
        for part, held in moves:
            part.at_moment("push", *held)
        self.parts["biases"].start(here, ins[3:4], outs[14:15], self.held(scratch, "biases"))
        self.parts["heads"].start(here, ins[4:6], outs[13:14], self.held(scratch, "heads"))
        for part, held in moves:
            part.finish(*held)
        outs[15][...] = scratch[9][...].astype(f32)
        gain, bias = (ref[self.layer : self.layer + 1, :] for ref in ins[self.base + 5 :])
        values = tokens[...].astype(f32)
        residual_ref[...] = values
        normal, factor = normalize(values)
        factor_ref[...] = wide_column(factor)
        normal_ref[...] = normal
        block[...] = (normal * gain + bias).astype(bf16)
        return block

    def finish(self, here, ins, outs, scratch):
        block_ref, doc_ref, scale_ref = ins[:3]
        scale_row = scale_of(here, scale_ref, self.layer, self.head_width)
        heads_ref, bias_ref = outs[13:15] if self.late else (ins[4], ins[3])
        if self.late:
            doc_ref = outs[15]
            block_ref = self.first_norm(here, ins, outs, scratch)
            self.parts[GATHER].start(
                here, (block_ref,), scratch[:1], self.held(scratch, GATHER)
            )
        out_ref, rows_out, q_ref, k_ref, v_ref, z_ref, o_ref, l_ref = outs[:8]
        rows_buf, v_cols, s_buf, acc, top, total, save = scratch[:7]
        rows, model_width = block_ref.shape
        wide = self.head_width
        width = 2 * wide

        def bias_row(at):
            pair = [
                bias_ref[2 * here.core + i, self.layer : self.layer + 1, at : at + width]
                for i in range(2)
            ]
            lane = lax.broadcasted_iota(jnp.int32, (1, width), 1)
            return jnp.where(lane < wide, pair[0], pair[1])

        def work(first):
            block = pl.ds(first, rows)
            projected = lax.dot_general(
                rows_buf[block, :],
                heads_ref[0:3].reshape(3 * width, model_width),
                (((1,), (1,)), ((), ())),
                preferred_element_type=f32,
            )
            q = (projected[:, :width] + bias_row(0)).astype(bf16).astype(f32)
            q_ref[block, :] = (q * wide**-0.5).astype(bf16)
            k_ref[block, :] = projected[:, width : 2 * width].astype(bf16)
            v = (projected[:, 2 * width :] + bias_row(width)).astype(bf16)
            v_ref[block, :] = v
            v_cols[:, block] = turned(v)

        self.parts[GATHER].finish(
            here,
            (block_ref,),
            scratch[:1],
            self.held(scratch, GATHER),
            None if self.late else work,
        )
        keep_rows = pltpu.make_async_copy(rows_buf, rows_out, save.at[0])
        keep_rows.start()
        if self.late:
            self.parts["heads"].arrive(0, outs[13:14], self.held(scratch, "heads"))
            self.parts["biases"].finish(here, ins[3:4], outs[14:15], self.held(scratch, "biases"))
            in_chunks(8 * rows, rows, work)
            self.parts["heads"].arrive(1, outs[13:14], self.held(scratch, "heads"))
        self.moment(MIDWAY)

        def rows_of(first):
            out = attend_block(
                wide, first, q_ref, k_ref, v_cols, doc_ref, o_ref, l_ref, s_buf, acc, top, total
            )
            z = (out * scale_row).astype(bf16)
            z_ref[pl.ds(first, rows), :] = z
            return z

        self.parts[SCATTER].finish(
            here,
            None,
            (out_ref,),
            self.held(scratch, SCATTER),
            rows_of,
            lambda: heads_ref[3].reshape(width, model_width),
            idle=lambda: self.moment("closing"),
        )
        residual_ref = outs[16] if self.late else ins[self.base + 5]
        layer = slice(self.layer, self.layer + 1)
        shift, gain_1, bias_1, gain_2, bias_2 = (
            ref[layer, :] for ref in ins[self.base : self.base + 5]
        )
        normal_1, factor_1, normal_2, factor_2, next_ref = outs[8:13]

        def settle(at):
            piece = pl.ds(at, NARROW)
            normal, factor = normalize(out_ref[piece, :] + shift)
            normal_1[piece, :] = normal
            factor_1[piece, :] = wide_column(factor)
            middle = residual_ref[piece, :] + (normal * gain_1 + bias_1)
            out_ref[piece, :] = middle
            normal, factor = normalize(middle)
            normal_2[piece, :] = normal
            factor_2[piece, :] = wide_column(factor)
            next_ref[piece, :] = (normal * gain_2 + bias_2).astype(bf16)

        in_chunks(rows, NARROW, settle)
        keep_rows.wait()
        if self.late:
            held = self.held(scratch, "heads")
            self.parts["heads"].sent(here, ins[4:6], outs[13:14], held)


class AttnBackward(Parts):
    def __init__(
        self, block, docs, scale, heads, q, k, v, z, o, logs, attn_rows, norm, hidden, layer, end
    ):
        self.end = end
        self.layer = layer
        rows, width = block.shape
        kinds, _, wide, _ = heads.shape
        self.head_width = wide
        here = 2 * wide
        self.arrays = (block, docs, scale, heads, q, k, v, z, o, logs, attn_rows)
        self.spaces = (pltpu.VMEM,) * 10 + (pltpu.HBM,)
        self.arrays += (*norm, hidden)
        self.spaces += (pltpu.VMEM,) * 5
        self.shipped = kinds if end else kinds // 2
        leaving = jax.ShapeDtypeStruct((self.shipped, *heads.shape[1:]), bf16)
        staying = jax.ShapeDtypeStruct((kinds - self.shipped, *heads.shape[1:]), bf16)
        heads_sum = HeadScatter(leaving)
        half_rows = jax.ShapeDtypeStruct((rows // 2, width), bf16)
        vector, sums = jax.ShapeDtypeStruct((8, width), f32), jax.ShapeDtypeStruct((4, 4, here), f32)
        quarter = heads_sum.outs[0]
        if end:
            tail = {("move", i): PlaneMove(half_rows, True, "push") for i in range(2)}
            tail.update(
                vectors=PlaneSum(vector),
                line=LineSum(vector),
                rows=RowsGather(quarter),
                hidden=ThenRows(LineScatter(sums), "push"),
            )
            self.outs = (jax.ShapeDtypeStruct((rows, width), bf16), vector) + tail["rows"].outs + tail["hidden"].outs
            self.out_spaces = (pltpu.HBM, pltpu.VMEM, pltpu.HBM, pltpu.HBM)
        else:
            self.outs = (jax.ShapeDtypeStruct((rows, width), f32), quarter, sums)
            self.outs += (jax.ShapeDtypeStruct((rows, width), bf16), vector, staying)
            self.out_spaces = (pltpu.VMEM,) * 6
        self.scratch = (
            pltpu.VMEM((8 * rows, width), bf16),
            pltpu.VMEM((8 * rows, width), bf16),
            pltpu.VMEM((here, 8 * rows), bf16),
            pltpu.VMEM((8 * rows, here), f32),
            pltpu.VMEM((8 * rows, here), f32),
            pltpu.VMEM((here, 2 * BLOCK), f32),
            pltpu.VMEM((8 * rows, 3 * here), bf16),
            pltpu.VMEM((here, width), f32),
            pltpu.VMEM((3, 8, here), f32),
            dma_sems(1),
            pltpu.VMEM((2, 8, width), f32),
            pltpu.VMEM(heads.shape, bf16),
        )
        if end:
            self.scratch += (
                pltpu.VMEM((rows, width), f32),
                pltpu.VMEM(quarter.shape, bf16),
                pltpu.VMEM(sums.shape, f32),
                pltpu.VMEM((rows, width), bf16),
                pltpu.VMEM(vector.shape, f32),
                pltpu.VMEM(vector.shape, f32),
            )
        parts = dict(gather=OrderedGather(block), scatter=PlaneScatter(rows, width, 0))
        parts.update(tail if end else {})
        parts["heads"] = heads_sum
        self.use(parts)

    def load(self, ins, scratch):
        return pltpu.make_async_copy(ins[10], scratch[1], scratch[9].at[0])

    def start(self, here, ins, outs, scratch):
        self.parts[GATHER].start(here, ins[:1], scratch[:1], self.held(scratch, GATHER))
        self.load(ins, scratch).start()

    def finish(self, here, ins, outs, scratch):
        block_ref, doc_ref, scale_ref, heads_ref, q_ref, k_ref, v_ref, z_ref, o_ref, l_ref = ins[:10]
        results = scratch[12:17] if self.end else outs
        out_ref, quarter_ref, hidden_ref, rounded_ref, vector_ref = results[:5]
        middle_ref, normal_ref, factor_ref, gain_ref, sums_ref = ins[11:16]
        (
            rows_buf,
            attn_rows,
            k_cols,
            acc_k,
            acc_v,
            acc_q,
            proj,
            out_sum,
            small,
        ) = scratch[:9]
        vectors = scratch[10]
        heads_grad = scratch[11]
        leaving = (heads_grad.at[pl.ds(0, self.shipped)],)
        scale_row = scale_of(here, scale_ref, self.layer, self.head_width)
        rows, model_width = block_ref.shape
        wide = self.head_width
        width = 2 * wide
        acc_k[...] = jnp.zeros_like(acc_k)
        acc_v[...] = jnp.zeros_like(acc_v)
        out_sum[...] = jnp.zeros_like(out_sum)
        small[...] = jnp.zeros_like(small)
        k_cols[...] = turned(k_ref[...])

        def work(first):
            block = pl.ds(first, rows)
            scaled_grad = lax.dot_general(
                rows_buf[block, :],
                heads_ref[3].reshape(width, model_width),
                (((1,), (1,)), ((), ())),
                preferred_element_type=f32,
            )
            out_sum[...] += lax.dot_general(
                z_ref[block, :],
                rows_buf[block, :],
                (((0,), (0,)), ((), ())),
                preferred_element_type=f32,
            )
            small[0] += fold(o_ref[block, :] * scaled_grad)
            grad = attend_block_back(
                wide,
                first,
                (scaled_grad * scale_row).astype(bf16),
                q_ref,
                k_ref,
                k_cols,
                v_ref,
                o_ref,
                l_ref,
                doc_ref,
                acc_k,
                acc_v,
                acc_q,
            )
            proj[block, 0:width] = grad
            small[1] += fold(grad.astype(f32))

        self.parts[GATHER].finish(
            here,
            ins[:1],
            scratch[:1],
            self.held(scratch, GATHER),
            work,
            self.moment,
        )

        def settle(first):
            block = pl.ds(first, rows)
            proj[block, width : 2 * width] = acc_k[block, :].astype(bf16)
            value_grad = acc_v[block, :].astype(bf16)
            proj[block, 2 * width : 3 * width] = value_grad
            small[2] += fold(value_grad.astype(f32))

        in_chunks(8 * rows, rows, settle)
        self.moment(MIDWAY)

        def early():
            self.load(ins, scratch).wait()
            qkv_grad = lax.dot_general(
                proj[...],
                attn_rows[...],
                (((0,), (0,)), ((), ())),
                preferred_element_type=f32,
            )
            heads_grad[0:3] = qkv_grad.astype(bf16).reshape(3, 2, wide, model_width)
            heads_grad[3] = out_sum[...].astype(bf16).reshape(2, wide, model_width)
            self.parts["heads"].start(here, leaving, None, self.held(scratch, "heads"))
            if not self.end:
                outs[5][...] = heads_grad[self.shipped :]

        early()
        self.parts[SCATTER].finish(
            here,
            None,
            (out_ref,),
            self.held(scratch, SCATTER),
            lambda first: proj[pl.ds(first, rows), :],
            lambda: heads_ref[0:3].reshape(3 * width, model_width),
            idle=lambda: self.moment("closing"),
        )
        vectors[...] = jnp.zeros_like(vectors)
        layer = slice(self.layer, self.layer + 1)

        def pull(at):
            piece = pl.ds(at, NARROW)
            grad, normal = out_ref[piece, :], normal_ref[piece, :]
            vectors[0] += fold(grad * normal)
            vectors[1] += fold(grad)
            gradient = middle_ref[piece, :] + norm_pull(
                grad, normal, factor_ref[piece, 0:1], gain_ref[layer, :]
            )
            out_ref[piece, :] = gradient
            rounded_ref[piece, :] = gradient.astype(bf16)

        home = []
        if self.end:
            for i in range(2):
                piece = pl.ds(i * (rows // 2), rows // 2)
                held = self.held(scratch, ("move", i))
                refs = (rounded_ref.at[piece],), (outs[0].at[piece],)
                home.append((self.parts["move", i], (here, *refs, held)))
                pull(i * NARROW)
                home[i][0].start(*home[i][1])
        else:
            in_chunks(rows, NARROW, pull)
        scale_cols, query_cols, value_cols = (
            jnp.sum(small[i], axis=0, keepdims=True) for i in range(3)
        )
        vector_ref[...] = jnp.zeros_like(vector_ref)
        for i in range(2):
            vector_ref[i : i + 1, :] = jnp.sum(vectors[i], axis=0, keepdims=True)
        lane = lax.broadcasted_iota(jnp.int32, (1, width), 1)
        place = lax.broadcasted_iota(jnp.int32, (1, model_width), 1)
        head_sums = jnp.zeros((1, model_width), f32)
        for i in range(2):
            head = ((2 * here.core + i) * 2 + here.x) * 2 + here.y
            own = (lane >= i * wide) & (lane < (i + 1) * wide)
            total = jnp.sum(jnp.where(own, scale_cols, 0.0), axis=1, keepdims=True)
            head_sums = head_sums + jnp.where(place == head, total, 0.0)
        vector_ref[2:3, :] = head_sums
        pairs = [
            jnp.concatenate(
                [cols[:, i * wide : (i + 1) * wide] for cols in (query_cols, value_cols)], axis=1
            )
            for i in range(2)
        ]
        for shard in range(4):
            for row, source in enumerate((2, 0, 1)):
                cut = sums_ref[source : source + 1, shard * width : (shard + 1) * width]
                hidden_ref[shard, row : row + 1, :] = cut
            own = here.core == shard // 2
            hidden_ref[shard, 3:4, :] = jnp.where(own, pairs[shard % 2], 0.0)
        self.moment("tail")
        held = (here, leaving, (quarter_ref,), self.held(scratch, "heads"))
        if not self.end:
            self.parts["heads"].finish(*held)
            return
        sum_held = (here, (vector_ref,), (scratch[17],), self.held(scratch, "vectors"))
        line_held = (here, (scratch[17],), outs[1:2], self.held(scratch, "line"))
        rows_held = (here, (quarter_ref,), outs[2:3], self.held(scratch, "rows"))
        hidden_held = (here, (hidden_ref,), outs[3:4], self.held(scratch, "hidden"))
        self.parts["vectors"].start(*sum_held)
        self.parts["hidden"].start(*hidden_held)
        self.parts["heads"].finish(*held)
        self.parts["rows"].begin(*rows_held)
        self.parts["vectors"].finish(*sum_held)
        self.parts["line"].start(*line_held)
        for part, refs in home:
            part.at_moment("push", *refs)
        self.parts["hidden"].at_moment("push", *hidden_held)
        self.parts["line"].finish(*line_held)
        self.parts["rows"].finish(*rows_held)
        self.parts["hidden"].finish(*hidden_held)
        for part, refs in home:
            part.finish(*refs)


def finish_kernel(layers, *refs):
    count = 2 + 6 * layers
    far, refs, sems = refs[:count], refs[count:-1], refs[-1]
    refs, near = refs[: len(refs) - count], refs[len(refs) - count :]
    loads = [pltpu.make_async_copy(a, b, sems.at[i]) for i, (a, b) in enumerate(zip(far, near))]
    order = [0, 1] + [2 + g * layers + i for i in range(layers - 1, -1, -1) for g in range(6)]
    for index in order:
        loads[index].start()
    refs = (*near, *refs)
    (layer_ref, grad_ref), refs = refs[:2], refs[2:]
    groups = []
    for _ in range(6):
        groups.append(refs[:layers])
        refs = refs[layers:]
    firsts, seconds, heads_all, hiddens, earlies, lates = groups
    (
        layer_out,
        grad_out,
        attn_gain,
        attn_bias,
        qkv_out,
        bias_out,
        scale_out,
        out_out,
        out_shift,
        post_gain,
        post_bias,
        ffn_gain,
        ffn_bias,
        first_out,
        first_shift,
        mid_gain,
        mid_bias,
        second_out,
        second_shift,
    ) = refs
    loads[0].wait()
    layer_out[...] = layer_ref[...]
    loads[1].wait()
    grad_out[...] = grad_ref[...].astype(f32)
    for layer in range(layers - 1, -1, -1):
        for group in range(6):
            loads[2 + group * layers + layer].wait()
        first, second, heads, hidden = (g[layer] for g in (firsts, seconds, heads_all, hiddens))
        part = first.shape[2]
        wide, half = heads.shape[2:]
        row = slice(layer, layer + 1)
        for i, ref in enumerate((out_shift, post_gain, post_bias, ffn_gain, ffn_bias, second_shift)):
            ref[row, :] = earlies[layer][i : i + 1, :]
        for i, ref in enumerate((attn_gain, attn_bias)):
            ref[row, :] = lates[layer][i : i + 1, :]
        scale_out[row, :] = lates[layer][2:3, 0 : scale_out.shape[1]]
        for i in range(4):
            cut = slice(i * part, (i + 1) * part)
            first_out[layer, :, cut] = first[i].astype(f32)
            second_out[layer, cut, :] = second[i].astype(f32)
            for at, ref in enumerate((first_shift, mid_gain, mid_bias)):
                ref[row, cut] = hidden[i, at : at + 1, :]
        biases = [hidden[2 * y, 3:4, :] + hidden[2 * y + 1, 3:4, :] for y in range(2)]
        for i in range(2):
            bias_out[layer, i : i + 1, :] = jnp.concatenate(
                [each[:, i * wide : (i + 1) * wide] for each in biases], axis=1
            )
        for core in range(2):
            here = slice(core * half, (core + 1) * half)
            for kind in range(3):
                pair = jnp.concatenate([heads[core, kind], heads[2 + core, kind]], axis=0)
                qkv_out[layer, kind, here, :] = jnp.transpose(pair.astype(f32))
            for y in range(2):
                out_out[layer, y * wide : (y + 1) * wide, here] = heads[2 * y + core, 3].astype(f32)


def finish_all(layer_output, gradient, heads_count, *groups):
    firsts, seconds, heads = groups[:3]
    layers = len(firsts)
    rows, width = layer_output.shape
    part = firsts[0].shape[2]
    wide = heads[0].shape[2]
    vector = jax.ShapeDtypeStruct((layers, width), f32)
    hidden = jax.ShapeDtypeStruct((layers, 4 * part), f32)
    outs = (
        jax.ShapeDtypeStruct((rows, width), bf16),
        jax.ShapeDtypeStruct((rows, width), f32),
        vector,
        vector,
        jax.ShapeDtypeStruct((layers, 3, width, 2 * wide), f32),
        jax.ShapeDtypeStruct((layers, 2, 2 * wide), f32),
        jax.ShapeDtypeStruct((layers, heads_count), f32),
        jax.ShapeDtypeStruct((layers, 2 * wide, width), f32),
        vector,
        vector,
        vector,
        vector,
        vector,
        jax.ShapeDtypeStruct((layers, width, 4 * part), f32),
        hidden,
        hidden,
        hidden,
        jax.ShapeDtypeStruct((layers, 4 * part, width), f32),
        vector,
    )
    arrays = [layer_output, gradient] + [each for group in groups for each in group]
    results = list(
        pl.pallas_call(
            partial(finish_kernel, layers),
            out_shape=outs,
            in_specs=[pl.BlockSpec(memory_space=pltpu.HBM)] * len(arrays),
            out_specs=[pl.BlockSpec(memory_space=pltpu.VMEM)] * len(outs),
            scratch_shapes=[
                *[pltpu.VMEM(each.shape, each.dtype) for each in arrays],
                dma_sems(len(arrays)),
            ],
            compiler_params=vmem_params(None, 60),
        )(*arrays)
    )
    results[4] = jnp.transpose(results[4], (0, 2, 1, 3))
    return tuple(results)


def plane_device(
    tokens,
    segment_ids,
    cotangent,
    ln_attn_gain,
    ln_attn_bias,
    qkv_weight,
    qv_bias,
    head_scale,
    out_weight,
    out_bias,
    ln_post_gain,
    ln_post_bias,
    ln_ffn_gain,
    ln_ffn_bias,
    fc1_weight,
    fc1_bias,
    mid_gain,
    mid_bias,
    fc2_weight,
    fc2_bias,
):
    layers = qkv_weight.shape[0]
    model_width = tokens.shape[1]
    heads_all = head_scale.shape[1]
    head_width = model_width // heads_all
    hidden_here = fc1_weight.shape[2]
    hidden_all = hidden_here * 8
    quarter = hidden_here // 4
    half_width = model_width // 2
    x, y, core = lax.axis_index("x"), lax.axis_index("y"), lax.axis_index("core")
    quarter_at = 2 * y + core
    width = 2 * head_width
    ids = iter(range(1, 64))

    docs = segment_ids[None, :]

    def cut(values, at, size, axis):
        return lax.dynamic_slice_in_dim(values, at * size, size, axis)

    qkv_rows = jnp.transpose(qkv_weight, (0, 2, 3, 1))
    bias_heads = cut(qv_bias, y, head_width, 2)
    small = jnp.concatenate(
        [
            jnp.concatenate([bias_heads, bias_heads], axis=2).reshape(layers, 2 * width),
            cut(fc1_bias, quarter_at, quarter, 1),
            cut(mid_gain, quarter_at, quarter, 1),
            cut(mid_bias, quarter_at, quarter, 1),
        ],
        axis=1,
    )
    heads_here = [None] * layers
    norms = (out_bias, ln_post_gain, ln_post_bias, ln_ffn_gain, ln_ffn_bias)
    attn_norm = (ln_attn_gain, ln_attn_bias)

    stored = []
    for layer in range(layers):
        first, last = layer == 0, layer + 1 == layers
        if first:
            task = AttnForward(
                tokens,
                docs,
                head_scale,
                (qkv_rows, out_weight),
                small,
                head_width,
                layer,
                norms,
                late=attn_norm,
            )
            sides = [WeightGather(fc1_weight, layer, 1, MIDWAY)]
        else:
            task = AttnForward(
                block,
                docs,
                head_scale,
                (heads_here[layer],),
                small,
                head_width,
                layer,
                norms,
                residual=residual,
            )
            sides = [WeightGather(fc1_weight, layer, 1)]
        if last:
            sides.append(PlaneMove(cotangent, when="closing", first=MIDWAY))
        (got, (first_here,), *rest) = run_tasks(ids, task, *sides)
        middle, attn_rows, q, k, v, scaled, attended, logs = got[:8]
        post_normal, post_factor, ffn_normal, ffn_factor, block = got[8:13]
        if first:
            heads_here[0], small, docs, _, attn_normal, attn_factor = got[13:]
        here = (attn_normal, attn_factor)
        if last:
            gradient = gradient_b = rest[0][0]
        sides = []
        if not last:
            sides = [HeadGather(qkv_rows, out_weight, layer + 1, MIDWAY if first else "start")]
        (got, *rest) = run_tasks(
            ids,
            FfnForward(
                block,
                first_here,
                fc2_weight,
                small,
                middle,
                fc2_bias,
                None if last else attn_norm,
                layer,
                True,
            ),
            *sides,
        )
        residual, ffn_rows, slope, hidden_normal, mixed, totals, block = got[:7]
        second_here = got[-1]
        if not last:
            attn_normal, attn_factor = got[7:9]
            heads_here[layer + 1] = rest[0][0]
        stored.append(
            (
                first_here,
                second_here,
                *here,
                attn_rows,
                q,
                k,
                v,
                attended,
                logs,
                scaled,
                post_normal,
                post_factor,
                ffn_normal,
                ffn_factor,
                ffn_rows,
                slope,
                hidden_normal,
                mixed,
                totals,
            )
        )
    first_done, second_done = [None] * layers, [None] * layers
    heads_done, hidden_done = [None] * layers, [None] * layers
    early_done, late_done = [None] * layers, [None] * layers
    late_vectors = None
    for layer in reversed(range(layers)):
        (
            first_here,
            second_here,
            attn_normal,
            attn_factor,
            attn_rows,
            q,
            k,
            v,
            attended,
            logs,
            scaled,
            post_normal,
            post_factor,
            ffn_normal,
            ffn_factor,
            ffn_rows,
            slope,
            hidden_normal,
            mixed,
            totals,
        ) = stored[layer]
        last = layer + 1 == layers
        if last:
            sides = [PlaneMove(block, back=True)]
        else:
            sides = [HeadScatter(heads_rest), ThenRows(LineScatter(hidden_grad), "closing")]
            sides += [LineSum(early_vectors), StepSum(late_vectors)]
        ((gradient, first_grad, second_grad, hidden_sums, branch_b, early_vectors), *got) = (
            run_tasks(
                ids,
                FfnBackward(
                    gradient_b,
                    first_here,
                    second_here,
                    small,
                    slope,
                    hidden_normal,
                    mixed,
                    ffn_rows,
                    totals,
                    gradient,
                    (
                        ffn_normal,
                        ffn_factor,
                        ln_ffn_gain,
                        post_normal,
                        post_factor,
                        ln_post_gain,
                    ),
                    layer,
                ),
                *sides,
            )
        )
        if last:
            layer_output = got[0][0]
        else:
            heads_rest, hidden_done[layer + 1], early_done[layer + 1], late_vectors = (
                each[0] for each in got
            )
            heads_grad = jnp.concatenate([heads_grad, heads_rest], axis=0)
        sides = [ThenRows(LineScatter(first_grad), "soon"), RowsGather(second_grad, "spare")]
        sides.append(StepThenLine(early_vectors) if layer == 0 else StepSum(early_vectors))
        if not last:
            sides += [LineSum(late_vectors), RowsGather(heads_grad, "spare")]
        (results, *got) = run_tasks(
            ids,
            AttnBackward(
                branch_b,
                docs,
                head_scale,
                heads_here[layer],
                q,
                k,
                v,
                scaled,
                attended,
                logs,
                attn_rows,
                (gradient, attn_normal, attn_factor, ln_attn_gain),
                hidden_sums,
                layer,
                layer == 0,
            ),
            *sides,
        )
        first_done[layer], second_done[layer], early_vectors = got[0][0], got[1][0], got[2][0]
        if not last:
            late_done[layer + 1], heads_done[layer + 1] = got[3][0], got[4][0]
        if layer == 0:
            input_grad, late_done[0], heads_done[0], hidden_done[0] = results
            early_done[0] = early_vectors
        else:
            gradient, heads_grad, hidden_grad, gradient_b, late_vectors, heads_rest = results
    return finish_all(
        layer_output,
        input_grad,
        heads_all,
        first_done,
        second_done,
        heads_done,
        hidden_done,
        early_done,
        late_done,
    )


def split_specs(rows, mp):
    both = tuple(rows) + tuple(mp)
    in_specs = (
        P(both, None),
        P(rows),
        P(both, None),
        P(),
        P(),
        P(None, None, None, mp),
        P(None, None, mp),
        P(),
        P(None, mp, None),
        P(),
        P(),
        P(),
        P(),
        P(),
        P(None, None, mp),
        P(None, mp),
        P(None, mp),
        P(None, mp),
        P(None, mp, None),
        P(),
    )
    out_specs = (
        P(both, None),
        P(both, None),
        P(),
        P(),
        P(None, None, None, mp),
        P(None, None, mp),
        P(),
        P(None, mp, None),
        P(),
        P(),
        P(),
        P(),
        P(),
        P(None, None, mp),
        P(None, mp),
        P(None, mp),
        P(None, mp),
        P(None, mp, None),
        P(),
    )
    return in_specs, out_specs


def solution(mesh):
    if mesh.shape["rows"] == 4 and mesh.shape["mp"] == 8:
        planes = Mesh(mesh.devices.reshape(2, 2, 4, 2), ("y", "core", "z", "x"))
        in_specs, out_specs = split_specs(("y", "core"), ("z", "x"))
        return jax.shard_map(
            plane_device, mesh=planes, in_specs=in_specs, out_specs=out_specs, check_vma=False
        )
    in_specs, out_specs = split_specs(("rows",), ("mp",))
    return jax.shard_map(
        per_device, mesh=mesh, in_specs=in_specs, out_specs=out_specs, check_vma=False
    )
```
